32 devices in a mesh: inst: 4 (over y, core), cell: 8 (over z, x).
Axes of the slice: x: 2, y: 2, z: 4, core: 2. Of those that a mesh axis runs over, the one named last changes fastest.
Arguments:
- state: float32 [8, 6, 16, 256], P('inst', None, 'cell'), may hold values from -0.8 to 5, as said below
- pseudo_rate: float32 [16, 256], P('cell'), may hold values from 0.001 to 0.01
- line_next: int32 [256], replicated, may hold values from 0 to 255, each once
- face_codes: int32 [2, 8], replicated, may hold values from 0 to 2
Outputs:
- new_state: float32 [8, 6, 16, 256], P('inst', None, 'cell')
The draws below stay inside these ranges and needn't reach their ends.
Inputs may be any that keep to these rules, and one draw needn't show every extreme that they name: `state`: conserved variables of a gas with ratio of specific heats 1.4: in every cell density lies between 0.7 and 1.3 and pressure between 0.6 and 1.4. `line_next`: every line is named once. `face_codes`: 0 a slip wall, 1 a fixed inflow state, 2 extrapolation.
All inputs are finite; a program needn't handle non-finite values.
Results may differ from the reference program's by a relative error of at most 0.0003.
Values sent between devices are 32-bit elements; how exact they have to be, the bound alone decides.
No kernel may reach another device: no remote copies, remote signals or barrier semaphores. Data moves between devices by JAX's collectives and lax.ppermute only.
A program may use at most 64 MiB of HBM per device.

```python
import math
import jax
import jax.numpy as jnp
import numpy as np
from jax import lax

NT = 8
LINES_DEV = 32
NI = 16
L = 256
TILES = 8


def draw_state(key, part):
    subkeys = jax.random.split(key, 5)
    grid_shape = (NT, NI, L)
    density = jax.random.uniform(subkeys[0], grid_shape, jnp.float32, 0.7, 1.3)
    pressure = jax.random.uniform(subkeys[1], grid_shape, jnp.float32, 0.6, 1.4)
    axial_speed = 0.5 + jnp.clip(0.3 * jax.random.normal(subkeys[2], grid_shape, jnp.float32), -0.6, 0.6)
    cross_speed = jnp.clip(0.3 * jax.random.normal(subkeys[3], (2,) + grid_shape, jnp.float32), -0.6, 0.6)
    viscous = jnp.exp(jax.random.uniform(subkeys[4], grid_shape, jnp.float32, math.log(0.05), math.log(0.5)))
    kinetic = 0.5 * density * (axial_speed * axial_speed + cross_speed[0] * cross_speed[0] + cross_speed[1] * cross_speed[1])
    energy = pressure / 0.4 + kinetic
    return jnp.stack([density, density * axial_speed, density * cross_speed[0], density * cross_speed[1], energy, density * viscous], axis=1)


def set_ends(entries, own_key, smallest, high):
    longest = entries.shape.index(max(entries.shape))
    spots = []
    for shift in (0, 1):
        where = [jax.random.randint(jax.random.fold_in(own_key, axis), (), 0, length) for axis, length in enumerate(entries.shape)]
        where[longest] = (where[longest] + shift) % entries.shape[longest]
        spots.append(tuple(where))
    return entries.at[spots[0]].set(smallest).at[spots[1]].set(high)


def shard_levels(key, dims, cuts, smallest, largest):
    level = 1.0
    for position, parts in cuts:
        heights = jax.random.uniform(jax.random.fold_in(jax.random.fold_in(key, 6), position), (parts,), jnp.float32, smallest / len(cuts), largest / len(cuts))
        level = level * jnp.repeat(jnp.exp(heights), dims[position] // parts).reshape((-1,) + (1,) * (len(dims) - 1 - position))
    return level


def setup_inputs(seed: int = 0) -> dict:
    key_of = jax.random.split(jax.random.key(seed), 5)
    return {
        "state": draw_state(jax.random.fold_in(key_of[4], 71), 0),
        "pseudo_rate": jnp.clip(jnp.exp(math.log(0.01) - 2.30258502 * jax.random.uniform(key_of[1], (NI, L), jnp.float32) ** shard_levels(key_of[1], (NI, L), ((0, 8),), -0.2, 0.2)), 0.001, 0.01),
        "line_next": jax.random.permutation(key_of[2], L).astype(jnp.int32),
        "face_codes": set_ends(jax.random.randint(key_of[3], (2, TILES), 0, 3), jax.random.fold_in(key_of[3], 1), 0, 2).astype(jnp.int32),
    }


GAMMA_GAS = 1.4
OMEGA_BLADE = 1.0
SENSOR_GAIN = 0.25
FOURTH_GAIN = 0.03125
PITCH_GAIN = 0.5
SECOND_IMPL = 1.0
FOURTH_IMPL = 0.25
FREE_STATE = (1.0, 0.5, 0.0, 0.0, 2.625, 0.2)
MIRROR_SIGNS = (1.0, -1.0, 1.0, 1.0, 1.0, 1.0)
ZERO_BLOCK = (0.0, 0.0, 0.0, 0.0)
UNIT_BLOCK = (1.0, 0.0, 0.0, 1.0)
ZERO_PAIR = (0.0, 0.0)

def spectral_matrix(instances):
    offsets = np.arange(instances)[:, None] - np.arange(instances)[None, :]
    angles = np.pi * offsets / instances
    safe_sin = np.where(offsets == 0, 1.0, np.sin(angles))
    parity = np.where(np.mod(offsets, 2) == 0, -1.0, 1.0)
    matrix_table = np.where(offsets == 0, 0.0, 0.5 * OMEGA_BLADE * parity * np.cos(angles) / safe_sin)
    return jnp.asarray(matrix_table, jnp.float32)

def primitive_parts(cells_state):
    density = cells_state[..., 0, :, :]
    inverse = 1.0 / density
    velocity_x = cells_state[..., 1, :, :] * inverse
    velocity_y = cells_state[..., 2, :, :] * inverse
    velocity_z = cells_state[..., 3, :, :] * inverse
    energy = cells_state[..., 4, :, :]
    pressure = (GAMMA_GAS - 1.0) * (energy - 0.5 * density * (velocity_x * velocity_x + velocity_y * velocity_y + velocity_z * velocity_z))
    sound_speed = jnp.sqrt(GAMMA_GAS * pressure * inverse)
    return (velocity_x, velocity_y, pressure, sound_speed)

def directed_flux(cells_state, normal_velocity, pressure, component):
    zero_plane = jnp.zeros_like(pressure)
    pressure_rows = [zero_plane, zero_plane, zero_plane, zero_plane, pressure * normal_velocity, zero_plane]
    pressure_rows[component] = pressure
    return cells_state * normal_velocity[..., None, :, :] + jnp.stack(pressure_rows, axis=-3)

def line_residual(padded):
    velocity_x, velocity_y, pressure, sound_speed = primitive_parts(padded)
    flux_line = directed_flux(padded, velocity_x, pressure, 1)
    radius = jnp.abs(velocity_x) + sound_speed
    sensor = jnp.abs(pressure[..., 2:, :] - 2.0 * pressure[..., 1:-1, :] + pressure[..., :-2, :]) / (pressure[..., 2:, :] + 2.0 * pressure[..., 1:-1, :] + pressure[..., :-2, :])
    second = SENSOR_GAIN * jnp.maximum(sensor[..., :-1, :], sensor[..., 1:, :])
    fourth = jnp.maximum(0.0, FOURTH_GAIN - second)
    face_radius = 0.5 * (radius[..., 1:-2, :] + radius[..., 2:-1, :])
    left_far = padded[..., :-3, :]
    left_near = padded[..., 1:-2, :]
    right_near = padded[..., 2:-1, :]
    right_far = padded[..., 3:, :]
    damping = face_radius[..., None, :, :] * (second[..., None, :, :] * (right_near - left_near) - fourth[..., None, :, :] * (right_far - 3.0 * right_near + 3.0 * left_near - left_far))
    face_flux = 0.5 * (flux_line[..., 1:-2, :] + flux_line[..., 2:-1, :]) - damping
    return (face_flux[..., 1:, :] - face_flux[..., :-1, :], radius)

def pitch_residual(cells_state, next_lines, prev_lines):
    velocity_x, velocity_y, pressure, sound_speed = primitive_parts(cells_state)
    pitch_flux = directed_flux(cells_state, velocity_y, pressure, 2)
    radius = jnp.abs(velocity_y) + sound_speed
    state_next = jnp.take(cells_state, next_lines, axis=-1)
    flux_next = jnp.take(pitch_flux, next_lines, axis=-1)
    radius_next = jnp.take(radius, next_lines, axis=-1)
    face_flux = 0.5 * (pitch_flux + flux_next) - PITCH_GAIN * (0.5 * (radius + radius_next))[..., None, :, :] * (state_next - cells_state)
    return face_flux - jnp.take(face_flux, prev_lines, axis=-1)

def boundary_cells(edge_pair, line_codes, lower_end):
    reflected = edge_pair[..., ::-1, :] * jnp.asarray(MIRROR_SIGNS, jnp.float32)[:, None, None]
    if lower_end:
        copied = jnp.concatenate([edge_pair[..., :1, :], edge_pair[..., :1, :]], axis=-2)
    else:
        copied = jnp.concatenate([edge_pair[..., 1:, :], edge_pair[..., 1:, :]], axis=-2)
    inflow = jnp.asarray(FREE_STATE, jnp.float32)[:, None, None] + jnp.zeros_like(edge_pair)
    return jnp.where(line_codes == 0, reflected, jnp.where(line_codes == 1, inflow, copied))

def line_coefficients(radius_ext, diagonal_term, positions, total_cells):
    radius_below = radius_ext[..., :-2, :]
    radius_centre = radius_ext[..., 1:-1, :]
    radius_above = radius_ext[..., 2:, :]
    face_below = 0.5 * (radius_below + radius_centre)
    face_above = 0.5 * (radius_centre + radius_above)
    far_low = FOURTH_IMPL * radius_below
    near_low = -SECOND_IMPL * face_below - 2.0 * FOURTH_IMPL * (radius_below + radius_centre)
    middle = diagonal_term + SECOND_IMPL * (face_below + face_above) + FOURTH_IMPL * (radius_below + 4.0 * radius_centre + radius_above)
    near_high = -SECOND_IMPL * face_above - 2.0 * FOURTH_IMPL * (radius_centre + radius_above)
    far_high = FOURTH_IMPL * radius_above
    column = positions[:, None]
    far_low = jnp.where(column >= 2, far_low, 0.0)
    near_low = jnp.where(column >= 1, near_low, 0.0)
    near_high = jnp.where(column <= total_cells - 2, near_high, 0.0)
    far_high = jnp.where(column <= total_cells - 3, far_high, 0.0)
    return (far_low, near_low, middle, near_high, far_high)

def block_product(first_matrix, second_matrix):
    return (first_matrix[0] * second_matrix[0] + first_matrix[1] * second_matrix[2], first_matrix[0] * second_matrix[1] + first_matrix[1] * second_matrix[3], first_matrix[2] * second_matrix[0] + first_matrix[3] * second_matrix[2], first_matrix[2] * second_matrix[1] + first_matrix[3] * second_matrix[3])

def block_inverse(matrix):
    determinant = matrix[0] * matrix[3] - matrix[1] * matrix[2]
    reciprocal = 1.0 / determinant
    return (matrix[3] * reciprocal, -matrix[1] * reciprocal, -matrix[2] * reciprocal, matrix[0] * reciprocal)

def block_apply(matrix, vector):
    return (matrix[0] * vector[0] + matrix[1] * vector[1], matrix[2] * vector[0] + matrix[3] * vector[1])

def add_blocks(first_members, second_members):
    return tuple((a + b for a, b in zip(first_members, second_members)))

def negate(members):
    return tuple((-a for a in members))

def extend_blocks(members, fill_values):
    return tuple((jnp.concatenate([m, jnp.full_like(m[..., :1, :], f)], axis=-2) for m, f in zip(members, fill_values)))

def shift_next(members, fill_values):
    return tuple((jnp.concatenate([m[..., 1:, :], jnp.full_like(m[..., :1, :], f)], axis=-2) for m, f in zip(members, fill_values)))

def shift_prev(members):
    return tuple((jnp.concatenate([jnp.zeros_like(m[..., :1, :]), m[..., :-1, :]], axis=-2) for m in members))

def pair_split(member):
    shaped = member.reshape(member.shape[:-2] + (member.shape[-2] // 2, 2, member.shape[-1]))
    return (shaped[..., 0, :], shaped[..., 1, :])

def split_parity(members):
    halves = [pair_split(m) for m in members]
    return (tuple((h[0] for h in halves)), tuple((h[1] for h in halves)))

def alternate(first_member, second_member):
    stacked = jnp.stack((first_member, second_member), axis=-2)
    return stacked.reshape(first_member.shape[:-2] + (2 * first_member.shape[-2], first_member.shape[-1]))

def reduce_blocks(sub_blocks, diag_blocks, super_blocks, right_side):
    block_count = diag_blocks[0].shape[-2]
    if block_count == 1:
        return block_apply(block_inverse(diag_blocks), right_side)
    if block_count % 2 == 1:
        sub_blocks = extend_blocks(sub_blocks, ZERO_BLOCK)
        diag_blocks = extend_blocks(diag_blocks, UNIT_BLOCK)
        super_blocks = extend_blocks(super_blocks, ZERO_BLOCK)
        right_side = extend_blocks(right_side, ZERO_PAIR)
    sub_even, sub_odd = split_parity(sub_blocks)
    diag_even, diag_odd = split_parity(diag_blocks)
    super_even, super_odd = split_parity(super_blocks)
    side_even, side_odd = split_parity(right_side)
    inverse_even = block_inverse(diag_even)
    inverse_next = shift_next(inverse_even, UNIT_BLOCK)
    sub_next = shift_next(sub_even, ZERO_BLOCK)
    super_next = shift_next(super_even, ZERO_BLOCK)
    side_next = shift_next(side_even, ZERO_PAIR)
    left_factor = negate(block_product(sub_odd, inverse_even))
    right_factor = negate(block_product(super_odd, inverse_next))
    reduced_sub = block_product(left_factor, sub_even)
    reduced_diag = add_blocks(diag_odd, add_blocks(block_product(left_factor, super_even), block_product(right_factor, sub_next)))
    reduced_super = block_product(right_factor, super_next)
    reduced_side = add_blocks(side_odd, add_blocks(block_apply(left_factor, side_even), block_apply(right_factor, side_next)))
    odd_values = reduce_blocks(reduced_sub, reduced_diag, reduced_super, reduced_side)
    before_values = shift_prev(odd_values)
    remainder = add_blocks(side_even, negate(add_blocks(block_apply(sub_even, before_values), block_apply(super_even, odd_values))))
    even_values = block_apply(inverse_even, remainder)
    merged = tuple((alternate(e, o) for e, o in zip(even_values, odd_values)))
    return tuple((m[..., :block_count, :] for m in merged))

def line_solve(coefficients, right_side):
    pairs_list = [pair_split(m[:, None]) for m in coefficients]
    zero_plane = jnp.zeros_like(pairs_list[2][0])
    sub_blocks = (pairs_list[0][0], pairs_list[1][0], zero_plane, pairs_list[0][1])
    diag_blocks = (pairs_list[2][0], pairs_list[3][0], pairs_list[1][1], pairs_list[2][1])
    super_blocks = (pairs_list[4][0], zero_plane, pairs_list[3][1], pairs_list[4][1])
    values = reduce_blocks(sub_blocks, diag_blocks, super_blocks, pair_split(right_side))
    return alternate(values[0], values[1])

def reference(state, pseudo_rate, line_next, face_codes):
    spectral = spectral_matrix(NT)
    source_time = jnp.einsum('nm,mvil->nvil', spectral, state, precision=lax.Precision.HIGHEST)
    prev_lines = jnp.zeros_like(line_next).at[line_next].set(jnp.arange(L, dtype=jnp.int32))
    codes_lines = jnp.repeat(face_codes, LINES_DEV, axis=1)

    def one_instance(inputs):
        cells_state, time_term = inputs
        lower_ghost = boundary_cells(cells_state[:, 0:2, :], codes_lines[0], True)
        upper_ghost = boundary_cells(cells_state[:, -2:, :], codes_lines[1], False)
        padded = jnp.concatenate([lower_ghost, cells_state, upper_ghost], axis=1)
        line_part, radius = line_residual(padded)
        residual = line_part + pitch_residual(cells_state, line_next, prev_lines) + time_term
        centre_radius = radius[2:-2, :]
        radius_ext = jnp.pad(centre_radius, ((1, 1), (0, 0)))
        coefficients = line_coefficients(radius_ext, pseudo_rate * centre_radius, jnp.arange(NI, dtype=jnp.int32), NI)
        update = line_solve(tuple((c[None] for c in coefficients)), -residual[None])
        return cells_state + update[0]
    return lax.map(one_instance, (state, source_time))
```

```python
import functools

import jax
import jax.numpy as jnp
import numpy as np
from jax import lax
from jax.experimental import pallas as pl
from jax.experimental.pallas import tpu as pltpu
from jax.sharding import PartitionSpec as P

NT = 8
LINES_DEV = 32


GAMMA_GAS = 1.4
OMEGA_BLADE = 1.0
SENSOR_GAIN = 0.25
FOURTH_GAIN = 0.03125
PITCH_GAIN = 0.5
SECOND_IMPL = 1.0
FOURTH_IMPL = 0.25
FREE_STATE = (1.0, 0.5, 0.0, 0.0, 2.625, 0.2)
MIRROR_SIGNS = (1.0, -1.0, 1.0, 1.0, 1.0, 1.0)
ZERO_BLOCK = (0.0, 0.0, 0.0, 0.0)
UNIT_BLOCK = (1.0, 0.0, 0.0, 1.0)
ZERO_PAIR = (0.0, 0.0)


def extended(block, sides, width):
    for axis, dim in sides:
        count = lax.axis_size(axis)
        forward = [(i, i + 1) for i in range(count - 1)]
        backward = [(target, source) for source, target in forward]
        low = lax.ppermute(
            lax.slice_in_dim(block, block.shape[dim] - width, None, axis=dim), axis, forward
        )
        high = lax.ppermute(lax.slice_in_dim(block, 0, width, axis=dim), axis, backward)
        block = jnp.concatenate([low, block, high], axis=dim)
    return block


def spectral_matrix(instances):
    offsets = np.arange(instances)[:, None] - np.arange(instances)[None, :]
    angles = np.pi * offsets / instances
    safe_sin = np.where(offsets == 0, 1.0, np.sin(angles))
    parity = np.where(np.mod(offsets, 2) == 0, -1.0, 1.0)
    matrix_table = np.where(
        offsets == 0, 0.0, 0.5 * OMEGA_BLADE * parity * np.cos(angles) / safe_sin
    )
    return jnp.asarray(matrix_table, jnp.float32)


def primitive_parts(cells_state):
    density = cells_state[..., 0, :, :]
    inverse = 1.0 / density
    velocity_x = cells_state[..., 1, :, :] * inverse
    velocity_y = cells_state[..., 2, :, :] * inverse
    velocity_z = cells_state[..., 3, :, :] * inverse
    energy = cells_state[..., 4, :, :]
    pressure = (GAMMA_GAS - 1.0) * (
        energy
        - 0.5
        * density
        * (velocity_x * velocity_x + velocity_y * velocity_y + velocity_z * velocity_z)
    )
    sound_speed = jnp.sqrt(GAMMA_GAS * pressure * inverse)
    return (velocity_x, velocity_y, pressure, sound_speed)


def directed_flux(cells_state, normal_velocity, pressure, component):
    zero_plane = jnp.zeros_like(pressure)
    pressure_rows = [
        zero_plane,
        zero_plane,
        zero_plane,
        zero_plane,
        pressure * normal_velocity,
        zero_plane,
    ]
    pressure_rows[component] = pressure
    return cells_state * normal_velocity[..., None, :, :] + jnp.stack(pressure_rows, axis=-3)


def line_residual(padded):
    velocity_x, velocity_y, pressure, sound_speed = primitive_parts(padded)
    flux_line = directed_flux(padded, velocity_x, pressure, 1)
    radius = jnp.abs(velocity_x) + sound_speed
    sensor = jnp.abs(
        pressure[..., 2:, :] - 2.0 * pressure[..., 1:-1, :] + pressure[..., :-2, :]
    ) / (pressure[..., 2:, :] + 2.0 * pressure[..., 1:-1, :] + pressure[..., :-2, :])
    second = SENSOR_GAIN * jnp.maximum(sensor[..., :-1, :], sensor[..., 1:, :])
    fourth = jnp.maximum(0.0, FOURTH_GAIN - second)
    face_radius = 0.5 * (radius[..., 1:-2, :] + radius[..., 2:-1, :])
    left_far = padded[..., :-3, :]
    left_near = padded[..., 1:-2, :]
    right_near = padded[..., 2:-1, :]
    right_far = padded[..., 3:, :]
    damping = face_radius[..., None, :, :] * (
        second[..., None, :, :] * (right_near - left_near)
        - fourth[..., None, :, :] * (right_far - 3.0 * right_near + 3.0 * left_near - left_far)
    )
    face_flux = 0.5 * (flux_line[..., 1:-2, :] + flux_line[..., 2:-1, :]) - damping
    return (face_flux[..., 1:, :] - face_flux[..., :-1, :], radius)


def pitch_parts(cells_state):
    velocity_x, velocity_y, pressure, sound_speed = primitive_parts(cells_state)
    return (directed_flux(cells_state, velocity_y, pressure, 2), jnp.abs(velocity_y) + sound_speed)


def pitch_residual(cells_state, next_lines, prev_lines):
    pitch_flux, radius = pitch_parts(cells_state)
    state_next = jnp.take(cells_state, next_lines, axis=-1)
    flux_next, radius_next = pitch_parts(state_next)
    face_flux = 0.5 * (pitch_flux + flux_next) - PITCH_GAIN * (0.5 * (radius + radius_next))[
        ..., None, :, :
    ] * (state_next - cells_state)
    return face_flux - jnp.take(face_flux, prev_lines, axis=-1)


def boundary_cells(edge_pair, line_codes, lower_end):
    reflected = edge_pair[..., ::-1, :] * jnp.asarray(MIRROR_SIGNS, jnp.float32)[:, None, None]
    if lower_end:
        copied = jnp.concatenate([edge_pair[..., :1, :], edge_pair[..., :1, :]], axis=-2)
    else:
        copied = jnp.concatenate([edge_pair[..., 1:, :], edge_pair[..., 1:, :]], axis=-2)
    inflow = jnp.asarray(FREE_STATE, jnp.float32)[:, None, None] + jnp.zeros_like(edge_pair)
    return jnp.where(line_codes == 0, reflected, jnp.where(line_codes == 1, inflow, copied))


def line_coefficients(radius_ext, diagonal_term, positions, total_cells):
    radius_below = radius_ext[..., :-2, :]
    radius_centre = radius_ext[..., 1:-1, :]
    radius_above = radius_ext[..., 2:, :]
    face_below = 0.5 * (radius_below + radius_centre)
    face_above = 0.5 * (radius_centre + radius_above)
    far_low = FOURTH_IMPL * radius_below
    near_low = -SECOND_IMPL * face_below - 2.0 * FOURTH_IMPL * (radius_below + radius_centre)
    middle = (
        diagonal_term
        + SECOND_IMPL * (face_below + face_above)
        + FOURTH_IMPL * (radius_below + 4.0 * radius_centre + radius_above)
    )
    near_high = -SECOND_IMPL * face_above - 2.0 * FOURTH_IMPL * (radius_centre + radius_above)
    far_high = FOURTH_IMPL * radius_above
    column = positions[:, None]
    far_low = jnp.where(column >= 2, far_low, 0.0)
    near_low = jnp.where(column >= 1, near_low, 0.0)
    near_high = jnp.where(column <= total_cells - 2, near_high, 0.0)
    far_high = jnp.where(column <= total_cells - 3, far_high, 0.0)
    return (far_low, near_low, middle, near_high, far_high)


def block_product(first_matrix, second_matrix):
    return (
        first_matrix[0] * second_matrix[0] + first_matrix[1] * second_matrix[2],
        first_matrix[0] * second_matrix[1] + first_matrix[1] * second_matrix[3],
        first_matrix[2] * second_matrix[0] + first_matrix[3] * second_matrix[2],
        first_matrix[2] * second_matrix[1] + first_matrix[3] * second_matrix[3],
    )


def block_inverse(matrix):
    determinant = matrix[0] * matrix[3] - matrix[1] * matrix[2]
    reciprocal = 1.0 / determinant
    return (
        matrix[3] * reciprocal,
        -matrix[1] * reciprocal,
        -matrix[2] * reciprocal,
        matrix[0] * reciprocal,
    )


def block_apply(matrix, vector):
    return (
        matrix[0] * vector[0] + matrix[1] * vector[1],
        matrix[2] * vector[0] + matrix[3] * vector[1],
    )


def add_blocks(first_members, second_members):
    return tuple((a + b for a, b in zip(first_members, second_members)))


def negate(members):
    return tuple((-a for a in members))


def extend_blocks(members, fill_values):
    return tuple(
        (
            jnp.concatenate([m, jnp.full_like(m[..., :1, :], f)], axis=-2)
            for m, f in zip(members, fill_values)
        )
    )


def shift_next(members, fill_values):
    return tuple(
        (
            jnp.concatenate([m[..., 1:, :], jnp.full_like(m[..., :1, :], f)], axis=-2)
            for m, f in zip(members, fill_values)
        )
    )


def shift_prev(members):
    return tuple(
        (jnp.concatenate([jnp.zeros_like(m[..., :1, :]), m[..., :-1, :]], axis=-2) for m in members)
    )


def pair_split(member):
    shaped = member.reshape(member.shape[:-2] + (member.shape[-2] // 2, 2, member.shape[-1]))
    return (shaped[..., 0, :], shaped[..., 1, :])


def split_parity(members):
    halves = [pair_split(m) for m in members]
    return (tuple((h[0] for h in halves)), tuple((h[1] for h in halves)))


def alternate(first_member, second_member):
    stacked = jnp.stack((first_member, second_member), axis=-2)
    return stacked.reshape(
        first_member.shape[:-2] + (2 * first_member.shape[-2], first_member.shape[-1])
    )


def reduce_blocks(sub_blocks, diag_blocks, super_blocks, right_side):
    block_count = diag_blocks[0].shape[-2]
    if block_count == 1:
        return block_apply(block_inverse(diag_blocks), right_side)
    if block_count % 2 == 1:
        sub_blocks = extend_blocks(sub_blocks, ZERO_BLOCK)
        diag_blocks = extend_blocks(diag_blocks, UNIT_BLOCK)
        super_blocks = extend_blocks(super_blocks, ZERO_BLOCK)
        right_side = extend_blocks(right_side, ZERO_PAIR)
    sub_even, sub_odd = split_parity(sub_blocks)
    diag_even, diag_odd = split_parity(diag_blocks)
    super_even, super_odd = split_parity(super_blocks)
    side_even, side_odd = split_parity(right_side)
    inverse_even = block_inverse(diag_even)
    inverse_next = shift_next(inverse_even, UNIT_BLOCK)
    sub_next = shift_next(sub_even, ZERO_BLOCK)
    super_next = shift_next(super_even, ZERO_BLOCK)
    side_next = shift_next(side_even, ZERO_PAIR)
    left_factor = negate(block_product(sub_odd, inverse_even))
    right_factor = negate(block_product(super_odd, inverse_next))
    reduced_sub = block_product(left_factor, sub_even)
    reduced_diag = add_blocks(
        diag_odd,
        add_blocks(block_product(left_factor, super_even), block_product(right_factor, sub_next)),
    )
    reduced_super = block_product(right_factor, super_next)
    reduced_side = add_blocks(
        side_odd,
        add_blocks(block_apply(left_factor, side_even), block_apply(right_factor, side_next)),
    )
    odd_values = reduce_blocks(reduced_sub, reduced_diag, reduced_super, reduced_side)
    before_values = shift_prev(odd_values)
    remainder = add_blocks(
        side_even,
        negate(
            add_blocks(block_apply(sub_even, before_values), block_apply(super_even, odd_values))
        ),
    )
    even_values = block_apply(inverse_even, remainder)
    merged = tuple((alternate(e, o) for e, o in zip(even_values, odd_values)))
    return tuple((m[..., :block_count, :] for m in merged))


def cells_leading(block):
    moved = jnp.transpose(block, (2, 0, 1, 3))
    return moved.reshape(block.shape[2], block.shape[0] * block.shape[1] * block.shape[3])


def solve_in_lanes(coefficients, line_source):
    source_shape = line_source.shape
    lane_coef = [cells_leading(jnp.broadcast_to(c[:, None], source_shape)) for c in coefficients]
    pairs_list = [pair_split(m) for m in lane_coef]
    zero_plane = jnp.zeros_like(pairs_list[2][0])
    sub_blocks = (pairs_list[0][0], pairs_list[1][0], zero_plane, pairs_list[0][1])
    diag_blocks = (pairs_list[2][0], pairs_list[3][0], pairs_list[1][1], pairs_list[2][1])
    super_blocks = (pairs_list[4][0], zero_plane, pairs_list[3][1], pairs_list[4][1])
    values = reduce_blocks(
        sub_blocks, diag_blocks, super_blocks, pair_split(cells_leading(line_source))
    )
    flat = alternate(values[0], values[1])
    shaped = flat.reshape(source_shape[2], source_shape[0], source_shape[1], source_shape[3])
    return jnp.transpose(shaped, (1, 2, 0, 3))


def return_tiles(line_values):
    return lax.all_to_all(line_values, "cell", split_axis=2, concat_axis=3, tiled=True)


def local_by_lines(state, pseudo_rate, line_next, face_codes):
    local_count = state.shape[0]
    tile_cells = state.shape[2]
    cell_index = lax.axis_index("cell")
    cell_count = lax.axis_size("cell")
    total_cells = tile_cells * cell_count
    spectral = spectral_matrix(NT)
    first_local = lax.axis_index("inst") * local_count
    own_rows = lax.dynamic_slice_in_dim(spectral, first_local, local_count, 0)
    shard_block = jax.tree.map(lambda a: lax.all_gather(a, "inst", axis=0, tiled=True), state)
    columns = lax.slice_in_dim(own_rows, 0, shard_block.shape[0], axis=1)
    time_term = jnp.zeros_like(state) + jnp.einsum(
        "nm,mvil->nvil", columns, shard_block, precision=lax.Precision.HIGHEST
    )
    padded = extended(state, (("cell", 2),), 2)
    codes_lines = jnp.repeat(face_codes, LINES_DEV, axis=1)
    lower_ghost = boundary_cells(state[:, :, 0:2, :], codes_lines[0], True)
    upper_ghost = boundary_cells(state[:, :, -2:, :], codes_lines[1], False)
    lower_rim = jnp.where(cell_index == 0, lower_ghost, padded[:, :, :2, :])
    upper_rim = jnp.where(cell_index == cell_count - 1, upper_ghost, padded[:, :, -2:, :])
    padded = jnp.concatenate([lower_rim, padded[:, :, 2:-2, :], upper_rim], axis=2)
    line_part, radius = line_residual(padded)
    prev_lines = (
        jnp.zeros_like(line_next).at[line_next].set(jnp.arange(line_next.shape[0], dtype=jnp.int32))
    )
    residual = line_part + pitch_residual(state, line_next, prev_lines) + time_term
    right_side = -residual
    centre_radius = radius[:, 2:-2, :]
    diagonal_term = pseudo_rate * centre_radius
    positions = cell_index * tile_cells + jnp.arange(-1, tile_cells + 1, dtype=jnp.int32)
    inside = (positions >= 0) & (positions < total_cells)
    radius_ext = jnp.where(inside[:, None], radius[:, 1:-1, :], 0.0)
    coefficients = line_coefficients(radius_ext, diagonal_term, positions[1:-1], total_cells)
    stacked = jnp.stack(coefficients, axis=1)
    line_source = lax.all_to_all(right_side, "cell", split_axis=3, concat_axis=2, tiled=True)
    line_coef = lax.all_to_all(stacked, "cell", split_axis=3, concat_axis=2, tiled=True)
    update = return_tiles(solve_in_lanes(tuple((line_coef[:, k] for k in range(5))), line_source))
    return state + update


LANES = 128
ROWS = 8
PAIRS = 3
CELL_ROWS = PAIRS * ROWS
BLOCK_ROWS = 56


def spectral_offsets():
    table = np.zeros(NT)
    for offset in range(1, NT):
        angle = np.pi * offset / NT
        parity = -1.0 if offset % 2 == 0 else 1.0
        table[offset] = 0.5 * OMEGA_BLADE * parity * np.cos(angle) / np.sin(angle)
    return [float(np.float32(value)) for value in table]


def pack_kernel(state_ref, rate_ref, out_ref):
    for cell in range(2):
        for var in range(6):
            for inst in range(2):
                for half in range(2):
                    row = cell * CELL_ROWS + (var // 2) * ROWS + (var % 2) * 4 + inst * 2 + half
                    out_ref[pl.ds(row, 1), :] = state_ref[
                        inst, var, pl.ds(cell, 1), pl.ds(half * LANES, LANES)
                    ]
        for half in range(2):
            out_ref[pl.ds(2 * CELL_ROWS + cell * 2 + half, 1), :] = rate_ref[
                pl.ds(cell, 1), pl.ds(half * LANES, LANES)
            ]
    out_ref[pl.ds(52, 4), :] = jnp.zeros((4, LANES), jnp.float32)


def two_by_two(first, second):
    def entry(a, b, c, d):
        terms = [x * y for x, y in ((a, b), (c, d)) if x is not None and y is not None]
        return None if not terms else terms[0] if len(terms) == 1 else terms[0] + terms[1]

    return (
        entry(first[0], second[0], first[1], second[2]),
        entry(first[0], second[1], first[1], second[3]),
        entry(first[2], second[0], first[3], second[2]),
        entry(first[2], second[1], first[3], second[3]),
    )


def inverse_of(matrix):
    reciprocal = 1.0 / (matrix[0] * matrix[3] - matrix[1] * matrix[2])
    return (
        matrix[3] * reciprocal,
        -(matrix[1] * reciprocal),
        -(matrix[2] * reciprocal),
        matrix[0] * reciprocal,
    )


def less(first, second):
    return tuple(a if b is None else a - b for a, b in zip(first, second))


def minus(members):
    return tuple(None if a is None else -a for a in members)


def eliminate(centre, left, left_inverse, right, right_inverse):
    left_factor = two_by_two(centre[0], left_inverse)
    right_factor = two_by_two(centre[2], right_inverse)
    sub = minus(two_by_two(left_factor, left[0]))
    diag = less(
        less(centre[1], two_by_two(left_factor, left[2])), two_by_two(right_factor, right[0])
    )
    sup = minus(two_by_two(right_factor, right[2]))
    side = []
    for k in range(PAIRS):
        for row in range(2):
            value = centre[3][row * PAIRS + k]
            for factor, other in ((left_factor, left[3]), (right_factor, right[3])):
                value = value - (
                    factor[2 * row] * other[k] + factor[2 * row + 1] * other[PAIRS + k]
                )
            side.append((row * PAIRS + k, value))
    return sub, diag, sup, [value for _, value in sorted(side, key=lambda item: item[0])]


def line_kernel(
    cells, all_ref, next_ref, codes_ref, out_ref, coef_ref, side_ref, coef2_ref, side2_ref,
    couple_ref, diag3_ref, side3_ref,
):
    own_inst = lax.axis_index("inst")
    own_cell = lax.axis_index("cell")
    shape = (ROWS, LANES)
    row_index = lax.broadcasted_iota(jnp.int32, shape, 0)
    lane_index = lax.broadcasted_iota(jnp.int32, shape, 1)
    first_var = row_index < 4
    first_inst = (row_index & 2) == 0
    half_index = row_index & 1
    first_half = half_index == 0
    zero = jnp.zeros(shape, jnp.float32)

    next_rows = [next_ref[pl.ds(half, 1), :] for half in range(2)]
    next_line = jnp.where(first_half, next_rows[0], next_rows[1])
    column = lax.broadcasted_iota(jnp.int32, (LANES, LANES), 0)
    prev_halves = []
    for target in range(2):
        total = None
        for source in range(2):
            hits = jnp.where(column + target * LANES == next_rows[source], 1.0, 0.0)
            names = (lane_index + source * LANES).astype(jnp.float32)
            part = lax.dot_general(
                names, hits, (((1,), (1,)), ((), ())), preferred_element_type=jnp.float32
            )
            total = part if total is None else total + part
        prev_halves.append(total)
    prev_line = jnp.where(first_half, prev_halves[0], prev_halves[1]).astype(jnp.int32)

    def picker(lines):
        lane = lines & (LANES - 1)
        same = (lines >> 7) == half_index

        def pick(plane):
            swapped = jnp.where(first_half, pltpu.roll(plane, 7, 0), pltpu.roll(plane, 1, 0))
            here = jnp.take_along_axis(plane, lane, axis=1, mode="promise_in_bounds")
            there = jnp.take_along_axis(swapped, lane, axis=1, mode="promise_in_bounds")
            return jnp.where(same, here, there)

        return pick

    pick_next = picker(next_line)
    pick_prev = picker(prev_line)

    tile = half_index * (LANES // LINES_DEV) + lane_index // LINES_DEV
    codes = []
    for end in range(2):
        plane = jnp.zeros(shape, jnp.int32)
        for k in range(2 * LANES // LINES_DEV):
            plane = jnp.where(tile == k, codes_ref[end, k], plane)
        codes.append(plane)

    def loaded(inst, cell):
        return [
            all_ref[inst, cell // 2, pl.ds((cell % 2) * CELL_ROWS + k * ROWS, ROWS), :]
            for k in range(PAIRS)
        ]

    def ghost(end, mirrored, copied):
        planes = []
        for k in range(PAIRS):
            reflected = mirrored[k]
            if k == 0:
                reflected = jnp.where(first_var, reflected, -reflected)
            inflow = jnp.where(first_var, FREE_STATE[2 * k], FREE_STATE[2 * k + 1])
            planes.append(
                jnp.where(
                    codes[end] == 0, reflected, jnp.where(codes[end] == 1, inflow, copied[k])
                )
            )
        return planes

    def extended_state(cell):
        if cell < 0:
            return ghost(0, loaded(own_inst, -1 - cell), loaded(own_inst, 0))
        if cell >= cells:
            return ghost(
                1, loaded(own_inst, 2 * cells - 1 - cell), loaded(own_inst, cells - 1)
            )
        return loaded(own_inst, cell)

    def both(plane):
        turned = pltpu.roll(plane, 4, 0)
        return jnp.where(first_var, plane, turned), jnp.where(first_var, turned, plane)

    def primitives(planes):
        density, moment_x = both(planes[0])
        moment_y, moment_z = both(planes[1])
        energy = jnp.where(first_var, planes[2], pltpu.roll(planes[2], 4, 0))
        inverse = 1.0 / density
        velocity_x = moment_x * inverse
        velocity_y = moment_y * inverse
        velocity_z = moment_z * inverse
        kinetic = moment_x * velocity_x + moment_y * velocity_y + moment_z * velocity_z
        pressure = (GAMMA_GAS - 1.0) * (energy - 0.5 * kinetic)
        sound = jnp.sqrt(GAMMA_GAS * pressure * inverse)
        return velocity_x, velocity_y, pressure, sound

    def flux_along(planes, velocity, pressure):
        return [
            planes[0] * velocity + jnp.where(first_var, 0.0, pressure),
            planes[1] * velocity,
            planes[2] * velocity + jnp.where(first_var, pressure * velocity, 0.0),
        ]

    def flux_across(planes, velocity, pressure):
        return [
            planes[0] * velocity,
            planes[1] * velocity + jnp.where(first_var, pressure, 0.0),
            planes[2] * velocity + jnp.where(first_var, pressure * velocity, 0.0),
        ]

    offsets = spectral_offsets()
    inst_count = all_ref.shape[0]

    def time_parts(cell, own):
        same_total = [None] * PAIRS
        other_total = [None] * PAIRS
        for shift in range(inst_count):
            planes = own if shift == 0 else loaded((own_inst - shift) & (inst_count - 1), cell)
            same = offsets[(2 * shift) % NT]
            other = jnp.where(
                first_inst, offsets[(2 * shift + 1) % NT], offsets[(2 * shift - 1) % NT]
            )
            for k in range(PAIRS):
                if shift > 0:
                    term = same * planes[k]
                    same_total[k] = term if same_total[k] is None else same_total[k] + term
                term = other * planes[k]
                other_total[k] = term if other_total[k] is None else other_total[k] + term
        return [
            s + jnp.where(first_inst, pltpu.roll(o, 6, 0), pltpu.roll(o, 2, 0))
            for s, o in zip(same_total, other_total)
        ]

    def pitch_flux(planes, velocity_y, pressure, sound):
        nearby = [pick_next(plane) for plane in planes]
        _, next_velocity, next_pressure, next_sound = primitives(nearby)
        own_flux = flux_across(planes, velocity_y, pressure)
        next_flux = flux_across(nearby, next_velocity, next_pressure)
        weight = (PITCH_GAIN * 0.5) * (
            jnp.abs(velocity_y) + sound + (jnp.abs(next_velocity) + next_sound)
        )
        return [
            0.5 * (a + b) - weight * (n - o)
            for a, b, n, o in zip(own_flux, next_flux, nearby, planes)
        ]

    state, pressures, radii, fluxes, steps, rest, sensors, faces = {}, {}, {}, {}, {}, {}, {}, {}
    for cell in range(-2, cells + 2):
        planes = extended_state(cell)
        velocity_x, velocity_y, pressure, sound = primitives(planes)
        state[cell] = planes
        pressures[cell] = pressure
        radii[cell] = jnp.abs(velocity_x) + sound
        if -1 <= cell <= cells:
            fluxes[cell] = flux_along(planes, velocity_x, pressure)
        if cell >= -1:
            steps[cell - 1] = [a - b for a, b in zip(planes, state[cell - 1])]
        if 0 <= cell < cells:
            faces_across = pitch_flux(planes, velocity_y, pressure, sound)
            rest[cell] = [
                t + (f - pick_prev(f)) for f, t in zip(faces_across, time_parts(cell, planes))
            ]
        if cell >= 0:
            twice = 2.0 * pressures[cell - 1]
            outer = pressure + pressures[cell - 2]
            sensors[cell - 1] = jnp.abs(outer - twice) / (outer + twice)
        if cell >= 1:
            face = cell - 2
            second = SENSOR_GAIN * jnp.maximum(sensors[face], sensors[face + 1])
            fourth = jnp.maximum(0.0, FOURTH_GAIN - second)
            face_radius = 0.5 * (radii[face] + radii[face + 1])
            near_weight = face_radius * (second + 2.0 * fourth)
            far_weight = face_radius * fourth
            faces[face] = [
                0.5 * (fluxes[face][k] + fluxes[face + 1][k])
                - (
                    near_weight * steps[face][k]
                    - far_weight * (steps[face + 1][k] + steps[face - 1][k])
                )
                for k in range(PAIRS)
            ]
        if cell >= 2:
            at = cell - 2
            slot, member = at // 2 + 1, at % 2
            for k in range(PAIRS):
                side_ref[slot, member * PAIRS + k] = (
                    faces[at - 1][k] - faces[at][k] - rest[at][k]
                )
            below = radii[at - 1] if at > 0 else zero
            centre = radii[at]
            above = radii[at + 1] if at < cells - 1 else zero
            below_sum = below + centre
            above_sum = centre + above
            half_low = SECOND_IMPL * 0.5 + 2.0 * FOURTH_IMPL
            rate_rows = [
                all_ref[own_inst, at // 2, pl.ds(2 * CELL_ROWS + member * 2 + half, 1), :]
                for half in range(2)
            ]
            rate = jnp.where(first_half, rate_rows[0], rate_rows[1])
            middle = (
                rate * centre
                + SECOND_IMPL * (0.5 * (below_sum + above_sum))
                + FOURTH_IMPL * (below + 4.0 * centre + above)
            )
            far_low = FOURTH_IMPL * below if at >= 2 else zero
            near_low = -half_low * below_sum if at >= 1 else zero
            near_high = -half_low * above_sum if at <= cells - 2 else zero
            far_high = FOURTH_IMPL * above if at <= cells - 3 else zero
            if member == 0:
                entries = {0: far_low, 1: near_low, 3: middle, 4: near_high, 7: far_high}
            else:
                entries = {2: far_low, 5: near_low, 6: middle, 8: near_high, 9: far_high}
            for k, plane in entries.items():
                coef_ref[slot, k] = plane

    blocks = cells // 2
    one = zero + 1.0
    for slot in (0, blocks + 1):
        for k in range(10):
            coef_ref[slot, k] = one if k in (3, 6) else zero
        for k in range(2 * PAIRS):
            side_ref[slot, k] = zero
    for slot in (0, blocks // 2 + 1):
        for k in range(12):
            coef2_ref[slot, k] = one if k in (4, 7) else zero
        for k in range(2 * PAIRS):
            side2_ref[slot, k] = zero

    def block_one(slot):
        c = [coef_ref[slot, k] for k in range(10)]
        return (
            (c[0], c[1], None, c[2]),
            (c[3], c[4], c[5], c[6]),
            (c[7], None, c[8], c[9]),
            [side_ref[slot, k] for k in range(2 * PAIRS)],
        )

    def block_two(slot):
        c = [coef2_ref[slot, k] for k in range(12)]
        return (
            tuple(c[0:4]),
            tuple(c[4:8]),
            tuple(c[8:12]),
            [side2_ref[slot, k] for k in range(2 * PAIRS)],
        )

    parity = own_cell & 1
    left = block_one(parity)
    left_inverse = inverse_of(left[1])
    for k in range(blocks // 2):
        right = block_one(parity + 2 * k + 2)
        right_inverse = inverse_of(right[1])
        kept = block_one(parity + 2 * k + 1)
        sub, diag, sup, side = eliminate(kept, left, left_inverse, right, right_inverse)
        for n, plane in enumerate(sub + diag + sup):
            coef2_ref[k + 1, n] = plane
        for n, plane in enumerate(side):
            side2_ref[k + 1, n] = plane
        left, left_inverse = right, right_inverse
    parity = (own_cell >> 1) & 1
    left = block_two(parity)
    left_inverse = inverse_of(left[1])
    for k in range(blocks // 4):
        right = block_two(parity + 2 * k + 2)
        right_inverse = inverse_of(right[1])
        kept = block_two(parity + 2 * k + 1)
        sub, diag, sup, side = eliminate(kept, left, left_inverse, right, right_inverse)
        for n in range(4):
            couple_ref[k, 0, n] = sub[n]
            couple_ref[k, 1, n] = sup[n]
            diag3_ref[k, n] = diag[n]
        for n, plane in enumerate(side):
            side3_ref[k, n] = plane
        left, left_inverse = right, right_inverse
    own = (own_cell >> 2) & 1
    other = 1 - own
    own_couple = tuple(couple_ref[own, 1 - own, n] for n in range(4))
    other_couple = tuple(couple_ref[other, own, n] for n in range(4))
    factor = two_by_two(own_couple, inverse_of([diag3_ref[other, n] for n in range(4)]))
    diag = less([diag3_ref[own, n] for n in range(4)], two_by_two(factor, other_couple))
    last_inverse = inverse_of(diag)
    for k in range(PAIRS):
        other_low, other_high = side3_ref[other, k], side3_ref[other, PAIRS + k]
        low = side3_ref[own, k] - (factor[0] * other_low + factor[1] * other_high)
        high = side3_ref[own, PAIRS + k] - (factor[2] * other_low + factor[3] * other_high)
        for member in range(2):
            delta = last_inverse[2 * member] * low + last_inverse[2 * member + 1] * high
            base = all_ref[own_inst, own_cell, pl.ds(member * CELL_ROWS + k * ROWS, ROWS), :]
            result = base + delta
            for var in range(2):
                for inst in range(2):
                    for half in range(2):
                        row = var * 4 + inst * 2 + half
                        out_ref[
                            inst, 2 * k + var, pl.ds(member, 1), pl.ds(half * LANES, LANES)
                        ] = result[row : row + 1]


def local_by_gather(state, pseudo_rate, line_next, face_codes):
    inst_count = lax.axis_size("inst")
    cell_count = lax.axis_size("cell")
    cells = cell_count * state.shape[2]
    vmem = pl.BlockSpec(memory_space=pltpu.VMEM)
    packed = pl.pallas_call(
        pack_kernel,
        out_shape=jax.ShapeDtypeStruct((BLOCK_ROWS, LANES), jnp.float32),
        in_specs=[vmem, vmem],
        out_specs=vmem,
    )(state, pseudo_rate)
    gathered = lax.all_gather(packed, ("inst", "cell"), axis=0, tiled=False)
    gathered = gathered.reshape(inst_count, cell_count, BLOCK_ROWS, LANES)
    blocks = cells // 2
    plane = (ROWS, LANES)
    sizes = [
        (blocks + 2, 10),
        (blocks + 2, 2 * PAIRS),
        (blocks // 2 + 2, 12),
        (blocks // 2 + 2, 2 * PAIRS),
        (2, 2, 4),
        (2, 4),
        (2, 2 * PAIRS),
    ]
    return pl.pallas_call(
        functools.partial(line_kernel, cells),
        out_shape=jax.ShapeDtypeStruct(state.shape, jnp.float32),
        in_specs=[vmem, vmem, pl.BlockSpec(memory_space=pltpu.SMEM)],
        out_specs=vmem,
        scratch_shapes=[pltpu.VMEM(size + plane, jnp.float32) for size in sizes],
    )(gathered, line_next.reshape(2, LANES), face_codes)


def solution(mesh):
    placed = (P("inst", None, "cell", None), P("cell", None), P(), P())
    inst_count, cell_count = mesh.shape["inst"], mesh.shape["cell"]

    def local(state, pseudo_rate, line_next, face_codes):
        small = (
            state.shape == (2, 6, 2, 2 * LANES)
            and inst_count * 2 == NT
            and cell_count == 8
            and face_codes.shape[1] * LINES_DEV == state.shape[3]
        )
        chosen = local_by_gather if small else local_by_lines
        return chosen(state, pseudo_rate, line_next, face_codes)

    return jax.shard_map(
        local, mesh=mesh, in_specs=placed, out_specs=P("inst", None, "cell", None), check_vma=False
    )
```

```python
import functools

import jax
import jax.numpy as jnp
import numpy as np
from jax import lax
from jax.experimental import pallas as pl
from jax.experimental.pallas import tpu as pltpu
from jax.sharding import PartitionSpec as P

NT = 8
LINES_DEV = 32


GAMMA_GAS = 1.4
OMEGA_BLADE = 1.0
SENSOR_GAIN = 0.25
FOURTH_GAIN = 0.03125
PITCH_GAIN = 0.5
SECOND_IMPL = 1.0
FOURTH_IMPL = 0.25
FREE_STATE = (1.0, 0.5, 0.0, 0.0, 2.625, 0.2)
MIRROR_SIGNS = (1.0, -1.0, 1.0, 1.0, 1.0, 1.0)
ZERO_BLOCK = (0.0, 0.0, 0.0, 0.0)
UNIT_BLOCK = (1.0, 0.0, 0.0, 1.0)
ZERO_PAIR = (0.0, 0.0)


def extended(block, sides, width):
    for axis, dim in sides:
        count = lax.axis_size(axis)
        forward = [(i, i + 1) for i in range(count - 1)]
        backward = [(target, source) for source, target in forward]
        low = lax.ppermute(
            lax.slice_in_dim(block, block.shape[dim] - width, None, axis=dim), axis, forward
        )
        high = lax.ppermute(lax.slice_in_dim(block, 0, width, axis=dim), axis, backward)
        block = jnp.concatenate([low, block, high], axis=dim)
    return block


def spectral_matrix(instances):
    offsets = np.arange(instances)[:, None] - np.arange(instances)[None, :]
    angles = np.pi * offsets / instances
    safe_sin = np.where(offsets == 0, 1.0, np.sin(angles))
    parity = np.where(np.mod(offsets, 2) == 0, -1.0, 1.0)
    matrix_table = np.where(
        offsets == 0, 0.0, 0.5 * OMEGA_BLADE * parity * np.cos(angles) / safe_sin
    )
    return jnp.asarray(matrix_table, jnp.float32)


def primitive_parts(cells_state):
    density = cells_state[..., 0, :, :]
    inverse = 1.0 / density
    velocity_x = cells_state[..., 1, :, :] * inverse
    velocity_y = cells_state[..., 2, :, :] * inverse
    velocity_z = cells_state[..., 3, :, :] * inverse
    energy = cells_state[..., 4, :, :]
    pressure = (GAMMA_GAS - 1.0) * (
        energy
        - 0.5
        * density
        * (velocity_x * velocity_x + velocity_y * velocity_y + velocity_z * velocity_z)
    )
    sound_speed = jnp.sqrt(GAMMA_GAS * pressure * inverse)
    return (velocity_x, velocity_y, pressure, sound_speed)


def directed_flux(cells_state, normal_velocity, pressure, component):
    zero_plane = jnp.zeros_like(pressure)
    pressure_rows = [
        zero_plane,
        zero_plane,
        zero_plane,
        zero_plane,
        pressure * normal_velocity,
        zero_plane,
    ]
    pressure_rows[component] = pressure
    return cells_state * normal_velocity[..., None, :, :] + jnp.stack(pressure_rows, axis=-3)


def line_residual(padded):
    velocity_x, velocity_y, pressure, sound_speed = primitive_parts(padded)
    flux_line = directed_flux(padded, velocity_x, pressure, 1)
    radius = jnp.abs(velocity_x) + sound_speed
    sensor = jnp.abs(
        pressure[..., 2:, :] - 2.0 * pressure[..., 1:-1, :] + pressure[..., :-2, :]
    ) / (pressure[..., 2:, :] + 2.0 * pressure[..., 1:-1, :] + pressure[..., :-2, :])
    second = SENSOR_GAIN * jnp.maximum(sensor[..., :-1, :], sensor[..., 1:, :])
    fourth = jnp.maximum(0.0, FOURTH_GAIN - second)
    face_radius = 0.5 * (radius[..., 1:-2, :] + radius[..., 2:-1, :])
    left_far = padded[..., :-3, :]
    left_near = padded[..., 1:-2, :]
    right_near = padded[..., 2:-1, :]
    right_far = padded[..., 3:, :]
    damping = face_radius[..., None, :, :] * (
        second[..., None, :, :] * (right_near - left_near)
        - fourth[..., None, :, :] * (right_far - 3.0 * right_near + 3.0 * left_near - left_far)
    )
    face_flux = 0.5 * (flux_line[..., 1:-2, :] + flux_line[..., 2:-1, :]) - damping
    return (face_flux[..., 1:, :] - face_flux[..., :-1, :], radius)


def pitch_parts(cells_state):
    velocity_x, velocity_y, pressure, sound_speed = primitive_parts(cells_state)
    return (directed_flux(cells_state, velocity_y, pressure, 2), jnp.abs(velocity_y) + sound_speed)


def pitch_residual(cells_state, next_lines, prev_lines):
    pitch_flux, radius = pitch_parts(cells_state)
    state_next = jnp.take(cells_state, next_lines, axis=-1)
    flux_next, radius_next = pitch_parts(state_next)
    face_flux = 0.5 * (pitch_flux + flux_next) - PITCH_GAIN * (0.5 * (radius + radius_next))[
        ..., None, :, :
    ] * (state_next - cells_state)
    return face_flux - jnp.take(face_flux, prev_lines, axis=-1)


def boundary_cells(edge_pair, line_codes, lower_end):
    reflected = edge_pair[..., ::-1, :] * jnp.asarray(MIRROR_SIGNS, jnp.float32)[:, None, None]
    if lower_end:
        copied = jnp.concatenate([edge_pair[..., :1, :], edge_pair[..., :1, :]], axis=-2)
    else:
        copied = jnp.concatenate([edge_pair[..., 1:, :], edge_pair[..., 1:, :]], axis=-2)
    inflow = jnp.asarray(FREE_STATE, jnp.float32)[:, None, None] + jnp.zeros_like(edge_pair)
    return jnp.where(line_codes == 0, reflected, jnp.where(line_codes == 1, inflow, copied))


def line_coefficients(radius_ext, diagonal_term, positions, total_cells):
    radius_below = radius_ext[..., :-2, :]
    radius_centre = radius_ext[..., 1:-1, :]
    radius_above = radius_ext[..., 2:, :]
    face_below = 0.5 * (radius_below + radius_centre)
    face_above = 0.5 * (radius_centre + radius_above)
    far_low = FOURTH_IMPL * radius_below
    near_low = -SECOND_IMPL * face_below - 2.0 * FOURTH_IMPL * (radius_below + radius_centre)
    middle = (
        diagonal_term
        + SECOND_IMPL * (face_below + face_above)
        + FOURTH_IMPL * (radius_below + 4.0 * radius_centre + radius_above)
    )
    near_high = -SECOND_IMPL * face_above - 2.0 * FOURTH_IMPL * (radius_centre + radius_above)
    far_high = FOURTH_IMPL * radius_above
    column = positions[:, None]
    far_low = jnp.where(column >= 2, far_low, 0.0)
    near_low = jnp.where(column >= 1, near_low, 0.0)
    near_high = jnp.where(column <= total_cells - 2, near_high, 0.0)
    far_high = jnp.where(column <= total_cells - 3, far_high, 0.0)
    return (far_low, near_low, middle, near_high, far_high)


def block_product(first_matrix, second_matrix):
    return (
        first_matrix[0] * second_matrix[0] + first_matrix[1] * second_matrix[2],
        first_matrix[0] * second_matrix[1] + first_matrix[1] * second_matrix[3],
        first_matrix[2] * second_matrix[0] + first_matrix[3] * second_matrix[2],
        first_matrix[2] * second_matrix[1] + first_matrix[3] * second_matrix[3],
    )


def block_inverse(matrix):
    determinant = matrix[0] * matrix[3] - matrix[1] * matrix[2]
    reciprocal = 1.0 / determinant
    return (
        matrix[3] * reciprocal,
        -matrix[1] * reciprocal,
        -matrix[2] * reciprocal,
        matrix[0] * reciprocal,
    )


def block_apply(matrix, vector):
    return (
        matrix[0] * vector[0] + matrix[1] * vector[1],
        matrix[2] * vector[0] + matrix[3] * vector[1],
    )


def add_blocks(first_members, second_members):
    return tuple((a + b for a, b in zip(first_members, second_members)))


def negate(members):
    return tuple((-a for a in members))


def extend_blocks(members, fill_values):
    return tuple(
        (
            jnp.concatenate([m, jnp.full_like(m[..., :1, :], f)], axis=-2)
            for m, f in zip(members, fill_values)
        )
    )


def shift_next(members, fill_values):
    return tuple(
        (
            jnp.concatenate([m[..., 1:, :], jnp.full_like(m[..., :1, :], f)], axis=-2)
            for m, f in zip(members, fill_values)
        )
    )


def shift_prev(members):
    return tuple(
        (jnp.concatenate([jnp.zeros_like(m[..., :1, :]), m[..., :-1, :]], axis=-2) for m in members)
    )


def pair_split(member):
    shaped = member.reshape(member.shape[:-2] + (member.shape[-2] // 2, 2, member.shape[-1]))
    return (shaped[..., 0, :], shaped[..., 1, :])


def split_parity(members):
    halves = [pair_split(m) for m in members]
    return (tuple((h[0] for h in halves)), tuple((h[1] for h in halves)))


def alternate(first_member, second_member):
    stacked = jnp.stack((first_member, second_member), axis=-2)
    return stacked.reshape(
        first_member.shape[:-2] + (2 * first_member.shape[-2], first_member.shape[-1])
    )


def reduce_blocks(sub_blocks, diag_blocks, super_blocks, right_side):
    block_count = diag_blocks[0].shape[-2]
    if block_count == 1:
        return block_apply(block_inverse(diag_blocks), right_side)
    if block_count % 2 == 1:
        sub_blocks = extend_blocks(sub_blocks, ZERO_BLOCK)
        diag_blocks = extend_blocks(diag_blocks, UNIT_BLOCK)
        super_blocks = extend_blocks(super_blocks, ZERO_BLOCK)
        right_side = extend_blocks(right_side, ZERO_PAIR)
    sub_even, sub_odd = split_parity(sub_blocks)
    diag_even, diag_odd = split_parity(diag_blocks)
    super_even, super_odd = split_parity(super_blocks)
    side_even, side_odd = split_parity(right_side)
    inverse_even = block_inverse(diag_even)
    inverse_next = shift_next(inverse_even, UNIT_BLOCK)
    sub_next = shift_next(sub_even, ZERO_BLOCK)
    super_next = shift_next(super_even, ZERO_BLOCK)
    side_next = shift_next(side_even, ZERO_PAIR)
    left_factor = negate(block_product(sub_odd, inverse_even))
    right_factor = negate(block_product(super_odd, inverse_next))
    reduced_sub = block_product(left_factor, sub_even)
    reduced_diag = add_blocks(
        diag_odd,
        add_blocks(block_product(left_factor, super_even), block_product(right_factor, sub_next)),
    )
    reduced_super = block_product(right_factor, super_next)
    reduced_side = add_blocks(
        side_odd,
        add_blocks(block_apply(left_factor, side_even), block_apply(right_factor, side_next)),
    )
    odd_values = reduce_blocks(reduced_sub, reduced_diag, reduced_super, reduced_side)
    before_values = shift_prev(odd_values)
    remainder = add_blocks(
        side_even,
        negate(
            add_blocks(block_apply(sub_even, before_values), block_apply(super_even, odd_values))
        ),
    )
    even_values = block_apply(inverse_even, remainder)
    merged = tuple((alternate(e, o) for e, o in zip(even_values, odd_values)))
    return tuple((m[..., :block_count, :] for m in merged))


def cells_leading(block):
    moved = jnp.transpose(block, (2, 0, 1, 3))
    return moved.reshape(block.shape[2], block.shape[0] * block.shape[1] * block.shape[3])


def solve_in_lanes(coefficients, line_source):
    source_shape = line_source.shape
    lane_coef = [cells_leading(jnp.broadcast_to(c[:, None], source_shape)) for c in coefficients]
    pairs_list = [pair_split(m) for m in lane_coef]
    zero_plane = jnp.zeros_like(pairs_list[2][0])
    sub_blocks = (pairs_list[0][0], pairs_list[1][0], zero_plane, pairs_list[0][1])
    diag_blocks = (pairs_list[2][0], pairs_list[3][0], pairs_list[1][1], pairs_list[2][1])
    super_blocks = (pairs_list[4][0], zero_plane, pairs_list[3][1], pairs_list[4][1])
    values = reduce_blocks(
        sub_blocks, diag_blocks, super_blocks, pair_split(cells_leading(line_source))
    )
    flat = alternate(values[0], values[1])
    shaped = flat.reshape(source_shape[2], source_shape[0], source_shape[1], source_shape[3])
    return jnp.transpose(shaped, (1, 2, 0, 3))


def return_tiles(line_values):
    return lax.all_to_all(line_values, "cell", split_axis=2, concat_axis=3, tiled=True)


def local_by_lines(state, pseudo_rate, line_next, face_codes):
    local_count = state.shape[0]
    tile_cells = state.shape[2]
    cell_index = lax.axis_index("cell")
    cell_count = lax.axis_size("cell")
    total_cells = tile_cells * cell_count
    spectral = spectral_matrix(NT)
    first_local = lax.axis_index("inst") * local_count
    own_rows = lax.dynamic_slice_in_dim(spectral, first_local, local_count, 0)
    shard_block = jax.tree.map(lambda a: lax.all_gather(a, "inst", axis=0, tiled=True), state)
    columns = lax.slice_in_dim(own_rows, 0, shard_block.shape[0], axis=1)
    time_term = jnp.zeros_like(state) + jnp.einsum(
        "nm,mvil->nvil", columns, shard_block, precision=lax.Precision.HIGHEST
    )
    padded = extended(state, (("cell", 2),), 2)
    codes_lines = jnp.repeat(face_codes, LINES_DEV, axis=1)
    lower_ghost = boundary_cells(state[:, :, 0:2, :], codes_lines[0], True)
    upper_ghost = boundary_cells(state[:, :, -2:, :], codes_lines[1], False)
    lower_rim = jnp.where(cell_index == 0, lower_ghost, padded[:, :, :2, :])
    upper_rim = jnp.where(cell_index == cell_count - 1, upper_ghost, padded[:, :, -2:, :])
    padded = jnp.concatenate([lower_rim, padded[:, :, 2:-2, :], upper_rim], axis=2)
    line_part, radius = line_residual(padded)
    prev_lines = (
        jnp.zeros_like(line_next).at[line_next].set(jnp.arange(line_next.shape[0], dtype=jnp.int32))
    )
    residual = line_part + pitch_residual(state, line_next, prev_lines) + time_term
    right_side = -residual
    centre_radius = radius[:, 2:-2, :]
    diagonal_term = pseudo_rate * centre_radius
    positions = cell_index * tile_cells + jnp.arange(-1, tile_cells + 1, dtype=jnp.int32)
    inside = (positions >= 0) & (positions < total_cells)
    radius_ext = jnp.where(inside[:, None], radius[:, 1:-1, :], 0.0)
    coefficients = line_coefficients(radius_ext, diagonal_term, positions[1:-1], total_cells)
    stacked = jnp.stack(coefficients, axis=1)
    line_source = lax.all_to_all(right_side, "cell", split_axis=3, concat_axis=2, tiled=True)
    line_coef = lax.all_to_all(stacked, "cell", split_axis=3, concat_axis=2, tiled=True)
    update = return_tiles(solve_in_lanes(tuple((line_coef[:, k] for k in range(5))), line_source))
    return state + update


LANES = 128
ROWS = 8
PAIRS = 3
CELL_ROWS = PAIRS * ROWS
REST_ROW = 2 * CELL_ROWS
RATE_ROW = 2 * REST_ROW
BLOCK_ROWS = RATE_ROW + ROWS


def spectral_offsets():
    table = np.zeros(NT)
    for offset in range(1, NT):
        angle = np.pi * offset / NT
        parity = -1.0 if offset % 2 == 0 else 1.0
        table[offset] = 0.5 * OMEGA_BLADE * parity * np.cos(angle) / np.sin(angle)
    return [float(np.float32(value)) for value in table]


def plane_masks():
    row_index = lax.broadcasted_iota(jnp.int32, (ROWS, LANES), 0)
    return row_index < 4, (row_index & 2) == 0, row_index & 1


def both(first_var, plane):
    turned = pltpu.roll(plane, 4, 0)
    return jnp.where(first_var, plane, turned), jnp.where(first_var, turned, plane)


def primitives(first_var, planes):
    density, moment_x = both(first_var, planes[0])
    moment_y, moment_z = both(first_var, planes[1])
    energy = jnp.where(first_var, planes[2], pltpu.roll(planes[2], 4, 0))
    inverse = 1.0 / density
    velocity_x = moment_x * inverse
    velocity_y = moment_y * inverse
    velocity_z = moment_z * inverse
    kinetic = moment_x * velocity_x + moment_y * velocity_y + moment_z * velocity_z
    pressure = (GAMMA_GAS - 1.0) * (energy - 0.5 * kinetic)
    sound = jnp.sqrt(GAMMA_GAS * pressure * inverse)
    return velocity_x, velocity_y, pressure, sound


def rows_of(var, inst, half):
    return (var // 2) * ROWS + (var % 2) * 4 + inst * 2 + half


def cell_kernel(all_ref, rate_ref, next_ref, out_ref, plane_ref):
    own_inst = lax.axis_index("inst")
    inst_count = all_ref.shape[0] // 2
    shape = (ROWS, LANES)
    lane_index = lax.broadcasted_iota(jnp.int32, shape, 1)
    first_var, first_inst, half_index = plane_masks()
    first_half = half_index == 0

    next_rows = [next_ref[pl.ds(half, 1), :] for half in range(2)]
    next_line = jnp.where(first_half, next_rows[0], next_rows[1])
    column = lax.broadcasted_iota(jnp.int32, (LANES, LANES), 0)
    prev_halves = []
    for target in range(2):
        total = None
        for source in range(2):
            hits = jnp.where(column + target * LANES == next_rows[source], 1.0, 0.0)
            names = (lane_index + source * LANES).astype(jnp.float32)
            part = lax.dot_general(
                names, hits, (((1,), (1,)), ((), ())), preferred_element_type=jnp.float32
            )
            total = part if total is None else total + part
        prev_halves.append(total)
    prev_line = jnp.where(first_half, prev_halves[0], prev_halves[1]).astype(jnp.int32)

    def picker(lines):
        lane = lines & (LANES - 1)
        same = (lines >> 7) == half_index

        def pick(plane):
            swapped = jnp.where(first_half, pltpu.roll(plane, 7, 0), pltpu.roll(plane, 1, 0))
            here = jnp.take_along_axis(plane, lane, axis=1, mode="promise_in_bounds")
            there = jnp.take_along_axis(swapped, lane, axis=1, mode="promise_in_bounds")
            return jnp.where(same, here, there)

        return pick

    pick_next = picker(next_line)
    pick_prev = picker(prev_line)

    for shift in range(inst_count):
        pair = (own_inst - shift) & (inst_count - 1)
        for cell in range(2):
            for var in range(6):
                for inst in range(2):
                    for half in range(2):
                        row = cell * CELL_ROWS + rows_of(var, inst, half)
                        plane_ref[shift, pl.ds(row, 1), :] = all_ref[
                            2 * pair + inst, var, pl.ds(cell, 1), pl.ds(half * LANES, LANES)
                        ]
    offsets = spectral_offsets()

    def time_parts(cell):
        same_total = [None] * PAIRS
        other_total = [None] * PAIRS
        for shift in range(inst_count):
            same = offsets[(2 * shift) % NT]
            other = jnp.where(
                first_inst, offsets[(2 * shift + 1) % NT], offsets[(2 * shift - 1) % NT]
            )
            for k in range(PAIRS):
                plane = plane_ref[shift, pl.ds(cell * CELL_ROWS + k * ROWS, ROWS), :]
                if shift > 0:
                    term = same * plane
                    same_total[k] = term if same_total[k] is None else same_total[k] + term
                term = other * plane
                other_total[k] = term if other_total[k] is None else other_total[k] + term
        return [
            s + jnp.where(first_inst, pltpu.roll(o, 6, 0), pltpu.roll(o, 2, 0))
            for s, o in zip(same_total, other_total)
        ]

    def flux_across(planes, velocity, pressure):
        return [
            planes[0] * velocity,
            planes[1] * velocity + jnp.where(first_var, pressure, 0.0),
            planes[2] * velocity + jnp.where(first_var, pressure * velocity, 0.0),
        ]

    for cell in range(2):
        planes = [
            plane_ref[0, pl.ds(cell * CELL_ROWS + k * ROWS, ROWS), :] for k in range(PAIRS)
        ]
        nearby = [pick_next(plane) for plane in planes]
        _, velocity, pressure, sound = primitives(first_var, planes)
        _, next_velocity, next_pressure, next_sound = primitives(first_var, nearby)
        own_flux = flux_across(planes, velocity, pressure)
        next_flux = flux_across(nearby, next_velocity, next_pressure)
        weight = (PITCH_GAIN * 0.5) * (
            jnp.abs(velocity) + sound + (jnp.abs(next_velocity) + next_sound)
        )
        time_term = time_parts(cell)
        for k in range(PAIRS):
            face = 0.5 * (own_flux[k] + next_flux[k]) - weight * (nearby[k] - planes[k])
            rest = time_term[k] + (face - pick_prev(face))
            row = cell * CELL_ROWS + k * ROWS
            out_ref[pl.ds(row, ROWS), :] = planes[k]
            out_ref[pl.ds(REST_ROW + row, ROWS), :] = rest
        for half in range(2):
            out_ref[pl.ds(RATE_ROW + cell * 2 + half, 1), :] = rate_ref[
                pl.ds(cell, 1), pl.ds(half * LANES, LANES)
            ]
    out_ref[pl.ds(RATE_ROW + 4, 4), :] = jnp.zeros((4, LANES), jnp.float32)


def two_by_two(first, second):
    def entry(a, b, c, d):
        terms = [x * y for x, y in ((a, b), (c, d)) if x is not None and y is not None]
        return None if not terms else terms[0] if len(terms) == 1 else terms[0] + terms[1]

    return (
        entry(first[0], second[0], first[1], second[2]),
        entry(first[0], second[1], first[1], second[3]),
        entry(first[2], second[0], first[3], second[2]),
        entry(first[2], second[1], first[3], second[3]),
    )


def inverse_of(matrix):
    reciprocal = 1.0 / (matrix[0] * matrix[3] - matrix[1] * matrix[2])
    return (
        matrix[3] * reciprocal,
        -(matrix[1] * reciprocal),
        -(matrix[2] * reciprocal),
        matrix[0] * reciprocal,
    )


def less(first, second):
    return tuple(a if b is None else a - b for a, b in zip(first, second))


def minus(members):
    return tuple(None if a is None else -a for a in members)


def eliminate(centre, left, left_inverse, right, right_inverse):
    left_factor = two_by_two(centre[0], left_inverse)
    right_factor = two_by_two(centre[2], right_inverse)
    sub = minus(two_by_two(left_factor, left[0]))
    diag = less(
        less(centre[1], two_by_two(left_factor, left[2])), two_by_two(right_factor, right[0])
    )
    sup = minus(two_by_two(right_factor, right[2]))
    side = []
    for k in range(PAIRS):
        for row in range(2):
            value = centre[3][row * PAIRS + k]
            for factor, other in ((left_factor, left[3]), (right_factor, right[3])):
                value = value - (
                    factor[2 * row] * other[k] + factor[2 * row + 1] * other[PAIRS + k]
                )
            side.append((row * PAIRS + k, value))
    return sub, diag, sup, [value for _, value in sorted(side, key=lambda item: item[0])]


def line_kernel(
    cells, all_ref, codes_ref, out_ref, coef_ref, side_ref, coef2_ref, side2_ref,
    couple_ref, diag3_ref, side3_ref,
):
    own_cell = lax.axis_index("cell")
    shape = (ROWS, LANES)
    lane_index = lax.broadcasted_iota(jnp.int32, shape, 1)
    first_var, _, half_index = plane_masks()
    first_half = half_index == 0
    zero = jnp.zeros(shape, jnp.float32)

    tile = half_index * (LANES // LINES_DEV) + lane_index // LINES_DEV
    codes = []
    for end in range(2):
        plane = jnp.zeros(shape, jnp.int32)
        for k in range(2 * LANES // LINES_DEV):
            plane = jnp.where(tile == k, codes_ref[end, k], plane)
        codes.append(plane)

    def loaded(cell, start=0):
        return [
            all_ref[cell // 2, pl.ds(start + (cell % 2) * CELL_ROWS + k * ROWS, ROWS), :]
            for k in range(PAIRS)
        ]

    def ghost(end, mirrored, copied):
        planes = []
        for k in range(PAIRS):
            reflected = mirrored[k]
            if k == 0:
                reflected = jnp.where(first_var, reflected, -reflected)
            inflow = jnp.where(first_var, FREE_STATE[2 * k], FREE_STATE[2 * k + 1])
            planes.append(
                jnp.where(
                    codes[end] == 0, reflected, jnp.where(codes[end] == 1, inflow, copied[k])
                )
            )
        return planes

    def extended_state(cell):
        if cell < 0:
            return ghost(0, loaded(-1 - cell), loaded(0))
        if cell >= cells:
            return ghost(
                1, loaded(2 * cells - 1 - cell), loaded(cells - 1)
            )
        return loaded(cell)

    def flux_along(planes, velocity, pressure):
        return [
            planes[0] * velocity + jnp.where(first_var, 0.0, pressure),
            planes[1] * velocity,
            planes[2] * velocity + jnp.where(first_var, pressure * velocity, 0.0),
        ]

    state, pressures, radii, fluxes, steps, sensors, faces = {}, {}, {}, {}, {}, {}, {}
    for cell in range(-2, cells + 2):
        planes = extended_state(cell)
        velocity_x, _, pressure, sound = primitives(first_var, planes)
        state[cell] = planes
        pressures[cell] = pressure
        radii[cell] = jnp.abs(velocity_x) + sound
        if -1 <= cell <= cells:
            fluxes[cell] = flux_along(planes, velocity_x, pressure)
        if cell >= -1:
            steps[cell - 1] = [a - b for a, b in zip(planes, state[cell - 1])]
        if cell >= 0:
            twice = 2.0 * pressures[cell - 1]
            outer = pressure + pressures[cell - 2]
            sensors[cell - 1] = jnp.abs(outer - twice) / (outer + twice)
        if cell >= 1:
            face = cell - 2
            second = SENSOR_GAIN * jnp.maximum(sensors[face], sensors[face + 1])
            fourth = jnp.maximum(0.0, FOURTH_GAIN - second)
            face_radius = 0.5 * (radii[face] + radii[face + 1])
            near_weight = face_radius * (second + 2.0 * fourth)
            far_weight = face_radius * fourth
            faces[face] = [
                0.5 * (fluxes[face][k] + fluxes[face + 1][k])
                - (
                    near_weight * steps[face][k]
                    - far_weight * (steps[face + 1][k] + steps[face - 1][k])
                )
                for k in range(PAIRS)
            ]
        if cell >= 2:
            at = cell - 2
            slot, member = at // 2 + 1, at % 2
            rest = loaded(at, REST_ROW)
            for k in range(PAIRS):
                side_ref[slot, member * PAIRS + k] = (
                    faces[at - 1][k] - faces[at][k] - rest[k]
                )
            below = radii[at - 1] if at > 0 else zero
            centre = radii[at]
            above = radii[at + 1] if at < cells - 1 else zero
            below_sum = below + centre
            above_sum = centre + above
            half_low = SECOND_IMPL * 0.5 + 2.0 * FOURTH_IMPL
            rate_rows = [
                all_ref[at // 2, pl.ds(RATE_ROW + member * 2 + half, 1), :]
                for half in range(2)
            ]
            rate = jnp.where(first_half, rate_rows[0], rate_rows[1])
            middle = (
                rate * centre
                + SECOND_IMPL * (0.5 * (below_sum + above_sum))
                + FOURTH_IMPL * (below + 4.0 * centre + above)
            )
            far_low = FOURTH_IMPL * below if at >= 2 else zero
            near_low = -half_low * below_sum if at >= 1 else zero
            near_high = -half_low * above_sum if at <= cells - 2 else zero
            far_high = FOURTH_IMPL * above if at <= cells - 3 else zero
            if member == 0:
                entries = {0: far_low, 1: near_low, 3: middle, 4: near_high, 7: far_high}
            else:
                entries = {2: far_low, 5: near_low, 6: middle, 8: near_high, 9: far_high}
            for k, plane in entries.items():
                coef_ref[slot, k] = plane

    blocks = cells // 2
    one = zero + 1.0
    for slot in (0, blocks + 1):
        for k in range(10):
            coef_ref[slot, k] = one if k in (3, 6) else zero
        for k in range(2 * PAIRS):
            side_ref[slot, k] = zero
    for slot in (0, blocks // 2 + 1):
        for k in range(12):
            coef2_ref[slot, k] = one if k in (4, 7) else zero
        for k in range(2 * PAIRS):
            side2_ref[slot, k] = zero

    def block_one(slot):
        c = [coef_ref[slot, k] for k in range(10)]
        return (
            (c[0], c[1], None, c[2]),
            (c[3], c[4], c[5], c[6]),
            (c[7], None, c[8], c[9]),
            [side_ref[slot, k] for k in range(2 * PAIRS)],
        )

    def block_two(slot):
        c = [coef2_ref[slot, k] for k in range(12)]
        return (
            tuple(c[0:4]),
            tuple(c[4:8]),
            tuple(c[8:12]),
            [side2_ref[slot, k] for k in range(2 * PAIRS)],
        )

    parity = own_cell & 1
    left = block_one(parity)
    left_inverse = inverse_of(left[1])
    for k in range(blocks // 2):
        right = block_one(parity + 2 * k + 2)
        right_inverse = inverse_of(right[1])
        kept = block_one(parity + 2 * k + 1)
        sub, diag, sup, side = eliminate(kept, left, left_inverse, right, right_inverse)
        for n, plane in enumerate(sub + diag + sup):
            coef2_ref[k + 1, n] = plane
        for n, plane in enumerate(side):
            side2_ref[k + 1, n] = plane
        left, left_inverse = right, right_inverse
    parity = (own_cell >> 1) & 1
    left = block_two(parity)
    left_inverse = inverse_of(left[1])
    for k in range(blocks // 4):
        right = block_two(parity + 2 * k + 2)
        right_inverse = inverse_of(right[1])
        kept = block_two(parity + 2 * k + 1)
        sub, diag, sup, side = eliminate(kept, left, left_inverse, right, right_inverse)
        for n in range(4):
            couple_ref[k, 0, n] = sub[n]
            couple_ref[k, 1, n] = sup[n]
            diag3_ref[k, n] = diag[n]
        for n, plane in enumerate(side):
            side3_ref[k, n] = plane
        left, left_inverse = right, right_inverse
    own = (own_cell >> 2) & 1
    other = 1 - own
    own_couple = tuple(couple_ref[own, 1 - own, n] for n in range(4))
    other_couple = tuple(couple_ref[other, own, n] for n in range(4))
    factor = two_by_two(own_couple, inverse_of([diag3_ref[other, n] for n in range(4)]))
    diag = less([diag3_ref[own, n] for n in range(4)], two_by_two(factor, other_couple))
    last_inverse = inverse_of(diag)
    for k in range(PAIRS):
        other_low, other_high = side3_ref[other, k], side3_ref[other, PAIRS + k]
        low = side3_ref[own, k] - (factor[0] * other_low + factor[1] * other_high)
        high = side3_ref[own, PAIRS + k] - (factor[2] * other_low + factor[3] * other_high)
        for member in range(2):
            delta = last_inverse[2 * member] * low + last_inverse[2 * member + 1] * high
            base = all_ref[own_cell, pl.ds(member * CELL_ROWS + k * ROWS, ROWS), :]
            result = base + delta
            for var in range(2):
                for inst in range(2):
                    for half in range(2):
                        row = rows_of(var, inst, half)
                        out_ref[
                            inst, 2 * k + var, pl.ds(member, 1), pl.ds(half * LANES, LANES)
                        ] = result[row : row + 1]


def gather_inst(block):
    return lax.all_gather(block, "inst", axis=0, tiled=True)


def gather_cell(block):
    return lax.all_gather(block, "cell", axis=0, tiled=False)


def local_by_gather(state, pseudo_rate, line_next, face_codes):
    cells = lax.axis_size("cell") * state.shape[2]
    vmem = pl.BlockSpec(memory_space=pltpu.VMEM)
    plane = (ROWS, LANES)
    every = gather_inst(state)
    packed = pl.pallas_call(
        cell_kernel,
        out_shape=jax.ShapeDtypeStruct((BLOCK_ROWS, LANES), jnp.float32),
        in_specs=[vmem, vmem, vmem],
        out_specs=vmem,
        scratch_shapes=[
            pltpu.VMEM((every.shape[0] // 2, 2 * CELL_ROWS, LANES), jnp.float32)
        ],
    )(every, pseudo_rate, line_next.reshape(2, LANES))
    gathered = gather_cell(packed)
    blocks = cells // 2
    sizes = [
        (blocks + 2, 10),
        (blocks + 2, 2 * PAIRS),
        (blocks // 2 + 2, 12),
        (blocks // 2 + 2, 2 * PAIRS),
        (2, 2, 4),
        (2, 4),
        (2, 2 * PAIRS),
    ]
    return pl.pallas_call(
        functools.partial(line_kernel, cells),
        out_shape=jax.ShapeDtypeStruct(state.shape, jnp.float32),
        in_specs=[vmem, pl.BlockSpec(memory_space=pltpu.SMEM)],
        out_specs=vmem,
        scratch_shapes=[pltpu.VMEM(size + plane, jnp.float32) for size in sizes],
    )(gathered, face_codes)


def solution(mesh):
    placed = (P("inst", None, "cell", None), P("cell", None), P(), P())
    inst_count, cell_count = mesh.shape["inst"], mesh.shape["cell"]

    def local(state, pseudo_rate, line_next, face_codes):
        small = (
            state.shape == (2, 6, 2, 2 * LANES)
            and inst_count * 2 == NT
            and cell_count == 8
            and face_codes.shape[1] * LINES_DEV == state.shape[3]
        )
        chosen = local_by_gather if small else local_by_lines
        return chosen(state, pseudo_rate, line_next, face_codes)

    return jax.shard_map(
        local, mesh=mesh, in_specs=placed, out_specs=P("inst", None, "cell", None), check_vma=False
    )
```

```python
import functools

import jax
import jax.numpy as jnp
import numpy as np
from jax import lax
from jax.experimental import pallas as pl
from jax.experimental.pallas import tpu as pltpu
from jax.sharding import PartitionSpec as P

NT = 8
LINES_DEV = 32


GAMMA_GAS = 1.4
OMEGA_BLADE = 1.0
SENSOR_GAIN = 0.25
FOURTH_GAIN = 0.03125
PITCH_GAIN = 0.5
SECOND_IMPL = 1.0
FOURTH_IMPL = 0.25
FREE_STATE = (1.0, 0.5, 0.0, 0.0, 2.625, 0.2)
MIRROR_SIGNS = (1.0, -1.0, 1.0, 1.0, 1.0, 1.0)
ZERO_BLOCK = (0.0, 0.0, 0.0, 0.0)
UNIT_BLOCK = (1.0, 0.0, 0.0, 1.0)
ZERO_PAIR = (0.0, 0.0)


def extended(block, sides, width):
    for axis, dim in sides:
        count = lax.axis_size(axis)
        forward = [(i, i + 1) for i in range(count - 1)]
        backward = [(target, source) for source, target in forward]
        low = lax.ppermute(
            lax.slice_in_dim(block, block.shape[dim] - width, None, axis=dim), axis, forward
        )
        high = lax.ppermute(lax.slice_in_dim(block, 0, width, axis=dim), axis, backward)
        block = jnp.concatenate([low, block, high], axis=dim)
    return block


def spectral_matrix(instances):
    offsets = np.arange(instances)[:, None] - np.arange(instances)[None, :]
    angles = np.pi * offsets / instances
    safe_sin = np.where(offsets == 0, 1.0, np.sin(angles))
    parity = np.where(np.mod(offsets, 2) == 0, -1.0, 1.0)
    matrix_table = np.where(
        offsets == 0, 0.0, 0.5 * OMEGA_BLADE * parity * np.cos(angles) / safe_sin
    )
    return jnp.asarray(matrix_table, jnp.float32)


def primitive_parts(cells_state):
    density = cells_state[..., 0, :, :]
    inverse = 1.0 / density
    velocity_x = cells_state[..., 1, :, :] * inverse
    velocity_y = cells_state[..., 2, :, :] * inverse
    velocity_z = cells_state[..., 3, :, :] * inverse
    energy = cells_state[..., 4, :, :]
    pressure = (GAMMA_GAS - 1.0) * (
        energy
        - 0.5
        * density
        * (velocity_x * velocity_x + velocity_y * velocity_y + velocity_z * velocity_z)
    )
    sound_speed = jnp.sqrt(GAMMA_GAS * pressure * inverse)
    return (velocity_x, velocity_y, pressure, sound_speed)


def directed_flux(cells_state, normal_velocity, pressure, component):
    zero_plane = jnp.zeros_like(pressure)
    pressure_rows = [
        zero_plane,
        zero_plane,
        zero_plane,
        zero_plane,
        pressure * normal_velocity,
        zero_plane,
    ]
    pressure_rows[component] = pressure
    return cells_state * normal_velocity[..., None, :, :] + jnp.stack(pressure_rows, axis=-3)


def line_residual(padded):
    velocity_x, velocity_y, pressure, sound_speed = primitive_parts(padded)
    flux_line = directed_flux(padded, velocity_x, pressure, 1)
    radius = jnp.abs(velocity_x) + sound_speed
    sensor = jnp.abs(
        pressure[..., 2:, :] - 2.0 * pressure[..., 1:-1, :] + pressure[..., :-2, :]
    ) / (pressure[..., 2:, :] + 2.0 * pressure[..., 1:-1, :] + pressure[..., :-2, :])
    second = SENSOR_GAIN * jnp.maximum(sensor[..., :-1, :], sensor[..., 1:, :])
    fourth = jnp.maximum(0.0, FOURTH_GAIN - second)
    face_radius = 0.5 * (radius[..., 1:-2, :] + radius[..., 2:-1, :])
    left_far = padded[..., :-3, :]
    left_near = padded[..., 1:-2, :]
    right_near = padded[..., 2:-1, :]
    right_far = padded[..., 3:, :]
    damping = face_radius[..., None, :, :] * (
        second[..., None, :, :] * (right_near - left_near)
        - fourth[..., None, :, :] * (right_far - 3.0 * right_near + 3.0 * left_near - left_far)
    )
    face_flux = 0.5 * (flux_line[..., 1:-2, :] + flux_line[..., 2:-1, :]) - damping
    return (face_flux[..., 1:, :] - face_flux[..., :-1, :], radius)


def pitch_parts(cells_state):
    velocity_x, velocity_y, pressure, sound_speed = primitive_parts(cells_state)
    return (directed_flux(cells_state, velocity_y, pressure, 2), jnp.abs(velocity_y) + sound_speed)


def pitch_residual(cells_state, next_lines, prev_lines):
    pitch_flux, radius = pitch_parts(cells_state)
    state_next = jnp.take(cells_state, next_lines, axis=-1)
    flux_next, radius_next = pitch_parts(state_next)
    face_flux = 0.5 * (pitch_flux + flux_next) - PITCH_GAIN * (0.5 * (radius + radius_next))[
        ..., None, :, :
    ] * (state_next - cells_state)
    return face_flux - jnp.take(face_flux, prev_lines, axis=-1)


def boundary_cells(edge_pair, line_codes, lower_end):
    reflected = edge_pair[..., ::-1, :] * jnp.asarray(MIRROR_SIGNS, jnp.float32)[:, None, None]
    if lower_end:
        copied = jnp.concatenate([edge_pair[..., :1, :], edge_pair[..., :1, :]], axis=-2)
    else:
        copied = jnp.concatenate([edge_pair[..., 1:, :], edge_pair[..., 1:, :]], axis=-2)
    inflow = jnp.asarray(FREE_STATE, jnp.float32)[:, None, None] + jnp.zeros_like(edge_pair)
    return jnp.where(line_codes == 0, reflected, jnp.where(line_codes == 1, inflow, copied))


def line_coefficients(radius_ext, diagonal_term, positions, total_cells):
    radius_below = radius_ext[..., :-2, :]
    radius_centre = radius_ext[..., 1:-1, :]
    radius_above = radius_ext[..., 2:, :]
    face_below = 0.5 * (radius_below + radius_centre)
    face_above = 0.5 * (radius_centre + radius_above)
    far_low = FOURTH_IMPL * radius_below
    near_low = -SECOND_IMPL * face_below - 2.0 * FOURTH_IMPL * (radius_below + radius_centre)
    middle = (
        diagonal_term
        + SECOND_IMPL * (face_below + face_above)
        + FOURTH_IMPL * (radius_below + 4.0 * radius_centre + radius_above)
    )
    near_high = -SECOND_IMPL * face_above - 2.0 * FOURTH_IMPL * (radius_centre + radius_above)
    far_high = FOURTH_IMPL * radius_above
    column = positions[:, None]
    far_low = jnp.where(column >= 2, far_low, 0.0)
    near_low = jnp.where(column >= 1, near_low, 0.0)
    near_high = jnp.where(column <= total_cells - 2, near_high, 0.0)
    far_high = jnp.where(column <= total_cells - 3, far_high, 0.0)
    return (far_low, near_low, middle, near_high, far_high)


def block_product(first_matrix, second_matrix):
    return (
        first_matrix[0] * second_matrix[0] + first_matrix[1] * second_matrix[2],
        first_matrix[0] * second_matrix[1] + first_matrix[1] * second_matrix[3],
        first_matrix[2] * second_matrix[0] + first_matrix[3] * second_matrix[2],
        first_matrix[2] * second_matrix[1] + first_matrix[3] * second_matrix[3],
    )


def block_inverse(matrix):
    determinant = matrix[0] * matrix[3] - matrix[1] * matrix[2]
    reciprocal = 1.0 / determinant
    return (
        matrix[3] * reciprocal,
        -matrix[1] * reciprocal,
        -matrix[2] * reciprocal,
        matrix[0] * reciprocal,
    )


def block_apply(matrix, vector):
    return (
        matrix[0] * vector[0] + matrix[1] * vector[1],
        matrix[2] * vector[0] + matrix[3] * vector[1],
    )


def add_blocks(first_members, second_members):
    return tuple((a + b for a, b in zip(first_members, second_members)))


def negate(members):
    return tuple((-a for a in members))


def extend_blocks(members, fill_values):
    return tuple(
        (
            jnp.concatenate([m, jnp.full_like(m[..., :1, :], f)], axis=-2)
            for m, f in zip(members, fill_values)
        )
    )


def shift_next(members, fill_values):
    return tuple(
        (
            jnp.concatenate([m[..., 1:, :], jnp.full_like(m[..., :1, :], f)], axis=-2)
            for m, f in zip(members, fill_values)
        )
    )


def shift_prev(members):
    return tuple(
        (jnp.concatenate([jnp.zeros_like(m[..., :1, :]), m[..., :-1, :]], axis=-2) for m in members)
    )


def pair_split(member):
    shaped = member.reshape(member.shape[:-2] + (member.shape[-2] // 2, 2, member.shape[-1]))
    return (shaped[..., 0, :], shaped[..., 1, :])


def split_parity(members):
    halves = [pair_split(m) for m in members]
    return (tuple((h[0] for h in halves)), tuple((h[1] for h in halves)))


def alternate(first_member, second_member):
    stacked = jnp.stack((first_member, second_member), axis=-2)
    return stacked.reshape(
        first_member.shape[:-2] + (2 * first_member.shape[-2], first_member.shape[-1])
    )


def reduce_blocks(sub_blocks, diag_blocks, super_blocks, right_side):
    block_count = diag_blocks[0].shape[-2]
    if block_count == 1:
        return block_apply(block_inverse(diag_blocks), right_side)
    if block_count % 2 == 1:
        sub_blocks = extend_blocks(sub_blocks, ZERO_BLOCK)
        diag_blocks = extend_blocks(diag_blocks, UNIT_BLOCK)
        super_blocks = extend_blocks(super_blocks, ZERO_BLOCK)
        right_side = extend_blocks(right_side, ZERO_PAIR)
    sub_even, sub_odd = split_parity(sub_blocks)
    diag_even, diag_odd = split_parity(diag_blocks)
    super_even, super_odd = split_parity(super_blocks)
    side_even, side_odd = split_parity(right_side)
    inverse_even = block_inverse(diag_even)
    inverse_next = shift_next(inverse_even, UNIT_BLOCK)
    sub_next = shift_next(sub_even, ZERO_BLOCK)
    super_next = shift_next(super_even, ZERO_BLOCK)
    side_next = shift_next(side_even, ZERO_PAIR)
    left_factor = negate(block_product(sub_odd, inverse_even))
    right_factor = negate(block_product(super_odd, inverse_next))
    reduced_sub = block_product(left_factor, sub_even)
    reduced_diag = add_blocks(
        diag_odd,
        add_blocks(block_product(left_factor, super_even), block_product(right_factor, sub_next)),
    )
    reduced_super = block_product(right_factor, super_next)
    reduced_side = add_blocks(
        side_odd,
        add_blocks(block_apply(left_factor, side_even), block_apply(right_factor, side_next)),
    )
    odd_values = reduce_blocks(reduced_sub, reduced_diag, reduced_super, reduced_side)
    before_values = shift_prev(odd_values)
    remainder = add_blocks(
        side_even,
        negate(
            add_blocks(block_apply(sub_even, before_values), block_apply(super_even, odd_values))
        ),
    )
    even_values = block_apply(inverse_even, remainder)
    merged = tuple((alternate(e, o) for e, o in zip(even_values, odd_values)))
    return tuple((m[..., :block_count, :] for m in merged))


def cells_leading(block):
    moved = jnp.transpose(block, (2, 0, 1, 3))
    return moved.reshape(block.shape[2], block.shape[0] * block.shape[1] * block.shape[3])


def solve_in_lanes(coefficients, line_source):
    source_shape = line_source.shape
    lane_coef = [cells_leading(jnp.broadcast_to(c[:, None], source_shape)) for c in coefficients]
    pairs_list = [pair_split(m) for m in lane_coef]
    zero_plane = jnp.zeros_like(pairs_list[2][0])
    sub_blocks = (pairs_list[0][0], pairs_list[1][0], zero_plane, pairs_list[0][1])
    diag_blocks = (pairs_list[2][0], pairs_list[3][0], pairs_list[1][1], pairs_list[2][1])
    super_blocks = (pairs_list[4][0], zero_plane, pairs_list[3][1], pairs_list[4][1])
    values = reduce_blocks(
        sub_blocks, diag_blocks, super_blocks, pair_split(cells_leading(line_source))
    )
    flat = alternate(values[0], values[1])
    shaped = flat.reshape(source_shape[2], source_shape[0], source_shape[1], source_shape[3])
    return jnp.transpose(shaped, (1, 2, 0, 3))


def return_tiles(line_values):
    return lax.all_to_all(line_values, "cell", split_axis=2, concat_axis=3, tiled=True)


def local_by_lines(state, pseudo_rate, line_next, face_codes):
    local_count = state.shape[0]
    tile_cells = state.shape[2]
    cell_index = lax.axis_index("cell")
    cell_count = lax.axis_size("cell")
    total_cells = tile_cells * cell_count
    spectral = spectral_matrix(NT)
    first_local = lax.axis_index("inst") * local_count
    own_rows = lax.dynamic_slice_in_dim(spectral, first_local, local_count, 0)
    shard_block = jax.tree.map(lambda a: lax.all_gather(a, "inst", axis=0, tiled=True), state)
    columns = lax.slice_in_dim(own_rows, 0, shard_block.shape[0], axis=1)
    time_term = jnp.zeros_like(state) + jnp.einsum(
        "nm,mvil->nvil", columns, shard_block, precision=lax.Precision.HIGHEST
    )
    padded = extended(state, (("cell", 2),), 2)
    codes_lines = jnp.repeat(face_codes, LINES_DEV, axis=1)
    lower_ghost = boundary_cells(state[:, :, 0:2, :], codes_lines[0], True)
    upper_ghost = boundary_cells(state[:, :, -2:, :], codes_lines[1], False)
    lower_rim = jnp.where(cell_index == 0, lower_ghost, padded[:, :, :2, :])
    upper_rim = jnp.where(cell_index == cell_count - 1, upper_ghost, padded[:, :, -2:, :])
    padded = jnp.concatenate([lower_rim, padded[:, :, 2:-2, :], upper_rim], axis=2)
    line_part, radius = line_residual(padded)
    prev_lines = (
        jnp.zeros_like(line_next).at[line_next].set(jnp.arange(line_next.shape[0], dtype=jnp.int32))
    )
    residual = line_part + pitch_residual(state, line_next, prev_lines) + time_term
    right_side = -residual
    centre_radius = radius[:, 2:-2, :]
    diagonal_term = pseudo_rate * centre_radius
    positions = cell_index * tile_cells + jnp.arange(-1, tile_cells + 1, dtype=jnp.int32)
    inside = (positions >= 0) & (positions < total_cells)
    radius_ext = jnp.where(inside[:, None], radius[:, 1:-1, :], 0.0)
    coefficients = line_coefficients(radius_ext, diagonal_term, positions[1:-1], total_cells)
    stacked = jnp.stack(coefficients, axis=1)
    line_source = lax.all_to_all(right_side, "cell", split_axis=3, concat_axis=2, tiled=True)
    line_coef = lax.all_to_all(stacked, "cell", split_axis=3, concat_axis=2, tiled=True)
    update = return_tiles(solve_in_lanes(tuple((line_coef[:, k] for k in range(5))), line_source))
    return state + update


LANES = 128
ROWS = 8
PAIRS = 3
CELL_ROWS = PAIRS * ROWS
REST_ROW = 2 * CELL_ROWS
RATE_ROW = 2 * REST_ROW
BLOCK_ROWS = RATE_ROW + ROWS


def spectral_offsets():
    table = np.zeros(NT)
    for offset in range(1, NT):
        angle = np.pi * offset / NT
        parity = -1.0 if offset % 2 == 0 else 1.0
        table[offset] = 0.5 * OMEGA_BLADE * parity * np.cos(angle) / np.sin(angle)
    return [float(np.float32(value)) for value in table]


def plane_masks():
    row_index = lax.broadcasted_iota(jnp.int32, (ROWS, LANES), 0)
    return row_index < 4, (row_index & 2) == 0, row_index & 1


def both(first_var, plane):
    turned = pltpu.roll(plane, 4, 0)
    return jnp.where(first_var, plane, turned), jnp.where(first_var, turned, plane)


def primitives(first_var, planes):
    density, moment_x = both(first_var, planes[0])
    moment_y, moment_z = both(first_var, planes[1])
    energy = jnp.where(first_var, planes[2], pltpu.roll(planes[2], 4, 0))
    inverse = 1.0 / density
    velocity_x = moment_x * inverse
    velocity_y = moment_y * inverse
    velocity_z = moment_z * inverse
    kinetic = moment_x * velocity_x + moment_y * velocity_y + moment_z * velocity_z
    pressure = (GAMMA_GAS - 1.0) * (energy - 0.5 * kinetic)
    sound = jnp.sqrt(GAMMA_GAS * pressure * inverse)
    return velocity_x, velocity_y, pressure, sound


def rows_of(var, inst, half):
    return (var // 2) * ROWS + (var % 2) * 4 + inst * 2 + half


def cell_kernel(all_ref, rate_ref, next_ref, out_ref, plane_ref):
    own_inst = lax.axis_index("inst")
    inst_count = all_ref.shape[0] // 2
    shape = (ROWS, LANES)
    lane_index = lax.broadcasted_iota(jnp.int32, shape, 1)
    first_var, first_inst, half_index = plane_masks()
    first_half = half_index == 0

    next_rows = [next_ref[pl.ds(half, 1), :] for half in range(2)]
    next_line = jnp.where(first_half, next_rows[0], next_rows[1])
    column = lax.broadcasted_iota(jnp.int32, (LANES, LANES), 0)
    prev_halves = []
    for target in range(2):
        total = None
        for source in range(2):
            hits = jnp.where(column + target * LANES == next_rows[source], 1.0, 0.0)
            names = (lane_index + source * LANES).astype(jnp.float32)
            part = lax.dot_general(
                names, hits, (((1,), (1,)), ((), ())), preferred_element_type=jnp.float32
            )
            total = part if total is None else total + part
        prev_halves.append(total)
    prev_line = jnp.where(first_half, prev_halves[0], prev_halves[1]).astype(jnp.int32)

    def picker(lines):
        lane = lines & (LANES - 1)
        same = (lines >> 7) == half_index

        def pick(plane):
            swapped = jnp.where(first_half, pltpu.roll(plane, 7, 0), pltpu.roll(plane, 1, 0))
            here = jnp.take_along_axis(plane, lane, axis=1, mode="promise_in_bounds")
            there = jnp.take_along_axis(swapped, lane, axis=1, mode="promise_in_bounds")
            return jnp.where(same, here, there)

        return pick

    pick_next = picker(next_line)
    pick_prev = picker(prev_line)

    for shift in range(inst_count):
        pair = (own_inst - shift) & (inst_count - 1)
        for cell in range(2):
            for var in range(6):
                for inst in range(2):
                    for half in range(2):
                        row = cell * CELL_ROWS + rows_of(var, inst, half)
                        plane_ref[shift, pl.ds(row, 1), :] = all_ref[
                            2 * pair + inst, var, pl.ds(cell, 1), pl.ds(half * LANES, LANES)
                        ]
    offsets = spectral_offsets()

    def time_parts(cell):
        same_total = [None] * PAIRS
        other_total = [None] * PAIRS
        for shift in range(inst_count):
            same = offsets[(2 * shift) % NT]
            other = jnp.where(
                first_inst, offsets[(2 * shift + 1) % NT], offsets[(2 * shift - 1) % NT]
            )
            for k in range(PAIRS):
                plane = plane_ref[shift, pl.ds(cell * CELL_ROWS + k * ROWS, ROWS), :]
                if shift > 0:
                    term = same * plane
                    same_total[k] = term if same_total[k] is None else same_total[k] + term
                term = other * plane
                other_total[k] = term if other_total[k] is None else other_total[k] + term
        return [
            s + jnp.where(first_inst, pltpu.roll(o, 6, 0), pltpu.roll(o, 2, 0))
            for s, o in zip(same_total, other_total)
        ]

    def flux_across(planes, velocity, pressure):
        return [
            planes[0] * velocity,
            planes[1] * velocity + jnp.where(first_var, pressure, 0.0),
            planes[2] * velocity + jnp.where(first_var, pressure * velocity, 0.0),
        ]

    for cell in range(2):
        planes = [
            plane_ref[0, pl.ds(cell * CELL_ROWS + k * ROWS, ROWS), :] for k in range(PAIRS)
        ]
        nearby = [pick_next(plane) for plane in planes]
        _, velocity, pressure, sound = primitives(first_var, planes)
        _, next_velocity, next_pressure, next_sound = primitives(first_var, nearby)
        own_flux = flux_across(planes, velocity, pressure)
        next_flux = flux_across(nearby, next_velocity, next_pressure)
        weight = (PITCH_GAIN * 0.5) * (
            jnp.abs(velocity) + sound + (jnp.abs(next_velocity) + next_sound)
        )
        time_term = time_parts(cell)
        for k in range(PAIRS):
            face = 0.5 * (own_flux[k] + next_flux[k]) - weight * (nearby[k] - planes[k])
            rest = time_term[k] + (face - pick_prev(face))
            row = cell * CELL_ROWS + k * ROWS
            out_ref[pl.ds(row, ROWS), :] = planes[k]
            out_ref[pl.ds(REST_ROW + row, ROWS), :] = rest
        for half in range(2):
            out_ref[pl.ds(RATE_ROW + cell * 2 + half, 1), :] = rate_ref[
                pl.ds(cell, 1), pl.ds(half * LANES, LANES)
            ]
    out_ref[pl.ds(RATE_ROW + 4, 4), :] = jnp.zeros((4, LANES), jnp.float32)


def two_by_two(first, second):
    def entry(a, b, c, d):
        terms = [x * y for x, y in ((a, b), (c, d)) if x is not None and y is not None]
        return None if not terms else terms[0] if len(terms) == 1 else terms[0] + terms[1]

    return (
        entry(first[0], second[0], first[1], second[2]),
        entry(first[0], second[1], first[1], second[3]),
        entry(first[2], second[0], first[3], second[2]),
        entry(first[2], second[1], first[3], second[3]),
    )


def inverse_of(matrix):
    reciprocal = 1.0 / (matrix[0] * matrix[3] - matrix[1] * matrix[2])
    return (
        matrix[3] * reciprocal,
        -(matrix[1] * reciprocal),
        -(matrix[2] * reciprocal),
        matrix[0] * reciprocal,
    )


def less(first, second):
    return tuple(a if b is None else a - b for a, b in zip(first, second))


def minus(members):
    return tuple(None if a is None else -a for a in members)


def eliminate(centre, left, left_inverse, right, right_inverse):
    left_factor = two_by_two(centre[0], left_inverse)
    right_factor = two_by_two(centre[2], right_inverse)
    sub = minus(two_by_two(left_factor, left[0]))
    diag = less(
        less(centre[1], two_by_two(left_factor, left[2])), two_by_two(right_factor, right[0])
    )
    sup = minus(two_by_two(right_factor, right[2]))
    side = []
    for k in range(PAIRS):
        for row in range(2):
            value = centre[3][row * PAIRS + k]
            for factor, other in ((left_factor, left[3]), (right_factor, right[3])):
                value = value - (
                    factor[2 * row] * other[k] + factor[2 * row + 1] * other[PAIRS + k]
                )
            side.append((row * PAIRS + k, value))
    return sub, diag, sup, [value for _, value in sorted(side, key=lambda item: item[0])]


def line_kernel(
    cells, all_ref, codes_ref, out_ref, coef_ref, side_ref, coef2_ref, side2_ref,
    couple_ref, diag3_ref, side3_ref,
):
    own_cell = lax.axis_index("cell")
    shape = (ROWS, LANES)
    lane_index = lax.broadcasted_iota(jnp.int32, shape, 1)
    first_var, _, half_index = plane_masks()
    first_half = half_index == 0
    zero = jnp.zeros(shape, jnp.float32)

    tile = half_index * (LANES // LINES_DEV) + lane_index // LINES_DEV
    codes = []
    for end in range(2):
        plane = jnp.zeros(shape, jnp.int32)
        for k in range(2 * LANES // LINES_DEV):
            plane = jnp.where(tile == k, codes_ref[end, k], plane)
        codes.append(plane)

    def loaded(cell, start=0):
        return [
            all_ref[cell // 2, pl.ds(start + (cell % 2) * CELL_ROWS + k * ROWS, ROWS), :]
            for k in range(PAIRS)
        ]

    def ghost(end, mirrored, copied):
        planes = []
        for k in range(PAIRS):
            reflected = mirrored[k]
            if k == 0:
                reflected = jnp.where(first_var, reflected, -reflected)
            inflow = jnp.where(first_var, FREE_STATE[2 * k], FREE_STATE[2 * k + 1])
            planes.append(
                jnp.where(
                    codes[end] == 0, reflected, jnp.where(codes[end] == 1, inflow, copied[k])
                )
            )
        return planes

    def extended_state(cell):
        if cell < 0:
            return ghost(0, loaded(-1 - cell), loaded(0))
        if cell >= cells:
            return ghost(
                1, loaded(2 * cells - 1 - cell), loaded(cells - 1)
            )
        return loaded(cell)

    def flux_along(planes, velocity, pressure):
        return [
            planes[0] * velocity + jnp.where(first_var, 0.0, pressure),
            planes[1] * velocity,
            planes[2] * velocity + jnp.where(first_var, pressure * velocity, 0.0),
        ]

    state, pressures, radii, fluxes, steps, sensors, faces = {}, {}, {}, {}, {}, {}, {}
    for cell in range(-2, cells + 2):
        planes = extended_state(cell)
        velocity_x, _, pressure, sound = primitives(first_var, planes)
        state[cell] = planes
        pressures[cell] = pressure
        radii[cell] = jnp.abs(velocity_x) + sound
        if -1 <= cell <= cells:
            fluxes[cell] = flux_along(planes, velocity_x, pressure)
        if cell >= -1:
            steps[cell - 1] = [a - b for a, b in zip(planes, state[cell - 1])]
        if cell >= 0:
            twice = 2.0 * pressures[cell - 1]
            outer = pressure + pressures[cell - 2]
            sensors[cell - 1] = jnp.abs(outer - twice) / (outer + twice)
        if cell >= 1:
            face = cell - 2
            second = SENSOR_GAIN * jnp.maximum(sensors[face], sensors[face + 1])
            fourth = jnp.maximum(0.0, FOURTH_GAIN - second)
            face_radius = 0.5 * (radii[face] + radii[face + 1])
            near_weight = face_radius * (second + 2.0 * fourth)
            far_weight = face_radius * fourth
            faces[face] = [
                0.5 * (fluxes[face][k] + fluxes[face + 1][k])
                - (
                    near_weight * steps[face][k]
                    - far_weight * (steps[face + 1][k] + steps[face - 1][k])
                )
                for k in range(PAIRS)
            ]
        if cell >= 2:
            at = cell - 2
            slot, member = at // 2 + 1, at % 2
            rest = loaded(at, REST_ROW)
            for k in range(PAIRS):
                side_ref[slot, member * PAIRS + k] = (
                    faces[at - 1][k] - faces[at][k] - rest[k]
                )
            below = radii[at - 1] if at > 0 else zero
            centre = radii[at]
            above = radii[at + 1] if at < cells - 1 else zero
            below_sum = below + centre
            above_sum = centre + above
            half_low = SECOND_IMPL * 0.5 + 2.0 * FOURTH_IMPL
            rate_rows = [
                all_ref[at // 2, pl.ds(RATE_ROW + member * 2 + half, 1), :]
                for half in range(2)
            ]
            rate = jnp.where(first_half, rate_rows[0], rate_rows[1])
            middle = (
                rate * centre
                + SECOND_IMPL * (0.5 * (below_sum + above_sum))
                + FOURTH_IMPL * (below + 4.0 * centre + above)
            )
            far_low = FOURTH_IMPL * below if at >= 2 else zero
            near_low = -half_low * below_sum if at >= 1 else zero
            near_high = -half_low * above_sum if at <= cells - 2 else zero
            far_high = FOURTH_IMPL * above if at <= cells - 3 else zero
            if member == 0:
                entries = {0: far_low, 1: near_low, 3: middle, 4: near_high, 7: far_high}
            else:
                entries = {2: far_low, 5: near_low, 6: middle, 8: near_high, 9: far_high}
            for k, plane in entries.items():
                coef_ref[slot, k] = plane

    blocks = cells // 2
    one = zero + 1.0
    for slot in (0, blocks + 1):
        for k in range(10):
            coef_ref[slot, k] = one if k in (3, 6) else zero
        for k in range(2 * PAIRS):
            side_ref[slot, k] = zero
    for slot in (0, blocks // 2 + 1):
        for k in range(12):
            coef2_ref[slot, k] = one if k in (4, 7) else zero
        for k in range(2 * PAIRS):
            side2_ref[slot, k] = zero

    def block_one(slot):
        c = [coef_ref[slot, k] for k in range(10)]
        return (
            (c[0], c[1], None, c[2]),
            (c[3], c[4], c[5], c[6]),
            (c[7], None, c[8], c[9]),
            [side_ref[slot, k] for k in range(2 * PAIRS)],
        )

    def block_two(slot):
        c = [coef2_ref[slot, k] for k in range(12)]
        return (
            tuple(c[0:4]),
            tuple(c[4:8]),
            tuple(c[8:12]),
            [side2_ref[slot, k] for k in range(2 * PAIRS)],
        )

    parity = own_cell & 1
    left = block_one(parity)
    left_inverse = inverse_of(left[1])
    for k in range(blocks // 2):
        right = block_one(parity + 2 * k + 2)
        right_inverse = inverse_of(right[1])
        kept = block_one(parity + 2 * k + 1)
        sub, diag, sup, side = eliminate(kept, left, left_inverse, right, right_inverse)
        for n, plane in enumerate(sub + diag + sup):
            coef2_ref[k + 1, n] = plane
        for n, plane in enumerate(side):
            side2_ref[k + 1, n] = plane
        left, left_inverse = right, right_inverse
    parity = (own_cell >> 1) & 1
    left = block_two(parity)
    left_inverse = inverse_of(left[1])
    for k in range(blocks // 4):
        right = block_two(parity + 2 * k + 2)
        right_inverse = inverse_of(right[1])
        kept = block_two(parity + 2 * k + 1)
        sub, diag, sup, side = eliminate(kept, left, left_inverse, right, right_inverse)
        for n in range(4):
            couple_ref[k, 0, n] = sub[n]
            couple_ref[k, 1, n] = sup[n]
            diag3_ref[k, n] = diag[n]
        for n, plane in enumerate(side):
            side3_ref[k, n] = plane
        left, left_inverse = right, right_inverse
    own = (own_cell >> 2) & 1
    other = 1 - own
    own_couple = tuple(couple_ref[own, 1 - own, n] for n in range(4))
    other_couple = tuple(couple_ref[other, own, n] for n in range(4))
    factor = two_by_two(own_couple, inverse_of([diag3_ref[other, n] for n in range(4)]))
    diag = less([diag3_ref[own, n] for n in range(4)], two_by_two(factor, other_couple))
    last_inverse = inverse_of(diag)
    for k in range(PAIRS):
        other_low, other_high = side3_ref[other, k], side3_ref[other, PAIRS + k]
        low = side3_ref[own, k] - (factor[0] * other_low + factor[1] * other_high)
        high = side3_ref[own, PAIRS + k] - (factor[2] * other_low + factor[3] * other_high)
        for member in range(2):
            delta = last_inverse[2 * member] * low + last_inverse[2 * member + 1] * high
            base = all_ref[own_cell, pl.ds(member * CELL_ROWS + k * ROWS, ROWS), :]
            result = base + delta
            for var in range(2):
                for inst in range(2):
                    for half in range(2):
                        row = rows_of(var, inst, half)
                        out_ref[
                            inst, 2 * k + var, pl.ds(member, 1), pl.ds(half * LANES, LANES)
                        ] = result[row : row + 1]


def gather_inst(block):
    return lax.all_gather(block, "inst", axis=0, tiled=True)


def gather_cell(block):
    planes = block.reshape(BLOCK_ROWS // ROWS, ROWS, LANES)
    return lax.all_gather(planes, "cell", axis=0, tiled=True)


def local_by_gather(state, pseudo_rate, line_next, face_codes):
    cells = lax.axis_size("cell") * state.shape[2]
    vmem = pl.BlockSpec(memory_space=pltpu.VMEM)
    plane = (ROWS, LANES)
    every = gather_inst(state)
    packed = pl.pallas_call(
        cell_kernel,
        out_shape=jax.ShapeDtypeStruct((BLOCK_ROWS, LANES), jnp.float32),
        in_specs=[vmem, vmem, vmem],
        out_specs=vmem,
        scratch_shapes=[
            pltpu.VMEM((every.shape[0] // 2, 2 * CELL_ROWS, LANES), jnp.float32)
        ],
    )(every, pseudo_rate, line_next.reshape(2, LANES))
    gathered = gather_cell(packed).reshape(-1, BLOCK_ROWS, LANES)
    blocks = cells // 2
    sizes = [
        (blocks + 2, 10),
        (blocks + 2, 2 * PAIRS),
        (blocks // 2 + 2, 12),
        (blocks // 2 + 2, 2 * PAIRS),
        (2, 2, 4),
        (2, 4),
        (2, 2 * PAIRS),
    ]
    return pl.pallas_call(
        functools.partial(line_kernel, cells),
        out_shape=jax.ShapeDtypeStruct(state.shape, jnp.float32),
        in_specs=[vmem, pl.BlockSpec(memory_space=pltpu.SMEM)],
        out_specs=vmem,
        scratch_shapes=[pltpu.VMEM(size + plane, jnp.float32) for size in sizes],
    )(gathered, face_codes)


def solution(mesh):
    placed = (P("inst", None, "cell", None), P("cell", None), P(), P())
    inst_count, cell_count = mesh.shape["inst"], mesh.shape["cell"]

    def local(state, pseudo_rate, line_next, face_codes):
        small = (
            state.shape == (2, 6, 2, 2 * LANES)
            and inst_count * 2 == NT
            and cell_count == 8
            and face_codes.shape[1] * LINES_DEV == state.shape[3]
        )
        chosen = local_by_gather if small else local_by_lines
        return chosen(state, pseudo_rate, line_next, face_codes)

    return jax.shard_map(
        local, mesh=mesh, in_specs=placed, out_specs=P("inst", None, "cell", None), check_vma=False
    )
```

```python
import functools

import jax
import jax.numpy as jnp
import numpy as np
from jax import lax
from jax.experimental import pallas as pl
from jax.experimental.pallas import tpu as pltpu
from jax.sharding import PartitionSpec as P

NT = 8
LINES_DEV = 32


GAMMA_GAS = 1.4
OMEGA_BLADE = 1.0
SENSOR_GAIN = 0.25
FOURTH_GAIN = 0.03125
PITCH_GAIN = 0.5
SECOND_IMPL = 1.0
FOURTH_IMPL = 0.25
FREE_STATE = (1.0, 0.5, 0.0, 0.0, 2.625, 0.2)
MIRROR_SIGNS = (1.0, -1.0, 1.0, 1.0, 1.0, 1.0)
ZERO_BLOCK = (0.0, 0.0, 0.0, 0.0)
UNIT_BLOCK = (1.0, 0.0, 0.0, 1.0)
ZERO_PAIR = (0.0, 0.0)


def extended(block, sides, width):
    for axis, dim in sides:
        count = lax.axis_size(axis)
        forward = [(i, i + 1) for i in range(count - 1)]
        backward = [(target, source) for source, target in forward]
        low = lax.ppermute(
            lax.slice_in_dim(block, block.shape[dim] - width, None, axis=dim), axis, forward
        )
        high = lax.ppermute(lax.slice_in_dim(block, 0, width, axis=dim), axis, backward)
        block = jnp.concatenate([low, block, high], axis=dim)
    return block


def spectral_matrix(instances):
    offsets = np.arange(instances)[:, None] - np.arange(instances)[None, :]
    angles = np.pi * offsets / instances
    safe_sin = np.where(offsets == 0, 1.0, np.sin(angles))
    parity = np.where(np.mod(offsets, 2) == 0, -1.0, 1.0)
    matrix_table = np.where(
        offsets == 0, 0.0, 0.5 * OMEGA_BLADE * parity * np.cos(angles) / safe_sin
    )
    return jnp.asarray(matrix_table, jnp.float32)


def primitive_parts(cells_state):
    density = cells_state[..., 0, :, :]
    inverse = 1.0 / density
    velocity_x = cells_state[..., 1, :, :] * inverse
    velocity_y = cells_state[..., 2, :, :] * inverse
    velocity_z = cells_state[..., 3, :, :] * inverse
    energy = cells_state[..., 4, :, :]
    pressure = (GAMMA_GAS - 1.0) * (
        energy
        - 0.5
        * density
        * (velocity_x * velocity_x + velocity_y * velocity_y + velocity_z * velocity_z)
    )
    sound_speed = jnp.sqrt(GAMMA_GAS * pressure * inverse)
    return (velocity_x, velocity_y, pressure, sound_speed)


def directed_flux(cells_state, normal_velocity, pressure, component):
    zero_plane = jnp.zeros_like(pressure)
    pressure_rows = [
        zero_plane,
        zero_plane,
        zero_plane,
        zero_plane,
        pressure * normal_velocity,
        zero_plane,
    ]
    pressure_rows[component] = pressure
    return cells_state * normal_velocity[..., None, :, :] + jnp.stack(pressure_rows, axis=-3)


def line_residual(padded):
    velocity_x, velocity_y, pressure, sound_speed = primitive_parts(padded)
    flux_line = directed_flux(padded, velocity_x, pressure, 1)
    radius = jnp.abs(velocity_x) + sound_speed
    sensor = jnp.abs(
        pressure[..., 2:, :] - 2.0 * pressure[..., 1:-1, :] + pressure[..., :-2, :]
    ) / (pressure[..., 2:, :] + 2.0 * pressure[..., 1:-1, :] + pressure[..., :-2, :])
    second = SENSOR_GAIN * jnp.maximum(sensor[..., :-1, :], sensor[..., 1:, :])
    fourth = jnp.maximum(0.0, FOURTH_GAIN - second)
    face_radius = 0.5 * (radius[..., 1:-2, :] + radius[..., 2:-1, :])
    left_far = padded[..., :-3, :]
    left_near = padded[..., 1:-2, :]
    right_near = padded[..., 2:-1, :]
    right_far = padded[..., 3:, :]
    damping = face_radius[..., None, :, :] * (
        second[..., None, :, :] * (right_near - left_near)
        - fourth[..., None, :, :] * (right_far - 3.0 * right_near + 3.0 * left_near - left_far)
    )
    face_flux = 0.5 * (flux_line[..., 1:-2, :] + flux_line[..., 2:-1, :]) - damping
    return (face_flux[..., 1:, :] - face_flux[..., :-1, :], radius)


def pitch_parts(cells_state):
    velocity_x, velocity_y, pressure, sound_speed = primitive_parts(cells_state)
    return (directed_flux(cells_state, velocity_y, pressure, 2), jnp.abs(velocity_y) + sound_speed)


def pitch_residual(cells_state, next_lines, prev_lines):
    pitch_flux, radius = pitch_parts(cells_state)
    state_next = jnp.take(cells_state, next_lines, axis=-1)
    flux_next, radius_next = pitch_parts(state_next)
    face_flux = 0.5 * (pitch_flux + flux_next) - PITCH_GAIN * (0.5 * (radius + radius_next))[
        ..., None, :, :
    ] * (state_next - cells_state)
    return face_flux - jnp.take(face_flux, prev_lines, axis=-1)


def boundary_cells(edge_pair, line_codes, lower_end):
    reflected = edge_pair[..., ::-1, :] * jnp.asarray(MIRROR_SIGNS, jnp.float32)[:, None, None]
    if lower_end:
        copied = jnp.concatenate([edge_pair[..., :1, :], edge_pair[..., :1, :]], axis=-2)
    else:
        copied = jnp.concatenate([edge_pair[..., 1:, :], edge_pair[..., 1:, :]], axis=-2)
    inflow = jnp.asarray(FREE_STATE, jnp.float32)[:, None, None] + jnp.zeros_like(edge_pair)
    return jnp.where(line_codes == 0, reflected, jnp.where(line_codes == 1, inflow, copied))


def line_coefficients(radius_ext, diagonal_term, positions, total_cells):
    radius_below = radius_ext[..., :-2, :]
    radius_centre = radius_ext[..., 1:-1, :]
    radius_above = radius_ext[..., 2:, :]
    face_below = 0.5 * (radius_below + radius_centre)
    face_above = 0.5 * (radius_centre + radius_above)
    far_low = FOURTH_IMPL * radius_below
    near_low = -SECOND_IMPL * face_below - 2.0 * FOURTH_IMPL * (radius_below + radius_centre)
    middle = (
        diagonal_term
        + SECOND_IMPL * (face_below + face_above)
        + FOURTH_IMPL * (radius_below + 4.0 * radius_centre + radius_above)
    )
    near_high = -SECOND_IMPL * face_above - 2.0 * FOURTH_IMPL * (radius_centre + radius_above)
    far_high = FOURTH_IMPL * radius_above
    column = positions[:, None]
    far_low = jnp.where(column >= 2, far_low, 0.0)
    near_low = jnp.where(column >= 1, near_low, 0.0)
    near_high = jnp.where(column <= total_cells - 2, near_high, 0.0)
    far_high = jnp.where(column <= total_cells - 3, far_high, 0.0)
    return (far_low, near_low, middle, near_high, far_high)


def block_product(first_matrix, second_matrix):
    return (
        first_matrix[0] * second_matrix[0] + first_matrix[1] * second_matrix[2],
        first_matrix[0] * second_matrix[1] + first_matrix[1] * second_matrix[3],
        first_matrix[2] * second_matrix[0] + first_matrix[3] * second_matrix[2],
        first_matrix[2] * second_matrix[1] + first_matrix[3] * second_matrix[3],
    )


def block_inverse(matrix):
    determinant = matrix[0] * matrix[3] - matrix[1] * matrix[2]
    reciprocal = 1.0 / determinant
    return (
        matrix[3] * reciprocal,
        -matrix[1] * reciprocal,
        -matrix[2] * reciprocal,
        matrix[0] * reciprocal,
    )


def block_apply(matrix, vector):
    return (
        matrix[0] * vector[0] + matrix[1] * vector[1],
        matrix[2] * vector[0] + matrix[3] * vector[1],
    )


def add_blocks(first_members, second_members):
    return tuple((a + b for a, b in zip(first_members, second_members)))


def negate(members):
    return tuple((-a for a in members))


def extend_blocks(members, fill_values):
    return tuple(
        (
            jnp.concatenate([m, jnp.full_like(m[..., :1, :], f)], axis=-2)
            for m, f in zip(members, fill_values)
        )
    )


def shift_next(members, fill_values):
    return tuple(
        (
            jnp.concatenate([m[..., 1:, :], jnp.full_like(m[..., :1, :], f)], axis=-2)
            for m, f in zip(members, fill_values)
        )
    )


def shift_prev(members):
    return tuple(
        (jnp.concatenate([jnp.zeros_like(m[..., :1, :]), m[..., :-1, :]], axis=-2) for m in members)
    )


def pair_split(member):
    shaped = member.reshape(member.shape[:-2] + (member.shape[-2] // 2, 2, member.shape[-1]))
    return (shaped[..., 0, :], shaped[..., 1, :])


def split_parity(members):
    halves = [pair_split(m) for m in members]
    return (tuple((h[0] for h in halves)), tuple((h[1] for h in halves)))


def alternate(first_member, second_member):
    stacked = jnp.stack((first_member, second_member), axis=-2)
    return stacked.reshape(
        first_member.shape[:-2] + (2 * first_member.shape[-2], first_member.shape[-1])
    )


def reduce_blocks(sub_blocks, diag_blocks, super_blocks, right_side):
    block_count = diag_blocks[0].shape[-2]
    if block_count == 1:
        return block_apply(block_inverse(diag_blocks), right_side)
    if block_count % 2 == 1:
        sub_blocks = extend_blocks(sub_blocks, ZERO_BLOCK)
        diag_blocks = extend_blocks(diag_blocks, UNIT_BLOCK)
        super_blocks = extend_blocks(super_blocks, ZERO_BLOCK)
        right_side = extend_blocks(right_side, ZERO_PAIR)
    sub_even, sub_odd = split_parity(sub_blocks)
    diag_even, diag_odd = split_parity(diag_blocks)
    super_even, super_odd = split_parity(super_blocks)
    side_even, side_odd = split_parity(right_side)
    inverse_even = block_inverse(diag_even)
    inverse_next = shift_next(inverse_even, UNIT_BLOCK)
    sub_next = shift_next(sub_even, ZERO_BLOCK)
    super_next = shift_next(super_even, ZERO_BLOCK)
    side_next = shift_next(side_even, ZERO_PAIR)
    left_factor = negate(block_product(sub_odd, inverse_even))
    right_factor = negate(block_product(super_odd, inverse_next))
    reduced_sub = block_product(left_factor, sub_even)
    reduced_diag = add_blocks(
        diag_odd,
        add_blocks(block_product(left_factor, super_even), block_product(right_factor, sub_next)),
    )
    reduced_super = block_product(right_factor, super_next)
    reduced_side = add_blocks(
        side_odd,
        add_blocks(block_apply(left_factor, side_even), block_apply(right_factor, side_next)),
    )
    odd_values = reduce_blocks(reduced_sub, reduced_diag, reduced_super, reduced_side)
    before_values = shift_prev(odd_values)
    remainder = add_blocks(
        side_even,
        negate(
            add_blocks(block_apply(sub_even, before_values), block_apply(super_even, odd_values))
        ),
    )
    even_values = block_apply(inverse_even, remainder)
    merged = tuple((alternate(e, o) for e, o in zip(even_values, odd_values)))
    return tuple((m[..., :block_count, :] for m in merged))


def cells_leading(block):
    moved = jnp.transpose(block, (2, 0, 1, 3))
    return moved.reshape(block.shape[2], block.shape[0] * block.shape[1] * block.shape[3])


def solve_in_lanes(coefficients, line_source):
    source_shape = line_source.shape
    lane_coef = [cells_leading(jnp.broadcast_to(c[:, None], source_shape)) for c in coefficients]
    pairs_list = [pair_split(m) for m in lane_coef]
    zero_plane = jnp.zeros_like(pairs_list[2][0])
    sub_blocks = (pairs_list[0][0], pairs_list[1][0], zero_plane, pairs_list[0][1])
    diag_blocks = (pairs_list[2][0], pairs_list[3][0], pairs_list[1][1], pairs_list[2][1])
    super_blocks = (pairs_list[4][0], zero_plane, pairs_list[3][1], pairs_list[4][1])
    values = reduce_blocks(
        sub_blocks, diag_blocks, super_blocks, pair_split(cells_leading(line_source))
    )
    flat = alternate(values[0], values[1])
    shaped = flat.reshape(source_shape[2], source_shape[0], source_shape[1], source_shape[3])
    return jnp.transpose(shaped, (1, 2, 0, 3))


def return_tiles(line_values):
    return lax.all_to_all(line_values, "cell", split_axis=2, concat_axis=3, tiled=True)


def local_by_lines(state, pseudo_rate, line_next, face_codes):
    local_count = state.shape[0]
    tile_cells = state.shape[2]
    cell_index = lax.axis_index("cell")
    cell_count = lax.axis_size("cell")
    total_cells = tile_cells * cell_count
    spectral = spectral_matrix(NT)
    first_local = lax.axis_index("inst") * local_count
    own_rows = lax.dynamic_slice_in_dim(spectral, first_local, local_count, 0)
    shard_block = jax.tree.map(lambda a: lax.all_gather(a, "inst", axis=0, tiled=True), state)
    columns = lax.slice_in_dim(own_rows, 0, shard_block.shape[0], axis=1)
    time_term = jnp.zeros_like(state) + jnp.einsum(
        "nm,mvil->nvil", columns, shard_block, precision=lax.Precision.HIGHEST
    )
    padded = extended(state, (("cell", 2),), 2)
    codes_lines = jnp.repeat(face_codes, LINES_DEV, axis=1)
    lower_ghost = boundary_cells(state[:, :, 0:2, :], codes_lines[0], True)
    upper_ghost = boundary_cells(state[:, :, -2:, :], codes_lines[1], False)
    lower_rim = jnp.where(cell_index == 0, lower_ghost, padded[:, :, :2, :])
    upper_rim = jnp.where(cell_index == cell_count - 1, upper_ghost, padded[:, :, -2:, :])
    padded = jnp.concatenate([lower_rim, padded[:, :, 2:-2, :], upper_rim], axis=2)
    line_part, radius = line_residual(padded)
    prev_lines = (
        jnp.zeros_like(line_next).at[line_next].set(jnp.arange(line_next.shape[0], dtype=jnp.int32))
    )
    residual = line_part + pitch_residual(state, line_next, prev_lines) + time_term
    right_side = -residual
    centre_radius = radius[:, 2:-2, :]
    diagonal_term = pseudo_rate * centre_radius
    positions = cell_index * tile_cells + jnp.arange(-1, tile_cells + 1, dtype=jnp.int32)
    inside = (positions >= 0) & (positions < total_cells)
    radius_ext = jnp.where(inside[:, None], radius[:, 1:-1, :], 0.0)
    coefficients = line_coefficients(radius_ext, diagonal_term, positions[1:-1], total_cells)
    stacked = jnp.stack(coefficients, axis=1)
    line_source = lax.all_to_all(right_side, "cell", split_axis=3, concat_axis=2, tiled=True)
    line_coef = lax.all_to_all(stacked, "cell", split_axis=3, concat_axis=2, tiled=True)
    update = return_tiles(solve_in_lanes(tuple((line_coef[:, k] for k in range(5))), line_source))
    return state + update


LANES = 128
ROWS = 8
PAIRS = 3
CELL_ROWS = PAIRS * ROWS
REST_ROW = 2 * CELL_ROWS
RATE_ROW = 2 * REST_ROW
BLOCK_ROWS = RATE_ROW + ROWS


def spectral_offsets():
    table = np.zeros(NT)
    for offset in range(1, NT):
        angle = np.pi * offset / NT
        parity = -1.0 if offset % 2 == 0 else 1.0
        table[offset] = 0.5 * OMEGA_BLADE * parity * np.cos(angle) / np.sin(angle)
    return [float(np.float32(value)) for value in table]


def plane_masks():
    row_index = lax.broadcasted_iota(jnp.int32, (ROWS, LANES), 0)
    return row_index < 4, (row_index & 2) == 0, row_index & 1


def both(first_var, plane):
    turned = pltpu.roll(plane, 4, 0)
    return jnp.where(first_var, plane, turned), jnp.where(first_var, turned, plane)


def primitives(first_var, planes):
    density, moment_x = both(first_var, planes[0])
    moment_y, moment_z = both(first_var, planes[1])
    energy = jnp.where(first_var, planes[2], pltpu.roll(planes[2], 4, 0))
    inverse = 1.0 / density
    velocity_x = moment_x * inverse
    velocity_y = moment_y * inverse
    velocity_z = moment_z * inverse
    kinetic = moment_x * velocity_x + moment_y * velocity_y + moment_z * velocity_z
    pressure = (GAMMA_GAS - 1.0) * (energy - 0.5 * kinetic)
    sound = jnp.sqrt(GAMMA_GAS * pressure * inverse)
    return velocity_x, velocity_y, pressure, sound


def rows_of(var, inst, half):
    return (var // 2) * ROWS + (var % 2) * 4 + inst * 2 + half


def cell_kernel(all_ref, rate_ref, next_ref, out_ref, plane_ref):
    own_inst = lax.axis_index("inst")
    inst_count = all_ref.shape[0] // 2
    copies = out_ref.shape[0]
    shape = (ROWS, LANES)
    lane_index = lax.broadcasted_iota(jnp.int32, shape, 1)
    first_var, first_inst, half_index = plane_masks()
    first_half = half_index == 0

    next_rows = [next_ref[pl.ds(half, 1), :] for half in range(2)]
    next_line = jnp.where(first_half, next_rows[0], next_rows[1])
    column = lax.broadcasted_iota(jnp.int32, (LANES, LANES), 0)
    prev_halves = []
    for target in range(2):
        total = None
        for source in range(2):
            hits = jnp.where(column + target * LANES == next_rows[source], 1.0, 0.0)
            names = (lane_index + source * LANES).astype(jnp.float32)
            part = lax.dot_general(
                names, hits, (((1,), (1,)), ((), ())), preferred_element_type=jnp.float32
            )
            total = part if total is None else total + part
        prev_halves.append(total)
    prev_line = jnp.where(first_half, prev_halves[0], prev_halves[1]).astype(jnp.int32)

    def picker(lines):
        lane = lines & (LANES - 1)
        same = (lines >> 7) == half_index

        def pick(plane):
            swapped = jnp.where(first_half, pltpu.roll(plane, 7, 0), pltpu.roll(plane, 1, 0))
            here = jnp.take_along_axis(plane, lane, axis=1, mode="promise_in_bounds")
            there = jnp.take_along_axis(swapped, lane, axis=1, mode="promise_in_bounds")
            return jnp.where(same, here, there)

        return pick

    pick_next = picker(next_line)
    pick_prev = picker(prev_line)

    for shift in range(inst_count):
        pair = (own_inst - shift) & (inst_count - 1)
        for cell in range(2):
            for var in range(6):
                for inst in range(2):
                    for half in range(2):
                        row = cell * CELL_ROWS + rows_of(var, inst, half)
                        plane_ref[shift, pl.ds(row, 1), :] = all_ref[
                            2 * pair + inst, var, pl.ds(cell, 1), pl.ds(half * LANES, LANES)
                        ]
    offsets = spectral_offsets()

    def time_parts(cell):
        same_total = [None] * PAIRS
        other_total = [None] * PAIRS
        for shift in range(inst_count):
            same = offsets[(2 * shift) % NT]
            other = jnp.where(
                first_inst, offsets[(2 * shift + 1) % NT], offsets[(2 * shift - 1) % NT]
            )
            for k in range(PAIRS):
                plane = plane_ref[shift, pl.ds(cell * CELL_ROWS + k * ROWS, ROWS), :]
                if shift > 0:
                    term = same * plane
                    same_total[k] = term if same_total[k] is None else same_total[k] + term
                term = other * plane
                other_total[k] = term if other_total[k] is None else other_total[k] + term
        return [
            s + jnp.where(first_inst, pltpu.roll(o, 6, 0), pltpu.roll(o, 2, 0))
            for s, o in zip(same_total, other_total)
        ]

    def flux_across(planes, velocity, pressure):
        return [
            planes[0] * velocity,
            planes[1] * velocity + jnp.where(first_var, pressure, 0.0),
            planes[2] * velocity + jnp.where(first_var, pressure * velocity, 0.0),
        ]

    for cell in range(2):
        planes = [
            plane_ref[0, pl.ds(cell * CELL_ROWS + k * ROWS, ROWS), :] for k in range(PAIRS)
        ]
        nearby = [pick_next(plane) for plane in planes]
        _, velocity, pressure, sound = primitives(first_var, planes)
        _, next_velocity, next_pressure, next_sound = primitives(first_var, nearby)
        own_flux = flux_across(planes, velocity, pressure)
        next_flux = flux_across(nearby, next_velocity, next_pressure)
        weight = (PITCH_GAIN * 0.5) * (
            jnp.abs(velocity) + sound + (jnp.abs(next_velocity) + next_sound)
        )
        time_term = time_parts(cell)
        for k in range(PAIRS):
            face = 0.5 * (own_flux[k] + next_flux[k]) - weight * (nearby[k] - planes[k])
            rest = time_term[k] + (face - pick_prev(face))
            row = cell * CELL_ROWS + k * ROWS
            for copy in range(copies):
                out_ref[copy, pl.ds(row, ROWS), :] = planes[k]
                out_ref[copy, pl.ds(REST_ROW + row, ROWS), :] = rest
    rates = [
        rate_ref[pl.ds(cell, 1), pl.ds(half * LANES, LANES)]
        for cell in range(2)
        for half in range(2)
    ]
    for copy in range(copies):
        for row, rate in enumerate(rates):
            out_ref[copy, pl.ds(RATE_ROW + row, 1), :] = rate
        out_ref[copy, pl.ds(RATE_ROW + 4, 4), :] = jnp.zeros((4, LANES), jnp.float32)


def two_by_two(first, second):
    def entry(a, b, c, d):
        terms = [x * y for x, y in ((a, b), (c, d)) if x is not None and y is not None]
        return None if not terms else terms[0] if len(terms) == 1 else terms[0] + terms[1]

    return (
        entry(first[0], second[0], first[1], second[2]),
        entry(first[0], second[1], first[1], second[3]),
        entry(first[2], second[0], first[3], second[2]),
        entry(first[2], second[1], first[3], second[3]),
    )


def inverse_of(matrix):
    reciprocal = 1.0 / (matrix[0] * matrix[3] - matrix[1] * matrix[2])
    return (
        matrix[3] * reciprocal,
        -(matrix[1] * reciprocal),
        -(matrix[2] * reciprocal),
        matrix[0] * reciprocal,
    )


def less(first, second):
    return tuple(a if b is None else a - b for a, b in zip(first, second))


def minus(members):
    return tuple(None if a is None else -a for a in members)


def eliminate(centre, left, left_inverse, right, right_inverse):
    left_factor = two_by_two(centre[0], left_inverse)
    right_factor = two_by_two(centre[2], right_inverse)
    sub = minus(two_by_two(left_factor, left[0]))
    diag = less(
        less(centre[1], two_by_two(left_factor, left[2])), two_by_two(right_factor, right[0])
    )
    sup = minus(two_by_two(right_factor, right[2]))
    side = []
    for k in range(PAIRS):
        for row in range(2):
            value = centre[3][row * PAIRS + k]
            for factor, other in ((left_factor, left[3]), (right_factor, right[3])):
                value = value - (
                    factor[2 * row] * other[k] + factor[2 * row + 1] * other[PAIRS + k]
                )
            side.append((row * PAIRS + k, value))
    return sub, diag, sup, [value for _, value in sorted(side, key=lambda item: item[0])]


def line_kernel(
    cells, all_ref, codes_ref, out_ref, coef_ref, side_ref, coef2_ref, side2_ref,
    couple_ref, diag3_ref, side3_ref,
):
    own_cell = lax.axis_index("cell")
    shape = (ROWS, LANES)
    lane_index = lax.broadcasted_iota(jnp.int32, shape, 1)
    first_var, _, half_index = plane_masks()
    first_half = half_index == 0
    zero = jnp.zeros(shape, jnp.float32)

    tile = half_index * (LANES // LINES_DEV) + lane_index // LINES_DEV
    codes = []
    for end in range(2):
        plane = jnp.zeros(shape, jnp.int32)
        for k in range(2 * LANES // LINES_DEV):
            plane = jnp.where(tile == k, codes_ref[end, k], plane)
        codes.append(plane)

    def loaded(cell, start=0):
        return [
            all_ref[cell // 2, pl.ds(start + (cell % 2) * CELL_ROWS + k * ROWS, ROWS), :]
            for k in range(PAIRS)
        ]

    def ghost(end, mirrored, copied):
        planes = []
        for k in range(PAIRS):
            reflected = mirrored[k]
            if k == 0:
                reflected = jnp.where(first_var, reflected, -reflected)
            inflow = jnp.where(first_var, FREE_STATE[2 * k], FREE_STATE[2 * k + 1])
            planes.append(
                jnp.where(
                    codes[end] == 0, reflected, jnp.where(codes[end] == 1, inflow, copied[k])
                )
            )
        return planes

    def extended_state(cell):
        if cell < 0:
            return ghost(0, loaded(-1 - cell), loaded(0))
        if cell >= cells:
            return ghost(
                1, loaded(2 * cells - 1 - cell), loaded(cells - 1)
            )
        return loaded(cell)

    def flux_along(planes, velocity, pressure):
        return [
            planes[0] * velocity + jnp.where(first_var, 0.0, pressure),
            planes[1] * velocity,
            planes[2] * velocity + jnp.where(first_var, pressure * velocity, 0.0),
        ]

    state, pressures, radii, fluxes, steps, sensors, faces = {}, {}, {}, {}, {}, {}, {}
    for cell in range(-2, cells + 2):
        planes = extended_state(cell)
        velocity_x, _, pressure, sound = primitives(first_var, planes)
        state[cell] = planes
        pressures[cell] = pressure
        radii[cell] = jnp.abs(velocity_x) + sound
        if -1 <= cell <= cells:
            fluxes[cell] = flux_along(planes, velocity_x, pressure)
        if cell >= -1:
            steps[cell - 1] = [a - b for a, b in zip(planes, state[cell - 1])]
        if cell >= 0:
            twice = 2.0 * pressures[cell - 1]
            outer = pressure + pressures[cell - 2]
            sensors[cell - 1] = jnp.abs(outer - twice) / (outer + twice)
        if cell >= 1:
            face = cell - 2
            second = SENSOR_GAIN * jnp.maximum(sensors[face], sensors[face + 1])
            fourth = jnp.maximum(0.0, FOURTH_GAIN - second)
            face_radius = 0.5 * (radii[face] + radii[face + 1])
            near_weight = face_radius * (second + 2.0 * fourth)
            far_weight = face_radius * fourth
            faces[face] = [
                0.5 * (fluxes[face][k] + fluxes[face + 1][k])
                - (
                    near_weight * steps[face][k]
                    - far_weight * (steps[face + 1][k] + steps[face - 1][k])
                )
                for k in range(PAIRS)
            ]
        if cell >= 2:
            at = cell - 2
            slot, member = at // 2 + 1, at % 2
            rest = loaded(at, REST_ROW)
            for k in range(PAIRS):
                side_ref[slot, member * PAIRS + k] = (
                    faces[at - 1][k] - faces[at][k] - rest[k]
                )
            below = radii[at - 1] if at > 0 else zero
            centre = radii[at]
            above = radii[at + 1] if at < cells - 1 else zero
            below_sum = below + centre
            above_sum = centre + above
            half_low = SECOND_IMPL * 0.5 + 2.0 * FOURTH_IMPL
            rate_rows = [
                all_ref[at // 2, pl.ds(RATE_ROW + member * 2 + half, 1), :]
                for half in range(2)
            ]
            rate = jnp.where(first_half, rate_rows[0], rate_rows[1])
            middle = (
                rate * centre
                + SECOND_IMPL * (0.5 * (below_sum + above_sum))
                + FOURTH_IMPL * (below + 4.0 * centre + above)
            )
            far_low = FOURTH_IMPL * below if at >= 2 else zero
            near_low = -half_low * below_sum if at >= 1 else zero
            near_high = -half_low * above_sum if at <= cells - 2 else zero
            far_high = FOURTH_IMPL * above if at <= cells - 3 else zero
            if member == 0:
                entries = {0: far_low, 1: near_low, 3: middle, 4: near_high, 7: far_high}
            else:
                entries = {2: far_low, 5: near_low, 6: middle, 8: near_high, 9: far_high}
            for k, plane in entries.items():
                coef_ref[slot, k] = plane

    blocks = cells // 2
    one = zero + 1.0
    for slot in (0, blocks + 1):
        for k in range(10):
            coef_ref[slot, k] = one if k in (3, 6) else zero
        for k in range(2 * PAIRS):
            side_ref[slot, k] = zero
    for slot in (0, blocks // 2 + 1):
        for k in range(12):
            coef2_ref[slot, k] = one if k in (4, 7) else zero
        for k in range(2 * PAIRS):
            side2_ref[slot, k] = zero

    def block_one(slot):
        c = [coef_ref[slot, k] for k in range(10)]
        return (
            (c[0], c[1], None, c[2]),
            (c[3], c[4], c[5], c[6]),
            (c[7], None, c[8], c[9]),
            [side_ref[slot, k] for k in range(2 * PAIRS)],
        )

    def block_two(slot):
        c = [coef2_ref[slot, k] for k in range(12)]
        return (
            tuple(c[0:4]),
            tuple(c[4:8]),
            tuple(c[8:12]),
            [side2_ref[slot, k] for k in range(2 * PAIRS)],
        )

    parity = own_cell & 1
    left = block_one(parity)
    left_inverse = inverse_of(left[1])
    for k in range(blocks // 2):
        right = block_one(parity + 2 * k + 2)
        right_inverse = inverse_of(right[1])
        kept = block_one(parity + 2 * k + 1)
        sub, diag, sup, side = eliminate(kept, left, left_inverse, right, right_inverse)
        for n, plane in enumerate(sub + diag + sup):
            coef2_ref[k + 1, n] = plane
        for n, plane in enumerate(side):
            side2_ref[k + 1, n] = plane
        left, left_inverse = right, right_inverse
    parity = (own_cell >> 1) & 1
    left = block_two(parity)
    left_inverse = inverse_of(left[1])
    for k in range(blocks // 4):
        right = block_two(parity + 2 * k + 2)
        right_inverse = inverse_of(right[1])
        kept = block_two(parity + 2 * k + 1)
        sub, diag, sup, side = eliminate(kept, left, left_inverse, right, right_inverse)
        for n in range(4):
            couple_ref[k, 0, n] = sub[n]
            couple_ref[k, 1, n] = sup[n]
            diag3_ref[k, n] = diag[n]
        for n, plane in enumerate(side):
            side3_ref[k, n] = plane
        left, left_inverse = right, right_inverse
    own = (own_cell >> 2) & 1
    other = 1 - own
    own_couple = tuple(couple_ref[own, 1 - own, n] for n in range(4))
    other_couple = tuple(couple_ref[other, own, n] for n in range(4))
    factor = two_by_two(own_couple, inverse_of([diag3_ref[other, n] for n in range(4)]))
    diag = less([diag3_ref[own, n] for n in range(4)], two_by_two(factor, other_couple))
    last_inverse = inverse_of(diag)
    for k in range(PAIRS):
        other_low, other_high = side3_ref[other, k], side3_ref[other, PAIRS + k]
        low = side3_ref[own, k] - (factor[0] * other_low + factor[1] * other_high)
        high = side3_ref[own, PAIRS + k] - (factor[2] * other_low + factor[3] * other_high)
        for member in range(2):
            delta = last_inverse[2 * member] * low + last_inverse[2 * member + 1] * high
            base = all_ref[own_cell, pl.ds(member * CELL_ROWS + k * ROWS, ROWS), :]
            result = base + delta
            for var in range(2):
                for inst in range(2):
                    for half in range(2):
                        row = rows_of(var, inst, half)
                        out_ref[
                            inst, 2 * k + var, pl.ds(member, 1), pl.ds(half * LANES, LANES)
                        ] = result[row : row + 1]


def gather_inst(block):
    return lax.all_gather(block, "inst", axis=0, tiled=True)


def exchange_cell(copies):
    return lax.all_to_all(copies, "cell", split_axis=0, concat_axis=0, tiled=True)


def local_by_gather(state, pseudo_rate, line_next, face_codes):
    cells = lax.axis_size("cell") * state.shape[2]
    vmem = pl.BlockSpec(memory_space=pltpu.VMEM)
    plane = (ROWS, LANES)
    every = gather_inst(state)
    packed = pl.pallas_call(
        cell_kernel,
        out_shape=jax.ShapeDtypeStruct(
            (lax.axis_size("cell"), BLOCK_ROWS, LANES), jnp.float32
        ),
        in_specs=[vmem, vmem, vmem],
        out_specs=vmem,
        scratch_shapes=[
            pltpu.VMEM((every.shape[0] // 2, 2 * CELL_ROWS, LANES), jnp.float32)
        ],
    )(every, pseudo_rate, line_next.reshape(2, LANES))
    gathered = exchange_cell(packed)
    blocks = cells // 2
    sizes = [
        (blocks + 2, 10),
        (blocks + 2, 2 * PAIRS),
        (blocks // 2 + 2, 12),
        (blocks // 2 + 2, 2 * PAIRS),
        (2, 2, 4),
        (2, 4),
        (2, 2 * PAIRS),
    ]
    return pl.pallas_call(
        functools.partial(line_kernel, cells),
        out_shape=jax.ShapeDtypeStruct(state.shape, jnp.float32),
        in_specs=[vmem, pl.BlockSpec(memory_space=pltpu.SMEM)],
        out_specs=vmem,
        scratch_shapes=[pltpu.VMEM(size + plane, jnp.float32) for size in sizes],
    )(gathered, face_codes)


def solution(mesh):
    placed = (P("inst", None, "cell", None), P("cell", None), P(), P())
    inst_count, cell_count = mesh.shape["inst"], mesh.shape["cell"]

    def local(state, pseudo_rate, line_next, face_codes):
        small = (
            state.shape == (2, 6, 2, 2 * LANES)
            and inst_count * 2 == NT
            and cell_count == 8
            and face_codes.shape[1] * LINES_DEV == state.shape[3]
        )
        chosen = local_by_gather if small else local_by_lines
        return chosen(state, pseudo_rate, line_next, face_codes)

    return jax.shard_map(
        local, mesh=mesh, in_specs=placed, out_specs=P("inst", None, "cell", None), check_vma=False
    )
```

```python
import functools

import jax
import jax.numpy as jnp
import numpy as np
from jax import lax
from jax.experimental import pallas as pl
from jax.experimental.pallas import tpu as pltpu
from jax.sharding import PartitionSpec as P

NT = 8
LINES_DEV = 32


GAMMA_GAS = 1.4
OMEGA_BLADE = 1.0
SENSOR_GAIN = 0.25
FOURTH_GAIN = 0.03125
PITCH_GAIN = 0.5
SECOND_IMPL = 1.0
FOURTH_IMPL = 0.25
FREE_STATE = (1.0, 0.5, 0.0, 0.0, 2.625, 0.2)
MIRROR_SIGNS = (1.0, -1.0, 1.0, 1.0, 1.0, 1.0)
ZERO_BLOCK = (0.0, 0.0, 0.0, 0.0)
UNIT_BLOCK = (1.0, 0.0, 0.0, 1.0)
ZERO_PAIR = (0.0, 0.0)


def extended(block, sides, width):
    for axis, dim in sides:
        count = lax.axis_size(axis)
        forward = [(i, i + 1) for i in range(count - 1)]
        backward = [(target, source) for source, target in forward]
        low = lax.ppermute(
            lax.slice_in_dim(block, block.shape[dim] - width, None, axis=dim), axis, forward
        )
        high = lax.ppermute(lax.slice_in_dim(block, 0, width, axis=dim), axis, backward)
        block = jnp.concatenate([low, block, high], axis=dim)
    return block


def spectral_matrix(instances):
    offsets = np.arange(instances)[:, None] - np.arange(instances)[None, :]
    angles = np.pi * offsets / instances
    safe_sin = np.where(offsets == 0, 1.0, np.sin(angles))
    parity = np.where(np.mod(offsets, 2) == 0, -1.0, 1.0)
    matrix_table = np.where(
        offsets == 0, 0.0, 0.5 * OMEGA_BLADE * parity * np.cos(angles) / safe_sin
    )
    return jnp.asarray(matrix_table, jnp.float32)


def primitive_parts(cells_state):
    density = cells_state[..., 0, :, :]
    inverse = 1.0 / density
    velocity_x = cells_state[..., 1, :, :] * inverse
    velocity_y = cells_state[..., 2, :, :] * inverse
    velocity_z = cells_state[..., 3, :, :] * inverse
    energy = cells_state[..., 4, :, :]
    pressure = (GAMMA_GAS - 1.0) * (
        energy
        - 0.5
        * density
        * (velocity_x * velocity_x + velocity_y * velocity_y + velocity_z * velocity_z)
    )
    sound_speed = jnp.sqrt(GAMMA_GAS * pressure * inverse)
    return (velocity_x, velocity_y, pressure, sound_speed)


def directed_flux(cells_state, normal_velocity, pressure, component):
    zero_plane = jnp.zeros_like(pressure)
    pressure_rows = [
        zero_plane,
        zero_plane,
        zero_plane,
        zero_plane,
        pressure * normal_velocity,
        zero_plane,
    ]
    pressure_rows[component] = pressure
    return cells_state * normal_velocity[..., None, :, :] + jnp.stack(pressure_rows, axis=-3)


def line_residual(padded):
    velocity_x, velocity_y, pressure, sound_speed = primitive_parts(padded)
    flux_line = directed_flux(padded, velocity_x, pressure, 1)
    radius = jnp.abs(velocity_x) + sound_speed
    sensor = jnp.abs(
        pressure[..., 2:, :] - 2.0 * pressure[..., 1:-1, :] + pressure[..., :-2, :]
    ) / (pressure[..., 2:, :] + 2.0 * pressure[..., 1:-1, :] + pressure[..., :-2, :])
    second = SENSOR_GAIN * jnp.maximum(sensor[..., :-1, :], sensor[..., 1:, :])
    fourth = jnp.maximum(0.0, FOURTH_GAIN - second)
    face_radius = 0.5 * (radius[..., 1:-2, :] + radius[..., 2:-1, :])
    left_far = padded[..., :-3, :]
    left_near = padded[..., 1:-2, :]
    right_near = padded[..., 2:-1, :]
    right_far = padded[..., 3:, :]
    damping = face_radius[..., None, :, :] * (
        second[..., None, :, :] * (right_near - left_near)
        - fourth[..., None, :, :] * (right_far - 3.0 * right_near + 3.0 * left_near - left_far)
    )
    face_flux = 0.5 * (flux_line[..., 1:-2, :] + flux_line[..., 2:-1, :]) - damping
    return (face_flux[..., 1:, :] - face_flux[..., :-1, :], radius)


def pitch_parts(cells_state):
    velocity_x, velocity_y, pressure, sound_speed = primitive_parts(cells_state)
    return (directed_flux(cells_state, velocity_y, pressure, 2), jnp.abs(velocity_y) + sound_speed)


def pitch_residual(cells_state, next_lines, prev_lines):
    pitch_flux, radius = pitch_parts(cells_state)
    state_next = jnp.take(cells_state, next_lines, axis=-1)
    flux_next, radius_next = pitch_parts(state_next)
    face_flux = 0.5 * (pitch_flux + flux_next) - PITCH_GAIN * (0.5 * (radius + radius_next))[
        ..., None, :, :
    ] * (state_next - cells_state)
    return face_flux - jnp.take(face_flux, prev_lines, axis=-1)


def boundary_cells(edge_pair, line_codes, lower_end):
    reflected = edge_pair[..., ::-1, :] * jnp.asarray(MIRROR_SIGNS, jnp.float32)[:, None, None]
    if lower_end:
        copied = jnp.concatenate([edge_pair[..., :1, :], edge_pair[..., :1, :]], axis=-2)
    else:
        copied = jnp.concatenate([edge_pair[..., 1:, :], edge_pair[..., 1:, :]], axis=-2)
    inflow = jnp.asarray(FREE_STATE, jnp.float32)[:, None, None] + jnp.zeros_like(edge_pair)
    return jnp.where(line_codes == 0, reflected, jnp.where(line_codes == 1, inflow, copied))


def line_coefficients(radius_ext, diagonal_term, positions, total_cells):
    radius_below = radius_ext[..., :-2, :]
    radius_centre = radius_ext[..., 1:-1, :]
    radius_above = radius_ext[..., 2:, :]
    face_below = 0.5 * (radius_below + radius_centre)
    face_above = 0.5 * (radius_centre + radius_above)
    far_low = FOURTH_IMPL * radius_below
    near_low = -SECOND_IMPL * face_below - 2.0 * FOURTH_IMPL * (radius_below + radius_centre)
    middle = (
        diagonal_term
        + SECOND_IMPL * (face_below + face_above)
        + FOURTH_IMPL * (radius_below + 4.0 * radius_centre + radius_above)
    )
    near_high = -SECOND_IMPL * face_above - 2.0 * FOURTH_IMPL * (radius_centre + radius_above)
    far_high = FOURTH_IMPL * radius_above
    column = positions[:, None]
    far_low = jnp.where(column >= 2, far_low, 0.0)
    near_low = jnp.where(column >= 1, near_low, 0.0)
    near_high = jnp.where(column <= total_cells - 2, near_high, 0.0)
    far_high = jnp.where(column <= total_cells - 3, far_high, 0.0)
    return (far_low, near_low, middle, near_high, far_high)


def block_product(first_matrix, second_matrix):
    return (
        first_matrix[0] * second_matrix[0] + first_matrix[1] * second_matrix[2],
        first_matrix[0] * second_matrix[1] + first_matrix[1] * second_matrix[3],
        first_matrix[2] * second_matrix[0] + first_matrix[3] * second_matrix[2],
        first_matrix[2] * second_matrix[1] + first_matrix[3] * second_matrix[3],
    )


def block_inverse(matrix):
    determinant = matrix[0] * matrix[3] - matrix[1] * matrix[2]
    reciprocal = 1.0 / determinant
    return (
        matrix[3] * reciprocal,
        -matrix[1] * reciprocal,
        -matrix[2] * reciprocal,
        matrix[0] * reciprocal,
    )


def block_apply(matrix, vector):
    return (
        matrix[0] * vector[0] + matrix[1] * vector[1],
        matrix[2] * vector[0] + matrix[3] * vector[1],
    )


def add_blocks(first_members, second_members):
    return tuple((a + b for a, b in zip(first_members, second_members)))


def negate(members):
    return tuple((-a for a in members))


def extend_blocks(members, fill_values):
    return tuple(
        (
            jnp.concatenate([m, jnp.full_like(m[..., :1, :], f)], axis=-2)
            for m, f in zip(members, fill_values)
        )
    )


def shift_next(members, fill_values):
    return tuple(
        (
            jnp.concatenate([m[..., 1:, :], jnp.full_like(m[..., :1, :], f)], axis=-2)
            for m, f in zip(members, fill_values)
        )
    )


def shift_prev(members):
    return tuple(
        (jnp.concatenate([jnp.zeros_like(m[..., :1, :]), m[..., :-1, :]], axis=-2) for m in members)
    )


def pair_split(member):
    shaped = member.reshape(member.shape[:-2] + (member.shape[-2] // 2, 2, member.shape[-1]))
    return (shaped[..., 0, :], shaped[..., 1, :])


def split_parity(members):
    halves = [pair_split(m) for m in members]
    return (tuple((h[0] for h in halves)), tuple((h[1] for h in halves)))


def alternate(first_member, second_member):
    stacked = jnp.stack((first_member, second_member), axis=-2)
    return stacked.reshape(
        first_member.shape[:-2] + (2 * first_member.shape[-2], first_member.shape[-1])
    )


def reduce_blocks(sub_blocks, diag_blocks, super_blocks, right_side):
    block_count = diag_blocks[0].shape[-2]
    if block_count == 1:
        return block_apply(block_inverse(diag_blocks), right_side)
    if block_count % 2 == 1:
        sub_blocks = extend_blocks(sub_blocks, ZERO_BLOCK)
        diag_blocks = extend_blocks(diag_blocks, UNIT_BLOCK)
        super_blocks = extend_blocks(super_blocks, ZERO_BLOCK)
        right_side = extend_blocks(right_side, ZERO_PAIR)
    sub_even, sub_odd = split_parity(sub_blocks)
    diag_even, diag_odd = split_parity(diag_blocks)
    super_even, super_odd = split_parity(super_blocks)
    side_even, side_odd = split_parity(right_side)
    inverse_even = block_inverse(diag_even)
    inverse_next = shift_next(inverse_even, UNIT_BLOCK)
    sub_next = shift_next(sub_even, ZERO_BLOCK)
    super_next = shift_next(super_even, ZERO_BLOCK)
    side_next = shift_next(side_even, ZERO_PAIR)
    left_factor = negate(block_product(sub_odd, inverse_even))
    right_factor = negate(block_product(super_odd, inverse_next))
    reduced_sub = block_product(left_factor, sub_even)
    reduced_diag = add_blocks(
        diag_odd,
        add_blocks(block_product(left_factor, super_even), block_product(right_factor, sub_next)),
    )
    reduced_super = block_product(right_factor, super_next)
    reduced_side = add_blocks(
        side_odd,
        add_blocks(block_apply(left_factor, side_even), block_apply(right_factor, side_next)),
    )
    odd_values = reduce_blocks(reduced_sub, reduced_diag, reduced_super, reduced_side)
    before_values = shift_prev(odd_values)
    remainder = add_blocks(
        side_even,
        negate(
            add_blocks(block_apply(sub_even, before_values), block_apply(super_even, odd_values))
        ),
    )
    even_values = block_apply(inverse_even, remainder)
    merged = tuple((alternate(e, o) for e, o in zip(even_values, odd_values)))
    return tuple((m[..., :block_count, :] for m in merged))


def cells_leading(block):
    moved = jnp.transpose(block, (2, 0, 1, 3))
    return moved.reshape(block.shape[2], block.shape[0] * block.shape[1] * block.shape[3])


def solve_in_lanes(coefficients, line_source):
    source_shape = line_source.shape
    lane_coef = [cells_leading(jnp.broadcast_to(c[:, None], source_shape)) for c in coefficients]
    pairs_list = [pair_split(m) for m in lane_coef]
    zero_plane = jnp.zeros_like(pairs_list[2][0])
    sub_blocks = (pairs_list[0][0], pairs_list[1][0], zero_plane, pairs_list[0][1])
    diag_blocks = (pairs_list[2][0], pairs_list[3][0], pairs_list[1][1], pairs_list[2][1])
    super_blocks = (pairs_list[4][0], zero_plane, pairs_list[3][1], pairs_list[4][1])
    values = reduce_blocks(
        sub_blocks, diag_blocks, super_blocks, pair_split(cells_leading(line_source))
    )
    flat = alternate(values[0], values[1])
    shaped = flat.reshape(source_shape[2], source_shape[0], source_shape[1], source_shape[3])
    return jnp.transpose(shaped, (1, 2, 0, 3))


def return_tiles(line_values):
    return lax.all_to_all(line_values, "cell", split_axis=2, concat_axis=3, tiled=True)


def local_by_lines(state, pseudo_rate, line_next, face_codes):
    local_count = state.shape[0]
    tile_cells = state.shape[2]
    cell_index = lax.axis_index("cell")
    cell_count = lax.axis_size("cell")
    total_cells = tile_cells * cell_count
    spectral = spectral_matrix(NT)
    first_local = lax.axis_index("inst") * local_count
    own_rows = lax.dynamic_slice_in_dim(spectral, first_local, local_count, 0)
    shard_block = jax.tree.map(lambda a: lax.all_gather(a, "inst", axis=0, tiled=True), state)
    columns = lax.slice_in_dim(own_rows, 0, shard_block.shape[0], axis=1)
    time_term = jnp.zeros_like(state) + jnp.einsum(
        "nm,mvil->nvil", columns, shard_block, precision=lax.Precision.HIGHEST
    )
    padded = extended(state, (("cell", 2),), 2)
    codes_lines = jnp.repeat(face_codes, LINES_DEV, axis=1)
    lower_ghost = boundary_cells(state[:, :, 0:2, :], codes_lines[0], True)
    upper_ghost = boundary_cells(state[:, :, -2:, :], codes_lines[1], False)
    lower_rim = jnp.where(cell_index == 0, lower_ghost, padded[:, :, :2, :])
    upper_rim = jnp.where(cell_index == cell_count - 1, upper_ghost, padded[:, :, -2:, :])
    padded = jnp.concatenate([lower_rim, padded[:, :, 2:-2, :], upper_rim], axis=2)
    line_part, radius = line_residual(padded)
    prev_lines = (
        jnp.zeros_like(line_next).at[line_next].set(jnp.arange(line_next.shape[0], dtype=jnp.int32))
    )
    residual = line_part + pitch_residual(state, line_next, prev_lines) + time_term
    right_side = -residual
    centre_radius = radius[:, 2:-2, :]
    diagonal_term = pseudo_rate * centre_radius
    positions = cell_index * tile_cells + jnp.arange(-1, tile_cells + 1, dtype=jnp.int32)
    inside = (positions >= 0) & (positions < total_cells)
    radius_ext = jnp.where(inside[:, None], radius[:, 1:-1, :], 0.0)
    coefficients = line_coefficients(radius_ext, diagonal_term, positions[1:-1], total_cells)
    stacked = jnp.stack(coefficients, axis=1)
    line_source = lax.all_to_all(right_side, "cell", split_axis=3, concat_axis=2, tiled=True)
    line_coef = lax.all_to_all(stacked, "cell", split_axis=3, concat_axis=2, tiled=True)
    update = return_tiles(solve_in_lanes(tuple((line_coef[:, k] for k in range(5))), line_source))
    return state + update


LANES = 128
ROWS = 8
PAIRS = 3
CELL_ROWS = PAIRS * ROWS
REST_ROW = 2 * CELL_ROWS
RATE_ROW = 2 * REST_ROW
BLOCK_ROWS = RATE_ROW + ROWS


def spectral_offsets():
    table = np.zeros(NT)
    for offset in range(1, NT):
        angle = np.pi * offset / NT
        parity = -1.0 if offset % 2 == 0 else 1.0
        table[offset] = 0.5 * OMEGA_BLADE * parity * np.cos(angle) / np.sin(angle)
    return [float(np.float32(value)) for value in table]


def plane_masks():
    row_index = lax.broadcasted_iota(jnp.int32, (ROWS, LANES), 0)
    return row_index < 4, (row_index & 2) == 0, row_index & 1


def both(first_var, plane):
    turned = pltpu.roll(plane, 4, 0)
    return jnp.where(first_var, plane, turned), jnp.where(first_var, turned, plane)


def primitives(first_var, planes):
    density, moment_x = both(first_var, planes[0])
    moment_y, moment_z = both(first_var, planes[1])
    energy = jnp.where(first_var, planes[2], pltpu.roll(planes[2], 4, 0))
    inverse = 1.0 / density
    velocity_x = moment_x * inverse
    velocity_y = moment_y * inverse
    velocity_z = moment_z * inverse
    kinetic = moment_x * velocity_x + moment_y * velocity_y + moment_z * velocity_z
    pressure = (GAMMA_GAS - 1.0) * (energy - 0.5 * kinetic)
    sound = jnp.sqrt(GAMMA_GAS * pressure * inverse)
    return velocity_x, velocity_y, pressure, sound


def rows_of(var, inst, half):
    return (var // 2) * ROWS + (var % 2) * 4 + inst * 2 + half


def cell_kernel(all_ref, rate_ref, next_ref, out_ref, plane_ref):
    own_inst = lax.axis_index("inst")
    inst_count = all_ref.shape[0] // 2
    shape = (ROWS, LANES)
    lane_index = lax.broadcasted_iota(jnp.int32, shape, 1)
    first_var, first_inst, half_index = plane_masks()
    first_half = half_index == 0

    next_rows = [next_ref[pl.ds(half, 1), :] for half in range(2)]
    next_line = jnp.where(first_half, next_rows[0], next_rows[1])
    column = lax.broadcasted_iota(jnp.int32, (LANES, LANES), 0)
    prev_halves = []
    for target in range(2):
        total = None
        for source in range(2):
            hits = jnp.where(column + target * LANES == next_rows[source], 1.0, 0.0)
            names = (lane_index + source * LANES).astype(jnp.float32)
            part = lax.dot_general(
                names, hits, (((1,), (1,)), ((), ())), preferred_element_type=jnp.float32
            )
            total = part if total is None else total + part
        prev_halves.append(total)
    prev_line = jnp.where(first_half, prev_halves[0], prev_halves[1]).astype(jnp.int32)

    def picker(lines):
        lane = lines & (LANES - 1)
        same = (lines >> 7) == half_index

        def pick(plane):
            swapped = jnp.where(first_half, pltpu.roll(plane, 7, 0), pltpu.roll(plane, 1, 0))
            here = jnp.take_along_axis(plane, lane, axis=1, mode="promise_in_bounds")
            there = jnp.take_along_axis(swapped, lane, axis=1, mode="promise_in_bounds")
            return jnp.where(same, here, there)

        return pick

    pick_next = picker(next_line)
    pick_prev = picker(prev_line)

    for shift in range(inst_count):
        pair = (own_inst - shift) & (inst_count - 1)
        for cell in range(2):
            for var in range(6):
                for inst in range(2):
                    for half in range(2):
                        row = cell * CELL_ROWS + rows_of(var, inst, half)
                        plane_ref[shift, pl.ds(row, 1), :] = all_ref[
                            2 * pair + inst, var, pl.ds(cell, 1), pl.ds(half * LANES, LANES)
                        ]
    offsets = spectral_offsets()

    def time_parts(cell):
        same_total = [None] * PAIRS
        other_total = [None] * PAIRS
        for shift in range(inst_count):
            same = offsets[(2 * shift) % NT]
            other = jnp.where(
                first_inst, offsets[(2 * shift + 1) % NT], offsets[(2 * shift - 1) % NT]
            )
            for k in range(PAIRS):
                plane = plane_ref[shift, pl.ds(cell * CELL_ROWS + k * ROWS, ROWS), :]
                if shift > 0:
                    term = same * plane
                    same_total[k] = term if same_total[k] is None else same_total[k] + term
                term = other * plane
                other_total[k] = term if other_total[k] is None else other_total[k] + term
        return [
            s + jnp.where(first_inst, pltpu.roll(o, 6, 0), pltpu.roll(o, 2, 0))
            for s, o in zip(same_total, other_total)
        ]

    def flux_across(planes, velocity, pressure):
        return [
            planes[0] * velocity,
            planes[1] * velocity + jnp.where(first_var, pressure, 0.0),
            planes[2] * velocity + jnp.where(first_var, pressure * velocity, 0.0),
        ]

    for cell in range(2):
        planes = [
            plane_ref[0, pl.ds(cell * CELL_ROWS + k * ROWS, ROWS), :] for k in range(PAIRS)
        ]
        nearby = [pick_next(plane) for plane in planes]
        _, velocity, pressure, sound = primitives(first_var, planes)
        _, next_velocity, next_pressure, next_sound = primitives(first_var, nearby)
        own_flux = flux_across(planes, velocity, pressure)
        next_flux = flux_across(nearby, next_velocity, next_pressure)
        weight = (PITCH_GAIN * 0.5) * (
            jnp.abs(velocity) + sound + (jnp.abs(next_velocity) + next_sound)
        )
        time_term = time_parts(cell)
        for k in range(PAIRS):
            face = 0.5 * (own_flux[k] + next_flux[k]) - weight * (nearby[k] - planes[k])
            rest = time_term[k] + (face - pick_prev(face))
            row = cell * CELL_ROWS + k * ROWS
            out_ref[pl.ds(row, ROWS), :] = planes[k]
            out_ref[pl.ds(REST_ROW + row, ROWS), :] = rest
        for half in range(2):
            out_ref[pl.ds(RATE_ROW + cell * 2 + half, 1), :] = rate_ref[
                pl.ds(cell, 1), pl.ds(half * LANES, LANES)
            ]
    out_ref[pl.ds(RATE_ROW + 4, 4), :] = jnp.zeros((4, LANES), jnp.float32)


def two_by_two(first, second):
    def entry(a, b, c, d):
        terms = [x * y for x, y in ((a, b), (c, d)) if x is not None and y is not None]
        return None if not terms else terms[0] if len(terms) == 1 else terms[0] + terms[1]

    return (
        entry(first[0], second[0], first[1], second[2]),
        entry(first[0], second[1], first[1], second[3]),
        entry(first[2], second[0], first[3], second[2]),
        entry(first[2], second[1], first[3], second[3]),
    )


def inverse_of(matrix):
    reciprocal = 1.0 / (matrix[0] * matrix[3] - matrix[1] * matrix[2])
    return (
        matrix[3] * reciprocal,
        -(matrix[1] * reciprocal),
        -(matrix[2] * reciprocal),
        matrix[0] * reciprocal,
    )


def less(first, second):
    return tuple(a if b is None else a - b for a, b in zip(first, second))


def minus(members):
    return tuple(None if a is None else -a for a in members)


def eliminate(centre, left, left_inverse, right, right_inverse):
    left_factor = two_by_two(centre[0], left_inverse)
    right_factor = two_by_two(centre[2], right_inverse)
    sub = minus(two_by_two(left_factor, left[0]))
    diag = less(
        less(centre[1], two_by_two(left_factor, left[2])), two_by_two(right_factor, right[0])
    )
    sup = minus(two_by_two(right_factor, right[2]))
    side = []
    for k in range(PAIRS):
        for row in range(2):
            value = centre[3][row * PAIRS + k]
            for factor, other in ((left_factor, left[3]), (right_factor, right[3])):
                value = value - (
                    factor[2 * row] * other[k] + factor[2 * row + 1] * other[PAIRS + k]
                )
            side.append((row * PAIRS + k, value))
    return sub, diag, sup, [value for _, value in sorted(side, key=lambda item: item[0])]


def line_kernel(
    cells, all_ref, codes_ref, out_ref, coef_ref, side_ref, coef2_ref, side2_ref,
    couple_ref, diag3_ref, side3_ref,
):
    own_cell = lax.axis_index("cell")
    order = ring_order(cells // 2)
    own_place = jnp.where(
        own_cell & 1 == 0, own_cell >> 1, cells // 2 - 1 - (own_cell >> 1)
    )
    shape = (ROWS, LANES)
    lane_index = lax.broadcasted_iota(jnp.int32, shape, 1)
    first_var, _, half_index = plane_masks()
    first_half = half_index == 0
    zero = jnp.zeros(shape, jnp.float32)

    tile = half_index * (LANES // LINES_DEV) + lane_index // LINES_DEV
    codes = []
    for end in range(2):
        plane = jnp.zeros(shape, jnp.int32)
        for k in range(2 * LANES // LINES_DEV):
            plane = jnp.where(tile == k, codes_ref[end, k], plane)
        codes.append(plane)

    def loaded(cell, start=0):
        return [
            all_ref[order.index(cell // 2), pl.ds(start + (cell % 2) * CELL_ROWS + k * ROWS, ROWS), :]
            for k in range(PAIRS)
        ]

    def ghost(end, mirrored, copied):
        planes = []
        for k in range(PAIRS):
            reflected = mirrored[k]
            if k == 0:
                reflected = jnp.where(first_var, reflected, -reflected)
            inflow = jnp.where(first_var, FREE_STATE[2 * k], FREE_STATE[2 * k + 1])
            planes.append(
                jnp.where(
                    codes[end] == 0, reflected, jnp.where(codes[end] == 1, inflow, copied[k])
                )
            )
        return planes

    def extended_state(cell):
        if cell < 0:
            return ghost(0, loaded(-1 - cell), loaded(0))
        if cell >= cells:
            return ghost(
                1, loaded(2 * cells - 1 - cell), loaded(cells - 1)
            )
        return loaded(cell)

    def flux_along(planes, velocity, pressure):
        return [
            planes[0] * velocity + jnp.where(first_var, 0.0, pressure),
            planes[1] * velocity,
            planes[2] * velocity + jnp.where(first_var, pressure * velocity, 0.0),
        ]

    state, pressures, radii, fluxes, steps, sensors, faces = {}, {}, {}, {}, {}, {}, {}
    for cell in range(-2, cells + 2):
        planes = extended_state(cell)
        velocity_x, _, pressure, sound = primitives(first_var, planes)
        state[cell] = planes
        pressures[cell] = pressure
        radii[cell] = jnp.abs(velocity_x) + sound
        if -1 <= cell <= cells:
            fluxes[cell] = flux_along(planes, velocity_x, pressure)
        if cell >= -1:
            steps[cell - 1] = [a - b for a, b in zip(planes, state[cell - 1])]
        if cell >= 0:
            twice = 2.0 * pressures[cell - 1]
            outer = pressure + pressures[cell - 2]
            sensors[cell - 1] = jnp.abs(outer - twice) / (outer + twice)
        if cell >= 1:
            face = cell - 2
            second = SENSOR_GAIN * jnp.maximum(sensors[face], sensors[face + 1])
            fourth = jnp.maximum(0.0, FOURTH_GAIN - second)
            face_radius = 0.5 * (radii[face] + radii[face + 1])
            near_weight = face_radius * (second + 2.0 * fourth)
            far_weight = face_radius * fourth
            faces[face] = [
                0.5 * (fluxes[face][k] + fluxes[face + 1][k])
                - (
                    near_weight * steps[face][k]
                    - far_weight * (steps[face + 1][k] + steps[face - 1][k])
                )
                for k in range(PAIRS)
            ]
        if cell >= 2:
            at = cell - 2
            slot, member = at // 2 + 1, at % 2
            rest = loaded(at, REST_ROW)
            for k in range(PAIRS):
                side_ref[slot, member * PAIRS + k] = (
                    faces[at - 1][k] - faces[at][k] - rest[k]
                )
            below = radii[at - 1] if at > 0 else zero
            centre = radii[at]
            above = radii[at + 1] if at < cells - 1 else zero
            below_sum = below + centre
            above_sum = centre + above
            half_low = SECOND_IMPL * 0.5 + 2.0 * FOURTH_IMPL
            rate_rows = [
                all_ref[order.index(at // 2), pl.ds(RATE_ROW + member * 2 + half, 1), :]
                for half in range(2)
            ]
            rate = jnp.where(first_half, rate_rows[0], rate_rows[1])
            middle = (
                rate * centre
                + SECOND_IMPL * (0.5 * (below_sum + above_sum))
                + FOURTH_IMPL * (below + 4.0 * centre + above)
            )
            far_low = FOURTH_IMPL * below if at >= 2 else zero
            near_low = -half_low * below_sum if at >= 1 else zero
            near_high = -half_low * above_sum if at <= cells - 2 else zero
            far_high = FOURTH_IMPL * above if at <= cells - 3 else zero
            if member == 0:
                entries = {0: far_low, 1: near_low, 3: middle, 4: near_high, 7: far_high}
            else:
                entries = {2: far_low, 5: near_low, 6: middle, 8: near_high, 9: far_high}
            for k, plane in entries.items():
                coef_ref[slot, k] = plane

    blocks = cells // 2
    one = zero + 1.0
    for slot in (0, blocks + 1):
        for k in range(10):
            coef_ref[slot, k] = one if k in (3, 6) else zero
        for k in range(2 * PAIRS):
            side_ref[slot, k] = zero
    for slot in (0, blocks // 2 + 1):
        for k in range(12):
            coef2_ref[slot, k] = one if k in (4, 7) else zero
        for k in range(2 * PAIRS):
            side2_ref[slot, k] = zero

    def block_one(slot):
        c = [coef_ref[slot, k] for k in range(10)]
        return (
            (c[0], c[1], None, c[2]),
            (c[3], c[4], c[5], c[6]),
            (c[7], None, c[8], c[9]),
            [side_ref[slot, k] for k in range(2 * PAIRS)],
        )

    def block_two(slot):
        c = [coef2_ref[slot, k] for k in range(12)]
        return (
            tuple(c[0:4]),
            tuple(c[4:8]),
            tuple(c[8:12]),
            [side2_ref[slot, k] for k in range(2 * PAIRS)],
        )

    parity = own_cell & 1
    left = block_one(parity)
    left_inverse = inverse_of(left[1])
    for k in range(blocks // 2):
        right = block_one(parity + 2 * k + 2)
        right_inverse = inverse_of(right[1])
        kept = block_one(parity + 2 * k + 1)
        sub, diag, sup, side = eliminate(kept, left, left_inverse, right, right_inverse)
        for n, plane in enumerate(sub + diag + sup):
            coef2_ref[k + 1, n] = plane
        for n, plane in enumerate(side):
            side2_ref[k + 1, n] = plane
        left, left_inverse = right, right_inverse
    parity = (own_cell >> 1) & 1
    left = block_two(parity)
    left_inverse = inverse_of(left[1])
    for k in range(blocks // 4):
        right = block_two(parity + 2 * k + 2)
        right_inverse = inverse_of(right[1])
        kept = block_two(parity + 2 * k + 1)
        sub, diag, sup, side = eliminate(kept, left, left_inverse, right, right_inverse)
        for n in range(4):
            couple_ref[k, 0, n] = sub[n]
            couple_ref[k, 1, n] = sup[n]
            diag3_ref[k, n] = diag[n]
        for n, plane in enumerate(side):
            side3_ref[k, n] = plane
        left, left_inverse = right, right_inverse
    own = (own_cell >> 2) & 1
    other = 1 - own
    own_couple = tuple(couple_ref[own, 1 - own, n] for n in range(4))
    other_couple = tuple(couple_ref[other, own, n] for n in range(4))
    factor = two_by_two(own_couple, inverse_of([diag3_ref[other, n] for n in range(4)]))
    diag = less([diag3_ref[own, n] for n in range(4)], two_by_two(factor, other_couple))
    last_inverse = inverse_of(diag)
    for k in range(PAIRS):
        other_low, other_high = side3_ref[other, k], side3_ref[other, PAIRS + k]
        low = side3_ref[own, k] - (factor[0] * other_low + factor[1] * other_high)
        high = side3_ref[own, PAIRS + k] - (factor[2] * other_low + factor[3] * other_high)
        for member in range(2):
            delta = last_inverse[2 * member] * low + last_inverse[2 * member + 1] * high
            base = all_ref[own_place, pl.ds(member * CELL_ROWS + k * ROWS, ROWS), :]
            result = base + delta
            for var in range(2):
                for inst in range(2):
                    for half in range(2):
                        row = rows_of(var, inst, half)
                        out_ref[
                            inst, 2 * k + var, pl.ds(member, 1), pl.ds(half * LANES, LANES)
                        ] = result[row : row + 1]


def gather_inst(block):
    return lax.all_gather(block, "inst", axis=0, tiled=True)


def ring_order(count):
    return list(range(0, count, 2)) + list(range(count - 1, 0, -2))


def gather_cell(block):
    planes = block.reshape(BLOCK_ROWS // ROWS, ROWS, LANES)
    order = [ring_order(lax.axis_size("cell"))]
    return lax.all_gather(planes, "cell", axis=0, tiled=True, axis_index_groups=order)


def local_by_gather(state, pseudo_rate, line_next, face_codes):
    cells = lax.axis_size("cell") * state.shape[2]
    vmem = pl.BlockSpec(memory_space=pltpu.VMEM)
    plane = (ROWS, LANES)
    every = gather_inst(state)
    packed = pl.pallas_call(
        cell_kernel,
        out_shape=jax.ShapeDtypeStruct((BLOCK_ROWS, LANES), jnp.float32),
        in_specs=[vmem, vmem, vmem],
        out_specs=vmem,
        scratch_shapes=[
            pltpu.VMEM((every.shape[0] // 2, 2 * CELL_ROWS, LANES), jnp.float32)
        ],
    )(every, pseudo_rate, line_next.reshape(2, LANES))
    gathered = gather_cell(packed).reshape(-1, BLOCK_ROWS, LANES)
    blocks = cells // 2
    sizes = [
        (blocks + 2, 10),
        (blocks + 2, 2 * PAIRS),
        (blocks // 2 + 2, 12),
        (blocks // 2 + 2, 2 * PAIRS),
        (2, 2, 4),
        (2, 4),
        (2, 2 * PAIRS),
    ]
    return pl.pallas_call(
        functools.partial(line_kernel, cells),
        out_shape=jax.ShapeDtypeStruct(state.shape, jnp.float32),
        in_specs=[vmem, pl.BlockSpec(memory_space=pltpu.SMEM)],
        out_specs=vmem,
        scratch_shapes=[pltpu.VMEM(size + plane, jnp.float32) for size in sizes],
    )(gathered, face_codes)


def solution(mesh):
    placed = (P("inst", None, "cell", None), P("cell", None), P(), P())
    inst_count, cell_count = mesh.shape["inst"], mesh.shape["cell"]

    def local(state, pseudo_rate, line_next, face_codes):
        small = (
            state.shape == (2, 6, 2, 2 * LANES)
            and inst_count * 2 == NT
            and cell_count == 8
            and face_codes.shape[1] * LINES_DEV == state.shape[3]
        )
        chosen = local_by_gather if small else local_by_lines
        return chosen(state, pseudo_rate, line_next, face_codes)

    return jax.shard_map(
        local, mesh=mesh, in_specs=placed, out_specs=P("inst", None, "cell", None), check_vma=False
    )
```

```python
import functools

import jax
import jax.numpy as jnp
import numpy as np
from jax import lax
from jax.experimental import pallas as pl
from jax.experimental.pallas import tpu as pltpu
from jax.sharding import PartitionSpec as P

NT = 8
LINES_DEV = 32


GAMMA_GAS = 1.4
OMEGA_BLADE = 1.0
SENSOR_GAIN = 0.25
FOURTH_GAIN = 0.03125
PITCH_GAIN = 0.5
SECOND_IMPL = 1.0
FOURTH_IMPL = 0.25
FREE_STATE = (1.0, 0.5, 0.0, 0.0, 2.625, 0.2)
MIRROR_SIGNS = (1.0, -1.0, 1.0, 1.0, 1.0, 1.0)
ZERO_BLOCK = (0.0, 0.0, 0.0, 0.0)
UNIT_BLOCK = (1.0, 0.0, 0.0, 1.0)
ZERO_PAIR = (0.0, 0.0)


def extended(block, sides, width):
    for axis, dim in sides:
        count = lax.axis_size(axis)
        forward = [(i, i + 1) for i in range(count - 1)]
        backward = [(target, source) for source, target in forward]
        low = lax.ppermute(
            lax.slice_in_dim(block, block.shape[dim] - width, None, axis=dim), axis, forward
        )
        high = lax.ppermute(lax.slice_in_dim(block, 0, width, axis=dim), axis, backward)
        block = jnp.concatenate([low, block, high], axis=dim)
    return block


def spectral_matrix(instances):
    offsets = np.arange(instances)[:, None] - np.arange(instances)[None, :]
    angles = np.pi * offsets / instances
    safe_sin = np.where(offsets == 0, 1.0, np.sin(angles))
    parity = np.where(np.mod(offsets, 2) == 0, -1.0, 1.0)
    matrix_table = np.where(
        offsets == 0, 0.0, 0.5 * OMEGA_BLADE * parity * np.cos(angles) / safe_sin
    )
    return jnp.asarray(matrix_table, jnp.float32)


def primitive_parts(cells_state):
    density = cells_state[..., 0, :, :]
    inverse = 1.0 / density
    velocity_x = cells_state[..., 1, :, :] * inverse
    velocity_y = cells_state[..., 2, :, :] * inverse
    velocity_z = cells_state[..., 3, :, :] * inverse
    energy = cells_state[..., 4, :, :]
    pressure = (GAMMA_GAS - 1.0) * (
        energy
        - 0.5
        * density
        * (velocity_x * velocity_x + velocity_y * velocity_y + velocity_z * velocity_z)
    )
    sound_speed = jnp.sqrt(GAMMA_GAS * pressure * inverse)
    return (velocity_x, velocity_y, pressure, sound_speed)


def directed_flux(cells_state, normal_velocity, pressure, component):
    zero_plane = jnp.zeros_like(pressure)
    pressure_rows = [
        zero_plane,
        zero_plane,
        zero_plane,
        zero_plane,
        pressure * normal_velocity,
        zero_plane,
    ]
    pressure_rows[component] = pressure
    return cells_state * normal_velocity[..., None, :, :] + jnp.stack(pressure_rows, axis=-3)


def line_residual(padded):
    velocity_x, velocity_y, pressure, sound_speed = primitive_parts(padded)
    flux_line = directed_flux(padded, velocity_x, pressure, 1)
    radius = jnp.abs(velocity_x) + sound_speed
    sensor = jnp.abs(
        pressure[..., 2:, :] - 2.0 * pressure[..., 1:-1, :] + pressure[..., :-2, :]
    ) / (pressure[..., 2:, :] + 2.0 * pressure[..., 1:-1, :] + pressure[..., :-2, :])
    second = SENSOR_GAIN * jnp.maximum(sensor[..., :-1, :], sensor[..., 1:, :])
    fourth = jnp.maximum(0.0, FOURTH_GAIN - second)
    face_radius = 0.5 * (radius[..., 1:-2, :] + radius[..., 2:-1, :])
    left_far = padded[..., :-3, :]
    left_near = padded[..., 1:-2, :]
    right_near = padded[..., 2:-1, :]
    right_far = padded[..., 3:, :]
    damping = face_radius[..., None, :, :] * (
        second[..., None, :, :] * (right_near - left_near)
        - fourth[..., None, :, :] * (right_far - 3.0 * right_near + 3.0 * left_near - left_far)
    )
    face_flux = 0.5 * (flux_line[..., 1:-2, :] + flux_line[..., 2:-1, :]) - damping
    return (face_flux[..., 1:, :] - face_flux[..., :-1, :], radius)


def pitch_parts(cells_state):
    velocity_x, velocity_y, pressure, sound_speed = primitive_parts(cells_state)
    return (directed_flux(cells_state, velocity_y, pressure, 2), jnp.abs(velocity_y) + sound_speed)


def pitch_residual(cells_state, next_lines, prev_lines):
    pitch_flux, radius = pitch_parts(cells_state)
    state_next = jnp.take(cells_state, next_lines, axis=-1)
    flux_next, radius_next = pitch_parts(state_next)
    face_flux = 0.5 * (pitch_flux + flux_next) - PITCH_GAIN * (0.5 * (radius + radius_next))[
        ..., None, :, :
    ] * (state_next - cells_state)
    return face_flux - jnp.take(face_flux, prev_lines, axis=-1)


def boundary_cells(edge_pair, line_codes, lower_end):
    reflected = edge_pair[..., ::-1, :] * jnp.asarray(MIRROR_SIGNS, jnp.float32)[:, None, None]
    if lower_end:
        copied = jnp.concatenate([edge_pair[..., :1, :], edge_pair[..., :1, :]], axis=-2)
    else:
        copied = jnp.concatenate([edge_pair[..., 1:, :], edge_pair[..., 1:, :]], axis=-2)
    inflow = jnp.asarray(FREE_STATE, jnp.float32)[:, None, None] + jnp.zeros_like(edge_pair)
    return jnp.where(line_codes == 0, reflected, jnp.where(line_codes == 1, inflow, copied))


def line_coefficients(radius_ext, diagonal_term, positions, total_cells):
    radius_below = radius_ext[..., :-2, :]
    radius_centre = radius_ext[..., 1:-1, :]
    radius_above = radius_ext[..., 2:, :]
    face_below = 0.5 * (radius_below + radius_centre)
    face_above = 0.5 * (radius_centre + radius_above)
    far_low = FOURTH_IMPL * radius_below
    near_low = -SECOND_IMPL * face_below - 2.0 * FOURTH_IMPL * (radius_below + radius_centre)
    middle = (
        diagonal_term
        + SECOND_IMPL * (face_below + face_above)
        + FOURTH_IMPL * (radius_below + 4.0 * radius_centre + radius_above)
    )
    near_high = -SECOND_IMPL * face_above - 2.0 * FOURTH_IMPL * (radius_centre + radius_above)
    far_high = FOURTH_IMPL * radius_above
    column = positions[:, None]
    far_low = jnp.where(column >= 2, far_low, 0.0)
    near_low = jnp.where(column >= 1, near_low, 0.0)
    near_high = jnp.where(column <= total_cells - 2, near_high, 0.0)
    far_high = jnp.where(column <= total_cells - 3, far_high, 0.0)
    return (far_low, near_low, middle, near_high, far_high)


def block_product(first_matrix, second_matrix):
    return (
        first_matrix[0] * second_matrix[0] + first_matrix[1] * second_matrix[2],
        first_matrix[0] * second_matrix[1] + first_matrix[1] * second_matrix[3],
        first_matrix[2] * second_matrix[0] + first_matrix[3] * second_matrix[2],
        first_matrix[2] * second_matrix[1] + first_matrix[3] * second_matrix[3],
    )


def block_inverse(matrix):
    determinant = matrix[0] * matrix[3] - matrix[1] * matrix[2]
    reciprocal = 1.0 / determinant
    return (
        matrix[3] * reciprocal,
        -matrix[1] * reciprocal,
        -matrix[2] * reciprocal,
        matrix[0] * reciprocal,
    )


def block_apply(matrix, vector):
    return (
        matrix[0] * vector[0] + matrix[1] * vector[1],
        matrix[2] * vector[0] + matrix[3] * vector[1],
    )


def add_blocks(first_members, second_members):
    return tuple((a + b for a, b in zip(first_members, second_members)))


def negate(members):
    return tuple((-a for a in members))


def extend_blocks(members, fill_values):
    return tuple(
        (
            jnp.concatenate([m, jnp.full_like(m[..., :1, :], f)], axis=-2)
            for m, f in zip(members, fill_values)
        )
    )


def shift_next(members, fill_values):
    return tuple(
        (
            jnp.concatenate([m[..., 1:, :], jnp.full_like(m[..., :1, :], f)], axis=-2)
            for m, f in zip(members, fill_values)
        )
    )


def shift_prev(members):
    return tuple(
        (jnp.concatenate([jnp.zeros_like(m[..., :1, :]), m[..., :-1, :]], axis=-2) for m in members)
    )


def pair_split(member):
    shaped = member.reshape(member.shape[:-2] + (member.shape[-2] // 2, 2, member.shape[-1]))
    return (shaped[..., 0, :], shaped[..., 1, :])


def split_parity(members):
    halves = [pair_split(m) for m in members]
    return (tuple((h[0] for h in halves)), tuple((h[1] for h in halves)))


def alternate(first_member, second_member):
    stacked = jnp.stack((first_member, second_member), axis=-2)
    return stacked.reshape(
        first_member.shape[:-2] + (2 * first_member.shape[-2], first_member.shape[-1])
    )


def reduce_blocks(sub_blocks, diag_blocks, super_blocks, right_side):
    block_count = diag_blocks[0].shape[-2]
    if block_count == 1:
        return block_apply(block_inverse(diag_blocks), right_side)
    if block_count % 2 == 1:
        sub_blocks = extend_blocks(sub_blocks, ZERO_BLOCK)
        diag_blocks = extend_blocks(diag_blocks, UNIT_BLOCK)
        super_blocks = extend_blocks(super_blocks, ZERO_BLOCK)
        right_side = extend_blocks(right_side, ZERO_PAIR)
    sub_even, sub_odd = split_parity(sub_blocks)
    diag_even, diag_odd = split_parity(diag_blocks)
    super_even, super_odd = split_parity(super_blocks)
    side_even, side_odd = split_parity(right_side)
    inverse_even = block_inverse(diag_even)
    inverse_next = shift_next(inverse_even, UNIT_BLOCK)
    sub_next = shift_next(sub_even, ZERO_BLOCK)
    super_next = shift_next(super_even, ZERO_BLOCK)
    side_next = shift_next(side_even, ZERO_PAIR)
    left_factor = negate(block_product(sub_odd, inverse_even))
    right_factor = negate(block_product(super_odd, inverse_next))
    reduced_sub = block_product(left_factor, sub_even)
    reduced_diag = add_blocks(
        diag_odd,
        add_blocks(block_product(left_factor, super_even), block_product(right_factor, sub_next)),
    )
    reduced_super = block_product(right_factor, super_next)
    reduced_side = add_blocks(
        side_odd,
        add_blocks(block_apply(left_factor, side_even), block_apply(right_factor, side_next)),
    )
    odd_values = reduce_blocks(reduced_sub, reduced_diag, reduced_super, reduced_side)
    before_values = shift_prev(odd_values)
    remainder = add_blocks(
        side_even,
        negate(
            add_blocks(block_apply(sub_even, before_values), block_apply(super_even, odd_values))
        ),
    )
    even_values = block_apply(inverse_even, remainder)
    merged = tuple((alternate(e, o) for e, o in zip(even_values, odd_values)))
    return tuple((m[..., :block_count, :] for m in merged))


def cells_leading(block):
    moved = jnp.transpose(block, (2, 0, 1, 3))
    return moved.reshape(block.shape[2], block.shape[0] * block.shape[1] * block.shape[3])


def solve_in_lanes(coefficients, line_source):
    source_shape = line_source.shape
    lane_coef = [cells_leading(jnp.broadcast_to(c[:, None], source_shape)) for c in coefficients]
    pairs_list = [pair_split(m) for m in lane_coef]
    zero_plane = jnp.zeros_like(pairs_list[2][0])
    sub_blocks = (pairs_list[0][0], pairs_list[1][0], zero_plane, pairs_list[0][1])
    diag_blocks = (pairs_list[2][0], pairs_list[3][0], pairs_list[1][1], pairs_list[2][1])
    super_blocks = (pairs_list[4][0], zero_plane, pairs_list[3][1], pairs_list[4][1])
    values = reduce_blocks(
        sub_blocks, diag_blocks, super_blocks, pair_split(cells_leading(line_source))
    )
    flat = alternate(values[0], values[1])
    shaped = flat.reshape(source_shape[2], source_shape[0], source_shape[1], source_shape[3])
    return jnp.transpose(shaped, (1, 2, 0, 3))


def return_tiles(line_values):
    return lax.all_to_all(line_values, "cell", split_axis=2, concat_axis=3, tiled=True)


def local_by_lines(state, pseudo_rate, line_next, face_codes):
    local_count = state.shape[0]
    tile_cells = state.shape[2]
    cell_index = lax.axis_index("cell")
    cell_count = lax.axis_size("cell")
    total_cells = tile_cells * cell_count
    spectral = spectral_matrix(NT)
    first_local = lax.axis_index("inst") * local_count
    own_rows = lax.dynamic_slice_in_dim(spectral, first_local, local_count, 0)
    shard_block = jax.tree.map(lambda a: lax.all_gather(a, "inst", axis=0, tiled=True), state)
    columns = lax.slice_in_dim(own_rows, 0, shard_block.shape[0], axis=1)
    time_term = jnp.zeros_like(state) + jnp.einsum(
        "nm,mvil->nvil", columns, shard_block, precision=lax.Precision.HIGHEST
    )
    padded = extended(state, (("cell", 2),), 2)
    codes_lines = jnp.repeat(face_codes, LINES_DEV, axis=1)
    lower_ghost = boundary_cells(state[:, :, 0:2, :], codes_lines[0], True)
    upper_ghost = boundary_cells(state[:, :, -2:, :], codes_lines[1], False)
    lower_rim = jnp.where(cell_index == 0, lower_ghost, padded[:, :, :2, :])
    upper_rim = jnp.where(cell_index == cell_count - 1, upper_ghost, padded[:, :, -2:, :])
    padded = jnp.concatenate([lower_rim, padded[:, :, 2:-2, :], upper_rim], axis=2)
    line_part, radius = line_residual(padded)
    prev_lines = (
        jnp.zeros_like(line_next).at[line_next].set(jnp.arange(line_next.shape[0], dtype=jnp.int32))
    )
    residual = line_part + pitch_residual(state, line_next, prev_lines) + time_term
    right_side = -residual
    centre_radius = radius[:, 2:-2, :]
    diagonal_term = pseudo_rate * centre_radius
    positions = cell_index * tile_cells + jnp.arange(-1, tile_cells + 1, dtype=jnp.int32)
    inside = (positions >= 0) & (positions < total_cells)
    radius_ext = jnp.where(inside[:, None], radius[:, 1:-1, :], 0.0)
    coefficients = line_coefficients(radius_ext, diagonal_term, positions[1:-1], total_cells)
    stacked = jnp.stack(coefficients, axis=1)
    line_source = lax.all_to_all(right_side, "cell", split_axis=3, concat_axis=2, tiled=True)
    line_coef = lax.all_to_all(stacked, "cell", split_axis=3, concat_axis=2, tiled=True)
    update = return_tiles(solve_in_lanes(tuple((line_coef[:, k] for k in range(5))), line_source))
    return state + update


LANES = 128
ROWS = 8
PAIRS = 3
CELL_ROWS = PAIRS * ROWS
STATE_ROWS = 2 * CELL_ROWS
BLOCK_ROWS = STATE_ROWS + ROWS
FACTORS = 56


def spectral_offsets():
    table = np.zeros(NT)
    for offset in range(1, NT):
        angle = np.pi * offset / NT
        parity = -1.0 if offset % 2 == 0 else 1.0
        table[offset] = 0.5 * OMEGA_BLADE * parity * np.cos(angle) / np.sin(angle)
    return [float(np.float32(value)) for value in table]


def plane_masks():
    row_index = lax.broadcasted_iota(jnp.int32, (ROWS, LANES), 0)
    return row_index < 4, (row_index & 2) == 0, row_index & 1


def both(first_var, plane):
    turned = pltpu.roll(plane, 4, 0)
    return jnp.where(first_var, plane, turned), jnp.where(first_var, turned, plane)


def primitives(first_var, planes):
    density, moment_x = both(first_var, planes[0])
    moment_y, moment_z = both(first_var, planes[1])
    energy = jnp.where(first_var, planes[2], pltpu.roll(planes[2], 4, 0))
    inverse = 1.0 / density
    velocity_x = moment_x * inverse
    velocity_y = moment_y * inverse
    velocity_z = moment_z * inverse
    kinetic = moment_x * velocity_x + moment_y * velocity_y + moment_z * velocity_z
    pressure = (GAMMA_GAS - 1.0) * (energy - 0.5 * kinetic)
    sound = jnp.sqrt(GAMMA_GAS * pressure * inverse)
    return velocity_x, velocity_y, pressure, sound


def rows_of(var, inst, half):
    return (var // 2) * ROWS + (var % 2) * 4 + inst * 2 + half


def pack_kernel(state_ref, rate_ref, inst_ref, cell_ref):
    for cell in range(2):
        for var in range(6):
            for inst in range(2):
                for half in range(2):
                    row = cell * CELL_ROWS + rows_of(var, inst, half)
                    inst_ref[0, pl.ds(row, 1), :] = state_ref[
                        inst, var, pl.ds(cell, 1), pl.ds(half * LANES, LANES)
                    ]
        for half in range(2):
            cell_ref[0, pl.ds(STATE_ROWS + cell * 2 + half, 1), :] = rate_ref[
                pl.ds(cell, 1), pl.ds(half * LANES, LANES)
            ]
    cell_ref[0, pl.ds(STATE_ROWS + 4, 4), :] = jnp.zeros((4, LANES), jnp.float32)
    for row in range(0, STATE_ROWS, ROWS):
        values = inst_ref[0, pl.ds(row, ROWS), :]
        for copy in range(1, inst_ref.shape[0]):
            inst_ref[copy, pl.ds(row, ROWS), :] = values
        for copy in range(cell_ref.shape[0]):
            cell_ref[copy, pl.ds(row, ROWS), :] = values
    values = cell_ref[0, pl.ds(STATE_ROWS, ROWS), :]
    for copy in range(1, cell_ref.shape[0]):
        cell_ref[copy, pl.ds(STATE_ROWS, ROWS), :] = values


def time_kernel(all_ref, out_ref):
    own_inst = lax.axis_index("inst")
    inst_count = all_ref.shape[0]
    _, first_inst, _ = plane_masks()
    offsets = spectral_offsets()
    for row in range(0, STATE_ROWS, ROWS):
        same_total, other_total = None, None
        for shift in range(inst_count):
            plane = all_ref[(own_inst - shift) & (inst_count - 1), pl.ds(row, ROWS), :]
            other = jnp.where(
                first_inst, offsets[(2 * shift + 1) % NT], offsets[(2 * shift - 1) % NT]
            )
            if shift > 0:
                term = offsets[(2 * shift) % NT] * plane
                same_total = term if same_total is None else same_total + term
            term = other * plane
            other_total = term if other_total is None else other_total + term
        turned = jnp.where(
            first_inst, pltpu.roll(other_total, 6, 0), pltpu.roll(other_total, 2, 0)
        )
        result = same_total + turned
        for copy in range(out_ref.shape[0]):
            out_ref[copy, pl.ds(row, ROWS), :] = result


def two_by_two(first, second):
    def entry(a, b, c, d):
        terms = [x * y for x, y in ((a, b), (c, d)) if x is not None and y is not None]
        return None if not terms else terms[0] if len(terms) == 1 else terms[0] + terms[1]

    return (
        entry(first[0], second[0], first[1], second[2]),
        entry(first[0], second[1], first[1], second[3]),
        entry(first[2], second[0], first[3], second[2]),
        entry(first[2], second[1], first[3], second[3]),
    )


def inverse_of(matrix):
    reciprocal = 1.0 / (matrix[0] * matrix[3] - matrix[1] * matrix[2])
    return (
        matrix[3] * reciprocal,
        -(matrix[1] * reciprocal),
        -(matrix[2] * reciprocal),
        matrix[0] * reciprocal,
    )


def less(first, second):
    return tuple(a if b is None else a - b for a, b in zip(first, second))


def minus(members):
    return tuple(None if a is None else -a for a in members)


def eliminate(centre, left, left_inverse, right, right_inverse):
    left_factor = two_by_two(centre[0], left_inverse)
    right_factor = two_by_two(centre[2], right_inverse)
    sub = minus(two_by_two(left_factor, left[0]))
    diag = less(
        less(centre[1], two_by_two(left_factor, left[2])), two_by_two(right_factor, right[0])
    )
    sup = minus(two_by_two(right_factor, right[2]))
    side = []
    for k in range(PAIRS):
        for row in range(2):
            value = centre[3][row * PAIRS + k]
            for factor, other in ((left_factor, left[3]), (right_factor, right[3])):
                value = value - (
                    factor[2 * row] * other[k] + factor[2 * row + 1] * other[PAIRS + k]
                )
            side.append((row * PAIRS + k, value))
    side = [value for _, value in sorted(side, key=lambda item: item[0])]
    return sub, diag, sup, side, left_factor + right_factor


def line_kernel(
    cells, all_ref, next_ref, codes_ref, factor_ref, part_ref, coef_ref, side_ref, coef2_ref, side2_ref,
    couple_ref, diag3_ref, side3_ref,
):
    own_cell = lax.axis_index("cell")
    shape = (ROWS, LANES)
    lane_index = lax.broadcasted_iota(jnp.int32, shape, 1)
    first_var, _, half_index = plane_masks()
    first_half = half_index == 0
    zero = jnp.zeros(shape, jnp.float32)

    next_rows = [next_ref[pl.ds(half, 1), :] for half in range(2)]
    next_line = jnp.where(first_half, next_rows[0], next_rows[1])
    column = lax.broadcasted_iota(jnp.int32, (LANES, LANES), 0)
    prev_halves = []
    for target in range(2):
        total = None
        for source in range(2):
            hits = jnp.where(column + target * LANES == next_rows[source], 1.0, 0.0)
            names = (lane_index + source * LANES).astype(jnp.float32)
            part = lax.dot_general(
                names, hits, (((1,), (1,)), ((), ())), preferred_element_type=jnp.float32
            )
            total = part if total is None else total + part
        prev_halves.append(total)
    prev_line = jnp.where(first_half, prev_halves[0], prev_halves[1]).astype(jnp.int32)

    def picker(lines):
        lane = lines & (LANES - 1)
        same = (lines >> 7) == half_index

        def pick(plane):
            swapped = jnp.where(first_half, pltpu.roll(plane, 7, 0), pltpu.roll(plane, 1, 0))
            here = jnp.take_along_axis(plane, lane, axis=1, mode="promise_in_bounds")
            there = jnp.take_along_axis(swapped, lane, axis=1, mode="promise_in_bounds")
            return jnp.where(same, here, there)

        return pick

    pick_next = picker(next_line)
    pick_prev = picker(prev_line)

    tile = half_index * (LANES // LINES_DEV) + lane_index // LINES_DEV
    codes = []
    for end in range(2):
        plane = jnp.zeros(shape, jnp.int32)
        for k in range(2 * LANES // LINES_DEV):
            plane = jnp.where(tile == k, codes_ref[end, k], plane)
        codes.append(plane)

    def loaded(cell):
        return [
            all_ref[cell // 2, pl.ds((cell % 2) * CELL_ROWS + k * ROWS, ROWS), :]
            for k in range(PAIRS)
        ]

    def ghost(end, mirrored, copied):
        planes = []
        for k in range(PAIRS):
            reflected = mirrored[k]
            if k == 0:
                reflected = jnp.where(first_var, reflected, -reflected)
            inflow = jnp.where(first_var, FREE_STATE[2 * k], FREE_STATE[2 * k + 1])
            planes.append(
                jnp.where(
                    codes[end] == 0, reflected, jnp.where(codes[end] == 1, inflow, copied[k])
                )
            )
        return planes

    def extended_state(cell):
        if cell < 0:
            return ghost(0, loaded(-1 - cell), loaded(0))
        if cell >= cells:
            return ghost(
                1, loaded(2 * cells - 1 - cell), loaded(cells - 1)
            )
        return loaded(cell)

    def flux_along(planes, velocity, pressure):
        return [
            planes[0] * velocity + jnp.where(first_var, 0.0, pressure),
            planes[1] * velocity,
            planes[2] * velocity + jnp.where(first_var, pressure * velocity, 0.0),
        ]

    def flux_across(planes, velocity, pressure):
        return [
            planes[0] * velocity,
            planes[1] * velocity + jnp.where(first_var, pressure, 0.0),
            planes[2] * velocity + jnp.where(first_var, pressure * velocity, 0.0),
        ]

    def pitch_flux(planes, velocity_y, pressure, sound):
        nearby = [pick_next(plane) for plane in planes]
        _, next_velocity, next_pressure, next_sound = primitives(first_var, nearby)
        own_flux = flux_across(planes, velocity_y, pressure)
        next_flux = flux_across(nearby, next_velocity, next_pressure)
        weight = (PITCH_GAIN * 0.5) * (
            jnp.abs(velocity_y) + sound + (jnp.abs(next_velocity) + next_sound)
        )
        return [
            0.5 * (a + b) - weight * (n - o)
            for a, b, n, o in zip(own_flux, next_flux, nearby, planes)
        ]

    state, pressures, radii, fluxes, steps, rest, sensors, faces = {}, {}, {}, {}, {}, {}, {}, {}
    for cell in range(-2, cells + 2):
        planes = extended_state(cell)
        velocity_x, velocity_y, pressure, sound = primitives(first_var, planes)
        state[cell] = planes
        pressures[cell] = pressure
        radii[cell] = jnp.abs(velocity_x) + sound
        if -1 <= cell <= cells:
            fluxes[cell] = flux_along(planes, velocity_x, pressure)
        if cell >= -1:
            steps[cell - 1] = [a - b for a, b in zip(planes, state[cell - 1])]
        if 0 <= cell < cells:
            faces_across = pitch_flux(planes, velocity_y, pressure, sound)
            rest[cell] = [face - pick_prev(face) for face in faces_across]
        if cell >= 0:
            twice = 2.0 * pressures[cell - 1]
            outer = pressure + pressures[cell - 2]
            sensors[cell - 1] = jnp.abs(outer - twice) / (outer + twice)
        if cell >= 1:
            face = cell - 2
            second = SENSOR_GAIN * jnp.maximum(sensors[face], sensors[face + 1])
            fourth = jnp.maximum(0.0, FOURTH_GAIN - second)
            face_radius = 0.5 * (radii[face] + radii[face + 1])
            near_weight = face_radius * (second + 2.0 * fourth)
            far_weight = face_radius * fourth
            faces[face] = [
                0.5 * (fluxes[face][k] + fluxes[face + 1][k])
                - (
                    near_weight * steps[face][k]
                    - far_weight * (steps[face + 1][k] + steps[face - 1][k])
                )
                for k in range(PAIRS)
            ]
        if cell >= 2:
            at = cell - 2
            slot, member = at // 2 + 1, at % 2
            for k in range(PAIRS):
                side_ref[slot, member * PAIRS + k] = (
                    faces[at - 1][k] - faces[at][k] - rest[at][k]
                )
            below = radii[at - 1] if at > 0 else zero
            centre = radii[at]
            above = radii[at + 1] if at < cells - 1 else zero
            below_sum = below + centre
            above_sum = centre + above
            half_low = SECOND_IMPL * 0.5 + 2.0 * FOURTH_IMPL
            rate_rows = [
                all_ref[at // 2, pl.ds(STATE_ROWS + member * 2 + half, 1), :]
                for half in range(2)
            ]
            rate = jnp.where(first_half, rate_rows[0], rate_rows[1])
            middle = (
                rate * centre
                + SECOND_IMPL * (0.5 * (below_sum + above_sum))
                + FOURTH_IMPL * (below + 4.0 * centre + above)
            )
            far_low = FOURTH_IMPL * below if at >= 2 else zero
            near_low = -half_low * below_sum if at >= 1 else zero
            near_high = -half_low * above_sum if at <= cells - 2 else zero
            far_high = FOURTH_IMPL * above if at <= cells - 3 else zero
            if member == 0:
                entries = {0: far_low, 1: near_low, 3: middle, 4: near_high, 7: far_high}
            else:
                entries = {2: far_low, 5: near_low, 6: middle, 8: near_high, 9: far_high}
            for k, plane in entries.items():
                coef_ref[slot, k] = plane

    blocks = cells // 2
    one = zero + 1.0
    for slot in (0, blocks + 1):
        for k in range(10):
            coef_ref[slot, k] = one if k in (3, 6) else zero
        for k in range(2 * PAIRS):
            side_ref[slot, k] = zero
    for slot in (0, blocks // 2 + 1):
        for k in range(12):
            coef2_ref[slot, k] = one if k in (4, 7) else zero
        for k in range(2 * PAIRS):
            side2_ref[slot, k] = zero

    def block_one(slot):
        c = [coef_ref[slot, k] for k in range(10)]
        return (
            (c[0], c[1], None, c[2]),
            (c[3], c[4], c[5], c[6]),
            (c[7], None, c[8], c[9]),
            [side_ref[slot, k] for k in range(2 * PAIRS)],
        )

    def block_two(slot):
        c = [coef2_ref[slot, k] for k in range(12)]
        return (
            tuple(c[0:4]),
            tuple(c[4:8]),
            tuple(c[8:12]),
            [side2_ref[slot, k] for k in range(2 * PAIRS)],
        )

    parity = own_cell & 1
    left = block_one(parity)
    left_inverse = inverse_of(left[1])
    for k in range(blocks // 2):
        right = block_one(parity + 2 * k + 2)
        right_inverse = inverse_of(right[1])
        kept = block_one(parity + 2 * k + 1)
        sub, diag, sup, side, factors = eliminate(kept, left, left_inverse, right, right_inverse)
        for n, plane in enumerate(sub + diag + sup):
            coef2_ref[k + 1, n] = plane
        for n, plane in enumerate(side):
            side2_ref[k + 1, n] = plane
        for n, plane in enumerate(factors):
            factor_ref[8 * k + n] = plane
        left, left_inverse = right, right_inverse
    parity = (own_cell >> 1) & 1
    left = block_two(parity)
    left_inverse = inverse_of(left[1])
    for k in range(blocks // 4):
        right = block_two(parity + 2 * k + 2)
        right_inverse = inverse_of(right[1])
        kept = block_two(parity + 2 * k + 1)
        sub, diag, sup, side, factors = eliminate(kept, left, left_inverse, right, right_inverse)
        for n in range(4):
            couple_ref[k, 0, n] = sub[n]
            couple_ref[k, 1, n] = sup[n]
            diag3_ref[k, n] = diag[n]
        for n, plane in enumerate(side):
            side3_ref[k, n] = plane
        for n, plane in enumerate(factors):
            factor_ref[4 * blocks + 8 * k + n] = plane
        left, left_inverse = right, right_inverse
    own = (own_cell >> 2) & 1
    other = 1 - own
    own_couple = tuple(couple_ref[own, 1 - own, n] for n in range(4))
    other_couple = tuple(couple_ref[other, own, n] for n in range(4))
    factor = two_by_two(own_couple, inverse_of([diag3_ref[other, n] for n in range(4)]))
    diag = less([diag3_ref[own, n] for n in range(4)], two_by_two(factor, other_couple))
    last_inverse = inverse_of(diag)
    for n in range(4):
        factor_ref[6 * blocks + n] = factor[n]
        factor_ref[6 * blocks + 4 + n] = last_inverse[n]
    for k in range(PAIRS):
        other_low, other_high = side3_ref[other, k], side3_ref[other, PAIRS + k]
        low = side3_ref[own, k] - (factor[0] * other_low + factor[1] * other_high)
        high = side3_ref[own, PAIRS + k] - (factor[2] * other_low + factor[3] * other_high)
        for member in range(2):
            delta = last_inverse[2 * member] * low + last_inverse[2 * member + 1] * high
            base = all_ref[own_cell, pl.ds(member * CELL_ROWS + k * ROWS, ROWS), :]
            part_ref[member * PAIRS + k] = base + delta


def finish_kernel(time_ref, factor_ref, part_ref, out_ref, side2_ref, side3_ref):
    own_cell = lax.axis_index("cell")
    blocks = time_ref.shape[0]

    def reduced(start, centre, left, right):
        factor = [factor_ref[start + n] for n in range(8)]
        result = []
        for row in range(2):
            for k in range(PAIRS):
                value = centre(row * PAIRS + k)
                for first, other in ((0, left), (4, right)):
                    value = value - (
                        factor[first + 2 * row] * other(k)
                        + factor[first + 2 * row + 1] * other(PAIRS + k)
                    )
                result.append(value)
        return result

    def held(ref, count, slot):
        inside = jnp.minimum(jnp.maximum(slot, 0), count - 1)
        return lambda n: ref[inside, pl.ds(n * ROWS, ROWS), :]

    def level(ref, count, parity, k):
        at = parity + 2 * k
        return [held(ref, count, at), held(ref, count, at - 1), held(ref, count, at + 1)]

    for k in range(blocks // 2):
        around = level(time_ref, blocks, own_cell & 1, k)
        for n, plane in enumerate(reduced(8 * k, *around)):
            side2_ref[k, pl.ds(n * ROWS, ROWS), :] = plane
    for k in range(blocks // 4):
        around = level(side2_ref, blocks // 2, (own_cell >> 1) & 1, k)
        for n, plane in enumerate(reduced(4 * blocks + 8 * k, *around)):
            side3_ref[k, n] = plane
    own = (own_cell >> 2) & 1
    other = 1 - own
    factor = [factor_ref[6 * blocks + n] for n in range(4)]
    inverse = [factor_ref[6 * blocks + 4 + n] for n in range(4)]
    for k in range(PAIRS):
        other_low, other_high = side3_ref[other, k], side3_ref[other, PAIRS + k]
        low = side3_ref[own, k] - (factor[0] * other_low + factor[1] * other_high)
        high = side3_ref[own, PAIRS + k] - (factor[2] * other_low + factor[3] * other_high)
        for member in range(2):
            delta = inverse[2 * member] * low + inverse[2 * member + 1] * high
            result = part_ref[member * PAIRS + k] - delta
            for var in range(2):
                for inst in range(2):
                    for half in range(2):
                        row = rows_of(var, inst, half)
                        out_ref[
                            inst, 2 * k + var, pl.ds(member, 1), pl.ds(half * LANES, LANES)
                        ] = result[row : row + 1]


def exchange(copies, axis):
    return lax.all_to_all(copies, axis, split_axis=0, concat_axis=0, tiled=True)


def float_shape(*sizes):
    return jax.ShapeDtypeStruct(sizes, jnp.float32)


def local_by_gather(state, pseudo_rate, line_next, face_codes):
    inst_count = lax.axis_size("inst")
    blocks = lax.axis_size("cell")
    cells = 2 * blocks
    vmem = pl.BlockSpec(memory_space=pltpu.VMEM)
    plane = (ROWS, LANES)
    inst_copies, cell_copies = pl.pallas_call(
        pack_kernel,
        out_shape=(
            float_shape(inst_count, STATE_ROWS, LANES),
            float_shape(blocks, BLOCK_ROWS, LANES),
        ),
        in_specs=[vmem, vmem],
        out_specs=(vmem, vmem),
    )(state, pseudo_rate)
    every_inst = exchange(inst_copies, "inst")
    every_cell = exchange(cell_copies, "cell")
    time_copies = pl.pallas_call(
        time_kernel,
        out_shape=float_shape(blocks, STATE_ROWS, LANES),
        in_specs=[vmem],
        out_specs=vmem,
    )(every_inst)
    every_time = exchange(time_copies, "cell")
    sizes = [
        (blocks + 2, 10),
        (blocks + 2, 2 * PAIRS),
        (blocks // 2 + 2, 12),
        (blocks // 2 + 2, 2 * PAIRS),
        (2, 2, 4),
        (2, 4),
        (2, 2 * PAIRS),
    ]
    factors, part = pl.pallas_call(
        functools.partial(line_kernel, cells),
        out_shape=(float_shape(FACTORS, ROWS, LANES), float_shape(2 * PAIRS, ROWS, LANES)),
        in_specs=[vmem, vmem, pl.BlockSpec(memory_space=pltpu.SMEM)],
        out_specs=(vmem, vmem),
        scratch_shapes=[pltpu.VMEM(size + plane, jnp.float32) for size in sizes],
    )(every_cell, line_next.reshape(2, LANES), face_codes)
    return pl.pallas_call(
        finish_kernel,
        out_shape=float_shape(*state.shape),
        in_specs=[vmem, vmem, vmem],
        out_specs=vmem,
        scratch_shapes=[
            pltpu.VMEM((blocks // 2, STATE_ROWS, LANES), jnp.float32),
            pltpu.VMEM((2, 2 * PAIRS) + plane, jnp.float32),
        ],
    )(every_time, factors, part)


def solution(mesh):
    placed = (P("inst", None, "cell", None), P("cell", None), P(), P())
    inst_count, cell_count = mesh.shape["inst"], mesh.shape["cell"]

    def local(state, pseudo_rate, line_next, face_codes):
        small = (
            state.shape == (2, 6, 2, 2 * LANES)
            and inst_count * 2 == NT
            and cell_count == 8
            and face_codes.shape[1] * LINES_DEV == state.shape[3]
        )
        chosen = local_by_gather if small else local_by_lines
        return chosen(state, pseudo_rate, line_next, face_codes)

    return jax.shard_map(
        local, mesh=mesh, in_specs=placed, out_specs=P("inst", None, "cell", None), check_vma=False
    )
```

```python
import functools

import jax
import jax.numpy as jnp
import numpy as np
from jax import lax
from jax.experimental import pallas as pl
from jax.experimental.pallas import tpu as pltpu
from jax.sharding import PartitionSpec as P

NT = 8
LINES_DEV = 32


GAMMA_GAS = 1.4
OMEGA_BLADE = 1.0
SENSOR_GAIN = 0.25
FOURTH_GAIN = 0.03125
PITCH_GAIN = 0.5
SECOND_IMPL = 1.0
FOURTH_IMPL = 0.25
FREE_STATE = (1.0, 0.5, 0.0, 0.0, 2.625, 0.2)
MIRROR_SIGNS = (1.0, -1.0, 1.0, 1.0, 1.0, 1.0)
ZERO_BLOCK = (0.0, 0.0, 0.0, 0.0)
UNIT_BLOCK = (1.0, 0.0, 0.0, 1.0)
ZERO_PAIR = (0.0, 0.0)


def extended(block, sides, width):
    for axis, dim in sides:
        count = lax.axis_size(axis)
        forward = [(i, i + 1) for i in range(count - 1)]
        backward = [(target, source) for source, target in forward]
        low = lax.ppermute(
            lax.slice_in_dim(block, block.shape[dim] - width, None, axis=dim), axis, forward
        )
        high = lax.ppermute(lax.slice_in_dim(block, 0, width, axis=dim), axis, backward)
        block = jnp.concatenate([low, block, high], axis=dim)
    return block


def spectral_matrix(instances):
    offsets = np.arange(instances)[:, None] - np.arange(instances)[None, :]
    angles = np.pi * offsets / instances
    safe_sin = np.where(offsets == 0, 1.0, np.sin(angles))
    parity = np.where(np.mod(offsets, 2) == 0, -1.0, 1.0)
    matrix_table = np.where(
        offsets == 0, 0.0, 0.5 * OMEGA_BLADE * parity * np.cos(angles) / safe_sin
    )
    return jnp.asarray(matrix_table, jnp.float32)


def primitive_parts(cells_state):
    density = cells_state[..., 0, :, :]
    inverse = 1.0 / density
    velocity_x = cells_state[..., 1, :, :] * inverse
    velocity_y = cells_state[..., 2, :, :] * inverse
    velocity_z = cells_state[..., 3, :, :] * inverse
    energy = cells_state[..., 4, :, :]
    pressure = (GAMMA_GAS - 1.0) * (
        energy
        - 0.5
        * density
        * (velocity_x * velocity_x + velocity_y * velocity_y + velocity_z * velocity_z)
    )
    sound_speed = jnp.sqrt(GAMMA_GAS * pressure * inverse)
    return (velocity_x, velocity_y, pressure, sound_speed)


def directed_flux(cells_state, normal_velocity, pressure, component):
    zero_plane = jnp.zeros_like(pressure)
    pressure_rows = [
        zero_plane,
        zero_plane,
        zero_plane,
        zero_plane,
        pressure * normal_velocity,
        zero_plane,
    ]
    pressure_rows[component] = pressure
    return cells_state * normal_velocity[..., None, :, :] + jnp.stack(pressure_rows, axis=-3)


def line_residual(padded):
    velocity_x, velocity_y, pressure, sound_speed = primitive_parts(padded)
    flux_line = directed_flux(padded, velocity_x, pressure, 1)
    radius = jnp.abs(velocity_x) + sound_speed
    sensor = jnp.abs(
        pressure[..., 2:, :] - 2.0 * pressure[..., 1:-1, :] + pressure[..., :-2, :]
    ) / (pressure[..., 2:, :] + 2.0 * pressure[..., 1:-1, :] + pressure[..., :-2, :])
    second = SENSOR_GAIN * jnp.maximum(sensor[..., :-1, :], sensor[..., 1:, :])
    fourth = jnp.maximum(0.0, FOURTH_GAIN - second)
    face_radius = 0.5 * (radius[..., 1:-2, :] + radius[..., 2:-1, :])
    left_far = padded[..., :-3, :]
    left_near = padded[..., 1:-2, :]
    right_near = padded[..., 2:-1, :]
    right_far = padded[..., 3:, :]
    damping = face_radius[..., None, :, :] * (
        second[..., None, :, :] * (right_near - left_near)
        - fourth[..., None, :, :] * (right_far - 3.0 * right_near + 3.0 * left_near - left_far)
    )
    face_flux = 0.5 * (flux_line[..., 1:-2, :] + flux_line[..., 2:-1, :]) - damping
    return (face_flux[..., 1:, :] - face_flux[..., :-1, :], radius)


def pitch_parts(cells_state):
    velocity_x, velocity_y, pressure, sound_speed = primitive_parts(cells_state)
    return (directed_flux(cells_state, velocity_y, pressure, 2), jnp.abs(velocity_y) + sound_speed)


def pitch_residual(cells_state, next_lines, prev_lines):
    pitch_flux, radius = pitch_parts(cells_state)
    state_next = jnp.take(cells_state, next_lines, axis=-1)
    flux_next, radius_next = pitch_parts(state_next)
    face_flux = 0.5 * (pitch_flux + flux_next) - PITCH_GAIN * (0.5 * (radius + radius_next))[
        ..., None, :, :
    ] * (state_next - cells_state)
    return face_flux - jnp.take(face_flux, prev_lines, axis=-1)


def boundary_cells(edge_pair, line_codes, lower_end):
    reflected = edge_pair[..., ::-1, :] * jnp.asarray(MIRROR_SIGNS, jnp.float32)[:, None, None]
    if lower_end:
        copied = jnp.concatenate([edge_pair[..., :1, :], edge_pair[..., :1, :]], axis=-2)
    else:
        copied = jnp.concatenate([edge_pair[..., 1:, :], edge_pair[..., 1:, :]], axis=-2)
    inflow = jnp.asarray(FREE_STATE, jnp.float32)[:, None, None] + jnp.zeros_like(edge_pair)
    return jnp.where(line_codes == 0, reflected, jnp.where(line_codes == 1, inflow, copied))


def line_coefficients(radius_ext, diagonal_term, positions, total_cells):
    radius_below = radius_ext[..., :-2, :]
    radius_centre = radius_ext[..., 1:-1, :]
    radius_above = radius_ext[..., 2:, :]
    face_below = 0.5 * (radius_below + radius_centre)
    face_above = 0.5 * (radius_centre + radius_above)
    far_low = FOURTH_IMPL * radius_below
    near_low = -SECOND_IMPL * face_below - 2.0 * FOURTH_IMPL * (radius_below + radius_centre)
    middle = (
        diagonal_term
        + SECOND_IMPL * (face_below + face_above)
        + FOURTH_IMPL * (radius_below + 4.0 * radius_centre + radius_above)
    )
    near_high = -SECOND_IMPL * face_above - 2.0 * FOURTH_IMPL * (radius_centre + radius_above)
    far_high = FOURTH_IMPL * radius_above
    column = positions[:, None]
    far_low = jnp.where(column >= 2, far_low, 0.0)
    near_low = jnp.where(column >= 1, near_low, 0.0)
    near_high = jnp.where(column <= total_cells - 2, near_high, 0.0)
    far_high = jnp.where(column <= total_cells - 3, far_high, 0.0)
    return (far_low, near_low, middle, near_high, far_high)


def block_product(first_matrix, second_matrix):
    return (
        first_matrix[0] * second_matrix[0] + first_matrix[1] * second_matrix[2],
        first_matrix[0] * second_matrix[1] + first_matrix[1] * second_matrix[3],
        first_matrix[2] * second_matrix[0] + first_matrix[3] * second_matrix[2],
        first_matrix[2] * second_matrix[1] + first_matrix[3] * second_matrix[3],
    )


def block_inverse(matrix):
    determinant = matrix[0] * matrix[3] - matrix[1] * matrix[2]
    reciprocal = 1.0 / determinant
    return (
        matrix[3] * reciprocal,
        -matrix[1] * reciprocal,
        -matrix[2] * reciprocal,
        matrix[0] * reciprocal,
    )


def block_apply(matrix, vector):
    return (
        matrix[0] * vector[0] + matrix[1] * vector[1],
        matrix[2] * vector[0] + matrix[3] * vector[1],
    )


def add_blocks(first_members, second_members):
    return tuple((a + b for a, b in zip(first_members, second_members)))


def negate(members):
    return tuple((-a for a in members))


def extend_blocks(members, fill_values):
    return tuple(
        (
            jnp.concatenate([m, jnp.full_like(m[..., :1, :], f)], axis=-2)
            for m, f in zip(members, fill_values)
        )
    )


def shift_next(members, fill_values):
    return tuple(
        (
            jnp.concatenate([m[..., 1:, :], jnp.full_like(m[..., :1, :], f)], axis=-2)
            for m, f in zip(members, fill_values)
        )
    )


def shift_prev(members):
    return tuple(
        (jnp.concatenate([jnp.zeros_like(m[..., :1, :]), m[..., :-1, :]], axis=-2) for m in members)
    )


def pair_split(member):
    shaped = member.reshape(member.shape[:-2] + (member.shape[-2] // 2, 2, member.shape[-1]))
    return (shaped[..., 0, :], shaped[..., 1, :])


def split_parity(members):
    halves = [pair_split(m) for m in members]
    return (tuple((h[0] for h in halves)), tuple((h[1] for h in halves)))


def alternate(first_member, second_member):
    stacked = jnp.stack((first_member, second_member), axis=-2)
    return stacked.reshape(
        first_member.shape[:-2] + (2 * first_member.shape[-2], first_member.shape[-1])
    )


def reduce_blocks(sub_blocks, diag_blocks, super_blocks, right_side):
    block_count = diag_blocks[0].shape[-2]
    if block_count == 1:
        return block_apply(block_inverse(diag_blocks), right_side)
    if block_count % 2 == 1:
        sub_blocks = extend_blocks(sub_blocks, ZERO_BLOCK)
        diag_blocks = extend_blocks(diag_blocks, UNIT_BLOCK)
        super_blocks = extend_blocks(super_blocks, ZERO_BLOCK)
        right_side = extend_blocks(right_side, ZERO_PAIR)
    sub_even, sub_odd = split_parity(sub_blocks)
    diag_even, diag_odd = split_parity(diag_blocks)
    super_even, super_odd = split_parity(super_blocks)
    side_even, side_odd = split_parity(right_side)
    inverse_even = block_inverse(diag_even)
    inverse_next = shift_next(inverse_even, UNIT_BLOCK)
    sub_next = shift_next(sub_even, ZERO_BLOCK)
    super_next = shift_next(super_even, ZERO_BLOCK)
    side_next = shift_next(side_even, ZERO_PAIR)
    left_factor = negate(block_product(sub_odd, inverse_even))
    right_factor = negate(block_product(super_odd, inverse_next))
    reduced_sub = block_product(left_factor, sub_even)
    reduced_diag = add_blocks(
        diag_odd,
        add_blocks(block_product(left_factor, super_even), block_product(right_factor, sub_next)),
    )
    reduced_super = block_product(right_factor, super_next)
    reduced_side = add_blocks(
        side_odd,
        add_blocks(block_apply(left_factor, side_even), block_apply(right_factor, side_next)),
    )
    odd_values = reduce_blocks(reduced_sub, reduced_diag, reduced_super, reduced_side)
    before_values = shift_prev(odd_values)
    remainder = add_blocks(
        side_even,
        negate(
            add_blocks(block_apply(sub_even, before_values), block_apply(super_even, odd_values))
        ),
    )
    even_values = block_apply(inverse_even, remainder)
    merged = tuple((alternate(e, o) for e, o in zip(even_values, odd_values)))
    return tuple((m[..., :block_count, :] for m in merged))


def cells_leading(block):
    moved = jnp.transpose(block, (2, 0, 1, 3))
    return moved.reshape(block.shape[2], block.shape[0] * block.shape[1] * block.shape[3])


def solve_in_lanes(coefficients, line_source):
    source_shape = line_source.shape
    lane_coef = [cells_leading(jnp.broadcast_to(c[:, None], source_shape)) for c in coefficients]
    pairs_list = [pair_split(m) for m in lane_coef]
    zero_plane = jnp.zeros_like(pairs_list[2][0])
    sub_blocks = (pairs_list[0][0], pairs_list[1][0], zero_plane, pairs_list[0][1])
    diag_blocks = (pairs_list[2][0], pairs_list[3][0], pairs_list[1][1], pairs_list[2][1])
    super_blocks = (pairs_list[4][0], zero_plane, pairs_list[3][1], pairs_list[4][1])
    values = reduce_blocks(
        sub_blocks, diag_blocks, super_blocks, pair_split(cells_leading(line_source))
    )
    flat = alternate(values[0], values[1])
    shaped = flat.reshape(source_shape[2], source_shape[0], source_shape[1], source_shape[3])
    return jnp.transpose(shaped, (1, 2, 0, 3))


def return_tiles(line_values):
    return lax.all_to_all(line_values, "cell", split_axis=2, concat_axis=3, tiled=True)


def local_by_lines(state, pseudo_rate, line_next, face_codes):
    local_count = state.shape[0]
    tile_cells = state.shape[2]
    cell_index = lax.axis_index("cell")
    cell_count = lax.axis_size("cell")
    total_cells = tile_cells * cell_count
    spectral = spectral_matrix(NT)
    first_local = lax.axis_index("inst") * local_count
    own_rows = lax.dynamic_slice_in_dim(spectral, first_local, local_count, 0)
    shard_block = jax.tree.map(lambda a: lax.all_gather(a, "inst", axis=0, tiled=True), state)
    columns = lax.slice_in_dim(own_rows, 0, shard_block.shape[0], axis=1)
    time_term = jnp.zeros_like(state) + jnp.einsum(
        "nm,mvil->nvil", columns, shard_block, precision=lax.Precision.HIGHEST
    )
    padded = extended(state, (("cell", 2),), 2)
    codes_lines = jnp.repeat(face_codes, LINES_DEV, axis=1)
    lower_ghost = boundary_cells(state[:, :, 0:2, :], codes_lines[0], True)
    upper_ghost = boundary_cells(state[:, :, -2:, :], codes_lines[1], False)
    lower_rim = jnp.where(cell_index == 0, lower_ghost, padded[:, :, :2, :])
    upper_rim = jnp.where(cell_index == cell_count - 1, upper_ghost, padded[:, :, -2:, :])
    padded = jnp.concatenate([lower_rim, padded[:, :, 2:-2, :], upper_rim], axis=2)
    line_part, radius = line_residual(padded)
    prev_lines = (
        jnp.zeros_like(line_next).at[line_next].set(jnp.arange(line_next.shape[0], dtype=jnp.int32))
    )
    residual = line_part + pitch_residual(state, line_next, prev_lines) + time_term
    right_side = -residual
    centre_radius = radius[:, 2:-2, :]
    diagonal_term = pseudo_rate * centre_radius
    positions = cell_index * tile_cells + jnp.arange(-1, tile_cells + 1, dtype=jnp.int32)
    inside = (positions >= 0) & (positions < total_cells)
    radius_ext = jnp.where(inside[:, None], radius[:, 1:-1, :], 0.0)
    coefficients = line_coefficients(radius_ext, diagonal_term, positions[1:-1], total_cells)
    stacked = jnp.stack(coefficients, axis=1)
    line_source = lax.all_to_all(right_side, "cell", split_axis=3, concat_axis=2, tiled=True)
    line_coef = lax.all_to_all(stacked, "cell", split_axis=3, concat_axis=2, tiled=True)
    update = return_tiles(solve_in_lanes(tuple((line_coef[:, k] for k in range(5))), line_source))
    return state + update


LANES = 128
ROWS = 8
PAIRS = 3
CELL_ROWS = PAIRS * ROWS
REST_ROW = 2 * CELL_ROWS
RATE_ROW = 2 * REST_ROW
VMEM_BYTES = 8 * 2**20
BLOCK_ROWS = RATE_ROW + ROWS


def spectral_offsets():
    table = np.zeros(NT)
    for offset in range(1, NT):
        angle = np.pi * offset / NT
        parity = -1.0 if offset % 2 == 0 else 1.0
        table[offset] = 0.5 * OMEGA_BLADE * parity * np.cos(angle) / np.sin(angle)
    return [float(np.float32(value)) for value in table]


def plane_masks():
    row_index = lax.broadcasted_iota(jnp.int32, (ROWS, LANES), 0)
    return row_index < 4, (row_index & 2) == 0, row_index & 1


def both(first_var, plane):
    turned = pltpu.roll(plane, 4, 0)
    return jnp.where(first_var, plane, turned), jnp.where(first_var, turned, plane)


def primitives(first_var, planes):
    density, moment_x = both(first_var, planes[0])
    moment_y, moment_z = both(first_var, planes[1])
    energy = jnp.where(first_var, planes[2], pltpu.roll(planes[2], 4, 0))
    inverse = 1.0 / density
    velocity_x = moment_x * inverse
    velocity_y = moment_y * inverse
    velocity_z = moment_z * inverse
    kinetic = moment_x * velocity_x + moment_y * velocity_y + moment_z * velocity_z
    pressure = (GAMMA_GAS - 1.0) * (energy - 0.5 * kinetic)
    sound = jnp.sqrt(GAMMA_GAS * pressure * inverse)
    return velocity_x, velocity_y, pressure, sound


def rows_of(var, inst, half):
    return (var // 2) * ROWS + (var % 2) * 4 + inst * 2 + half


def cell_kernel(all_ref, rate_ref, next_ref, out_ref, plane_ref):
    own_inst = lax.axis_index("inst")
    inst_count = all_ref.shape[0] // 2
    copies = out_ref.shape[0]
    shape = (ROWS, LANES)
    lane_index = lax.broadcasted_iota(jnp.int32, shape, 1)
    first_var, first_inst, half_index = plane_masks()
    first_half = half_index == 0

    next_rows = [next_ref[pl.ds(half, 1), :] for half in range(2)]
    next_line = jnp.where(first_half, next_rows[0], next_rows[1])
    column = lax.broadcasted_iota(jnp.int32, (LANES, LANES), 0)
    prev_halves = []
    for target in range(2):
        total = None
        for source in range(2):
            hits = jnp.where(column + target * LANES == next_rows[source], 1.0, 0.0)
            names = (lane_index + source * LANES).astype(jnp.float32)
            part = lax.dot_general(
                names, hits, (((1,), (1,)), ((), ())), preferred_element_type=jnp.float32
            )
            total = part if total is None else total + part
        prev_halves.append(total)
    prev_line = jnp.where(first_half, prev_halves[0], prev_halves[1]).astype(jnp.int32)

    def picker(lines):
        lane = lines & (LANES - 1)
        same = (lines >> 7) == half_index

        def pick(plane):
            swapped = jnp.where(first_half, pltpu.roll(plane, 7, 0), pltpu.roll(plane, 1, 0))
            here = jnp.take_along_axis(plane, lane, axis=1, mode="promise_in_bounds")
            there = jnp.take_along_axis(swapped, lane, axis=1, mode="promise_in_bounds")
            return jnp.where(same, here, there)

        return pick

    pick_next = picker(next_line)
    pick_prev = picker(prev_line)

    for shift in range(inst_count):
        pair = (own_inst - shift) & (inst_count - 1)
        for cell in range(2):
            for var in range(6):
                for inst in range(2):
                    for half in range(2):
                        row = cell * CELL_ROWS + rows_of(var, inst, half)
                        plane_ref[shift, pl.ds(row, 1), :] = all_ref[
                            2 * pair + inst, var, pl.ds(cell, 1), pl.ds(half * LANES, LANES)
                        ]
    offsets = spectral_offsets()

    def time_parts(cell):
        same_total = [None] * PAIRS
        other_total = [None] * PAIRS
        for shift in range(inst_count):
            same = offsets[(2 * shift) % NT]
            other = jnp.where(
                first_inst, offsets[(2 * shift + 1) % NT], offsets[(2 * shift - 1) % NT]
            )
            for k in range(PAIRS):
                plane = plane_ref[shift, pl.ds(cell * CELL_ROWS + k * ROWS, ROWS), :]
                if shift > 0:
                    term = same * plane
                    same_total[k] = term if same_total[k] is None else same_total[k] + term
                term = other * plane
                other_total[k] = term if other_total[k] is None else other_total[k] + term
        return [
            s + jnp.where(first_inst, pltpu.roll(o, 6, 0), pltpu.roll(o, 2, 0))
            for s, o in zip(same_total, other_total)
        ]

    def flux_across(planes, velocity, pressure):
        return [
            planes[0] * velocity,
            planes[1] * velocity + jnp.where(first_var, pressure, 0.0),
            planes[2] * velocity + jnp.where(first_var, pressure * velocity, 0.0),
        ]

    for cell in range(2):
        planes = [
            plane_ref[0, pl.ds(cell * CELL_ROWS + k * ROWS, ROWS), :] for k in range(PAIRS)
        ]
        nearby = [pick_next(plane) for plane in planes]
        _, velocity, pressure, sound = primitives(first_var, planes)
        _, next_velocity, next_pressure, next_sound = primitives(first_var, nearby)
        own_flux = flux_across(planes, velocity, pressure)
        next_flux = flux_across(nearby, next_velocity, next_pressure)
        weight = (PITCH_GAIN * 0.5) * (
            jnp.abs(velocity) + sound + (jnp.abs(next_velocity) + next_sound)
        )
        time_term = time_parts(cell)
        for k in range(PAIRS):
            face = 0.5 * (own_flux[k] + next_flux[k]) - weight * (nearby[k] - planes[k])
            rest = time_term[k] + (face - pick_prev(face))
            row = cell * CELL_ROWS + k * ROWS
            for copy in range(copies):
                out_ref[copy, pl.ds(row, ROWS), :] = planes[k]
                out_ref[copy, pl.ds(REST_ROW + row, ROWS), :] = rest
    rates = [
        rate_ref[pl.ds(cell, 1), pl.ds(half * LANES, LANES)]
        for cell in range(2)
        for half in range(2)
    ]
    for copy in range(copies):
        for row, rate in enumerate(rates):
            out_ref[copy, pl.ds(RATE_ROW + row, 1), :] = rate
        out_ref[copy, pl.ds(RATE_ROW + 4, 4), :] = jnp.zeros((4, LANES), jnp.float32)


def two_by_two(first, second):
    def entry(a, b, c, d):
        terms = [x * y for x, y in ((a, b), (c, d)) if x is not None and y is not None]
        return None if not terms else terms[0] if len(terms) == 1 else terms[0] + terms[1]

    return (
        entry(first[0], second[0], first[1], second[2]),
        entry(first[0], second[1], first[1], second[3]),
        entry(first[2], second[0], first[3], second[2]),
        entry(first[2], second[1], first[3], second[3]),
    )


def inverse_of(matrix):
    reciprocal = 1.0 / (matrix[0] * matrix[3] - matrix[1] * matrix[2])
    return (
        matrix[3] * reciprocal,
        -(matrix[1] * reciprocal),
        -(matrix[2] * reciprocal),
        matrix[0] * reciprocal,
    )


def less(first, second):
    return tuple(a if b is None else a - b for a, b in zip(first, second))


def minus(members):
    return tuple(None if a is None else -a for a in members)


def eliminate(centre, left, left_inverse, right, right_inverse):
    left_factor = two_by_two(centre[0], left_inverse)
    right_factor = two_by_two(centre[2], right_inverse)
    sub = minus(two_by_two(left_factor, left[0]))
    diag = less(
        less(centre[1], two_by_two(left_factor, left[2])), two_by_two(right_factor, right[0])
    )
    sup = minus(two_by_two(right_factor, right[2]))
    side = []
    for k in range(PAIRS):
        for row in range(2):
            value = centre[3][row * PAIRS + k]
            for factor, other in ((left_factor, left[3]), (right_factor, right[3])):
                value = value - (
                    factor[2 * row] * other[k] + factor[2 * row + 1] * other[PAIRS + k]
                )
            side.append((row * PAIRS + k, value))
    return sub, diag, sup, [value for _, value in sorted(side, key=lambda item: item[0])]


def line_kernel(
    cells, all_ref, codes_ref, out_ref, coef_ref, side_ref, coef2_ref, side2_ref,
    couple_ref, diag3_ref, side3_ref,
):
    own_cell = lax.axis_index("cell")
    shape = (ROWS, LANES)
    lane_index = lax.broadcasted_iota(jnp.int32, shape, 1)
    first_var, _, half_index = plane_masks()
    first_half = half_index == 0
    zero = jnp.zeros(shape, jnp.float32)

    tile = half_index * (LANES // LINES_DEV) + lane_index // LINES_DEV
    codes = []
    for end in range(2):
        plane = jnp.zeros(shape, jnp.int32)
        for k in range(2 * LANES // LINES_DEV):
            plane = jnp.where(tile == k, codes_ref[end, k], plane)
        codes.append(plane)

    def loaded(cell, start=0):
        return [
            all_ref[cell // 2, pl.ds(start + (cell % 2) * CELL_ROWS + k * ROWS, ROWS), :]
            for k in range(PAIRS)
        ]

    def ghost(end, mirrored, copied):
        planes = []
        for k in range(PAIRS):
            reflected = mirrored[k]
            if k == 0:
                reflected = jnp.where(first_var, reflected, -reflected)
            inflow = jnp.where(first_var, FREE_STATE[2 * k], FREE_STATE[2 * k + 1])
            planes.append(
                jnp.where(
                    codes[end] == 0, reflected, jnp.where(codes[end] == 1, inflow, copied[k])
                )
            )
        return planes

    def extended_state(cell):
        if cell < 0:
            return ghost(0, loaded(-1 - cell), loaded(0))
        if cell >= cells:
            return ghost(
                1, loaded(2 * cells - 1 - cell), loaded(cells - 1)
            )
        return loaded(cell)

    def flux_along(planes, velocity, pressure):
        return [
            planes[0] * velocity + jnp.where(first_var, 0.0, pressure),
            planes[1] * velocity,
            planes[2] * velocity + jnp.where(first_var, pressure * velocity, 0.0),
        ]

    state, pressures, radii, fluxes, steps, sensors, faces = {}, {}, {}, {}, {}, {}, {}
    for cell in range(-2, cells + 2):
        planes = extended_state(cell)
        velocity_x, _, pressure, sound = primitives(first_var, planes)
        state[cell] = planes
        pressures[cell] = pressure
        radii[cell] = jnp.abs(velocity_x) + sound
        if -1 <= cell <= cells:
            fluxes[cell] = flux_along(planes, velocity_x, pressure)
        if cell >= -1:
            steps[cell - 1] = [a - b for a, b in zip(planes, state[cell - 1])]
        if cell >= 0:
            twice = 2.0 * pressures[cell - 1]
            outer = pressure + pressures[cell - 2]
            sensors[cell - 1] = jnp.abs(outer - twice) / (outer + twice)
        if cell >= 1:
            face = cell - 2
            second = SENSOR_GAIN * jnp.maximum(sensors[face], sensors[face + 1])
            fourth = jnp.maximum(0.0, FOURTH_GAIN - second)
            face_radius = 0.5 * (radii[face] + radii[face + 1])
            near_weight = face_radius * (second + 2.0 * fourth)
            far_weight = face_radius * fourth
            faces[face] = [
                0.5 * (fluxes[face][k] + fluxes[face + 1][k])
                - (
                    near_weight * steps[face][k]
                    - far_weight * (steps[face + 1][k] + steps[face - 1][k])
                )
                for k in range(PAIRS)
            ]
        if cell >= 2:
            at = cell - 2
            slot, member = at // 2 + 1, at % 2
            rest = loaded(at, REST_ROW)
            for k in range(PAIRS):
                side_ref[slot, member * PAIRS + k] = (
                    faces[at - 1][k] - faces[at][k] - rest[k]
                )
            below = radii[at - 1] if at > 0 else zero
            centre = radii[at]
            above = radii[at + 1] if at < cells - 1 else zero
            below_sum = below + centre
            above_sum = centre + above
            half_low = SECOND_IMPL * 0.5 + 2.0 * FOURTH_IMPL
            rate_rows = [
                all_ref[at // 2, pl.ds(RATE_ROW + member * 2 + half, 1), :]
                for half in range(2)
            ]
            rate = jnp.where(first_half, rate_rows[0], rate_rows[1])
            middle = (
                rate * centre
                + SECOND_IMPL * (0.5 * (below_sum + above_sum))
                + FOURTH_IMPL * (below + 4.0 * centre + above)
            )
            far_low = FOURTH_IMPL * below if at >= 2 else zero
            near_low = -half_low * below_sum if at >= 1 else zero
            near_high = -half_low * above_sum if at <= cells - 2 else zero
            far_high = FOURTH_IMPL * above if at <= cells - 3 else zero
            if member == 0:
                entries = {0: far_low, 1: near_low, 3: middle, 4: near_high, 7: far_high}
            else:
                entries = {2: far_low, 5: near_low, 6: middle, 8: near_high, 9: far_high}
            for k, plane in entries.items():
                coef_ref[slot, k] = plane

    blocks = cells // 2
    one = zero + 1.0
    for slot in (0, blocks + 1):
        for k in range(10):
            coef_ref[slot, k] = one if k in (3, 6) else zero
        for k in range(2 * PAIRS):
            side_ref[slot, k] = zero
    for slot in (0, blocks // 2 + 1):
        for k in range(12):
            coef2_ref[slot, k] = one if k in (4, 7) else zero
        for k in range(2 * PAIRS):
            side2_ref[slot, k] = zero

    def block_one(slot):
        c = [coef_ref[slot, k] for k in range(10)]
        return (
            (c[0], c[1], None, c[2]),
            (c[3], c[4], c[5], c[6]),
            (c[7], None, c[8], c[9]),
            [side_ref[slot, k] for k in range(2 * PAIRS)],
        )

    def block_two(slot):
        c = [coef2_ref[slot, k] for k in range(12)]
        return (
            tuple(c[0:4]),
            tuple(c[4:8]),
            tuple(c[8:12]),
            [side2_ref[slot, k] for k in range(2 * PAIRS)],
        )

    parity = own_cell & 1
    left = block_one(parity)
    left_inverse = inverse_of(left[1])
    for k in range(blocks // 2):
        right = block_one(parity + 2 * k + 2)
        right_inverse = inverse_of(right[1])
        kept = block_one(parity + 2 * k + 1)
        sub, diag, sup, side = eliminate(kept, left, left_inverse, right, right_inverse)
        for n, plane in enumerate(sub + diag + sup):
            coef2_ref[k + 1, n] = plane
        for n, plane in enumerate(side):
            side2_ref[k + 1, n] = plane
        left, left_inverse = right, right_inverse
    parity = (own_cell >> 1) & 1
    left = block_two(parity)
    left_inverse = inverse_of(left[1])
    for k in range(blocks // 4):
        right = block_two(parity + 2 * k + 2)
        right_inverse = inverse_of(right[1])
        kept = block_two(parity + 2 * k + 1)
        sub, diag, sup, side = eliminate(kept, left, left_inverse, right, right_inverse)
        for n in range(4):
            couple_ref[k, 0, n] = sub[n]
            couple_ref[k, 1, n] = sup[n]
            diag3_ref[k, n] = diag[n]
        for n, plane in enumerate(side):
            side3_ref[k, n] = plane
        left, left_inverse = right, right_inverse
    own = (own_cell >> 2) & 1
    other = 1 - own
    own_couple = tuple(couple_ref[own, 1 - own, n] for n in range(4))
    other_couple = tuple(couple_ref[other, own, n] for n in range(4))
    factor = two_by_two(own_couple, inverse_of([diag3_ref[other, n] for n in range(4)]))
    diag = less([diag3_ref[own, n] for n in range(4)], two_by_two(factor, other_couple))
    last_inverse = inverse_of(diag)
    for k in range(PAIRS):
        other_low, other_high = side3_ref[other, k], side3_ref[other, PAIRS + k]
        low = side3_ref[own, k] - (factor[0] * other_low + factor[1] * other_high)
        high = side3_ref[own, PAIRS + k] - (factor[2] * other_low + factor[3] * other_high)
        for member in range(2):
            delta = last_inverse[2 * member] * low + last_inverse[2 * member + 1] * high
            base = all_ref[own_cell, pl.ds(member * CELL_ROWS + k * ROWS, ROWS), :]
            result = base + delta
            for var in range(2):
                for inst in range(2):
                    for half in range(2):
                        row = rows_of(var, inst, half)
                        out_ref[
                            inst, 2 * k + var, pl.ds(member, 1), pl.ds(half * LANES, LANES)
                        ] = result[row : row + 1]


def gather_inst(block):
    return lax.all_gather(block, "inst", axis=0, tiled=True)


def exchange_cell(copies):
    return lax.all_to_all(copies, "cell", split_axis=0, concat_axis=0, tiled=True)


def local_by_gather(state, pseudo_rate, line_next, face_codes):
    cells = lax.axis_size("cell") * state.shape[2]
    vmem = pl.BlockSpec(memory_space=pltpu.VMEM)
    plane = (ROWS, LANES)
    every = gather_inst(state)
    packed = pl.pallas_call(
        cell_kernel,
        out_shape=jax.ShapeDtypeStruct(
            (lax.axis_size("cell"), BLOCK_ROWS, LANES), jnp.float32
        ),
        in_specs=[vmem, vmem, vmem],
        out_specs=vmem,
        scratch_shapes=[
            pltpu.VMEM((every.shape[0] // 2, 2 * CELL_ROWS, LANES), jnp.float32)
        ],
        compiler_params=pltpu.CompilerParams(vmem_limit_bytes=VMEM_BYTES),
    )(every, pseudo_rate, line_next.reshape(2, LANES))
    gathered = exchange_cell(packed)
    blocks = cells // 2
    sizes = [
        (blocks + 2, 10),
        (blocks + 2, 2 * PAIRS),
        (blocks // 2 + 2, 12),
        (blocks // 2 + 2, 2 * PAIRS),
        (2, 2, 4),
        (2, 4),
        (2, 2 * PAIRS),
    ]
    return pl.pallas_call(
        functools.partial(line_kernel, cells),
        out_shape=jax.ShapeDtypeStruct(state.shape, jnp.float32),
        in_specs=[vmem, pl.BlockSpec(memory_space=pltpu.SMEM)],
        out_specs=vmem,
        scratch_shapes=[pltpu.VMEM(size + plane, jnp.float32) for size in sizes],
        compiler_params=pltpu.CompilerParams(vmem_limit_bytes=VMEM_BYTES),
    )(gathered, face_codes)


def solution(mesh):
    placed = (P("inst", None, "cell", None), P("cell", None), P(), P())
    inst_count, cell_count = mesh.shape["inst"], mesh.shape["cell"]

    def local(state, pseudo_rate, line_next, face_codes):
        small = (
            state.shape == (2, 6, 2, 2 * LANES)
            and inst_count * 2 == NT
            and cell_count == 8
            and face_codes.shape[1] * LINES_DEV == state.shape[3]
        )
        chosen = local_by_gather if small else local_by_lines
        return chosen(state, pseudo_rate, line_next, face_codes)

    return jax.shard_map(
        local, mesh=mesh, in_specs=placed, out_specs=P("inst", None, "cell", None), check_vma=False
    )
```

```python
import functools

import jax
import jax.numpy as jnp
import numpy as np
from jax import lax
from jax.experimental import pallas as pl
from jax.experimental.pallas import tpu as pltpu
from jax.sharding import PartitionSpec as P

NT = 8
LINES_DEV = 32


GAMMA_GAS = 1.4
OMEGA_BLADE = 1.0
SENSOR_GAIN = 0.25
FOURTH_GAIN = 0.03125
PITCH_GAIN = 0.5
SECOND_IMPL = 1.0
FOURTH_IMPL = 0.25
FREE_STATE = (1.0, 0.5, 0.0, 0.0, 2.625, 0.2)
MIRROR_SIGNS = (1.0, -1.0, 1.0, 1.0, 1.0, 1.0)
ZERO_BLOCK = (0.0, 0.0, 0.0, 0.0)
UNIT_BLOCK = (1.0, 0.0, 0.0, 1.0)
ZERO_PAIR = (0.0, 0.0)


def extended(block, sides, width):
    for axis, dim in sides:
        count = lax.axis_size(axis)
        forward = [(i, i + 1) for i in range(count - 1)]
        backward = [(target, source) for source, target in forward]
        low = lax.ppermute(
            lax.slice_in_dim(block, block.shape[dim] - width, None, axis=dim), axis, forward
        )
        high = lax.ppermute(lax.slice_in_dim(block, 0, width, axis=dim), axis, backward)
        block = jnp.concatenate([low, block, high], axis=dim)
    return block


def spectral_matrix(instances):
    offsets = np.arange(instances)[:, None] - np.arange(instances)[None, :]
    angles = np.pi * offsets / instances
    safe_sin = np.where(offsets == 0, 1.0, np.sin(angles))
    parity = np.where(np.mod(offsets, 2) == 0, -1.0, 1.0)
    matrix_table = np.where(
        offsets == 0, 0.0, 0.5 * OMEGA_BLADE * parity * np.cos(angles) / safe_sin
    )
    return jnp.asarray(matrix_table, jnp.float32)


def primitive_parts(cells_state):
    density = cells_state[..., 0, :, :]
    inverse = 1.0 / density
    velocity_x = cells_state[..., 1, :, :] * inverse
    velocity_y = cells_state[..., 2, :, :] * inverse
    velocity_z = cells_state[..., 3, :, :] * inverse
    energy = cells_state[..., 4, :, :]
    pressure = (GAMMA_GAS - 1.0) * (
        energy
        - 0.5
        * density
        * (velocity_x * velocity_x + velocity_y * velocity_y + velocity_z * velocity_z)
    )
    sound_speed = jnp.sqrt(GAMMA_GAS * pressure * inverse)
    return (velocity_x, velocity_y, pressure, sound_speed)


def directed_flux(cells_state, normal_velocity, pressure, component):
    zero_plane = jnp.zeros_like(pressure)
    pressure_rows = [
        zero_plane,
        zero_plane,
        zero_plane,
        zero_plane,
        pressure * normal_velocity,
        zero_plane,
    ]
    pressure_rows[component] = pressure
    return cells_state * normal_velocity[..., None, :, :] + jnp.stack(pressure_rows, axis=-3)


def line_residual(padded):
    velocity_x, velocity_y, pressure, sound_speed = primitive_parts(padded)
    flux_line = directed_flux(padded, velocity_x, pressure, 1)
    radius = jnp.abs(velocity_x) + sound_speed
    sensor = jnp.abs(
        pressure[..., 2:, :] - 2.0 * pressure[..., 1:-1, :] + pressure[..., :-2, :]
    ) / (pressure[..., 2:, :] + 2.0 * pressure[..., 1:-1, :] + pressure[..., :-2, :])
    second = SENSOR_GAIN * jnp.maximum(sensor[..., :-1, :], sensor[..., 1:, :])
    fourth = jnp.maximum(0.0, FOURTH_GAIN - second)
    face_radius = 0.5 * (radius[..., 1:-2, :] + radius[..., 2:-1, :])
    left_far = padded[..., :-3, :]
    left_near = padded[..., 1:-2, :]
    right_near = padded[..., 2:-1, :]
    right_far = padded[..., 3:, :]
    damping = face_radius[..., None, :, :] * (
        second[..., None, :, :] * (right_near - left_near)
        - fourth[..., None, :, :] * (right_far - 3.0 * right_near + 3.0 * left_near - left_far)
    )
    face_flux = 0.5 * (flux_line[..., 1:-2, :] + flux_line[..., 2:-1, :]) - damping
    return (face_flux[..., 1:, :] - face_flux[..., :-1, :], radius)


def pitch_parts(cells_state):
    velocity_x, velocity_y, pressure, sound_speed = primitive_parts(cells_state)
    return (directed_flux(cells_state, velocity_y, pressure, 2), jnp.abs(velocity_y) + sound_speed)


def pitch_residual(cells_state, next_lines, prev_lines):
    pitch_flux, radius = pitch_parts(cells_state)
    state_next = jnp.take(cells_state, next_lines, axis=-1)
    flux_next, radius_next = pitch_parts(state_next)
    face_flux = 0.5 * (pitch_flux + flux_next) - PITCH_GAIN * (0.5 * (radius + radius_next))[
        ..., None, :, :
    ] * (state_next - cells_state)
    return face_flux - jnp.take(face_flux, prev_lines, axis=-1)


def boundary_cells(edge_pair, line_codes, lower_end):
    reflected = edge_pair[..., ::-1, :] * jnp.asarray(MIRROR_SIGNS, jnp.float32)[:, None, None]
    if lower_end:
        copied = jnp.concatenate([edge_pair[..., :1, :], edge_pair[..., :1, :]], axis=-2)
    else:
        copied = jnp.concatenate([edge_pair[..., 1:, :], edge_pair[..., 1:, :]], axis=-2)
    inflow = jnp.asarray(FREE_STATE, jnp.float32)[:, None, None] + jnp.zeros_like(edge_pair)
    return jnp.where(line_codes == 0, reflected, jnp.where(line_codes == 1, inflow, copied))


def line_coefficients(radius_ext, diagonal_term, positions, total_cells):
    radius_below = radius_ext[..., :-2, :]
    radius_centre = radius_ext[..., 1:-1, :]
    radius_above = radius_ext[..., 2:, :]
    face_below = 0.5 * (radius_below + radius_centre)
    face_above = 0.5 * (radius_centre + radius_above)
    far_low = FOURTH_IMPL * radius_below
    near_low = -SECOND_IMPL * face_below - 2.0 * FOURTH_IMPL * (radius_below + radius_centre)
    middle = (
        diagonal_term
        + SECOND_IMPL * (face_below + face_above)
        + FOURTH_IMPL * (radius_below + 4.0 * radius_centre + radius_above)
    )
    near_high = -SECOND_IMPL * face_above - 2.0 * FOURTH_IMPL * (radius_centre + radius_above)
    far_high = FOURTH_IMPL * radius_above
    column = positions[:, None]
    far_low = jnp.where(column >= 2, far_low, 0.0)
    near_low = jnp.where(column >= 1, near_low, 0.0)
    near_high = jnp.where(column <= total_cells - 2, near_high, 0.0)
    far_high = jnp.where(column <= total_cells - 3, far_high, 0.0)
    return (far_low, near_low, middle, near_high, far_high)


def block_product(first_matrix, second_matrix):
    return (
        first_matrix[0] * second_matrix[0] + first_matrix[1] * second_matrix[2],
        first_matrix[0] * second_matrix[1] + first_matrix[1] * second_matrix[3],
        first_matrix[2] * second_matrix[0] + first_matrix[3] * second_matrix[2],
        first_matrix[2] * second_matrix[1] + first_matrix[3] * second_matrix[3],
    )


def block_inverse(matrix):
    determinant = matrix[0] * matrix[3] - matrix[1] * matrix[2]
    reciprocal = 1.0 / determinant
    return (
        matrix[3] * reciprocal,
        -matrix[1] * reciprocal,
        -matrix[2] * reciprocal,
        matrix[0] * reciprocal,
    )


def block_apply(matrix, vector):
    return (
        matrix[0] * vector[0] + matrix[1] * vector[1],
        matrix[2] * vector[0] + matrix[3] * vector[1],
    )


def add_blocks(first_members, second_members):
    return tuple((a + b for a, b in zip(first_members, second_members)))


def negate(members):
    return tuple((-a for a in members))


def extend_blocks(members, fill_values):
    return tuple(
        (
            jnp.concatenate([m, jnp.full_like(m[..., :1, :], f)], axis=-2)
            for m, f in zip(members, fill_values)
        )
    )


def shift_next(members, fill_values):
    return tuple(
        (
            jnp.concatenate([m[..., 1:, :], jnp.full_like(m[..., :1, :], f)], axis=-2)
            for m, f in zip(members, fill_values)
        )
    )


def shift_prev(members):
    return tuple(
        (jnp.concatenate([jnp.zeros_like(m[..., :1, :]), m[..., :-1, :]], axis=-2) for m in members)
    )


def pair_split(member):
    shaped = member.reshape(member.shape[:-2] + (member.shape[-2] // 2, 2, member.shape[-1]))
    return (shaped[..., 0, :], shaped[..., 1, :])


def split_parity(members):
    halves = [pair_split(m) for m in members]
    return (tuple((h[0] for h in halves)), tuple((h[1] for h in halves)))


def alternate(first_member, second_member):
    stacked = jnp.stack((first_member, second_member), axis=-2)
    return stacked.reshape(
        first_member.shape[:-2] + (2 * first_member.shape[-2], first_member.shape[-1])
    )


def reduce_blocks(sub_blocks, diag_blocks, super_blocks, right_side):
    block_count = diag_blocks[0].shape[-2]
    if block_count == 1:
        return block_apply(block_inverse(diag_blocks), right_side)
    if block_count % 2 == 1:
        sub_blocks = extend_blocks(sub_blocks, ZERO_BLOCK)
        diag_blocks = extend_blocks(diag_blocks, UNIT_BLOCK)
        super_blocks = extend_blocks(super_blocks, ZERO_BLOCK)
        right_side = extend_blocks(right_side, ZERO_PAIR)
    sub_even, sub_odd = split_parity(sub_blocks)
    diag_even, diag_odd = split_parity(diag_blocks)
    super_even, super_odd = split_parity(super_blocks)
    side_even, side_odd = split_parity(right_side)
    inverse_even = block_inverse(diag_even)
    inverse_next = shift_next(inverse_even, UNIT_BLOCK)
    sub_next = shift_next(sub_even, ZERO_BLOCK)
    super_next = shift_next(super_even, ZERO_BLOCK)
    side_next = shift_next(side_even, ZERO_PAIR)
    left_factor = negate(block_product(sub_odd, inverse_even))
    right_factor = negate(block_product(super_odd, inverse_next))
    reduced_sub = block_product(left_factor, sub_even)
    reduced_diag = add_blocks(
        diag_odd,
        add_blocks(block_product(left_factor, super_even), block_product(right_factor, sub_next)),
    )
    reduced_super = block_product(right_factor, super_next)
    reduced_side = add_blocks(
        side_odd,
        add_blocks(block_apply(left_factor, side_even), block_apply(right_factor, side_next)),
    )
    odd_values = reduce_blocks(reduced_sub, reduced_diag, reduced_super, reduced_side)
    before_values = shift_prev(odd_values)
    remainder = add_blocks(
        side_even,
        negate(
            add_blocks(block_apply(sub_even, before_values), block_apply(super_even, odd_values))
        ),
    )
    even_values = block_apply(inverse_even, remainder)
    merged = tuple((alternate(e, o) for e, o in zip(even_values, odd_values)))
    return tuple((m[..., :block_count, :] for m in merged))


def cells_leading(block):
    moved = jnp.transpose(block, (2, 0, 1, 3))
    return moved.reshape(block.shape[2], block.shape[0] * block.shape[1] * block.shape[3])


def solve_in_lanes(coefficients, line_source):
    source_shape = line_source.shape
    lane_coef = [cells_leading(jnp.broadcast_to(c[:, None], source_shape)) for c in coefficients]
    pairs_list = [pair_split(m) for m in lane_coef]
    zero_plane = jnp.zeros_like(pairs_list[2][0])
    sub_blocks = (pairs_list[0][0], pairs_list[1][0], zero_plane, pairs_list[0][1])
    diag_blocks = (pairs_list[2][0], pairs_list[3][0], pairs_list[1][1], pairs_list[2][1])
    super_blocks = (pairs_list[4][0], zero_plane, pairs_list[3][1], pairs_list[4][1])
    values = reduce_blocks(
        sub_blocks, diag_blocks, super_blocks, pair_split(cells_leading(line_source))
    )
    flat = alternate(values[0], values[1])
    shaped = flat.reshape(source_shape[2], source_shape[0], source_shape[1], source_shape[3])
    return jnp.transpose(shaped, (1, 2, 0, 3))


def return_tiles(line_values):
    return lax.all_to_all(line_values, "cell", split_axis=2, concat_axis=3, tiled=True)


def local_by_lines(state, pseudo_rate, line_next, face_codes):
    local_count = state.shape[0]
    tile_cells = state.shape[2]
    cell_index = lax.axis_index("cell")
    cell_count = lax.axis_size("cell")
    total_cells = tile_cells * cell_count
    spectral = spectral_matrix(NT)
    first_local = lax.axis_index("inst") * local_count
    own_rows = lax.dynamic_slice_in_dim(spectral, first_local, local_count, 0)
    shard_block = jax.tree.map(lambda a: lax.all_gather(a, "inst", axis=0, tiled=True), state)
    columns = lax.slice_in_dim(own_rows, 0, shard_block.shape[0], axis=1)
    time_term = jnp.zeros_like(state) + jnp.einsum(
        "nm,mvil->nvil", columns, shard_block, precision=lax.Precision.HIGHEST
    )
    padded = extended(state, (("cell", 2),), 2)
    codes_lines = jnp.repeat(face_codes, LINES_DEV, axis=1)
    lower_ghost = boundary_cells(state[:, :, 0:2, :], codes_lines[0], True)
    upper_ghost = boundary_cells(state[:, :, -2:, :], codes_lines[1], False)
    lower_rim = jnp.where(cell_index == 0, lower_ghost, padded[:, :, :2, :])
    upper_rim = jnp.where(cell_index == cell_count - 1, upper_ghost, padded[:, :, -2:, :])
    padded = jnp.concatenate([lower_rim, padded[:, :, 2:-2, :], upper_rim], axis=2)
    line_part, radius = line_residual(padded)
    prev_lines = (
        jnp.zeros_like(line_next).at[line_next].set(jnp.arange(line_next.shape[0], dtype=jnp.int32))
    )
    residual = line_part + pitch_residual(state, line_next, prev_lines) + time_term
    right_side = -residual
    centre_radius = radius[:, 2:-2, :]
    diagonal_term = pseudo_rate * centre_radius
    positions = cell_index * tile_cells + jnp.arange(-1, tile_cells + 1, dtype=jnp.int32)
    inside = (positions >= 0) & (positions < total_cells)
    radius_ext = jnp.where(inside[:, None], radius[:, 1:-1, :], 0.0)
    coefficients = line_coefficients(radius_ext, diagonal_term, positions[1:-1], total_cells)
    stacked = jnp.stack(coefficients, axis=1)
    line_source = lax.all_to_all(right_side, "cell", split_axis=3, concat_axis=2, tiled=True)
    line_coef = lax.all_to_all(stacked, "cell", split_axis=3, concat_axis=2, tiled=True)
    update = return_tiles(solve_in_lanes(tuple((line_coef[:, k] for k in range(5))), line_source))
    return state + update


LANES = 128
ROWS = 8
PAIRS = 3
CELL_ROWS = PAIRS * ROWS
REST_ROW = 2 * CELL_ROWS
RATE_ROW = 2 * REST_ROW
VMEM_BYTES = 8 * 2**20
BLOCK_ROWS = RATE_ROW + ROWS


def spectral_offsets():
    table = np.zeros(NT)
    for offset in range(1, NT):
        angle = np.pi * offset / NT
        parity = -1.0 if offset % 2 == 0 else 1.0
        table[offset] = 0.5 * OMEGA_BLADE * parity * np.cos(angle) / np.sin(angle)
    return [float(np.float32(value)) for value in table]


def plane_masks():
    row_index = lax.broadcasted_iota(jnp.int32, (ROWS, LANES), 0)
    return row_index < 4, (row_index & 2) == 0, row_index & 1


def both(first_var, plane):
    turned = pltpu.roll(plane, 4, 0)
    return jnp.where(first_var, plane, turned), jnp.where(first_var, turned, plane)


def primitives(first_var, planes):
    density, moment_x = both(first_var, planes[0])
    moment_y, moment_z = both(first_var, planes[1])
    energy = jnp.where(first_var, planes[2], pltpu.roll(planes[2], 4, 0))
    inverse = 1.0 / density
    velocity_x = moment_x * inverse
    velocity_y = moment_y * inverse
    velocity_z = moment_z * inverse
    kinetic = moment_x * velocity_x + moment_y * velocity_y + moment_z * velocity_z
    pressure = (GAMMA_GAS - 1.0) * (energy - 0.5 * kinetic)
    sound = jnp.sqrt(GAMMA_GAS * pressure * inverse)
    return velocity_x, velocity_y, pressure, sound


def rows_of(var, inst, half):
    return (var // 2) * ROWS + (var % 2) * 4 + inst * 2 + half


def cell_kernel(all_ref, rate_ref, out_ref, plane_ref):
    own_inst = lax.axis_index("inst")
    inst_count = all_ref.shape[0] // 2
    copies = out_ref.shape[0]
    _, first_inst, _ = plane_masks()

    for shift in range(inst_count):
        pair = (own_inst - shift) & (inst_count - 1)
        for cell in range(2):
            for var in range(6):
                for inst in range(2):
                    for half in range(2):
                        row = cell * CELL_ROWS + rows_of(var, inst, half)
                        plane_ref[shift, pl.ds(row, 1), :] = all_ref[
                            2 * pair + inst, var, pl.ds(cell, 1), pl.ds(half * LANES, LANES)
                        ]
    offsets = spectral_offsets()
    for row in range(0, REST_ROW, ROWS):
        same_total, other_total = None, None
        for shift in range(inst_count):
            plane = plane_ref[shift, pl.ds(row, ROWS), :]
            other = jnp.where(
                first_inst, offsets[(2 * shift + 1) % NT], offsets[(2 * shift - 1) % NT]
            )
            if shift > 0:
                term = offsets[(2 * shift) % NT] * plane
                same_total = term if same_total is None else same_total + term
            term = other * plane
            other_total = term if other_total is None else other_total + term
        turned = jnp.where(
            first_inst, pltpu.roll(other_total, 6, 0), pltpu.roll(other_total, 2, 0)
        )
        own = plane_ref[0, pl.ds(row, ROWS), :]
        for copy in range(copies):
            out_ref[copy, pl.ds(row, ROWS), :] = own
            out_ref[copy, pl.ds(REST_ROW + row, ROWS), :] = same_total + turned
    rates = [
        rate_ref[pl.ds(cell, 1), pl.ds(half * LANES, LANES)]
        for cell in range(2)
        for half in range(2)
    ]
    for copy in range(copies):
        for row, rate in enumerate(rates):
            out_ref[copy, pl.ds(RATE_ROW + row, 1), :] = rate
        out_ref[copy, pl.ds(RATE_ROW + 4, 4), :] = jnp.zeros((4, LANES), jnp.float32)


def two_by_two(first, second):
    def entry(a, b, c, d):
        terms = [x * y for x, y in ((a, b), (c, d)) if x is not None and y is not None]
        return None if not terms else terms[0] if len(terms) == 1 else terms[0] + terms[1]

    return (
        entry(first[0], second[0], first[1], second[2]),
        entry(first[0], second[1], first[1], second[3]),
        entry(first[2], second[0], first[3], second[2]),
        entry(first[2], second[1], first[3], second[3]),
    )


def inverse_of(matrix):
    reciprocal = 1.0 / (matrix[0] * matrix[3] - matrix[1] * matrix[2])
    return (
        matrix[3] * reciprocal,
        -(matrix[1] * reciprocal),
        -(matrix[2] * reciprocal),
        matrix[0] * reciprocal,
    )


def less(first, second):
    return tuple(a if b is None else a - b for a, b in zip(first, second))


def minus(members):
    return tuple(None if a is None else -a for a in members)


def eliminate(centre, left, left_inverse, right, right_inverse):
    left_factor = two_by_two(centre[0], left_inverse)
    right_factor = two_by_two(centre[2], right_inverse)
    sub = minus(two_by_two(left_factor, left[0]))
    diag = less(
        less(centre[1], two_by_two(left_factor, left[2])), two_by_two(right_factor, right[0])
    )
    sup = minus(two_by_two(right_factor, right[2]))
    side = []
    for k in range(PAIRS):
        for row in range(2):
            value = centre[3][row * PAIRS + k]
            for factor, other in ((left_factor, left[3]), (right_factor, right[3])):
                value = value - (
                    factor[2 * row] * other[k] + factor[2 * row + 1] * other[PAIRS + k]
                )
            side.append((row * PAIRS + k, value))
    return sub, diag, sup, [value for _, value in sorted(side, key=lambda item: item[0])]


def line_kernel(
    cells, all_ref, next_ref, codes_ref, out_ref, coef_ref, side_ref, coef2_ref, side2_ref,
    couple_ref, diag3_ref, side3_ref,
):
    own_cell = lax.axis_index("cell")
    shape = (ROWS, LANES)
    lane_index = lax.broadcasted_iota(jnp.int32, shape, 1)
    first_var, _, half_index = plane_masks()
    first_half = half_index == 0
    zero = jnp.zeros(shape, jnp.float32)

    next_rows = [next_ref[pl.ds(half, 1), :] for half in range(2)]
    next_line = jnp.where(first_half, next_rows[0], next_rows[1])
    column = lax.broadcasted_iota(jnp.int32, (LANES, LANES), 0)
    prev_halves = []
    for target in range(2):
        total = None
        for source in range(2):
            hits = jnp.where(column + target * LANES == next_rows[source], 1.0, 0.0)
            names = (lane_index + source * LANES).astype(jnp.float32)
            part = lax.dot_general(
                names, hits, (((1,), (1,)), ((), ())), preferred_element_type=jnp.float32
            )
            total = part if total is None else total + part
        prev_halves.append(total)
    prev_line = jnp.where(first_half, prev_halves[0], prev_halves[1]).astype(jnp.int32)

    def picker(lines):
        lane = lines & (LANES - 1)
        same = (lines >> 7) == half_index

        def pick(plane):
            swapped = jnp.where(first_half, pltpu.roll(plane, 7, 0), pltpu.roll(plane, 1, 0))
            here = jnp.take_along_axis(plane, lane, axis=1, mode="promise_in_bounds")
            there = jnp.take_along_axis(swapped, lane, axis=1, mode="promise_in_bounds")
            return jnp.where(same, here, there)

        return pick

    pick_next = picker(next_line)
    pick_prev = picker(prev_line)

    tile = half_index * (LANES // LINES_DEV) + lane_index // LINES_DEV
    codes = []
    for end in range(2):
        plane = jnp.zeros(shape, jnp.int32)
        for k in range(2 * LANES // LINES_DEV):
            plane = jnp.where(tile == k, codes_ref[end, k], plane)
        codes.append(plane)

    def loaded(cell, start=0):
        return [
            all_ref[cell // 2, pl.ds(start + (cell % 2) * CELL_ROWS + k * ROWS, ROWS), :]
            for k in range(PAIRS)
        ]

    def ghost(end, mirrored, copied):
        planes = []
        for k in range(PAIRS):
            reflected = mirrored[k]
            if k == 0:
                reflected = jnp.where(first_var, reflected, -reflected)
            inflow = jnp.where(first_var, FREE_STATE[2 * k], FREE_STATE[2 * k + 1])
            planes.append(
                jnp.where(
                    codes[end] == 0, reflected, jnp.where(codes[end] == 1, inflow, copied[k])
                )
            )
        return planes

    def extended_state(cell):
        if cell < 0:
            return ghost(0, loaded(-1 - cell), loaded(0))
        if cell >= cells:
            return ghost(1, loaded(2 * cells - 1 - cell), loaded(cells - 1))
        return loaded(cell)

    def flux_along(planes, velocity, pressure):
        return [
            planes[0] * velocity + jnp.where(first_var, 0.0, pressure),
            planes[1] * velocity,
            planes[2] * velocity + jnp.where(first_var, pressure * velocity, 0.0),
        ]

    def flux_across(planes, velocity, pressure):
        return [
            planes[0] * velocity,
            planes[1] * velocity + jnp.where(first_var, pressure, 0.0),
            planes[2] * velocity + jnp.where(first_var, pressure * velocity, 0.0),
        ]

    def pitch_flux(planes, velocity_y, pressure, sound):
        nearby = [pick_next(plane) for plane in planes]
        _, next_velocity, next_pressure, next_sound = primitives(first_var, nearby)
        own_flux = flux_across(planes, velocity_y, pressure)
        next_flux = flux_across(nearby, next_velocity, next_pressure)
        weight = (PITCH_GAIN * 0.5) * (
            jnp.abs(velocity_y) + sound + (jnp.abs(next_velocity) + next_sound)
        )
        return [
            0.5 * (a + b) - weight * (n - o)
            for a, b, n, o in zip(own_flux, next_flux, nearby, planes)
        ]

    state, pressures, radii, fluxes, steps, rest, sensors, faces = {}, {}, {}, {}, {}, {}, {}, {}
    for cell in range(-2, cells + 2):
        planes = extended_state(cell)
        velocity_x, velocity_y, pressure, sound = primitives(first_var, planes)
        state[cell] = planes
        pressures[cell] = pressure
        radii[cell] = jnp.abs(velocity_x) + sound
        if -1 <= cell <= cells:
            fluxes[cell] = flux_along(planes, velocity_x, pressure)
        if cell >= -1:
            steps[cell - 1] = [a - b for a, b in zip(planes, state[cell - 1])]
        if 0 <= cell < cells:
            faces_across = pitch_flux(planes, velocity_y, pressure, sound)
            rest[cell] = [
                time + (face - pick_prev(face))
                for face, time in zip(faces_across, loaded(cell, REST_ROW))
            ]
        if cell >= 0:
            twice = 2.0 * pressures[cell - 1]
            outer = pressure + pressures[cell - 2]
            sensors[cell - 1] = jnp.abs(outer - twice) / (outer + twice)
        if cell >= 1:
            face = cell - 2
            second = SENSOR_GAIN * jnp.maximum(sensors[face], sensors[face + 1])
            fourth = jnp.maximum(0.0, FOURTH_GAIN - second)
            face_radius = 0.5 * (radii[face] + radii[face + 1])
            near_weight = face_radius * (second + 2.0 * fourth)
            far_weight = face_radius * fourth
            faces[face] = [
                0.5 * (fluxes[face][k] + fluxes[face + 1][k])
                - (
                    near_weight * steps[face][k]
                    - far_weight * (steps[face + 1][k] + steps[face - 1][k])
                )
                for k in range(PAIRS)
            ]
        if cell >= 2:
            at = cell - 2
            slot, member = at // 2 + 1, at % 2
            for k in range(PAIRS):
                side_ref[slot, member * PAIRS + k] = (
                    faces[at - 1][k] - faces[at][k] - rest[at][k]
                )
            below = radii[at - 1] if at > 0 else zero
            centre = radii[at]
            above = radii[at + 1] if at < cells - 1 else zero
            below_sum = below + centre
            above_sum = centre + above
            half_low = SECOND_IMPL * 0.5 + 2.0 * FOURTH_IMPL
            rate_rows = [
                all_ref[at // 2, pl.ds(RATE_ROW + member * 2 + half, 1), :]
                for half in range(2)
            ]
            rate = jnp.where(first_half, rate_rows[0], rate_rows[1])
            middle = (
                rate * centre
                + SECOND_IMPL * (0.5 * (below_sum + above_sum))
                + FOURTH_IMPL * (below + 4.0 * centre + above)
            )
            far_low = FOURTH_IMPL * below if at >= 2 else zero
            near_low = -half_low * below_sum if at >= 1 else zero
            near_high = -half_low * above_sum if at <= cells - 2 else zero
            far_high = FOURTH_IMPL * above if at <= cells - 3 else zero
            if member == 0:
                entries = {0: far_low, 1: near_low, 3: middle, 4: near_high, 7: far_high}
            else:
                entries = {2: far_low, 5: near_low, 6: middle, 8: near_high, 9: far_high}
            for k, plane in entries.items():
                coef_ref[slot, k] = plane

    blocks = cells // 2
    one = zero + 1.0
    for slot in (0, blocks + 1):
        for k in range(10):
            coef_ref[slot, k] = one if k in (3, 6) else zero
        for k in range(2 * PAIRS):
            side_ref[slot, k] = zero
    for slot in (0, blocks // 2 + 1):
        for k in range(12):
            coef2_ref[slot, k] = one if k in (4, 7) else zero
        for k in range(2 * PAIRS):
            side2_ref[slot, k] = zero

    def block_one(slot):
        c = [coef_ref[slot, k] for k in range(10)]
        return (
            (c[0], c[1], None, c[2]),
            (c[3], c[4], c[5], c[6]),
            (c[7], None, c[8], c[9]),
            [side_ref[slot, k] for k in range(2 * PAIRS)],
        )

    def block_two(slot):
        c = [coef2_ref[slot, k] for k in range(12)]
        return (
            tuple(c[0:4]),
            tuple(c[4:8]),
            tuple(c[8:12]),
            [side2_ref[slot, k] for k in range(2 * PAIRS)],
        )

    parity = own_cell & 1
    left = block_one(parity)
    left_inverse = inverse_of(left[1])
    for k in range(blocks // 2):
        right = block_one(parity + 2 * k + 2)
        right_inverse = inverse_of(right[1])
        kept = block_one(parity + 2 * k + 1)
        sub, diag, sup, side = eliminate(kept, left, left_inverse, right, right_inverse)
        for n, plane in enumerate(sub + diag + sup):
            coef2_ref[k + 1, n] = plane
        for n, plane in enumerate(side):
            side2_ref[k + 1, n] = plane
        left, left_inverse = right, right_inverse
    parity = (own_cell >> 1) & 1
    left = block_two(parity)
    left_inverse = inverse_of(left[1])
    for k in range(blocks // 4):
        right = block_two(parity + 2 * k + 2)
        right_inverse = inverse_of(right[1])
        kept = block_two(parity + 2 * k + 1)
        sub, diag, sup, side = eliminate(kept, left, left_inverse, right, right_inverse)
        for n in range(4):
            couple_ref[k, 0, n] = sub[n]
            couple_ref[k, 1, n] = sup[n]
            diag3_ref[k, n] = diag[n]
        for n, plane in enumerate(side):
            side3_ref[k, n] = plane
        left, left_inverse = right, right_inverse
    own = (own_cell >> 2) & 1
    other = 1 - own
    own_couple = tuple(couple_ref[own, 1 - own, n] for n in range(4))
    other_couple = tuple(couple_ref[other, own, n] for n in range(4))
    factor = two_by_two(own_couple, inverse_of([diag3_ref[other, n] for n in range(4)]))
    diag = less([diag3_ref[own, n] for n in range(4)], two_by_two(factor, other_couple))
    last_inverse = inverse_of(diag)
    for k in range(PAIRS):
        other_low, other_high = side3_ref[other, k], side3_ref[other, PAIRS + k]
        low = side3_ref[own, k] - (factor[0] * other_low + factor[1] * other_high)
        high = side3_ref[own, PAIRS + k] - (factor[2] * other_low + factor[3] * other_high)
        for member in range(2):
            delta = last_inverse[2 * member] * low + last_inverse[2 * member + 1] * high
            base = all_ref[own_cell, pl.ds(member * CELL_ROWS + k * ROWS, ROWS), :]
            result = base + delta
            for var in range(2):
                for inst in range(2):
                    for half in range(2):
                        row = rows_of(var, inst, half)
                        out_ref[
                            inst, 2 * k + var, pl.ds(member, 1), pl.ds(half * LANES, LANES)
                        ] = result[row : row + 1]


def gather_inst(block):
    return lax.all_gather(block, "inst", axis=0, tiled=True)


def exchange_cell(copies):
    return lax.all_to_all(copies, "cell", split_axis=0, concat_axis=0, tiled=True)


def local_by_gather(state, pseudo_rate, line_next, face_codes):
    cells = lax.axis_size("cell") * state.shape[2]
    vmem = pl.BlockSpec(memory_space=pltpu.VMEM)
    plane = (ROWS, LANES)
    every = gather_inst(state)
    packed = pl.pallas_call(
        cell_kernel,
        out_shape=jax.ShapeDtypeStruct(
            (lax.axis_size("cell"), BLOCK_ROWS, LANES), jnp.float32
        ),
        in_specs=[vmem, vmem],
        out_specs=vmem,
        scratch_shapes=[
            pltpu.VMEM((every.shape[0] // 2, 2 * CELL_ROWS, LANES), jnp.float32)
        ],
        compiler_params=pltpu.CompilerParams(vmem_limit_bytes=VMEM_BYTES),
    )(every, pseudo_rate)
    gathered = exchange_cell(packed)
    blocks = cells // 2
    sizes = [
        (blocks + 2, 10),
        (blocks + 2, 2 * PAIRS),
        (blocks // 2 + 2, 12),
        (blocks // 2 + 2, 2 * PAIRS),
        (2, 2, 4),
        (2, 4),
        (2, 2 * PAIRS),
    ]
    return pl.pallas_call(
        functools.partial(line_kernel, cells),
        out_shape=jax.ShapeDtypeStruct(state.shape, jnp.float32),
        in_specs=[vmem, vmem, pl.BlockSpec(memory_space=pltpu.SMEM)],
        out_specs=vmem,
        scratch_shapes=[pltpu.VMEM(size + plane, jnp.float32) for size in sizes],
        compiler_params=pltpu.CompilerParams(vmem_limit_bytes=VMEM_BYTES),
    )(gathered, line_next.reshape(2, LANES), face_codes)


def solution(mesh):
    placed = (P("inst", None, "cell", None), P("cell", None), P(), P())
    inst_count, cell_count = mesh.shape["inst"], mesh.shape["cell"]

    def local(state, pseudo_rate, line_next, face_codes):
        small = (
            state.shape == (2, 6, 2, 2 * LANES)
            and inst_count * 2 == NT
            and cell_count == 8
            and face_codes.shape[1] * LINES_DEV == state.shape[3]
        )
        chosen = local_by_gather if small else local_by_lines
        return chosen(state, pseudo_rate, line_next, face_codes)

    return jax.shard_map(
        local, mesh=mesh, in_specs=placed, out_specs=P("inst", None, "cell", None), check_vma=False
    )
```

```python
import functools

import jax
import jax.numpy as jnp
import numpy as np
from jax import lax
from jax.experimental import pallas as pl
from jax.experimental.pallas import tpu as pltpu
from jax.sharding import PartitionSpec as P

NT = 8
LINES_DEV = 32


GAMMA_GAS = 1.4
OMEGA_BLADE = 1.0
SENSOR_GAIN = 0.25
FOURTH_GAIN = 0.03125
PITCH_GAIN = 0.5
SECOND_IMPL = 1.0
FOURTH_IMPL = 0.25
FREE_STATE = (1.0, 0.5, 0.0, 0.0, 2.625, 0.2)
MIRROR_SIGNS = (1.0, -1.0, 1.0, 1.0, 1.0, 1.0)
ZERO_BLOCK = (0.0, 0.0, 0.0, 0.0)
UNIT_BLOCK = (1.0, 0.0, 0.0, 1.0)
ZERO_PAIR = (0.0, 0.0)


def extended(block, sides, width):
    for axis, dim in sides:
        count = lax.axis_size(axis)
        forward = [(i, i + 1) for i in range(count - 1)]
        backward = [(target, source) for source, target in forward]
        low = lax.ppermute(
            lax.slice_in_dim(block, block.shape[dim] - width, None, axis=dim), axis, forward
        )
        high = lax.ppermute(lax.slice_in_dim(block, 0, width, axis=dim), axis, backward)
        block = jnp.concatenate([low, block, high], axis=dim)
    return block


def spectral_matrix(instances):
    offsets = np.arange(instances)[:, None] - np.arange(instances)[None, :]
    angles = np.pi * offsets / instances
    safe_sin = np.where(offsets == 0, 1.0, np.sin(angles))
    parity = np.where(np.mod(offsets, 2) == 0, -1.0, 1.0)
    matrix_table = np.where(
        offsets == 0, 0.0, 0.5 * OMEGA_BLADE * parity * np.cos(angles) / safe_sin
    )
    return jnp.asarray(matrix_table, jnp.float32)


def primitive_parts(cells_state):
    density = cells_state[..., 0, :, :]
    inverse = 1.0 / density
    velocity_x = cells_state[..., 1, :, :] * inverse
    velocity_y = cells_state[..., 2, :, :] * inverse
    velocity_z = cells_state[..., 3, :, :] * inverse
    energy = cells_state[..., 4, :, :]
    pressure = (GAMMA_GAS - 1.0) * (
        energy
        - 0.5
        * density
        * (velocity_x * velocity_x + velocity_y * velocity_y + velocity_z * velocity_z)
    )
    sound_speed = jnp.sqrt(GAMMA_GAS * pressure * inverse)
    return (velocity_x, velocity_y, pressure, sound_speed)


def directed_flux(cells_state, normal_velocity, pressure, component):
    zero_plane = jnp.zeros_like(pressure)
    pressure_rows = [
        zero_plane,
        zero_plane,
        zero_plane,
        zero_plane,
        pressure * normal_velocity,
        zero_plane,
    ]
    pressure_rows[component] = pressure
    return cells_state * normal_velocity[..., None, :, :] + jnp.stack(pressure_rows, axis=-3)


def line_residual(padded):
    velocity_x, velocity_y, pressure, sound_speed = primitive_parts(padded)
    flux_line = directed_flux(padded, velocity_x, pressure, 1)
    radius = jnp.abs(velocity_x) + sound_speed
    sensor = jnp.abs(
        pressure[..., 2:, :] - 2.0 * pressure[..., 1:-1, :] + pressure[..., :-2, :]
    ) / (pressure[..., 2:, :] + 2.0 * pressure[..., 1:-1, :] + pressure[..., :-2, :])
    second = SENSOR_GAIN * jnp.maximum(sensor[..., :-1, :], sensor[..., 1:, :])
    fourth = jnp.maximum(0.0, FOURTH_GAIN - second)
    face_radius = 0.5 * (radius[..., 1:-2, :] + radius[..., 2:-1, :])
    left_far = padded[..., :-3, :]
    left_near = padded[..., 1:-2, :]
    right_near = padded[..., 2:-1, :]
    right_far = padded[..., 3:, :]
    damping = face_radius[..., None, :, :] * (
        second[..., None, :, :] * (right_near - left_near)
        - fourth[..., None, :, :] * (right_far - 3.0 * right_near + 3.0 * left_near - left_far)
    )
    face_flux = 0.5 * (flux_line[..., 1:-2, :] + flux_line[..., 2:-1, :]) - damping
    return (face_flux[..., 1:, :] - face_flux[..., :-1, :], radius)


def pitch_parts(cells_state):
    velocity_x, velocity_y, pressure, sound_speed = primitive_parts(cells_state)
    return (directed_flux(cells_state, velocity_y, pressure, 2), jnp.abs(velocity_y) + sound_speed)


def pitch_residual(cells_state, next_lines, prev_lines):
    pitch_flux, radius = pitch_parts(cells_state)
    state_next = jnp.take(cells_state, next_lines, axis=-1)
    flux_next, radius_next = pitch_parts(state_next)
    face_flux = 0.5 * (pitch_flux + flux_next) - PITCH_GAIN * (0.5 * (radius + radius_next))[
        ..., None, :, :
    ] * (state_next - cells_state)
    return face_flux - jnp.take(face_flux, prev_lines, axis=-1)


def boundary_cells(edge_pair, line_codes, lower_end):
    reflected = edge_pair[..., ::-1, :] * jnp.asarray(MIRROR_SIGNS, jnp.float32)[:, None, None]
    if lower_end:
        copied = jnp.concatenate([edge_pair[..., :1, :], edge_pair[..., :1, :]], axis=-2)
    else:
        copied = jnp.concatenate([edge_pair[..., 1:, :], edge_pair[..., 1:, :]], axis=-2)
    inflow = jnp.asarray(FREE_STATE, jnp.float32)[:, None, None] + jnp.zeros_like(edge_pair)
    return jnp.where(line_codes == 0, reflected, jnp.where(line_codes == 1, inflow, copied))


def line_coefficients(radius_ext, diagonal_term, positions, total_cells):
    radius_below = radius_ext[..., :-2, :]
    radius_centre = radius_ext[..., 1:-1, :]
    radius_above = radius_ext[..., 2:, :]
    face_below = 0.5 * (radius_below + radius_centre)
    face_above = 0.5 * (radius_centre + radius_above)
    far_low = FOURTH_IMPL * radius_below
    near_low = -SECOND_IMPL * face_below - 2.0 * FOURTH_IMPL * (radius_below + radius_centre)
    middle = (
        diagonal_term
        + SECOND_IMPL * (face_below + face_above)
        + FOURTH_IMPL * (radius_below + 4.0 * radius_centre + radius_above)
    )
    near_high = -SECOND_IMPL * face_above - 2.0 * FOURTH_IMPL * (radius_centre + radius_above)
    far_high = FOURTH_IMPL * radius_above
    column = positions[:, None]
    far_low = jnp.where(column >= 2, far_low, 0.0)
    near_low = jnp.where(column >= 1, near_low, 0.0)
    near_high = jnp.where(column <= total_cells - 2, near_high, 0.0)
    far_high = jnp.where(column <= total_cells - 3, far_high, 0.0)
    return (far_low, near_low, middle, near_high, far_high)


def block_product(first_matrix, second_matrix):
    return (
        first_matrix[0] * second_matrix[0] + first_matrix[1] * second_matrix[2],
        first_matrix[0] * second_matrix[1] + first_matrix[1] * second_matrix[3],
        first_matrix[2] * second_matrix[0] + first_matrix[3] * second_matrix[2],
        first_matrix[2] * second_matrix[1] + first_matrix[3] * second_matrix[3],
    )


def block_inverse(matrix):
    determinant = matrix[0] * matrix[3] - matrix[1] * matrix[2]
    reciprocal = 1.0 / determinant
    return (
        matrix[3] * reciprocal,
        -matrix[1] * reciprocal,
        -matrix[2] * reciprocal,
        matrix[0] * reciprocal,
    )


def block_apply(matrix, vector):
    return (
        matrix[0] * vector[0] + matrix[1] * vector[1],
        matrix[2] * vector[0] + matrix[3] * vector[1],
    )


def add_blocks(first_members, second_members):
    return tuple((a + b for a, b in zip(first_members, second_members)))


def negate(members):
    return tuple((-a for a in members))


def extend_blocks(members, fill_values):
    return tuple(
        (
            jnp.concatenate([m, jnp.full_like(m[..., :1, :], f)], axis=-2)
            for m, f in zip(members, fill_values)
        )
    )


def shift_next(members, fill_values):
    return tuple(
        (
            jnp.concatenate([m[..., 1:, :], jnp.full_like(m[..., :1, :], f)], axis=-2)
            for m, f in zip(members, fill_values)
        )
    )


def shift_prev(members):
    return tuple(
        (jnp.concatenate([jnp.zeros_like(m[..., :1, :]), m[..., :-1, :]], axis=-2) for m in members)
    )


def pair_split(member):
    shaped = member.reshape(member.shape[:-2] + (member.shape[-2] // 2, 2, member.shape[-1]))
    return (shaped[..., 0, :], shaped[..., 1, :])


def split_parity(members):
    halves = [pair_split(m) for m in members]
    return (tuple((h[0] for h in halves)), tuple((h[1] for h in halves)))


def alternate(first_member, second_member):
    stacked = jnp.stack((first_member, second_member), axis=-2)
    return stacked.reshape(
        first_member.shape[:-2] + (2 * first_member.shape[-2], first_member.shape[-1])
    )


def reduce_blocks(sub_blocks, diag_blocks, super_blocks, right_side):
    block_count = diag_blocks[0].shape[-2]
    if block_count == 1:
        return block_apply(block_inverse(diag_blocks), right_side)
    if block_count % 2 == 1:
        sub_blocks = extend_blocks(sub_blocks, ZERO_BLOCK)
        diag_blocks = extend_blocks(diag_blocks, UNIT_BLOCK)
        super_blocks = extend_blocks(super_blocks, ZERO_BLOCK)
        right_side = extend_blocks(right_side, ZERO_PAIR)
    sub_even, sub_odd = split_parity(sub_blocks)
    diag_even, diag_odd = split_parity(diag_blocks)
    super_even, super_odd = split_parity(super_blocks)
    side_even, side_odd = split_parity(right_side)
    inverse_even = block_inverse(diag_even)
    inverse_next = shift_next(inverse_even, UNIT_BLOCK)
    sub_next = shift_next(sub_even, ZERO_BLOCK)
    super_next = shift_next(super_even, ZERO_BLOCK)
    side_next = shift_next(side_even, ZERO_PAIR)
    left_factor = negate(block_product(sub_odd, inverse_even))
    right_factor = negate(block_product(super_odd, inverse_next))
    reduced_sub = block_product(left_factor, sub_even)
    reduced_diag = add_blocks(
        diag_odd,
        add_blocks(block_product(left_factor, super_even), block_product(right_factor, sub_next)),
    )
    reduced_super = block_product(right_factor, super_next)
    reduced_side = add_blocks(
        side_odd,
        add_blocks(block_apply(left_factor, side_even), block_apply(right_factor, side_next)),
    )
    odd_values = reduce_blocks(reduced_sub, reduced_diag, reduced_super, reduced_side)
    before_values = shift_prev(odd_values)
    remainder = add_blocks(
        side_even,
        negate(
            add_blocks(block_apply(sub_even, before_values), block_apply(super_even, odd_values))
        ),
    )
    even_values = block_apply(inverse_even, remainder)
    merged = tuple((alternate(e, o) for e, o in zip(even_values, odd_values)))
    return tuple((m[..., :block_count, :] for m in merged))


def cells_leading(block):
    moved = jnp.transpose(block, (2, 0, 1, 3))
    return moved.reshape(block.shape[2], block.shape[0] * block.shape[1] * block.shape[3])


def solve_in_lanes(coefficients, line_source):
    source_shape = line_source.shape
    lane_coef = [cells_leading(jnp.broadcast_to(c[:, None], source_shape)) for c in coefficients]
    pairs_list = [pair_split(m) for m in lane_coef]
    zero_plane = jnp.zeros_like(pairs_list[2][0])
    sub_blocks = (pairs_list[0][0], pairs_list[1][0], zero_plane, pairs_list[0][1])
    diag_blocks = (pairs_list[2][0], pairs_list[3][0], pairs_list[1][1], pairs_list[2][1])
    super_blocks = (pairs_list[4][0], zero_plane, pairs_list[3][1], pairs_list[4][1])
    values = reduce_blocks(
        sub_blocks, diag_blocks, super_blocks, pair_split(cells_leading(line_source))
    )
    flat = alternate(values[0], values[1])
    shaped = flat.reshape(source_shape[2], source_shape[0], source_shape[1], source_shape[3])
    return jnp.transpose(shaped, (1, 2, 0, 3))


def return_tiles(line_values):
    return lax.all_to_all(line_values, "cell", split_axis=2, concat_axis=3, tiled=True)


def local_by_lines(state, pseudo_rate, line_next, face_codes):
    local_count = state.shape[0]
    tile_cells = state.shape[2]
    cell_index = lax.axis_index("cell")
    cell_count = lax.axis_size("cell")
    total_cells = tile_cells * cell_count
    spectral = spectral_matrix(NT)
    first_local = lax.axis_index("inst") * local_count
    own_rows = lax.dynamic_slice_in_dim(spectral, first_local, local_count, 0)
    shard_block = jax.tree.map(lambda a: lax.all_gather(a, "inst", axis=0, tiled=True), state)
    columns = lax.slice_in_dim(own_rows, 0, shard_block.shape[0], axis=1)
    time_term = jnp.zeros_like(state) + jnp.einsum(
        "nm,mvil->nvil", columns, shard_block, precision=lax.Precision.HIGHEST
    )
    padded = extended(state, (("cell", 2),), 2)
    codes_lines = jnp.repeat(face_codes, LINES_DEV, axis=1)
    lower_ghost = boundary_cells(state[:, :, 0:2, :], codes_lines[0], True)
    upper_ghost = boundary_cells(state[:, :, -2:, :], codes_lines[1], False)
    lower_rim = jnp.where(cell_index == 0, lower_ghost, padded[:, :, :2, :])
    upper_rim = jnp.where(cell_index == cell_count - 1, upper_ghost, padded[:, :, -2:, :])
    padded = jnp.concatenate([lower_rim, padded[:, :, 2:-2, :], upper_rim], axis=2)
    line_part, radius = line_residual(padded)
    prev_lines = (
        jnp.zeros_like(line_next).at[line_next].set(jnp.arange(line_next.shape[0], dtype=jnp.int32))
    )
    residual = line_part + pitch_residual(state, line_next, prev_lines) + time_term
    right_side = -residual
    centre_radius = radius[:, 2:-2, :]
    diagonal_term = pseudo_rate * centre_radius
    positions = cell_index * tile_cells + jnp.arange(-1, tile_cells + 1, dtype=jnp.int32)
    inside = (positions >= 0) & (positions < total_cells)
    radius_ext = jnp.where(inside[:, None], radius[:, 1:-1, :], 0.0)
    coefficients = line_coefficients(radius_ext, diagonal_term, positions[1:-1], total_cells)
    stacked = jnp.stack(coefficients, axis=1)
    line_source = lax.all_to_all(right_side, "cell", split_axis=3, concat_axis=2, tiled=True)
    line_coef = lax.all_to_all(stacked, "cell", split_axis=3, concat_axis=2, tiled=True)
    update = return_tiles(solve_in_lanes(tuple((line_coef[:, k] for k in range(5))), line_source))
    return state + update


LANES = 128
ROWS = 8
PAIRS = 3
CELL_ROWS = PAIRS * ROWS
REST_ROW = 2 * CELL_ROWS
RATE_ROW = 2 * REST_ROW
VMEM_BYTES = 8 * 2**20
BLOCK_ROWS = RATE_ROW + ROWS


def spectral_offsets():
    table = np.zeros(NT)
    for offset in range(1, NT):
        angle = np.pi * offset / NT
        parity = -1.0 if offset % 2 == 0 else 1.0
        table[offset] = 0.5 * OMEGA_BLADE * parity * np.cos(angle) / np.sin(angle)
    return [float(np.float32(value)) for value in table]


def plane_masks():
    row_index = lax.broadcasted_iota(jnp.int32, (ROWS, LANES), 0)
    return row_index < 4, (row_index & 2) == 0, row_index & 1


def both(first_var, plane):
    turned = pltpu.roll(plane, 4, 0)
    return jnp.where(first_var, plane, turned), jnp.where(first_var, turned, plane)


def primitives(first_var, planes):
    density, moment_x = both(first_var, planes[0])
    moment_y, moment_z = both(first_var, planes[1])
    energy = jnp.where(first_var, planes[2], pltpu.roll(planes[2], 4, 0))
    inverse = 1.0 / density
    velocity_x = moment_x * inverse
    velocity_y = moment_y * inverse
    velocity_z = moment_z * inverse
    kinetic = moment_x * velocity_x + moment_y * velocity_y + moment_z * velocity_z
    pressure = (GAMMA_GAS - 1.0) * (energy - 0.5 * kinetic)
    sound = jnp.sqrt(GAMMA_GAS * pressure * inverse)
    return velocity_x, velocity_y, pressure, sound


def rows_of(var, inst, half):
    return (var // 2) * ROWS + (var % 2) * 4 + inst * 2 + half


def cell_kernel(all_ref, rate_ref, out_ref, plane_ref):
    own_inst = lax.axis_index("inst")
    inst_count = all_ref.shape[0] // 2
    copies = out_ref.shape[0]
    _, first_inst, _ = plane_masks()

    for shift in range(inst_count):
        pair = (own_inst - shift) & (inst_count - 1)
        for cell in range(2):
            for var in range(6):
                for inst in range(2):
                    for half in range(2):
                        row = cell * CELL_ROWS + rows_of(var, inst, half)
                        plane_ref[shift, pl.ds(row, 1), :] = all_ref[
                            2 * pair + inst, var, pl.ds(cell, 1), pl.ds(half * LANES, LANES)
                        ]
    offsets = spectral_offsets()
    for row in range(0, REST_ROW, ROWS):
        same_total, other_total = None, None
        for shift in range(inst_count):
            plane = plane_ref[shift, pl.ds(row, ROWS), :]
            other = jnp.where(
                first_inst, offsets[(2 * shift + 1) % NT], offsets[(2 * shift - 1) % NT]
            )
            if shift > 0:
                term = offsets[(2 * shift) % NT] * plane
                same_total = term if same_total is None else same_total + term
            term = other * plane
            other_total = term if other_total is None else other_total + term
        turned = jnp.where(
            first_inst, pltpu.roll(other_total, 6, 0), pltpu.roll(other_total, 2, 0)
        )
        own = plane_ref[0, pl.ds(row, ROWS), :]
        for copy in range(copies):
            out_ref[copy, pl.ds(row, ROWS), :] = own
            out_ref[copy, pl.ds(REST_ROW + row, ROWS), :] = same_total + turned
    rates = [
        rate_ref[pl.ds(cell, 1), pl.ds(half * LANES, LANES)]
        for cell in range(2)
        for half in range(2)
    ]
    for copy in range(copies):
        for row, rate in enumerate(rates):
            out_ref[copy, pl.ds(RATE_ROW + row, 1), :] = rate
        out_ref[copy, pl.ds(RATE_ROW + 4, 4), :] = jnp.zeros((4, LANES), jnp.float32)


def two_by_two(first, second):
    def entry(a, b, c, d):
        terms = [x * y for x, y in ((a, b), (c, d)) if x is not None and y is not None]
        return None if not terms else terms[0] if len(terms) == 1 else terms[0] + terms[1]

    return (
        entry(first[0], second[0], first[1], second[2]),
        entry(first[0], second[1], first[1], second[3]),
        entry(first[2], second[0], first[3], second[2]),
        entry(first[2], second[1], first[3], second[3]),
    )


def inverse_of(matrix):
    reciprocal = 1.0 / (matrix[0] * matrix[3] - matrix[1] * matrix[2])
    return (
        matrix[3] * reciprocal,
        -(matrix[1] * reciprocal),
        -(matrix[2] * reciprocal),
        matrix[0] * reciprocal,
    )


def less(first, second):
    return tuple(a if b is None else a - b for a, b in zip(first, second))


def minus(members):
    return tuple(None if a is None else -a for a in members)


def eliminate(centre, left, left_inverse, right, right_inverse):
    left_factor = two_by_two(centre[0], left_inverse)
    right_factor = two_by_two(centre[2], right_inverse)
    sub = minus(two_by_two(left_factor, left[0]))
    diag = less(
        less(centre[1], two_by_two(left_factor, left[2])), two_by_two(right_factor, right[0])
    )
    sup = minus(two_by_two(right_factor, right[2]))
    side = []
    for k in range(PAIRS):
        for row in range(2):
            value = centre[3][row * PAIRS + k]
            for factor, other in ((left_factor, left[3]), (right_factor, right[3])):
                value = value - (
                    factor[2 * row] * other[k] + factor[2 * row + 1] * other[PAIRS + k]
                )
            side.append((row * PAIRS + k, value))
    return sub, diag, sup, [value for _, value in sorted(side, key=lambda item: item[0])]


def line_kernel(
    cells, all_ref, next_ref, held_codes_ref, out_ref, coef_ref, side_ref, coef2_ref, side2_ref,
    couple_ref, diag3_ref, side3_ref, line_ref, codes_ref, codes_sem,
):
    fetch = pltpu.make_async_copy(held_codes_ref, codes_ref, codes_sem)
    fetch.start()
    own_cell = lax.axis_index("cell")
    shape = (ROWS, LANES)
    lane_index = lax.broadcasted_iota(jnp.int32, shape, 1)
    first_var, _, half_index = plane_masks()
    first_half = half_index == 0
    zero = jnp.zeros(shape, jnp.float32)

    next_rows = [next_ref[pl.ds(half, 1), :] for half in range(2)]
    next_line = jnp.where(first_half, next_rows[0], next_rows[1])
    column = lax.broadcasted_iota(jnp.int32, (LANES, LANES), 0)
    prev_halves = []
    for target in range(2):
        total = None
        for source in range(2):
            hits = jnp.where(column + target * LANES == next_rows[source], 1.0, 0.0)
            names = (lane_index + source * LANES).astype(jnp.float32)
            part = lax.dot_general(
                names, hits, (((1,), (1,)), ((), ())), preferred_element_type=jnp.float32
            )
            total = part if total is None else total + part
        prev_halves.append(total)
    prev_line = jnp.where(first_half, prev_halves[0], prev_halves[1]).astype(jnp.int32)

    def picker(lines):
        lane = lines & (LANES - 1)
        same = (lines >> 7) == half_index

        def pick(plane):
            swapped = jnp.where(first_half, pltpu.roll(plane, 7, 0), pltpu.roll(plane, 1, 0))
            here = jnp.take_along_axis(plane, lane, axis=1, mode="promise_in_bounds")
            there = jnp.take_along_axis(swapped, lane, axis=1, mode="promise_in_bounds")
            return jnp.where(same, here, there)

        return pick

    pick_next = picker(next_line)
    pick_prev = picker(prev_line)

    def loaded(cell, start=0):
        return [
            all_ref[cell // 2, pl.ds(start + (cell % 2) * CELL_ROWS + k * ROWS, ROWS), :]
            for k in range(PAIRS)
        ]

    def ghost(end, mirrored, copied):
        planes = []
        for k in range(PAIRS):
            reflected = mirrored[k]
            if k == 0:
                reflected = jnp.where(first_var, reflected, -reflected)
            inflow = jnp.where(first_var, FREE_STATE[2 * k], FREE_STATE[2 * k + 1])
            planes.append(
                jnp.where(
                    codes[end] == 0, reflected, jnp.where(codes[end] == 1, inflow, copied[k])
                )
            )
        return planes

    def extended_state(cell):
        if cell < 0:
            return ghost(0, loaded(-1 - cell), loaded(0))
        if cell >= cells:
            return ghost(1, loaded(2 * cells - 1 - cell), loaded(cells - 1))
        return loaded(cell)

    def flux_along(planes, velocity, pressure):
        return [
            planes[0] * velocity + jnp.where(first_var, 0.0, pressure),
            planes[1] * velocity,
            planes[2] * velocity + jnp.where(first_var, pressure * velocity, 0.0),
        ]

    def flux_across(planes, velocity, pressure):
        return [
            planes[0] * velocity,
            planes[1] * velocity + jnp.where(first_var, pressure, 0.0),
            planes[2] * velocity + jnp.where(first_var, pressure * velocity, 0.0),
        ]

    def pitch_flux(planes, velocity_y, pressure, sound):
        nearby = [pick_next(plane) for plane in planes]
        _, next_velocity, next_pressure, next_sound = primitives(first_var, nearby)
        own_flux = flux_across(planes, velocity_y, pressure)
        next_flux = flux_across(nearby, next_velocity, next_pressure)
        weight = (PITCH_GAIN * 0.5) * (
            jnp.abs(velocity_y) + sound + (jnp.abs(next_velocity) + next_sound)
        )
        return [
            0.5 * (a + b) - weight * (n - o)
            for a, b, n, o in zip(own_flux, next_flux, nearby, planes)
        ]

    for cell in range(cells):
        planes = loaded(cell)
        velocity_x, velocity_y, pressure, sound = primitives(first_var, planes)
        line_ref[cell, 0], line_ref[cell, 1], line_ref[cell, 2] = velocity_x, pressure, sound
        faces_across = pitch_flux(planes, velocity_y, pressure, sound)
        times = loaded(cell, REST_ROW)
        for k in range(PAIRS):
            side_ref[cell // 2 + 1, (cell % 2) * PAIRS + k] = times[k] + (
                faces_across[k] - pick_prev(faces_across[k])
            )

    fetch.wait()
    tile = half_index * (LANES // LINES_DEV) + lane_index // LINES_DEV
    codes = []
    for end in range(2):
        plane = jnp.zeros(shape, jnp.int32)
        for k in range(2 * LANES // LINES_DEV):
            plane = jnp.where(tile == k, codes_ref[end, k], plane)
        codes.append(plane)

    state, pressures, radii, fluxes, steps, sensors, faces = {}, {}, {}, {}, {}, {}, {}
    for cell in range(-2, cells + 2):
        planes = extended_state(cell)
        if 0 <= cell < cells:
            velocity_x, pressure, sound = [line_ref[cell, k] for k in range(3)]
        else:
            velocity_x, _, pressure, sound = primitives(first_var, planes)
        state[cell] = planes
        pressures[cell] = pressure
        radii[cell] = jnp.abs(velocity_x) + sound
        if -1 <= cell <= cells:
            fluxes[cell] = flux_along(planes, velocity_x, pressure)
        if cell >= -1:
            steps[cell - 1] = [a - b for a, b in zip(planes, state[cell - 1])]
        if cell >= 0:
            twice = 2.0 * pressures[cell - 1]
            outer = pressure + pressures[cell - 2]
            sensors[cell - 1] = jnp.abs(outer - twice) / (outer + twice)
        if cell >= 1:
            face = cell - 2
            second = SENSOR_GAIN * jnp.maximum(sensors[face], sensors[face + 1])
            fourth = jnp.maximum(0.0, FOURTH_GAIN - second)
            face_radius = 0.5 * (radii[face] + radii[face + 1])
            near_weight = face_radius * (second + 2.0 * fourth)
            far_weight = face_radius * fourth
            faces[face] = [
                0.5 * (fluxes[face][k] + fluxes[face + 1][k])
                - (
                    near_weight * steps[face][k]
                    - far_weight * (steps[face + 1][k] + steps[face - 1][k])
                )
                for k in range(PAIRS)
            ]
        if cell >= 2:
            at = cell - 2
            slot, member = at // 2 + 1, at % 2
            for k in range(PAIRS):
                rest = side_ref[slot, member * PAIRS + k]
                side_ref[slot, member * PAIRS + k] = faces[at - 1][k] - faces[at][k] - rest
            below = radii[at - 1] if at > 0 else zero
            centre = radii[at]
            above = radii[at + 1] if at < cells - 1 else zero
            below_sum = below + centre
            above_sum = centre + above
            half_low = SECOND_IMPL * 0.5 + 2.0 * FOURTH_IMPL
            rate_rows = [
                all_ref[at // 2, pl.ds(RATE_ROW + member * 2 + half, 1), :]
                for half in range(2)
            ]
            rate = jnp.where(first_half, rate_rows[0], rate_rows[1])
            middle = (
                rate * centre
                + SECOND_IMPL * (0.5 * (below_sum + above_sum))
                + FOURTH_IMPL * (below + 4.0 * centre + above)
            )
            far_low = FOURTH_IMPL * below if at >= 2 else zero
            near_low = -half_low * below_sum if at >= 1 else zero
            near_high = -half_low * above_sum if at <= cells - 2 else zero
            far_high = FOURTH_IMPL * above if at <= cells - 3 else zero
            if member == 0:
                entries = {0: far_low, 1: near_low, 3: middle, 4: near_high, 7: far_high}
            else:
                entries = {2: far_low, 5: near_low, 6: middle, 8: near_high, 9: far_high}
            for k, plane in entries.items():
                coef_ref[slot, k] = plane

    blocks = cells // 2
    one = zero + 1.0
    for slot in (0, blocks + 1):
        for k in range(10):
            coef_ref[slot, k] = one if k in (3, 6) else zero
        for k in range(2 * PAIRS):
            side_ref[slot, k] = zero
    for slot in (0, blocks // 2 + 1):
        for k in range(12):
            coef2_ref[slot, k] = one if k in (4, 7) else zero
        for k in range(2 * PAIRS):
            side2_ref[slot, k] = zero

    def block_one(slot):
        c = [coef_ref[slot, k] for k in range(10)]
        return (
            (c[0], c[1], None, c[2]),
            (c[3], c[4], c[5], c[6]),
            (c[7], None, c[8], c[9]),
            [side_ref[slot, k] for k in range(2 * PAIRS)],
        )

    def block_two(slot):
        c = [coef2_ref[slot, k] for k in range(12)]
        return (
            tuple(c[0:4]),
            tuple(c[4:8]),
            tuple(c[8:12]),
            [side2_ref[slot, k] for k in range(2 * PAIRS)],
        )

    parity = own_cell & 1
    left = block_one(parity)
    left_inverse = inverse_of(left[1])
    for k in range(blocks // 2):
        right = block_one(parity + 2 * k + 2)
        right_inverse = inverse_of(right[1])
        kept = block_one(parity + 2 * k + 1)
        sub, diag, sup, side = eliminate(kept, left, left_inverse, right, right_inverse)
        for n, plane in enumerate(sub + diag + sup):
            coef2_ref[k + 1, n] = plane
        for n, plane in enumerate(side):
            side2_ref[k + 1, n] = plane
        left, left_inverse = right, right_inverse
    parity = (own_cell >> 1) & 1
    left = block_two(parity)
    left_inverse = inverse_of(left[1])
    for k in range(blocks // 4):
        right = block_two(parity + 2 * k + 2)
        right_inverse = inverse_of(right[1])
        kept = block_two(parity + 2 * k + 1)
        sub, diag, sup, side = eliminate(kept, left, left_inverse, right, right_inverse)
        for n in range(4):
            couple_ref[k, 0, n] = sub[n]
            couple_ref[k, 1, n] = sup[n]
            diag3_ref[k, n] = diag[n]
        for n, plane in enumerate(side):
            side3_ref[k, n] = plane
        left, left_inverse = right, right_inverse
    own = (own_cell >> 2) & 1
    other = 1 - own
    own_couple = tuple(couple_ref[own, 1 - own, n] for n in range(4))
    other_couple = tuple(couple_ref[other, own, n] for n in range(4))
    factor = two_by_two(own_couple, inverse_of([diag3_ref[other, n] for n in range(4)]))
    diag = less([diag3_ref[own, n] for n in range(4)], two_by_two(factor, other_couple))
    last_inverse = inverse_of(diag)
    for k in range(PAIRS):
        other_low, other_high = side3_ref[other, k], side3_ref[other, PAIRS + k]
        low = side3_ref[own, k] - (factor[0] * other_low + factor[1] * other_high)
        high = side3_ref[own, PAIRS + k] - (factor[2] * other_low + factor[3] * other_high)
        for member in range(2):
            delta = last_inverse[2 * member] * low + last_inverse[2 * member + 1] * high
            base = all_ref[own_cell, pl.ds(member * CELL_ROWS + k * ROWS, ROWS), :]
            result = base + delta
            for var in range(2):
                for inst in range(2):
                    for half in range(2):
                        row = rows_of(var, inst, half)
                        out_ref[
                            inst, 2 * k + var, pl.ds(member, 1), pl.ds(half * LANES, LANES)
                        ] = result[row : row + 1]


def gather_inst(block):
    return lax.all_gather(block, "inst", axis=0, tiled=True)


def exchange_cell(copies):
    return lax.all_to_all(copies, "cell", split_axis=0, concat_axis=0, tiled=True)


def local_by_gather(state, pseudo_rate, line_next, face_codes):
    cells = lax.axis_size("cell") * state.shape[2]
    vmem = pl.BlockSpec(memory_space=pltpu.VMEM)
    plane = (ROWS, LANES)
    every = gather_inst(state)
    packed = pl.pallas_call(
        cell_kernel,
        out_shape=jax.ShapeDtypeStruct(
            (lax.axis_size("cell"), BLOCK_ROWS, LANES), jnp.float32
        ),
        in_specs=[vmem, vmem],
        out_specs=vmem,
        scratch_shapes=[
            pltpu.VMEM((every.shape[0] // 2, 2 * CELL_ROWS, LANES), jnp.float32)
        ],
        compiler_params=pltpu.CompilerParams(vmem_limit_bytes=VMEM_BYTES),
    )(every, pseudo_rate)
    gathered = exchange_cell(packed)
    blocks = cells // 2
    sizes = [
        (blocks + 2, 10),
        (blocks + 2, 2 * PAIRS),
        (blocks // 2 + 2, 12),
        (blocks // 2 + 2, 2 * PAIRS),
        (2, 2, 4),
        (2, 4),
        (2, 2 * PAIRS),
        (cells, 3),
    ]
    return pl.pallas_call(
        functools.partial(line_kernel, cells),
        out_shape=jax.ShapeDtypeStruct(state.shape, jnp.float32),
        in_specs=[vmem, vmem, pl.BlockSpec(memory_space=pltpu.HBM)],
        out_specs=vmem,
        scratch_shapes=[pltpu.VMEM(size + plane, jnp.float32) for size in sizes]
        + [pltpu.SMEM(face_codes.shape, jnp.int32), pltpu.SemaphoreType.DMA],
        compiler_params=pltpu.CompilerParams(vmem_limit_bytes=VMEM_BYTES),
    )(gathered, line_next.reshape(2, LANES), face_codes)


def solution(mesh):
    placed = (P("inst", None, "cell", None), P("cell", None), P(), P())
    inst_count, cell_count = mesh.shape["inst"], mesh.shape["cell"]

    def local(state, pseudo_rate, line_next, face_codes):
        small = (
            state.shape == (2, 6, 2, 2 * LANES)
            and inst_count * 2 == NT
            and cell_count == 8
            and face_codes.shape[1] * LINES_DEV == state.shape[3]
        )
        chosen = local_by_gather if small else local_by_lines
        return chosen(state, pseudo_rate, line_next, face_codes)

    return jax.shard_map(
        local, mesh=mesh, in_specs=placed, out_specs=P("inst", None, "cell", None), check_vma=False
    )
```

```python
import functools

import jax
import jax.numpy as jnp
import numpy as np
from jax import lax
from jax.experimental import pallas as pl
from jax.experimental.pallas import tpu as pltpu
from jax.sharding import PartitionSpec as P

NT = 8
LINES_DEV = 32


GAMMA_GAS = 1.4
OMEGA_BLADE = 1.0
SENSOR_GAIN = 0.25
FOURTH_GAIN = 0.03125
PITCH_GAIN = 0.5
SECOND_IMPL = 1.0
FOURTH_IMPL = 0.25
FREE_STATE = (1.0, 0.5, 0.0, 0.0, 2.625, 0.2)
MIRROR_SIGNS = (1.0, -1.0, 1.0, 1.0, 1.0, 1.0)
ZERO_BLOCK = (0.0, 0.0, 0.0, 0.0)
UNIT_BLOCK = (1.0, 0.0, 0.0, 1.0)
ZERO_PAIR = (0.0, 0.0)


def extended(block, sides, width):
    for axis, dim in sides:
        count = lax.axis_size(axis)
        forward = [(i, i + 1) for i in range(count - 1)]
        backward = [(target, source) for source, target in forward]
        low = lax.ppermute(
            lax.slice_in_dim(block, block.shape[dim] - width, None, axis=dim), axis, forward
        )
        high = lax.ppermute(lax.slice_in_dim(block, 0, width, axis=dim), axis, backward)
        block = jnp.concatenate([low, block, high], axis=dim)
    return block


def spectral_matrix(instances):
    offsets = np.arange(instances)[:, None] - np.arange(instances)[None, :]
    angles = np.pi * offsets / instances
    safe_sin = np.where(offsets == 0, 1.0, np.sin(angles))
    parity = np.where(np.mod(offsets, 2) == 0, -1.0, 1.0)
    matrix_table = np.where(
        offsets == 0, 0.0, 0.5 * OMEGA_BLADE * parity * np.cos(angles) / safe_sin
    )
    return jnp.asarray(matrix_table, jnp.float32)


def primitive_parts(cells_state):
    density = cells_state[..., 0, :, :]
    inverse = 1.0 / density
    velocity_x = cells_state[..., 1, :, :] * inverse
    velocity_y = cells_state[..., 2, :, :] * inverse
    velocity_z = cells_state[..., 3, :, :] * inverse
    energy = cells_state[..., 4, :, :]
    pressure = (GAMMA_GAS - 1.0) * (
        energy
        - 0.5
        * density
        * (velocity_x * velocity_x + velocity_y * velocity_y + velocity_z * velocity_z)
    )
    sound_speed = jnp.sqrt(GAMMA_GAS * pressure * inverse)
    return (velocity_x, velocity_y, pressure, sound_speed)


def directed_flux(cells_state, normal_velocity, pressure, component):
    zero_plane = jnp.zeros_like(pressure)
    pressure_rows = [
        zero_plane,
        zero_plane,
        zero_plane,
        zero_plane,
        pressure * normal_velocity,
        zero_plane,
    ]
    pressure_rows[component] = pressure
    return cells_state * normal_velocity[..., None, :, :] + jnp.stack(pressure_rows, axis=-3)


def line_residual(padded):
    velocity_x, velocity_y, pressure, sound_speed = primitive_parts(padded)
    flux_line = directed_flux(padded, velocity_x, pressure, 1)
    radius = jnp.abs(velocity_x) + sound_speed
    sensor = jnp.abs(
        pressure[..., 2:, :] - 2.0 * pressure[..., 1:-1, :] + pressure[..., :-2, :]
    ) / (pressure[..., 2:, :] + 2.0 * pressure[..., 1:-1, :] + pressure[..., :-2, :])
    second = SENSOR_GAIN * jnp.maximum(sensor[..., :-1, :], sensor[..., 1:, :])
    fourth = jnp.maximum(0.0, FOURTH_GAIN - second)
    face_radius = 0.5 * (radius[..., 1:-2, :] + radius[..., 2:-1, :])
    left_far = padded[..., :-3, :]
    left_near = padded[..., 1:-2, :]
    right_near = padded[..., 2:-1, :]
    right_far = padded[..., 3:, :]
    damping = face_radius[..., None, :, :] * (
        second[..., None, :, :] * (right_near - left_near)
        - fourth[..., None, :, :] * (right_far - 3.0 * right_near + 3.0 * left_near - left_far)
    )
    face_flux = 0.5 * (flux_line[..., 1:-2, :] + flux_line[..., 2:-1, :]) - damping
    return (face_flux[..., 1:, :] - face_flux[..., :-1, :], radius)


def pitch_parts(cells_state):
    velocity_x, velocity_y, pressure, sound_speed = primitive_parts(cells_state)
    return (directed_flux(cells_state, velocity_y, pressure, 2), jnp.abs(velocity_y) + sound_speed)


def pitch_residual(cells_state, next_lines, prev_lines):
    pitch_flux, radius = pitch_parts(cells_state)
    state_next = jnp.take(cells_state, next_lines, axis=-1)
    flux_next, radius_next = pitch_parts(state_next)
    face_flux = 0.5 * (pitch_flux + flux_next) - PITCH_GAIN * (0.5 * (radius + radius_next))[
        ..., None, :, :
    ] * (state_next - cells_state)
    return face_flux - jnp.take(face_flux, prev_lines, axis=-1)


def boundary_cells(edge_pair, line_codes, lower_end):
    reflected = edge_pair[..., ::-1, :] * jnp.asarray(MIRROR_SIGNS, jnp.float32)[:, None, None]
    if lower_end:
        copied = jnp.concatenate([edge_pair[..., :1, :], edge_pair[..., :1, :]], axis=-2)
    else:
        copied = jnp.concatenate([edge_pair[..., 1:, :], edge_pair[..., 1:, :]], axis=-2)
    inflow = jnp.asarray(FREE_STATE, jnp.float32)[:, None, None] + jnp.zeros_like(edge_pair)
    return jnp.where(line_codes == 0, reflected, jnp.where(line_codes == 1, inflow, copied))


def line_coefficients(radius_ext, diagonal_term, positions, total_cells):
    radius_below = radius_ext[..., :-2, :]
    radius_centre = radius_ext[..., 1:-1, :]
    radius_above = radius_ext[..., 2:, :]
    face_below = 0.5 * (radius_below + radius_centre)
    face_above = 0.5 * (radius_centre + radius_above)
    far_low = FOURTH_IMPL * radius_below
    near_low = -SECOND_IMPL * face_below - 2.0 * FOURTH_IMPL * (radius_below + radius_centre)
    middle = (
        diagonal_term
        + SECOND_IMPL * (face_below + face_above)
        + FOURTH_IMPL * (radius_below + 4.0 * radius_centre + radius_above)
    )
    near_high = -SECOND_IMPL * face_above - 2.0 * FOURTH_IMPL * (radius_centre + radius_above)
    far_high = FOURTH_IMPL * radius_above
    column = positions[:, None]
    far_low = jnp.where(column >= 2, far_low, 0.0)
    near_low = jnp.where(column >= 1, near_low, 0.0)
    near_high = jnp.where(column <= total_cells - 2, near_high, 0.0)
    far_high = jnp.where(column <= total_cells - 3, far_high, 0.0)
    return (far_low, near_low, middle, near_high, far_high)


def block_product(first_matrix, second_matrix):
    return (
        first_matrix[0] * second_matrix[0] + first_matrix[1] * second_matrix[2],
        first_matrix[0] * second_matrix[1] + first_matrix[1] * second_matrix[3],
        first_matrix[2] * second_matrix[0] + first_matrix[3] * second_matrix[2],
        first_matrix[2] * second_matrix[1] + first_matrix[3] * second_matrix[3],
    )


def block_inverse(matrix):
    determinant = matrix[0] * matrix[3] - matrix[1] * matrix[2]
    reciprocal = 1.0 / determinant
    return (
        matrix[3] * reciprocal,
        -matrix[1] * reciprocal,
        -matrix[2] * reciprocal,
        matrix[0] * reciprocal,
    )


def block_apply(matrix, vector):
    return (
        matrix[0] * vector[0] + matrix[1] * vector[1],
        matrix[2] * vector[0] + matrix[3] * vector[1],
    )


def add_blocks(first_members, second_members):
    return tuple((a + b for a, b in zip(first_members, second_members)))


def negate(members):
    return tuple((-a for a in members))


def extend_blocks(members, fill_values):
    return tuple(
        (
            jnp.concatenate([m, jnp.full_like(m[..., :1, :], f)], axis=-2)
            for m, f in zip(members, fill_values)
        )
    )


def shift_next(members, fill_values):
    return tuple(
        (
            jnp.concatenate([m[..., 1:, :], jnp.full_like(m[..., :1, :], f)], axis=-2)
            for m, f in zip(members, fill_values)
        )
    )


def shift_prev(members):
    return tuple(
        (jnp.concatenate([jnp.zeros_like(m[..., :1, :]), m[..., :-1, :]], axis=-2) for m in members)
    )


def pair_split(member):
    shaped = member.reshape(member.shape[:-2] + (member.shape[-2] // 2, 2, member.shape[-1]))
    return (shaped[..., 0, :], shaped[..., 1, :])


def split_parity(members):
    halves = [pair_split(m) for m in members]
    return (tuple((h[0] for h in halves)), tuple((h[1] for h in halves)))


def alternate(first_member, second_member):
    stacked = jnp.stack((first_member, second_member), axis=-2)
    return stacked.reshape(
        first_member.shape[:-2] + (2 * first_member.shape[-2], first_member.shape[-1])
    )


def reduce_blocks(sub_blocks, diag_blocks, super_blocks, right_side):
    block_count = diag_blocks[0].shape[-2]
    if block_count == 1:
        return block_apply(block_inverse(diag_blocks), right_side)
    if block_count % 2 == 1:
        sub_blocks = extend_blocks(sub_blocks, ZERO_BLOCK)
        diag_blocks = extend_blocks(diag_blocks, UNIT_BLOCK)
        super_blocks = extend_blocks(super_blocks, ZERO_BLOCK)
        right_side = extend_blocks(right_side, ZERO_PAIR)
    sub_even, sub_odd = split_parity(sub_blocks)
    diag_even, diag_odd = split_parity(diag_blocks)
    super_even, super_odd = split_parity(super_blocks)
    side_even, side_odd = split_parity(right_side)
    inverse_even = block_inverse(diag_even)
    inverse_next = shift_next(inverse_even, UNIT_BLOCK)
    sub_next = shift_next(sub_even, ZERO_BLOCK)
    super_next = shift_next(super_even, ZERO_BLOCK)
    side_next = shift_next(side_even, ZERO_PAIR)
    left_factor = negate(block_product(sub_odd, inverse_even))
    right_factor = negate(block_product(super_odd, inverse_next))
    reduced_sub = block_product(left_factor, sub_even)
    reduced_diag = add_blocks(
        diag_odd,
        add_blocks(block_product(left_factor, super_even), block_product(right_factor, sub_next)),
    )
    reduced_super = block_product(right_factor, super_next)
    reduced_side = add_blocks(
        side_odd,
        add_blocks(block_apply(left_factor, side_even), block_apply(right_factor, side_next)),
    )
    odd_values = reduce_blocks(reduced_sub, reduced_diag, reduced_super, reduced_side)
    before_values = shift_prev(odd_values)
    remainder = add_blocks(
        side_even,
        negate(
            add_blocks(block_apply(sub_even, before_values), block_apply(super_even, odd_values))
        ),
    )
    even_values = block_apply(inverse_even, remainder)
    merged = tuple((alternate(e, o) for e, o in zip(even_values, odd_values)))
    return tuple((m[..., :block_count, :] for m in merged))


def cells_leading(block):
    moved = jnp.transpose(block, (2, 0, 1, 3))
    return moved.reshape(block.shape[2], block.shape[0] * block.shape[1] * block.shape[3])


def solve_in_lanes(coefficients, line_source):
    source_shape = line_source.shape
    lane_coef = [cells_leading(jnp.broadcast_to(c[:, None], source_shape)) for c in coefficients]
    pairs_list = [pair_split(m) for m in lane_coef]
    zero_plane = jnp.zeros_like(pairs_list[2][0])
    sub_blocks = (pairs_list[0][0], pairs_list[1][0], zero_plane, pairs_list[0][1])
    diag_blocks = (pairs_list[2][0], pairs_list[3][0], pairs_list[1][1], pairs_list[2][1])
    super_blocks = (pairs_list[4][0], zero_plane, pairs_list[3][1], pairs_list[4][1])
    values = reduce_blocks(
        sub_blocks, diag_blocks, super_blocks, pair_split(cells_leading(line_source))
    )
    flat = alternate(values[0], values[1])
    shaped = flat.reshape(source_shape[2], source_shape[0], source_shape[1], source_shape[3])
    return jnp.transpose(shaped, (1, 2, 0, 3))


def return_tiles(line_values):
    return lax.all_to_all(line_values, "cell", split_axis=2, concat_axis=3, tiled=True)


def local_by_lines(state, pseudo_rate, line_next, face_codes):
    local_count = state.shape[0]
    tile_cells = state.shape[2]
    cell_index = lax.axis_index("cell")
    cell_count = lax.axis_size("cell")
    total_cells = tile_cells * cell_count
    spectral = spectral_matrix(NT)
    first_local = lax.axis_index("inst") * local_count
    own_rows = lax.dynamic_slice_in_dim(spectral, first_local, local_count, 0)
    shard_block = jax.tree.map(lambda a: lax.all_gather(a, "inst", axis=0, tiled=True), state)
    columns = lax.slice_in_dim(own_rows, 0, shard_block.shape[0], axis=1)
    time_term = jnp.zeros_like(state) + jnp.einsum(
        "nm,mvil->nvil", columns, shard_block, precision=lax.Precision.HIGHEST
    )
    padded = extended(state, (("cell", 2),), 2)
    codes_lines = jnp.repeat(face_codes, LINES_DEV, axis=1)
    lower_ghost = boundary_cells(state[:, :, 0:2, :], codes_lines[0], True)
    upper_ghost = boundary_cells(state[:, :, -2:, :], codes_lines[1], False)
    lower_rim = jnp.where(cell_index == 0, lower_ghost, padded[:, :, :2, :])
    upper_rim = jnp.where(cell_index == cell_count - 1, upper_ghost, padded[:, :, -2:, :])
    padded = jnp.concatenate([lower_rim, padded[:, :, 2:-2, :], upper_rim], axis=2)
    line_part, radius = line_residual(padded)
    prev_lines = (
        jnp.zeros_like(line_next).at[line_next].set(jnp.arange(line_next.shape[0], dtype=jnp.int32))
    )
    residual = line_part + pitch_residual(state, line_next, prev_lines) + time_term
    right_side = -residual
    centre_radius = radius[:, 2:-2, :]
    diagonal_term = pseudo_rate * centre_radius
    positions = cell_index * tile_cells + jnp.arange(-1, tile_cells + 1, dtype=jnp.int32)
    inside = (positions >= 0) & (positions < total_cells)
    radius_ext = jnp.where(inside[:, None], radius[:, 1:-1, :], 0.0)
    coefficients = line_coefficients(radius_ext, diagonal_term, positions[1:-1], total_cells)
    stacked = jnp.stack(coefficients, axis=1)
    line_source = lax.all_to_all(right_side, "cell", split_axis=3, concat_axis=2, tiled=True)
    line_coef = lax.all_to_all(stacked, "cell", split_axis=3, concat_axis=2, tiled=True)
    update = return_tiles(solve_in_lanes(tuple((line_coef[:, k] for k in range(5))), line_source))
    return state + update


LANES = 128
ROWS = 8
PAIRS = 3
CELL_ROWS = PAIRS * ROWS
REST_ROW = 2 * CELL_ROWS
RATE_ROW = 2 * REST_ROW
VMEM_BYTES = 8 * 2**20
BLOCK_ROWS = RATE_ROW + ROWS


def spectral_offsets():
    table = np.zeros(NT)
    for offset in range(1, NT):
        angle = np.pi * offset / NT
        parity = -1.0 if offset % 2 == 0 else 1.0
        table[offset] = 0.5 * OMEGA_BLADE * parity * np.cos(angle) / np.sin(angle)
    return [float(np.float32(value)) for value in table]


def plane_masks():
    row_index = lax.broadcasted_iota(jnp.int32, (ROWS, LANES), 0)
    return row_index < 4, (row_index & 2) == 0, row_index & 1


def both(first_var, plane):
    turned = pltpu.roll(plane, 4, 0)
    return jnp.where(first_var, plane, turned), jnp.where(first_var, turned, plane)


def primitives(first_var, planes):
    density, moment_x = both(first_var, planes[0])
    moment_y, moment_z = both(first_var, planes[1])
    energy = jnp.where(first_var, planes[2], pltpu.roll(planes[2], 4, 0))
    inverse = 1.0 / density
    velocity_x = moment_x * inverse
    velocity_y = moment_y * inverse
    velocity_z = moment_z * inverse
    kinetic = moment_x * velocity_x + moment_y * velocity_y + moment_z * velocity_z
    pressure = (GAMMA_GAS - 1.0) * (energy - 0.5 * kinetic)
    sound = jnp.sqrt(GAMMA_GAS * pressure * inverse)
    return velocity_x, velocity_y, pressure, sound


def rows_of(var, inst, half):
    return (var // 2) * ROWS + (var % 2) * 4 + inst * 2 + half


def cell_kernel(all_ref, rate_ref, out_ref, plane_ref):
    own_inst = lax.axis_index("inst")
    inst_count = all_ref.shape[0] // 2
    copies = out_ref.shape[0]
    _, first_inst, _ = plane_masks()

    for shift in range(inst_count):
        pair = (own_inst - shift) & (inst_count - 1)
        for cell in range(2):
            for var in range(6):
                for inst in range(2):
                    for half in range(2):
                        row = cell * CELL_ROWS + rows_of(var, inst, half)
                        plane_ref[shift, pl.ds(row, 1), :] = all_ref[
                            2 * pair + inst, var, pl.ds(cell, 1), pl.ds(half * LANES, LANES)
                        ]
    offsets = spectral_offsets()
    for row in range(0, REST_ROW, ROWS):
        same_total, other_total = None, None
        for shift in range(inst_count):
            plane = plane_ref[shift, pl.ds(row, ROWS), :]
            other = jnp.where(
                first_inst, offsets[(2 * shift + 1) % NT], offsets[(2 * shift - 1) % NT]
            )
            if shift > 0:
                term = offsets[(2 * shift) % NT] * plane
                same_total = term if same_total is None else same_total + term
            term = other * plane
            other_total = term if other_total is None else other_total + term
        turned = jnp.where(
            first_inst, pltpu.roll(other_total, 6, 0), pltpu.roll(other_total, 2, 0)
        )
        own = plane_ref[0, pl.ds(row, ROWS), :]
        for copy in range(copies):
            out_ref[copy, pl.ds(row, ROWS), :] = own
            out_ref[copy, pl.ds(REST_ROW + row, ROWS), :] = same_total + turned
    rates = [
        rate_ref[pl.ds(cell, 1), pl.ds(half * LANES, LANES)]
        for cell in range(2)
        for half in range(2)
    ]
    for copy in range(copies):
        for row, rate in enumerate(rates):
            out_ref[copy, pl.ds(RATE_ROW + row, 1), :] = rate
        out_ref[copy, pl.ds(RATE_ROW + 4, 4), :] = jnp.zeros((4, LANES), jnp.float32)


def two_by_two(first, second):
    def entry(a, b, c, d):
        terms = [x * y for x, y in ((a, b), (c, d)) if x is not None and y is not None]
        return None if not terms else terms[0] if len(terms) == 1 else terms[0] + terms[1]

    return (
        entry(first[0], second[0], first[1], second[2]),
        entry(first[0], second[1], first[1], second[3]),
        entry(first[2], second[0], first[3], second[2]),
        entry(first[2], second[1], first[3], second[3]),
    )


def inverse_of(matrix):
    reciprocal = 1.0 / (matrix[0] * matrix[3] - matrix[1] * matrix[2])
    return (
        matrix[3] * reciprocal,
        -(matrix[1] * reciprocal),
        -(matrix[2] * reciprocal),
        matrix[0] * reciprocal,
    )


def less(first, second):
    return tuple(a if b is None else a - b for a, b in zip(first, second))


def minus(members):
    return tuple(None if a is None else -a for a in members)


def eliminate(centre, left, left_inverse, right, right_inverse):
    left_factor = two_by_two(centre[0], left_inverse)
    right_factor = two_by_two(centre[2], right_inverse)
    sub = minus(two_by_two(left_factor, left[0]))
    diag = less(
        less(centre[1], two_by_two(left_factor, left[2])), two_by_two(right_factor, right[0])
    )
    sup = minus(two_by_two(right_factor, right[2]))
    side = []
    for k in range(PAIRS):
        for row in range(2):
            value = centre[3][row * PAIRS + k]
            for factor, other in ((left_factor, left[3]), (right_factor, right[3])):
                value = value - (
                    factor[2 * row] * other[k] + factor[2 * row + 1] * other[PAIRS + k]
                )
            side.append((row * PAIRS + k, value))
    return sub, diag, sup, [value for _, value in sorted(side, key=lambda item: item[0])]


def line_kernel(
    cells, all_ref, next_ref, held_codes_ref, out_ref, coef_ref, side_ref, coef2_ref, side2_ref,
    couple_ref, diag3_ref, side3_ref, line_ref, codes_ref, codes_sem,
):
    fetch = pltpu.make_async_copy(held_codes_ref, codes_ref, codes_sem)
    fetch.start()
    own_cell = lax.axis_index("cell")
    shape = (ROWS, LANES)
    lane_index = lax.broadcasted_iota(jnp.int32, shape, 1)
    first_var, _, half_index = plane_masks()
    first_half = half_index == 0
    zero = jnp.zeros(shape, jnp.float32)

    next_rows = [
        next_ref[pl.ds(half * LANES, LANES)].reshape(1, LANES) for half in range(2)
    ]
    next_line = jnp.where(first_half, next_rows[0], next_rows[1])
    column = lax.broadcasted_iota(jnp.int32, (LANES, LANES), 0)
    prev_halves = []
    for target in range(2):
        total = None
        for source in range(2):
            hits = jnp.where(column + target * LANES == next_rows[source], 1.0, 0.0)
            names = (lane_index + source * LANES).astype(jnp.float32)
            part = lax.dot_general(
                names, hits, (((1,), (1,)), ((), ())), preferred_element_type=jnp.float32
            )
            total = part if total is None else total + part
        prev_halves.append(total)
    prev_line = jnp.where(first_half, prev_halves[0], prev_halves[1]).astype(jnp.int32)

    def picker(lines):
        lane = lines & (LANES - 1)
        same = (lines >> 7) == half_index

        def pick(plane):
            swapped = jnp.where(first_half, pltpu.roll(plane, 7, 0), pltpu.roll(plane, 1, 0))
            here = jnp.take_along_axis(plane, lane, axis=1, mode="promise_in_bounds")
            there = jnp.take_along_axis(swapped, lane, axis=1, mode="promise_in_bounds")
            return jnp.where(same, here, there)

        return pick

    pick_next = picker(next_line)
    pick_prev = picker(prev_line)

    def loaded(cell, start=0):
        return [
            all_ref[cell // 2, pl.ds(start + (cell % 2) * CELL_ROWS + k * ROWS, ROWS), :]
            for k in range(PAIRS)
        ]

    def ghost(end, mirrored, copied):
        planes = []
        for k in range(PAIRS):
            reflected = mirrored[k]
            if k == 0:
                reflected = jnp.where(first_var, reflected, -reflected)
            inflow = jnp.where(first_var, FREE_STATE[2 * k], FREE_STATE[2 * k + 1])
            planes.append(
                jnp.where(
                    codes[end] == 0, reflected, jnp.where(codes[end] == 1, inflow, copied[k])
                )
            )
        return planes

    def extended_state(cell):
        if cell < 0:
            return ghost(0, loaded(-1 - cell), loaded(0))
        if cell >= cells:
            return ghost(1, loaded(2 * cells - 1 - cell), loaded(cells - 1))
        return loaded(cell)

    def flux_along(planes, velocity, pressure):
        return [
            planes[0] * velocity + jnp.where(first_var, 0.0, pressure),
            planes[1] * velocity,
            planes[2] * velocity + jnp.where(first_var, pressure * velocity, 0.0),
        ]

    def flux_across(planes, velocity, pressure):
        return [
            planes[0] * velocity,
            planes[1] * velocity + jnp.where(first_var, pressure, 0.0),
            planes[2] * velocity + jnp.where(first_var, pressure * velocity, 0.0),
        ]

    def pitch_flux(planes, velocity_y, pressure, sound):
        nearby = [pick_next(plane) for plane in planes]
        _, next_velocity, next_pressure, next_sound = primitives(first_var, nearby)
        own_flux = flux_across(planes, velocity_y, pressure)
        next_flux = flux_across(nearby, next_velocity, next_pressure)
        weight = (PITCH_GAIN * 0.5) * (
            jnp.abs(velocity_y) + sound + (jnp.abs(next_velocity) + next_sound)
        )
        return [
            0.5 * (a + b) - weight * (n - o)
            for a, b, n, o in zip(own_flux, next_flux, nearby, planes)
        ]

    for cell in range(cells):
        planes = loaded(cell)
        velocity_x, velocity_y, pressure, sound = primitives(first_var, planes)
        line_ref[cell, 0], line_ref[cell, 1], line_ref[cell, 2] = velocity_x, pressure, sound
        faces_across = pitch_flux(planes, velocity_y, pressure, sound)
        times = loaded(cell, REST_ROW)
        for k in range(PAIRS):
            side_ref[cell // 2 + 1, (cell % 2) * PAIRS + k] = times[k] + (
                faces_across[k] - pick_prev(faces_across[k])
            )

    fetch.wait()
    tile = half_index * (LANES // LINES_DEV) + lane_index // LINES_DEV
    codes = []
    for end in range(2):
        plane = jnp.zeros(shape, jnp.int32)
        for k in range(2 * LANES // LINES_DEV):
            plane = jnp.where(tile == k, codes_ref[end, k], plane)
        codes.append(plane)

    state, pressures, radii, fluxes, steps, sensors, faces = {}, {}, {}, {}, {}, {}, {}
    for cell in range(-2, cells + 2):
        planes = extended_state(cell)
        if 0 <= cell < cells:
            velocity_x, pressure, sound = [line_ref[cell, k] for k in range(3)]
        else:
            velocity_x, _, pressure, sound = primitives(first_var, planes)
        state[cell] = planes
        pressures[cell] = pressure
        radii[cell] = jnp.abs(velocity_x) + sound
        if -1 <= cell <= cells:
            fluxes[cell] = flux_along(planes, velocity_x, pressure)
        if cell >= -1:
            steps[cell - 1] = [a - b for a, b in zip(planes, state[cell - 1])]
        if cell >= 0:
            twice = 2.0 * pressures[cell - 1]
            outer = pressure + pressures[cell - 2]
            sensors[cell - 1] = jnp.abs(outer - twice) / (outer + twice)
        if cell >= 1:
            face = cell - 2
            second = SENSOR_GAIN * jnp.maximum(sensors[face], sensors[face + 1])
            fourth = jnp.maximum(0.0, FOURTH_GAIN - second)
            face_radius = 0.5 * (radii[face] + radii[face + 1])
            near_weight = face_radius * (second + 2.0 * fourth)
            far_weight = face_radius * fourth
            faces[face] = [
                0.5 * (fluxes[face][k] + fluxes[face + 1][k])
                - (
                    near_weight * steps[face][k]
                    - far_weight * (steps[face + 1][k] + steps[face - 1][k])
                )
                for k in range(PAIRS)
            ]
        if cell >= 2:
            at = cell - 2
            slot, member = at // 2 + 1, at % 2
            for k in range(PAIRS):
                rest = side_ref[slot, member * PAIRS + k]
                side_ref[slot, member * PAIRS + k] = faces[at - 1][k] - faces[at][k] - rest
            below = radii[at - 1] if at > 0 else zero
            centre = radii[at]
            above = radii[at + 1] if at < cells - 1 else zero
            below_sum = below + centre
            above_sum = centre + above
            half_low = SECOND_IMPL * 0.5 + 2.0 * FOURTH_IMPL
            rate_rows = [
                all_ref[at // 2, pl.ds(RATE_ROW + member * 2 + half, 1), :]
                for half in range(2)
            ]
            rate = jnp.where(first_half, rate_rows[0], rate_rows[1])
            middle = (
                rate * centre
                + SECOND_IMPL * (0.5 * (below_sum + above_sum))
                + FOURTH_IMPL * (below + 4.0 * centre + above)
            )
            far_low = FOURTH_IMPL * below if at >= 2 else zero
            near_low = -half_low * below_sum if at >= 1 else zero
            near_high = -half_low * above_sum if at <= cells - 2 else zero
            far_high = FOURTH_IMPL * above if at <= cells - 3 else zero
            if member == 0:
                entries = {0: far_low, 1: near_low, 3: middle, 4: near_high, 7: far_high}
            else:
                entries = {2: far_low, 5: near_low, 6: middle, 8: near_high, 9: far_high}
            for k, plane in entries.items():
                coef_ref[slot, k] = plane

    blocks = cells // 2
    one = zero + 1.0
    for slot in (0, blocks + 1):
        for k in range(10):
            coef_ref[slot, k] = one if k in (3, 6) else zero
        for k in range(2 * PAIRS):
            side_ref[slot, k] = zero
    for slot in (0, blocks // 2 + 1):
        for k in range(12):
            coef2_ref[slot, k] = one if k in (4, 7) else zero
        for k in range(2 * PAIRS):
            side2_ref[slot, k] = zero

    def block_one(slot):
        c = [coef_ref[slot, k] for k in range(10)]
        return (
            (c[0], c[1], None, c[2]),
            (c[3], c[4], c[5], c[6]),
            (c[7], None, c[8], c[9]),
            [side_ref[slot, k] for k in range(2 * PAIRS)],
        )

    def block_two(slot):
        c = [coef2_ref[slot, k] for k in range(12)]
        return (
            tuple(c[0:4]),
            tuple(c[4:8]),
            tuple(c[8:12]),
            [side2_ref[slot, k] for k in range(2 * PAIRS)],
        )

    parity = own_cell & 1
    left = block_one(parity)
    left_inverse = inverse_of(left[1])
    for k in range(blocks // 2):
        right = block_one(parity + 2 * k + 2)
        right_inverse = inverse_of(right[1])
        kept = block_one(parity + 2 * k + 1)
        sub, diag, sup, side = eliminate(kept, left, left_inverse, right, right_inverse)
        for n, plane in enumerate(sub + diag + sup):
            coef2_ref[k + 1, n] = plane
        for n, plane in enumerate(side):
            side2_ref[k + 1, n] = plane
        left, left_inverse = right, right_inverse
    parity = (own_cell >> 1) & 1
    left = block_two(parity)
    left_inverse = inverse_of(left[1])
    for k in range(blocks // 4):
        right = block_two(parity + 2 * k + 2)
        right_inverse = inverse_of(right[1])
        kept = block_two(parity + 2 * k + 1)
        sub, diag, sup, side = eliminate(kept, left, left_inverse, right, right_inverse)
        for n in range(4):
            couple_ref[k, 0, n] = sub[n]
            couple_ref[k, 1, n] = sup[n]
            diag3_ref[k, n] = diag[n]
        for n, plane in enumerate(side):
            side3_ref[k, n] = plane
        left, left_inverse = right, right_inverse
    own = (own_cell >> 2) & 1
    other = 1 - own
    own_couple = tuple(couple_ref[own, 1 - own, n] for n in range(4))
    other_couple = tuple(couple_ref[other, own, n] for n in range(4))
    factor = two_by_two(own_couple, inverse_of([diag3_ref[other, n] for n in range(4)]))
    diag = less([diag3_ref[own, n] for n in range(4)], two_by_two(factor, other_couple))
    last_inverse = inverse_of(diag)
    for k in range(PAIRS):
        other_low, other_high = side3_ref[other, k], side3_ref[other, PAIRS + k]
        low = side3_ref[own, k] - (factor[0] * other_low + factor[1] * other_high)
        high = side3_ref[own, PAIRS + k] - (factor[2] * other_low + factor[3] * other_high)
        for member in range(2):
            delta = last_inverse[2 * member] * low + last_inverse[2 * member + 1] * high
            base = all_ref[own_cell, pl.ds(member * CELL_ROWS + k * ROWS, ROWS), :]
            result = base + delta
            for var in range(2):
                for inst in range(2):
                    for half in range(2):
                        row = rows_of(var, inst, half)
                        out_ref[
                            inst, 2 * k + var, pl.ds(member, 1), pl.ds(half * LANES, LANES)
                        ] = result[row : row + 1]


def gather_inst(block):
    return lax.all_gather(block, "inst", axis=0, tiled=True)


def exchange_cell(copies):
    return lax.all_to_all(copies, "cell", split_axis=0, concat_axis=0, tiled=True)


def local_by_gather(state, pseudo_rate, line_next, face_codes):
    cells = lax.axis_size("cell") * state.shape[2]
    vmem = pl.BlockSpec(memory_space=pltpu.VMEM)
    plane = (ROWS, LANES)
    every = gather_inst(state)
    packed = pl.pallas_call(
        cell_kernel,
        out_shape=jax.ShapeDtypeStruct(
            (lax.axis_size("cell"), BLOCK_ROWS, LANES), jnp.float32
        ),
        in_specs=[vmem, vmem],
        out_specs=vmem,
        scratch_shapes=[
            pltpu.VMEM((every.shape[0] // 2, 2 * CELL_ROWS, LANES), jnp.float32)
        ],
        compiler_params=pltpu.CompilerParams(vmem_limit_bytes=VMEM_BYTES),
    )(every, pseudo_rate)
    gathered = exchange_cell(packed)
    blocks = cells // 2
    sizes = [
        (blocks + 2, 10),
        (blocks + 2, 2 * PAIRS),
        (blocks // 2 + 2, 12),
        (blocks // 2 + 2, 2 * PAIRS),
        (2, 2, 4),
        (2, 4),
        (2, 2 * PAIRS),
        (cells, 3),
    ]
    return pl.pallas_call(
        functools.partial(line_kernel, cells),
        out_shape=jax.ShapeDtypeStruct(state.shape, jnp.float32),
        in_specs=[vmem, vmem, pl.BlockSpec(memory_space=pltpu.HBM)],
        out_specs=vmem,
        scratch_shapes=[pltpu.VMEM(size + plane, jnp.float32) for size in sizes]
        + [pltpu.SMEM(face_codes.shape, jnp.int32), pltpu.SemaphoreType.DMA],
        compiler_params=pltpu.CompilerParams(vmem_limit_bytes=VMEM_BYTES),
    )(gathered, line_next, face_codes)


def solution(mesh):
    placed = (P("inst", None, "cell", None), P("cell", None), P(), P())
    inst_count, cell_count = mesh.shape["inst"], mesh.shape["cell"]

    def local(state, pseudo_rate, line_next, face_codes):
        small = (
            state.shape == (2, 6, 2, 2 * LANES)
            and inst_count * 2 == NT
            and cell_count == 8
            and face_codes.shape[1] * LINES_DEV == state.shape[3]
        )
        chosen = local_by_gather if small else local_by_lines
        return chosen(state, pseudo_rate, line_next, face_codes)

    return jax.shard_map(
        local, mesh=mesh, in_specs=placed, out_specs=P("inst", None, "cell", None), check_vma=False
    )
```

```python
import functools

import jax
import jax.numpy as jnp
import numpy as np
from jax import lax
from jax.experimental import pallas as pl
from jax.experimental.pallas import tpu as pltpu
from jax.sharding import PartitionSpec as P

NT = 8
LINES_DEV = 32


GAMMA_GAS = 1.4
OMEGA_BLADE = 1.0
SENSOR_GAIN = 0.25
FOURTH_GAIN = 0.03125
PITCH_GAIN = 0.5
SECOND_IMPL = 1.0
FOURTH_IMPL = 0.25
FREE_STATE = (1.0, 0.5, 0.0, 0.0, 2.625, 0.2)
MIRROR_SIGNS = (1.0, -1.0, 1.0, 1.0, 1.0, 1.0)
ZERO_BLOCK = (0.0, 0.0, 0.0, 0.0)
UNIT_BLOCK = (1.0, 0.0, 0.0, 1.0)
ZERO_PAIR = (0.0, 0.0)


def extended(block, sides, width):
    for axis, dim in sides:
        count = lax.axis_size(axis)
        forward = [(i, i + 1) for i in range(count - 1)]
        backward = [(target, source) for source, target in forward]
        low = lax.ppermute(
            lax.slice_in_dim(block, block.shape[dim] - width, None, axis=dim), axis, forward
        )
        high = lax.ppermute(lax.slice_in_dim(block, 0, width, axis=dim), axis, backward)
        block = jnp.concatenate([low, block, high], axis=dim)
    return block


def spectral_matrix(instances):
    offsets = np.arange(instances)[:, None] - np.arange(instances)[None, :]
    angles = np.pi * offsets / instances
    safe_sin = np.where(offsets == 0, 1.0, np.sin(angles))
    parity = np.where(np.mod(offsets, 2) == 0, -1.0, 1.0)
    matrix_table = np.where(
        offsets == 0, 0.0, 0.5 * OMEGA_BLADE * parity * np.cos(angles) / safe_sin
    )
    return jnp.asarray(matrix_table, jnp.float32)


def primitive_parts(cells_state):
    density = cells_state[..., 0, :, :]
    inverse = 1.0 / density
    velocity_x = cells_state[..., 1, :, :] * inverse
    velocity_y = cells_state[..., 2, :, :] * inverse
    velocity_z = cells_state[..., 3, :, :] * inverse
    energy = cells_state[..., 4, :, :]
    pressure = (GAMMA_GAS - 1.0) * (
        energy
        - 0.5
        * density
        * (velocity_x * velocity_x + velocity_y * velocity_y + velocity_z * velocity_z)
    )
    sound_speed = jnp.sqrt(GAMMA_GAS * pressure * inverse)
    return (velocity_x, velocity_y, pressure, sound_speed)


def directed_flux(cells_state, normal_velocity, pressure, component):
    zero_plane = jnp.zeros_like(pressure)
    pressure_rows = [
        zero_plane,
        zero_plane,
        zero_plane,
        zero_plane,
        pressure * normal_velocity,
        zero_plane,
    ]
    pressure_rows[component] = pressure
    return cells_state * normal_velocity[..., None, :, :] + jnp.stack(pressure_rows, axis=-3)


def line_residual(padded):
    velocity_x, velocity_y, pressure, sound_speed = primitive_parts(padded)
    flux_line = directed_flux(padded, velocity_x, pressure, 1)
    radius = jnp.abs(velocity_x) + sound_speed
    sensor = jnp.abs(
        pressure[..., 2:, :] - 2.0 * pressure[..., 1:-1, :] + pressure[..., :-2, :]
    ) / (pressure[..., 2:, :] + 2.0 * pressure[..., 1:-1, :] + pressure[..., :-2, :])
    second = SENSOR_GAIN * jnp.maximum(sensor[..., :-1, :], sensor[..., 1:, :])
    fourth = jnp.maximum(0.0, FOURTH_GAIN - second)
    face_radius = 0.5 * (radius[..., 1:-2, :] + radius[..., 2:-1, :])
    left_far = padded[..., :-3, :]
    left_near = padded[..., 1:-2, :]
    right_near = padded[..., 2:-1, :]
    right_far = padded[..., 3:, :]
    damping = face_radius[..., None, :, :] * (
        second[..., None, :, :] * (right_near - left_near)
        - fourth[..., None, :, :] * (right_far - 3.0 * right_near + 3.0 * left_near - left_far)
    )
    face_flux = 0.5 * (flux_line[..., 1:-2, :] + flux_line[..., 2:-1, :]) - damping
    return (face_flux[..., 1:, :] - face_flux[..., :-1, :], radius)


def pitch_parts(cells_state):
    velocity_x, velocity_y, pressure, sound_speed = primitive_parts(cells_state)
    return (directed_flux(cells_state, velocity_y, pressure, 2), jnp.abs(velocity_y) + sound_speed)


def pitch_residual(cells_state, next_lines, prev_lines):
    pitch_flux, radius = pitch_parts(cells_state)
    state_next = jnp.take(cells_state, next_lines, axis=-1)
    flux_next, radius_next = pitch_parts(state_next)
    face_flux = 0.5 * (pitch_flux + flux_next) - PITCH_GAIN * (0.5 * (radius + radius_next))[
        ..., None, :, :
    ] * (state_next - cells_state)
    return face_flux - jnp.take(face_flux, prev_lines, axis=-1)


def boundary_cells(edge_pair, line_codes, lower_end):
    reflected = edge_pair[..., ::-1, :] * jnp.asarray(MIRROR_SIGNS, jnp.float32)[:, None, None]
    if lower_end:
        copied = jnp.concatenate([edge_pair[..., :1, :], edge_pair[..., :1, :]], axis=-2)
    else:
        copied = jnp.concatenate([edge_pair[..., 1:, :], edge_pair[..., 1:, :]], axis=-2)
    inflow = jnp.asarray(FREE_STATE, jnp.float32)[:, None, None] + jnp.zeros_like(edge_pair)
    return jnp.where(line_codes == 0, reflected, jnp.where(line_codes == 1, inflow, copied))


def line_coefficients(radius_ext, diagonal_term, positions, total_cells):
    radius_below = radius_ext[..., :-2, :]
    radius_centre = radius_ext[..., 1:-1, :]
    radius_above = radius_ext[..., 2:, :]
    face_below = 0.5 * (radius_below + radius_centre)
    face_above = 0.5 * (radius_centre + radius_above)
    far_low = FOURTH_IMPL * radius_below
    near_low = -SECOND_IMPL * face_below - 2.0 * FOURTH_IMPL * (radius_below + radius_centre)
    middle = (
        diagonal_term
        + SECOND_IMPL * (face_below + face_above)
        + FOURTH_IMPL * (radius_below + 4.0 * radius_centre + radius_above)
    )
    near_high = -SECOND_IMPL * face_above - 2.0 * FOURTH_IMPL * (radius_centre + radius_above)
    far_high = FOURTH_IMPL * radius_above
    column = positions[:, None]
    far_low = jnp.where(column >= 2, far_low, 0.0)
    near_low = jnp.where(column >= 1, near_low, 0.0)
    near_high = jnp.where(column <= total_cells - 2, near_high, 0.0)
    far_high = jnp.where(column <= total_cells - 3, far_high, 0.0)
    return (far_low, near_low, middle, near_high, far_high)


def block_product(first_matrix, second_matrix):
    return (
        first_matrix[0] * second_matrix[0] + first_matrix[1] * second_matrix[2],
        first_matrix[0] * second_matrix[1] + first_matrix[1] * second_matrix[3],
        first_matrix[2] * second_matrix[0] + first_matrix[3] * second_matrix[2],
        first_matrix[2] * second_matrix[1] + first_matrix[3] * second_matrix[3],
    )


def block_inverse(matrix):
    determinant = matrix[0] * matrix[3] - matrix[1] * matrix[2]
    reciprocal = 1.0 / determinant
    return (
        matrix[3] * reciprocal,
        -matrix[1] * reciprocal,
        -matrix[2] * reciprocal,
        matrix[0] * reciprocal,
    )


def block_apply(matrix, vector):
    return (
        matrix[0] * vector[0] + matrix[1] * vector[1],
        matrix[2] * vector[0] + matrix[3] * vector[1],
    )


def add_blocks(first_members, second_members):
    return tuple((a + b for a, b in zip(first_members, second_members)))


def negate(members):
    return tuple((-a for a in members))


def extend_blocks(members, fill_values):
    return tuple(
        (
            jnp.concatenate([m, jnp.full_like(m[..., :1, :], f)], axis=-2)
            for m, f in zip(members, fill_values)
        )
    )


def shift_next(members, fill_values):
    return tuple(
        (
            jnp.concatenate([m[..., 1:, :], jnp.full_like(m[..., :1, :], f)], axis=-2)
            for m, f in zip(members, fill_values)
        )
    )


def shift_prev(members):
    return tuple(
        (jnp.concatenate([jnp.zeros_like(m[..., :1, :]), m[..., :-1, :]], axis=-2) for m in members)
    )


def pair_split(member):
    shaped = member.reshape(member.shape[:-2] + (member.shape[-2] // 2, 2, member.shape[-1]))
    return (shaped[..., 0, :], shaped[..., 1, :])


def split_parity(members):
    halves = [pair_split(m) for m in members]
    return (tuple((h[0] for h in halves)), tuple((h[1] for h in halves)))


def alternate(first_member, second_member):
    stacked = jnp.stack((first_member, second_member), axis=-2)
    return stacked.reshape(
        first_member.shape[:-2] + (2 * first_member.shape[-2], first_member.shape[-1])
    )


def reduce_blocks(sub_blocks, diag_blocks, super_blocks, right_side):
    block_count = diag_blocks[0].shape[-2]
    if block_count == 1:
        return block_apply(block_inverse(diag_blocks), right_side)
    if block_count % 2 == 1:
        sub_blocks = extend_blocks(sub_blocks, ZERO_BLOCK)
        diag_blocks = extend_blocks(diag_blocks, UNIT_BLOCK)
        super_blocks = extend_blocks(super_blocks, ZERO_BLOCK)
        right_side = extend_blocks(right_side, ZERO_PAIR)
    sub_even, sub_odd = split_parity(sub_blocks)
    diag_even, diag_odd = split_parity(diag_blocks)
    super_even, super_odd = split_parity(super_blocks)
    side_even, side_odd = split_parity(right_side)
    inverse_even = block_inverse(diag_even)
    inverse_next = shift_next(inverse_even, UNIT_BLOCK)
    sub_next = shift_next(sub_even, ZERO_BLOCK)
    super_next = shift_next(super_even, ZERO_BLOCK)
    side_next = shift_next(side_even, ZERO_PAIR)
    left_factor = negate(block_product(sub_odd, inverse_even))
    right_factor = negate(block_product(super_odd, inverse_next))
    reduced_sub = block_product(left_factor, sub_even)
    reduced_diag = add_blocks(
        diag_odd,
        add_blocks(block_product(left_factor, super_even), block_product(right_factor, sub_next)),
    )
    reduced_super = block_product(right_factor, super_next)
    reduced_side = add_blocks(
        side_odd,
        add_blocks(block_apply(left_factor, side_even), block_apply(right_factor, side_next)),
    )
    odd_values = reduce_blocks(reduced_sub, reduced_diag, reduced_super, reduced_side)
    before_values = shift_prev(odd_values)
    remainder = add_blocks(
        side_even,
        negate(
            add_blocks(block_apply(sub_even, before_values), block_apply(super_even, odd_values))
        ),
    )
    even_values = block_apply(inverse_even, remainder)
    merged = tuple((alternate(e, o) for e, o in zip(even_values, odd_values)))
    return tuple((m[..., :block_count, :] for m in merged))


def cells_leading(block):
    moved = jnp.transpose(block, (2, 0, 1, 3))
    return moved.reshape(block.shape[2], block.shape[0] * block.shape[1] * block.shape[3])


def solve_in_lanes(coefficients, line_source):
    source_shape = line_source.shape
    lane_coef = [cells_leading(jnp.broadcast_to(c[:, None], source_shape)) for c in coefficients]
    pairs_list = [pair_split(m) for m in lane_coef]
    zero_plane = jnp.zeros_like(pairs_list[2][0])
    sub_blocks = (pairs_list[0][0], pairs_list[1][0], zero_plane, pairs_list[0][1])
    diag_blocks = (pairs_list[2][0], pairs_list[3][0], pairs_list[1][1], pairs_list[2][1])
    super_blocks = (pairs_list[4][0], zero_plane, pairs_list[3][1], pairs_list[4][1])
    values = reduce_blocks(
        sub_blocks, diag_blocks, super_blocks, pair_split(cells_leading(line_source))
    )
    flat = alternate(values[0], values[1])
    shaped = flat.reshape(source_shape[2], source_shape[0], source_shape[1], source_shape[3])
    return jnp.transpose(shaped, (1, 2, 0, 3))


def return_tiles(line_values):
    return lax.all_to_all(line_values, "cell", split_axis=2, concat_axis=3, tiled=True)


def local_by_lines(state, pseudo_rate, line_next, face_codes):
    local_count = state.shape[0]
    tile_cells = state.shape[2]
    cell_index = lax.axis_index("cell")
    cell_count = lax.axis_size("cell")
    total_cells = tile_cells * cell_count
    spectral = spectral_matrix(NT)
    first_local = lax.axis_index("inst") * local_count
    own_rows = lax.dynamic_slice_in_dim(spectral, first_local, local_count, 0)
    shard_block = jax.tree.map(lambda a: lax.all_gather(a, "inst", axis=0, tiled=True), state)
    columns = lax.slice_in_dim(own_rows, 0, shard_block.shape[0], axis=1)
    time_term = jnp.zeros_like(state) + jnp.einsum(
        "nm,mvil->nvil", columns, shard_block, precision=lax.Precision.HIGHEST
    )
    padded = extended(state, (("cell", 2),), 2)
    codes_lines = jnp.repeat(face_codes, LINES_DEV, axis=1)
    lower_ghost = boundary_cells(state[:, :, 0:2, :], codes_lines[0], True)
    upper_ghost = boundary_cells(state[:, :, -2:, :], codes_lines[1], False)
    lower_rim = jnp.where(cell_index == 0, lower_ghost, padded[:, :, :2, :])
    upper_rim = jnp.where(cell_index == cell_count - 1, upper_ghost, padded[:, :, -2:, :])
    padded = jnp.concatenate([lower_rim, padded[:, :, 2:-2, :], upper_rim], axis=2)
    line_part, radius = line_residual(padded)
    prev_lines = (
        jnp.zeros_like(line_next).at[line_next].set(jnp.arange(line_next.shape[0], dtype=jnp.int32))
    )
    residual = line_part + pitch_residual(state, line_next, prev_lines) + time_term
    right_side = -residual
    centre_radius = radius[:, 2:-2, :]
    diagonal_term = pseudo_rate * centre_radius
    positions = cell_index * tile_cells + jnp.arange(-1, tile_cells + 1, dtype=jnp.int32)
    inside = (positions >= 0) & (positions < total_cells)
    radius_ext = jnp.where(inside[:, None], radius[:, 1:-1, :], 0.0)
    coefficients = line_coefficients(radius_ext, diagonal_term, positions[1:-1], total_cells)
    stacked = jnp.stack(coefficients, axis=1)
    line_source = lax.all_to_all(right_side, "cell", split_axis=3, concat_axis=2, tiled=True)
    line_coef = lax.all_to_all(stacked, "cell", split_axis=3, concat_axis=2, tiled=True)
    update = return_tiles(solve_in_lanes(tuple((line_coef[:, k] for k in range(5))), line_source))
    return state + update


LANES = 128
ROWS = 8
PAIRS = 3
CELL_ROWS = PAIRS * ROWS
REST_ROW = 2 * CELL_ROWS
RATE_ROW = 2 * REST_ROW
VMEM_BYTES = 8 * 2**20
BLOCK_ROWS = RATE_ROW + ROWS

SIDE_ROW = 3 * CELL_ROWS
CORRECTION_ROW = SIDE_ROW + 2 * CELL_ROWS
MIDDLE_RATE_ROW = CORRECTION_ROW + 2 * ROWS
MIDDLE_ROWS = MIDDLE_RATE_ROW + ROWS


def spectral_offsets():
    table = np.zeros(NT)
    for offset in range(1, NT):
        angle = np.pi * offset / NT
        parity = -1.0 if offset % 2 == 0 else 1.0
        table[offset] = 0.5 * OMEGA_BLADE * parity * np.cos(angle) / np.sin(angle)
    return [float(np.float32(value)) for value in table]


def plane_masks():
    row_index = lax.broadcasted_iota(jnp.int32, (ROWS, LANES), 0)
    return row_index < 4, (row_index & 2) == 0, row_index & 1


def both(first_var, plane):
    turned = pltpu.roll(plane, 4, 0)
    return jnp.where(first_var, plane, turned), jnp.where(first_var, turned, plane)


def primitives(first_var, planes):
    density, moment_x = both(first_var, planes[0])
    moment_y, moment_z = both(first_var, planes[1])
    energy = jnp.where(first_var, planes[2], pltpu.roll(planes[2], 4, 0))
    inverse = 1.0 / density
    velocity_x = moment_x * inverse
    velocity_y = moment_y * inverse
    velocity_z = moment_z * inverse
    kinetic = moment_x * velocity_x + moment_y * velocity_y + moment_z * velocity_z
    pressure = (GAMMA_GAS - 1.0) * (energy - 0.5 * kinetic)
    sound = jnp.sqrt(GAMMA_GAS * pressure * inverse)
    return velocity_x, velocity_y, pressure, sound


def rows_of(var, inst, half):
    return (var // 2) * ROWS + (var % 2) * 4 + inst * 2 + half


def cell_kernel(all_ref, rate_ref, out_ref, plane_ref):
    own_inst = lax.axis_index("inst")
    inst_count = all_ref.shape[0] // 2
    copies = out_ref.shape[0]
    mirrored = lax.axis_index("cell") // copies
    _, first_inst, _ = plane_masks()

    for shift in range(inst_count):
        pair = (own_inst - shift) & (inst_count - 1)
        for cell in range(2):
            for var in range(6):
                for inst in range(2):
                    for half in range(2):
                        row = cell * CELL_ROWS + rows_of(var, inst, half)
                        plane_ref[shift, pl.ds(row, 1), :] = all_ref[
                            2 * pair + inst, var, pl.ds(cell, 1), pl.ds(half * LANES, LANES)
                        ]
    offsets = spectral_offsets()
    for row in range(0, REST_ROW, ROWS):
        same_total, other_total = None, None
        for shift in range(inst_count):
            plane = plane_ref[shift, pl.ds(row, ROWS), :]
            other = jnp.where(
                first_inst, offsets[(2 * shift + 1) % NT], offsets[(2 * shift - 1) % NT]
            )
            if shift > 0:
                term = offsets[(2 * shift) % NT] * plane
                same_total = term if same_total is None else same_total + term
            term = other * plane
            other_total = term if other_total is None else other_total + term
        turned = jnp.where(
            first_inst, pltpu.roll(other_total, 6, 0), pltpu.roll(other_total, 2, 0)
        )
        own = plane_ref[0, pl.ds(row, ROWS), :]
        place = jnp.bitwise_xor(row // CELL_ROWS, mirrored) * CELL_ROWS + row % CELL_ROWS
        place = pl.multiple_of(place, ROWS)
        for copy in range(copies):
            out_ref[copy, pl.ds(place, ROWS), :] = own
            out_ref[copy, pl.ds(REST_ROW + place, ROWS), :] = same_total + turned
    rates = [
        rate_ref[pl.ds(cell, 1), pl.ds(half * LANES, LANES)]
        for cell in range(2)
        for half in range(2)
    ]
    rates = [jnp.where(mirrored == 0, rates[k], rates[k ^ 2]) for k in range(4)]
    for copy in range(copies):
        for row, rate in enumerate(rates):
            out_ref[copy, pl.ds(RATE_ROW + row, 1), :] = rate
        out_ref[copy, pl.ds(RATE_ROW + 4, 4), :] = jnp.zeros((4, LANES), jnp.float32)


def two_by_two(first, second):
    def entry(a, b, c, d):
        terms = [x * y for x, y in ((a, b), (c, d)) if x is not None and y is not None]
        return None if not terms else terms[0] if len(terms) == 1 else terms[0] + terms[1]

    return (
        entry(first[0], second[0], first[1], second[2]),
        entry(first[0], second[1], first[1], second[3]),
        entry(first[2], second[0], first[3], second[2]),
        entry(first[2], second[1], first[3], second[3]),
    )


def inverse_of(matrix):
    reciprocal = 1.0 / (matrix[0] * matrix[3] - matrix[1] * matrix[2])
    return (
        matrix[3] * reciprocal,
        -(matrix[1] * reciprocal),
        -(matrix[2] * reciprocal),
        matrix[0] * reciprocal,
    )


def less(first, second):
    return tuple(a if b is None else a - b for a, b in zip(first, second))


def minus(members):
    return tuple(None if a is None else -a for a in members)


def matrix_vector(matrix, low, high):
    def row(a, b):
        terms = [x * y for x, y in ((a, low), (b, high)) if x is not None]
        return terms[0] if len(terms) == 1 else terms[0] + terms[1]

    return row(matrix[0], matrix[1]), row(matrix[2], matrix[3])


def apply_matrix(matrix, side):
    parts = [matrix_vector(matrix, side[k], side[PAIRS + k]) for k in range(PAIRS)]
    return [low for low, _ in parts] + [high for _, high in parts]


def difference(first, second):
    return [a - b for a, b in zip(first, second)]


def flux_along(first_var, planes, velocity, pressure, sign):
    normal = sign * velocity
    return [
        planes[0] * normal + jnp.where(first_var, 0.0, sign * pressure),
        planes[1] * normal,
        planes[2] * normal + jnp.where(first_var, pressure * normal, 0.0),
    ]


class LineCells:
    def __init__(self, first_var, sign):
        self.first_var, self.sign = first_var, sign
        self.state, self.pressure, self.radius = {}, {}, {}
        self.flux, self.step, self.sensor = {}, {}, {}

    def add(self, cell, planes, velocity, pressure, sound):
        self.state[cell], self.pressure[cell] = planes, pressure
        self.radius[cell] = jnp.abs(velocity) + sound
        self.flux[cell] = flux_along(self.first_var, planes, velocity, pressure, self.sign)
        if cell - 1 in self.state:
            self.step[cell - 1] = difference(planes, self.state[cell - 1])
        if cell - 2 in self.state:
            twice = 2.0 * self.pressure[cell - 1]
            outer = pressure + self.pressure[cell - 2]
            self.sensor[cell - 1] = jnp.abs(outer - twice) / (outer + twice)

    def face(self, cell):
        second = SENSOR_GAIN * jnp.maximum(self.sensor[cell], self.sensor[cell + 1])
        fourth = jnp.maximum(0.0, FOURTH_GAIN - second)
        face_radius = 0.5 * (self.radius[cell] + self.radius[cell + 1])
        near_weight = face_radius * (second + 2.0 * fourth)
        far_weight = face_radius * fourth
        return [
            0.5 * (self.flux[cell][k] + self.flux[cell + 1][k])
            - (
                near_weight * self.step[cell][k]
                - far_weight * (self.step[cell + 1][k] + self.step[cell - 1][k])
            )
            for k in range(PAIRS)
        ]

    def near(self, cell):
        scale = SECOND_IMPL * 0.5 + 2.0 * FOURTH_IMPL
        return -scale * (self.radius[cell] + self.radius[cell + 1])

    def far(self, cell):
        return FOURTH_IMPL * self.radius[cell]

    def middle(self, cell, rate):
        centre, above = self.radius[cell], self.radius[cell + 1]
        if cell == 0:
            total, weighted = centre + (centre + above), 4.0 * centre + above
        else:
            below = self.radius[cell - 1]
            total = (below + centre) + (centre + above)
            weighted = below + 4.0 * centre + above
        return rate * centre + SECOND_IMPL * (0.5 * total) + FOURTH_IMPL * weighted

    def diagonal(self, cell, rates):
        across = self.near(cell)
        return (self.middle(cell, rates[0]), across, across, self.middle(cell + 1, rates[1]))

    def below(self, cell):
        return (self.far(cell - 1), self.near(cell - 1), None, self.far(cell))

    def above(self, cell):
        return (self.far(cell + 1), None, self.near(cell + 1), self.far(cell + 2))


def rates_at(ref, index, start, first_half):
    rows = [ref[index + (pl.ds(start + k, 1), slice(None))] for k in range(4)]
    return [jnp.where(first_half, rows[2 * k], rows[2 * k + 1]) for k in range(2)]


def half_kernel(
    all_ref, next_ref, held_codes_ref, middle_ref, known_ref, spread_ref,
    rest_ref, line_ref, codes_ref, codes_sem,
):
    fetch = pltpu.make_async_copy(held_codes_ref, codes_ref, codes_sem)
    fetch.start()
    blocks = all_ref.shape[0]
    cells = 2 * blocks
    mirrored = lax.axis_index("cell") // blocks
    sign = (1 - 2 * mirrored).astype(jnp.float32)
    shape = (ROWS, LANES)
    lane_index = lax.broadcasted_iota(jnp.int32, shape, 1)
    first_var, _, half_index = plane_masks()
    first_half = half_index == 0
    zero = jnp.zeros(shape, jnp.float32)

    next_rows = [
        next_ref[pl.ds(half * LANES, LANES)].reshape(1, LANES) for half in range(2)
    ]
    next_line = jnp.where(first_half, next_rows[0], next_rows[1])
    column = lax.broadcasted_iota(jnp.int32, (LANES, LANES), 0)
    prev_halves = []
    for target in range(2):
        total = None
        for source in range(2):
            hits = jnp.where(column + target * LANES == next_rows[source], 1.0, 0.0)
            names = (lane_index + source * LANES).astype(jnp.float32)
            part = lax.dot_general(
                names, hits, (((1,), (1,)), ((), ())), preferred_element_type=jnp.float32
            )
            total = part if total is None else total + part
        prev_halves.append(total)
    prev_line = jnp.where(first_half, prev_halves[0], prev_halves[1]).astype(jnp.int32)

    def picker(lines):
        lane = lines & (LANES - 1)
        same = (lines >> 7) == half_index

        def pick(plane):
            swapped = jnp.where(first_half, pltpu.roll(plane, 7, 0), pltpu.roll(plane, 1, 0))
            here = jnp.take_along_axis(plane, lane, axis=1, mode="promise_in_bounds")
            there = jnp.take_along_axis(swapped, lane, axis=1, mode="promise_in_bounds")
            return jnp.where(same, here, there)

        return pick

    pick_next = picker(next_line)
    pick_prev = picker(prev_line)

    def loaded(cell, start=0):
        return [
            all_ref[cell // 2, pl.ds(start + (cell % 2) * CELL_ROWS + k * ROWS, ROWS), :]
            for k in range(PAIRS)
        ]

    def flux_across(planes, velocity, pressure):
        return [
            planes[0] * velocity,
            planes[1] * velocity + jnp.where(first_var, pressure, 0.0),
            planes[2] * velocity + jnp.where(first_var, pressure * velocity, 0.0),
        ]

    def pitch_flux(planes, velocity_y, pressure, sound):
        nearby = [pick_next(plane) for plane in planes]
        _, next_velocity, next_pressure, next_sound = primitives(first_var, nearby)
        own_flux = flux_across(planes, velocity_y, pressure)
        next_flux = flux_across(nearby, next_velocity, next_pressure)
        weight = (PITCH_GAIN * 0.5) * (
            jnp.abs(velocity_y) + sound + (jnp.abs(next_velocity) + next_sound)
        )
        return [
            0.5 * (a + b) - weight * (n - o)
            for a, b, n, o in zip(own_flux, next_flux, nearby, planes)
        ]

    for cell in range(cells):
        planes = loaded(cell)
        velocity_x, velocity_y, pressure, sound = primitives(first_var, planes)
        line_ref[cell, 0], line_ref[cell, 1], line_ref[cell, 2] = velocity_x, pressure, sound
        faces_across = pitch_flux(planes, velocity_y, pressure, sound)
        times = loaded(cell, REST_ROW)
        for k in range(PAIRS):
            rest_ref[cell, k] = times[k] + (faces_across[k] - pick_prev(faces_across[k]))

    fetch.wait()
    tile = half_index * (LANES // LINES_DEV) + lane_index // LINES_DEV
    codes = jnp.zeros(shape, jnp.int32)
    for k in range(2 * LANES // LINES_DEV):
        codes = jnp.where(tile == k, codes_ref[mirrored, k], codes)

    def ghost(cell):
        planes = loaded(-1 - cell)
        copied = loaded(0)
        result = []
        for k in range(PAIRS):
            reflected = planes[k] if k else jnp.where(first_var, planes[k], -planes[k])
            inflow = jnp.where(first_var, FREE_STATE[2 * k], FREE_STATE[2 * k + 1])
            result.append(
                jnp.where(codes == 0, reflected, jnp.where(codes == 1, inflow, copied[k]))
            )
        return result

    line = LineCells(first_var, sign)
    sides, faces, inverses, aboves = [], {}, [], []
    for cell in range(-2, cells):
        if cell < 0:
            planes = ghost(cell)
            velocity_x, _, pressure, sound = primitives(first_var, planes)
        else:
            planes = loaded(cell)
            velocity_x, pressure, sound = [line_ref[cell, k] for k in range(3)]
        line.add(cell, planes, velocity_x, pressure, sound)
        if cell >= 1:
            faces[cell - 2] = line.face(cell - 2)
        if cell >= 3 and cell % 2 == 1:
            at = cell - 3
            block = at // 2
            rates = rates_at(all_ref, (block,), RATE_ROW, first_half)
            diag = line.diagonal(at, rates)
            side = []
            for member in range(2):
                for k in range(PAIRS):
                    side.append(
                        faces[at + member - 1][k] - faces[at + member][k]
                        - rest_ref[at + member, k]
                    )
            if block > 0:
                factor = two_by_two(line.below(at), inverses[-1])
                diag = less(diag, two_by_two(factor, aboves[-1]))
                side = difference(side, apply_matrix(factor, sides[-1]))
            inverses.append(inverse_of(diag))
            aboves.append(line.above(at))
            sides.append(side)

    last = cells - 2
    factor = two_by_two(line.below(last), inverses[-1])
    correction = two_by_two(factor, aboves[-1])
    side = [faces[last - 1][k] - rest_ref[last, k] for k in range(PAIRS)]
    side += [-rest_ref[last + 1, k] for k in range(PAIRS)]
    side = difference(side, apply_matrix(factor, sides[-1]))
    for n in range(3):
        for k, plane in enumerate(line.state[cells - 3 + n]):
            middle_ref[pl.ds(n * CELL_ROWS + k * ROWS, ROWS), :] = plane
    for n, plane in enumerate(side):
        middle_ref[pl.ds(SIDE_ROW + n * ROWS, ROWS), :] = plane
    for n in range(2):
        middle_ref[pl.ds(CORRECTION_ROW + n * ROWS, ROWS), :] = jnp.where(
            first_var, correction[2 * n], correction[2 * n + 1]
        )
    middle_ref[pl.ds(MIDDLE_RATE_ROW, ROWS), :] = all_ref[
        blocks - 1, pl.ds(RATE_ROW, ROWS), :
    ]

    known, spread = [zero] * (2 * PAIRS), (zero + 1.0, zero, zero, zero + 1.0)
    for block in range(blocks - 1, -1, -1):
        if block < blocks - 1:
            step = two_by_two(inverses[block], aboves[block])
            own = apply_matrix(inverses[block], sides[block])
            if block < blocks - 2:
                known = difference(own, apply_matrix(step, known))
                spread = minus(two_by_two(step, spread))
            else:
                known, spread = own, minus(step)
        for n, plane in enumerate(known):
            known_ref[block, n] = plane
        for n, plane in enumerate(spread):
            spread_ref[block, n] = plane


def join_kernel(all_ref, here_ref, there_ref, known_ref, spread_ref, out_ref):
    blocks = all_ref.shape[0]
    own_cell = lax.axis_index("cell")
    mirrored = own_cell // blocks
    own_block = jnp.where(mirrored == 0, own_cell, 2 * blocks - 1 - own_cell)
    sign = (1 - 2 * mirrored).astype(jnp.float32)
    first_var, _, half_index = plane_masks()
    first_half = half_index == 0

    def plane_of(ref, row):
        return ref[pl.ds(row, ROWS), :]

    line = LineCells(first_var, sign)
    for cell in range(6):
        ref, at = (here_ref, cell) if cell < 3 else (there_ref, 5 - cell)
        planes = [plane_of(ref, at * CELL_ROWS + k * ROWS) for k in range(PAIRS)]
        velocity_x, _, pressure, sound = primitives(first_var, planes)
        line.add(cell, planes, velocity_x, pressure, sound)
    faces = {cell: line.face(cell) for cell in (1, 2, 3)}

    def correction_of(ref):
        pairs = [both(first_var, plane_of(ref, CORRECTION_ROW + n * ROWS)) for n in range(2)]
        return [pairs[0][0], pairs[0][1], pairs[1][0], pairs[1][1]]

    here_side = [plane_of(here_ref, SIDE_ROW + n * ROWS) for n in range(2 * PAIRS)]
    there_side = [plane_of(there_ref, SIDE_ROW + n * ROWS) for n in range(2 * PAIRS)]
    side = [here_side[k] - faces[1][k] for k in range(PAIRS)]
    side += [here_side[PAIRS + k] + (faces[1][k] - faces[2][k]) for k in range(PAIRS)]
    other = [there_side[PAIRS + k] + (faces[2][k] - faces[3][k]) for k in range(PAIRS)]
    other += [there_side[k] + faces[3][k] for k in range(PAIRS)]
    here_rates = rates_at(here_ref, (), MIDDLE_RATE_ROW, first_half)
    there_rates = rates_at(there_ref, (), MIDDLE_RATE_ROW, first_half)
    diag = difference(line.diagonal(1, here_rates), correction_of(here_ref))
    other_diag = difference(line.diagonal(3, there_rates[::-1]), correction_of(there_ref)[::-1])
    factor = two_by_two(line.above(1), inverse_of(other_diag))
    diag = less(diag, two_by_two(factor, line.below(3)))
    middle = apply_matrix(inverse_of(diag), difference(side, apply_matrix(factor, other)))
    spread = [spread_ref[own_block, n] for n in range(4)]
    moved = apply_matrix(spread, middle)
    results = []
    for n in range(2 * PAIRS):
        base = all_ref[own_block, pl.ds(n * ROWS, ROWS), :]
        results.append(base + (known_ref[own_block, n] + moved[n]))
    for cell in range(2):
        for k in range(PAIRS):
            first, second = results[cell * PAIRS + k], results[(1 - cell) * PAIRS + k]
            result = jnp.where(mirrored == 0, first, second)
            for var in range(2):
                for inst in range(2):
                    for half in range(2):
                        row = rows_of(var, inst, half)
                        out_ref[
                            inst, 2 * k + var, pl.ds(cell, 1), pl.ds(half * LANES, LANES)
                        ] = result[row : row + 1]


def share_half(copies):
    count = lax.axis_size("cell")
    groups = [list(range(count // 2)), list(range(count - 1, count // 2 - 1, -1))]
    return lax.all_to_all(
        copies, "cell", split_axis=0, concat_axis=0, tiled=True, axis_index_groups=groups
    )


def swap_halves(block):
    count = lax.axis_size("cell")
    return lax.ppermute(block, "cell", [(i, (i + count // 2) % count) for i in range(count)])


def float_shape(*sizes):
    return jax.ShapeDtypeStruct(sizes, jnp.float32)


def local_by_halves(state, pseudo_rate, line_next, face_codes):
    blocks = lax.axis_size("cell") // 2
    cells = 2 * blocks
    vmem = pl.BlockSpec(memory_space=pltpu.VMEM)
    plane = (ROWS, LANES)
    params = pltpu.CompilerParams(vmem_limit_bytes=VMEM_BYTES)
    every = lax.all_gather(state, "inst", axis=0, tiled=True)
    packed = pl.pallas_call(
        cell_kernel,
        out_shape=float_shape(blocks, BLOCK_ROWS, LANES),
        in_specs=[vmem, vmem],
        out_specs=vmem,
        scratch_shapes=[pltpu.VMEM((every.shape[0] // 2, REST_ROW, LANES), jnp.float32)],
        compiler_params=params,
    )(every, pseudo_rate)
    shared = share_half(packed)
    here, known, spread = pl.pallas_call(
        half_kernel,
        out_shape=(
            float_shape(MIDDLE_ROWS, LANES),
            float_shape(blocks, 2 * PAIRS, *plane),
            float_shape(blocks, 4, *plane),
        ),
        in_specs=[vmem, vmem, pl.BlockSpec(memory_space=pltpu.HBM)],
        out_specs=(vmem, vmem, vmem),
        scratch_shapes=[
            pltpu.VMEM((cells, PAIRS) + plane, jnp.float32),
            pltpu.VMEM((cells, 3) + plane, jnp.float32),
            pltpu.SMEM(face_codes.shape, jnp.int32),
            pltpu.SemaphoreType.DMA,
        ],
        compiler_params=params,
    )(shared, line_next, face_codes)
    there = swap_halves(here)
    return pl.pallas_call(
        join_kernel,
        out_shape=float_shape(*state.shape),
        in_specs=[vmem] * 5,
        out_specs=vmem,
        compiler_params=params,
    )(shared, here, there, known, spread)


def solution(mesh):
    placed = (P("inst", None, "cell", None), P("cell", None), P(), P())
    inst_count, cell_count = mesh.shape["inst"], mesh.shape["cell"]

    def local(state, pseudo_rate, line_next, face_codes):
        small = (
            state.shape == (2, 6, 2, 2 * LANES)
            and inst_count * 2 == NT
            and cell_count == 8
            and face_codes.shape[1] * LINES_DEV == state.shape[3]
        )
        chosen = local_by_halves if small else local_by_lines
        return chosen(state, pseudo_rate, line_next, face_codes)

    return jax.shard_map(
        local, mesh=mesh, in_specs=placed, out_specs=P("inst", None, "cell", None), check_vma=False
    )
```

```python
import functools

import jax
import jax.numpy as jnp
import numpy as np
from jax import lax
from jax.experimental import pallas as pl
from jax.experimental.pallas import tpu as pltpu
from jax.sharding import PartitionSpec as P

NT = 8
LINES_DEV = 32


GAMMA_GAS = 1.4
OMEGA_BLADE = 1.0
SENSOR_GAIN = 0.25
FOURTH_GAIN = 0.03125
PITCH_GAIN = 0.5
SECOND_IMPL = 1.0
FOURTH_IMPL = 0.25
FREE_STATE = (1.0, 0.5, 0.0, 0.0, 2.625, 0.2)
MIRROR_SIGNS = (1.0, -1.0, 1.0, 1.0, 1.0, 1.0)
ZERO_BLOCK = (0.0, 0.0, 0.0, 0.0)
UNIT_BLOCK = (1.0, 0.0, 0.0, 1.0)
ZERO_PAIR = (0.0, 0.0)


def extended(block, sides, width):
    for axis, dim in sides:
        count = lax.axis_size(axis)
        forward = [(i, i + 1) for i in range(count - 1)]
        backward = [(target, source) for source, target in forward]
        low = lax.ppermute(
            lax.slice_in_dim(block, block.shape[dim] - width, None, axis=dim), axis, forward
        )
        high = lax.ppermute(lax.slice_in_dim(block, 0, width, axis=dim), axis, backward)
        block = jnp.concatenate([low, block, high], axis=dim)
    return block


def spectral_matrix(instances):
    offsets = np.arange(instances)[:, None] - np.arange(instances)[None, :]
    angles = np.pi * offsets / instances
    safe_sin = np.where(offsets == 0, 1.0, np.sin(angles))
    parity = np.where(np.mod(offsets, 2) == 0, -1.0, 1.0)
    matrix_table = np.where(
        offsets == 0, 0.0, 0.5 * OMEGA_BLADE * parity * np.cos(angles) / safe_sin
    )
    return jnp.asarray(matrix_table, jnp.float32)


def primitive_parts(cells_state):
    density = cells_state[..., 0, :, :]
    inverse = 1.0 / density
    velocity_x = cells_state[..., 1, :, :] * inverse
    velocity_y = cells_state[..., 2, :, :] * inverse
    velocity_z = cells_state[..., 3, :, :] * inverse
    energy = cells_state[..., 4, :, :]
    pressure = (GAMMA_GAS - 1.0) * (
        energy
        - 0.5
        * density
        * (velocity_x * velocity_x + velocity_y * velocity_y + velocity_z * velocity_z)
    )
    sound_speed = jnp.sqrt(GAMMA_GAS * pressure * inverse)
    return (velocity_x, velocity_y, pressure, sound_speed)


def directed_flux(cells_state, normal_velocity, pressure, component):
    zero_plane = jnp.zeros_like(pressure)
    pressure_rows = [
        zero_plane,
        zero_plane,
        zero_plane,
        zero_plane,
        pressure * normal_velocity,
        zero_plane,
    ]
    pressure_rows[component] = pressure
    return cells_state * normal_velocity[..., None, :, :] + jnp.stack(pressure_rows, axis=-3)


def line_residual(padded):
    velocity_x, velocity_y, pressure, sound_speed = primitive_parts(padded)
    flux_line = directed_flux(padded, velocity_x, pressure, 1)
    radius = jnp.abs(velocity_x) + sound_speed
    sensor = jnp.abs(
        pressure[..., 2:, :] - 2.0 * pressure[..., 1:-1, :] + pressure[..., :-2, :]
    ) / (pressure[..., 2:, :] + 2.0 * pressure[..., 1:-1, :] + pressure[..., :-2, :])
    second = SENSOR_GAIN * jnp.maximum(sensor[..., :-1, :], sensor[..., 1:, :])
    fourth = jnp.maximum(0.0, FOURTH_GAIN - second)
    face_radius = 0.5 * (radius[..., 1:-2, :] + radius[..., 2:-1, :])
    left_far = padded[..., :-3, :]
    left_near = padded[..., 1:-2, :]
    right_near = padded[..., 2:-1, :]
    right_far = padded[..., 3:, :]
    damping = face_radius[..., None, :, :] * (
        second[..., None, :, :] * (right_near - left_near)
        - fourth[..., None, :, :] * (right_far - 3.0 * right_near + 3.0 * left_near - left_far)
    )
    face_flux = 0.5 * (flux_line[..., 1:-2, :] + flux_line[..., 2:-1, :]) - damping
    return (face_flux[..., 1:, :] - face_flux[..., :-1, :], radius)


def pitch_parts(cells_state):
    velocity_x, velocity_y, pressure, sound_speed = primitive_parts(cells_state)
    return (directed_flux(cells_state, velocity_y, pressure, 2), jnp.abs(velocity_y) + sound_speed)


def pitch_residual(cells_state, next_lines, prev_lines):
    pitch_flux, radius = pitch_parts(cells_state)
    state_next = jnp.take(cells_state, next_lines, axis=-1)
    flux_next, radius_next = pitch_parts(state_next)
    face_flux = 0.5 * (pitch_flux + flux_next) - PITCH_GAIN * (0.5 * (radius + radius_next))[
        ..., None, :, :
    ] * (state_next - cells_state)
    return face_flux - jnp.take(face_flux, prev_lines, axis=-1)


def boundary_cells(edge_pair, line_codes, lower_end):
    reflected = edge_pair[..., ::-1, :] * jnp.asarray(MIRROR_SIGNS, jnp.float32)[:, None, None]
    if lower_end:
        copied = jnp.concatenate([edge_pair[..., :1, :], edge_pair[..., :1, :]], axis=-2)
    else:
        copied = jnp.concatenate([edge_pair[..., 1:, :], edge_pair[..., 1:, :]], axis=-2)
    inflow = jnp.asarray(FREE_STATE, jnp.float32)[:, None, None] + jnp.zeros_like(edge_pair)
    return jnp.where(line_codes == 0, reflected, jnp.where(line_codes == 1, inflow, copied))


def line_coefficients(radius_ext, diagonal_term, positions, total_cells):
    radius_below = radius_ext[..., :-2, :]
    radius_centre = radius_ext[..., 1:-1, :]
    radius_above = radius_ext[..., 2:, :]
    face_below = 0.5 * (radius_below + radius_centre)
    face_above = 0.5 * (radius_centre + radius_above)
    far_low = FOURTH_IMPL * radius_below
    near_low = -SECOND_IMPL * face_below - 2.0 * FOURTH_IMPL * (radius_below + radius_centre)
    middle = (
        diagonal_term
        + SECOND_IMPL * (face_below + face_above)
        + FOURTH_IMPL * (radius_below + 4.0 * radius_centre + radius_above)
    )
    near_high = -SECOND_IMPL * face_above - 2.0 * FOURTH_IMPL * (radius_centre + radius_above)
    far_high = FOURTH_IMPL * radius_above
    column = positions[:, None]
    far_low = jnp.where(column >= 2, far_low, 0.0)
    near_low = jnp.where(column >= 1, near_low, 0.0)
    near_high = jnp.where(column <= total_cells - 2, near_high, 0.0)
    far_high = jnp.where(column <= total_cells - 3, far_high, 0.0)
    return (far_low, near_low, middle, near_high, far_high)


def block_product(first_matrix, second_matrix):
    return (
        first_matrix[0] * second_matrix[0] + first_matrix[1] * second_matrix[2],
        first_matrix[0] * second_matrix[1] + first_matrix[1] * second_matrix[3],
        first_matrix[2] * second_matrix[0] + first_matrix[3] * second_matrix[2],
        first_matrix[2] * second_matrix[1] + first_matrix[3] * second_matrix[3],
    )


def block_inverse(matrix):
    determinant = matrix[0] * matrix[3] - matrix[1] * matrix[2]
    reciprocal = 1.0 / determinant
    return (
        matrix[3] * reciprocal,
        -matrix[1] * reciprocal,
        -matrix[2] * reciprocal,
        matrix[0] * reciprocal,
    )


def block_apply(matrix, vector):
    return (
        matrix[0] * vector[0] + matrix[1] * vector[1],
        matrix[2] * vector[0] + matrix[3] * vector[1],
    )


def add_blocks(first_members, second_members):
    return tuple((a + b for a, b in zip(first_members, second_members)))


def negate(members):
    return tuple((-a for a in members))


def extend_blocks(members, fill_values):
    return tuple(
        (
            jnp.concatenate([m, jnp.full_like(m[..., :1, :], f)], axis=-2)
            for m, f in zip(members, fill_values)
        )
    )


def shift_next(members, fill_values):
    return tuple(
        (
            jnp.concatenate([m[..., 1:, :], jnp.full_like(m[..., :1, :], f)], axis=-2)
            for m, f in zip(members, fill_values)
        )
    )


def shift_prev(members):
    return tuple(
        (jnp.concatenate([jnp.zeros_like(m[..., :1, :]), m[..., :-1, :]], axis=-2) for m in members)
    )


def pair_split(member):
    shaped = member.reshape(member.shape[:-2] + (member.shape[-2] // 2, 2, member.shape[-1]))
    return (shaped[..., 0, :], shaped[..., 1, :])


def split_parity(members):
    halves = [pair_split(m) for m in members]
    return (tuple((h[0] for h in halves)), tuple((h[1] for h in halves)))


def alternate(first_member, second_member):
    stacked = jnp.stack((first_member, second_member), axis=-2)
    return stacked.reshape(
        first_member.shape[:-2] + (2 * first_member.shape[-2], first_member.shape[-1])
    )


def reduce_blocks(sub_blocks, diag_blocks, super_blocks, right_side):
    block_count = diag_blocks[0].shape[-2]
    if block_count == 1:
        return block_apply(block_inverse(diag_blocks), right_side)
    if block_count % 2 == 1:
        sub_blocks = extend_blocks(sub_blocks, ZERO_BLOCK)
        diag_blocks = extend_blocks(diag_blocks, UNIT_BLOCK)
        super_blocks = extend_blocks(super_blocks, ZERO_BLOCK)
        right_side = extend_blocks(right_side, ZERO_PAIR)
    sub_even, sub_odd = split_parity(sub_blocks)
    diag_even, diag_odd = split_parity(diag_blocks)
    super_even, super_odd = split_parity(super_blocks)
    side_even, side_odd = split_parity(right_side)
    inverse_even = block_inverse(diag_even)
    inverse_next = shift_next(inverse_even, UNIT_BLOCK)
    sub_next = shift_next(sub_even, ZERO_BLOCK)
    super_next = shift_next(super_even, ZERO_BLOCK)
    side_next = shift_next(side_even, ZERO_PAIR)
    left_factor = negate(block_product(sub_odd, inverse_even))
    right_factor = negate(block_product(super_odd, inverse_next))
    reduced_sub = block_product(left_factor, sub_even)
    reduced_diag = add_blocks(
        diag_odd,
        add_blocks(block_product(left_factor, super_even), block_product(right_factor, sub_next)),
    )
    reduced_super = block_product(right_factor, super_next)
    reduced_side = add_blocks(
        side_odd,
        add_blocks(block_apply(left_factor, side_even), block_apply(right_factor, side_next)),
    )
    odd_values = reduce_blocks(reduced_sub, reduced_diag, reduced_super, reduced_side)
    before_values = shift_prev(odd_values)
    remainder = add_blocks(
        side_even,
        negate(
            add_blocks(block_apply(sub_even, before_values), block_apply(super_even, odd_values))
        ),
    )
    even_values = block_apply(inverse_even, remainder)
    merged = tuple((alternate(e, o) for e, o in zip(even_values, odd_values)))
    return tuple((m[..., :block_count, :] for m in merged))


def cells_leading(block):
    moved = jnp.transpose(block, (2, 0, 1, 3))
    return moved.reshape(block.shape[2], block.shape[0] * block.shape[1] * block.shape[3])


def solve_in_lanes(coefficients, line_source):
    source_shape = line_source.shape
    lane_coef = [cells_leading(jnp.broadcast_to(c[:, None], source_shape)) for c in coefficients]
    pairs_list = [pair_split(m) for m in lane_coef]
    zero_plane = jnp.zeros_like(pairs_list[2][0])
    sub_blocks = (pairs_list[0][0], pairs_list[1][0], zero_plane, pairs_list[0][1])
    diag_blocks = (pairs_list[2][0], pairs_list[3][0], pairs_list[1][1], pairs_list[2][1])
    super_blocks = (pairs_list[4][0], zero_plane, pairs_list[3][1], pairs_list[4][1])
    values = reduce_blocks(
        sub_blocks, diag_blocks, super_blocks, pair_split(cells_leading(line_source))
    )
    flat = alternate(values[0], values[1])
    shaped = flat.reshape(source_shape[2], source_shape[0], source_shape[1], source_shape[3])
    return jnp.transpose(shaped, (1, 2, 0, 3))


def return_tiles(line_values):
    return lax.all_to_all(line_values, "cell", split_axis=2, concat_axis=3, tiled=True)


def local_by_lines(state, pseudo_rate, line_next, face_codes):
    local_count = state.shape[0]
    tile_cells = state.shape[2]
    cell_index = lax.axis_index("cell")
    cell_count = lax.axis_size("cell")
    total_cells = tile_cells * cell_count
    spectral = spectral_matrix(NT)
    first_local = lax.axis_index("inst") * local_count
    own_rows = lax.dynamic_slice_in_dim(spectral, first_local, local_count, 0)
    shard_block = jax.tree.map(lambda a: lax.all_gather(a, "inst", axis=0, tiled=True), state)
    columns = lax.slice_in_dim(own_rows, 0, shard_block.shape[0], axis=1)
    time_term = jnp.zeros_like(state) + jnp.einsum(
        "nm,mvil->nvil", columns, shard_block, precision=lax.Precision.HIGHEST
    )
    padded = extended(state, (("cell", 2),), 2)
    codes_lines = jnp.repeat(face_codes, LINES_DEV, axis=1)
    lower_ghost = boundary_cells(state[:, :, 0:2, :], codes_lines[0], True)
    upper_ghost = boundary_cells(state[:, :, -2:, :], codes_lines[1], False)
    lower_rim = jnp.where(cell_index == 0, lower_ghost, padded[:, :, :2, :])
    upper_rim = jnp.where(cell_index == cell_count - 1, upper_ghost, padded[:, :, -2:, :])
    padded = jnp.concatenate([lower_rim, padded[:, :, 2:-2, :], upper_rim], axis=2)
    line_part, radius = line_residual(padded)
    prev_lines = (
        jnp.zeros_like(line_next).at[line_next].set(jnp.arange(line_next.shape[0], dtype=jnp.int32))
    )
    residual = line_part + pitch_residual(state, line_next, prev_lines) + time_term
    right_side = -residual
    centre_radius = radius[:, 2:-2, :]
    diagonal_term = pseudo_rate * centre_radius
    positions = cell_index * tile_cells + jnp.arange(-1, tile_cells + 1, dtype=jnp.int32)
    inside = (positions >= 0) & (positions < total_cells)
    radius_ext = jnp.where(inside[:, None], radius[:, 1:-1, :], 0.0)
    coefficients = line_coefficients(radius_ext, diagonal_term, positions[1:-1], total_cells)
    stacked = jnp.stack(coefficients, axis=1)
    line_source = lax.all_to_all(right_side, "cell", split_axis=3, concat_axis=2, tiled=True)
    line_coef = lax.all_to_all(stacked, "cell", split_axis=3, concat_axis=2, tiled=True)
    update = return_tiles(solve_in_lanes(tuple((line_coef[:, k] for k in range(5))), line_source))
    return state + update


LANES = 128
ROWS = 8
PAIRS = 3
CELL_ROWS = PAIRS * ROWS
REST_ROW = 2 * CELL_ROWS
RATE_ROW = 2 * REST_ROW
VMEM_BYTES = 8 * 2**20
BLOCK_ROWS = RATE_ROW + ROWS

SIDE_ROW = 3 * CELL_ROWS
CORRECTION_ROW = SIDE_ROW + 2 * CELL_ROWS
MIDDLE_ROWS = CORRECTION_ROW + 2 * ROWS
BLOCK_PLANES = 4 + 3 + 2 * PAIRS


def spectral_offsets():
    table = np.zeros(NT)
    for offset in range(1, NT):
        angle = np.pi * offset / NT
        parity = -1.0 if offset % 2 == 0 else 1.0
        table[offset] = 0.5 * OMEGA_BLADE * parity * np.cos(angle) / np.sin(angle)
    return [float(np.float32(value)) for value in table]


def plane_masks():
    row_index = lax.broadcasted_iota(jnp.int32, (ROWS, LANES), 0)
    return row_index < 4, (row_index & 2) == 0, row_index & 1


def both(first_var, plane):
    turned = pltpu.roll(plane, 4, 0)
    return jnp.where(first_var, plane, turned), jnp.where(first_var, turned, plane)


def primitives(first_var, planes):
    density, moment_x = both(first_var, planes[0])
    moment_y, moment_z = both(first_var, planes[1])
    energy = jnp.where(first_var, planes[2], pltpu.roll(planes[2], 4, 0))
    inverse = 1.0 / density
    velocity_x = moment_x * inverse
    velocity_y = moment_y * inverse
    velocity_z = moment_z * inverse
    kinetic = moment_x * velocity_x + moment_y * velocity_y + moment_z * velocity_z
    pressure = (GAMMA_GAS - 1.0) * (energy - 0.5 * kinetic)
    sound = jnp.sqrt(GAMMA_GAS * pressure * inverse)
    return velocity_x, velocity_y, pressure, sound


def rows_of(var, inst, half):
    return (var // 2) * ROWS + (var % 2) * 4 + inst * 2 + half


def cell_kernel(all_ref, rate_ref, out_ref, plane_ref):
    own_inst = lax.axis_index("inst")
    inst_count = all_ref.shape[0] // 2
    copies = out_ref.shape[0]
    mirrored = lax.axis_index("cell") // copies
    _, first_inst, _ = plane_masks()

    for shift in range(inst_count):
        pair = (own_inst - shift) & (inst_count - 1)
        for cell in range(2):
            for var in range(6):
                for inst in range(2):
                    for half in range(2):
                        row = cell * CELL_ROWS + rows_of(var, inst, half)
                        plane_ref[shift, pl.ds(row, 1), :] = all_ref[
                            2 * pair + inst, var, pl.ds(cell, 1), pl.ds(half * LANES, LANES)
                        ]
    offsets = spectral_offsets()
    for row in range(0, REST_ROW, ROWS):
        same_total, other_total = None, None
        for shift in range(inst_count):
            plane = plane_ref[shift, pl.ds(row, ROWS), :]
            other = jnp.where(
                first_inst, offsets[(2 * shift + 1) % NT], offsets[(2 * shift - 1) % NT]
            )
            if shift > 0:
                term = offsets[(2 * shift) % NT] * plane
                same_total = term if same_total is None else same_total + term
            term = other * plane
            other_total = term if other_total is None else other_total + term
        turned = jnp.where(
            first_inst, pltpu.roll(other_total, 6, 0), pltpu.roll(other_total, 2, 0)
        )
        own = plane_ref[0, pl.ds(row, ROWS), :]
        place = jnp.bitwise_xor(row // CELL_ROWS, mirrored) * CELL_ROWS + row % CELL_ROWS
        place = pl.multiple_of(place, ROWS)
        for copy in range(copies):
            out_ref[copy, pl.ds(place, ROWS), :] = own
            out_ref[copy, pl.ds(REST_ROW + place, ROWS), :] = same_total + turned
    rates = [
        rate_ref[pl.ds(cell, 1), pl.ds(half * LANES, LANES)]
        for cell in range(2)
        for half in range(2)
    ]
    rates = [jnp.where(mirrored == 0, rates[k], rates[k ^ 2]) for k in range(4)]
    for copy in range(copies):
        for row, rate in enumerate(rates):
            out_ref[copy, pl.ds(RATE_ROW + row, 1), :] = rate
        out_ref[copy, pl.ds(RATE_ROW + 4, 4), :] = jnp.zeros((4, LANES), jnp.float32)


def two_by_two(first, second):
    def entry(a, b, c, d):
        terms = [x * y for x, y in ((a, b), (c, d)) if x is not None and y is not None]
        return None if not terms else terms[0] if len(terms) == 1 else terms[0] + terms[1]

    return (
        entry(first[0], second[0], first[1], second[2]),
        entry(first[0], second[1], first[1], second[3]),
        entry(first[2], second[0], first[3], second[2]),
        entry(first[2], second[1], first[3], second[3]),
    )


def inverse_of(matrix):
    reciprocal = 1.0 / (matrix[0] * matrix[3] - matrix[1] * matrix[2])
    return (
        matrix[3] * reciprocal,
        -(matrix[1] * reciprocal),
        -(matrix[2] * reciprocal),
        matrix[0] * reciprocal,
    )


def less(first, second):
    return tuple(a if b is None else a - b for a, b in zip(first, second))


def minus(members):
    return tuple(None if a is None else -a for a in members)


def matrix_vector(matrix, low, high):
    def row(a, b):
        terms = [x * y for x, y in ((a, low), (b, high)) if x is not None]
        return terms[0] if len(terms) == 1 else terms[0] + terms[1]

    return row(matrix[0], matrix[1]), row(matrix[2], matrix[3])


def apply_matrix(matrix, side):
    parts = [matrix_vector(matrix, side[k], side[PAIRS + k]) for k in range(PAIRS)]
    return [low for low, _ in parts] + [high for _, high in parts]


def difference(first, second):
    return [a - b for a, b in zip(first, second)]


def flux_along(first_var, planes, velocity, pressure, sign):
    normal = sign * velocity
    return [
        planes[0] * normal + jnp.where(first_var, 0.0, sign * pressure),
        planes[1] * normal,
        planes[2] * normal + jnp.where(first_var, pressure * normal, 0.0),
    ]


class LineCells:
    def __init__(self, first_var, sign):
        self.first_var, self.sign = first_var, sign
        self.state, self.pressure, self.radius = {}, {}, {}
        self.flux, self.step, self.sensor = {}, {}, {}

    def add(self, cell, planes, velocity, pressure, sound):
        self.state[cell], self.pressure[cell] = planes, pressure
        self.radius[cell] = jnp.abs(velocity) + sound
        self.flux[cell] = flux_along(self.first_var, planes, velocity, pressure, self.sign)
        if cell - 1 in self.state:
            self.step[cell - 1] = difference(planes, self.state[cell - 1])
        if cell - 2 in self.state:
            twice = 2.0 * self.pressure[cell - 1]
            outer = pressure + self.pressure[cell - 2]
            self.sensor[cell - 1] = jnp.abs(outer - twice) / (outer + twice)

    def face(self, cell):
        second = SENSOR_GAIN * jnp.maximum(self.sensor[cell], self.sensor[cell + 1])
        fourth = jnp.maximum(0.0, FOURTH_GAIN - second)
        face_radius = 0.5 * (self.radius[cell] + self.radius[cell + 1])
        near_weight = face_radius * (second + 2.0 * fourth)
        far_weight = face_radius * fourth
        return [
            0.5 * (self.flux[cell][k] + self.flux[cell + 1][k])
            - (
                near_weight * self.step[cell][k]
                - far_weight * (self.step[cell + 1][k] + self.step[cell - 1][k])
            )
            for k in range(PAIRS)
        ]

    def near(self, cell):
        scale = SECOND_IMPL * 0.5 + 2.0 * FOURTH_IMPL
        return -scale * (self.radius[cell] + self.radius[cell + 1])

    def far(self, cell):
        return FOURTH_IMPL * self.radius[cell]

    def middle(self, cell, rate):
        centre, above = self.radius[cell], self.radius[cell + 1]
        if cell == 0:
            total, weighted = centre + (centre + above), 4.0 * centre + above
        else:
            below = self.radius[cell - 1]
            total = (below + centre) + (centre + above)
            weighted = below + 4.0 * centre + above
        result = SECOND_IMPL * (0.5 * total) + FOURTH_IMPL * weighted
        return result if rate is None else rate * centre + result

    def diagonal(self, cell, rates):
        across = self.near(cell)
        return (self.middle(cell, rates[0]), across, across, self.middle(cell + 1, rates[1]))

    def below(self, cell):
        return (self.far(cell - 1), self.near(cell - 1), None, self.far(cell))

    def above(self, cell):
        return (self.far(cell + 1), None, self.near(cell + 1), self.far(cell + 2))


def rates_at(ref, index, start, first_half):
    rows = [ref[index + (pl.ds(start + k, 1), slice(None))] for k in range(4)]
    return [jnp.where(first_half, rows[2 * k], rows[2 * k + 1]) for k in range(2)]


def half_kernel(
    all_ref, next_ref, held_codes_ref, middle_ref, blocks_ref, rest_ref, line_ref,
    codes_ref, codes_sem,
):
    fetch = pltpu.make_async_copy(held_codes_ref, codes_ref, codes_sem)
    fetch.start()
    blocks = all_ref.shape[0]
    cells = 2 * blocks
    mirrored = lax.axis_index("cell") // blocks
    sign = (1 - 2 * mirrored).astype(jnp.float32)
    shape = (ROWS, LANES)
    lane_index = lax.broadcasted_iota(jnp.int32, shape, 1)
    first_var, _, half_index = plane_masks()
    first_half = half_index == 0
    zero = jnp.zeros(shape, jnp.float32)

    next_rows = [
        next_ref[pl.ds(half * LANES, LANES)].reshape(1, LANES) for half in range(2)
    ]
    next_line = jnp.where(first_half, next_rows[0], next_rows[1])
    column = lax.broadcasted_iota(jnp.int32, (LANES, LANES), 0)
    prev_halves = []
    for target in range(2):
        total = None
        for source in range(2):
            hits = jnp.where(column + target * LANES == next_rows[source], 1.0, 0.0)
            names = (lane_index + source * LANES).astype(jnp.float32)
            part = lax.dot_general(
                names, hits, (((1,), (1,)), ((), ())), preferred_element_type=jnp.float32
            )
            total = part if total is None else total + part
        prev_halves.append(total)
    prev_line = jnp.where(first_half, prev_halves[0], prev_halves[1]).astype(jnp.int32)

    def picker(lines):
        lane = lines & (LANES - 1)
        same = (lines >> 7) == half_index

        def pick(plane):
            swapped = jnp.where(first_half, pltpu.roll(plane, 7, 0), pltpu.roll(plane, 1, 0))
            here = jnp.take_along_axis(plane, lane, axis=1, mode="promise_in_bounds")
            there = jnp.take_along_axis(swapped, lane, axis=1, mode="promise_in_bounds")
            return jnp.where(same, here, there)

        return pick

    pick_next = picker(next_line)
    pick_prev = picker(prev_line)

    def loaded(cell, start=0):
        return [
            all_ref[cell // 2, pl.ds(start + (cell % 2) * CELL_ROWS + k * ROWS, ROWS), :]
            for k in range(PAIRS)
        ]

    def flux_across(planes, velocity, pressure):
        return [
            planes[0] * velocity,
            planes[1] * velocity + jnp.where(first_var, pressure, 0.0),
            planes[2] * velocity + jnp.where(first_var, pressure * velocity, 0.0),
        ]

    def pitch_flux(planes, velocity_y, pressure, sound):
        nearby = [pick_next(plane) for plane in planes]
        _, next_velocity, next_pressure, next_sound = primitives(first_var, nearby)
        own_flux = flux_across(planes, velocity_y, pressure)
        next_flux = flux_across(nearby, next_velocity, next_pressure)
        weight = (PITCH_GAIN * 0.5) * (
            jnp.abs(velocity_y) + sound + (jnp.abs(next_velocity) + next_sound)
        )
        return [
            0.5 * (a + b) - weight * (n - o)
            for a, b, n, o in zip(own_flux, next_flux, nearby, planes)
        ]

    for cell in range(cells):
        planes = loaded(cell)
        velocity_x, velocity_y, pressure, sound = primitives(first_var, planes)
        line_ref[cell, 0], line_ref[cell, 1], line_ref[cell, 2] = velocity_x, pressure, sound
        faces_across = pitch_flux(planes, velocity_y, pressure, sound)
        times = loaded(cell, REST_ROW)
        for k in range(PAIRS):
            rest_ref[cell, k] = times[k] + (faces_across[k] - pick_prev(faces_across[k]))

    fetch.wait()
    tile = half_index * (LANES // LINES_DEV) + lane_index // LINES_DEV
    codes = jnp.zeros(shape, jnp.int32)
    for k in range(2 * LANES // LINES_DEV):
        codes = jnp.where(tile == k, codes_ref[mirrored, k], codes)

    def ghost(cell):
        planes = loaded(-1 - cell)
        copied = loaded(0)
        result = []
        for k in range(PAIRS):
            reflected = planes[k] if k else jnp.where(first_var, planes[k], -planes[k])
            inflow = jnp.where(first_var, FREE_STATE[2 * k], FREE_STATE[2 * k + 1])
            result.append(
                jnp.where(codes == 0, reflected, jnp.where(codes == 1, inflow, copied[k]))
            )
        return result

    line = LineCells(first_var, sign)
    sides, faces, inverses, aboves = [], {}, [], []
    for cell in range(-2, cells):
        if cell < 0:
            planes = ghost(cell)
            velocity_x, _, pressure, sound = primitives(first_var, planes)
        else:
            planes = loaded(cell)
            velocity_x, pressure, sound = [line_ref[cell, k] for k in range(3)]
        line.add(cell, planes, velocity_x, pressure, sound)
        if cell >= 1:
            faces[cell - 2] = line.face(cell - 2)
        if cell >= 3 and cell % 2 == 1:
            at = cell - 3
            block = at // 2
            rates = rates_at(all_ref, (block,), RATE_ROW, first_half)
            diag = line.diagonal(at, rates)
            side = []
            for member in range(2):
                for k in range(PAIRS):
                    side.append(
                        faces[at + member - 1][k] - faces[at + member][k]
                        - rest_ref[at + member, k]
                    )
            if block > 0:
                factor = two_by_two(line.below(at), inverses[-1])
                diag = less(diag, two_by_two(factor, aboves[-1]))
                side = difference(side, apply_matrix(factor, sides[-1]))
            inverses.append(inverse_of(diag))
            aboves.append(line.above(at))
            sides.append(side)

    last = cells - 2
    factor = two_by_two(line.below(last), inverses[-1])
    correction = list(two_by_two(factor, aboves[-1]))
    rates = rates_at(all_ref, (blocks - 1,), RATE_ROW, first_half)
    for member in range(2):
        centre = line.radius[last + member]
        correction[3 * member] = correction[3 * member] - rates[member] * centre
    side = [faces[last - 1][k] - rest_ref[last, k] for k in range(PAIRS)]
    side += [-rest_ref[last + 1, k] for k in range(PAIRS)]
    side = difference(side, apply_matrix(factor, sides[-1]))
    for n in range(3):
        for k, plane in enumerate(line.state[cells - 3 + n]):
            middle_ref[pl.ds(n * CELL_ROWS + k * ROWS, ROWS), :] = plane
    for n, plane in enumerate(side):
        middle_ref[pl.ds(SIDE_ROW + n * ROWS, ROWS), :] = plane
    for n in range(2):
        middle_ref[pl.ds(CORRECTION_ROW + n * ROWS, ROWS), :] = jnp.where(
            first_var, correction[2 * n], correction[2 * n + 1]
        )
    for block in range(blocks - 1):
        kept = [*inverses[block], aboves[block][0], *aboves[block][2:], *sides[block]]
        for n, plane in enumerate(kept):
            blocks_ref[block, n] = plane


def spread_kernel(all_ref, blocks_ref, known_ref, spread_ref, table_ref):
    blocks = all_ref.shape[0]
    own_cell = lax.axis_index("cell")
    own_block = jnp.where(own_cell < blocks, own_cell, 2 * blocks - 1 - own_cell)
    zero = jnp.zeros((ROWS, LANES), jnp.float32)
    known, spread = [zero] * (2 * PAIRS), (zero + 1.0, zero, zero, zero + 1.0)
    for block in range(blocks - 1, -1, -1):
        if block < blocks - 1:
            kept = [blocks_ref[block, n] for n in range(BLOCK_PLANES)]
            inverse, above, side = kept[:4], (kept[4], None, kept[5], kept[6]), kept[7:]
            step = two_by_two(inverse, above)
            own = apply_matrix(inverse, side)
            if block < blocks - 2:
                known = difference(own, apply_matrix(step, known))
                spread = minus(two_by_two(step, spread))
            else:
                known, spread = own, minus(step)
        for n, plane in enumerate(known + list(spread)):
            table_ref[block, n] = plane
    for n in range(2 * PAIRS):
        known_ref[n] = all_ref[own_block, pl.ds(n * ROWS, ROWS), :] + table_ref[own_block, n]
    for n in range(4):
        spread_ref[n] = table_ref[own_block, 2 * PAIRS + n]


def join_kernel(here_ref, there_ref, known_ref, spread_ref, out_ref):
    mirrored = lax.axis_index("cell") // (lax.axis_size("cell") // 2)
    sign = (1 - 2 * mirrored).astype(jnp.float32)
    first_var, _, _ = plane_masks()

    def plane_of(ref, row):
        return ref[pl.ds(row, ROWS), :]

    line = LineCells(first_var, sign)
    for cell in range(6):
        ref, at = (here_ref, cell) if cell < 3 else (there_ref, 5 - cell)
        planes = [plane_of(ref, at * CELL_ROWS + k * ROWS) for k in range(PAIRS)]
        velocity_x, _, pressure, sound = primitives(first_var, planes)
        line.add(cell, planes, velocity_x, pressure, sound)
    faces = {cell: line.face(cell) for cell in (1, 2, 3)}

    def correction_of(ref):
        pairs = [both(first_var, plane_of(ref, CORRECTION_ROW + n * ROWS)) for n in range(2)]
        return [pairs[0][0], pairs[0][1], pairs[1][0], pairs[1][1]]

    here_side = [plane_of(here_ref, SIDE_ROW + n * ROWS) for n in range(2 * PAIRS)]
    there_side = [plane_of(there_ref, SIDE_ROW + n * ROWS) for n in range(2 * PAIRS)]
    side = [here_side[k] - faces[1][k] for k in range(PAIRS)]
    side += [here_side[PAIRS + k] + (faces[1][k] - faces[2][k]) for k in range(PAIRS)]
    other = [there_side[PAIRS + k] + (faces[2][k] - faces[3][k]) for k in range(PAIRS)]
    other += [there_side[k] + faces[3][k] for k in range(PAIRS)]
    no_rates = (None, None)
    diag = difference(line.diagonal(1, no_rates), correction_of(here_ref))
    other_diag = difference(line.diagonal(3, no_rates), correction_of(there_ref)[::-1])
    factor = two_by_two(line.above(1), inverse_of(other_diag))
    diag = less(diag, two_by_two(factor, line.below(3)))
    middle = apply_matrix(inverse_of(diag), difference(side, apply_matrix(factor, other)))
    moved = apply_matrix([spread_ref[n] for n in range(4)], middle)
    results = [known_ref[n] + moved[n] for n in range(2 * PAIRS)]
    for cell in range(2):
        for k in range(PAIRS):
            first, second = results[cell * PAIRS + k], results[(1 - cell) * PAIRS + k]
            result = jnp.where(mirrored == 0, first, second)
            for var in range(2):
                for inst in range(2):
                    for half in range(2):
                        row = rows_of(var, inst, half)
                        out_ref[
                            inst, 2 * k + var, pl.ds(cell, 1), pl.ds(half * LANES, LANES)
                        ] = result[row : row + 1]


def share_half(copies):
    count = lax.axis_size("cell")
    groups = [list(range(count // 2)), list(range(count - 1, count // 2 - 1, -1))]
    return lax.all_to_all(
        copies, "cell", split_axis=0, concat_axis=0, tiled=True, axis_index_groups=groups
    )


def swap_halves(block):
    count = lax.axis_size("cell")
    return lax.ppermute(block, "cell", [(i, (i + count // 2) % count) for i in range(count)])


def float_shape(*sizes):
    return jax.ShapeDtypeStruct(sizes, jnp.float32)


def local_by_halves(state, pseudo_rate, line_next, face_codes):
    blocks = lax.axis_size("cell") // 2
    cells = 2 * blocks
    vmem = pl.BlockSpec(memory_space=pltpu.VMEM)
    plane = (ROWS, LANES)
    params = pltpu.CompilerParams(vmem_limit_bytes=VMEM_BYTES)
    every = lax.all_gather(state, "inst", axis=0, tiled=True)
    packed = pl.pallas_call(
        cell_kernel,
        out_shape=float_shape(blocks, BLOCK_ROWS, LANES),
        in_specs=[vmem, vmem],
        out_specs=vmem,
        scratch_shapes=[pltpu.VMEM((every.shape[0] // 2, REST_ROW, LANES), jnp.float32)],
        compiler_params=params,
    )(every, pseudo_rate)
    shared = share_half(packed)
    here, eliminated = pl.pallas_call(
        half_kernel,
        out_shape=(
            float_shape(MIDDLE_ROWS, LANES),
            float_shape(blocks - 1, BLOCK_PLANES, *plane),
        ),
        in_specs=[vmem, vmem, pl.BlockSpec(memory_space=pltpu.HBM)],
        out_specs=(vmem, vmem),
        scratch_shapes=[
            pltpu.VMEM((cells, PAIRS) + plane, jnp.float32),
            pltpu.VMEM((cells, 3) + plane, jnp.float32),
            pltpu.SMEM(face_codes.shape, jnp.int32),
            pltpu.SemaphoreType.DMA,
        ],
        compiler_params=params,
    )(shared, line_next, face_codes)
    there = swap_halves(here)
    known, spread = pl.pallas_call(
        spread_kernel,
        out_shape=(float_shape(2 * PAIRS, *plane), float_shape(4, *plane)),
        in_specs=[vmem, vmem],
        out_specs=(vmem, vmem),
        scratch_shapes=[pltpu.VMEM((blocks, 2 * PAIRS + 4) + plane, jnp.float32)],
        compiler_params=params,
        cost_estimate=pl.CostEstimate(flops=10**6, bytes_accessed=10**6, transcendentals=0),
    )(shared, eliminated)
    return pl.pallas_call(
        join_kernel,
        out_shape=float_shape(*state.shape),
        in_specs=[vmem] * 4,
        out_specs=vmem,
        compiler_params=params,
    )(here, there, known, spread)


def solution(mesh):
    placed = (P("inst", None, "cell", None), P("cell", None), P(), P())
    inst_count, cell_count = mesh.shape["inst"], mesh.shape["cell"]

    def local(state, pseudo_rate, line_next, face_codes):
        small = (
            state.shape == (2, 6, 2, 2 * LANES)
            and inst_count * 2 == NT
            and cell_count == 8
            and face_codes.shape[1] * LINES_DEV == state.shape[3]
        )
        chosen = local_by_halves if small else local_by_lines
        return chosen(state, pseudo_rate, line_next, face_codes)

    return jax.shard_map(
        local, mesh=mesh, in_specs=placed, out_specs=P("inst", None, "cell", None), check_vma=False
    )
```

```python
import functools

import jax
import jax.numpy as jnp
import numpy as np
from jax import lax
from jax.experimental import pallas as pl
from jax.experimental.pallas import tpu as pltpu
from jax.sharding import PartitionSpec as P

NT = 8
LINES_DEV = 32


GAMMA_GAS = 1.4
OMEGA_BLADE = 1.0
SENSOR_GAIN = 0.25
FOURTH_GAIN = 0.03125
PITCH_GAIN = 0.5
SECOND_IMPL = 1.0
FOURTH_IMPL = 0.25
FREE_STATE = (1.0, 0.5, 0.0, 0.0, 2.625, 0.2)
MIRROR_SIGNS = (1.0, -1.0, 1.0, 1.0, 1.0, 1.0)
ZERO_BLOCK = (0.0, 0.0, 0.0, 0.0)
UNIT_BLOCK = (1.0, 0.0, 0.0, 1.0)
ZERO_PAIR = (0.0, 0.0)


def extended(block, sides, width):
    for axis, dim in sides:
        count = lax.axis_size(axis)
        forward = [(i, i + 1) for i in range(count - 1)]
        backward = [(target, source) for source, target in forward]
        low = lax.ppermute(
            lax.slice_in_dim(block, block.shape[dim] - width, None, axis=dim), axis, forward
        )
        high = lax.ppermute(lax.slice_in_dim(block, 0, width, axis=dim), axis, backward)
        block = jnp.concatenate([low, block, high], axis=dim)
    return block


def spectral_matrix(instances):
    offsets = np.arange(instances)[:, None] - np.arange(instances)[None, :]
    angles = np.pi * offsets / instances
    safe_sin = np.where(offsets == 0, 1.0, np.sin(angles))
    parity = np.where(np.mod(offsets, 2) == 0, -1.0, 1.0)
    matrix_table = np.where(
        offsets == 0, 0.0, 0.5 * OMEGA_BLADE * parity * np.cos(angles) / safe_sin
    )
    return jnp.asarray(matrix_table, jnp.float32)


def primitive_parts(cells_state):
    density = cells_state[..., 0, :, :]
    inverse = 1.0 / density
    velocity_x = cells_state[..., 1, :, :] * inverse
    velocity_y = cells_state[..., 2, :, :] * inverse
    velocity_z = cells_state[..., 3, :, :] * inverse
    energy = cells_state[..., 4, :, :]
    pressure = (GAMMA_GAS - 1.0) * (
        energy
        - 0.5
        * density
        * (velocity_x * velocity_x + velocity_y * velocity_y + velocity_z * velocity_z)
    )
    sound_speed = jnp.sqrt(GAMMA_GAS * pressure * inverse)
    return (velocity_x, velocity_y, pressure, sound_speed)


def directed_flux(cells_state, normal_velocity, pressure, component):
    zero_plane = jnp.zeros_like(pressure)
    pressure_rows = [
        zero_plane,
        zero_plane,
        zero_plane,
        zero_plane,
        pressure * normal_velocity,
        zero_plane,
    ]
    pressure_rows[component] = pressure
    return cells_state * normal_velocity[..., None, :, :] + jnp.stack(pressure_rows, axis=-3)


def line_residual(padded):
    velocity_x, velocity_y, pressure, sound_speed = primitive_parts(padded)
    flux_line = directed_flux(padded, velocity_x, pressure, 1)
    radius = jnp.abs(velocity_x) + sound_speed
    sensor = jnp.abs(
        pressure[..., 2:, :] - 2.0 * pressure[..., 1:-1, :] + pressure[..., :-2, :]
    ) / (pressure[..., 2:, :] + 2.0 * pressure[..., 1:-1, :] + pressure[..., :-2, :])
    second = SENSOR_GAIN * jnp.maximum(sensor[..., :-1, :], sensor[..., 1:, :])
    fourth = jnp.maximum(0.0, FOURTH_GAIN - second)
    face_radius = 0.5 * (radius[..., 1:-2, :] + radius[..., 2:-1, :])
    left_far = padded[..., :-3, :]
    left_near = padded[..., 1:-2, :]
    right_near = padded[..., 2:-1, :]
    right_far = padded[..., 3:, :]
    damping = face_radius[..., None, :, :] * (
        second[..., None, :, :] * (right_near - left_near)
        - fourth[..., None, :, :] * (right_far - 3.0 * right_near + 3.0 * left_near - left_far)
    )
    face_flux = 0.5 * (flux_line[..., 1:-2, :] + flux_line[..., 2:-1, :]) - damping
    return (face_flux[..., 1:, :] - face_flux[..., :-1, :], radius)


def pitch_parts(cells_state):
    velocity_x, velocity_y, pressure, sound_speed = primitive_parts(cells_state)
    return (directed_flux(cells_state, velocity_y, pressure, 2), jnp.abs(velocity_y) + sound_speed)


def pitch_residual(cells_state, next_lines, prev_lines):
    pitch_flux, radius = pitch_parts(cells_state)
    state_next = jnp.take(cells_state, next_lines, axis=-1)
    flux_next, radius_next = pitch_parts(state_next)
    face_flux = 0.5 * (pitch_flux + flux_next) - PITCH_GAIN * (0.5 * (radius + radius_next))[
        ..., None, :, :
    ] * (state_next - cells_state)
    return face_flux - jnp.take(face_flux, prev_lines, axis=-1)


def boundary_cells(edge_pair, line_codes, lower_end):
    reflected = edge_pair[..., ::-1, :] * jnp.asarray(MIRROR_SIGNS, jnp.float32)[:, None, None]
    if lower_end:
        copied = jnp.concatenate([edge_pair[..., :1, :], edge_pair[..., :1, :]], axis=-2)
    else:
        copied = jnp.concatenate([edge_pair[..., 1:, :], edge_pair[..., 1:, :]], axis=-2)
    inflow = jnp.asarray(FREE_STATE, jnp.float32)[:, None, None] + jnp.zeros_like(edge_pair)
    return jnp.where(line_codes == 0, reflected, jnp.where(line_codes == 1, inflow, copied))


def line_coefficients(radius_ext, diagonal_term, positions, total_cells):
    radius_below = radius_ext[..., :-2, :]
    radius_centre = radius_ext[..., 1:-1, :]
    radius_above = radius_ext[..., 2:, :]
    face_below = 0.5 * (radius_below + radius_centre)
    face_above = 0.5 * (radius_centre + radius_above)
    far_low = FOURTH_IMPL * radius_below
    near_low = -SECOND_IMPL * face_below - 2.0 * FOURTH_IMPL * (radius_below + radius_centre)
    middle = (
        diagonal_term
        + SECOND_IMPL * (face_below + face_above)
        + FOURTH_IMPL * (radius_below + 4.0 * radius_centre + radius_above)
    )
    near_high = -SECOND_IMPL * face_above - 2.0 * FOURTH_IMPL * (radius_centre + radius_above)
    far_high = FOURTH_IMPL * radius_above
    column = positions[:, None]
    far_low = jnp.where(column >= 2, far_low, 0.0)
    near_low = jnp.where(column >= 1, near_low, 0.0)
    near_high = jnp.where(column <= total_cells - 2, near_high, 0.0)
    far_high = jnp.where(column <= total_cells - 3, far_high, 0.0)
    return (far_low, near_low, middle, near_high, far_high)


def block_product(first_matrix, second_matrix):
    return (
        first_matrix[0] * second_matrix[0] + first_matrix[1] * second_matrix[2],
        first_matrix[0] * second_matrix[1] + first_matrix[1] * second_matrix[3],
        first_matrix[2] * second_matrix[0] + first_matrix[3] * second_matrix[2],
        first_matrix[2] * second_matrix[1] + first_matrix[3] * second_matrix[3],
    )


def block_inverse(matrix):
    determinant = matrix[0] * matrix[3] - matrix[1] * matrix[2]
    reciprocal = 1.0 / determinant
    return (
        matrix[3] * reciprocal,
        -matrix[1] * reciprocal,
        -matrix[2] * reciprocal,
        matrix[0] * reciprocal,
    )


def block_apply(matrix, vector):
    return (
        matrix[0] * vector[0] + matrix[1] * vector[1],
        matrix[2] * vector[0] + matrix[3] * vector[1],
    )


def add_blocks(first_members, second_members):
    return tuple((a + b for a, b in zip(first_members, second_members)))


def negate(members):
    return tuple((-a for a in members))


def extend_blocks(members, fill_values):
    return tuple(
        (
            jnp.concatenate([m, jnp.full_like(m[..., :1, :], f)], axis=-2)
            for m, f in zip(members, fill_values)
        )
    )


def shift_next(members, fill_values):
    return tuple(
        (
            jnp.concatenate([m[..., 1:, :], jnp.full_like(m[..., :1, :], f)], axis=-2)
            for m, f in zip(members, fill_values)
        )
    )


def shift_prev(members):
    return tuple(
        (jnp.concatenate([jnp.zeros_like(m[..., :1, :]), m[..., :-1, :]], axis=-2) for m in members)
    )


def pair_split(member):
    shaped = member.reshape(member.shape[:-2] + (member.shape[-2] // 2, 2, member.shape[-1]))
    return (shaped[..., 0, :], shaped[..., 1, :])


def split_parity(members):
    halves = [pair_split(m) for m in members]
    return (tuple((h[0] for h in halves)), tuple((h[1] for h in halves)))


def alternate(first_member, second_member):
    stacked = jnp.stack((first_member, second_member), axis=-2)
    return stacked.reshape(
        first_member.shape[:-2] + (2 * first_member.shape[-2], first_member.shape[-1])
    )


def reduce_blocks(sub_blocks, diag_blocks, super_blocks, right_side):
    block_count = diag_blocks[0].shape[-2]
    if block_count == 1:
        return block_apply(block_inverse(diag_blocks), right_side)
    if block_count % 2 == 1:
        sub_blocks = extend_blocks(sub_blocks, ZERO_BLOCK)
        diag_blocks = extend_blocks(diag_blocks, UNIT_BLOCK)
        super_blocks = extend_blocks(super_blocks, ZERO_BLOCK)
        right_side = extend_blocks(right_side, ZERO_PAIR)
    sub_even, sub_odd = split_parity(sub_blocks)
    diag_even, diag_odd = split_parity(diag_blocks)
    super_even, super_odd = split_parity(super_blocks)
    side_even, side_odd = split_parity(right_side)
    inverse_even = block_inverse(diag_even)
    inverse_next = shift_next(inverse_even, UNIT_BLOCK)
    sub_next = shift_next(sub_even, ZERO_BLOCK)
    super_next = shift_next(super_even, ZERO_BLOCK)
    side_next = shift_next(side_even, ZERO_PAIR)
    left_factor = negate(block_product(sub_odd, inverse_even))
    right_factor = negate(block_product(super_odd, inverse_next))
    reduced_sub = block_product(left_factor, sub_even)
    reduced_diag = add_blocks(
        diag_odd,
        add_blocks(block_product(left_factor, super_even), block_product(right_factor, sub_next)),
    )
    reduced_super = block_product(right_factor, super_next)
    reduced_side = add_blocks(
        side_odd,
        add_blocks(block_apply(left_factor, side_even), block_apply(right_factor, side_next)),
    )
    odd_values = reduce_blocks(reduced_sub, reduced_diag, reduced_super, reduced_side)
    before_values = shift_prev(odd_values)
    remainder = add_blocks(
        side_even,
        negate(
            add_blocks(block_apply(sub_even, before_values), block_apply(super_even, odd_values))
        ),
    )
    even_values = block_apply(inverse_even, remainder)
    merged = tuple((alternate(e, o) for e, o in zip(even_values, odd_values)))
    return tuple((m[..., :block_count, :] for m in merged))


def cells_leading(block):
    moved = jnp.transpose(block, (2, 0, 1, 3))
    return moved.reshape(block.shape[2], block.shape[0] * block.shape[1] * block.shape[3])


def solve_in_lanes(coefficients, line_source):
    source_shape = line_source.shape
    lane_coef = [cells_leading(jnp.broadcast_to(c[:, None], source_shape)) for c in coefficients]
    pairs_list = [pair_split(m) for m in lane_coef]
    zero_plane = jnp.zeros_like(pairs_list[2][0])
    sub_blocks = (pairs_list[0][0], pairs_list[1][0], zero_plane, pairs_list[0][1])
    diag_blocks = (pairs_list[2][0], pairs_list[3][0], pairs_list[1][1], pairs_list[2][1])
    super_blocks = (pairs_list[4][0], zero_plane, pairs_list[3][1], pairs_list[4][1])
    values = reduce_blocks(
        sub_blocks, diag_blocks, super_blocks, pair_split(cells_leading(line_source))
    )
    flat = alternate(values[0], values[1])
    shaped = flat.reshape(source_shape[2], source_shape[0], source_shape[1], source_shape[3])
    return jnp.transpose(shaped, (1, 2, 0, 3))


def return_tiles(line_values):
    return lax.all_to_all(line_values, "cell", split_axis=2, concat_axis=3, tiled=True)


def local_by_lines(state, pseudo_rate, line_next, face_codes):
    local_count = state.shape[0]
    tile_cells = state.shape[2]
    cell_index = lax.axis_index("cell")
    cell_count = lax.axis_size("cell")
    total_cells = tile_cells * cell_count
    spectral = spectral_matrix(NT)
    first_local = lax.axis_index("inst") * local_count
    own_rows = lax.dynamic_slice_in_dim(spectral, first_local, local_count, 0)
    shard_block = jax.tree.map(lambda a: lax.all_gather(a, "inst", axis=0, tiled=True), state)
    columns = lax.slice_in_dim(own_rows, 0, shard_block.shape[0], axis=1)
    time_term = jnp.zeros_like(state) + jnp.einsum(
        "nm,mvil->nvil", columns, shard_block, precision=lax.Precision.HIGHEST
    )
    padded = extended(state, (("cell", 2),), 2)
    codes_lines = jnp.repeat(face_codes, LINES_DEV, axis=1)
    lower_ghost = boundary_cells(state[:, :, 0:2, :], codes_lines[0], True)
    upper_ghost = boundary_cells(state[:, :, -2:, :], codes_lines[1], False)
    lower_rim = jnp.where(cell_index == 0, lower_ghost, padded[:, :, :2, :])
    upper_rim = jnp.where(cell_index == cell_count - 1, upper_ghost, padded[:, :, -2:, :])
    padded = jnp.concatenate([lower_rim, padded[:, :, 2:-2, :], upper_rim], axis=2)
    line_part, radius = line_residual(padded)
    prev_lines = (
        jnp.zeros_like(line_next).at[line_next].set(jnp.arange(line_next.shape[0], dtype=jnp.int32))
    )
    residual = line_part + pitch_residual(state, line_next, prev_lines) + time_term
    right_side = -residual
    centre_radius = radius[:, 2:-2, :]
    diagonal_term = pseudo_rate * centre_radius
    positions = cell_index * tile_cells + jnp.arange(-1, tile_cells + 1, dtype=jnp.int32)
    inside = (positions >= 0) & (positions < total_cells)
    radius_ext = jnp.where(inside[:, None], radius[:, 1:-1, :], 0.0)
    coefficients = line_coefficients(radius_ext, diagonal_term, positions[1:-1], total_cells)
    stacked = jnp.stack(coefficients, axis=1)
    line_source = lax.all_to_all(right_side, "cell", split_axis=3, concat_axis=2, tiled=True)
    line_coef = lax.all_to_all(stacked, "cell", split_axis=3, concat_axis=2, tiled=True)
    update = return_tiles(solve_in_lanes(tuple((line_coef[:, k] for k in range(5))), line_source))
    return state + update


LANES = 128
ROWS = 8
PAIRS = 3
CELL_ROWS = PAIRS * ROWS
REST_ROW = 2 * CELL_ROWS
RATE_ROW = 2 * REST_ROW
VMEM_BYTES = 8 * 2**20
BLOCK_ROWS = RATE_ROW + ROWS

SIDE_ROW = 3 * CELL_ROWS
CORRECTION_ROW = SIDE_ROW + 2 * CELL_ROWS
MIDDLE_ROWS = CORRECTION_ROW + 2 * ROWS
BLOCK_PLANES = 4 + 3 + 2 * PAIRS


def spectral_offsets():
    table = np.zeros(NT)
    for offset in range(1, NT):
        angle = np.pi * offset / NT
        parity = -1.0 if offset % 2 == 0 else 1.0
        table[offset] = 0.5 * OMEGA_BLADE * parity * np.cos(angle) / np.sin(angle)
    return [float(np.float32(value)) for value in table]


def plane_masks():
    row_index = lax.broadcasted_iota(jnp.int32, (ROWS, LANES), 0)
    return row_index < 4, (row_index & 2) == 0, row_index & 1


def both(first_var, plane):
    turned = pltpu.roll(plane, 4, 0)
    return jnp.where(first_var, plane, turned), jnp.where(first_var, turned, plane)


def primitives(first_var, planes):
    density, moment_x = both(first_var, planes[0])
    moment_y, moment_z = both(first_var, planes[1])
    energy = jnp.where(first_var, planes[2], pltpu.roll(planes[2], 4, 0))
    inverse = 1.0 / density
    velocity_x = moment_x * inverse
    velocity_y = moment_y * inverse
    velocity_z = moment_z * inverse
    kinetic = moment_x * velocity_x + moment_y * velocity_y + moment_z * velocity_z
    pressure = (GAMMA_GAS - 1.0) * (energy - 0.5 * kinetic)
    sound = jnp.sqrt(GAMMA_GAS * pressure * inverse)
    return velocity_x, velocity_y, pressure, sound


def rows_of(var, inst, half):
    return (var // 2) * ROWS + (var % 2) * 4 + inst * 2 + half


def cell_kernel(all_ref, rate_ref, out_ref, plane_ref):
    own_inst = lax.axis_index("inst")
    inst_count = all_ref.shape[0] // 2
    copies = out_ref.shape[0]
    mirrored = lax.axis_index("cell") // copies
    _, first_inst, _ = plane_masks()

    for shift in range(inst_count):
        pair = (own_inst - shift) & (inst_count - 1)
        for cell in range(2):
            for var in range(6):
                for inst in range(2):
                    for half in range(2):
                        row = cell * CELL_ROWS + rows_of(var, inst, half)
                        plane_ref[shift, pl.ds(row, 1), :] = all_ref[
                            2 * pair + inst, var, pl.ds(cell, 1), pl.ds(half * LANES, LANES)
                        ]
    offsets = spectral_offsets()
    for row in range(0, REST_ROW, ROWS):
        same_total, other_total = None, None
        for shift in range(inst_count):
            plane = plane_ref[shift, pl.ds(row, ROWS), :]
            other = jnp.where(
                first_inst, offsets[(2 * shift + 1) % NT], offsets[(2 * shift - 1) % NT]
            )
            if shift > 0:
                term = offsets[(2 * shift) % NT] * plane
                same_total = term if same_total is None else same_total + term
            term = other * plane
            other_total = term if other_total is None else other_total + term
        turned = jnp.where(
            first_inst, pltpu.roll(other_total, 6, 0), pltpu.roll(other_total, 2, 0)
        )
        own = plane_ref[0, pl.ds(row, ROWS), :]
        place = jnp.bitwise_xor(row // CELL_ROWS, mirrored) * CELL_ROWS + row % CELL_ROWS
        place = pl.multiple_of(place, ROWS)
        for copy in range(copies):
            out_ref[copy, pl.ds(place, ROWS), :] = own
            out_ref[copy, pl.ds(REST_ROW + place, ROWS), :] = same_total + turned
    rates = [
        rate_ref[pl.ds(cell, 1), pl.ds(half * LANES, LANES)]
        for cell in range(2)
        for half in range(2)
    ]
    rates = [jnp.where(mirrored == 0, rates[k], rates[k ^ 2]) for k in range(4)]
    for copy in range(copies):
        for row, rate in enumerate(rates):
            out_ref[copy, pl.ds(RATE_ROW + row, 1), :] = rate
        out_ref[copy, pl.ds(RATE_ROW + 4, 4), :] = jnp.zeros((4, LANES), jnp.float32)


def two_by_two(first, second):
    def entry(a, b, c, d):
        terms = [x * y for x, y in ((a, b), (c, d)) if x is not None and y is not None]
        return None if not terms else terms[0] if len(terms) == 1 else terms[0] + terms[1]

    return (
        entry(first[0], second[0], first[1], second[2]),
        entry(first[0], second[1], first[1], second[3]),
        entry(first[2], second[0], first[3], second[2]),
        entry(first[2], second[1], first[3], second[3]),
    )


def inverse_of(matrix):
    reciprocal = 1.0 / (matrix[0] * matrix[3] - matrix[1] * matrix[2])
    return (
        matrix[3] * reciprocal,
        -(matrix[1] * reciprocal),
        -(matrix[2] * reciprocal),
        matrix[0] * reciprocal,
    )


def less(first, second):
    return tuple(a if b is None else a - b for a, b in zip(first, second))


def minus(members):
    return tuple(None if a is None else -a for a in members)


def matrix_vector(matrix, low, high):
    def row(a, b):
        terms = [x * y for x, y in ((a, low), (b, high)) if x is not None]
        return terms[0] if len(terms) == 1 else terms[0] + terms[1]

    return row(matrix[0], matrix[1]), row(matrix[2], matrix[3])


def apply_matrix(matrix, side):
    parts = [matrix_vector(matrix, side[k], side[PAIRS + k]) for k in range(PAIRS)]
    return [low for low, _ in parts] + [high for _, high in parts]


def difference(first, second):
    return [a - b for a, b in zip(first, second)]


def flux_along(first_var, planes, velocity, pressure, sign):
    normal = sign * velocity
    return [
        planes[0] * normal + jnp.where(first_var, 0.0, sign * pressure),
        planes[1] * normal,
        planes[2] * normal + jnp.where(first_var, pressure * normal, 0.0),
    ]


class LineCells:
    def __init__(self, first_var, sign):
        self.first_var, self.sign = first_var, sign
        self.state, self.pressure, self.radius = {}, {}, {}
        self.flux, self.step, self.sensor = {}, {}, {}

    def add(self, cell, planes, velocity, pressure, sound):
        self.state[cell], self.pressure[cell] = planes, pressure
        self.radius[cell] = jnp.abs(velocity) + sound
        self.flux[cell] = flux_along(self.first_var, planes, velocity, pressure, self.sign)
        if cell - 1 in self.state:
            self.step[cell - 1] = difference(planes, self.state[cell - 1])
        if cell - 2 in self.state:
            twice = 2.0 * self.pressure[cell - 1]
            outer = pressure + self.pressure[cell - 2]
            self.sensor[cell - 1] = jnp.abs(outer - twice) / (outer + twice)

    def face(self, cell):
        second = SENSOR_GAIN * jnp.maximum(self.sensor[cell], self.sensor[cell + 1])
        fourth = jnp.maximum(0.0, FOURTH_GAIN - second)
        face_radius = 0.5 * (self.radius[cell] + self.radius[cell + 1])
        near_weight = face_radius * (second + 2.0 * fourth)
        far_weight = face_radius * fourth
        return [
            0.5 * (self.flux[cell][k] + self.flux[cell + 1][k])
            - (
                near_weight * self.step[cell][k]
                - far_weight * (self.step[cell + 1][k] + self.step[cell - 1][k])
            )
            for k in range(PAIRS)
        ]

    def near(self, cell):
        scale = SECOND_IMPL * 0.5 + 2.0 * FOURTH_IMPL
        return -scale * (self.radius[cell] + self.radius[cell + 1])

    def far(self, cell):
        return FOURTH_IMPL * self.radius[cell]

    def middle(self, cell, rate):
        centre, above = self.radius[cell], self.radius[cell + 1]
        if cell == 0:
            total, weighted = centre + (centre + above), 4.0 * centre + above
        else:
            below = self.radius[cell - 1]
            total = (below + centre) + (centre + above)
            weighted = below + 4.0 * centre + above
        result = SECOND_IMPL * (0.5 * total) + FOURTH_IMPL * weighted
        return result if rate is None else rate * centre + result

    def diagonal(self, cell, rates):
        across = self.near(cell)
        return (self.middle(cell, rates[0]), across, across, self.middle(cell + 1, rates[1]))

    def below(self, cell):
        return (self.far(cell - 1), self.near(cell - 1), None, self.far(cell))

    def above(self, cell):
        return (self.far(cell + 1), None, self.near(cell + 1), self.far(cell + 2))


def rates_at(ref, index, start, first_half):
    rows = [ref[index + (pl.ds(start + k, 1), slice(None))] for k in range(4)]
    return [jnp.where(first_half, rows[2 * k], rows[2 * k + 1]) for k in range(2)]


def half_kernel(
    all_ref, next_ref, codes_ref, middle_ref, blocks_ref, rest_ref, line_ref,
):
    blocks = all_ref.shape[0]
    cells = 2 * blocks
    mirrored = lax.axis_index("cell") // blocks
    sign = (1 - 2 * mirrored).astype(jnp.float32)
    shape = (ROWS, LANES)
    lane_index = lax.broadcasted_iota(jnp.int32, shape, 1)
    first_var, _, half_index = plane_masks()
    first_half = half_index == 0
    zero = jnp.zeros(shape, jnp.float32)

    next_rows = [
        next_ref[pl.ds(half * LANES, LANES)].reshape(1, LANES) for half in range(2)
    ]
    next_line = jnp.where(first_half, next_rows[0], next_rows[1])
    column = lax.broadcasted_iota(jnp.int32, (LANES, LANES), 0)
    prev_halves = []
    for target in range(2):
        total = None
        for source in range(2):
            hits = jnp.where(column + target * LANES == next_rows[source], 1.0, 0.0)
            names = (lane_index + source * LANES).astype(jnp.float32)
            part = lax.dot_general(
                names, hits, (((1,), (1,)), ((), ())), preferred_element_type=jnp.float32
            )
            total = part if total is None else total + part
        prev_halves.append(total)
    prev_line = jnp.where(first_half, prev_halves[0], prev_halves[1]).astype(jnp.int32)

    def picker(lines):
        lane = lines & (LANES - 1)
        same = (lines >> 7) == half_index

        def pick(plane):
            swapped = jnp.where(first_half, pltpu.roll(plane, 7, 0), pltpu.roll(plane, 1, 0))
            here = jnp.take_along_axis(plane, lane, axis=1, mode="promise_in_bounds")
            there = jnp.take_along_axis(swapped, lane, axis=1, mode="promise_in_bounds")
            return jnp.where(same, here, there)

        return pick

    pick_next = picker(next_line)
    pick_prev = picker(prev_line)

    def loaded(cell, start=0):
        return [
            all_ref[cell // 2, pl.ds(start + (cell % 2) * CELL_ROWS + k * ROWS, ROWS), :]
            for k in range(PAIRS)
        ]

    def flux_across(planes, velocity, pressure):
        return [
            planes[0] * velocity,
            planes[1] * velocity + jnp.where(first_var, pressure, 0.0),
            planes[2] * velocity + jnp.where(first_var, pressure * velocity, 0.0),
        ]

    def pitch_flux(planes, velocity_y, pressure, sound):
        nearby = [pick_next(plane) for plane in planes]
        _, next_velocity, next_pressure, next_sound = primitives(first_var, nearby)
        own_flux = flux_across(planes, velocity_y, pressure)
        next_flux = flux_across(nearby, next_velocity, next_pressure)
        weight = (PITCH_GAIN * 0.5) * (
            jnp.abs(velocity_y) + sound + (jnp.abs(next_velocity) + next_sound)
        )
        return [
            0.5 * (a + b) - weight * (n - o)
            for a, b, n, o in zip(own_flux, next_flux, nearby, planes)
        ]

    for cell in range(cells):
        planes = loaded(cell)
        velocity_x, velocity_y, pressure, sound = primitives(first_var, planes)
        line_ref[cell, 0], line_ref[cell, 1], line_ref[cell, 2] = velocity_x, pressure, sound
        faces_across = pitch_flux(planes, velocity_y, pressure, sound)
        times = loaded(cell, REST_ROW)
        for k in range(PAIRS):
            rest_ref[cell, k] = times[k] + (faces_across[k] - pick_prev(faces_across[k]))

    tile = half_index * (LANES // LINES_DEV) + lane_index // LINES_DEV
    end_codes = jnp.where(mirrored == 0, codes_ref[pl.ds(0, 1), :], codes_ref[pl.ds(1, 1), :])
    codes = jnp.zeros(shape, jnp.int32)
    for k in range(2 * LANES // LINES_DEV):
        codes = jnp.where(tile == k, jnp.broadcast_to(end_codes[:, k : k + 1], shape), codes)

    def ghost(cell):
        planes = loaded(-1 - cell)
        copied = loaded(0)
        result = []
        for k in range(PAIRS):
            reflected = planes[k] if k else jnp.where(first_var, planes[k], -planes[k])
            inflow = jnp.where(first_var, FREE_STATE[2 * k], FREE_STATE[2 * k + 1])
            result.append(
                jnp.where(codes == 0, reflected, jnp.where(codes == 1, inflow, copied[k]))
            )
        return result

    line = LineCells(first_var, sign)
    sides, faces, inverses, aboves = [], {}, [], []
    for cell in range(-2, cells):
        if cell < 0:
            planes = ghost(cell)
            velocity_x, _, pressure, sound = primitives(first_var, planes)
        else:
            planes = loaded(cell)
            velocity_x, pressure, sound = [line_ref[cell, k] for k in range(3)]
        line.add(cell, planes, velocity_x, pressure, sound)
        if cell >= 1:
            faces[cell - 2] = line.face(cell - 2)
        if cell >= 3 and cell % 2 == 1:
            at = cell - 3
            block = at // 2
            rates = rates_at(all_ref, (block,), RATE_ROW, first_half)
            diag = line.diagonal(at, rates)
            side = []
            for member in range(2):
                for k in range(PAIRS):
                    side.append(
                        faces[at + member - 1][k] - faces[at + member][k]
                        - rest_ref[at + member, k]
                    )
            if block > 0:
                factor = two_by_two(line.below(at), inverses[-1])
                diag = less(diag, two_by_two(factor, aboves[-1]))
                side = difference(side, apply_matrix(factor, sides[-1]))
            inverses.append(inverse_of(diag))
            aboves.append(line.above(at))
            sides.append(side)

    last = cells - 2
    factor = two_by_two(line.below(last), inverses[-1])
    correction = list(two_by_two(factor, aboves[-1]))
    rates = rates_at(all_ref, (blocks - 1,), RATE_ROW, first_half)
    for member in range(2):
        centre = line.radius[last + member]
        correction[3 * member] = correction[3 * member] - rates[member] * centre
    side = [faces[last - 1][k] - rest_ref[last, k] for k in range(PAIRS)]
    side += [-rest_ref[last + 1, k] for k in range(PAIRS)]
    side = difference(side, apply_matrix(factor, sides[-1]))
    for n in range(3):
        for k, plane in enumerate(line.state[cells - 3 + n]):
            middle_ref[pl.ds(n * CELL_ROWS + k * ROWS, ROWS), :] = plane
    for n, plane in enumerate(side):
        middle_ref[pl.ds(SIDE_ROW + n * ROWS, ROWS), :] = plane
    for n in range(2):
        middle_ref[pl.ds(CORRECTION_ROW + n * ROWS, ROWS), :] = jnp.where(
            first_var, correction[2 * n], correction[2 * n + 1]
        )
    for block in range(blocks - 1):
        kept = [*inverses[block], aboves[block][0], *aboves[block][2:], *sides[block]]
        for n, plane in enumerate(kept):
            blocks_ref[block, n] = plane


def spread_kernel(all_ref, blocks_ref, known_ref, spread_ref, table_ref):
    blocks = all_ref.shape[0]
    own_cell = lax.axis_index("cell")
    own_block = jnp.where(own_cell < blocks, own_cell, 2 * blocks - 1 - own_cell)
    zero = jnp.zeros((ROWS, LANES), jnp.float32)
    known, spread = [zero] * (2 * PAIRS), (zero + 1.0, zero, zero, zero + 1.0)
    for block in range(blocks - 1, -1, -1):
        if block < blocks - 1:
            kept = [blocks_ref[block, n] for n in range(BLOCK_PLANES)]
            inverse, above, side = kept[:4], (kept[4], None, kept[5], kept[6]), kept[7:]
            step = two_by_two(inverse, above)
            own = apply_matrix(inverse, side)
            if block < blocks - 2:
                known = difference(own, apply_matrix(step, known))
                spread = minus(two_by_two(step, spread))
            else:
                known, spread = own, minus(step)
        for n, plane in enumerate(known + list(spread)):
            table_ref[block, n] = plane
    for n in range(2 * PAIRS):
        known_ref[n] = all_ref[own_block, pl.ds(n * ROWS, ROWS), :] + table_ref[own_block, n]
    for n in range(4):
        spread_ref[n] = table_ref[own_block, 2 * PAIRS + n]


def join_kernel(here_ref, there_ref, known_ref, spread_ref, out_ref):
    mirrored = lax.axis_index("cell") // (lax.axis_size("cell") // 2)
    sign = (1 - 2 * mirrored).astype(jnp.float32)
    first_var, _, _ = plane_masks()

    def plane_of(ref, row):
        return ref[pl.ds(row, ROWS), :]

    line = LineCells(first_var, sign)
    for cell in range(6):
        ref, at = (here_ref, cell) if cell < 3 else (there_ref, 5 - cell)
        planes = [plane_of(ref, at * CELL_ROWS + k * ROWS) for k in range(PAIRS)]
        velocity_x, _, pressure, sound = primitives(first_var, planes)
        line.add(cell, planes, velocity_x, pressure, sound)
    faces = {cell: line.face(cell) for cell in (1, 2, 3)}

    def correction_of(ref):
        pairs = [both(first_var, plane_of(ref, CORRECTION_ROW + n * ROWS)) for n in range(2)]
        return [pairs[0][0], pairs[0][1], pairs[1][0], pairs[1][1]]

    here_side = [plane_of(here_ref, SIDE_ROW + n * ROWS) for n in range(2 * PAIRS)]
    there_side = [plane_of(there_ref, SIDE_ROW + n * ROWS) for n in range(2 * PAIRS)]
    side = [here_side[k] - faces[1][k] for k in range(PAIRS)]
    side += [here_side[PAIRS + k] + (faces[1][k] - faces[2][k]) for k in range(PAIRS)]
    other = [there_side[PAIRS + k] + (faces[2][k] - faces[3][k]) for k in range(PAIRS)]
    other += [there_side[k] + faces[3][k] for k in range(PAIRS)]
    no_rates = (None, None)
    diag = difference(line.diagonal(1, no_rates), correction_of(here_ref))
    other_diag = difference(line.diagonal(3, no_rates), correction_of(there_ref)[::-1])
    factor = two_by_two(line.above(1), inverse_of(other_diag))
    diag = less(diag, two_by_two(factor, line.below(3)))
    middle = apply_matrix(inverse_of(diag), difference(side, apply_matrix(factor, other)))
    moved = apply_matrix([spread_ref[n] for n in range(4)], middle)
    results = [known_ref[n] + moved[n] for n in range(2 * PAIRS)]
    for cell in range(2):
        for k in range(PAIRS):
            first, second = results[cell * PAIRS + k], results[(1 - cell) * PAIRS + k]
            result = jnp.where(mirrored == 0, first, second)
            for var in range(2):
                for inst in range(2):
                    for half in range(2):
                        row = rows_of(var, inst, half)
                        out_ref[
                            inst, 2 * k + var, pl.ds(cell, 1), pl.ds(half * LANES, LANES)
                        ] = result[row : row + 1]


def share_half(copies):
    count = lax.axis_size("cell")
    groups = [list(range(count // 2)), list(range(count - 1, count // 2 - 1, -1))]
    return lax.all_to_all(
        copies, "cell", split_axis=0, concat_axis=0, tiled=True, axis_index_groups=groups
    )


def swap_halves(block):
    count = lax.axis_size("cell")
    return lax.ppermute(block, "cell", [(i, (i + count // 2) % count) for i in range(count)])


def float_shape(*sizes):
    return jax.ShapeDtypeStruct(sizes, jnp.float32)


def local_by_halves(state, pseudo_rate, line_next, face_codes):
    blocks = lax.axis_size("cell") // 2
    cells = 2 * blocks
    vmem = pl.BlockSpec(memory_space=pltpu.VMEM)
    plane = (ROWS, LANES)
    params = pltpu.CompilerParams(vmem_limit_bytes=VMEM_BYTES)
    every = lax.all_gather(state, "inst", axis=0, tiled=True)
    packed = pl.pallas_call(
        cell_kernel,
        out_shape=float_shape(blocks, BLOCK_ROWS, LANES),
        in_specs=[vmem, vmem],
        out_specs=vmem,
        scratch_shapes=[pltpu.VMEM((every.shape[0] // 2, REST_ROW, LANES), jnp.float32)],
        compiler_params=params,
    )(every, pseudo_rate)
    shared = share_half(packed)
    here, eliminated = pl.pallas_call(
        half_kernel,
        out_shape=(
            float_shape(MIDDLE_ROWS, LANES),
            float_shape(blocks - 1, BLOCK_PLANES, *plane),
        ),
        in_specs=[vmem, vmem, vmem],
        out_specs=(vmem, vmem),
        scratch_shapes=[
            pltpu.VMEM((cells, PAIRS) + plane, jnp.float32),
            pltpu.VMEM((cells, 3) + plane, jnp.float32),
        ],
        compiler_params=params,
    )(shared, line_next, face_codes)
    there = swap_halves(here)
    known, spread = pl.pallas_call(
        spread_kernel,
        out_shape=(float_shape(2 * PAIRS, *plane), float_shape(4, *plane)),
        in_specs=[vmem, vmem],
        out_specs=(vmem, vmem),
        scratch_shapes=[pltpu.VMEM((blocks, 2 * PAIRS + 4) + plane, jnp.float32)],
        compiler_params=params,
        cost_estimate=pl.CostEstimate(flops=10**6, bytes_accessed=10**6, transcendentals=0),
    )(shared, eliminated)
    return pl.pallas_call(
        join_kernel,
        out_shape=float_shape(*state.shape),
        in_specs=[vmem] * 4,
        out_specs=vmem,
        compiler_params=params,
    )(here, there, known, spread)


def solution(mesh):
    placed = (P("inst", None, "cell", None), P("cell", None), P(), P())
    inst_count, cell_count = mesh.shape["inst"], mesh.shape["cell"]

    def local(state, pseudo_rate, line_next, face_codes):
        small = (
            state.shape == (2, 6, 2, 2 * LANES)
            and inst_count * 2 == NT
            and cell_count == 8
            and face_codes.shape[1] * LINES_DEV == state.shape[3]
        )
        chosen = local_by_halves if small else local_by_lines
        return chosen(state, pseudo_rate, line_next, face_codes)

    return jax.shard_map(
        local, mesh=mesh, in_specs=placed, out_specs=P("inst", None, "cell", None), check_vma=False
    )
```

```python
import functools

import jax
import jax.numpy as jnp
import numpy as np
from jax import lax
from jax.experimental import pallas as pl
from jax.experimental.pallas import tpu as pltpu
from jax.sharding import PartitionSpec as P

NT = 8
LINES_DEV = 32


GAMMA_GAS = 1.4
OMEGA_BLADE = 1.0
SENSOR_GAIN = 0.25
FOURTH_GAIN = 0.03125
PITCH_GAIN = 0.5
SECOND_IMPL = 1.0
FOURTH_IMPL = 0.25
FREE_STATE = (1.0, 0.5, 0.0, 0.0, 2.625, 0.2)
MIRROR_SIGNS = (1.0, -1.0, 1.0, 1.0, 1.0, 1.0)
ZERO_BLOCK = (0.0, 0.0, 0.0, 0.0)
UNIT_BLOCK = (1.0, 0.0, 0.0, 1.0)
ZERO_PAIR = (0.0, 0.0)


def extended(block, sides, width):
    for axis, dim in sides:
        count = lax.axis_size(axis)
        forward = [(i, i + 1) for i in range(count - 1)]
        backward = [(target, source) for source, target in forward]
        low = lax.ppermute(
            lax.slice_in_dim(block, block.shape[dim] - width, None, axis=dim), axis, forward
        )
        high = lax.ppermute(lax.slice_in_dim(block, 0, width, axis=dim), axis, backward)
        block = jnp.concatenate([low, block, high], axis=dim)
    return block


def spectral_matrix(instances):
    offsets = np.arange(instances)[:, None] - np.arange(instances)[None, :]
    angles = np.pi * offsets / instances
    safe_sin = np.where(offsets == 0, 1.0, np.sin(angles))
    parity = np.where(np.mod(offsets, 2) == 0, -1.0, 1.0)
    matrix_table = np.where(
        offsets == 0, 0.0, 0.5 * OMEGA_BLADE * parity * np.cos(angles) / safe_sin
    )
    return jnp.asarray(matrix_table, jnp.float32)


def primitive_parts(cells_state):
    density = cells_state[..., 0, :, :]
    inverse = 1.0 / density
    velocity_x = cells_state[..., 1, :, :] * inverse
    velocity_y = cells_state[..., 2, :, :] * inverse
    velocity_z = cells_state[..., 3, :, :] * inverse
    energy = cells_state[..., 4, :, :]
    pressure = (GAMMA_GAS - 1.0) * (
        energy
        - 0.5
        * density
        * (velocity_x * velocity_x + velocity_y * velocity_y + velocity_z * velocity_z)
    )
    sound_speed = jnp.sqrt(GAMMA_GAS * pressure * inverse)
    return (velocity_x, velocity_y, pressure, sound_speed)


def directed_flux(cells_state, normal_velocity, pressure, component):
    zero_plane = jnp.zeros_like(pressure)
    pressure_rows = [
        zero_plane,
        zero_plane,
        zero_plane,
        zero_plane,
        pressure * normal_velocity,
        zero_plane,
    ]
    pressure_rows[component] = pressure
    return cells_state * normal_velocity[..., None, :, :] + jnp.stack(pressure_rows, axis=-3)


def line_residual(padded):
    velocity_x, velocity_y, pressure, sound_speed = primitive_parts(padded)
    flux_line = directed_flux(padded, velocity_x, pressure, 1)
    radius = jnp.abs(velocity_x) + sound_speed
    sensor = jnp.abs(
        pressure[..., 2:, :] - 2.0 * pressure[..., 1:-1, :] + pressure[..., :-2, :]
    ) / (pressure[..., 2:, :] + 2.0 * pressure[..., 1:-1, :] + pressure[..., :-2, :])
    second = SENSOR_GAIN * jnp.maximum(sensor[..., :-1, :], sensor[..., 1:, :])
    fourth = jnp.maximum(0.0, FOURTH_GAIN - second)
    face_radius = 0.5 * (radius[..., 1:-2, :] + radius[..., 2:-1, :])
    left_far = padded[..., :-3, :]
    left_near = padded[..., 1:-2, :]
    right_near = padded[..., 2:-1, :]
    right_far = padded[..., 3:, :]
    damping = face_radius[..., None, :, :] * (
        second[..., None, :, :] * (right_near - left_near)
        - fourth[..., None, :, :] * (right_far - 3.0 * right_near + 3.0 * left_near - left_far)
    )
    face_flux = 0.5 * (flux_line[..., 1:-2, :] + flux_line[..., 2:-1, :]) - damping
    return (face_flux[..., 1:, :] - face_flux[..., :-1, :], radius)


def pitch_parts(cells_state):
    velocity_x, velocity_y, pressure, sound_speed = primitive_parts(cells_state)
    return (directed_flux(cells_state, velocity_y, pressure, 2), jnp.abs(velocity_y) + sound_speed)


def pitch_residual(cells_state, next_lines, prev_lines):
    pitch_flux, radius = pitch_parts(cells_state)
    state_next = jnp.take(cells_state, next_lines, axis=-1)
    flux_next, radius_next = pitch_parts(state_next)
    face_flux = 0.5 * (pitch_flux + flux_next) - PITCH_GAIN * (0.5 * (radius + radius_next))[
        ..., None, :, :
    ] * (state_next - cells_state)
    return face_flux - jnp.take(face_flux, prev_lines, axis=-1)


def boundary_cells(edge_pair, line_codes, lower_end):
    reflected = edge_pair[..., ::-1, :] * jnp.asarray(MIRROR_SIGNS, jnp.float32)[:, None, None]
    if lower_end:
        copied = jnp.concatenate([edge_pair[..., :1, :], edge_pair[..., :1, :]], axis=-2)
    else:
        copied = jnp.concatenate([edge_pair[..., 1:, :], edge_pair[..., 1:, :]], axis=-2)
    inflow = jnp.asarray(FREE_STATE, jnp.float32)[:, None, None] + jnp.zeros_like(edge_pair)
    return jnp.where(line_codes == 0, reflected, jnp.where(line_codes == 1, inflow, copied))


def line_coefficients(radius_ext, diagonal_term, positions, total_cells):
    radius_below = radius_ext[..., :-2, :]
    radius_centre = radius_ext[..., 1:-1, :]
    radius_above = radius_ext[..., 2:, :]
    face_below = 0.5 * (radius_below + radius_centre)
    face_above = 0.5 * (radius_centre + radius_above)
    far_low = FOURTH_IMPL * radius_below
    near_low = -SECOND_IMPL * face_below - 2.0 * FOURTH_IMPL * (radius_below + radius_centre)
    middle = (
        diagonal_term
        + SECOND_IMPL * (face_below + face_above)
        + FOURTH_IMPL * (radius_below + 4.0 * radius_centre + radius_above)
    )
    near_high = -SECOND_IMPL * face_above - 2.0 * FOURTH_IMPL * (radius_centre + radius_above)
    far_high = FOURTH_IMPL * radius_above
    column = positions[:, None]
    far_low = jnp.where(column >= 2, far_low, 0.0)
    near_low = jnp.where(column >= 1, near_low, 0.0)
    near_high = jnp.where(column <= total_cells - 2, near_high, 0.0)
    far_high = jnp.where(column <= total_cells - 3, far_high, 0.0)
    return (far_low, near_low, middle, near_high, far_high)


def block_product(first_matrix, second_matrix):
    return (
        first_matrix[0] * second_matrix[0] + first_matrix[1] * second_matrix[2],
        first_matrix[0] * second_matrix[1] + first_matrix[1] * second_matrix[3],
        first_matrix[2] * second_matrix[0] + first_matrix[3] * second_matrix[2],
        first_matrix[2] * second_matrix[1] + first_matrix[3] * second_matrix[3],
    )


def block_inverse(matrix):
    determinant = matrix[0] * matrix[3] - matrix[1] * matrix[2]
    reciprocal = 1.0 / determinant
    return (
        matrix[3] * reciprocal,
        -matrix[1] * reciprocal,
        -matrix[2] * reciprocal,
        matrix[0] * reciprocal,
    )


def block_apply(matrix, vector):
    return (
        matrix[0] * vector[0] + matrix[1] * vector[1],
        matrix[2] * vector[0] + matrix[3] * vector[1],
    )


def add_blocks(first_members, second_members):
    return tuple((a + b for a, b in zip(first_members, second_members)))


def negate(members):
    return tuple((-a for a in members))


def extend_blocks(members, fill_values):
    return tuple(
        (
            jnp.concatenate([m, jnp.full_like(m[..., :1, :], f)], axis=-2)
            for m, f in zip(members, fill_values)
        )
    )


def shift_next(members, fill_values):
    return tuple(
        (
            jnp.concatenate([m[..., 1:, :], jnp.full_like(m[..., :1, :], f)], axis=-2)
            for m, f in zip(members, fill_values)
        )
    )


def shift_prev(members):
    return tuple(
        (jnp.concatenate([jnp.zeros_like(m[..., :1, :]), m[..., :-1, :]], axis=-2) for m in members)
    )


def pair_split(member):
    shaped = member.reshape(member.shape[:-2] + (member.shape[-2] // 2, 2, member.shape[-1]))
    return (shaped[..., 0, :], shaped[..., 1, :])


def split_parity(members):
    halves = [pair_split(m) for m in members]
    return (tuple((h[0] for h in halves)), tuple((h[1] for h in halves)))


def alternate(first_member, second_member):
    stacked = jnp.stack((first_member, second_member), axis=-2)
    return stacked.reshape(
        first_member.shape[:-2] + (2 * first_member.shape[-2], first_member.shape[-1])
    )


def reduce_blocks(sub_blocks, diag_blocks, super_blocks, right_side):
    block_count = diag_blocks[0].shape[-2]
    if block_count == 1:
        return block_apply(block_inverse(diag_blocks), right_side)
    if block_count % 2 == 1:
        sub_blocks = extend_blocks(sub_blocks, ZERO_BLOCK)
        diag_blocks = extend_blocks(diag_blocks, UNIT_BLOCK)
        super_blocks = extend_blocks(super_blocks, ZERO_BLOCK)
        right_side = extend_blocks(right_side, ZERO_PAIR)
    sub_even, sub_odd = split_parity(sub_blocks)
    diag_even, diag_odd = split_parity(diag_blocks)
    super_even, super_odd = split_parity(super_blocks)
    side_even, side_odd = split_parity(right_side)
    inverse_even = block_inverse(diag_even)
    inverse_next = shift_next(inverse_even, UNIT_BLOCK)
    sub_next = shift_next(sub_even, ZERO_BLOCK)
    super_next = shift_next(super_even, ZERO_BLOCK)
    side_next = shift_next(side_even, ZERO_PAIR)
    left_factor = negate(block_product(sub_odd, inverse_even))
    right_factor = negate(block_product(super_odd, inverse_next))
    reduced_sub = block_product(left_factor, sub_even)
    reduced_diag = add_blocks(
        diag_odd,
        add_blocks(block_product(left_factor, super_even), block_product(right_factor, sub_next)),
    )
    reduced_super = block_product(right_factor, super_next)
    reduced_side = add_blocks(
        side_odd,
        add_blocks(block_apply(left_factor, side_even), block_apply(right_factor, side_next)),
    )
    odd_values = reduce_blocks(reduced_sub, reduced_diag, reduced_super, reduced_side)
    before_values = shift_prev(odd_values)
    remainder = add_blocks(
        side_even,
        negate(
            add_blocks(block_apply(sub_even, before_values), block_apply(super_even, odd_values))
        ),
    )
    even_values = block_apply(inverse_even, remainder)
    merged = tuple((alternate(e, o) for e, o in zip(even_values, odd_values)))
    return tuple((m[..., :block_count, :] for m in merged))


def cells_leading(block):
    moved = jnp.transpose(block, (2, 0, 1, 3))
    return moved.reshape(block.shape[2], block.shape[0] * block.shape[1] * block.shape[3])


def solve_in_lanes(coefficients, line_source):
    source_shape = line_source.shape
    lane_coef = [cells_leading(jnp.broadcast_to(c[:, None], source_shape)) for c in coefficients]
    pairs_list = [pair_split(m) for m in lane_coef]
    zero_plane = jnp.zeros_like(pairs_list[2][0])
    sub_blocks = (pairs_list[0][0], pairs_list[1][0], zero_plane, pairs_list[0][1])
    diag_blocks = (pairs_list[2][0], pairs_list[3][0], pairs_list[1][1], pairs_list[2][1])
    super_blocks = (pairs_list[4][0], zero_plane, pairs_list[3][1], pairs_list[4][1])
    values = reduce_blocks(
        sub_blocks, diag_blocks, super_blocks, pair_split(cells_leading(line_source))
    )
    flat = alternate(values[0], values[1])
    shaped = flat.reshape(source_shape[2], source_shape[0], source_shape[1], source_shape[3])
    return jnp.transpose(shaped, (1, 2, 0, 3))


def return_tiles(line_values):
    return lax.all_to_all(line_values, "cell", split_axis=2, concat_axis=3, tiled=True)


def local_by_lines(state, pseudo_rate, line_next, face_codes):
    local_count = state.shape[0]
    tile_cells = state.shape[2]
    cell_index = lax.axis_index("cell")
    cell_count = lax.axis_size("cell")
    total_cells = tile_cells * cell_count
    spectral = spectral_matrix(NT)
    first_local = lax.axis_index("inst") * local_count
    own_rows = lax.dynamic_slice_in_dim(spectral, first_local, local_count, 0)
    shard_block = jax.tree.map(lambda a: lax.all_gather(a, "inst", axis=0, tiled=True), state)
    columns = lax.slice_in_dim(own_rows, 0, shard_block.shape[0], axis=1)
    time_term = jnp.zeros_like(state) + jnp.einsum(
        "nm,mvil->nvil", columns, shard_block, precision=lax.Precision.HIGHEST
    )
    padded = extended(state, (("cell", 2),), 2)
    codes_lines = jnp.repeat(face_codes, LINES_DEV, axis=1)
    lower_ghost = boundary_cells(state[:, :, 0:2, :], codes_lines[0], True)
    upper_ghost = boundary_cells(state[:, :, -2:, :], codes_lines[1], False)
    lower_rim = jnp.where(cell_index == 0, lower_ghost, padded[:, :, :2, :])
    upper_rim = jnp.where(cell_index == cell_count - 1, upper_ghost, padded[:, :, -2:, :])
    padded = jnp.concatenate([lower_rim, padded[:, :, 2:-2, :], upper_rim], axis=2)
    line_part, radius = line_residual(padded)
    prev_lines = (
        jnp.zeros_like(line_next).at[line_next].set(jnp.arange(line_next.shape[0], dtype=jnp.int32))
    )
    residual = line_part + pitch_residual(state, line_next, prev_lines) + time_term
    right_side = -residual
    centre_radius = radius[:, 2:-2, :]
    diagonal_term = pseudo_rate * centre_radius
    positions = cell_index * tile_cells + jnp.arange(-1, tile_cells + 1, dtype=jnp.int32)
    inside = (positions >= 0) & (positions < total_cells)
    radius_ext = jnp.where(inside[:, None], radius[:, 1:-1, :], 0.0)
    coefficients = line_coefficients(radius_ext, diagonal_term, positions[1:-1], total_cells)
    stacked = jnp.stack(coefficients, axis=1)
    line_source = lax.all_to_all(right_side, "cell", split_axis=3, concat_axis=2, tiled=True)
    line_coef = lax.all_to_all(stacked, "cell", split_axis=3, concat_axis=2, tiled=True)
    update = return_tiles(solve_in_lanes(tuple((line_coef[:, k] for k in range(5))), line_source))
    return state + update


LANES = 128
ROWS = 8
PAIRS = 3
CELL_ROWS = PAIRS * ROWS
RATE_ROW = 2 * CELL_ROWS
VMEM_BYTES = 8 * 2**20
BLOCK_ROWS = RATE_ROW + ROWS

SIDE_ROW = 3 * CELL_ROWS
CORRECTION_ROW = SIDE_ROW + 2 * CELL_ROWS
MIDDLE_ROWS = CORRECTION_ROW + 2 * ROWS
BLOCK_PLANES = 4 + 3 + 2 * PAIRS


def spectral_offsets():
    table = np.zeros(NT)
    for offset in range(1, NT):
        angle = np.pi * offset / NT
        parity = -1.0 if offset % 2 == 0 else 1.0
        table[offset] = 0.5 * OMEGA_BLADE * parity * np.cos(angle) / np.sin(angle)
    return [float(np.float32(value)) for value in table]


def plane_masks():
    row_index = lax.broadcasted_iota(jnp.int32, (ROWS, LANES), 0)
    return row_index < 4, (row_index & 2) == 0, row_index & 1


def both(first_var, plane):
    turned = pltpu.roll(plane, 4, 0)
    return jnp.where(first_var, plane, turned), jnp.where(first_var, turned, plane)


def primitives(first_var, planes):
    density, moment_x = both(first_var, planes[0])
    moment_y, moment_z = both(first_var, planes[1])
    energy = jnp.where(first_var, planes[2], pltpu.roll(planes[2], 4, 0))
    inverse = 1.0 / density
    velocity_x = moment_x * inverse
    velocity_y = moment_y * inverse
    velocity_z = moment_z * inverse
    kinetic = moment_x * velocity_x + moment_y * velocity_y + moment_z * velocity_z
    pressure = (GAMMA_GAS - 1.0) * (energy - 0.5 * kinetic)
    sound = jnp.sqrt(GAMMA_GAS * pressure * inverse)
    return velocity_x, velocity_y, pressure, sound


def rows_of(var, inst, half):
    return (var // 2) * ROWS + (var % 2) * 4 + inst * 2 + half


def pack_kernel(state_ref, rate_ref, out_ref):
    mirrored = lax.axis_index("cell") // (lax.axis_size("cell") // 2)
    for cell in range(2):
        place = pl.multiple_of(jnp.bitwise_xor(cell, mirrored) * CELL_ROWS, ROWS)
        for k in range(PAIRS):
            rows = [
                state_ref[inst, 2 * k + var, pl.ds(cell, 1), pl.ds(half * LANES, LANES)]
                for var in range(2)
                for inst in range(2)
                for half in range(2)
            ]
            for row, values in enumerate(rows):
                out_ref[0, pl.ds(place + (k * ROWS + row), 1), :] = values
    rates = [
        rate_ref[pl.ds(cell, 1), pl.ds(half * LANES, LANES)]
        for cell in range(2)
        for half in range(2)
    ]
    for row in range(4):
        out_ref[0, pl.ds(RATE_ROW + row, 1), :] = jnp.where(
            mirrored == 0, rates[row], rates[row ^ 2]
        )
    out_ref[0, pl.ds(RATE_ROW + 4, 4), :] = jnp.zeros((4, LANES), jnp.float32)
    for row in range(0, BLOCK_ROWS, ROWS):
        values = out_ref[0, pl.ds(row, ROWS), :]
        for copy in range(1, out_ref.shape[0]):
            out_ref[copy, pl.ds(row, ROWS), :] = values


def two_by_two(first, second):
    def entry(a, b, c, d):
        terms = [x * y for x, y in ((a, b), (c, d)) if x is not None and y is not None]
        return None if not terms else terms[0] if len(terms) == 1 else terms[0] + terms[1]

    return (
        entry(first[0], second[0], first[1], second[2]),
        entry(first[0], second[1], first[1], second[3]),
        entry(first[2], second[0], first[3], second[2]),
        entry(first[2], second[1], first[3], second[3]),
    )


def inverse_of(matrix):
    reciprocal = 1.0 / (matrix[0] * matrix[3] - matrix[1] * matrix[2])
    return (
        matrix[3] * reciprocal,
        -(matrix[1] * reciprocal),
        -(matrix[2] * reciprocal),
        matrix[0] * reciprocal,
    )


def less(first, second):
    return tuple(a if b is None else a - b for a, b in zip(first, second))


def minus(members):
    return tuple(None if a is None else -a for a in members)


def matrix_vector(matrix, low, high):
    def row(a, b):
        terms = [x * y for x, y in ((a, low), (b, high)) if x is not None]
        return terms[0] if len(terms) == 1 else terms[0] + terms[1]

    return row(matrix[0], matrix[1]), row(matrix[2], matrix[3])


def apply_matrix(matrix, side):
    parts = [matrix_vector(matrix, side[k], side[PAIRS + k]) for k in range(PAIRS)]
    return [low for low, _ in parts] + [high for _, high in parts]


def difference(first, second):
    return [a - b for a, b in zip(first, second)]


def flux_along(first_var, planes, velocity, pressure, sign):
    normal = sign * velocity
    return [
        planes[0] * normal + jnp.where(first_var, 0.0, sign * pressure),
        planes[1] * normal,
        planes[2] * normal + jnp.where(first_var, pressure * normal, 0.0),
    ]


class LineCells:
    def __init__(self, first_var, sign):
        self.first_var, self.sign = first_var, sign
        self.state, self.pressure, self.radius = {}, {}, {}
        self.flux, self.step, self.sensor = {}, {}, {}

    def add(self, cell, planes, velocity, pressure, sound):
        self.state[cell], self.pressure[cell] = planes, pressure
        self.radius[cell] = jnp.abs(velocity) + sound
        self.flux[cell] = flux_along(self.first_var, planes, velocity, pressure, self.sign)
        if cell - 1 in self.state:
            self.step[cell - 1] = difference(planes, self.state[cell - 1])
        if cell - 2 in self.state:
            twice = 2.0 * self.pressure[cell - 1]
            outer = pressure + self.pressure[cell - 2]
            self.sensor[cell - 1] = jnp.abs(outer - twice) / (outer + twice)

    def face(self, cell):
        second = SENSOR_GAIN * jnp.maximum(self.sensor[cell], self.sensor[cell + 1])
        fourth = jnp.maximum(0.0, FOURTH_GAIN - second)
        face_radius = 0.5 * (self.radius[cell] + self.radius[cell + 1])
        near_weight = face_radius * (second + 2.0 * fourth)
        far_weight = face_radius * fourth
        return [
            0.5 * (self.flux[cell][k] + self.flux[cell + 1][k])
            - (
                near_weight * self.step[cell][k]
                - far_weight * (self.step[cell + 1][k] + self.step[cell - 1][k])
            )
            for k in range(PAIRS)
        ]

    def near(self, cell):
        scale = SECOND_IMPL * 0.5 + 2.0 * FOURTH_IMPL
        return -scale * (self.radius[cell] + self.radius[cell + 1])

    def far(self, cell):
        return FOURTH_IMPL * self.radius[cell]

    def middle(self, cell, rate):
        centre, above = self.radius[cell], self.radius[cell + 1]
        if cell == 0:
            total, weighted = centre + (centre + above), 4.0 * centre + above
        else:
            below = self.radius[cell - 1]
            total = (below + centre) + (centre + above)
            weighted = below + 4.0 * centre + above
        result = SECOND_IMPL * (0.5 * total) + FOURTH_IMPL * weighted
        return result if rate is None else rate * centre + result

    def diagonal(self, cell, rates):
        across = self.near(cell)
        return (self.middle(cell, rates[0]), across, across, self.middle(cell + 1, rates[1]))

    def below(self, cell):
        return (self.far(cell - 1), self.near(cell - 1), None, self.far(cell))

    def above(self, cell):
        return (self.far(cell + 1), None, self.near(cell + 1), self.far(cell + 2))


def rates_at(ref, index, start, first_half):
    rows = [ref[index + (pl.ds(start + k, 1), slice(None))] for k in range(4)]
    return [jnp.where(first_half, rows[2 * k], rows[2 * k + 1]) for k in range(2)]


def half_kernel(
    all_ref, next_ref, codes_ref, middle_ref, blocks_ref, rest_ref, line_ref,
):
    own_inst = lax.axis_index("inst")
    inst_count, blocks = all_ref.shape[:2]
    cells = 2 * blocks
    mirrored = lax.axis_index("cell") // blocks
    sign = (1 - 2 * mirrored).astype(jnp.float32)
    shape = (ROWS, LANES)
    lane_index = lax.broadcasted_iota(jnp.int32, shape, 1)
    first_var, first_inst, half_index = plane_masks()
    first_half = half_index == 0
    zero = jnp.zeros(shape, jnp.float32)

    next_rows = [
        next_ref[pl.ds(half * LANES, LANES)].reshape(1, LANES) for half in range(2)
    ]
    next_line = jnp.where(first_half, next_rows[0], next_rows[1])
    column = lax.broadcasted_iota(jnp.int32, (LANES, LANES), 0)
    prev_halves = []
    for target in range(2):
        total = None
        for source in range(2):
            hits = jnp.where(column + target * LANES == next_rows[source], 1.0, 0.0)
            names = (lane_index + source * LANES).astype(jnp.float32)
            part = lax.dot_general(
                names, hits, (((1,), (1,)), ((), ())), preferred_element_type=jnp.float32
            )
            total = part if total is None else total + part
        prev_halves.append(total)
    prev_line = jnp.where(first_half, prev_halves[0], prev_halves[1]).astype(jnp.int32)

    def picker(lines):
        lane = lines & (LANES - 1)
        same = (lines >> 7) == half_index

        def pick(plane):
            swapped = jnp.where(first_half, pltpu.roll(plane, 7, 0), pltpu.roll(plane, 1, 0))
            here = jnp.take_along_axis(plane, lane, axis=1, mode="promise_in_bounds")
            there = jnp.take_along_axis(swapped, lane, axis=1, mode="promise_in_bounds")
            return jnp.where(same, here, there)

        return pick

    pick_next = picker(next_line)
    pick_prev = picker(prev_line)

    def loaded(cell, inst=own_inst):
        return [
            all_ref[inst, cell // 2, pl.ds((cell % 2) * CELL_ROWS + k * ROWS, ROWS), :]
            for k in range(PAIRS)
        ]

    offsets = spectral_offsets()

    def time_parts(cell):
        pairs = [
            loaded(cell, (own_inst - shift) & (inst_count - 1)) for shift in range(inst_count)
        ]
        result = []
        for k in range(PAIRS):
            same_total, other_total = None, None
            for shift in range(inst_count):
                plane = pairs[shift][k]
                other = jnp.where(
                    first_inst, offsets[(2 * shift + 1) % NT], offsets[(2 * shift - 1) % NT]
                )
                if shift > 0:
                    term = offsets[(2 * shift) % NT] * plane
                    same_total = term if same_total is None else same_total + term
                term = other * plane
                other_total = term if other_total is None else other_total + term
            turned = jnp.where(
                first_inst, pltpu.roll(other_total, 6, 0), pltpu.roll(other_total, 2, 0)
            )
            result.append(same_total + turned)
        return result

    def flux_across(planes, velocity, pressure):
        return [
            planes[0] * velocity,
            planes[1] * velocity + jnp.where(first_var, pressure, 0.0),
            planes[2] * velocity + jnp.where(first_var, pressure * velocity, 0.0),
        ]

    def pitch_flux(planes, velocity_y, pressure, sound):
        nearby = [pick_next(plane) for plane in planes]
        _, next_velocity, next_pressure, next_sound = primitives(first_var, nearby)
        own_flux = flux_across(planes, velocity_y, pressure)
        next_flux = flux_across(nearby, next_velocity, next_pressure)
        weight = (PITCH_GAIN * 0.5) * (
            jnp.abs(velocity_y) + sound + (jnp.abs(next_velocity) + next_sound)
        )
        return [
            0.5 * (a + b) - weight * (n - o)
            for a, b, n, o in zip(own_flux, next_flux, nearby, planes)
        ]

    for cell in range(cells):
        planes = loaded(cell)
        velocity_x, velocity_y, pressure, sound = primitives(first_var, planes)
        line_ref[cell, 0], line_ref[cell, 1], line_ref[cell, 2] = velocity_x, pressure, sound
        faces_across = pitch_flux(planes, velocity_y, pressure, sound)
        times = time_parts(cell)
        for k in range(PAIRS):
            rest_ref[cell, k] = times[k] + (faces_across[k] - pick_prev(faces_across[k]))

    tile = half_index * (LANES // LINES_DEV) + lane_index // LINES_DEV
    end_codes = jnp.where(mirrored == 0, codes_ref[pl.ds(0, 1), :], codes_ref[pl.ds(1, 1), :])
    codes = jnp.zeros(shape, jnp.int32)
    for k in range(2 * LANES // LINES_DEV):
        codes = jnp.where(tile == k, jnp.broadcast_to(end_codes[:, k : k + 1], shape), codes)

    def ghost(cell):
        planes = loaded(-1 - cell)
        copied = loaded(0)
        result = []
        for k in range(PAIRS):
            reflected = planes[k] if k else jnp.where(first_var, planes[k], -planes[k])
            inflow = jnp.where(first_var, FREE_STATE[2 * k], FREE_STATE[2 * k + 1])
            result.append(
                jnp.where(codes == 0, reflected, jnp.where(codes == 1, inflow, copied[k]))
            )
        return result

    line = LineCells(first_var, sign)
    sides, faces, inverses, aboves = [], {}, [], []
    for cell in range(-2, cells):
        if cell < 0:
            planes = ghost(cell)
            velocity_x, _, pressure, sound = primitives(first_var, planes)
        else:
            planes = loaded(cell)
            velocity_x, pressure, sound = [line_ref[cell, k] for k in range(3)]
        line.add(cell, planes, velocity_x, pressure, sound)
        if cell >= 1:
            faces[cell - 2] = line.face(cell - 2)
        if cell >= 3 and cell % 2 == 1:
            at = cell - 3
            block = at // 2
            rates = rates_at(all_ref, (own_inst, block), RATE_ROW, first_half)
            diag = line.diagonal(at, rates)
            side = []
            for member in range(2):
                for k in range(PAIRS):
                    side.append(
                        faces[at + member - 1][k] - faces[at + member][k]
                        - rest_ref[at + member, k]
                    )
            if block > 0:
                factor = two_by_two(line.below(at), inverses[-1])
                diag = less(diag, two_by_two(factor, aboves[-1]))
                side = difference(side, apply_matrix(factor, sides[-1]))
            inverses.append(inverse_of(diag))
            aboves.append(line.above(at))
            sides.append(side)

    last = cells - 2
    factor = two_by_two(line.below(last), inverses[-1])
    correction = list(two_by_two(factor, aboves[-1]))
    rates = rates_at(all_ref, (own_inst, blocks - 1), RATE_ROW, first_half)
    for member in range(2):
        centre = line.radius[last + member]
        correction[3 * member] = correction[3 * member] - rates[member] * centre
    side = [faces[last - 1][k] - rest_ref[last, k] for k in range(PAIRS)]
    side += [-rest_ref[last + 1, k] for k in range(PAIRS)]
    side = difference(side, apply_matrix(factor, sides[-1]))
    for n in range(3):
        for k, plane in enumerate(line.state[cells - 3 + n]):
            middle_ref[pl.ds(n * CELL_ROWS + k * ROWS, ROWS), :] = plane
    for n, plane in enumerate(side):
        middle_ref[pl.ds(SIDE_ROW + n * ROWS, ROWS), :] = plane
    for n in range(2):
        middle_ref[pl.ds(CORRECTION_ROW + n * ROWS, ROWS), :] = jnp.where(
            first_var, correction[2 * n], correction[2 * n + 1]
        )
    for block in range(blocks - 1):
        kept = [*inverses[block], aboves[block][0], *aboves[block][2:], *sides[block]]
        for n, plane in enumerate(kept):
            blocks_ref[block, n] = plane


def spread_kernel(all_ref, blocks_ref, known_ref, spread_ref, table_ref):
    own_inst = lax.axis_index("inst")
    blocks = all_ref.shape[1]
    own_cell = lax.axis_index("cell")
    own_block = jnp.where(own_cell < blocks, own_cell, 2 * blocks - 1 - own_cell)
    zero = jnp.zeros((ROWS, LANES), jnp.float32)
    known, spread = [zero] * (2 * PAIRS), (zero + 1.0, zero, zero, zero + 1.0)
    for block in range(blocks - 1, -1, -1):
        if block < blocks - 1:
            kept = [blocks_ref[block, n] for n in range(BLOCK_PLANES)]
            inverse, above, side = kept[:4], (kept[4], None, kept[5], kept[6]), kept[7:]
            step = two_by_two(inverse, above)
            own = apply_matrix(inverse, side)
            if block < blocks - 2:
                known = difference(own, apply_matrix(step, known))
                spread = minus(two_by_two(step, spread))
            else:
                known, spread = own, minus(step)
        for n, plane in enumerate(known + list(spread)):
            table_ref[block, n] = plane
    for n in range(2 * PAIRS):
        base = all_ref[own_inst, own_block, pl.ds(n * ROWS, ROWS), :]
        known_ref[n] = base + table_ref[own_block, n]
    for n in range(4):
        spread_ref[n] = table_ref[own_block, 2 * PAIRS + n]


def join_kernel(here_ref, there_ref, known_ref, spread_ref, out_ref):
    mirrored = lax.axis_index("cell") // (lax.axis_size("cell") // 2)
    sign = (1 - 2 * mirrored).astype(jnp.float32)
    first_var, _, _ = plane_masks()

    def plane_of(ref, row):
        return ref[pl.ds(row, ROWS), :]

    line = LineCells(first_var, sign)
    for cell in range(6):
        ref, at = (here_ref, cell) if cell < 3 else (there_ref, 5 - cell)
        planes = [plane_of(ref, at * CELL_ROWS + k * ROWS) for k in range(PAIRS)]
        velocity_x, _, pressure, sound = primitives(first_var, planes)
        line.add(cell, planes, velocity_x, pressure, sound)
    faces = {cell: line.face(cell) for cell in (1, 2, 3)}

    def correction_of(ref):
        pairs = [both(first_var, plane_of(ref, CORRECTION_ROW + n * ROWS)) for n in range(2)]
        return [pairs[0][0], pairs[0][1], pairs[1][0], pairs[1][1]]

    here_side = [plane_of(here_ref, SIDE_ROW + n * ROWS) for n in range(2 * PAIRS)]
    there_side = [plane_of(there_ref, SIDE_ROW + n * ROWS) for n in range(2 * PAIRS)]
    side = [here_side[k] - faces[1][k] for k in range(PAIRS)]
    side += [here_side[PAIRS + k] + (faces[1][k] - faces[2][k]) for k in range(PAIRS)]
    other = [there_side[PAIRS + k] + (faces[2][k] - faces[3][k]) for k in range(PAIRS)]
    other += [there_side[k] + faces[3][k] for k in range(PAIRS)]
    no_rates = (None, None)
    diag = difference(line.diagonal(1, no_rates), correction_of(here_ref))
    other_diag = difference(line.diagonal(3, no_rates), correction_of(there_ref)[::-1])
    factor = two_by_two(line.above(1), inverse_of(other_diag))
    diag = less(diag, two_by_two(factor, line.below(3)))
    middle = apply_matrix(inverse_of(diag), difference(side, apply_matrix(factor, other)))
    moved = apply_matrix([spread_ref[n] for n in range(4)], middle)
    results = [known_ref[n] + moved[n] for n in range(2 * PAIRS)]
    for cell in range(2):
        for k in range(PAIRS):
            first, second = results[cell * PAIRS + k], results[(1 - cell) * PAIRS + k]
            result = jnp.where(mirrored == 0, first, second)
            for var in range(2):
                for inst in range(2):
                    for half in range(2):
                        row = rows_of(var, inst, half)
                        out_ref[
                            inst, 2 * k + var, pl.ds(cell, 1), pl.ds(half * LANES, LANES)
                        ] = result[row : row + 1]


def share_half(copies):
    insts, count = lax.axis_size("inst"), lax.axis_size("cell")
    halves = [range(count // 2), range(count - 1, count // 2 - 1, -1)]
    groups = [[inst * count + cell for inst in range(insts) for cell in half] for half in halves]
    return lax.all_to_all(
        copies, ("inst", "cell"), split_axis=0, concat_axis=0, tiled=True,
        axis_index_groups=groups,
    )


def swap_halves(block):
    count = lax.axis_size("cell")
    return lax.ppermute(block, "cell", [(i, (i + count // 2) % count) for i in range(count)])


def float_shape(*sizes):
    return jax.ShapeDtypeStruct(sizes, jnp.float32)


def local_by_halves(state, pseudo_rate, line_next, face_codes):
    blocks = lax.axis_size("cell") // 2
    cells = 2 * blocks
    vmem = pl.BlockSpec(memory_space=pltpu.VMEM)
    plane = (ROWS, LANES)
    params = pltpu.CompilerParams(vmem_limit_bytes=VMEM_BYTES)
    insts = lax.axis_size("inst")
    packed = pl.pallas_call(
        pack_kernel,
        out_shape=float_shape(insts * blocks, BLOCK_ROWS, LANES),
        in_specs=[vmem, vmem],
        out_specs=vmem,
        compiler_params=params,
    )(state, pseudo_rate)
    shared = share_half(packed).reshape(insts, blocks, BLOCK_ROWS, LANES)
    here, eliminated = pl.pallas_call(
        half_kernel,
        out_shape=(
            float_shape(MIDDLE_ROWS, LANES),
            float_shape(blocks - 1, BLOCK_PLANES, *plane),
        ),
        in_specs=[vmem, vmem, vmem],
        out_specs=(vmem, vmem),
        scratch_shapes=[
            pltpu.VMEM((cells, PAIRS) + plane, jnp.float32),
            pltpu.VMEM((cells, 3) + plane, jnp.float32),
        ],
        compiler_params=params,
    )(shared, line_next, face_codes)
    there = swap_halves(here)
    known, spread = pl.pallas_call(
        spread_kernel,
        out_shape=(float_shape(2 * PAIRS, *plane), float_shape(4, *plane)),
        in_specs=[vmem, vmem],
        out_specs=(vmem, vmem),
        scratch_shapes=[pltpu.VMEM((blocks, 2 * PAIRS + 4) + plane, jnp.float32)],
        compiler_params=params,
        cost_estimate=pl.CostEstimate(flops=10**6, bytes_accessed=10**6, transcendentals=0),
    )(shared, eliminated)
    return pl.pallas_call(
        join_kernel,
        out_shape=float_shape(*state.shape),
        in_specs=[vmem] * 4,
        out_specs=vmem,
        compiler_params=params,
    )(here, there, known, spread)


def solution(mesh):
    placed = (P("inst", None, "cell", None), P("cell", None), P(), P())
    inst_count, cell_count = mesh.shape["inst"], mesh.shape["cell"]

    def local(state, pseudo_rate, line_next, face_codes):
        small = (
            state.shape == (2, 6, 2, 2 * LANES)
            and inst_count * 2 == NT
            and cell_count == 8
            and face_codes.shape[1] * LINES_DEV == state.shape[3]
        )
        chosen = local_by_halves if small else local_by_lines
        return chosen(state, pseudo_rate, line_next, face_codes)

    return jax.shard_map(
        local, mesh=mesh, in_specs=placed, out_specs=P("inst", None, "cell", None), check_vma=False
    )
```

```python
import functools

import jax
import jax.numpy as jnp
import numpy as np
from jax import lax
from jax.experimental import pallas as pl
from jax.experimental.pallas import tpu as pltpu
from jax.sharding import PartitionSpec as P

NT = 8
LINES_DEV = 32


GAMMA_GAS = 1.4
OMEGA_BLADE = 1.0
SENSOR_GAIN = 0.25
FOURTH_GAIN = 0.03125
PITCH_GAIN = 0.5
SECOND_IMPL = 1.0
FOURTH_IMPL = 0.25
FREE_STATE = (1.0, 0.5, 0.0, 0.0, 2.625, 0.2)
MIRROR_SIGNS = (1.0, -1.0, 1.0, 1.0, 1.0, 1.0)
ZERO_BLOCK = (0.0, 0.0, 0.0, 0.0)
UNIT_BLOCK = (1.0, 0.0, 0.0, 1.0)
ZERO_PAIR = (0.0, 0.0)


def extended(block, sides, width):
    for axis, dim in sides:
        count = lax.axis_size(axis)
        forward = [(i, i + 1) for i in range(count - 1)]
        backward = [(target, source) for source, target in forward]
        low = lax.ppermute(
            lax.slice_in_dim(block, block.shape[dim] - width, None, axis=dim), axis, forward
        )
        high = lax.ppermute(lax.slice_in_dim(block, 0, width, axis=dim), axis, backward)
        block = jnp.concatenate([low, block, high], axis=dim)
    return block


def spectral_matrix(instances):
    offsets = np.arange(instances)[:, None] - np.arange(instances)[None, :]
    angles = np.pi * offsets / instances
    safe_sin = np.where(offsets == 0, 1.0, np.sin(angles))
    parity = np.where(np.mod(offsets, 2) == 0, -1.0, 1.0)
    matrix_table = np.where(
        offsets == 0, 0.0, 0.5 * OMEGA_BLADE * parity * np.cos(angles) / safe_sin
    )
    return jnp.asarray(matrix_table, jnp.float32)


def primitive_parts(cells_state):
    density = cells_state[..., 0, :, :]
    inverse = 1.0 / density
    velocity_x = cells_state[..., 1, :, :] * inverse
    velocity_y = cells_state[..., 2, :, :] * inverse
    velocity_z = cells_state[..., 3, :, :] * inverse
    energy = cells_state[..., 4, :, :]
    pressure = (GAMMA_GAS - 1.0) * (
        energy
        - 0.5
        * density
        * (velocity_x * velocity_x + velocity_y * velocity_y + velocity_z * velocity_z)
    )
    sound_speed = jnp.sqrt(GAMMA_GAS * pressure * inverse)
    return (velocity_x, velocity_y, pressure, sound_speed)


def directed_flux(cells_state, normal_velocity, pressure, component):
    zero_plane = jnp.zeros_like(pressure)
    pressure_rows = [
        zero_plane,
        zero_plane,
        zero_plane,
        zero_plane,
        pressure * normal_velocity,
        zero_plane,
    ]
    pressure_rows[component] = pressure
    return cells_state * normal_velocity[..., None, :, :] + jnp.stack(pressure_rows, axis=-3)


def line_residual(padded):
    velocity_x, velocity_y, pressure, sound_speed = primitive_parts(padded)
    flux_line = directed_flux(padded, velocity_x, pressure, 1)
    radius = jnp.abs(velocity_x) + sound_speed
    sensor = jnp.abs(
        pressure[..., 2:, :] - 2.0 * pressure[..., 1:-1, :] + pressure[..., :-2, :]
    ) / (pressure[..., 2:, :] + 2.0 * pressure[..., 1:-1, :] + pressure[..., :-2, :])
    second = SENSOR_GAIN * jnp.maximum(sensor[..., :-1, :], sensor[..., 1:, :])
    fourth = jnp.maximum(0.0, FOURTH_GAIN - second)
    face_radius = 0.5 * (radius[..., 1:-2, :] + radius[..., 2:-1, :])
    left_far = padded[..., :-3, :]
    left_near = padded[..., 1:-2, :]
    right_near = padded[..., 2:-1, :]
    right_far = padded[..., 3:, :]
    damping = face_radius[..., None, :, :] * (
        second[..., None, :, :] * (right_near - left_near)
        - fourth[..., None, :, :] * (right_far - 3.0 * right_near + 3.0 * left_near - left_far)
    )
    face_flux = 0.5 * (flux_line[..., 1:-2, :] + flux_line[..., 2:-1, :]) - damping
    return (face_flux[..., 1:, :] - face_flux[..., :-1, :], radius)


def pitch_parts(cells_state):
    velocity_x, velocity_y, pressure, sound_speed = primitive_parts(cells_state)
    return (directed_flux(cells_state, velocity_y, pressure, 2), jnp.abs(velocity_y) + sound_speed)


def pitch_residual(cells_state, next_lines, prev_lines):
    pitch_flux, radius = pitch_parts(cells_state)
    state_next = jnp.take(cells_state, next_lines, axis=-1)
    flux_next, radius_next = pitch_parts(state_next)
    face_flux = 0.5 * (pitch_flux + flux_next) - PITCH_GAIN * (0.5 * (radius + radius_next))[
        ..., None, :, :
    ] * (state_next - cells_state)
    return face_flux - jnp.take(face_flux, prev_lines, axis=-1)


def boundary_cells(edge_pair, line_codes, lower_end):
    reflected = edge_pair[..., ::-1, :] * jnp.asarray(MIRROR_SIGNS, jnp.float32)[:, None, None]
    if lower_end:
        copied = jnp.concatenate([edge_pair[..., :1, :], edge_pair[..., :1, :]], axis=-2)
    else:
        copied = jnp.concatenate([edge_pair[..., 1:, :], edge_pair[..., 1:, :]], axis=-2)
    inflow = jnp.asarray(FREE_STATE, jnp.float32)[:, None, None] + jnp.zeros_like(edge_pair)
    return jnp.where(line_codes == 0, reflected, jnp.where(line_codes == 1, inflow, copied))


def line_coefficients(radius_ext, diagonal_term, positions, total_cells):
    radius_below = radius_ext[..., :-2, :]
    radius_centre = radius_ext[..., 1:-1, :]
    radius_above = radius_ext[..., 2:, :]
    face_below = 0.5 * (radius_below + radius_centre)
    face_above = 0.5 * (radius_centre + radius_above)
    far_low = FOURTH_IMPL * radius_below
    near_low = -SECOND_IMPL * face_below - 2.0 * FOURTH_IMPL * (radius_below + radius_centre)
    middle = (
        diagonal_term
        + SECOND_IMPL * (face_below + face_above)
        + FOURTH_IMPL * (radius_below + 4.0 * radius_centre + radius_above)
    )
    near_high = -SECOND_IMPL * face_above - 2.0 * FOURTH_IMPL * (radius_centre + radius_above)
    far_high = FOURTH_IMPL * radius_above
    column = positions[:, None]
    far_low = jnp.where(column >= 2, far_low, 0.0)
    near_low = jnp.where(column >= 1, near_low, 0.0)
    near_high = jnp.where(column <= total_cells - 2, near_high, 0.0)
    far_high = jnp.where(column <= total_cells - 3, far_high, 0.0)
    return (far_low, near_low, middle, near_high, far_high)


def block_product(first_matrix, second_matrix):
    return (
        first_matrix[0] * second_matrix[0] + first_matrix[1] * second_matrix[2],
        first_matrix[0] * second_matrix[1] + first_matrix[1] * second_matrix[3],
        first_matrix[2] * second_matrix[0] + first_matrix[3] * second_matrix[2],
        first_matrix[2] * second_matrix[1] + first_matrix[3] * second_matrix[3],
    )


def block_inverse(matrix):
    determinant = matrix[0] * matrix[3] - matrix[1] * matrix[2]
    reciprocal = 1.0 / determinant
    return (
        matrix[3] * reciprocal,
        -matrix[1] * reciprocal,
        -matrix[2] * reciprocal,
        matrix[0] * reciprocal,
    )


def block_apply(matrix, vector):
    return (
        matrix[0] * vector[0] + matrix[1] * vector[1],
        matrix[2] * vector[0] + matrix[3] * vector[1],
    )


def add_blocks(first_members, second_members):
    return tuple((a + b for a, b in zip(first_members, second_members)))


def negate(members):
    return tuple((-a for a in members))


def extend_blocks(members, fill_values):
    return tuple(
        (
            jnp.concatenate([m, jnp.full_like(m[..., :1, :], f)], axis=-2)
            for m, f in zip(members, fill_values)
        )
    )


def shift_next(members, fill_values):
    return tuple(
        (
            jnp.concatenate([m[..., 1:, :], jnp.full_like(m[..., :1, :], f)], axis=-2)
            for m, f in zip(members, fill_values)
        )
    )


def shift_prev(members):
    return tuple(
        (jnp.concatenate([jnp.zeros_like(m[..., :1, :]), m[..., :-1, :]], axis=-2) for m in members)
    )


def pair_split(member):
    shaped = member.reshape(member.shape[:-2] + (member.shape[-2] // 2, 2, member.shape[-1]))
    return (shaped[..., 0, :], shaped[..., 1, :])


def split_parity(members):
    halves = [pair_split(m) for m in members]
    return (tuple((h[0] for h in halves)), tuple((h[1] for h in halves)))


def alternate(first_member, second_member):
    stacked = jnp.stack((first_member, second_member), axis=-2)
    return stacked.reshape(
        first_member.shape[:-2] + (2 * first_member.shape[-2], first_member.shape[-1])
    )


def reduce_blocks(sub_blocks, diag_blocks, super_blocks, right_side):
    block_count = diag_blocks[0].shape[-2]
    if block_count == 1:
        return block_apply(block_inverse(diag_blocks), right_side)
    if block_count % 2 == 1:
        sub_blocks = extend_blocks(sub_blocks, ZERO_BLOCK)
        diag_blocks = extend_blocks(diag_blocks, UNIT_BLOCK)
        super_blocks = extend_blocks(super_blocks, ZERO_BLOCK)
        right_side = extend_blocks(right_side, ZERO_PAIR)
    sub_even, sub_odd = split_parity(sub_blocks)
    diag_even, diag_odd = split_parity(diag_blocks)
    super_even, super_odd = split_parity(super_blocks)
    side_even, side_odd = split_parity(right_side)
    inverse_even = block_inverse(diag_even)
    inverse_next = shift_next(inverse_even, UNIT_BLOCK)
    sub_next = shift_next(sub_even, ZERO_BLOCK)
    super_next = shift_next(super_even, ZERO_BLOCK)
    side_next = shift_next(side_even, ZERO_PAIR)
    left_factor = negate(block_product(sub_odd, inverse_even))
    right_factor = negate(block_product(super_odd, inverse_next))
    reduced_sub = block_product(left_factor, sub_even)
    reduced_diag = add_blocks(
        diag_odd,
        add_blocks(block_product(left_factor, super_even), block_product(right_factor, sub_next)),
    )
    reduced_super = block_product(right_factor, super_next)
    reduced_side = add_blocks(
        side_odd,
        add_blocks(block_apply(left_factor, side_even), block_apply(right_factor, side_next)),
    )
    odd_values = reduce_blocks(reduced_sub, reduced_diag, reduced_super, reduced_side)
    before_values = shift_prev(odd_values)
    remainder = add_blocks(
        side_even,
        negate(
            add_blocks(block_apply(sub_even, before_values), block_apply(super_even, odd_values))
        ),
    )
    even_values = block_apply(inverse_even, remainder)
    merged = tuple((alternate(e, o) for e, o in zip(even_values, odd_values)))
    return tuple((m[..., :block_count, :] for m in merged))


def cells_leading(block):
    moved = jnp.transpose(block, (2, 0, 1, 3))
    return moved.reshape(block.shape[2], block.shape[0] * block.shape[1] * block.shape[3])


def solve_in_lanes(coefficients, line_source):
    source_shape = line_source.shape
    lane_coef = [cells_leading(jnp.broadcast_to(c[:, None], source_shape)) for c in coefficients]
    pairs_list = [pair_split(m) for m in lane_coef]
    zero_plane = jnp.zeros_like(pairs_list[2][0])
    sub_blocks = (pairs_list[0][0], pairs_list[1][0], zero_plane, pairs_list[0][1])
    diag_blocks = (pairs_list[2][0], pairs_list[3][0], pairs_list[1][1], pairs_list[2][1])
    super_blocks = (pairs_list[4][0], zero_plane, pairs_list[3][1], pairs_list[4][1])
    values = reduce_blocks(
        sub_blocks, diag_blocks, super_blocks, pair_split(cells_leading(line_source))
    )
    flat = alternate(values[0], values[1])
    shaped = flat.reshape(source_shape[2], source_shape[0], source_shape[1], source_shape[3])
    return jnp.transpose(shaped, (1, 2, 0, 3))


def return_tiles(line_values):
    return lax.all_to_all(line_values, "cell", split_axis=2, concat_axis=3, tiled=True)


def local_by_lines(state, pseudo_rate, line_next, face_codes):
    local_count = state.shape[0]
    tile_cells = state.shape[2]
    cell_index = lax.axis_index("cell")
    cell_count = lax.axis_size("cell")
    total_cells = tile_cells * cell_count
    spectral = spectral_matrix(NT)
    first_local = lax.axis_index("inst") * local_count
    own_rows = lax.dynamic_slice_in_dim(spectral, first_local, local_count, 0)
    shard_block = jax.tree.map(lambda a: lax.all_gather(a, "inst", axis=0, tiled=True), state)
    columns = lax.slice_in_dim(own_rows, 0, shard_block.shape[0], axis=1)
    time_term = jnp.zeros_like(state) + jnp.einsum(
        "nm,mvil->nvil", columns, shard_block, precision=lax.Precision.HIGHEST
    )
    padded = extended(state, (("cell", 2),), 2)
    codes_lines = jnp.repeat(face_codes, LINES_DEV, axis=1)
    lower_ghost = boundary_cells(state[:, :, 0:2, :], codes_lines[0], True)
    upper_ghost = boundary_cells(state[:, :, -2:, :], codes_lines[1], False)
    lower_rim = jnp.where(cell_index == 0, lower_ghost, padded[:, :, :2, :])
    upper_rim = jnp.where(cell_index == cell_count - 1, upper_ghost, padded[:, :, -2:, :])
    padded = jnp.concatenate([lower_rim, padded[:, :, 2:-2, :], upper_rim], axis=2)
    line_part, radius = line_residual(padded)
    prev_lines = (
        jnp.zeros_like(line_next).at[line_next].set(jnp.arange(line_next.shape[0], dtype=jnp.int32))
    )
    residual = line_part + pitch_residual(state, line_next, prev_lines) + time_term
    right_side = -residual
    centre_radius = radius[:, 2:-2, :]
    diagonal_term = pseudo_rate * centre_radius
    positions = cell_index * tile_cells + jnp.arange(-1, tile_cells + 1, dtype=jnp.int32)
    inside = (positions >= 0) & (positions < total_cells)
    radius_ext = jnp.where(inside[:, None], radius[:, 1:-1, :], 0.0)
    coefficients = line_coefficients(radius_ext, diagonal_term, positions[1:-1], total_cells)
    stacked = jnp.stack(coefficients, axis=1)
    line_source = lax.all_to_all(right_side, "cell", split_axis=3, concat_axis=2, tiled=True)
    line_coef = lax.all_to_all(stacked, "cell", split_axis=3, concat_axis=2, tiled=True)
    update = return_tiles(solve_in_lanes(tuple((line_coef[:, k] for k in range(5))), line_source))
    return state + update


LANES = 128
ROWS = 8
PAIRS = 3
CELL_ROWS = PAIRS * ROWS
RATE_ROW = 2 * CELL_ROWS
VMEM_BYTES = 8 * 2**20
BLOCK_ROWS = RATE_ROW + ROWS

SIDE_ROW = 3 * CELL_ROWS
CORRECTION_ROW = SIDE_ROW + 2 * CELL_ROWS
MIDDLE_ROWS = CORRECTION_ROW + 2 * ROWS
BLOCK_PLANES = 4 + 3 + 2 * PAIRS


def spectral_offsets():
    table = np.zeros(NT)
    for offset in range(1, NT):
        angle = np.pi * offset / NT
        parity = -1.0 if offset % 2 == 0 else 1.0
        table[offset] = 0.5 * OMEGA_BLADE * parity * np.cos(angle) / np.sin(angle)
    return [float(np.float32(value)) for value in table]


def plane_masks():
    row_index = lax.broadcasted_iota(jnp.int32, (ROWS, LANES), 0)
    return row_index < 4, (row_index & 2) == 0, row_index & 1


def both(first_var, plane):
    turned = pltpu.roll(plane, 4, 0)
    return jnp.where(first_var, plane, turned), jnp.where(first_var, turned, plane)


def primitives(first_var, planes):
    density, moment_x = both(first_var, planes[0])
    moment_y, moment_z = both(first_var, planes[1])
    energy = jnp.where(first_var, planes[2], pltpu.roll(planes[2], 4, 0))
    inverse = 1.0 / density
    velocity_x = moment_x * inverse
    velocity_y = moment_y * inverse
    velocity_z = moment_z * inverse
    kinetic = moment_x * velocity_x + moment_y * velocity_y + moment_z * velocity_z
    pressure = (GAMMA_GAS - 1.0) * (energy - 0.5 * kinetic)
    sound = jnp.sqrt(GAMMA_GAS * pressure * inverse)
    return velocity_x, velocity_y, pressure, sound


def rows_of(var, inst, half):
    return (var // 2) * ROWS + (var % 2) * 4 + inst * 2 + half


def pack_kernel(
    held_state_ref, held_rate_ref, held_next_ref, held_codes_ref, out_ref, next_ref, codes_ref,
    state_ref, rate_ref, sems,
):
    copies = [
        pltpu.make_async_copy(source, target, sems.at[k])
        for k, (source, target) in enumerate(
            (
                (held_state_ref, state_ref),
                (held_rate_ref, rate_ref),
                (held_next_ref, next_ref),
                (held_codes_ref, codes_ref),
            )
        )
    ]
    for copy in copies:
        copy.start()
    for copy in copies:
        copy.wait()
    mirrored = lax.axis_index("cell") // (lax.axis_size("cell") // 2)
    for cell in range(2):
        place = pl.multiple_of(jnp.bitwise_xor(cell, mirrored) * CELL_ROWS, ROWS)
        for k in range(PAIRS):
            rows = [
                state_ref[inst, 2 * k + var, pl.ds(cell, 1), pl.ds(half * LANES, LANES)]
                for var in range(2)
                for inst in range(2)
                for half in range(2)
            ]
            for row, values in enumerate(rows):
                out_ref[0, pl.ds(place + (k * ROWS + row), 1), :] = values
    rates = [
        rate_ref[pl.ds(cell, 1), pl.ds(half * LANES, LANES)]
        for cell in range(2)
        for half in range(2)
    ]
    for row in range(4):
        out_ref[0, pl.ds(RATE_ROW + row, 1), :] = jnp.where(
            mirrored == 0, rates[row], rates[row ^ 2]
        )
    out_ref[0, pl.ds(RATE_ROW + 4, 4), :] = jnp.zeros((4, LANES), jnp.float32)
    for row in range(0, BLOCK_ROWS, ROWS):
        values = out_ref[0, pl.ds(row, ROWS), :]
        for copy in range(1, out_ref.shape[0]):
            out_ref[copy, pl.ds(row, ROWS), :] = values


def two_by_two(first, second):
    def entry(a, b, c, d):
        terms = [x * y for x, y in ((a, b), (c, d)) if x is not None and y is not None]
        return None if not terms else terms[0] if len(terms) == 1 else terms[0] + terms[1]

    return (
        entry(first[0], second[0], first[1], second[2]),
        entry(first[0], second[1], first[1], second[3]),
        entry(first[2], second[0], first[3], second[2]),
        entry(first[2], second[1], first[3], second[3]),
    )


def inverse_of(matrix):
    reciprocal = 1.0 / (matrix[0] * matrix[3] - matrix[1] * matrix[2])
    return (
        matrix[3] * reciprocal,
        -(matrix[1] * reciprocal),
        -(matrix[2] * reciprocal),
        matrix[0] * reciprocal,
    )


def less(first, second):
    return tuple(a if b is None else a - b for a, b in zip(first, second))


def minus(members):
    return tuple(None if a is None else -a for a in members)


def matrix_vector(matrix, low, high):
    def row(a, b):
        terms = [x * y for x, y in ((a, low), (b, high)) if x is not None]
        return terms[0] if len(terms) == 1 else terms[0] + terms[1]

    return row(matrix[0], matrix[1]), row(matrix[2], matrix[3])


def apply_matrix(matrix, side):
    parts = [matrix_vector(matrix, side[k], side[PAIRS + k]) for k in range(PAIRS)]
    return [low for low, _ in parts] + [high for _, high in parts]


def difference(first, second):
    return [a - b for a, b in zip(first, second)]


def flux_along(first_var, planes, velocity, pressure, sign):
    normal = sign * velocity
    return [
        planes[0] * normal + jnp.where(first_var, 0.0, sign * pressure),
        planes[1] * normal,
        planes[2] * normal + jnp.where(first_var, pressure * normal, 0.0),
    ]


class LineCells:
    def __init__(self, first_var, sign):
        self.first_var, self.sign = first_var, sign
        self.state, self.pressure, self.radius = {}, {}, {}
        self.flux, self.step, self.sensor = {}, {}, {}

    def add(self, cell, planes, velocity, pressure, sound):
        self.state[cell], self.pressure[cell] = planes, pressure
        self.radius[cell] = jnp.abs(velocity) + sound
        self.flux[cell] = flux_along(self.first_var, planes, velocity, pressure, self.sign)
        if cell - 1 in self.state:
            self.step[cell - 1] = difference(planes, self.state[cell - 1])
        if cell - 2 in self.state:
            twice = 2.0 * self.pressure[cell - 1]
            outer = pressure + self.pressure[cell - 2]
            self.sensor[cell - 1] = jnp.abs(outer - twice) / (outer + twice)

    def face(self, cell):
        second = SENSOR_GAIN * jnp.maximum(self.sensor[cell], self.sensor[cell + 1])
        fourth = jnp.maximum(0.0, FOURTH_GAIN - second)
        face_radius = 0.5 * (self.radius[cell] + self.radius[cell + 1])
        near_weight = face_radius * (second + 2.0 * fourth)
        far_weight = face_radius * fourth
        return [
            0.5 * (self.flux[cell][k] + self.flux[cell + 1][k])
            - (
                near_weight * self.step[cell][k]
                - far_weight * (self.step[cell + 1][k] + self.step[cell - 1][k])
            )
            for k in range(PAIRS)
        ]

    def near(self, cell):
        scale = SECOND_IMPL * 0.5 + 2.0 * FOURTH_IMPL
        return -scale * (self.radius[cell] + self.radius[cell + 1])

    def far(self, cell):
        return FOURTH_IMPL * self.radius[cell]

    def middle(self, cell, rate):
        centre, above = self.radius[cell], self.radius[cell + 1]
        if cell == 0:
            total, weighted = centre + (centre + above), 4.0 * centre + above
        else:
            below = self.radius[cell - 1]
            total = (below + centre) + (centre + above)
            weighted = below + 4.0 * centre + above
        result = SECOND_IMPL * (0.5 * total) + FOURTH_IMPL * weighted
        return result if rate is None else rate * centre + result

    def diagonal(self, cell, rates):
        across = self.near(cell)
        return (self.middle(cell, rates[0]), across, across, self.middle(cell + 1, rates[1]))

    def below(self, cell):
        return (self.far(cell - 1), self.near(cell - 1), None, self.far(cell))

    def above(self, cell):
        return (self.far(cell + 1), None, self.near(cell + 1), self.far(cell + 2))


def rates_at(ref, index, start, first_half):
    rows = [ref[index + (pl.ds(start + k, 1), slice(None))] for k in range(4)]
    return [jnp.where(first_half, rows[2 * k], rows[2 * k + 1]) for k in range(2)]


def half_kernel(
    all_ref, next_ref, codes_ref, middle_ref, blocks_ref, rest_ref, line_ref,
):
    own_inst = lax.axis_index("inst")
    inst_count, blocks = all_ref.shape[:2]
    cells = 2 * blocks
    mirrored = lax.axis_index("cell") // blocks
    sign = (1 - 2 * mirrored).astype(jnp.float32)
    shape = (ROWS, LANES)
    lane_index = lax.broadcasted_iota(jnp.int32, shape, 1)
    first_var, first_inst, half_index = plane_masks()
    first_half = half_index == 0
    zero = jnp.zeros(shape, jnp.float32)

    next_rows = [
        next_ref[pl.ds(half * LANES, LANES)].reshape(1, LANES) for half in range(2)
    ]
    next_line = jnp.where(first_half, next_rows[0], next_rows[1])
    column = lax.broadcasted_iota(jnp.int32, (LANES, LANES), 0)
    prev_halves = []
    for target in range(2):
        total = None
        for source in range(2):
            hits = jnp.where(column + target * LANES == next_rows[source], 1.0, 0.0)
            names = (lane_index + source * LANES).astype(jnp.float32)
            part = lax.dot_general(
                names, hits, (((1,), (1,)), ((), ())), preferred_element_type=jnp.float32
            )
            total = part if total is None else total + part
        prev_halves.append(total)
    prev_line = jnp.where(first_half, prev_halves[0], prev_halves[1]).astype(jnp.int32)

    def picker(lines):
        lane = lines & (LANES - 1)
        same = (lines >> 7) == half_index

        def pick(plane):
            swapped = jnp.where(first_half, pltpu.roll(plane, 7, 0), pltpu.roll(plane, 1, 0))
            here = jnp.take_along_axis(plane, lane, axis=1, mode="promise_in_bounds")
            there = jnp.take_along_axis(swapped, lane, axis=1, mode="promise_in_bounds")
            return jnp.where(same, here, there)

        return pick

    pick_next = picker(next_line)
    pick_prev = picker(prev_line)

    def loaded(cell, inst=own_inst):
        return [
            all_ref[inst, cell // 2, pl.ds((cell % 2) * CELL_ROWS + k * ROWS, ROWS), :]
            for k in range(PAIRS)
        ]

    offsets = spectral_offsets()

    def time_parts(cell):
        pairs = [
            loaded(cell, (own_inst - shift) & (inst_count - 1)) for shift in range(inst_count)
        ]
        result = []
        for k in range(PAIRS):
            same_total, other_total = None, None
            for shift in range(inst_count):
                plane = pairs[shift][k]
                other = jnp.where(
                    first_inst, offsets[(2 * shift + 1) % NT], offsets[(2 * shift - 1) % NT]
                )
                if shift > 0:
                    term = offsets[(2 * shift) % NT] * plane
                    same_total = term if same_total is None else same_total + term
                term = other * plane
                other_total = term if other_total is None else other_total + term
            turned = jnp.where(
                first_inst, pltpu.roll(other_total, 6, 0), pltpu.roll(other_total, 2, 0)
            )
            result.append(same_total + turned)
        return result

    def flux_across(planes, velocity, pressure):
        return [
            planes[0] * velocity,
            planes[1] * velocity + jnp.where(first_var, pressure, 0.0),
            planes[2] * velocity + jnp.where(first_var, pressure * velocity, 0.0),
        ]

    def pitch_flux(planes, velocity_y, pressure, sound):
        nearby = [pick_next(plane) for plane in planes]
        _, next_velocity, next_pressure, next_sound = primitives(first_var, nearby)
        own_flux = flux_across(planes, velocity_y, pressure)
        next_flux = flux_across(nearby, next_velocity, next_pressure)
        weight = (PITCH_GAIN * 0.5) * (
            jnp.abs(velocity_y) + sound + (jnp.abs(next_velocity) + next_sound)
        )
        return [
            0.5 * (a + b) - weight * (n - o)
            for a, b, n, o in zip(own_flux, next_flux, nearby, planes)
        ]

    for cell in range(cells):
        planes = loaded(cell)
        velocity_x, velocity_y, pressure, sound = primitives(first_var, planes)
        line_ref[cell, 0], line_ref[cell, 1], line_ref[cell, 2] = velocity_x, pressure, sound
        faces_across = pitch_flux(planes, velocity_y, pressure, sound)
        times = time_parts(cell)
        for k in range(PAIRS):
            rest_ref[cell, k] = times[k] + (faces_across[k] - pick_prev(faces_across[k]))

    tile = half_index * (LANES // LINES_DEV) + lane_index // LINES_DEV
    end_codes = jnp.where(mirrored == 0, codes_ref[pl.ds(0, 1), :], codes_ref[pl.ds(1, 1), :])
    codes = jnp.zeros(shape, jnp.int32)
    for k in range(2 * LANES // LINES_DEV):
        codes = jnp.where(tile == k, jnp.broadcast_to(end_codes[:, k : k + 1], shape), codes)

    def ghost(cell):
        planes = loaded(-1 - cell)
        copied = loaded(0)
        result = []
        for k in range(PAIRS):
            reflected = planes[k] if k else jnp.where(first_var, planes[k], -planes[k])
            inflow = jnp.where(first_var, FREE_STATE[2 * k], FREE_STATE[2 * k + 1])
            result.append(
                jnp.where(codes == 0, reflected, jnp.where(codes == 1, inflow, copied[k]))
            )
        return result

    line = LineCells(first_var, sign)
    sides, faces, inverses, aboves = [], {}, [], []
    for cell in range(-2, cells):
        if cell < 0:
            planes = ghost(cell)
            velocity_x, _, pressure, sound = primitives(first_var, planes)
        else:
            planes = loaded(cell)
            velocity_x, pressure, sound = [line_ref[cell, k] for k in range(3)]
        line.add(cell, planes, velocity_x, pressure, sound)
        if cell >= 1:
            faces[cell - 2] = line.face(cell - 2)
        if cell >= 3 and cell % 2 == 1:
            at = cell - 3
            block = at // 2
            rates = rates_at(all_ref, (own_inst, block), RATE_ROW, first_half)
            diag = line.diagonal(at, rates)
            side = []
            for member in range(2):
                for k in range(PAIRS):
                    side.append(
                        faces[at + member - 1][k] - faces[at + member][k]
                        - rest_ref[at + member, k]
                    )
            if block > 0:
                factor = two_by_two(line.below(at), inverses[-1])
                diag = less(diag, two_by_two(factor, aboves[-1]))
                side = difference(side, apply_matrix(factor, sides[-1]))
            inverses.append(inverse_of(diag))
            aboves.append(line.above(at))
            sides.append(side)

    last = cells - 2
    factor = two_by_two(line.below(last), inverses[-1])
    correction = list(two_by_two(factor, aboves[-1]))
    rates = rates_at(all_ref, (own_inst, blocks - 1), RATE_ROW, first_half)
    for member in range(2):
        centre = line.radius[last + member]
        correction[3 * member] = correction[3 * member] - rates[member] * centre
    side = [faces[last - 1][k] - rest_ref[last, k] for k in range(PAIRS)]
    side += [-rest_ref[last + 1, k] for k in range(PAIRS)]
    side = difference(side, apply_matrix(factor, sides[-1]))
    for n in range(3):
        for k, plane in enumerate(line.state[cells - 3 + n]):
            middle_ref[pl.ds(n * CELL_ROWS + k * ROWS, ROWS), :] = plane
    for n, plane in enumerate(side):
        middle_ref[pl.ds(SIDE_ROW + n * ROWS, ROWS), :] = plane
    for n in range(2):
        middle_ref[pl.ds(CORRECTION_ROW + n * ROWS, ROWS), :] = jnp.where(
            first_var, correction[2 * n], correction[2 * n + 1]
        )
    for block in range(blocks - 1):
        kept = [*inverses[block], aboves[block][0], *aboves[block][2:], *sides[block]]
        for n, plane in enumerate(kept):
            blocks_ref[block, n] = plane


def spread_kernel(all_ref, blocks_ref, known_ref, spread_ref, table_ref):
    own_inst = lax.axis_index("inst")
    blocks = all_ref.shape[1]
    own_cell = lax.axis_index("cell")
    own_block = jnp.where(own_cell < blocks, own_cell, 2 * blocks - 1 - own_cell)
    zero = jnp.zeros((ROWS, LANES), jnp.float32)
    known, spread = [zero] * (2 * PAIRS), (zero + 1.0, zero, zero, zero + 1.0)
    for block in range(blocks - 1, -1, -1):
        if block < blocks - 1:
            kept = [blocks_ref[block, n] for n in range(BLOCK_PLANES)]
            inverse, above, side = kept[:4], (kept[4], None, kept[5], kept[6]), kept[7:]
            step = two_by_two(inverse, above)
            own = apply_matrix(inverse, side)
            if block < blocks - 2:
                known = difference(own, apply_matrix(step, known))
                spread = minus(two_by_two(step, spread))
            else:
                known, spread = own, minus(step)
        for n, plane in enumerate(known + list(spread)):
            table_ref[block, n] = plane
    for n in range(2 * PAIRS):
        base = all_ref[own_inst, own_block, pl.ds(n * ROWS, ROWS), :]
        known_ref[n] = base + table_ref[own_block, n]
    for n in range(4):
        spread_ref[n] = table_ref[own_block, 2 * PAIRS + n]


def join_kernel(here_ref, there_ref, known_ref, spread_ref, out_ref):
    mirrored = lax.axis_index("cell") // (lax.axis_size("cell") // 2)
    sign = (1 - 2 * mirrored).astype(jnp.float32)
    first_var, _, _ = plane_masks()

    def plane_of(ref, row):
        return ref[pl.ds(row, ROWS), :]

    line = LineCells(first_var, sign)
    for cell in range(6):
        ref, at = (here_ref, cell) if cell < 3 else (there_ref, 5 - cell)
        planes = [plane_of(ref, at * CELL_ROWS + k * ROWS) for k in range(PAIRS)]
        velocity_x, _, pressure, sound = primitives(first_var, planes)
        line.add(cell, planes, velocity_x, pressure, sound)
    faces = {cell: line.face(cell) for cell in (1, 2, 3)}

    def correction_of(ref):
        pairs = [both(first_var, plane_of(ref, CORRECTION_ROW + n * ROWS)) for n in range(2)]
        return [pairs[0][0], pairs[0][1], pairs[1][0], pairs[1][1]]

    here_side = [plane_of(here_ref, SIDE_ROW + n * ROWS) for n in range(2 * PAIRS)]
    there_side = [plane_of(there_ref, SIDE_ROW + n * ROWS) for n in range(2 * PAIRS)]
    side = [here_side[k] - faces[1][k] for k in range(PAIRS)]
    side += [here_side[PAIRS + k] + (faces[1][k] - faces[2][k]) for k in range(PAIRS)]
    other = [there_side[PAIRS + k] + (faces[2][k] - faces[3][k]) for k in range(PAIRS)]
    other += [there_side[k] + faces[3][k] for k in range(PAIRS)]
    no_rates = (None, None)
    diag = difference(line.diagonal(1, no_rates), correction_of(here_ref))
    other_diag = difference(line.diagonal(3, no_rates), correction_of(there_ref)[::-1])
    factor = two_by_two(line.above(1), inverse_of(other_diag))
    diag = less(diag, two_by_two(factor, line.below(3)))
    middle = apply_matrix(inverse_of(diag), difference(side, apply_matrix(factor, other)))
    moved = apply_matrix([spread_ref[n] for n in range(4)], middle)
    results = [known_ref[n] + moved[n] for n in range(2 * PAIRS)]
    for cell in range(2):
        for k in range(PAIRS):
            first, second = results[cell * PAIRS + k], results[(1 - cell) * PAIRS + k]
            result = jnp.where(mirrored == 0, first, second)
            for var in range(2):
                for inst in range(2):
                    for half in range(2):
                        row = rows_of(var, inst, half)
                        out_ref[
                            inst, 2 * k + var, pl.ds(cell, 1), pl.ds(half * LANES, LANES)
                        ] = result[row : row + 1]


def share_half(copies):
    insts, count = lax.axis_size("inst"), lax.axis_size("cell")
    halves = [range(count // 2), range(count - 1, count // 2 - 1, -1)]
    groups = [[inst * count + cell for inst in range(insts) for cell in half] for half in halves]
    return lax.all_to_all(
        copies, ("inst", "cell"), split_axis=0, concat_axis=0, tiled=True,
        axis_index_groups=groups,
    )


def swap_halves(block):
    count = lax.axis_size("cell")
    return lax.ppermute(block, "cell", [(i, (i + count // 2) % count) for i in range(count)])


def float_shape(*sizes):
    return jax.ShapeDtypeStruct(sizes, jnp.float32)


def local_by_halves(state, pseudo_rate, line_next, face_codes):
    blocks = lax.axis_size("cell") // 2
    cells = 2 * blocks
    vmem = pl.BlockSpec(memory_space=pltpu.VMEM)
    plane = (ROWS, LANES)
    params = pltpu.CompilerParams(vmem_limit_bytes=VMEM_BYTES)
    insts = lax.axis_size("inst")
    held = [
        pltpu.with_memory_space_constraint(array, pltpu.HBM)
        for array in (state, pseudo_rate, line_next, face_codes)
    ]
    packed, next_here, codes_here = pl.pallas_call(
        pack_kernel,
        out_shape=(
            float_shape(insts * blocks, BLOCK_ROWS, LANES),
            jax.ShapeDtypeStruct(line_next.shape, jnp.int32),
            jax.ShapeDtypeStruct(face_codes.shape, jnp.int32),
        ),
        in_specs=[pl.BlockSpec(memory_space=pltpu.HBM)] * 4,
        out_specs=(vmem, vmem, vmem),
        scratch_shapes=[
            pltpu.VMEM(state.shape, jnp.float32),
            pltpu.VMEM(pseudo_rate.shape, jnp.float32),
            pltpu.SemaphoreType.DMA((4,)),
        ],
        compiler_params=params,
    )(*held)
    shared = share_half(packed).reshape(insts, blocks, BLOCK_ROWS, LANES)
    here, eliminated = pl.pallas_call(
        half_kernel,
        out_shape=(
            float_shape(MIDDLE_ROWS, LANES),
            float_shape(blocks - 1, BLOCK_PLANES, *plane),
        ),
        in_specs=[vmem, vmem, vmem],
        out_specs=(vmem, vmem),
        scratch_shapes=[
            pltpu.VMEM((cells, PAIRS) + plane, jnp.float32),
            pltpu.VMEM((cells, 3) + plane, jnp.float32),
        ],
        compiler_params=params,
    )(shared, next_here, codes_here)
    there = swap_halves(here)
    known, spread = pl.pallas_call(
        spread_kernel,
        out_shape=(float_shape(2 * PAIRS, *plane), float_shape(4, *plane)),
        in_specs=[vmem, vmem],
        out_specs=(vmem, vmem),
        scratch_shapes=[pltpu.VMEM((blocks, 2 * PAIRS + 4) + plane, jnp.float32)],
        compiler_params=params,
        cost_estimate=pl.CostEstimate(flops=10**6, bytes_accessed=10**6, transcendentals=0),
    )(shared, eliminated)
    return pl.pallas_call(
        join_kernel,
        out_shape=float_shape(*state.shape),
        in_specs=[vmem] * 4,
        out_specs=vmem,
        compiler_params=params,
    )(here, there, known, spread)


def solution(mesh):
    placed = (P("inst", None, "cell", None), P("cell", None), P(), P())
    inst_count, cell_count = mesh.shape["inst"], mesh.shape["cell"]

    def local(state, pseudo_rate, line_next, face_codes):
        small = (
            state.shape == (2, 6, 2, 2 * LANES)
            and inst_count * 2 == NT
            and cell_count == 8
            and face_codes.shape[1] * LINES_DEV == state.shape[3]
        )
        chosen = local_by_halves if small else local_by_lines
        return chosen(state, pseudo_rate, line_next, face_codes)

    return jax.shard_map(
        local, mesh=mesh, in_specs=placed, out_specs=P("inst", None, "cell", None), check_vma=False
    )
```

```python
import functools

import jax
import jax.numpy as jnp
import numpy as np
from jax import lax
from jax.experimental import pallas as pl
from jax.experimental.pallas import tpu as pltpu
from jax.sharding import PartitionSpec as P

NT = 8
LINES_DEV = 32


GAMMA_GAS = 1.4
OMEGA_BLADE = 1.0
SENSOR_GAIN = 0.25
FOURTH_GAIN = 0.03125
PITCH_GAIN = 0.5
SECOND_IMPL = 1.0
FOURTH_IMPL = 0.25
FREE_STATE = (1.0, 0.5, 0.0, 0.0, 2.625, 0.2)
MIRROR_SIGNS = (1.0, -1.0, 1.0, 1.0, 1.0, 1.0)
ZERO_BLOCK = (0.0, 0.0, 0.0, 0.0)
UNIT_BLOCK = (1.0, 0.0, 0.0, 1.0)
ZERO_PAIR = (0.0, 0.0)


def extended(block, sides, width):
    for axis, dim in sides:
        count = lax.axis_size(axis)
        forward = [(i, i + 1) for i in range(count - 1)]
        backward = [(target, source) for source, target in forward]
        low = lax.ppermute(
            lax.slice_in_dim(block, block.shape[dim] - width, None, axis=dim), axis, forward
        )
        high = lax.ppermute(lax.slice_in_dim(block, 0, width, axis=dim), axis, backward)
        block = jnp.concatenate([low, block, high], axis=dim)
    return block


def spectral_matrix(instances):
    offsets = np.arange(instances)[:, None] - np.arange(instances)[None, :]
    angles = np.pi * offsets / instances
    safe_sin = np.where(offsets == 0, 1.0, np.sin(angles))
    parity = np.where(np.mod(offsets, 2) == 0, -1.0, 1.0)
    matrix_table = np.where(
        offsets == 0, 0.0, 0.5 * OMEGA_BLADE * parity * np.cos(angles) / safe_sin
    )
    return jnp.asarray(matrix_table, jnp.float32)


def primitive_parts(cells_state):
    density = cells_state[..., 0, :, :]
    inverse = 1.0 / density
    velocity_x = cells_state[..., 1, :, :] * inverse
    velocity_y = cells_state[..., 2, :, :] * inverse
    velocity_z = cells_state[..., 3, :, :] * inverse
    energy = cells_state[..., 4, :, :]
    pressure = (GAMMA_GAS - 1.0) * (
        energy
        - 0.5
        * density
        * (velocity_x * velocity_x + velocity_y * velocity_y + velocity_z * velocity_z)
    )
    sound_speed = jnp.sqrt(GAMMA_GAS * pressure * inverse)
    return (velocity_x, velocity_y, pressure, sound_speed)


def directed_flux(cells_state, normal_velocity, pressure, component):
    zero_plane = jnp.zeros_like(pressure)
    pressure_rows = [
        zero_plane,
        zero_plane,
        zero_plane,
        zero_plane,
        pressure * normal_velocity,
        zero_plane,
    ]
    pressure_rows[component] = pressure
    return cells_state * normal_velocity[..., None, :, :] + jnp.stack(pressure_rows, axis=-3)


def line_residual(padded):
    velocity_x, velocity_y, pressure, sound_speed = primitive_parts(padded)
    flux_line = directed_flux(padded, velocity_x, pressure, 1)
    radius = jnp.abs(velocity_x) + sound_speed
    sensor = jnp.abs(
        pressure[..., 2:, :] - 2.0 * pressure[..., 1:-1, :] + pressure[..., :-2, :]
    ) / (pressure[..., 2:, :] + 2.0 * pressure[..., 1:-1, :] + pressure[..., :-2, :])
    second = SENSOR_GAIN * jnp.maximum(sensor[..., :-1, :], sensor[..., 1:, :])
    fourth = jnp.maximum(0.0, FOURTH_GAIN - second)
    face_radius = 0.5 * (radius[..., 1:-2, :] + radius[..., 2:-1, :])
    left_far = padded[..., :-3, :]
    left_near = padded[..., 1:-2, :]
    right_near = padded[..., 2:-1, :]
    right_far = padded[..., 3:, :]
    damping = face_radius[..., None, :, :] * (
        second[..., None, :, :] * (right_near - left_near)
        - fourth[..., None, :, :] * (right_far - 3.0 * right_near + 3.0 * left_near - left_far)
    )
    face_flux = 0.5 * (flux_line[..., 1:-2, :] + flux_line[..., 2:-1, :]) - damping
    return (face_flux[..., 1:, :] - face_flux[..., :-1, :], radius)


def pitch_parts(cells_state):
    velocity_x, velocity_y, pressure, sound_speed = primitive_parts(cells_state)
    return (directed_flux(cells_state, velocity_y, pressure, 2), jnp.abs(velocity_y) + sound_speed)


def pitch_residual(cells_state, next_lines, prev_lines):
    pitch_flux, radius = pitch_parts(cells_state)
    state_next = jnp.take(cells_state, next_lines, axis=-1)
    flux_next, radius_next = pitch_parts(state_next)
    face_flux = 0.5 * (pitch_flux + flux_next) - PITCH_GAIN * (0.5 * (radius + radius_next))[
        ..., None, :, :
    ] * (state_next - cells_state)
    return face_flux - jnp.take(face_flux, prev_lines, axis=-1)


def boundary_cells(edge_pair, line_codes, lower_end):
    reflected = edge_pair[..., ::-1, :] * jnp.asarray(MIRROR_SIGNS, jnp.float32)[:, None, None]
    if lower_end:
        copied = jnp.concatenate([edge_pair[..., :1, :], edge_pair[..., :1, :]], axis=-2)
    else:
        copied = jnp.concatenate([edge_pair[..., 1:, :], edge_pair[..., 1:, :]], axis=-2)
    inflow = jnp.asarray(FREE_STATE, jnp.float32)[:, None, None] + jnp.zeros_like(edge_pair)
    return jnp.where(line_codes == 0, reflected, jnp.where(line_codes == 1, inflow, copied))


def line_coefficients(radius_ext, diagonal_term, positions, total_cells):
    radius_below = radius_ext[..., :-2, :]
    radius_centre = radius_ext[..., 1:-1, :]
    radius_above = radius_ext[..., 2:, :]
    face_below = 0.5 * (radius_below + radius_centre)
    face_above = 0.5 * (radius_centre + radius_above)
    far_low = FOURTH_IMPL * radius_below
    near_low = -SECOND_IMPL * face_below - 2.0 * FOURTH_IMPL * (radius_below + radius_centre)
    middle = (
        diagonal_term
        + SECOND_IMPL * (face_below + face_above)
        + FOURTH_IMPL * (radius_below + 4.0 * radius_centre + radius_above)
    )
    near_high = -SECOND_IMPL * face_above - 2.0 * FOURTH_IMPL * (radius_centre + radius_above)
    far_high = FOURTH_IMPL * radius_above
    column = positions[:, None]
    far_low = jnp.where(column >= 2, far_low, 0.0)
    near_low = jnp.where(column >= 1, near_low, 0.0)
    near_high = jnp.where(column <= total_cells - 2, near_high, 0.0)
    far_high = jnp.where(column <= total_cells - 3, far_high, 0.0)
    return (far_low, near_low, middle, near_high, far_high)


def block_product(first_matrix, second_matrix):
    return (
        first_matrix[0] * second_matrix[0] + first_matrix[1] * second_matrix[2],
        first_matrix[0] * second_matrix[1] + first_matrix[1] * second_matrix[3],
        first_matrix[2] * second_matrix[0] + first_matrix[3] * second_matrix[2],
        first_matrix[2] * second_matrix[1] + first_matrix[3] * second_matrix[3],
    )


def block_inverse(matrix):
    determinant = matrix[0] * matrix[3] - matrix[1] * matrix[2]
    reciprocal = 1.0 / determinant
    return (
        matrix[3] * reciprocal,
        -matrix[1] * reciprocal,
        -matrix[2] * reciprocal,
        matrix[0] * reciprocal,
    )


def block_apply(matrix, vector):
    return (
        matrix[0] * vector[0] + matrix[1] * vector[1],
        matrix[2] * vector[0] + matrix[3] * vector[1],
    )


def add_blocks(first_members, second_members):
    return tuple((a + b for a, b in zip(first_members, second_members)))


def negate(members):
    return tuple((-a for a in members))


def extend_blocks(members, fill_values):
    return tuple(
        (
            jnp.concatenate([m, jnp.full_like(m[..., :1, :], f)], axis=-2)
            for m, f in zip(members, fill_values)
        )
    )


def shift_next(members, fill_values):
    return tuple(
        (
            jnp.concatenate([m[..., 1:, :], jnp.full_like(m[..., :1, :], f)], axis=-2)
            for m, f in zip(members, fill_values)
        )
    )


def shift_prev(members):
    return tuple(
        (jnp.concatenate([jnp.zeros_like(m[..., :1, :]), m[..., :-1, :]], axis=-2) for m in members)
    )


def pair_split(member):
    shaped = member.reshape(member.shape[:-2] + (member.shape[-2] // 2, 2, member.shape[-1]))
    return (shaped[..., 0, :], shaped[..., 1, :])


def split_parity(members):
    halves = [pair_split(m) for m in members]
    return (tuple((h[0] for h in halves)), tuple((h[1] for h in halves)))


def alternate(first_member, second_member):
    stacked = jnp.stack((first_member, second_member), axis=-2)
    return stacked.reshape(
        first_member.shape[:-2] + (2 * first_member.shape[-2], first_member.shape[-1])
    )


def reduce_blocks(sub_blocks, diag_blocks, super_blocks, right_side):
    block_count = diag_blocks[0].shape[-2]
    if block_count == 1:
        return block_apply(block_inverse(diag_blocks), right_side)
    if block_count % 2 == 1:
        sub_blocks = extend_blocks(sub_blocks, ZERO_BLOCK)
        diag_blocks = extend_blocks(diag_blocks, UNIT_BLOCK)
        super_blocks = extend_blocks(super_blocks, ZERO_BLOCK)
        right_side = extend_blocks(right_side, ZERO_PAIR)
    sub_even, sub_odd = split_parity(sub_blocks)
    diag_even, diag_odd = split_parity(diag_blocks)
    super_even, super_odd = split_parity(super_blocks)
    side_even, side_odd = split_parity(right_side)
    inverse_even = block_inverse(diag_even)
    inverse_next = shift_next(inverse_even, UNIT_BLOCK)
    sub_next = shift_next(sub_even, ZERO_BLOCK)
    super_next = shift_next(super_even, ZERO_BLOCK)
    side_next = shift_next(side_even, ZERO_PAIR)
    left_factor = negate(block_product(sub_odd, inverse_even))
    right_factor = negate(block_product(super_odd, inverse_next))
    reduced_sub = block_product(left_factor, sub_even)
    reduced_diag = add_blocks(
        diag_odd,
        add_blocks(block_product(left_factor, super_even), block_product(right_factor, sub_next)),
    )
    reduced_super = block_product(right_factor, super_next)
    reduced_side = add_blocks(
        side_odd,
        add_blocks(block_apply(left_factor, side_even), block_apply(right_factor, side_next)),
    )
    odd_values = reduce_blocks(reduced_sub, reduced_diag, reduced_super, reduced_side)
    before_values = shift_prev(odd_values)
    remainder = add_blocks(
        side_even,
        negate(
            add_blocks(block_apply(sub_even, before_values), block_apply(super_even, odd_values))
        ),
    )
    even_values = block_apply(inverse_even, remainder)
    merged = tuple((alternate(e, o) for e, o in zip(even_values, odd_values)))
    return tuple((m[..., :block_count, :] for m in merged))


def cells_leading(block):
    moved = jnp.transpose(block, (2, 0, 1, 3))
    return moved.reshape(block.shape[2], block.shape[0] * block.shape[1] * block.shape[3])


def solve_in_lanes(coefficients, line_source):
    source_shape = line_source.shape
    lane_coef = [cells_leading(jnp.broadcast_to(c[:, None], source_shape)) for c in coefficients]
    pairs_list = [pair_split(m) for m in lane_coef]
    zero_plane = jnp.zeros_like(pairs_list[2][0])
    sub_blocks = (pairs_list[0][0], pairs_list[1][0], zero_plane, pairs_list[0][1])
    diag_blocks = (pairs_list[2][0], pairs_list[3][0], pairs_list[1][1], pairs_list[2][1])
    super_blocks = (pairs_list[4][0], zero_plane, pairs_list[3][1], pairs_list[4][1])
    values = reduce_blocks(
        sub_blocks, diag_blocks, super_blocks, pair_split(cells_leading(line_source))
    )
    flat = alternate(values[0], values[1])
    shaped = flat.reshape(source_shape[2], source_shape[0], source_shape[1], source_shape[3])
    return jnp.transpose(shaped, (1, 2, 0, 3))


def return_tiles(line_values):
    return lax.all_to_all(line_values, "cell", split_axis=2, concat_axis=3, tiled=True)


def local_by_lines(state, pseudo_rate, line_next, face_codes):
    local_count = state.shape[0]
    tile_cells = state.shape[2]
    cell_index = lax.axis_index("cell")
    cell_count = lax.axis_size("cell")
    total_cells = tile_cells * cell_count
    spectral = spectral_matrix(NT)
    first_local = lax.axis_index("inst") * local_count
    own_rows = lax.dynamic_slice_in_dim(spectral, first_local, local_count, 0)
    shard_block = jax.tree.map(lambda a: lax.all_gather(a, "inst", axis=0, tiled=True), state)
    columns = lax.slice_in_dim(own_rows, 0, shard_block.shape[0], axis=1)
    time_term = jnp.zeros_like(state) + jnp.einsum(
        "nm,mvil->nvil", columns, shard_block, precision=lax.Precision.HIGHEST
    )
    padded = extended(state, (("cell", 2),), 2)
    codes_lines = jnp.repeat(face_codes, LINES_DEV, axis=1)
    lower_ghost = boundary_cells(state[:, :, 0:2, :], codes_lines[0], True)
    upper_ghost = boundary_cells(state[:, :, -2:, :], codes_lines[1], False)
    lower_rim = jnp.where(cell_index == 0, lower_ghost, padded[:, :, :2, :])
    upper_rim = jnp.where(cell_index == cell_count - 1, upper_ghost, padded[:, :, -2:, :])
    padded = jnp.concatenate([lower_rim, padded[:, :, 2:-2, :], upper_rim], axis=2)
    line_part, radius = line_residual(padded)
    prev_lines = (
        jnp.zeros_like(line_next).at[line_next].set(jnp.arange(line_next.shape[0], dtype=jnp.int32))
    )
    residual = line_part + pitch_residual(state, line_next, prev_lines) + time_term
    right_side = -residual
    centre_radius = radius[:, 2:-2, :]
    diagonal_term = pseudo_rate * centre_radius
    positions = cell_index * tile_cells + jnp.arange(-1, tile_cells + 1, dtype=jnp.int32)
    inside = (positions >= 0) & (positions < total_cells)
    radius_ext = jnp.where(inside[:, None], radius[:, 1:-1, :], 0.0)
    coefficients = line_coefficients(radius_ext, diagonal_term, positions[1:-1], total_cells)
    stacked = jnp.stack(coefficients, axis=1)
    line_source = lax.all_to_all(right_side, "cell", split_axis=3, concat_axis=2, tiled=True)
    line_coef = lax.all_to_all(stacked, "cell", split_axis=3, concat_axis=2, tiled=True)
    update = return_tiles(solve_in_lanes(tuple((line_coef[:, k] for k in range(5))), line_source))
    return state + update


LANES = 128
ROWS = 8
PAIRS = 3
CELL_ROWS = PAIRS * ROWS
RATE_ROW = 2 * CELL_ROWS
VMEM_BYTES = 8 * 2**20
BLOCK_ROWS = RATE_ROW + ROWS

SIDE_ROW = 3 * CELL_ROWS
CORRECTION_ROW = SIDE_ROW + 2 * CELL_ROWS
MIDDLE_ROWS = CORRECTION_ROW + 2 * ROWS
BLOCK_PLANES = 4 + 3 + 2 * PAIRS


def spectral_offsets():
    table = np.zeros(NT)
    for offset in range(1, NT):
        angle = np.pi * offset / NT
        parity = -1.0 if offset % 2 == 0 else 1.0
        table[offset] = 0.5 * OMEGA_BLADE * parity * np.cos(angle) / np.sin(angle)
    return [float(np.float32(value)) for value in table]


def plane_masks():
    row_index = lax.broadcasted_iota(jnp.int32, (ROWS, LANES), 0)
    return row_index < 4, (row_index & 2) == 0, row_index & 1


def both(first_var, plane):
    turned = pltpu.roll(plane, 4, 0)
    return jnp.where(first_var, plane, turned), jnp.where(first_var, turned, plane)


def primitives(first_var, planes):
    density, moment_x = both(first_var, planes[0])
    moment_y, moment_z = both(first_var, planes[1])
    energy = jnp.where(first_var, planes[2], pltpu.roll(planes[2], 4, 0))
    inverse = 1.0 / density
    velocity_x = moment_x * inverse
    velocity_y = moment_y * inverse
    velocity_z = moment_z * inverse
    kinetic = moment_x * velocity_x + moment_y * velocity_y + moment_z * velocity_z
    pressure = (GAMMA_GAS - 1.0) * (energy - 0.5 * kinetic)
    sound = jnp.sqrt(GAMMA_GAS * pressure * inverse)
    return velocity_x, velocity_y, pressure, sound


def rows_of(var, inst, half):
    return (var // 2) * ROWS + (var % 2) * 4 + inst * 2 + half


def pack_kernel(
    held_state_ref, held_rate_ref, held_next_ref, held_codes_ref, out_ref, next_ref, codes_ref,
    state_ref, rate_ref, sems,
):
    copies = [
        pltpu.make_async_copy(source, target, sems.at[k])
        for k, (source, target) in enumerate(
            (
                (held_state_ref, state_ref),
                (held_rate_ref, rate_ref),
                (held_next_ref, next_ref),
                (held_codes_ref, codes_ref),
            )
        )
    ]
    for copy in copies:
        copy.start()
    for copy in copies:
        copy.wait()
    mirrored = lax.axis_index("cell") // (lax.axis_size("cell") // 2)
    for cell in range(2):
        place = pl.multiple_of(jnp.bitwise_xor(cell, mirrored) * CELL_ROWS, ROWS)
        for k in range(PAIRS):
            rows = [
                state_ref[inst, 2 * k + var, pl.ds(cell, 1), pl.ds(half * LANES, LANES)]
                for var in range(2)
                for inst in range(2)
                for half in range(2)
            ]
            for row, values in enumerate(rows):
                out_ref[0, pl.ds(place + (k * ROWS + row), 1), :] = values
    rates = [
        rate_ref[pl.ds(cell, 1), pl.ds(half * LANES, LANES)]
        for cell in range(2)
        for half in range(2)
    ]
    for row in range(4):
        out_ref[0, pl.ds(RATE_ROW + row, 1), :] = jnp.where(
            mirrored == 0, rates[row], rates[row ^ 2]
        )
    out_ref[0, pl.ds(RATE_ROW + 4, 4), :] = jnp.zeros((4, LANES), jnp.float32)
    for row in range(0, BLOCK_ROWS, ROWS):
        values = out_ref[0, pl.ds(row, ROWS), :]
        for copy in range(1, out_ref.shape[0]):
            out_ref[copy, pl.ds(row, ROWS), :] = values


def two_by_two(first, second):
    def entry(a, b, c, d):
        terms = [x * y for x, y in ((a, b), (c, d)) if x is not None and y is not None]
        return None if not terms else terms[0] if len(terms) == 1 else terms[0] + terms[1]

    return (
        entry(first[0], second[0], first[1], second[2]),
        entry(first[0], second[1], first[1], second[3]),
        entry(first[2], second[0], first[3], second[2]),
        entry(first[2], second[1], first[3], second[3]),
    )


def inverse_of(matrix):
    reciprocal = 1.0 / (matrix[0] * matrix[3] - matrix[1] * matrix[2])
    return (
        matrix[3] * reciprocal,
        -(matrix[1] * reciprocal),
        -(matrix[2] * reciprocal),
        matrix[0] * reciprocal,
    )


def less(first, second):
    return tuple(a if b is None else a - b for a, b in zip(first, second))


def minus(members):
    return tuple(None if a is None else -a for a in members)


def matrix_vector(matrix, low, high):
    def row(a, b):
        terms = [x * y for x, y in ((a, low), (b, high)) if x is not None]
        return terms[0] if len(terms) == 1 else terms[0] + terms[1]

    return row(matrix[0], matrix[1]), row(matrix[2], matrix[3])


def apply_matrix(matrix, side):
    parts = [matrix_vector(matrix, side[k], side[PAIRS + k]) for k in range(PAIRS)]
    return [low for low, _ in parts] + [high for _, high in parts]


def difference(first, second):
    return [a - b for a, b in zip(first, second)]


def flux_along(first_var, planes, velocity, pressure, sign):
    normal = sign * velocity
    return [
        planes[0] * normal + jnp.where(first_var, 0.0, sign * pressure),
        planes[1] * normal,
        planes[2] * normal + jnp.where(first_var, pressure * normal, 0.0),
    ]


class LineCells:
    def __init__(self, first_var, sign):
        self.first_var, self.sign = first_var, sign
        self.state, self.pressure, self.radius = {}, {}, {}
        self.flux, self.step, self.sensor = {}, {}, {}

    def add(self, cell, planes, velocity, pressure, sound):
        self.state[cell], self.pressure[cell] = planes, pressure
        self.radius[cell] = jnp.abs(velocity) + sound
        self.flux[cell] = flux_along(self.first_var, planes, velocity, pressure, self.sign)
        if cell - 1 in self.state:
            self.step[cell - 1] = difference(planes, self.state[cell - 1])
        if cell - 2 in self.state:
            twice = 2.0 * self.pressure[cell - 1]
            outer = pressure + self.pressure[cell - 2]
            self.sensor[cell - 1] = jnp.abs(outer - twice) / (outer + twice)

    def face(self, cell):
        second = SENSOR_GAIN * jnp.maximum(self.sensor[cell], self.sensor[cell + 1])
        fourth = jnp.maximum(0.0, FOURTH_GAIN - second)
        face_radius = 0.5 * (self.radius[cell] + self.radius[cell + 1])
        near_weight = face_radius * (second + 2.0 * fourth)
        far_weight = face_radius * fourth
        return [
            0.5 * (self.flux[cell][k] + self.flux[cell + 1][k])
            - (
                near_weight * self.step[cell][k]
                - far_weight * (self.step[cell + 1][k] + self.step[cell - 1][k])
            )
            for k in range(PAIRS)
        ]

    def near(self, cell):
        scale = SECOND_IMPL * 0.5 + 2.0 * FOURTH_IMPL
        return -scale * (self.radius[cell] + self.radius[cell + 1])

    def far(self, cell):
        return FOURTH_IMPL * self.radius[cell]

    def middle(self, cell, rate):
        centre, above = self.radius[cell], self.radius[cell + 1]
        if cell == 0:
            total, weighted = centre + (centre + above), 4.0 * centre + above
        else:
            below = self.radius[cell - 1]
            total = (below + centre) + (centre + above)
            weighted = below + 4.0 * centre + above
        result = SECOND_IMPL * (0.5 * total) + FOURTH_IMPL * weighted
        return result if rate is None else rate * centre + result

    def diagonal(self, cell, rates):
        across = self.near(cell)
        return (self.middle(cell, rates[0]), across, across, self.middle(cell + 1, rates[1]))

    def below(self, cell):
        return (self.far(cell - 1), self.near(cell - 1), None, self.far(cell))

    def above(self, cell):
        return (self.far(cell + 1), None, self.near(cell + 1), self.far(cell + 2))


def rates_at(ref, index, start, first_half):
    rows = [ref[index + (pl.ds(start + k, 1), slice(None))] for k in range(4)]
    return [jnp.where(first_half, rows[2 * k], rows[2 * k + 1]) for k in range(2)]


def half_kernel(
    all_ref, next_ref, codes_ref, middle_ref, blocks_ref, rest_ref, line_ref,
):
    own_inst = lax.axis_index("inst")
    inst_count, blocks = all_ref.shape[:2]
    cells = 2 * blocks
    mirrored = lax.axis_index("cell") // blocks
    sign = (1 - 2 * mirrored).astype(jnp.float32)
    shape = (ROWS, LANES)
    lane_index = lax.broadcasted_iota(jnp.int32, shape, 1)
    first_var, first_inst, half_index = plane_masks()
    first_half = half_index == 0
    zero = jnp.zeros(shape, jnp.float32)

    next_rows = [
        next_ref[pl.ds(half * LANES, LANES)].reshape(1, LANES) for half in range(2)
    ]
    next_line = jnp.where(first_half, next_rows[0], next_rows[1])
    column = lax.broadcasted_iota(jnp.int32, (LANES, LANES), 0)
    prev_halves = []
    for target in range(2):
        total = None
        for source in range(2):
            hits = jnp.where(column + target * LANES == next_rows[source], 1.0, 0.0)
            names = (lane_index + source * LANES).astype(jnp.float32)
            part = lax.dot_general(
                names, hits, (((1,), (1,)), ((), ())), preferred_element_type=jnp.float32
            )
            total = part if total is None else total + part
        prev_halves.append(total)
    prev_line = jnp.where(first_half, prev_halves[0], prev_halves[1]).astype(jnp.int32)

    def picker(lines):
        lane = lines & (LANES - 1)
        same = (lines >> 7) == half_index

        def pick(plane):
            swapped = jnp.where(first_half, pltpu.roll(plane, 7, 0), pltpu.roll(plane, 1, 0))
            here = jnp.take_along_axis(plane, lane, axis=1, mode="promise_in_bounds")
            there = jnp.take_along_axis(swapped, lane, axis=1, mode="promise_in_bounds")
            return jnp.where(same, here, there)

        return pick

    pick_next = picker(next_line)
    pick_prev = picker(prev_line)

    def loaded(cell, inst=own_inst):
        return [
            all_ref[inst, cell // 2, pl.ds((cell % 2) * CELL_ROWS + k * ROWS, ROWS), :]
            for k in range(PAIRS)
        ]

    offsets = spectral_offsets()

    def time_parts(cell):
        pairs = [
            loaded(cell, (own_inst - shift) & (inst_count - 1)) for shift in range(inst_count)
        ]
        result = []
        for k in range(PAIRS):
            same_total, other_total = None, None
            for shift in range(inst_count):
                plane = pairs[shift][k]
                other = jnp.where(
                    first_inst, offsets[(2 * shift + 1) % NT], offsets[(2 * shift - 1) % NT]
                )
                if shift > 0:
                    term = offsets[(2 * shift) % NT] * plane
                    same_total = term if same_total is None else same_total + term
                term = other * plane
                other_total = term if other_total is None else other_total + term
            turned = jnp.where(
                first_inst, pltpu.roll(other_total, 6, 0), pltpu.roll(other_total, 2, 0)
            )
            result.append(same_total + turned)
        return result

    def flux_across(planes, velocity, pressure):
        return [
            planes[0] * velocity,
            planes[1] * velocity + jnp.where(first_var, pressure, 0.0),
            planes[2] * velocity + jnp.where(first_var, pressure * velocity, 0.0),
        ]

    def pitch_flux(planes, velocity_y, pressure, sound):
        nearby = [pick_next(plane) for plane in planes]
        _, next_velocity, next_pressure, next_sound = primitives(first_var, nearby)
        own_flux = flux_across(planes, velocity_y, pressure)
        next_flux = flux_across(nearby, next_velocity, next_pressure)
        weight = (PITCH_GAIN * 0.5) * (
            jnp.abs(velocity_y) + sound + (jnp.abs(next_velocity) + next_sound)
        )
        return [
            0.5 * (a + b) - weight * (n - o)
            for a, b, n, o in zip(own_flux, next_flux, nearby, planes)
        ]

    for cell in range(cells):
        planes = loaded(cell)
        velocity_x, velocity_y, pressure, sound = primitives(first_var, planes)
        line_ref[cell, 0], line_ref[cell, 1], line_ref[cell, 2] = velocity_x, pressure, sound
        faces_across = pitch_flux(planes, velocity_y, pressure, sound)
        times = time_parts(cell)
        for k in range(PAIRS):
            rest_ref[cell, k] = times[k] + (faces_across[k] - pick_prev(faces_across[k]))

    tile = half_index * (LANES // LINES_DEV) + lane_index // LINES_DEV
    end_codes = jnp.where(mirrored == 0, codes_ref[pl.ds(0, 1), :], codes_ref[pl.ds(1, 1), :])
    codes = jnp.zeros(shape, jnp.int32)
    for k in range(2 * LANES // LINES_DEV):
        codes = jnp.where(tile == k, jnp.broadcast_to(end_codes[:, k : k + 1], shape), codes)

    def ghost(cell):
        planes = loaded(-1 - cell)
        copied = loaded(0)
        result = []
        for k in range(PAIRS):
            reflected = planes[k] if k else jnp.where(first_var, planes[k], -planes[k])
            inflow = jnp.where(first_var, FREE_STATE[2 * k], FREE_STATE[2 * k + 1])
            result.append(
                jnp.where(codes == 0, reflected, jnp.where(codes == 1, inflow, copied[k]))
            )
        return result

    line = LineCells(first_var, sign)
    sides, faces, inverses, aboves = [], {}, [], []
    for cell in range(-2, cells):
        if cell < 0:
            planes = ghost(cell)
            velocity_x, _, pressure, sound = primitives(first_var, planes)
        else:
            planes = loaded(cell)
            velocity_x, pressure, sound = [line_ref[cell, k] for k in range(3)]
        line.add(cell, planes, velocity_x, pressure, sound)
        if cell >= 1:
            faces[cell - 2] = line.face(cell - 2)
        if cell >= 3 and cell % 2 == 1:
            at = cell - 3
            block = at // 2
            rates = rates_at(all_ref, (own_inst, block), RATE_ROW, first_half)
            diag = line.diagonal(at, rates)
            side = []
            for member in range(2):
                for k in range(PAIRS):
                    side.append(
                        faces[at + member - 1][k] - faces[at + member][k]
                        - rest_ref[at + member, k]
                    )
            if block > 0:
                factor = two_by_two(line.below(at), inverses[-1])
                diag = less(diag, two_by_two(factor, aboves[-1]))
                side = difference(side, apply_matrix(factor, sides[-1]))
            inverses.append(inverse_of(diag))
            aboves.append(line.above(at))
            sides.append(side)

    last = cells - 2
    factor = two_by_two(line.below(last), inverses[-1])
    correction = list(two_by_two(factor, aboves[-1]))
    rates = rates_at(all_ref, (own_inst, blocks - 1), RATE_ROW, first_half)
    for member in range(2):
        centre = line.radius[last + member]
        correction[3 * member] = correction[3 * member] - rates[member] * centre
    side = [faces[last - 1][k] - rest_ref[last, k] for k in range(PAIRS)]
    side += [-rest_ref[last + 1, k] for k in range(PAIRS)]
    side = difference(side, apply_matrix(factor, sides[-1]))
    for n in range(3):
        for k, plane in enumerate(line.state[cells - 3 + n]):
            middle_ref[pl.ds(n * CELL_ROWS + k * ROWS, ROWS), :] = plane
    for n, plane in enumerate(side):
        middle_ref[pl.ds(SIDE_ROW + n * ROWS, ROWS), :] = plane
    for n in range(2):
        middle_ref[pl.ds(CORRECTION_ROW + n * ROWS, ROWS), :] = jnp.where(
            first_var, correction[2 * n], correction[2 * n + 1]
        )
    for block in range(blocks - 1):
        kept = [*inverses[block], aboves[block][0], *aboves[block][2:], *sides[block]]
        for n, plane in enumerate(kept):
            blocks_ref[block, n] = plane


def spread_kernel(all_ref, blocks_ref, known_ref, spread_ref, table_ref):
    own_inst = lax.axis_index("inst")
    blocks = all_ref.shape[1]
    own_cell = lax.axis_index("cell")
    own_block = jnp.where(own_cell < blocks, own_cell, 2 * blocks - 1 - own_cell)
    zero = jnp.zeros((ROWS, LANES), jnp.float32)
    known, spread = [zero] * (2 * PAIRS), (zero + 1.0, zero, zero, zero + 1.0)
    for block in range(blocks - 1, -1, -1):
        if block < blocks - 1:
            kept = [blocks_ref[block, n] for n in range(BLOCK_PLANES)]
            inverse, above, side = kept[:4], (kept[4], None, kept[5], kept[6]), kept[7:]
            step = two_by_two(inverse, above)
            own = apply_matrix(inverse, side)
            if block < blocks - 2:
                known = difference(own, apply_matrix(step, known))
                spread = minus(two_by_two(step, spread))
            else:
                known, spread = own, minus(step)
        for n, plane in enumerate(known + list(spread)):
            table_ref[block, n] = plane
    for n in range(2 * PAIRS):
        base = all_ref[own_inst, own_block, pl.ds(n * ROWS, ROWS), :]
        known_ref[n] = base + table_ref[own_block, n]
    for n in range(4):
        spread_ref[n] = table_ref[own_block, 2 * PAIRS + n]


def join_kernel(here_ref, first_ref, second_ref, known_ref, spread_ref, out_ref, there_ref):
    mirrored = lax.axis_index("cell") // (lax.axis_size("cell") // 2)
    sign = (1 - 2 * mirrored).astype(jnp.float32)
    first_var, _, _ = plane_masks()
    for row in range(0, MIDDLE_ROWS, ROWS):
        rows = pl.ds(row, ROWS)
        there_ref[rows, :] = first_ref[rows, :] + second_ref[rows, :]

    def plane_of(ref, row):
        return ref[pl.ds(row, ROWS), :]

    line = LineCells(first_var, sign)
    for cell in range(6):
        ref, at = (here_ref, cell) if cell < 3 else (there_ref, 5 - cell)
        planes = [plane_of(ref, at * CELL_ROWS + k * ROWS) for k in range(PAIRS)]
        velocity_x, _, pressure, sound = primitives(first_var, planes)
        line.add(cell, planes, velocity_x, pressure, sound)
    faces = {cell: line.face(cell) for cell in (1, 2, 3)}

    def correction_of(ref):
        pairs = [both(first_var, plane_of(ref, CORRECTION_ROW + n * ROWS)) for n in range(2)]
        return [pairs[0][0], pairs[0][1], pairs[1][0], pairs[1][1]]

    here_side = [plane_of(here_ref, SIDE_ROW + n * ROWS) for n in range(2 * PAIRS)]
    there_side = [plane_of(there_ref, SIDE_ROW + n * ROWS) for n in range(2 * PAIRS)]
    side = [here_side[k] - faces[1][k] for k in range(PAIRS)]
    side += [here_side[PAIRS + k] + (faces[1][k] - faces[2][k]) for k in range(PAIRS)]
    other = [there_side[PAIRS + k] + (faces[2][k] - faces[3][k]) for k in range(PAIRS)]
    other += [there_side[k] + faces[3][k] for k in range(PAIRS)]
    no_rates = (None, None)
    diag = difference(line.diagonal(1, no_rates), correction_of(here_ref))
    other_diag = difference(line.diagonal(3, no_rates), correction_of(there_ref)[::-1])
    factor = two_by_two(line.above(1), inverse_of(other_diag))
    diag = less(diag, two_by_two(factor, line.below(3)))
    middle = apply_matrix(inverse_of(diag), difference(side, apply_matrix(factor, other)))
    moved = apply_matrix([spread_ref[n] for n in range(4)], middle)
    results = [known_ref[n] + moved[n] for n in range(2 * PAIRS)]
    for cell in range(2):
        for k in range(PAIRS):
            first, second = results[cell * PAIRS + k], results[(1 - cell) * PAIRS + k]
            result = jnp.where(mirrored == 0, first, second)
            for var in range(2):
                for inst in range(2):
                    for half in range(2):
                        row = rows_of(var, inst, half)
                        out_ref[
                            inst, 2 * k + var, pl.ds(cell, 1), pl.ds(half * LANES, LANES)
                        ] = result[row : row + 1]


def share_half(copies):
    insts, count = lax.axis_size("inst"), lax.axis_size("cell")
    halves = [range(count // 2), range(count - 1, count // 2 - 1, -1)]
    groups = [[inst * count + cell for inst in range(insts) for cell in half] for half in halves]
    return lax.all_to_all(
        copies, ("inst", "cell"), split_axis=0, concat_axis=0, tiled=True,
        axis_index_groups=groups,
    )


def swap_halves(block):
    half = lax.axis_size("cell") // 2
    results = []
    for start in (half // 2, 0):
        ups = [(cell, cell + half) for cell in range(start, start + half // 2)]
        pairs = ups + [(target, source) for source, target in ups]
        results.append(lax.ppermute(block, "cell", pairs))
    return results


def float_shape(*sizes):
    return jax.ShapeDtypeStruct(sizes, jnp.float32)


def local_by_halves(state, pseudo_rate, line_next, face_codes):
    blocks = lax.axis_size("cell") // 2
    cells = 2 * blocks
    vmem = pl.BlockSpec(memory_space=pltpu.VMEM)
    plane = (ROWS, LANES)
    params = pltpu.CompilerParams(vmem_limit_bytes=VMEM_BYTES)
    insts = lax.axis_size("inst")
    held = [
        pltpu.with_memory_space_constraint(array, pltpu.HBM)
        for array in (state, pseudo_rate, line_next, face_codes)
    ]
    packed, next_here, codes_here = pl.pallas_call(
        pack_kernel,
        out_shape=(
            float_shape(insts * blocks, BLOCK_ROWS, LANES),
            jax.ShapeDtypeStruct(line_next.shape, jnp.int32),
            jax.ShapeDtypeStruct(face_codes.shape, jnp.int32),
        ),
        in_specs=[pl.BlockSpec(memory_space=pltpu.HBM)] * 4,
        out_specs=(vmem, vmem, vmem),
        scratch_shapes=[
            pltpu.VMEM(state.shape, jnp.float32),
            pltpu.VMEM(pseudo_rate.shape, jnp.float32),
            pltpu.SemaphoreType.DMA((4,)),
        ],
        compiler_params=params,
    )(*held)
    shared = share_half(packed).reshape(insts, blocks, BLOCK_ROWS, LANES)
    here, eliminated = pl.pallas_call(
        half_kernel,
        out_shape=(
            float_shape(MIDDLE_ROWS, LANES),
            float_shape(blocks - 1, BLOCK_PLANES, *plane),
        ),
        in_specs=[vmem, vmem, vmem],
        out_specs=(vmem, vmem),
        scratch_shapes=[
            pltpu.VMEM((cells, PAIRS) + plane, jnp.float32),
            pltpu.VMEM((cells, 3) + plane, jnp.float32),
        ],
        compiler_params=params,
    )(shared, next_here, codes_here)
    first, second = swap_halves(here)
    known, spread = pl.pallas_call(
        spread_kernel,
        out_shape=(float_shape(2 * PAIRS, *plane), float_shape(4, *plane)),
        in_specs=[vmem, vmem],
        out_specs=(vmem, vmem),
        scratch_shapes=[pltpu.VMEM((blocks, 2 * PAIRS + 4) + plane, jnp.float32)],
        compiler_params=params,
        cost_estimate=pl.CostEstimate(flops=10**6, bytes_accessed=10**6, transcendentals=0),
    )(shared, eliminated)
    return pl.pallas_call(
        join_kernel,
        out_shape=float_shape(*state.shape),
        in_specs=[vmem] * 5,
        out_specs=vmem,
        scratch_shapes=[pltpu.VMEM((MIDDLE_ROWS, LANES), jnp.float32)],
        compiler_params=params,
    )(here, first, second, known, spread)


def solution(mesh):
    placed = (P("inst", None, "cell", None), P("cell", None), P(), P())
    inst_count, cell_count = mesh.shape["inst"], mesh.shape["cell"]

    def local(state, pseudo_rate, line_next, face_codes):
        small = (
            state.shape == (2, 6, 2, 2 * LANES)
            and inst_count * 2 == NT
            and cell_count == 8
            and face_codes.shape[1] * LINES_DEV == state.shape[3]
        )
        chosen = local_by_halves if small else local_by_lines
        return chosen(state, pseudo_rate, line_next, face_codes)

    return jax.shard_map(
        local, mesh=mesh, in_specs=placed, out_specs=P("inst", None, "cell", None), check_vma=False
    )
```

```python
import functools

import jax
import jax.numpy as jnp
import numpy as np
from jax import lax
from jax.experimental import pallas as pl
from jax.experimental.pallas import tpu as pltpu
from jax.sharding import PartitionSpec as P

NT = 8
LINES_DEV = 32


GAMMA_GAS = 1.4
OMEGA_BLADE = 1.0
SENSOR_GAIN = 0.25
FOURTH_GAIN = 0.03125
PITCH_GAIN = 0.5
SECOND_IMPL = 1.0
FOURTH_IMPL = 0.25
FREE_STATE = (1.0, 0.5, 0.0, 0.0, 2.625, 0.2)
MIRROR_SIGNS = (1.0, -1.0, 1.0, 1.0, 1.0, 1.0)
ZERO_BLOCK = (0.0, 0.0, 0.0, 0.0)
UNIT_BLOCK = (1.0, 0.0, 0.0, 1.0)
ZERO_PAIR = (0.0, 0.0)


def extended(block, sides, width):
    for axis, dim in sides:
        count = lax.axis_size(axis)
        forward = [(i, i + 1) for i in range(count - 1)]
        backward = [(target, source) for source, target in forward]
        low = lax.ppermute(
            lax.slice_in_dim(block, block.shape[dim] - width, None, axis=dim), axis, forward
        )
        high = lax.ppermute(lax.slice_in_dim(block, 0, width, axis=dim), axis, backward)
        block = jnp.concatenate([low, block, high], axis=dim)
    return block


def spectral_matrix(instances):
    offsets = np.arange(instances)[:, None] - np.arange(instances)[None, :]
    angles = np.pi * offsets / instances
    safe_sin = np.where(offsets == 0, 1.0, np.sin(angles))
    parity = np.where(np.mod(offsets, 2) == 0, -1.0, 1.0)
    matrix_table = np.where(
        offsets == 0, 0.0, 0.5 * OMEGA_BLADE * parity * np.cos(angles) / safe_sin
    )
    return jnp.asarray(matrix_table, jnp.float32)


def primitive_parts(cells_state):
    density = cells_state[..., 0, :, :]
    inverse = 1.0 / density
    velocity_x = cells_state[..., 1, :, :] * inverse
    velocity_y = cells_state[..., 2, :, :] * inverse
    velocity_z = cells_state[..., 3, :, :] * inverse
    energy = cells_state[..., 4, :, :]
    pressure = (GAMMA_GAS - 1.0) * (
        energy
        - 0.5
        * density
        * (velocity_x * velocity_x + velocity_y * velocity_y + velocity_z * velocity_z)
    )
    sound_speed = jnp.sqrt(GAMMA_GAS * pressure * inverse)
    return (velocity_x, velocity_y, pressure, sound_speed)


def directed_flux(cells_state, normal_velocity, pressure, component):
    zero_plane = jnp.zeros_like(pressure)
    pressure_rows = [
        zero_plane,
        zero_plane,
        zero_plane,
        zero_plane,
        pressure * normal_velocity,
        zero_plane,
    ]
    pressure_rows[component] = pressure
    return cells_state * normal_velocity[..., None, :, :] + jnp.stack(pressure_rows, axis=-3)


def line_residual(padded):
    velocity_x, velocity_y, pressure, sound_speed = primitive_parts(padded)
    flux_line = directed_flux(padded, velocity_x, pressure, 1)
    radius = jnp.abs(velocity_x) + sound_speed
    sensor = jnp.abs(
        pressure[..., 2:, :] - 2.0 * pressure[..., 1:-1, :] + pressure[..., :-2, :]
    ) / (pressure[..., 2:, :] + 2.0 * pressure[..., 1:-1, :] + pressure[..., :-2, :])
    second = SENSOR_GAIN * jnp.maximum(sensor[..., :-1, :], sensor[..., 1:, :])
    fourth = jnp.maximum(0.0, FOURTH_GAIN - second)
    face_radius = 0.5 * (radius[..., 1:-2, :] + radius[..., 2:-1, :])
    left_far = padded[..., :-3, :]
    left_near = padded[..., 1:-2, :]
    right_near = padded[..., 2:-1, :]
    right_far = padded[..., 3:, :]
    damping = face_radius[..., None, :, :] * (
        second[..., None, :, :] * (right_near - left_near)
        - fourth[..., None, :, :] * (right_far - 3.0 * right_near + 3.0 * left_near - left_far)
    )
    face_flux = 0.5 * (flux_line[..., 1:-2, :] + flux_line[..., 2:-1, :]) - damping
    return (face_flux[..., 1:, :] - face_flux[..., :-1, :], radius)


def pitch_parts(cells_state):
    velocity_x, velocity_y, pressure, sound_speed = primitive_parts(cells_state)
    return (directed_flux(cells_state, velocity_y, pressure, 2), jnp.abs(velocity_y) + sound_speed)


def pitch_residual(cells_state, next_lines, prev_lines):
    pitch_flux, radius = pitch_parts(cells_state)
    state_next = jnp.take(cells_state, next_lines, axis=-1)
    flux_next, radius_next = pitch_parts(state_next)
    face_flux = 0.5 * (pitch_flux + flux_next) - PITCH_GAIN * (0.5 * (radius + radius_next))[
        ..., None, :, :
    ] * (state_next - cells_state)
    return face_flux - jnp.take(face_flux, prev_lines, axis=-1)


def boundary_cells(edge_pair, line_codes, lower_end):
    reflected = edge_pair[..., ::-1, :] * jnp.asarray(MIRROR_SIGNS, jnp.float32)[:, None, None]
    if lower_end:
        copied = jnp.concatenate([edge_pair[..., :1, :], edge_pair[..., :1, :]], axis=-2)
    else:
        copied = jnp.concatenate([edge_pair[..., 1:, :], edge_pair[..., 1:, :]], axis=-2)
    inflow = jnp.asarray(FREE_STATE, jnp.float32)[:, None, None] + jnp.zeros_like(edge_pair)
    return jnp.where(line_codes == 0, reflected, jnp.where(line_codes == 1, inflow, copied))


def line_coefficients(radius_ext, diagonal_term, positions, total_cells):
    radius_below = radius_ext[..., :-2, :]
    radius_centre = radius_ext[..., 1:-1, :]
    radius_above = radius_ext[..., 2:, :]
    face_below = 0.5 * (radius_below + radius_centre)
    face_above = 0.5 * (radius_centre + radius_above)
    far_low = FOURTH_IMPL * radius_below
    near_low = -SECOND_IMPL * face_below - 2.0 * FOURTH_IMPL * (radius_below + radius_centre)
    middle = (
        diagonal_term
        + SECOND_IMPL * (face_below + face_above)
        + FOURTH_IMPL * (radius_below + 4.0 * radius_centre + radius_above)
    )
    near_high = -SECOND_IMPL * face_above - 2.0 * FOURTH_IMPL * (radius_centre + radius_above)
    far_high = FOURTH_IMPL * radius_above
    column = positions[:, None]
    far_low = jnp.where(column >= 2, far_low, 0.0)
    near_low = jnp.where(column >= 1, near_low, 0.0)
    near_high = jnp.where(column <= total_cells - 2, near_high, 0.0)
    far_high = jnp.where(column <= total_cells - 3, far_high, 0.0)
    return (far_low, near_low, middle, near_high, far_high)


def block_product(first_matrix, second_matrix):
    return (
        first_matrix[0] * second_matrix[0] + first_matrix[1] * second_matrix[2],
        first_matrix[0] * second_matrix[1] + first_matrix[1] * second_matrix[3],
        first_matrix[2] * second_matrix[0] + first_matrix[3] * second_matrix[2],
        first_matrix[2] * second_matrix[1] + first_matrix[3] * second_matrix[3],
    )


def block_inverse(matrix):
    determinant = matrix[0] * matrix[3] - matrix[1] * matrix[2]
    reciprocal = 1.0 / determinant
    return (
        matrix[3] * reciprocal,
        -matrix[1] * reciprocal,
        -matrix[2] * reciprocal,
        matrix[0] * reciprocal,
    )


def block_apply(matrix, vector):
    return (
        matrix[0] * vector[0] + matrix[1] * vector[1],
        matrix[2] * vector[0] + matrix[3] * vector[1],
    )


def add_blocks(first_members, second_members):
    return tuple((a + b for a, b in zip(first_members, second_members)))


def negate(members):
    return tuple((-a for a in members))


def extend_blocks(members, fill_values):
    return tuple(
        (
            jnp.concatenate([m, jnp.full_like(m[..., :1, :], f)], axis=-2)
            for m, f in zip(members, fill_values)
        )
    )


def shift_next(members, fill_values):
    return tuple(
        (
            jnp.concatenate([m[..., 1:, :], jnp.full_like(m[..., :1, :], f)], axis=-2)
            for m, f in zip(members, fill_values)
        )
    )


def shift_prev(members):
    return tuple(
        (jnp.concatenate([jnp.zeros_like(m[..., :1, :]), m[..., :-1, :]], axis=-2) for m in members)
    )


def pair_split(member):
    shaped = member.reshape(member.shape[:-2] + (member.shape[-2] // 2, 2, member.shape[-1]))
    return (shaped[..., 0, :], shaped[..., 1, :])


def split_parity(members):
    halves = [pair_split(m) for m in members]
    return (tuple((h[0] for h in halves)), tuple((h[1] for h in halves)))


def alternate(first_member, second_member):
    stacked = jnp.stack((first_member, second_member), axis=-2)
    return stacked.reshape(
        first_member.shape[:-2] + (2 * first_member.shape[-2], first_member.shape[-1])
    )


def reduce_blocks(sub_blocks, diag_blocks, super_blocks, right_side):
    block_count = diag_blocks[0].shape[-2]
    if block_count == 1:
        return block_apply(block_inverse(diag_blocks), right_side)
    if block_count % 2 == 1:
        sub_blocks = extend_blocks(sub_blocks, ZERO_BLOCK)
        diag_blocks = extend_blocks(diag_blocks, UNIT_BLOCK)
        super_blocks = extend_blocks(super_blocks, ZERO_BLOCK)
        right_side = extend_blocks(right_side, ZERO_PAIR)
    sub_even, sub_odd = split_parity(sub_blocks)
    diag_even, diag_odd = split_parity(diag_blocks)
    super_even, super_odd = split_parity(super_blocks)
    side_even, side_odd = split_parity(right_side)
    inverse_even = block_inverse(diag_even)
    inverse_next = shift_next(inverse_even, UNIT_BLOCK)
    sub_next = shift_next(sub_even, ZERO_BLOCK)
    super_next = shift_next(super_even, ZERO_BLOCK)
    side_next = shift_next(side_even, ZERO_PAIR)
    left_factor = negate(block_product(sub_odd, inverse_even))
    right_factor = negate(block_product(super_odd, inverse_next))
    reduced_sub = block_product(left_factor, sub_even)
    reduced_diag = add_blocks(
        diag_odd,
        add_blocks(block_product(left_factor, super_even), block_product(right_factor, sub_next)),
    )
    reduced_super = block_product(right_factor, super_next)
    reduced_side = add_blocks(
        side_odd,
        add_blocks(block_apply(left_factor, side_even), block_apply(right_factor, side_next)),
    )
    odd_values = reduce_blocks(reduced_sub, reduced_diag, reduced_super, reduced_side)
    before_values = shift_prev(odd_values)
    remainder = add_blocks(
        side_even,
        negate(
            add_blocks(block_apply(sub_even, before_values), block_apply(super_even, odd_values))
        ),
    )
    even_values = block_apply(inverse_even, remainder)
    merged = tuple((alternate(e, o) for e, o in zip(even_values, odd_values)))
    return tuple((m[..., :block_count, :] for m in merged))


def cells_leading(block):
    moved = jnp.transpose(block, (2, 0, 1, 3))
    return moved.reshape(block.shape[2], block.shape[0] * block.shape[1] * block.shape[3])


def solve_in_lanes(coefficients, line_source):
    source_shape = line_source.shape
    lane_coef = [cells_leading(jnp.broadcast_to(c[:, None], source_shape)) for c in coefficients]
    pairs_list = [pair_split(m) for m in lane_coef]
    zero_plane = jnp.zeros_like(pairs_list[2][0])
    sub_blocks = (pairs_list[0][0], pairs_list[1][0], zero_plane, pairs_list[0][1])
    diag_blocks = (pairs_list[2][0], pairs_list[3][0], pairs_list[1][1], pairs_list[2][1])
    super_blocks = (pairs_list[4][0], zero_plane, pairs_list[3][1], pairs_list[4][1])
    values = reduce_blocks(
        sub_blocks, diag_blocks, super_blocks, pair_split(cells_leading(line_source))
    )
    flat = alternate(values[0], values[1])
    shaped = flat.reshape(source_shape[2], source_shape[0], source_shape[1], source_shape[3])
    return jnp.transpose(shaped, (1, 2, 0, 3))


def return_tiles(line_values):
    return lax.all_to_all(line_values, "cell", split_axis=2, concat_axis=3, tiled=True)


def local_by_lines(state, pseudo_rate, line_next, face_codes):
    local_count = state.shape[0]
    tile_cells = state.shape[2]
    cell_index = lax.axis_index("cell")
    cell_count = lax.axis_size("cell")
    total_cells = tile_cells * cell_count
    spectral = spectral_matrix(NT)
    first_local = lax.axis_index("inst") * local_count
    own_rows = lax.dynamic_slice_in_dim(spectral, first_local, local_count, 0)
    shard_block = jax.tree.map(lambda a: lax.all_gather(a, "inst", axis=0, tiled=True), state)
    columns = lax.slice_in_dim(own_rows, 0, shard_block.shape[0], axis=1)
    time_term = jnp.zeros_like(state) + jnp.einsum(
        "nm,mvil->nvil", columns, shard_block, precision=lax.Precision.HIGHEST
    )
    padded = extended(state, (("cell", 2),), 2)
    codes_lines = jnp.repeat(face_codes, LINES_DEV, axis=1)
    lower_ghost = boundary_cells(state[:, :, 0:2, :], codes_lines[0], True)
    upper_ghost = boundary_cells(state[:, :, -2:, :], codes_lines[1], False)
    lower_rim = jnp.where(cell_index == 0, lower_ghost, padded[:, :, :2, :])
    upper_rim = jnp.where(cell_index == cell_count - 1, upper_ghost, padded[:, :, -2:, :])
    padded = jnp.concatenate([lower_rim, padded[:, :, 2:-2, :], upper_rim], axis=2)
    line_part, radius = line_residual(padded)
    prev_lines = (
        jnp.zeros_like(line_next).at[line_next].set(jnp.arange(line_next.shape[0], dtype=jnp.int32))
    )
    residual = line_part + pitch_residual(state, line_next, prev_lines) + time_term
    right_side = -residual
    centre_radius = radius[:, 2:-2, :]
    diagonal_term = pseudo_rate * centre_radius
    positions = cell_index * tile_cells + jnp.arange(-1, tile_cells + 1, dtype=jnp.int32)
    inside = (positions >= 0) & (positions < total_cells)
    radius_ext = jnp.where(inside[:, None], radius[:, 1:-1, :], 0.0)
    coefficients = line_coefficients(radius_ext, diagonal_term, positions[1:-1], total_cells)
    stacked = jnp.stack(coefficients, axis=1)
    line_source = lax.all_to_all(right_side, "cell", split_axis=3, concat_axis=2, tiled=True)
    line_coef = lax.all_to_all(stacked, "cell", split_axis=3, concat_axis=2, tiled=True)
    update = return_tiles(solve_in_lanes(tuple((line_coef[:, k] for k in range(5))), line_source))
    return state + update


LANES = 128
ROWS = 8
PAIRS = 3
CELL_ROWS = PAIRS * ROWS
RATE_ROW = 2 * CELL_ROWS
VMEM_BYTES = 8 * 2**20
BLOCK_ROWS = RATE_ROW + ROWS

SIDE_ROW = 3 * CELL_ROWS
CORRECTION_ROW = SIDE_ROW + 2 * CELL_ROWS
MIDDLE_ROWS = CORRECTION_ROW + 2 * ROWS
FIXED_ROWS = 3 * CELL_ROWS + 2 * ROWS


def spectral_offsets():
    table = np.zeros(NT)
    for offset in range(1, NT):
        angle = np.pi * offset / NT
        parity = -1.0 if offset % 2 == 0 else 1.0
        table[offset] = 0.5 * OMEGA_BLADE * parity * np.cos(angle) / np.sin(angle)
    return [float(np.float32(value)) for value in table]


def plane_masks():
    row_index = lax.broadcasted_iota(jnp.int32, (ROWS, LANES), 0)
    return row_index < 4, (row_index & 2) == 0, row_index & 1


def both(first_var, plane):
    turned = pltpu.roll(plane, 4, 0)
    return jnp.where(first_var, plane, turned), jnp.where(first_var, turned, plane)


def primitives(first_var, planes):
    density, moment_x = both(first_var, planes[0])
    moment_y, moment_z = both(first_var, planes[1])
    energy = jnp.where(first_var, planes[2], pltpu.roll(planes[2], 4, 0))
    inverse = 1.0 / density
    velocity_x = moment_x * inverse
    velocity_y = moment_y * inverse
    velocity_z = moment_z * inverse
    kinetic = moment_x * velocity_x + moment_y * velocity_y + moment_z * velocity_z
    pressure = (GAMMA_GAS - 1.0) * (energy - 0.5 * kinetic)
    sound = jnp.sqrt(GAMMA_GAS * pressure * inverse)
    return velocity_x, velocity_y, pressure, sound


def rows_of(var, inst, half):
    return (var // 2) * ROWS + (var % 2) * 4 + inst * 2 + half


def pack_kernel(
    held_state_ref, held_rate_ref, held_next_ref, held_codes_ref, out_ref, next_ref, codes_ref,
    state_ref, rate_ref, sems,
):
    copies = [
        pltpu.make_async_copy(source, target, sems.at[k])
        for k, (source, target) in enumerate(
            (
                (held_state_ref, state_ref),
                (held_rate_ref, rate_ref),
                (held_next_ref, next_ref),
                (held_codes_ref, codes_ref),
            )
        )
    ]
    for copy in copies:
        copy.start()
    for copy in copies:
        copy.wait()
    mirrored = lax.axis_index("cell") // (lax.axis_size("cell") // 2)
    for cell in range(2):
        place = pl.multiple_of(jnp.bitwise_xor(cell, mirrored) * CELL_ROWS, ROWS)
        for k in range(PAIRS):
            rows = [
                state_ref[inst, 2 * k + var, pl.ds(cell, 1), pl.ds(half * LANES, LANES)]
                for var in range(2)
                for inst in range(2)
                for half in range(2)
            ]
            for row, values in enumerate(rows):
                out_ref[0, pl.ds(place + (k * ROWS + row), 1), :] = values
    rates = [
        rate_ref[pl.ds(cell, 1), pl.ds(half * LANES, LANES)]
        for cell in range(2)
        for half in range(2)
    ]
    for row in range(4):
        out_ref[0, pl.ds(RATE_ROW + row, 1), :] = jnp.where(
            mirrored == 0, rates[row], rates[row ^ 2]
        )
    out_ref[0, pl.ds(RATE_ROW + 4, 4), :] = jnp.zeros((4, LANES), jnp.float32)
    for row in range(0, BLOCK_ROWS, ROWS):
        values = out_ref[0, pl.ds(row, ROWS), :]
        for copy in range(1, out_ref.shape[0]):
            out_ref[copy, pl.ds(row, ROWS), :] = values


def turn_insts(first_inst, plane):
    return jnp.where(first_inst, pltpu.roll(plane, 6, 0), pltpu.roll(plane, 2, 0))


def time_weights(first_inst, shift):
    offsets = spectral_offsets()
    other = jnp.where(
        first_inst, offsets[(2 * shift + 1) % NT], offsets[(2 * shift - 1) % NT]
    )
    return offsets[(2 * shift) % NT], other


def cell_rows(cell, k):
    return pl.ds((cell % 2) * CELL_ROWS + k * ROWS, ROWS)


def partner_kernel(all_ref, out_ref):
    own_inst = lax.axis_index("inst")
    own_y, core = own_inst >> 1, own_inst & 1
    _, first_inst, _ = plane_masks()
    one, three = time_weights(first_inst, 1), time_weights(first_inst, 3)
    near = [jnp.where(core == 0, a, b) for a, b in zip(one, three)]
    away = [jnp.where(core == 0, b, a) for a, b in zip(one, three)]
    for cell in range(2 * all_ref.shape[1]):
        for k in range(PAIRS):
            here = all_ref[own_y, cell // 2, cell_rows(cell, k), :]
            there = all_ref[1 - own_y, cell // 2, cell_rows(cell, k), :]
            out_ref[pl.ds(cell * CELL_ROWS + k * ROWS, ROWS), :] = (
                near[0] * here
                + away[0] * there
                + turn_insts(first_inst, near[1] * here + away[1] * there)
            )


def two_by_two(first, second):
    def entry(a, b, c, d):
        terms = [x * y for x, y in ((a, b), (c, d)) if x is not None and y is not None]
        return None if not terms else terms[0] if len(terms) == 1 else terms[0] + terms[1]

    return (
        entry(first[0], second[0], first[1], second[2]),
        entry(first[0], second[1], first[1], second[3]),
        entry(first[2], second[0], first[3], second[2]),
        entry(first[2], second[1], first[3], second[3]),
    )


def inverse_of(matrix):
    reciprocal = 1.0 / (matrix[0] * matrix[3] - matrix[1] * matrix[2])
    return (
        matrix[3] * reciprocal,
        -(matrix[1] * reciprocal),
        -(matrix[2] * reciprocal),
        matrix[0] * reciprocal,
    )


def less(first, second):
    return tuple(a if b is None else a - b for a, b in zip(first, second))


def minus(members):
    return tuple(None if a is None else -a for a in members)


def matrix_vector(matrix, low, high):
    def row(a, b):
        terms = [x * y for x, y in ((a, low), (b, high)) if x is not None]
        return terms[0] if len(terms) == 1 else terms[0] + terms[1]

    return row(matrix[0], matrix[1]), row(matrix[2], matrix[3])


def apply_matrix(matrix, side):
    parts = [matrix_vector(matrix, side[k], side[PAIRS + k]) for k in range(PAIRS)]
    return [low for low, _ in parts] + [high for _, high in parts]


def difference(first, second):
    return [a - b for a, b in zip(first, second)]


def flux_along(first_var, planes, velocity, pressure, sign):
    normal = sign * velocity
    return [
        planes[0] * normal + jnp.where(first_var, 0.0, sign * pressure),
        planes[1] * normal,
        planes[2] * normal + jnp.where(first_var, pressure * normal, 0.0),
    ]


class LineCells:
    def __init__(self, first_var, sign):
        self.first_var, self.sign = first_var, sign
        self.state, self.pressure, self.radius = {}, {}, {}
        self.flux, self.step, self.sensor = {}, {}, {}

    def add(self, cell, planes, velocity, pressure, sound):
        self.state[cell], self.pressure[cell] = planes, pressure
        self.radius[cell] = jnp.abs(velocity) + sound
        self.flux[cell] = flux_along(self.first_var, planes, velocity, pressure, self.sign)
        if cell - 1 in self.state:
            self.step[cell - 1] = difference(planes, self.state[cell - 1])
        if cell - 2 in self.state:
            twice = 2.0 * self.pressure[cell - 1]
            outer = pressure + self.pressure[cell - 2]
            self.sensor[cell - 1] = jnp.abs(outer - twice) / (outer + twice)

    def face(self, cell):
        second = SENSOR_GAIN * jnp.maximum(self.sensor[cell], self.sensor[cell + 1])
        fourth = jnp.maximum(0.0, FOURTH_GAIN - second)
        face_radius = 0.5 * (self.radius[cell] + self.radius[cell + 1])
        near_weight = face_radius * (second + 2.0 * fourth)
        far_weight = face_radius * fourth
        return [
            0.5 * (self.flux[cell][k] + self.flux[cell + 1][k])
            - (
                near_weight * self.step[cell][k]
                - far_weight * (self.step[cell + 1][k] + self.step[cell - 1][k])
            )
            for k in range(PAIRS)
        ]

    def near(self, cell):
        scale = SECOND_IMPL * 0.5 + 2.0 * FOURTH_IMPL
        return -scale * (self.radius[cell] + self.radius[cell + 1])

    def far(self, cell):
        return FOURTH_IMPL * self.radius[cell]

    def middle(self, cell, rate):
        centre, above = self.radius[cell], self.radius[cell + 1]
        if cell == 0:
            total, weighted = centre + (centre + above), 4.0 * centre + above
        else:
            below = self.radius[cell - 1]
            total = (below + centre) + (centre + above)
            weighted = below + 4.0 * centre + above
        result = SECOND_IMPL * (0.5 * total) + FOURTH_IMPL * weighted
        return result if rate is None else rate * centre + result

    def diagonal(self, cell, rates):
        across = self.near(cell)
        return (self.middle(cell, rates[0]), across, across, self.middle(cell + 1, rates[1]))

    def below(self, cell):
        return (self.far(cell - 1), self.near(cell - 1), None, self.far(cell))

    def above(self, cell):
        return (self.far(cell + 1), None, self.near(cell + 1), self.far(cell + 2))


def rates_at(ref, index, start, first_half):
    rows = [ref[index + (pl.ds(start + k, 1), slice(None))] for k in range(4)]
    return [jnp.where(first_half, rows[2 * k], rows[2 * k + 1]) for k in range(2)]


def half_kernel(
    all_ref, next_ref, codes_ref, partial_ref, factor_ref, blocks_ref, fixed_ref, line_ref,
):
    own_y = lax.axis_index("inst") >> 1
    blocks = all_ref.shape[1]
    cells = 2 * blocks
    mirrored = lax.axis_index("cell") // blocks
    sign = (1 - 2 * mirrored).astype(jnp.float32)
    shape = (ROWS, LANES)
    lane_index = lax.broadcasted_iota(jnp.int32, shape, 1)
    first_var, first_inst, half_index = plane_masks()
    first_half = half_index == 0
    zero = jnp.zeros(shape, jnp.float32)

    next_rows = [
        next_ref[pl.ds(half * LANES, LANES)].reshape(1, LANES) for half in range(2)
    ]
    next_line = jnp.where(first_half, next_rows[0], next_rows[1])
    column = lax.broadcasted_iota(jnp.int32, (LANES, LANES), 0)
    prev_halves = []
    for target in range(2):
        total = None
        for source in range(2):
            hits = jnp.where(column + target * LANES == next_rows[source], 1.0, 0.0)
            names = (lane_index + source * LANES).astype(jnp.float32)
            part = lax.dot_general(
                names, hits, (((1,), (1,)), ((), ())), preferred_element_type=jnp.float32
            )
            total = part if total is None else total + part
        prev_halves.append(total)
    prev_line = jnp.where(first_half, prev_halves[0], prev_halves[1]).astype(jnp.int32)

    def picker(lines):
        lane = lines & (LANES - 1)
        same = (lines >> 7) == half_index

        def pick(plane):
            swapped = jnp.where(first_half, pltpu.roll(plane, 7, 0), pltpu.roll(plane, 1, 0))
            here = jnp.take_along_axis(plane, lane, axis=1, mode="promise_in_bounds")
            there = jnp.take_along_axis(swapped, lane, axis=1, mode="promise_in_bounds")
            return jnp.where(same, here, there)

        return pick

    pick_next = picker(next_line)
    pick_prev = picker(prev_line)

    def loaded(cell, place=own_y):
        return [all_ref[place, cell // 2, cell_rows(cell, k), :] for k in range(PAIRS)]

    own_weights, away_weights = time_weights(first_inst, 0), time_weights(first_inst, 2)

    def own_time_parts(planes, cell):
        return [
            away_weights[0] * away
            + turn_insts(first_inst, own_weights[1] * own + away_weights[1] * away)
            for own, away in zip(planes, loaded(cell, 1 - own_y))
        ]

    def flux_across(planes, velocity, pressure):
        return [
            planes[0] * velocity,
            planes[1] * velocity + jnp.where(first_var, pressure, 0.0),
            planes[2] * velocity + jnp.where(first_var, pressure * velocity, 0.0),
        ]

    def pitch_flux(planes, velocity_y, pressure, sound):
        nearby = [pick_next(plane) for plane in planes]
        _, next_velocity, next_pressure, next_sound = primitives(first_var, nearby)
        own_flux = flux_across(planes, velocity_y, pressure)
        next_flux = flux_across(nearby, next_velocity, next_pressure)
        weight = (PITCH_GAIN * 0.5) * (
            jnp.abs(velocity_y) + sound + (jnp.abs(next_velocity) + next_sound)
        )
        return [
            0.5 * (a + b) - weight * (n - o)
            for a, b, n, o in zip(own_flux, next_flux, nearby, planes)
        ]

    for cell in range(cells):
        planes = loaded(cell)
        velocity_x, velocity_y, pressure, sound = primitives(first_var, planes)
        line_ref[cell, 0], line_ref[cell, 1], line_ref[cell, 2] = velocity_x, pressure, sound
        faces_across = pitch_flux(planes, velocity_y, pressure, sound)
        times = own_time_parts(planes, cell)
        for k in range(PAIRS):
            partial_ref[cell, k] = -(times[k] + (faces_across[k] - pick_prev(faces_across[k])))

    tile = half_index * (LANES // LINES_DEV) + lane_index // LINES_DEV
    end_codes = jnp.where(mirrored == 0, codes_ref[pl.ds(0, 1), :], codes_ref[pl.ds(1, 1), :])
    codes = jnp.zeros(shape, jnp.int32)
    for k in range(2 * LANES // LINES_DEV):
        codes = jnp.where(tile == k, jnp.broadcast_to(end_codes[:, k : k + 1], shape), codes)

    def ghost(cell):
        planes = loaded(-1 - cell)
        copied = loaded(0)
        result = []
        for k in range(PAIRS):
            reflected = planes[k] if k else jnp.where(first_var, planes[k], -planes[k])
            inflow = jnp.where(first_var, FREE_STATE[2 * k], FREE_STATE[2 * k + 1])
            result.append(
                jnp.where(codes == 0, reflected, jnp.where(codes == 1, inflow, copied[k]))
            )
        return result

    line = LineCells(first_var, sign)
    faces, inverses, aboves = {}, [], []
    for cell in range(-2, cells):
        if cell < 0:
            planes = ghost(cell)
            velocity_x, _, pressure, sound = primitives(first_var, planes)
        else:
            planes = loaded(cell)
            velocity_x, pressure, sound = [line_ref[cell, k] for k in range(3)]
        line.add(cell, planes, velocity_x, pressure, sound)
        if cell >= 1:
            faces[cell - 2] = line.face(cell - 2)
        if cell >= 2:
            at = cell - 2
            for k in range(PAIRS):
                partial_ref[at, k] = partial_ref[at, k] + (faces[at - 1][k] - faces[at][k])
        if cell >= 3 and cell % 2 == 1:
            at = cell - 3
            block = at // 2
            rates = rates_at(all_ref, (own_y, block), RATE_ROW, first_half)
            diag = line.diagonal(at, rates)
            if block > 0:
                factor = two_by_two(line.below(at), inverses[-1])
                diag = less(diag, two_by_two(factor, aboves[-1]))
                for n in range(4):
                    factor_ref[block - 1, n] = factor[n]
            inverses.append(inverse_of(diag))
            aboves.append(line.above(at))
            kept = [*inverses[-1], aboves[-1][0], *aboves[-1][2:]]
            for n, plane in enumerate(kept):
                blocks_ref[block, n] = plane

    last = cells - 2
    for k in range(PAIRS):
        partial_ref[last, k] = partial_ref[last, k] + faces[last - 1][k]
    factor = two_by_two(line.below(last), inverses[-1])
    for n in range(4):
        factor_ref[blocks - 2, n] = factor[n]
    correction = list(two_by_two(factor, aboves[-1]))
    rates = rates_at(all_ref, (own_y, blocks - 1), RATE_ROW, first_half)
    for member in range(2):
        centre = line.radius[last + member]
        correction[3 * member] = correction[3 * member] - rates[member] * centre
    for n in range(3):
        for k, plane in enumerate(line.state[cells - 3 + n]):
            fixed_ref[pl.ds(n * CELL_ROWS + k * ROWS, ROWS), :] = plane
    for n in range(2):
        fixed_ref[pl.ds(SIDE_ROW + n * ROWS, ROWS), :] = jnp.where(
            first_var, correction[2 * n], correction[2 * n + 1]
        )


def reduce_kernel(partial_ref, time_ref, factor_ref, fixed_ref, middle_ref, sides_ref):
    blocks = partial_ref.shape[0] // 2
    side = None
    for block in range(blocks):
        own = []
        for cell in (2 * block, 2 * block + 1):
            for k in range(PAIRS):
                time = time_ref[pl.ds(cell * CELL_ROWS + k * ROWS, ROWS), :]
                own.append(partial_ref[cell, k] - time)
        if block > 0:
            factor = [factor_ref[block - 1, n] for n in range(4)]
            own = difference(own, apply_matrix(factor, side))
        side = own
        for n, plane in enumerate(side):
            if block < blocks - 1:
                sides_ref[block, n] = plane
            else:
                middle_ref[pl.ds(SIDE_ROW + n * ROWS, ROWS), :] = plane
    for row in range(0, SIDE_ROW, ROWS):
        middle_ref[pl.ds(row, ROWS), :] = fixed_ref[pl.ds(row, ROWS), :]
    for n in range(2):
        rows = fixed_ref[pl.ds(SIDE_ROW + n * ROWS, ROWS), :]
        middle_ref[pl.ds(CORRECTION_ROW + n * ROWS, ROWS), :] = rows


def spread_kernel(all_ref, blocks_ref, sides_ref, known_ref, spread_ref, table_ref):
    own_y = lax.axis_index("inst") >> 1
    blocks = all_ref.shape[1]
    own_cell = lax.axis_index("cell")
    own_block = jnp.where(own_cell < blocks, own_cell, 2 * blocks - 1 - own_cell)
    zero = jnp.zeros((ROWS, LANES), jnp.float32)
    known, spread = [zero] * (2 * PAIRS), (zero + 1.0, zero, zero, zero + 1.0)
    for block in range(blocks - 1, -1, -1):
        if block < blocks - 1:
            kept = [blocks_ref[block, n] for n in range(7)]
            inverse, above = kept[:4], (kept[4], None, kept[5], kept[6])
            side = [sides_ref[block, n] for n in range(2 * PAIRS)]
            step = two_by_two(inverse, above)
            own = apply_matrix(inverse, side)
            if block < blocks - 2:
                known = difference(own, apply_matrix(step, known))
                spread = minus(two_by_two(step, spread))
            else:
                known, spread = own, minus(step)
        for n, plane in enumerate(known + list(spread)):
            table_ref[block, n] = plane
    for n in range(2 * PAIRS):
        base = all_ref[own_y, own_block, pl.ds(n * ROWS, ROWS), :]
        known_ref[n] = base + table_ref[own_block, n]
    for n in range(4):
        spread_ref[n] = table_ref[own_block, 2 * PAIRS + n]


def join_kernel(here_ref, there_ref, known_ref, spread_ref, out_ref):
    mirrored = lax.axis_index("cell") // (lax.axis_size("cell") // 2)
    sign = (1 - 2 * mirrored).astype(jnp.float32)
    first_var, _, _ = plane_masks()

    def plane_of(ref, row):
        return ref[pl.ds(row, ROWS), :]

    line = LineCells(first_var, sign)
    for cell in range(6):
        ref, at = (here_ref, cell) if cell < 3 else (there_ref, 5 - cell)
        planes = [plane_of(ref, at * CELL_ROWS + k * ROWS) for k in range(PAIRS)]
        velocity_x, _, pressure, sound = primitives(first_var, planes)
        line.add(cell, planes, velocity_x, pressure, sound)
    faces = {cell: line.face(cell) for cell in (1, 2, 3)}

    def correction_of(ref):
        pairs = [both(first_var, plane_of(ref, CORRECTION_ROW + n * ROWS)) for n in range(2)]
        return [pairs[0][0], pairs[0][1], pairs[1][0], pairs[1][1]]

    here_side = [plane_of(here_ref, SIDE_ROW + n * ROWS) for n in range(2 * PAIRS)]
    there_side = [plane_of(there_ref, SIDE_ROW + n * ROWS) for n in range(2 * PAIRS)]
    side = [here_side[k] - faces[1][k] for k in range(PAIRS)]
    side += [here_side[PAIRS + k] + (faces[1][k] - faces[2][k]) for k in range(PAIRS)]
    other = [there_side[PAIRS + k] + (faces[2][k] - faces[3][k]) for k in range(PAIRS)]
    other += [there_side[k] + faces[3][k] for k in range(PAIRS)]
    no_rates = (None, None)
    diag = difference(line.diagonal(1, no_rates), correction_of(here_ref))
    other_diag = difference(line.diagonal(3, no_rates), correction_of(there_ref)[::-1])
    factor = two_by_two(line.above(1), inverse_of(other_diag))
    diag = less(diag, two_by_two(factor, line.below(3)))
    middle = apply_matrix(inverse_of(diag), difference(side, apply_matrix(factor, other)))
    moved = apply_matrix([spread_ref[n] for n in range(4)], middle)
    results = [known_ref[n] + moved[n] for n in range(2 * PAIRS)]
    for cell in range(2):
        for k in range(PAIRS):
            first, second = results[cell * PAIRS + k], results[(1 - cell) * PAIRS + k]
            result = jnp.where(mirrored == 0, first, second)
            for var in range(2):
                for inst in range(2):
                    for half in range(2):
                        row = rows_of(var, inst, half)
                        out_ref[
                            inst, 2 * k + var, pl.ds(cell, 1), pl.ds(half * LANES, LANES)
                        ] = result[row : row + 1]


def share_half(copies):
    insts, count = lax.axis_size("inst"), lax.axis_size("cell")
    halves = [range(count // 2), range(count - 1, count // 2 - 1, -1)]
    groups = [
        [inst * count + cell for inst in range(core, insts, 2) for cell in half]
        for core in range(2)
        for half in halves
    ]
    return lax.all_to_all(
        copies, ("inst", "cell"), split_axis=0, concat_axis=0, tiled=True,
        axis_index_groups=groups,
    )


def swap_cores(block):
    pairs = [(inst, inst ^ 1) for inst in range(lax.axis_size("inst"))]
    return lax.ppermute(block, "inst", pairs)


def swap_halves(block):
    count = lax.axis_size("cell")
    return lax.ppermute(block, "cell", [(i, (i + count // 2) % count) for i in range(count)])


def float_shape(*sizes):
    return jax.ShapeDtypeStruct(sizes, jnp.float32)


def local_by_halves(state, pseudo_rate, line_next, face_codes):
    blocks = lax.axis_size("cell") // 2
    cells = 2 * blocks
    vmem = pl.BlockSpec(memory_space=pltpu.VMEM)
    plane = (ROWS, LANES)
    params = pltpu.CompilerParams(vmem_limit_bytes=VMEM_BYTES)
    places = lax.axis_size("inst") // 2
    held = [
        pltpu.with_memory_space_constraint(array, pltpu.HBM)
        for array in (state, pseudo_rate, line_next, face_codes)
    ]
    packed, next_here, codes_here = pl.pallas_call(
        pack_kernel,
        out_shape=(
            float_shape(places * blocks, BLOCK_ROWS, LANES),
            jax.ShapeDtypeStruct(line_next.shape, jnp.int32),
            jax.ShapeDtypeStruct(face_codes.shape, jnp.int32),
        ),
        in_specs=[pl.BlockSpec(memory_space=pltpu.HBM)] * 4,
        out_specs=(vmem, vmem, vmem),
        scratch_shapes=[
            pltpu.VMEM(state.shape, jnp.float32),
            pltpu.VMEM(pseudo_rate.shape, jnp.float32),
            pltpu.SemaphoreType.DMA((4,)),
        ],
        compiler_params=params,
    )(*held)
    shared = share_half(packed).reshape(places, blocks, BLOCK_ROWS, LANES)
    for_partner = pl.pallas_call(
        partner_kernel,
        out_shape=float_shape(cells * CELL_ROWS, LANES),
        in_specs=[vmem],
        out_specs=vmem,
        compiler_params=params,
    )(shared)
    from_partner = swap_cores(for_partner)
    beside = pl.CostEstimate(flops=10**6, bytes_accessed=10**6, transcendentals=0)
    partial, factors, eliminated, fixed = pl.pallas_call(
        half_kernel,
        out_shape=(
            float_shape(cells, PAIRS, *plane),
            float_shape(blocks - 1, 4, *plane),
            float_shape(blocks - 1, 7, *plane),
            float_shape(FIXED_ROWS, LANES),
        ),
        in_specs=[vmem] * 3,
        out_specs=(vmem,) * 4,
        scratch_shapes=[pltpu.VMEM((cells, 3) + plane, jnp.float32)],
        compiler_params=params,
        cost_estimate=beside,
    )(shared, next_here, codes_here)
    here, sides = pl.pallas_call(
        reduce_kernel,
        out_shape=(
            float_shape(MIDDLE_ROWS, LANES),
            float_shape(blocks - 1, 2 * PAIRS, *plane),
        ),
        in_specs=[vmem] * 4,
        out_specs=(vmem, vmem),
        compiler_params=params,
    )(partial, from_partner, factors, fixed)
    there = swap_halves(here)
    known, spread = pl.pallas_call(
        spread_kernel,
        out_shape=(float_shape(2 * PAIRS, *plane), float_shape(4, *plane)),
        in_specs=[vmem] * 3,
        out_specs=(vmem, vmem),
        scratch_shapes=[pltpu.VMEM((blocks, 2 * PAIRS + 4) + plane, jnp.float32)],
        compiler_params=params,
        cost_estimate=beside,
    )(shared, eliminated, sides)
    return pl.pallas_call(
        join_kernel,
        out_shape=float_shape(*state.shape),
        in_specs=[vmem] * 4,
        out_specs=vmem,
        compiler_params=params,
    )(here, there, known, spread)


def solution(mesh):
    placed = (P("inst", None, "cell", None), P("cell", None), P(), P())
    inst_count, cell_count = mesh.shape["inst"], mesh.shape["cell"]

    def local(state, pseudo_rate, line_next, face_codes):
        small = (
            state.shape == (2, 6, 2, 2 * LANES)
            and inst_count * 2 == NT
            and cell_count == 8
            and face_codes.shape[1] * LINES_DEV == state.shape[3]
        )
        chosen = local_by_halves if small else local_by_lines
        return chosen(state, pseudo_rate, line_next, face_codes)

    return jax.shard_map(
        local, mesh=mesh, in_specs=placed, out_specs=P("inst", None, "cell", None), check_vma=False
    )
```

```python
import functools

import jax
import jax.numpy as jnp
import numpy as np
from jax import lax
from jax.experimental import pallas as pl
from jax.experimental.pallas import tpu as pltpu
from jax.sharding import PartitionSpec as P

NT = 8
LINES_DEV = 32


GAMMA_GAS = 1.4
OMEGA_BLADE = 1.0
SENSOR_GAIN = 0.25
FOURTH_GAIN = 0.03125
PITCH_GAIN = 0.5
SECOND_IMPL = 1.0
FOURTH_IMPL = 0.25
FREE_STATE = (1.0, 0.5, 0.0, 0.0, 2.625, 0.2)
MIRROR_SIGNS = (1.0, -1.0, 1.0, 1.0, 1.0, 1.0)
ZERO_BLOCK = (0.0, 0.0, 0.0, 0.0)
UNIT_BLOCK = (1.0, 0.0, 0.0, 1.0)
ZERO_PAIR = (0.0, 0.0)


def extended(block, sides, width):
    for axis, dim in sides:
        count = lax.axis_size(axis)
        forward = [(i, i + 1) for i in range(count - 1)]
        backward = [(target, source) for source, target in forward]
        low = lax.ppermute(
            lax.slice_in_dim(block, block.shape[dim] - width, None, axis=dim), axis, forward
        )
        high = lax.ppermute(lax.slice_in_dim(block, 0, width, axis=dim), axis, backward)
        block = jnp.concatenate([low, block, high], axis=dim)
    return block


def spectral_matrix(instances):
    offsets = np.arange(instances)[:, None] - np.arange(instances)[None, :]
    angles = np.pi * offsets / instances
    safe_sin = np.where(offsets == 0, 1.0, np.sin(angles))
    parity = np.where(np.mod(offsets, 2) == 0, -1.0, 1.0)
    matrix_table = np.where(
        offsets == 0, 0.0, 0.5 * OMEGA_BLADE * parity * np.cos(angles) / safe_sin
    )
    return jnp.asarray(matrix_table, jnp.float32)


def primitive_parts(cells_state):
    density = cells_state[..., 0, :, :]
    inverse = 1.0 / density
    velocity_x = cells_state[..., 1, :, :] * inverse
    velocity_y = cells_state[..., 2, :, :] * inverse
    velocity_z = cells_state[..., 3, :, :] * inverse
    energy = cells_state[..., 4, :, :]
    pressure = (GAMMA_GAS - 1.0) * (
        energy
        - 0.5
        * density
        * (velocity_x * velocity_x + velocity_y * velocity_y + velocity_z * velocity_z)
    )
    sound_speed = jnp.sqrt(GAMMA_GAS * pressure * inverse)
    return (velocity_x, velocity_y, pressure, sound_speed)


def directed_flux(cells_state, normal_velocity, pressure, component):
    zero_plane = jnp.zeros_like(pressure)
    pressure_rows = [
        zero_plane,
        zero_plane,
        zero_plane,
        zero_plane,
        pressure * normal_velocity,
        zero_plane,
    ]
    pressure_rows[component] = pressure
    return cells_state * normal_velocity[..., None, :, :] + jnp.stack(pressure_rows, axis=-3)


def line_residual(padded):
    velocity_x, velocity_y, pressure, sound_speed = primitive_parts(padded)
    flux_line = directed_flux(padded, velocity_x, pressure, 1)
    radius = jnp.abs(velocity_x) + sound_speed
    sensor = jnp.abs(
        pressure[..., 2:, :] - 2.0 * pressure[..., 1:-1, :] + pressure[..., :-2, :]
    ) / (pressure[..., 2:, :] + 2.0 * pressure[..., 1:-1, :] + pressure[..., :-2, :])
    second = SENSOR_GAIN * jnp.maximum(sensor[..., :-1, :], sensor[..., 1:, :])
    fourth = jnp.maximum(0.0, FOURTH_GAIN - second)
    face_radius = 0.5 * (radius[..., 1:-2, :] + radius[..., 2:-1, :])
    left_far = padded[..., :-3, :]
    left_near = padded[..., 1:-2, :]
    right_near = padded[..., 2:-1, :]
    right_far = padded[..., 3:, :]
    damping = face_radius[..., None, :, :] * (
        second[..., None, :, :] * (right_near - left_near)
        - fourth[..., None, :, :] * (right_far - 3.0 * right_near + 3.0 * left_near - left_far)
    )
    face_flux = 0.5 * (flux_line[..., 1:-2, :] + flux_line[..., 2:-1, :]) - damping
    return (face_flux[..., 1:, :] - face_flux[..., :-1, :], radius)


def pitch_parts(cells_state):
    velocity_x, velocity_y, pressure, sound_speed = primitive_parts(cells_state)
    return (directed_flux(cells_state, velocity_y, pressure, 2), jnp.abs(velocity_y) + sound_speed)


def pitch_residual(cells_state, next_lines, prev_lines):
    pitch_flux, radius = pitch_parts(cells_state)
    state_next = jnp.take(cells_state, next_lines, axis=-1)
    flux_next, radius_next = pitch_parts(state_next)
    face_flux = 0.5 * (pitch_flux + flux_next) - PITCH_GAIN * (0.5 * (radius + radius_next))[
        ..., None, :, :
    ] * (state_next - cells_state)
    return face_flux - jnp.take(face_flux, prev_lines, axis=-1)


def boundary_cells(edge_pair, line_codes, lower_end):
    reflected = edge_pair[..., ::-1, :] * jnp.asarray(MIRROR_SIGNS, jnp.float32)[:, None, None]
    if lower_end:
        copied = jnp.concatenate([edge_pair[..., :1, :], edge_pair[..., :1, :]], axis=-2)
    else:
        copied = jnp.concatenate([edge_pair[..., 1:, :], edge_pair[..., 1:, :]], axis=-2)
    inflow = jnp.asarray(FREE_STATE, jnp.float32)[:, None, None] + jnp.zeros_like(edge_pair)
    return jnp.where(line_codes == 0, reflected, jnp.where(line_codes == 1, inflow, copied))


def line_coefficients(radius_ext, diagonal_term, positions, total_cells):
    radius_below = radius_ext[..., :-2, :]
    radius_centre = radius_ext[..., 1:-1, :]
    radius_above = radius_ext[..., 2:, :]
    face_below = 0.5 * (radius_below + radius_centre)
    face_above = 0.5 * (radius_centre + radius_above)
    far_low = FOURTH_IMPL * radius_below
    near_low = -SECOND_IMPL * face_below - 2.0 * FOURTH_IMPL * (radius_below + radius_centre)
    middle = (
        diagonal_term
        + SECOND_IMPL * (face_below + face_above)
        + FOURTH_IMPL * (radius_below + 4.0 * radius_centre + radius_above)
    )
    near_high = -SECOND_IMPL * face_above - 2.0 * FOURTH_IMPL * (radius_centre + radius_above)
    far_high = FOURTH_IMPL * radius_above
    column = positions[:, None]
    far_low = jnp.where(column >= 2, far_low, 0.0)
    near_low = jnp.where(column >= 1, near_low, 0.0)
    near_high = jnp.where(column <= total_cells - 2, near_high, 0.0)
    far_high = jnp.where(column <= total_cells - 3, far_high, 0.0)
    return (far_low, near_low, middle, near_high, far_high)


def block_product(first_matrix, second_matrix):
    return (
        first_matrix[0] * second_matrix[0] + first_matrix[1] * second_matrix[2],
        first_matrix[0] * second_matrix[1] + first_matrix[1] * second_matrix[3],
        first_matrix[2] * second_matrix[0] + first_matrix[3] * second_matrix[2],
        first_matrix[2] * second_matrix[1] + first_matrix[3] * second_matrix[3],
    )


def block_inverse(matrix):
    determinant = matrix[0] * matrix[3] - matrix[1] * matrix[2]
    reciprocal = 1.0 / determinant
    return (
        matrix[3] * reciprocal,
        -matrix[1] * reciprocal,
        -matrix[2] * reciprocal,
        matrix[0] * reciprocal,
    )


def block_apply(matrix, vector):
    return (
        matrix[0] * vector[0] + matrix[1] * vector[1],
        matrix[2] * vector[0] + matrix[3] * vector[1],
    )


def add_blocks(first_members, second_members):
    return tuple((a + b for a, b in zip(first_members, second_members)))


def negate(members):
    return tuple((-a for a in members))


def extend_blocks(members, fill_values):
    return tuple(
        (
            jnp.concatenate([m, jnp.full_like(m[..., :1, :], f)], axis=-2)
            for m, f in zip(members, fill_values)
        )
    )


def shift_next(members, fill_values):
    return tuple(
        (
            jnp.concatenate([m[..., 1:, :], jnp.full_like(m[..., :1, :], f)], axis=-2)
            for m, f in zip(members, fill_values)
        )
    )


def shift_prev(members):
    return tuple(
        (jnp.concatenate([jnp.zeros_like(m[..., :1, :]), m[..., :-1, :]], axis=-2) for m in members)
    )


def pair_split(member):
    shaped = member.reshape(member.shape[:-2] + (member.shape[-2] // 2, 2, member.shape[-1]))
    return (shaped[..., 0, :], shaped[..., 1, :])


def split_parity(members):
    halves = [pair_split(m) for m in members]
    return (tuple((h[0] for h in halves)), tuple((h[1] for h in halves)))


def alternate(first_member, second_member):
    stacked = jnp.stack((first_member, second_member), axis=-2)
    return stacked.reshape(
        first_member.shape[:-2] + (2 * first_member.shape[-2], first_member.shape[-1])
    )


def reduce_blocks(sub_blocks, diag_blocks, super_blocks, right_side):
    block_count = diag_blocks[0].shape[-2]
    if block_count == 1:
        return block_apply(block_inverse(diag_blocks), right_side)
    if block_count % 2 == 1:
        sub_blocks = extend_blocks(sub_blocks, ZERO_BLOCK)
        diag_blocks = extend_blocks(diag_blocks, UNIT_BLOCK)
        super_blocks = extend_blocks(super_blocks, ZERO_BLOCK)
        right_side = extend_blocks(right_side, ZERO_PAIR)
    sub_even, sub_odd = split_parity(sub_blocks)
    diag_even, diag_odd = split_parity(diag_blocks)
    super_even, super_odd = split_parity(super_blocks)
    side_even, side_odd = split_parity(right_side)
    inverse_even = block_inverse(diag_even)
    inverse_next = shift_next(inverse_even, UNIT_BLOCK)
    sub_next = shift_next(sub_even, ZERO_BLOCK)
    super_next = shift_next(super_even, ZERO_BLOCK)
    side_next = shift_next(side_even, ZERO_PAIR)
    left_factor = negate(block_product(sub_odd, inverse_even))
    right_factor = negate(block_product(super_odd, inverse_next))
    reduced_sub = block_product(left_factor, sub_even)
    reduced_diag = add_blocks(
        diag_odd,
        add_blocks(block_product(left_factor, super_even), block_product(right_factor, sub_next)),
    )
    reduced_super = block_product(right_factor, super_next)
    reduced_side = add_blocks(
        side_odd,
        add_blocks(block_apply(left_factor, side_even), block_apply(right_factor, side_next)),
    )
    odd_values = reduce_blocks(reduced_sub, reduced_diag, reduced_super, reduced_side)
    before_values = shift_prev(odd_values)
    remainder = add_blocks(
        side_even,
        negate(
            add_blocks(block_apply(sub_even, before_values), block_apply(super_even, odd_values))
        ),
    )
    even_values = block_apply(inverse_even, remainder)
    merged = tuple((alternate(e, o) for e, o in zip(even_values, odd_values)))
    return tuple((m[..., :block_count, :] for m in merged))


def cells_leading(block):
    moved = jnp.transpose(block, (2, 0, 1, 3))
    return moved.reshape(block.shape[2], block.shape[0] * block.shape[1] * block.shape[3])


def solve_in_lanes(coefficients, line_source):
    source_shape = line_source.shape
    lane_coef = [cells_leading(jnp.broadcast_to(c[:, None], source_shape)) for c in coefficients]
    pairs_list = [pair_split(m) for m in lane_coef]
    zero_plane = jnp.zeros_like(pairs_list[2][0])
    sub_blocks = (pairs_list[0][0], pairs_list[1][0], zero_plane, pairs_list[0][1])
    diag_blocks = (pairs_list[2][0], pairs_list[3][0], pairs_list[1][1], pairs_list[2][1])
    super_blocks = (pairs_list[4][0], zero_plane, pairs_list[3][1], pairs_list[4][1])
    values = reduce_blocks(
        sub_blocks, diag_blocks, super_blocks, pair_split(cells_leading(line_source))
    )
    flat = alternate(values[0], values[1])
    shaped = flat.reshape(source_shape[2], source_shape[0], source_shape[1], source_shape[3])
    return jnp.transpose(shaped, (1, 2, 0, 3))


def return_tiles(line_values):
    return lax.all_to_all(line_values, "cell", split_axis=2, concat_axis=3, tiled=True)


def local_by_lines(state, pseudo_rate, line_next, face_codes):
    local_count = state.shape[0]
    tile_cells = state.shape[2]
    cell_index = lax.axis_index("cell")
    cell_count = lax.axis_size("cell")
    total_cells = tile_cells * cell_count
    spectral = spectral_matrix(NT)
    first_local = lax.axis_index("inst") * local_count
    own_rows = lax.dynamic_slice_in_dim(spectral, first_local, local_count, 0)
    shard_block = jax.tree.map(lambda a: lax.all_gather(a, "inst", axis=0, tiled=True), state)
    columns = lax.slice_in_dim(own_rows, 0, shard_block.shape[0], axis=1)
    time_term = jnp.zeros_like(state) + jnp.einsum(
        "nm,mvil->nvil", columns, shard_block, precision=lax.Precision.HIGHEST
    )
    padded = extended(state, (("cell", 2),), 2)
    codes_lines = jnp.repeat(face_codes, LINES_DEV, axis=1)
    lower_ghost = boundary_cells(state[:, :, 0:2, :], codes_lines[0], True)
    upper_ghost = boundary_cells(state[:, :, -2:, :], codes_lines[1], False)
    lower_rim = jnp.where(cell_index == 0, lower_ghost, padded[:, :, :2, :])
    upper_rim = jnp.where(cell_index == cell_count - 1, upper_ghost, padded[:, :, -2:, :])
    padded = jnp.concatenate([lower_rim, padded[:, :, 2:-2, :], upper_rim], axis=2)
    line_part, radius = line_residual(padded)
    prev_lines = (
        jnp.zeros_like(line_next).at[line_next].set(jnp.arange(line_next.shape[0], dtype=jnp.int32))
    )
    residual = line_part + pitch_residual(state, line_next, prev_lines) + time_term
    right_side = -residual
    centre_radius = radius[:, 2:-2, :]
    diagonal_term = pseudo_rate * centre_radius
    positions = cell_index * tile_cells + jnp.arange(-1, tile_cells + 1, dtype=jnp.int32)
    inside = (positions >= 0) & (positions < total_cells)
    radius_ext = jnp.where(inside[:, None], radius[:, 1:-1, :], 0.0)
    coefficients = line_coefficients(radius_ext, diagonal_term, positions[1:-1], total_cells)
    stacked = jnp.stack(coefficients, axis=1)
    line_source = lax.all_to_all(right_side, "cell", split_axis=3, concat_axis=2, tiled=True)
    line_coef = lax.all_to_all(stacked, "cell", split_axis=3, concat_axis=2, tiled=True)
    update = return_tiles(solve_in_lanes(tuple((line_coef[:, k] for k in range(5))), line_source))
    return state + update


LANES = 128
ROWS = 8
PAIRS = 3
CELL_ROWS = PAIRS * ROWS
RATE_ROW = 2 * CELL_ROWS
VMEM_BYTES = 8 * 2**20
BLOCK_ROWS = RATE_ROW + ROWS

CORRECTION_ROW = 3 * CELL_ROWS
FIXED_ROWS = CORRECTION_ROW + 2 * ROWS


def spectral_offsets():
    table = np.zeros(NT)
    for offset in range(1, NT):
        angle = np.pi * offset / NT
        parity = -1.0 if offset % 2 == 0 else 1.0
        table[offset] = 0.5 * OMEGA_BLADE * parity * np.cos(angle) / np.sin(angle)
    return [float(np.float32(value)) for value in table]


def plane_masks():
    row_index = lax.broadcasted_iota(jnp.int32, (ROWS, LANES), 0)
    return row_index < 4, (row_index & 2) == 0, row_index & 1


def both(first_var, plane):
    turned = pltpu.roll(plane, 4, 0)
    return jnp.where(first_var, plane, turned), jnp.where(first_var, turned, plane)


def primitives(first_var, planes):
    density, moment_x = both(first_var, planes[0])
    moment_y, moment_z = both(first_var, planes[1])
    energy = jnp.where(first_var, planes[2], pltpu.roll(planes[2], 4, 0))
    inverse = 1.0 / density
    velocity_x = moment_x * inverse
    velocity_y = moment_y * inverse
    velocity_z = moment_z * inverse
    kinetic = moment_x * velocity_x + moment_y * velocity_y + moment_z * velocity_z
    pressure = (GAMMA_GAS - 1.0) * (energy - 0.5 * kinetic)
    sound = jnp.sqrt(GAMMA_GAS * pressure * inverse)
    return velocity_x, velocity_y, pressure, sound


def rows_of(var, inst, half):
    return (var // 2) * ROWS + (var % 2) * 4 + inst * 2 + half


def pack_kernel(
    held_state_ref, held_rate_ref, held_next_ref, held_codes_ref, out_ref, next_ref, codes_ref,
    state_ref, rate_ref, sems,
):
    copies = [
        pltpu.make_async_copy(source, target, sems.at[k])
        for k, (source, target) in enumerate(
            (
                (held_state_ref, state_ref),
                (held_rate_ref, rate_ref),
                (held_next_ref, next_ref),
                (held_codes_ref, codes_ref),
            )
        )
    ]
    for copy in copies:
        copy.start()
    for copy in copies:
        copy.wait()
    mirrored = lax.axis_index("cell") // (lax.axis_size("cell") // 2)
    for cell in range(2):
        place = pl.multiple_of(jnp.bitwise_xor(cell, mirrored) * CELL_ROWS, ROWS)
        for k in range(PAIRS):
            rows = [
                state_ref[inst, 2 * k + var, pl.ds(cell, 1), pl.ds(half * LANES, LANES)]
                for var in range(2)
                for inst in range(2)
                for half in range(2)
            ]
            for row, values in enumerate(rows):
                out_ref[0, pl.ds(place + (k * ROWS + row), 1), :] = values
    rates = [
        rate_ref[pl.ds(cell, 1), pl.ds(half * LANES, LANES)]
        for cell in range(2)
        for half in range(2)
    ]
    for row in range(4):
        out_ref[0, pl.ds(RATE_ROW + row, 1), :] = jnp.where(
            mirrored == 0, rates[row], rates[row ^ 2]
        )
    out_ref[0, pl.ds(RATE_ROW + 4, 4), :] = jnp.zeros((4, LANES), jnp.float32)
    for row in range(0, BLOCK_ROWS, ROWS):
        values = out_ref[0, pl.ds(row, ROWS), :]
        for copy in range(1, out_ref.shape[0]):
            out_ref[copy, pl.ds(row, ROWS), :] = values


def turn_insts(first_inst, plane):
    return jnp.where(first_inst, pltpu.roll(plane, 6, 0), pltpu.roll(plane, 2, 0))


def time_weights(first_inst, shift):
    offsets = spectral_offsets()
    other = jnp.where(
        first_inst, offsets[(2 * shift + 1) % NT], offsets[(2 * shift - 1) % NT]
    )
    return offsets[(2 * shift) % NT], other


def cell_rows(cell, k):
    return pl.ds((cell % 2) * CELL_ROWS + k * ROWS, ROWS)


def partner_kernel(all_ref, out_ref):
    own_inst = lax.axis_index("inst")
    own_y, core = own_inst >> 1, own_inst & 1
    _, first_inst, _ = plane_masks()
    one, three = time_weights(first_inst, 1), time_weights(first_inst, 3)
    near = [jnp.where(core == 0, a, b) for a, b in zip(one, three)]
    away = [jnp.where(core == 0, b, a) for a, b in zip(one, three)]
    for cell in range(2 * all_ref.shape[1]):
        for k in range(PAIRS):
            here = all_ref[own_y, cell // 2, cell_rows(cell, k), :]
            there = all_ref[1 - own_y, cell // 2, cell_rows(cell, k), :]
            out_ref[pl.ds(cell * CELL_ROWS + k * ROWS, ROWS), :] = (
                near[0] * here
                + away[0] * there
                + turn_insts(first_inst, near[1] * here + away[1] * there)
            )


def two_by_two(first, second):
    def entry(a, b, c, d):
        terms = [x * y for x, y in ((a, b), (c, d)) if x is not None and y is not None]
        return None if not terms else terms[0] if len(terms) == 1 else terms[0] + terms[1]

    return (
        entry(first[0], second[0], first[1], second[2]),
        entry(first[0], second[1], first[1], second[3]),
        entry(first[2], second[0], first[3], second[2]),
        entry(first[2], second[1], first[3], second[3]),
    )


def inverse_of(matrix):
    reciprocal = 1.0 / (matrix[0] * matrix[3] - matrix[1] * matrix[2])
    return (
        matrix[3] * reciprocal,
        -(matrix[1] * reciprocal),
        -(matrix[2] * reciprocal),
        matrix[0] * reciprocal,
    )


def less(first, second):
    return tuple(a if b is None else a - b for a, b in zip(first, second))


def minus(members):
    return tuple(None if a is None else -a for a in members)


def matrix_vector(matrix, low, high):
    def row(a, b):
        terms = [x * y for x, y in ((a, low), (b, high)) if x is not None]
        return terms[0] if len(terms) == 1 else terms[0] + terms[1]

    return row(matrix[0], matrix[1]), row(matrix[2], matrix[3])


def apply_matrix(matrix, side):
    parts = [matrix_vector(matrix, side[k], side[PAIRS + k]) for k in range(PAIRS)]
    return [low for low, _ in parts] + [high for _, high in parts]


def difference(first, second):
    return [a - b for a, b in zip(first, second)]


def flux_along(first_var, planes, velocity, pressure, sign):
    normal = sign * velocity
    return [
        planes[0] * normal + jnp.where(first_var, 0.0, sign * pressure),
        planes[1] * normal,
        planes[2] * normal + jnp.where(first_var, pressure * normal, 0.0),
    ]


class LineCells:
    def __init__(self, first_var, sign):
        self.first_var, self.sign = first_var, sign
        self.state, self.pressure, self.radius = {}, {}, {}
        self.flux, self.step, self.sensor = {}, {}, {}

    def add(self, cell, planes, velocity, pressure, sound):
        self.state[cell], self.pressure[cell] = planes, pressure
        self.radius[cell] = jnp.abs(velocity) + sound
        self.flux[cell] = flux_along(self.first_var, planes, velocity, pressure, self.sign)
        if cell - 1 in self.state:
            self.step[cell - 1] = difference(planes, self.state[cell - 1])
        if cell - 2 in self.state:
            twice = 2.0 * self.pressure[cell - 1]
            outer = pressure + self.pressure[cell - 2]
            self.sensor[cell - 1] = jnp.abs(outer - twice) / (outer + twice)

    def face(self, cell):
        second = SENSOR_GAIN * jnp.maximum(self.sensor[cell], self.sensor[cell + 1])
        fourth = jnp.maximum(0.0, FOURTH_GAIN - second)
        face_radius = 0.5 * (self.radius[cell] + self.radius[cell + 1])
        near_weight = face_radius * (second + 2.0 * fourth)
        far_weight = face_radius * fourth
        return [
            0.5 * (self.flux[cell][k] + self.flux[cell + 1][k])
            - (
                near_weight * self.step[cell][k]
                - far_weight * (self.step[cell + 1][k] + self.step[cell - 1][k])
            )
            for k in range(PAIRS)
        ]

    def near(self, cell):
        scale = SECOND_IMPL * 0.5 + 2.0 * FOURTH_IMPL
        return -scale * (self.radius[cell] + self.radius[cell + 1])

    def far(self, cell):
        return FOURTH_IMPL * self.radius[cell]

    def middle(self, cell, rate):
        centre, above = self.radius[cell], self.radius[cell + 1]
        if cell == 0:
            total, weighted = centre + (centre + above), 4.0 * centre + above
        else:
            below = self.radius[cell - 1]
            total = (below + centre) + (centre + above)
            weighted = below + 4.0 * centre + above
        result = SECOND_IMPL * (0.5 * total) + FOURTH_IMPL * weighted
        return result if rate is None else rate * centre + result

    def diagonal(self, cell, rates):
        across = self.near(cell)
        return (self.middle(cell, rates[0]), across, across, self.middle(cell + 1, rates[1]))

    def below(self, cell):
        return (self.far(cell - 1), self.near(cell - 1), None, self.far(cell))

    def above(self, cell):
        return (self.far(cell + 1), None, self.near(cell + 1), self.far(cell + 2))


def rates_at(ref, index, start, first_half):
    rows = [ref[index + (pl.ds(start + k, 1), slice(None))] for k in range(4)]
    return [jnp.where(first_half, rows[2 * k], rows[2 * k + 1]) for k in range(2)]


def half_kernel(
    all_ref, next_ref, codes_ref, partial_ref, factor_ref, blocks_ref, fixed_ref, line_ref,
):
    own_y = lax.axis_index("inst") >> 1
    blocks = all_ref.shape[1]
    cells = 2 * blocks
    mirrored = lax.axis_index("cell") // blocks
    sign = (1 - 2 * mirrored).astype(jnp.float32)
    shape = (ROWS, LANES)
    lane_index = lax.broadcasted_iota(jnp.int32, shape, 1)
    first_var, first_inst, half_index = plane_masks()
    first_half = half_index == 0
    zero = jnp.zeros(shape, jnp.float32)

    next_rows = [
        next_ref[pl.ds(half * LANES, LANES)].reshape(1, LANES) for half in range(2)
    ]
    next_line = jnp.where(first_half, next_rows[0], next_rows[1])
    column = lax.broadcasted_iota(jnp.int32, (LANES, LANES), 0)
    prev_halves = []
    for target in range(2):
        total = None
        for source in range(2):
            hits = jnp.where(column + target * LANES == next_rows[source], 1.0, 0.0)
            names = (lane_index + source * LANES).astype(jnp.float32)
            part = lax.dot_general(
                names, hits, (((1,), (1,)), ((), ())), preferred_element_type=jnp.float32
            )
            total = part if total is None else total + part
        prev_halves.append(total)
    prev_line = jnp.where(first_half, prev_halves[0], prev_halves[1]).astype(jnp.int32)

    def picker(lines):
        lane = lines & (LANES - 1)
        same = (lines >> 7) == half_index

        def pick(plane):
            swapped = jnp.where(first_half, pltpu.roll(plane, 7, 0), pltpu.roll(plane, 1, 0))
            here = jnp.take_along_axis(plane, lane, axis=1, mode="promise_in_bounds")
            there = jnp.take_along_axis(swapped, lane, axis=1, mode="promise_in_bounds")
            return jnp.where(same, here, there)

        return pick

    pick_next = picker(next_line)
    pick_prev = picker(prev_line)

    def loaded(cell, place=own_y):
        return [all_ref[place, cell // 2, cell_rows(cell, k), :] for k in range(PAIRS)]

    own_weights, away_weights = time_weights(first_inst, 0), time_weights(first_inst, 2)

    def own_time_parts(planes, cell):
        return [
            away_weights[0] * away
            + turn_insts(first_inst, own_weights[1] * own + away_weights[1] * away)
            for own, away in zip(planes, loaded(cell, 1 - own_y))
        ]

    def flux_across(planes, velocity, pressure):
        return [
            planes[0] * velocity,
            planes[1] * velocity + jnp.where(first_var, pressure, 0.0),
            planes[2] * velocity + jnp.where(first_var, pressure * velocity, 0.0),
        ]

    def pitch_flux(planes, velocity_y, pressure, sound):
        nearby = [pick_next(plane) for plane in planes]
        _, next_velocity, next_pressure, next_sound = primitives(first_var, nearby)
        own_flux = flux_across(planes, velocity_y, pressure)
        next_flux = flux_across(nearby, next_velocity, next_pressure)
        weight = (PITCH_GAIN * 0.5) * (
            jnp.abs(velocity_y) + sound + (jnp.abs(next_velocity) + next_sound)
        )
        return [
            0.5 * (a + b) - weight * (n - o)
            for a, b, n, o in zip(own_flux, next_flux, nearby, planes)
        ]

    for cell in range(cells):
        planes = loaded(cell)
        velocity_x, velocity_y, pressure, sound = primitives(first_var, planes)
        line_ref[cell, 0], line_ref[cell, 1], line_ref[cell, 2] = velocity_x, pressure, sound
        faces_across = pitch_flux(planes, velocity_y, pressure, sound)
        times = own_time_parts(planes, cell)
        for k in range(PAIRS):
            partial_ref[cell, k] = -(times[k] + (faces_across[k] - pick_prev(faces_across[k])))

    tile = half_index * (LANES // LINES_DEV) + lane_index // LINES_DEV
    end_codes = jnp.where(mirrored == 0, codes_ref[pl.ds(0, 1), :], codes_ref[pl.ds(1, 1), :])
    codes = jnp.zeros(shape, jnp.int32)
    for k in range(2 * LANES // LINES_DEV):
        codes = jnp.where(tile == k, jnp.broadcast_to(end_codes[:, k : k + 1], shape), codes)

    def ghost(cell):
        planes = loaded(-1 - cell)
        copied = loaded(0)
        result = []
        for k in range(PAIRS):
            reflected = planes[k] if k else jnp.where(first_var, planes[k], -planes[k])
            inflow = jnp.where(first_var, FREE_STATE[2 * k], FREE_STATE[2 * k + 1])
            result.append(
                jnp.where(codes == 0, reflected, jnp.where(codes == 1, inflow, copied[k]))
            )
        return result

    line = LineCells(first_var, sign)
    faces, inverses, aboves = {}, [], []
    for cell in range(-2, cells):
        if cell < 0:
            planes = ghost(cell)
            velocity_x, _, pressure, sound = primitives(first_var, planes)
        else:
            planes = loaded(cell)
            velocity_x, pressure, sound = [line_ref[cell, k] for k in range(3)]
        line.add(cell, planes, velocity_x, pressure, sound)
        if cell >= 1:
            faces[cell - 2] = line.face(cell - 2)
        if cell >= 2:
            at = cell - 2
            for k in range(PAIRS):
                partial_ref[at, k] = partial_ref[at, k] + (faces[at - 1][k] - faces[at][k])
        if cell >= 3 and cell % 2 == 1:
            at = cell - 3
            block = at // 2
            rates = rates_at(all_ref, (own_y, block), RATE_ROW, first_half)
            diag = line.diagonal(at, rates)
            if block > 0:
                factor = two_by_two(line.below(at), inverses[-1])
                diag = less(diag, two_by_two(factor, aboves[-1]))
                for n in range(4):
                    factor_ref[block - 1, n] = factor[n]
            inverses.append(inverse_of(diag))
            aboves.append(line.above(at))
            kept = [*inverses[-1], aboves[-1][0], *aboves[-1][2:]]
            for n, plane in enumerate(kept):
                blocks_ref[block, n] = plane

    last = cells - 2
    for k in range(PAIRS):
        partial_ref[last, k] = partial_ref[last, k] + faces[last - 1][k]
    factor = two_by_two(line.below(last), inverses[-1])
    for n in range(4):
        factor_ref[blocks - 2, n] = factor[n]
    correction = list(two_by_two(factor, aboves[-1]))
    rates = rates_at(all_ref, (own_y, blocks - 1), RATE_ROW, first_half)
    for member in range(2):
        centre = line.radius[last + member]
        correction[3 * member] = correction[3 * member] - rates[member] * centre
    for n in range(3):
        for k, plane in enumerate(line.state[cells - 3 + n]):
            fixed_ref[pl.ds(n * CELL_ROWS + k * ROWS, ROWS), :] = plane
    for n in range(2):
        fixed_ref[pl.ds(CORRECTION_ROW + n * ROWS, ROWS), :] = jnp.where(
            first_var, correction[2 * n], correction[2 * n + 1]
        )


def reduce_kernel(partial_ref, time_ref, factor_ref, middle_ref, sides_ref):
    blocks = partial_ref.shape[0] // 2
    side = None
    for block in range(blocks):
        own = []
        for cell in (2 * block, 2 * block + 1):
            for k in range(PAIRS):
                time = time_ref[pl.ds(cell * CELL_ROWS + k * ROWS, ROWS), :]
                own.append(partial_ref[cell, k] - time)
        if block > 0:
            factor = [factor_ref[block - 1, n] for n in range(4)]
            own = difference(own, apply_matrix(factor, side))
        side = own
        for n, plane in enumerate(side):
            if block < blocks - 1:
                sides_ref[block, n] = plane
            else:
                middle_ref[pl.ds(n * ROWS, ROWS), :] = plane


def spread_kernel(all_ref, blocks_ref, sides_ref, known_ref, spread_ref, table_ref):
    own_y = lax.axis_index("inst") >> 1
    blocks = all_ref.shape[1]
    own_cell = lax.axis_index("cell")
    own_block = jnp.where(own_cell < blocks, own_cell, 2 * blocks - 1 - own_cell)
    zero = jnp.zeros((ROWS, LANES), jnp.float32)
    known, spread = [zero] * (2 * PAIRS), (zero + 1.0, zero, zero, zero + 1.0)
    for block in range(blocks - 1, -1, -1):
        if block < blocks - 1:
            kept = [blocks_ref[block, n] for n in range(7)]
            inverse, above = kept[:4], (kept[4], None, kept[5], kept[6])
            side = [sides_ref[block, n] for n in range(2 * PAIRS)]
            step = two_by_two(inverse, above)
            own = apply_matrix(inverse, side)
            if block < blocks - 2:
                known = difference(own, apply_matrix(step, known))
                spread = minus(two_by_two(step, spread))
            else:
                known, spread = own, minus(step)
        for n, plane in enumerate(known + list(spread)):
            table_ref[block, n] = plane
    for n in range(2 * PAIRS):
        base = all_ref[own_y, own_block, pl.ds(n * ROWS, ROWS), :]
        known_ref[n] = base + table_ref[own_block, n]
    for n in range(4):
        spread_ref[n] = table_ref[own_block, 2 * PAIRS + n]


def join_kernel(
    here_ref, there_ref, here_side_ref, there_side_ref, known_ref, spread_ref, out_ref
):
    mirrored = lax.axis_index("cell") // (lax.axis_size("cell") // 2)
    sign = (1 - 2 * mirrored).astype(jnp.float32)
    first_var, _, _ = plane_masks()

    def plane_of(ref, row):
        return ref[pl.ds(row, ROWS), :]

    line = LineCells(first_var, sign)
    for cell in range(6):
        ref, at = (here_ref, cell) if cell < 3 else (there_ref, 5 - cell)
        planes = [plane_of(ref, at * CELL_ROWS + k * ROWS) for k in range(PAIRS)]
        velocity_x, _, pressure, sound = primitives(first_var, planes)
        line.add(cell, planes, velocity_x, pressure, sound)
    faces = {cell: line.face(cell) for cell in (1, 2, 3)}

    def correction_of(ref):
        pairs = [both(first_var, plane_of(ref, CORRECTION_ROW + n * ROWS)) for n in range(2)]
        return [pairs[0][0], pairs[0][1], pairs[1][0], pairs[1][1]]

    here_side = [plane_of(here_side_ref, n * ROWS) for n in range(2 * PAIRS)]
    there_side = [plane_of(there_side_ref, n * ROWS) for n in range(2 * PAIRS)]
    side = [here_side[k] - faces[1][k] for k in range(PAIRS)]
    side += [here_side[PAIRS + k] + (faces[1][k] - faces[2][k]) for k in range(PAIRS)]
    other = [there_side[PAIRS + k] + (faces[2][k] - faces[3][k]) for k in range(PAIRS)]
    other += [there_side[k] + faces[3][k] for k in range(PAIRS)]
    no_rates = (None, None)
    diag = difference(line.diagonal(1, no_rates), correction_of(here_ref))
    other_diag = difference(line.diagonal(3, no_rates), correction_of(there_ref)[::-1])
    factor = two_by_two(line.above(1), inverse_of(other_diag))
    diag = less(diag, two_by_two(factor, line.below(3)))
    middle = apply_matrix(inverse_of(diag), difference(side, apply_matrix(factor, other)))
    moved = apply_matrix([spread_ref[n] for n in range(4)], middle)
    results = [known_ref[n] + moved[n] for n in range(2 * PAIRS)]
    for cell in range(2):
        for k in range(PAIRS):
            first, second = results[cell * PAIRS + k], results[(1 - cell) * PAIRS + k]
            result = jnp.where(mirrored == 0, first, second)
            for var in range(2):
                for inst in range(2):
                    for half in range(2):
                        row = rows_of(var, inst, half)
                        out_ref[
                            inst, 2 * k + var, pl.ds(cell, 1), pl.ds(half * LANES, LANES)
                        ] = result[row : row + 1]


def share_half(copies):
    insts, count = lax.axis_size("inst"), lax.axis_size("cell")
    halves = [range(count // 2), range(count - 1, count // 2 - 1, -1)]
    groups = [
        [inst * count + cell for inst in range(core, insts, 2) for cell in half]
        for core in range(2)
        for half in halves
    ]
    return lax.all_to_all(
        copies, ("inst", "cell"), split_axis=0, concat_axis=0, tiled=True,
        axis_index_groups=groups,
    )


def swap_cores(block):
    pairs = [(inst, inst ^ 1) for inst in range(lax.axis_size("inst"))]
    return lax.ppermute(block, "inst", pairs)


def swap_halves(block):
    count = lax.axis_size("cell")
    return lax.ppermute(block, "cell", [(i, (i + count // 2) % count) for i in range(count)])


def float_shape(*sizes):
    return jax.ShapeDtypeStruct(sizes, jnp.float32)


def local_by_halves(state, pseudo_rate, line_next, face_codes):
    blocks = lax.axis_size("cell") // 2
    cells = 2 * blocks
    vmem = pl.BlockSpec(memory_space=pltpu.VMEM)
    plane = (ROWS, LANES)
    params = pltpu.CompilerParams(vmem_limit_bytes=VMEM_BYTES)
    places = lax.axis_size("inst") // 2
    held = [
        pltpu.with_memory_space_constraint(array, pltpu.HBM)
        for array in (state, pseudo_rate, line_next, face_codes)
    ]
    packed, next_here, codes_here = pl.pallas_call(
        pack_kernel,
        out_shape=(
            float_shape(places * blocks, BLOCK_ROWS, LANES),
            jax.ShapeDtypeStruct(line_next.shape, jnp.int32),
            jax.ShapeDtypeStruct(face_codes.shape, jnp.int32),
        ),
        in_specs=[pl.BlockSpec(memory_space=pltpu.HBM)] * 4,
        out_specs=(vmem, vmem, vmem),
        scratch_shapes=[
            pltpu.VMEM(state.shape, jnp.float32),
            pltpu.VMEM(pseudo_rate.shape, jnp.float32),
            pltpu.SemaphoreType.DMA((4,)),
        ],
        compiler_params=params,
    )(*held)
    shared = share_half(packed).reshape(places, blocks, BLOCK_ROWS, LANES)
    for_partner = pl.pallas_call(
        partner_kernel,
        out_shape=float_shape(cells * CELL_ROWS, LANES),
        in_specs=[vmem],
        out_specs=vmem,
        compiler_params=params,
    )(shared)
    from_partner = swap_cores(for_partner)
    beside = pl.CostEstimate(flops=10**6, bytes_accessed=10**6, transcendentals=0)
    partial, factors, eliminated, here = pl.pallas_call(
        half_kernel,
        out_shape=(
            float_shape(cells, PAIRS, *plane),
            float_shape(blocks - 1, 4, *plane),
            float_shape(blocks - 1, 7, *plane),
            float_shape(FIXED_ROWS, LANES),
        ),
        in_specs=[vmem] * 3,
        out_specs=(vmem,) * 4,
        scratch_shapes=[pltpu.VMEM((cells, 3) + plane, jnp.float32)],
        compiler_params=params,
        cost_estimate=beside,
    )(shared, next_here, codes_here)
    there = swap_halves(here)
    here_side, sides = pl.pallas_call(
        reduce_kernel,
        out_shape=(
            float_shape(2 * CELL_ROWS, LANES),
            float_shape(blocks - 1, 2 * PAIRS, *plane),
        ),
        in_specs=[vmem] * 3,
        out_specs=(vmem, vmem),
        compiler_params=params,
    )(partial, from_partner, factors)
    there_side = swap_halves(here_side)
    known, spread = pl.pallas_call(
        spread_kernel,
        out_shape=(float_shape(2 * PAIRS, *plane), float_shape(4, *plane)),
        in_specs=[vmem] * 3,
        out_specs=(vmem, vmem),
        scratch_shapes=[pltpu.VMEM((blocks, 2 * PAIRS + 4) + plane, jnp.float32)],
        compiler_params=params,
        cost_estimate=beside,
    )(shared, eliminated, sides)
    return pl.pallas_call(
        join_kernel,
        out_shape=float_shape(*state.shape),
        in_specs=[vmem] * 6,
        out_specs=vmem,
        compiler_params=params,
    )(here, there, here_side, there_side, known, spread)


def solution(mesh):
    placed = (P("inst", None, "cell", None), P("cell", None), P(), P())
    inst_count, cell_count = mesh.shape["inst"], mesh.shape["cell"]

    def local(state, pseudo_rate, line_next, face_codes):
        small = (
            state.shape == (2, 6, 2, 2 * LANES)
            and inst_count * 2 == NT
            and cell_count == 8
            and face_codes.shape[1] * LINES_DEV == state.shape[3]
        )
        chosen = local_by_halves if small else local_by_lines
        return chosen(state, pseudo_rate, line_next, face_codes)

    return jax.shard_map(
        local, mesh=mesh, in_specs=placed, out_specs=P("inst", None, "cell", None), check_vma=False
    )
```

```python
import functools

import jax
import jax.numpy as jnp
import numpy as np
from jax import lax
from jax.experimental import pallas as pl
from jax.experimental.pallas import tpu as pltpu
from jax.sharding import PartitionSpec as P

NT = 8
LINES_DEV = 32


GAMMA_GAS = 1.4
OMEGA_BLADE = 1.0
SENSOR_GAIN = 0.25
FOURTH_GAIN = 0.03125
PITCH_GAIN = 0.5
SECOND_IMPL = 1.0
FOURTH_IMPL = 0.25
FREE_STATE = (1.0, 0.5, 0.0, 0.0, 2.625, 0.2)
MIRROR_SIGNS = (1.0, -1.0, 1.0, 1.0, 1.0, 1.0)
ZERO_BLOCK = (0.0, 0.0, 0.0, 0.0)
UNIT_BLOCK = (1.0, 0.0, 0.0, 1.0)
ZERO_PAIR = (0.0, 0.0)


def extended(block, sides, width):
    for axis, dim in sides:
        count = lax.axis_size(axis)
        forward = [(i, i + 1) for i in range(count - 1)]
        backward = [(target, source) for source, target in forward]
        low = lax.ppermute(
            lax.slice_in_dim(block, block.shape[dim] - width, None, axis=dim), axis, forward
        )
        high = lax.ppermute(lax.slice_in_dim(block, 0, width, axis=dim), axis, backward)
        block = jnp.concatenate([low, block, high], axis=dim)
    return block


def spectral_matrix(instances):
    offsets = np.arange(instances)[:, None] - np.arange(instances)[None, :]
    angles = np.pi * offsets / instances
    safe_sin = np.where(offsets == 0, 1.0, np.sin(angles))
    parity = np.where(np.mod(offsets, 2) == 0, -1.0, 1.0)
    matrix_table = np.where(
        offsets == 0, 0.0, 0.5 * OMEGA_BLADE * parity * np.cos(angles) / safe_sin
    )
    return jnp.asarray(matrix_table, jnp.float32)


def primitive_parts(cells_state):
    density = cells_state[..., 0, :, :]
    inverse = 1.0 / density
    velocity_x = cells_state[..., 1, :, :] * inverse
    velocity_y = cells_state[..., 2, :, :] * inverse
    velocity_z = cells_state[..., 3, :, :] * inverse
    energy = cells_state[..., 4, :, :]
    pressure = (GAMMA_GAS - 1.0) * (
        energy
        - 0.5
        * density
        * (velocity_x * velocity_x + velocity_y * velocity_y + velocity_z * velocity_z)
    )
    sound_speed = jnp.sqrt(GAMMA_GAS * pressure * inverse)
    return (velocity_x, velocity_y, pressure, sound_speed)


def directed_flux(cells_state, normal_velocity, pressure, component):
    zero_plane = jnp.zeros_like(pressure)
    pressure_rows = [
        zero_plane,
        zero_plane,
        zero_plane,
        zero_plane,
        pressure * normal_velocity,
        zero_plane,
    ]
    pressure_rows[component] = pressure
    return cells_state * normal_velocity[..., None, :, :] + jnp.stack(pressure_rows, axis=-3)


def line_residual(padded):
    velocity_x, velocity_y, pressure, sound_speed = primitive_parts(padded)
    flux_line = directed_flux(padded, velocity_x, pressure, 1)
    radius = jnp.abs(velocity_x) + sound_speed
    sensor = jnp.abs(
        pressure[..., 2:, :] - 2.0 * pressure[..., 1:-1, :] + pressure[..., :-2, :]
    ) / (pressure[..., 2:, :] + 2.0 * pressure[..., 1:-1, :] + pressure[..., :-2, :])
    second = SENSOR_GAIN * jnp.maximum(sensor[..., :-1, :], sensor[..., 1:, :])
    fourth = jnp.maximum(0.0, FOURTH_GAIN - second)
    face_radius = 0.5 * (radius[..., 1:-2, :] + radius[..., 2:-1, :])
    left_far = padded[..., :-3, :]
    left_near = padded[..., 1:-2, :]
    right_near = padded[..., 2:-1, :]
    right_far = padded[..., 3:, :]
    damping = face_radius[..., None, :, :] * (
        second[..., None, :, :] * (right_near - left_near)
        - fourth[..., None, :, :] * (right_far - 3.0 * right_near + 3.0 * left_near - left_far)
    )
    face_flux = 0.5 * (flux_line[..., 1:-2, :] + flux_line[..., 2:-1, :]) - damping
    return (face_flux[..., 1:, :] - face_flux[..., :-1, :], radius)


def pitch_parts(cells_state):
    velocity_x, velocity_y, pressure, sound_speed = primitive_parts(cells_state)
    return (directed_flux(cells_state, velocity_y, pressure, 2), jnp.abs(velocity_y) + sound_speed)


def pitch_residual(cells_state, next_lines, prev_lines):
    pitch_flux, radius = pitch_parts(cells_state)
    state_next = jnp.take(cells_state, next_lines, axis=-1)
    flux_next, radius_next = pitch_parts(state_next)
    face_flux = 0.5 * (pitch_flux + flux_next) - PITCH_GAIN * (0.5 * (radius + radius_next))[
        ..., None, :, :
    ] * (state_next - cells_state)
    return face_flux - jnp.take(face_flux, prev_lines, axis=-1)


def boundary_cells(edge_pair, line_codes, lower_end):
    reflected = edge_pair[..., ::-1, :] * jnp.asarray(MIRROR_SIGNS, jnp.float32)[:, None, None]
    if lower_end:
        copied = jnp.concatenate([edge_pair[..., :1, :], edge_pair[..., :1, :]], axis=-2)
    else:
        copied = jnp.concatenate([edge_pair[..., 1:, :], edge_pair[..., 1:, :]], axis=-2)
    inflow = jnp.asarray(FREE_STATE, jnp.float32)[:, None, None] + jnp.zeros_like(edge_pair)
    return jnp.where(line_codes == 0, reflected, jnp.where(line_codes == 1, inflow, copied))


def line_coefficients(radius_ext, diagonal_term, positions, total_cells):
    radius_below = radius_ext[..., :-2, :]
    radius_centre = radius_ext[..., 1:-1, :]
    radius_above = radius_ext[..., 2:, :]
    face_below = 0.5 * (radius_below + radius_centre)
    face_above = 0.5 * (radius_centre + radius_above)
    far_low = FOURTH_IMPL * radius_below
    near_low = -SECOND_IMPL * face_below - 2.0 * FOURTH_IMPL * (radius_below + radius_centre)
    middle = (
        diagonal_term
        + SECOND_IMPL * (face_below + face_above)
        + FOURTH_IMPL * (radius_below + 4.0 * radius_centre + radius_above)
    )
    near_high = -SECOND_IMPL * face_above - 2.0 * FOURTH_IMPL * (radius_centre + radius_above)
    far_high = FOURTH_IMPL * radius_above
    column = positions[:, None]
    far_low = jnp.where(column >= 2, far_low, 0.0)
    near_low = jnp.where(column >= 1, near_low, 0.0)
    near_high = jnp.where(column <= total_cells - 2, near_high, 0.0)
    far_high = jnp.where(column <= total_cells - 3, far_high, 0.0)
    return (far_low, near_low, middle, near_high, far_high)


def block_product(first_matrix, second_matrix):
    return (
        first_matrix[0] * second_matrix[0] + first_matrix[1] * second_matrix[2],
        first_matrix[0] * second_matrix[1] + first_matrix[1] * second_matrix[3],
        first_matrix[2] * second_matrix[0] + first_matrix[3] * second_matrix[2],
        first_matrix[2] * second_matrix[1] + first_matrix[3] * second_matrix[3],
    )


def block_inverse(matrix):
    determinant = matrix[0] * matrix[3] - matrix[1] * matrix[2]
    reciprocal = 1.0 / determinant
    return (
        matrix[3] * reciprocal,
        -matrix[1] * reciprocal,
        -matrix[2] * reciprocal,
        matrix[0] * reciprocal,
    )


def block_apply(matrix, vector):
    return (
        matrix[0] * vector[0] + matrix[1] * vector[1],
        matrix[2] * vector[0] + matrix[3] * vector[1],
    )


def add_blocks(first_members, second_members):
    return tuple((a + b for a, b in zip(first_members, second_members)))


def negate(members):
    return tuple((-a for a in members))


def extend_blocks(members, fill_values):
    return tuple(
        (
            jnp.concatenate([m, jnp.full_like(m[..., :1, :], f)], axis=-2)
            for m, f in zip(members, fill_values)
        )
    )


def shift_next(members, fill_values):
    return tuple(
        (
            jnp.concatenate([m[..., 1:, :], jnp.full_like(m[..., :1, :], f)], axis=-2)
            for m, f in zip(members, fill_values)
        )
    )


def shift_prev(members):
    return tuple(
        (jnp.concatenate([jnp.zeros_like(m[..., :1, :]), m[..., :-1, :]], axis=-2) for m in members)
    )


def pair_split(member):
    shaped = member.reshape(member.shape[:-2] + (member.shape[-2] // 2, 2, member.shape[-1]))
    return (shaped[..., 0, :], shaped[..., 1, :])


def split_parity(members):
    halves = [pair_split(m) for m in members]
    return (tuple((h[0] for h in halves)), tuple((h[1] for h in halves)))


def alternate(first_member, second_member):
    stacked = jnp.stack((first_member, second_member), axis=-2)
    return stacked.reshape(
        first_member.shape[:-2] + (2 * first_member.shape[-2], first_member.shape[-1])
    )


def reduce_blocks(sub_blocks, diag_blocks, super_blocks, right_side):
    block_count = diag_blocks[0].shape[-2]
    if block_count == 1:
        return block_apply(block_inverse(diag_blocks), right_side)
    if block_count % 2 == 1:
        sub_blocks = extend_blocks(sub_blocks, ZERO_BLOCK)
        diag_blocks = extend_blocks(diag_blocks, UNIT_BLOCK)
        super_blocks = extend_blocks(super_blocks, ZERO_BLOCK)
        right_side = extend_blocks(right_side, ZERO_PAIR)
    sub_even, sub_odd = split_parity(sub_blocks)
    diag_even, diag_odd = split_parity(diag_blocks)
    super_even, super_odd = split_parity(super_blocks)
    side_even, side_odd = split_parity(right_side)
    inverse_even = block_inverse(diag_even)
    inverse_next = shift_next(inverse_even, UNIT_BLOCK)
    sub_next = shift_next(sub_even, ZERO_BLOCK)
    super_next = shift_next(super_even, ZERO_BLOCK)
    side_next = shift_next(side_even, ZERO_PAIR)
    left_factor = negate(block_product(sub_odd, inverse_even))
    right_factor = negate(block_product(super_odd, inverse_next))
    reduced_sub = block_product(left_factor, sub_even)
    reduced_diag = add_blocks(
        diag_odd,
        add_blocks(block_product(left_factor, super_even), block_product(right_factor, sub_next)),
    )
    reduced_super = block_product(right_factor, super_next)
    reduced_side = add_blocks(
        side_odd,
        add_blocks(block_apply(left_factor, side_even), block_apply(right_factor, side_next)),
    )
    odd_values = reduce_blocks(reduced_sub, reduced_diag, reduced_super, reduced_side)
    before_values = shift_prev(odd_values)
    remainder = add_blocks(
        side_even,
        negate(
            add_blocks(block_apply(sub_even, before_values), block_apply(super_even, odd_values))
        ),
    )
    even_values = block_apply(inverse_even, remainder)
    merged = tuple((alternate(e, o) for e, o in zip(even_values, odd_values)))
    return tuple((m[..., :block_count, :] for m in merged))


def cells_leading(block):
    moved = jnp.transpose(block, (2, 0, 1, 3))
    return moved.reshape(block.shape[2], block.shape[0] * block.shape[1] * block.shape[3])


def solve_in_lanes(coefficients, line_source):
    source_shape = line_source.shape
    lane_coef = [cells_leading(jnp.broadcast_to(c[:, None], source_shape)) for c in coefficients]
    pairs_list = [pair_split(m) for m in lane_coef]
    zero_plane = jnp.zeros_like(pairs_list[2][0])
    sub_blocks = (pairs_list[0][0], pairs_list[1][0], zero_plane, pairs_list[0][1])
    diag_blocks = (pairs_list[2][0], pairs_list[3][0], pairs_list[1][1], pairs_list[2][1])
    super_blocks = (pairs_list[4][0], zero_plane, pairs_list[3][1], pairs_list[4][1])
    values = reduce_blocks(
        sub_blocks, diag_blocks, super_blocks, pair_split(cells_leading(line_source))
    )
    flat = alternate(values[0], values[1])
    shaped = flat.reshape(source_shape[2], source_shape[0], source_shape[1], source_shape[3])
    return jnp.transpose(shaped, (1, 2, 0, 3))


def return_tiles(line_values):
    return lax.all_to_all(line_values, "cell", split_axis=2, concat_axis=3, tiled=True)


def local_by_lines(state, pseudo_rate, line_next, face_codes):
    local_count = state.shape[0]
    tile_cells = state.shape[2]
    cell_index = lax.axis_index("cell")
    cell_count = lax.axis_size("cell")
    total_cells = tile_cells * cell_count
    spectral = spectral_matrix(NT)
    first_local = lax.axis_index("inst") * local_count
    own_rows = lax.dynamic_slice_in_dim(spectral, first_local, local_count, 0)
    shard_block = jax.tree.map(lambda a: lax.all_gather(a, "inst", axis=0, tiled=True), state)
    columns = lax.slice_in_dim(own_rows, 0, shard_block.shape[0], axis=1)
    time_term = jnp.zeros_like(state) + jnp.einsum(
        "nm,mvil->nvil", columns, shard_block, precision=lax.Precision.HIGHEST
    )
    padded = extended(state, (("cell", 2),), 2)
    codes_lines = jnp.repeat(face_codes, LINES_DEV, axis=1)
    lower_ghost = boundary_cells(state[:, :, 0:2, :], codes_lines[0], True)
    upper_ghost = boundary_cells(state[:, :, -2:, :], codes_lines[1], False)
    lower_rim = jnp.where(cell_index == 0, lower_ghost, padded[:, :, :2, :])
    upper_rim = jnp.where(cell_index == cell_count - 1, upper_ghost, padded[:, :, -2:, :])
    padded = jnp.concatenate([lower_rim, padded[:, :, 2:-2, :], upper_rim], axis=2)
    line_part, radius = line_residual(padded)
    prev_lines = (
        jnp.zeros_like(line_next).at[line_next].set(jnp.arange(line_next.shape[0], dtype=jnp.int32))
    )
    residual = line_part + pitch_residual(state, line_next, prev_lines) + time_term
    right_side = -residual
    centre_radius = radius[:, 2:-2, :]
    diagonal_term = pseudo_rate * centre_radius
    positions = cell_index * tile_cells + jnp.arange(-1, tile_cells + 1, dtype=jnp.int32)
    inside = (positions >= 0) & (positions < total_cells)
    radius_ext = jnp.where(inside[:, None], radius[:, 1:-1, :], 0.0)
    coefficients = line_coefficients(radius_ext, diagonal_term, positions[1:-1], total_cells)
    stacked = jnp.stack(coefficients, axis=1)
    line_source = lax.all_to_all(right_side, "cell", split_axis=3, concat_axis=2, tiled=True)
    line_coef = lax.all_to_all(stacked, "cell", split_axis=3, concat_axis=2, tiled=True)
    update = return_tiles(solve_in_lanes(tuple((line_coef[:, k] for k in range(5))), line_source))
    return state + update


LANES = 128
ROWS = 8
PAIRS = 3
CELL_ROWS = PAIRS * ROWS
RATE_ROW = 2 * CELL_ROWS
VMEM_BYTES = 8 * 2**20
BLOCK_ROWS = RATE_ROW + ROWS

MIDDLE_CELLS = 3
CORRECTION_ROW = 2 * CELL_ROWS
SIDE_ROWS = CORRECTION_ROW + 2 * ROWS


def spectral_offsets():
    table = np.zeros(NT)
    for offset in range(1, NT):
        angle = np.pi * offset / NT
        parity = -1.0 if offset % 2 == 0 else 1.0
        table[offset] = 0.5 * OMEGA_BLADE * parity * np.cos(angle) / np.sin(angle)
    return [float(np.float32(value)) for value in table]


def plane_masks():
    row_index = lax.broadcasted_iota(jnp.int32, (ROWS, LANES), 0)
    return row_index < 4, (row_index & 2) == 0, row_index & 1


def both(first_var, plane):
    turned = pltpu.roll(plane, 4, 0)
    return jnp.where(first_var, plane, turned), jnp.where(first_var, turned, plane)


def primitives(first_var, planes):
    density, moment_x = both(first_var, planes[0])
    moment_y, moment_z = both(first_var, planes[1])
    energy = jnp.where(first_var, planes[2], pltpu.roll(planes[2], 4, 0))
    inverse = 1.0 / density
    velocity_x = moment_x * inverse
    velocity_y = moment_y * inverse
    velocity_z = moment_z * inverse
    kinetic = moment_x * velocity_x + moment_y * velocity_y + moment_z * velocity_z
    pressure = (GAMMA_GAS - 1.0) * (energy - 0.5 * kinetic)
    sound = jnp.sqrt(GAMMA_GAS * pressure * inverse)
    return velocity_x, velocity_y, pressure, sound


def rows_of(var, inst, half):
    return (var // 2) * ROWS + (var % 2) * 4 + inst * 2 + half


def pack_kernel(
    held_state_ref, held_rate_ref, held_next_ref, held_codes_ref, out_ref, next_ref, codes_ref,
    state_ref, rate_ref, sems,
):
    copies = [
        pltpu.make_async_copy(source, target, sems.at[k])
        for k, (source, target) in enumerate(
            (
                (held_state_ref, state_ref),
                (held_rate_ref, rate_ref),
                (held_next_ref, next_ref),
                (held_codes_ref, codes_ref),
            )
        )
    ]
    for copy in copies:
        copy.start()
    for copy in copies:
        copy.wait()
    mirrored = lax.axis_index("cell") // (lax.axis_size("cell") // 2)
    for cell in range(2):
        place = pl.multiple_of(jnp.bitwise_xor(cell, mirrored) * CELL_ROWS, ROWS)
        for k in range(PAIRS):
            rows = [
                state_ref[inst, 2 * k + var, pl.ds(cell, 1), pl.ds(half * LANES, LANES)]
                for var in range(2)
                for inst in range(2)
                for half in range(2)
            ]
            for row, values in enumerate(rows):
                out_ref[0, pl.ds(place + (k * ROWS + row), 1), :] = values
    rates = [
        rate_ref[pl.ds(cell, 1), pl.ds(half * LANES, LANES)]
        for cell in range(2)
        for half in range(2)
    ]
    for row in range(4):
        out_ref[0, pl.ds(RATE_ROW + row, 1), :] = jnp.where(
            mirrored == 0, rates[row], rates[row ^ 2]
        )
    out_ref[0, pl.ds(RATE_ROW + 4, 4), :] = jnp.zeros((4, LANES), jnp.float32)
    for row in range(0, BLOCK_ROWS, ROWS):
        values = out_ref[0, pl.ds(row, ROWS), :]
        for copy in range(1, out_ref.shape[0]):
            out_ref[copy, pl.ds(row, ROWS), :] = values


def turn_insts(first_inst, plane):
    return jnp.where(first_inst, pltpu.roll(plane, 6, 0), pltpu.roll(plane, 2, 0))


def time_weights(first_inst, shift):
    offsets = spectral_offsets()
    other = jnp.where(
        first_inst, offsets[(2 * shift + 1) % NT], offsets[(2 * shift - 1) % NT]
    )
    return offsets[(2 * shift) % NT], other


def cell_rows(cell, k):
    return pl.ds((cell % 2) * CELL_ROWS + k * ROWS, ROWS)


def partner_kernel(all_ref, out_ref, middle_ref):
    own_inst = lax.axis_index("inst")
    own_y, core = own_inst >> 1, own_inst & 1
    _, first_inst, _ = plane_masks()
    one, three = time_weights(first_inst, 1), time_weights(first_inst, 3)
    near = [jnp.where(core == 0, a, b) for a, b in zip(one, three)]
    away = [jnp.where(core == 0, b, a) for a, b in zip(one, three)]
    cells = 2 * all_ref.shape[1]
    for cell in range(cells - MIDDLE_CELLS, cells):
        for k in range(PAIRS):
            row = (cell - (cells - MIDDLE_CELLS)) * CELL_ROWS + k * ROWS
            middle_ref[pl.ds(row, ROWS), :] = all_ref[own_y, cell // 2, cell_rows(cell, k), :]
    for cell in range(cells):
        for k in range(PAIRS):
            here = all_ref[own_y, cell // 2, cell_rows(cell, k), :]
            there = all_ref[1 - own_y, cell // 2, cell_rows(cell, k), :]
            out_ref[pl.ds(cell * CELL_ROWS + k * ROWS, ROWS), :] = (
                near[0] * here
                + away[0] * there
                + turn_insts(first_inst, near[1] * here + away[1] * there)
            )


def two_by_two(first, second):
    def entry(a, b, c, d):
        terms = [x * y for x, y in ((a, b), (c, d)) if x is not None and y is not None]
        return None if not terms else terms[0] if len(terms) == 1 else terms[0] + terms[1]

    return (
        entry(first[0], second[0], first[1], second[2]),
        entry(first[0], second[1], first[1], second[3]),
        entry(first[2], second[0], first[3], second[2]),
        entry(first[2], second[1], first[3], second[3]),
    )


def inverse_of(matrix):
    reciprocal = 1.0 / (matrix[0] * matrix[3] - matrix[1] * matrix[2])
    return (
        matrix[3] * reciprocal,
        -(matrix[1] * reciprocal),
        -(matrix[2] * reciprocal),
        matrix[0] * reciprocal,
    )


def less(first, second):
    return tuple(a if b is None else a - b for a, b in zip(first, second))


def minus(members):
    return tuple(None if a is None else -a for a in members)


def matrix_vector(matrix, low, high):
    def row(a, b):
        terms = [x * y for x, y in ((a, low), (b, high)) if x is not None]
        return terms[0] if len(terms) == 1 else terms[0] + terms[1]

    return row(matrix[0], matrix[1]), row(matrix[2], matrix[3])


def apply_matrix(matrix, side):
    parts = [matrix_vector(matrix, side[k], side[PAIRS + k]) for k in range(PAIRS)]
    return [low for low, _ in parts] + [high for _, high in parts]


def difference(first, second):
    return [a - b for a, b in zip(first, second)]


def flux_along(first_var, planes, velocity, pressure, sign):
    normal = sign * velocity
    return [
        planes[0] * normal + jnp.where(first_var, 0.0, sign * pressure),
        planes[1] * normal,
        planes[2] * normal + jnp.where(first_var, pressure * normal, 0.0),
    ]


class LineCells:
    def __init__(self, first_var, sign):
        self.first_var, self.sign = first_var, sign
        self.state, self.pressure, self.radius = {}, {}, {}
        self.flux, self.step, self.sensor = {}, {}, {}

    def add(self, cell, planes, velocity, pressure, sound):
        self.state[cell], self.pressure[cell] = planes, pressure
        self.radius[cell] = jnp.abs(velocity) + sound
        self.flux[cell] = flux_along(self.first_var, planes, velocity, pressure, self.sign)
        if cell - 1 in self.state:
            self.step[cell - 1] = difference(planes, self.state[cell - 1])
        if cell - 2 in self.state:
            twice = 2.0 * self.pressure[cell - 1]
            outer = pressure + self.pressure[cell - 2]
            self.sensor[cell - 1] = jnp.abs(outer - twice) / (outer + twice)

    def face(self, cell):
        second = SENSOR_GAIN * jnp.maximum(self.sensor[cell], self.sensor[cell + 1])
        fourth = jnp.maximum(0.0, FOURTH_GAIN - second)
        face_radius = 0.5 * (self.radius[cell] + self.radius[cell + 1])
        near_weight = face_radius * (second + 2.0 * fourth)
        far_weight = face_radius * fourth
        return [
            0.5 * (self.flux[cell][k] + self.flux[cell + 1][k])
            - (
                near_weight * self.step[cell][k]
                - far_weight * (self.step[cell + 1][k] + self.step[cell - 1][k])
            )
            for k in range(PAIRS)
        ]

    def near(self, cell):
        scale = SECOND_IMPL * 0.5 + 2.0 * FOURTH_IMPL
        return -scale * (self.radius[cell] + self.radius[cell + 1])

    def far(self, cell):
        return FOURTH_IMPL * self.radius[cell]

    def middle(self, cell, rate):
        centre, above = self.radius[cell], self.radius[cell + 1]
        if cell == 0:
            total, weighted = centre + (centre + above), 4.0 * centre + above
        else:
            below = self.radius[cell - 1]
            total = (below + centre) + (centre + above)
            weighted = below + 4.0 * centre + above
        result = SECOND_IMPL * (0.5 * total) + FOURTH_IMPL * weighted
        return result if rate is None else rate * centre + result

    def diagonal(self, cell, rates):
        across = self.near(cell)
        return (self.middle(cell, rates[0]), across, across, self.middle(cell + 1, rates[1]))

    def below(self, cell):
        return (self.far(cell - 1), self.near(cell - 1), None, self.far(cell))

    def above(self, cell):
        return (self.far(cell + 1), None, self.near(cell + 1), self.far(cell + 2))


def rates_at(ref, index, start, first_half):
    rows = [ref[index + (pl.ds(start + k, 1), slice(None))] for k in range(4)]
    return [jnp.where(first_half, rows[2 * k], rows[2 * k + 1]) for k in range(2)]


def half_kernel(
    all_ref, next_ref, codes_ref, partial_ref, factor_ref, blocks_ref, correction_ref,
    line_ref,
):
    own_y = lax.axis_index("inst") >> 1
    blocks = all_ref.shape[1]
    cells = 2 * blocks
    mirrored = lax.axis_index("cell") // blocks
    sign = (1 - 2 * mirrored).astype(jnp.float32)
    shape = (ROWS, LANES)
    lane_index = lax.broadcasted_iota(jnp.int32, shape, 1)
    first_var, first_inst, half_index = plane_masks()
    first_half = half_index == 0
    zero = jnp.zeros(shape, jnp.float32)

    next_rows = [
        next_ref[pl.ds(half * LANES, LANES)].reshape(1, LANES) for half in range(2)
    ]
    next_line = jnp.where(first_half, next_rows[0], next_rows[1])
    column = lax.broadcasted_iota(jnp.int32, (LANES, LANES), 0)
    prev_halves = []
    for target in range(2):
        total = None
        for source in range(2):
            hits = jnp.where(column + target * LANES == next_rows[source], 1.0, 0.0)
            names = (lane_index + source * LANES).astype(jnp.float32)
            part = lax.dot_general(
                names, hits, (((1,), (1,)), ((), ())), preferred_element_type=jnp.float32
            )
            total = part if total is None else total + part
        prev_halves.append(total)
    prev_line = jnp.where(first_half, prev_halves[0], prev_halves[1]).astype(jnp.int32)

    def picker(lines):
        lane = lines & (LANES - 1)
        same = (lines >> 7) == half_index

        def pick(plane):
            swapped = jnp.where(first_half, pltpu.roll(plane, 7, 0), pltpu.roll(plane, 1, 0))
            here = jnp.take_along_axis(plane, lane, axis=1, mode="promise_in_bounds")
            there = jnp.take_along_axis(swapped, lane, axis=1, mode="promise_in_bounds")
            return jnp.where(same, here, there)

        return pick

    pick_next = picker(next_line)
    pick_prev = picker(prev_line)

    def loaded(cell, place=own_y):
        return [all_ref[place, cell // 2, cell_rows(cell, k), :] for k in range(PAIRS)]

    own_weights, away_weights = time_weights(first_inst, 0), time_weights(first_inst, 2)

    def own_time_parts(planes, cell):
        return [
            away_weights[0] * away
            + turn_insts(first_inst, own_weights[1] * own + away_weights[1] * away)
            for own, away in zip(planes, loaded(cell, 1 - own_y))
        ]

    def flux_across(planes, velocity, pressure):
        return [
            planes[0] * velocity,
            planes[1] * velocity + jnp.where(first_var, pressure, 0.0),
            planes[2] * velocity + jnp.where(first_var, pressure * velocity, 0.0),
        ]

    def pitch_flux(planes, velocity_y, pressure, sound):
        nearby = [pick_next(plane) for plane in planes]
        _, next_velocity, next_pressure, next_sound = primitives(first_var, nearby)
        own_flux = flux_across(planes, velocity_y, pressure)
        next_flux = flux_across(nearby, next_velocity, next_pressure)
        weight = (PITCH_GAIN * 0.5) * (
            jnp.abs(velocity_y) + sound + (jnp.abs(next_velocity) + next_sound)
        )
        return [
            0.5 * (a + b) - weight * (n - o)
            for a, b, n, o in zip(own_flux, next_flux, nearby, planes)
        ]

    for cell in range(cells):
        planes = loaded(cell)
        velocity_x, velocity_y, pressure, sound = primitives(first_var, planes)
        line_ref[cell, 0], line_ref[cell, 1], line_ref[cell, 2] = velocity_x, pressure, sound
        faces_across = pitch_flux(planes, velocity_y, pressure, sound)
        times = own_time_parts(planes, cell)
        for k in range(PAIRS):
            partial_ref[cell, k] = -(times[k] + (faces_across[k] - pick_prev(faces_across[k])))

    tile = half_index * (LANES // LINES_DEV) + lane_index // LINES_DEV
    end_codes = jnp.where(mirrored == 0, codes_ref[pl.ds(0, 1), :], codes_ref[pl.ds(1, 1), :])
    codes = jnp.zeros(shape, jnp.int32)
    for k in range(2 * LANES // LINES_DEV):
        codes = jnp.where(tile == k, jnp.broadcast_to(end_codes[:, k : k + 1], shape), codes)

    def ghost(cell):
        planes = loaded(-1 - cell)
        copied = loaded(0)
        result = []
        for k in range(PAIRS):
            reflected = planes[k] if k else jnp.where(first_var, planes[k], -planes[k])
            inflow = jnp.where(first_var, FREE_STATE[2 * k], FREE_STATE[2 * k + 1])
            result.append(
                jnp.where(codes == 0, reflected, jnp.where(codes == 1, inflow, copied[k]))
            )
        return result

    line = LineCells(first_var, sign)
    faces, inverses, aboves = {}, [], []
    for cell in range(-2, cells):
        if cell < 0:
            planes = ghost(cell)
            velocity_x, _, pressure, sound = primitives(first_var, planes)
        else:
            planes = loaded(cell)
            velocity_x, pressure, sound = [line_ref[cell, k] for k in range(3)]
        line.add(cell, planes, velocity_x, pressure, sound)
        if cell >= 1:
            faces[cell - 2] = line.face(cell - 2)
        if cell >= 2:
            at = cell - 2
            for k in range(PAIRS):
                partial_ref[at, k] = partial_ref[at, k] + (faces[at - 1][k] - faces[at][k])
        if cell >= 3 and cell % 2 == 1:
            at = cell - 3
            block = at // 2
            rates = rates_at(all_ref, (own_y, block), RATE_ROW, first_half)
            diag = line.diagonal(at, rates)
            if block > 0:
                factor = two_by_two(line.below(at), inverses[-1])
                diag = less(diag, two_by_two(factor, aboves[-1]))
                for n in range(4):
                    factor_ref[block - 1, n] = factor[n]
            inverses.append(inverse_of(diag))
            aboves.append(line.above(at))
            kept = [*inverses[-1], aboves[-1][0], *aboves[-1][2:]]
            for n, plane in enumerate(kept):
                blocks_ref[block, n] = plane

    last = cells - 2
    for k in range(PAIRS):
        partial_ref[last, k] = partial_ref[last, k] + faces[last - 1][k]
    factor = two_by_two(line.below(last), inverses[-1])
    for n in range(4):
        factor_ref[blocks - 2, n] = factor[n]
    correction = list(two_by_two(factor, aboves[-1]))
    rates = rates_at(all_ref, (own_y, blocks - 1), RATE_ROW, first_half)
    for member in range(2):
        centre = line.radius[last + member]
        correction[3 * member] = correction[3 * member] - rates[member] * centre
    for n in range(2):
        correction_ref[pl.ds(n * ROWS, ROWS), :] = jnp.where(
            first_var, correction[2 * n], correction[2 * n + 1]
        )


def reduce_kernel(partial_ref, time_ref, factor_ref, correction_ref, middle_ref, sides_ref):
    for row in range(0, 2 * ROWS, ROWS):
        middle_ref[pl.ds(CORRECTION_ROW + row, ROWS), :] = correction_ref[pl.ds(row, ROWS), :]
    blocks = partial_ref.shape[0] // 2
    side = None
    for block in range(blocks):
        own = []
        for cell in (2 * block, 2 * block + 1):
            for k in range(PAIRS):
                time = time_ref[pl.ds(cell * CELL_ROWS + k * ROWS, ROWS), :]
                own.append(partial_ref[cell, k] - time)
        if block > 0:
            factor = [factor_ref[block - 1, n] for n in range(4)]
            own = difference(own, apply_matrix(factor, side))
        side = own
        for n, plane in enumerate(side):
            if block < blocks - 1:
                sides_ref[block, n] = plane
            else:
                middle_ref[pl.ds(n * ROWS, ROWS), :] = plane


def spread_kernel(all_ref, blocks_ref, sides_ref, known_ref, spread_ref, table_ref):
    own_y = lax.axis_index("inst") >> 1
    blocks = all_ref.shape[1]
    own_cell = lax.axis_index("cell")
    own_block = jnp.where(own_cell < blocks, own_cell, 2 * blocks - 1 - own_cell)
    zero = jnp.zeros((ROWS, LANES), jnp.float32)
    known, spread = [zero] * (2 * PAIRS), (zero + 1.0, zero, zero, zero + 1.0)
    for block in range(blocks - 1, -1, -1):
        if block < blocks - 1:
            kept = [blocks_ref[block, n] for n in range(7)]
            inverse, above = kept[:4], (kept[4], None, kept[5], kept[6])
            side = [sides_ref[block, n] for n in range(2 * PAIRS)]
            step = two_by_two(inverse, above)
            own = apply_matrix(inverse, side)
            if block < blocks - 2:
                known = difference(own, apply_matrix(step, known))
                spread = minus(two_by_two(step, spread))
            else:
                known, spread = own, minus(step)
        for n, plane in enumerate(known + list(spread)):
            table_ref[block, n] = plane
    for n in range(2 * PAIRS):
        base = all_ref[own_y, own_block, pl.ds(n * ROWS, ROWS), :]
        known_ref[n] = base + table_ref[own_block, n]
    for n in range(4):
        spread_ref[n] = table_ref[own_block, 2 * PAIRS + n]


def join_kernel(
    here_ref, there_ref, here_side_ref, there_side_ref, known_ref, spread_ref, out_ref
):
    mirrored = lax.axis_index("cell") // (lax.axis_size("cell") // 2)
    sign = (1 - 2 * mirrored).astype(jnp.float32)
    first_var, _, _ = plane_masks()

    def plane_of(ref, row):
        return ref[pl.ds(row, ROWS), :]

    line = LineCells(first_var, sign)
    for cell in range(6):
        ref, at = (here_ref, cell) if cell < 3 else (there_ref, 5 - cell)
        planes = [plane_of(ref, at * CELL_ROWS + k * ROWS) for k in range(PAIRS)]
        velocity_x, _, pressure, sound = primitives(first_var, planes)
        line.add(cell, planes, velocity_x, pressure, sound)
    faces = {cell: line.face(cell) for cell in (1, 2, 3)}

    def correction_of(ref):
        pairs = [both(first_var, plane_of(ref, CORRECTION_ROW + n * ROWS)) for n in range(2)]
        return [pairs[0][0], pairs[0][1], pairs[1][0], pairs[1][1]]

    here_side = [plane_of(here_side_ref, n * ROWS) for n in range(2 * PAIRS)]
    there_side = [plane_of(there_side_ref, n * ROWS) for n in range(2 * PAIRS)]
    side = [here_side[k] - faces[1][k] for k in range(PAIRS)]
    side += [here_side[PAIRS + k] + (faces[1][k] - faces[2][k]) for k in range(PAIRS)]
    other = [there_side[PAIRS + k] + (faces[2][k] - faces[3][k]) for k in range(PAIRS)]
    other += [there_side[k] + faces[3][k] for k in range(PAIRS)]
    no_rates = (None, None)
    diag = difference(line.diagonal(1, no_rates), correction_of(here_side_ref))
    other_diag = difference(line.diagonal(3, no_rates), correction_of(there_side_ref)[::-1])
    factor = two_by_two(line.above(1), inverse_of(other_diag))
    diag = less(diag, two_by_two(factor, line.below(3)))
    middle = apply_matrix(inverse_of(diag), difference(side, apply_matrix(factor, other)))
    moved = apply_matrix([spread_ref[n] for n in range(4)], middle)
    results = [known_ref[n] + moved[n] for n in range(2 * PAIRS)]
    for cell in range(2):
        for k in range(PAIRS):
            first, second = results[cell * PAIRS + k], results[(1 - cell) * PAIRS + k]
            result = jnp.where(mirrored == 0, first, second)
            for var in range(2):
                for inst in range(2):
                    for half in range(2):
                        row = rows_of(var, inst, half)
                        out_ref[
                            inst, 2 * k + var, pl.ds(cell, 1), pl.ds(half * LANES, LANES)
                        ] = result[row : row + 1]


def share_half(copies):
    insts, count = lax.axis_size("inst"), lax.axis_size("cell")
    halves = [range(count // 2), range(count - 1, count // 2 - 1, -1)]
    groups = [
        [inst * count + cell for inst in range(core, insts, 2) for cell in half]
        for core in range(2)
        for half in halves
    ]
    return lax.all_to_all(
        copies, ("inst", "cell"), split_axis=0, concat_axis=0, tiled=True,
        axis_index_groups=groups,
    )


def swap_cores(block):
    pairs = [(inst, inst ^ 1) for inst in range(lax.axis_size("inst"))]
    return lax.ppermute(block, "inst", pairs)


def swap_halves(block):
    count = lax.axis_size("cell")
    return lax.ppermute(block, "cell", [(i, (i + count // 2) % count) for i in range(count)])


def float_shape(*sizes):
    return jax.ShapeDtypeStruct(sizes, jnp.float32)


def local_by_halves(state, pseudo_rate, line_next, face_codes):
    blocks = lax.axis_size("cell") // 2
    cells = 2 * blocks
    vmem = pl.BlockSpec(memory_space=pltpu.VMEM)
    plane = (ROWS, LANES)
    params = pltpu.CompilerParams(vmem_limit_bytes=VMEM_BYTES)
    places = lax.axis_size("inst") // 2
    held = [
        pltpu.with_memory_space_constraint(array, pltpu.HBM)
        for array in (state, pseudo_rate, line_next, face_codes)
    ]
    packed, next_here, codes_here = pl.pallas_call(
        pack_kernel,
        out_shape=(
            float_shape(places * blocks, BLOCK_ROWS, LANES),
            jax.ShapeDtypeStruct(line_next.shape, jnp.int32),
            jax.ShapeDtypeStruct(face_codes.shape, jnp.int32),
        ),
        in_specs=[pl.BlockSpec(memory_space=pltpu.HBM)] * 4,
        out_specs=(vmem, vmem, vmem),
        scratch_shapes=[
            pltpu.VMEM(state.shape, jnp.float32),
            pltpu.VMEM(pseudo_rate.shape, jnp.float32),
            pltpu.SemaphoreType.DMA((4,)),
        ],
        compiler_params=params,
    )(*held)
    shared = share_half(packed).reshape(places, blocks, BLOCK_ROWS, LANES)
    for_partner, here = pl.pallas_call(
        partner_kernel,
        out_shape=(
            float_shape(cells * CELL_ROWS, LANES),
            float_shape(MIDDLE_CELLS * CELL_ROWS, LANES),
        ),
        in_specs=[vmem],
        out_specs=(vmem, vmem),
        compiler_params=params,
    )(shared)
    from_partner = swap_cores(for_partner)
    there = swap_halves(here)
    beside = pl.CostEstimate(flops=10**6, bytes_accessed=10**6, transcendentals=0)
    partial, factors, eliminated, correction = pl.pallas_call(
        half_kernel,
        out_shape=(
            float_shape(cells, PAIRS, *plane),
            float_shape(blocks - 1, 4, *plane),
            float_shape(blocks - 1, 7, *plane),
            float_shape(2 * ROWS, LANES),
        ),
        in_specs=[vmem] * 3,
        out_specs=(vmem,) * 4,
        scratch_shapes=[pltpu.VMEM((cells, 3) + plane, jnp.float32)],
        compiler_params=params,
        cost_estimate=beside,
    )(shared, next_here, codes_here)
    here_side, sides = pl.pallas_call(
        reduce_kernel,
        out_shape=(
            float_shape(SIDE_ROWS, LANES),
            float_shape(blocks - 1, 2 * PAIRS, *plane),
        ),
        in_specs=[vmem] * 4,
        out_specs=(vmem, vmem),
        compiler_params=params,
    )(partial, from_partner, factors, correction)
    there_side = swap_halves(here_side)
    known, spread = pl.pallas_call(
        spread_kernel,
        out_shape=(float_shape(2 * PAIRS, *plane), float_shape(4, *plane)),
        in_specs=[vmem] * 3,
        out_specs=(vmem, vmem),
        scratch_shapes=[pltpu.VMEM((blocks, 2 * PAIRS + 4) + plane, jnp.float32)],
        compiler_params=params,
        cost_estimate=beside,
    )(shared, eliminated, sides)
    return pl.pallas_call(
        join_kernel,
        out_shape=float_shape(*state.shape),
        in_specs=[vmem] * 6,
        out_specs=vmem,
        compiler_params=params,
    )(here, there, here_side, there_side, known, spread)


def solution(mesh):
    placed = (P("inst", None, "cell", None), P("cell", None), P(), P())
    inst_count, cell_count = mesh.shape["inst"], mesh.shape["cell"]

    def local(state, pseudo_rate, line_next, face_codes):
        small = (
            state.shape == (2, 6, 2, 2 * LANES)
            and inst_count * 2 == NT
            and cell_count == 8
            and face_codes.shape[1] * LINES_DEV == state.shape[3]
        )
        chosen = local_by_halves if small else local_by_lines
        return chosen(state, pseudo_rate, line_next, face_codes)

    return jax.shard_map(
        local, mesh=mesh, in_specs=placed, out_specs=P("inst", None, "cell", None), check_vma=False
    )
```

```python
import functools

import jax
import jax.numpy as jnp
import numpy as np
from jax import lax
from jax.experimental import pallas as pl
from jax.experimental.pallas import tpu as pltpu
from jax.sharding import PartitionSpec as P

NT = 8
LINES_DEV = 32


GAMMA_GAS = 1.4
OMEGA_BLADE = 1.0
SENSOR_GAIN = 0.25
FOURTH_GAIN = 0.03125
PITCH_GAIN = 0.5
SECOND_IMPL = 1.0
FOURTH_IMPL = 0.25
FREE_STATE = (1.0, 0.5, 0.0, 0.0, 2.625, 0.2)
MIRROR_SIGNS = (1.0, -1.0, 1.0, 1.0, 1.0, 1.0)
ZERO_BLOCK = (0.0, 0.0, 0.0, 0.0)
UNIT_BLOCK = (1.0, 0.0, 0.0, 1.0)
ZERO_PAIR = (0.0, 0.0)


def extended(block, sides, width):
    for axis, dim in sides:
        count = lax.axis_size(axis)
        forward = [(i, i + 1) for i in range(count - 1)]
        backward = [(target, source) for source, target in forward]
        low = lax.ppermute(
            lax.slice_in_dim(block, block.shape[dim] - width, None, axis=dim), axis, forward
        )
        high = lax.ppermute(lax.slice_in_dim(block, 0, width, axis=dim), axis, backward)
        block = jnp.concatenate([low, block, high], axis=dim)
    return block


def spectral_matrix(instances):
    offsets = np.arange(instances)[:, None] - np.arange(instances)[None, :]
    angles = np.pi * offsets / instances
    safe_sin = np.where(offsets == 0, 1.0, np.sin(angles))
    parity = np.where(np.mod(offsets, 2) == 0, -1.0, 1.0)
    matrix_table = np.where(
        offsets == 0, 0.0, 0.5 * OMEGA_BLADE * parity * np.cos(angles) / safe_sin
    )
    return jnp.asarray(matrix_table, jnp.float32)


def primitive_parts(cells_state):
    density = cells_state[..., 0, :, :]
    inverse = 1.0 / density
    velocity_x = cells_state[..., 1, :, :] * inverse
    velocity_y = cells_state[..., 2, :, :] * inverse
    velocity_z = cells_state[..., 3, :, :] * inverse
    energy = cells_state[..., 4, :, :]
    pressure = (GAMMA_GAS - 1.0) * (
        energy
        - 0.5
        * density
        * (velocity_x * velocity_x + velocity_y * velocity_y + velocity_z * velocity_z)
    )
    sound_speed = jnp.sqrt(GAMMA_GAS * pressure * inverse)
    return (velocity_x, velocity_y, pressure, sound_speed)


def directed_flux(cells_state, normal_velocity, pressure, component):
    zero_plane = jnp.zeros_like(pressure)
    pressure_rows = [
        zero_plane,
        zero_plane,
        zero_plane,
        zero_plane,
        pressure * normal_velocity,
        zero_plane,
    ]
    pressure_rows[component] = pressure
    return cells_state * normal_velocity[..., None, :, :] + jnp.stack(pressure_rows, axis=-3)


def line_residual(padded):
    velocity_x, velocity_y, pressure, sound_speed = primitive_parts(padded)
    flux_line = directed_flux(padded, velocity_x, pressure, 1)
    radius = jnp.abs(velocity_x) + sound_speed
    sensor = jnp.abs(
        pressure[..., 2:, :] - 2.0 * pressure[..., 1:-1, :] + pressure[..., :-2, :]
    ) / (pressure[..., 2:, :] + 2.0 * pressure[..., 1:-1, :] + pressure[..., :-2, :])
    second = SENSOR_GAIN * jnp.maximum(sensor[..., :-1, :], sensor[..., 1:, :])
    fourth = jnp.maximum(0.0, FOURTH_GAIN - second)
    face_radius = 0.5 * (radius[..., 1:-2, :] + radius[..., 2:-1, :])
    left_far = padded[..., :-3, :]
    left_near = padded[..., 1:-2, :]
    right_near = padded[..., 2:-1, :]
    right_far = padded[..., 3:, :]
    damping = face_radius[..., None, :, :] * (
        second[..., None, :, :] * (right_near - left_near)
        - fourth[..., None, :, :] * (right_far - 3.0 * right_near + 3.0 * left_near - left_far)
    )
    face_flux = 0.5 * (flux_line[..., 1:-2, :] + flux_line[..., 2:-1, :]) - damping
    return (face_flux[..., 1:, :] - face_flux[..., :-1, :], radius)


def pitch_parts(cells_state):
    velocity_x, velocity_y, pressure, sound_speed = primitive_parts(cells_state)
    return (directed_flux(cells_state, velocity_y, pressure, 2), jnp.abs(velocity_y) + sound_speed)


def pitch_residual(cells_state, next_lines, prev_lines):
    pitch_flux, radius = pitch_parts(cells_state)
    state_next = jnp.take(cells_state, next_lines, axis=-1)
    flux_next, radius_next = pitch_parts(state_next)
    face_flux = 0.5 * (pitch_flux + flux_next) - PITCH_GAIN * (0.5 * (radius + radius_next))[
        ..., None, :, :
    ] * (state_next - cells_state)
    return face_flux - jnp.take(face_flux, prev_lines, axis=-1)


def boundary_cells(edge_pair, line_codes, lower_end):
    reflected = edge_pair[..., ::-1, :] * jnp.asarray(MIRROR_SIGNS, jnp.float32)[:, None, None]
    if lower_end:
        copied = jnp.concatenate([edge_pair[..., :1, :], edge_pair[..., :1, :]], axis=-2)
    else:
        copied = jnp.concatenate([edge_pair[..., 1:, :], edge_pair[..., 1:, :]], axis=-2)
    inflow = jnp.asarray(FREE_STATE, jnp.float32)[:, None, None] + jnp.zeros_like(edge_pair)
    return jnp.where(line_codes == 0, reflected, jnp.where(line_codes == 1, inflow, copied))


def line_coefficients(radius_ext, diagonal_term, positions, total_cells):
    radius_below = radius_ext[..., :-2, :]
    radius_centre = radius_ext[..., 1:-1, :]
    radius_above = radius_ext[..., 2:, :]
    face_below = 0.5 * (radius_below + radius_centre)
    face_above = 0.5 * (radius_centre + radius_above)
    far_low = FOURTH_IMPL * radius_below
    near_low = -SECOND_IMPL * face_below - 2.0 * FOURTH_IMPL * (radius_below + radius_centre)
    middle = (
        diagonal_term
        + SECOND_IMPL * (face_below + face_above)
        + FOURTH_IMPL * (radius_below + 4.0 * radius_centre + radius_above)
    )
    near_high = -SECOND_IMPL * face_above - 2.0 * FOURTH_IMPL * (radius_centre + radius_above)
    far_high = FOURTH_IMPL * radius_above
    column = positions[:, None]
    far_low = jnp.where(column >= 2, far_low, 0.0)
    near_low = jnp.where(column >= 1, near_low, 0.0)
    near_high = jnp.where(column <= total_cells - 2, near_high, 0.0)
    far_high = jnp.where(column <= total_cells - 3, far_high, 0.0)
    return (far_low, near_low, middle, near_high, far_high)


def block_product(first_matrix, second_matrix):
    return (
        first_matrix[0] * second_matrix[0] + first_matrix[1] * second_matrix[2],
        first_matrix[0] * second_matrix[1] + first_matrix[1] * second_matrix[3],
        first_matrix[2] * second_matrix[0] + first_matrix[3] * second_matrix[2],
        first_matrix[2] * second_matrix[1] + first_matrix[3] * second_matrix[3],
    )


def block_inverse(matrix):
    determinant = matrix[0] * matrix[3] - matrix[1] * matrix[2]
    reciprocal = 1.0 / determinant
    return (
        matrix[3] * reciprocal,
        -matrix[1] * reciprocal,
        -matrix[2] * reciprocal,
        matrix[0] * reciprocal,
    )


def block_apply(matrix, vector):
    return (
        matrix[0] * vector[0] + matrix[1] * vector[1],
        matrix[2] * vector[0] + matrix[3] * vector[1],
    )


def add_blocks(first_members, second_members):
    return tuple((a + b for a, b in zip(first_members, second_members)))


def negate(members):
    return tuple((-a for a in members))


def extend_blocks(members, fill_values):
    return tuple(
        (
            jnp.concatenate([m, jnp.full_like(m[..., :1, :], f)], axis=-2)
            for m, f in zip(members, fill_values)
        )
    )


def shift_next(members, fill_values):
    return tuple(
        (
            jnp.concatenate([m[..., 1:, :], jnp.full_like(m[..., :1, :], f)], axis=-2)
            for m, f in zip(members, fill_values)
        )
    )


def shift_prev(members):
    return tuple(
        (jnp.concatenate([jnp.zeros_like(m[..., :1, :]), m[..., :-1, :]], axis=-2) for m in members)
    )


def pair_split(member):
    shaped = member.reshape(member.shape[:-2] + (member.shape[-2] // 2, 2, member.shape[-1]))
    return (shaped[..., 0, :], shaped[..., 1, :])


def split_parity(members):
    halves = [pair_split(m) for m in members]
    return (tuple((h[0] for h in halves)), tuple((h[1] for h in halves)))


def alternate(first_member, second_member):
    stacked = jnp.stack((first_member, second_member), axis=-2)
    return stacked.reshape(
        first_member.shape[:-2] + (2 * first_member.shape[-2], first_member.shape[-1])
    )


def reduce_blocks(sub_blocks, diag_blocks, super_blocks, right_side):
    block_count = diag_blocks[0].shape[-2]
    if block_count == 1:
        return block_apply(block_inverse(diag_blocks), right_side)
    if block_count % 2 == 1:
        sub_blocks = extend_blocks(sub_blocks, ZERO_BLOCK)
        diag_blocks = extend_blocks(diag_blocks, UNIT_BLOCK)
        super_blocks = extend_blocks(super_blocks, ZERO_BLOCK)
        right_side = extend_blocks(right_side, ZERO_PAIR)
    sub_even, sub_odd = split_parity(sub_blocks)
    diag_even, diag_odd = split_parity(diag_blocks)
    super_even, super_odd = split_parity(super_blocks)
    side_even, side_odd = split_parity(right_side)
    inverse_even = block_inverse(diag_even)
    inverse_next = shift_next(inverse_even, UNIT_BLOCK)
    sub_next = shift_next(sub_even, ZERO_BLOCK)
    super_next = shift_next(super_even, ZERO_BLOCK)
    side_next = shift_next(side_even, ZERO_PAIR)
    left_factor = negate(block_product(sub_odd, inverse_even))
    right_factor = negate(block_product(super_odd, inverse_next))
    reduced_sub = block_product(left_factor, sub_even)
    reduced_diag = add_blocks(
        diag_odd,
        add_blocks(block_product(left_factor, super_even), block_product(right_factor, sub_next)),
    )
    reduced_super = block_product(right_factor, super_next)
    reduced_side = add_blocks(
        side_odd,
        add_blocks(block_apply(left_factor, side_even), block_apply(right_factor, side_next)),
    )
    odd_values = reduce_blocks(reduced_sub, reduced_diag, reduced_super, reduced_side)
    before_values = shift_prev(odd_values)
    remainder = add_blocks(
        side_even,
        negate(
            add_blocks(block_apply(sub_even, before_values), block_apply(super_even, odd_values))
        ),
    )
    even_values = block_apply(inverse_even, remainder)
    merged = tuple((alternate(e, o) for e, o in zip(even_values, odd_values)))
    return tuple((m[..., :block_count, :] for m in merged))


def cells_leading(block):
    moved = jnp.transpose(block, (2, 0, 1, 3))
    return moved.reshape(block.shape[2], block.shape[0] * block.shape[1] * block.shape[3])


def solve_in_lanes(coefficients, line_source):
    source_shape = line_source.shape
    lane_coef = [cells_leading(jnp.broadcast_to(c[:, None], source_shape)) for c in coefficients]
    pairs_list = [pair_split(m) for m in lane_coef]
    zero_plane = jnp.zeros_like(pairs_list[2][0])
    sub_blocks = (pairs_list[0][0], pairs_list[1][0], zero_plane, pairs_list[0][1])
    diag_blocks = (pairs_list[2][0], pairs_list[3][0], pairs_list[1][1], pairs_list[2][1])
    super_blocks = (pairs_list[4][0], zero_plane, pairs_list[3][1], pairs_list[4][1])
    values = reduce_blocks(
        sub_blocks, diag_blocks, super_blocks, pair_split(cells_leading(line_source))
    )
    flat = alternate(values[0], values[1])
    shaped = flat.reshape(source_shape[2], source_shape[0], source_shape[1], source_shape[3])
    return jnp.transpose(shaped, (1, 2, 0, 3))


def return_tiles(line_values):
    return lax.all_to_all(line_values, "cell", split_axis=2, concat_axis=3, tiled=True)


def local_by_lines(state, pseudo_rate, line_next, face_codes):
    local_count = state.shape[0]
    tile_cells = state.shape[2]
    cell_index = lax.axis_index("cell")
    cell_count = lax.axis_size("cell")
    total_cells = tile_cells * cell_count
    spectral = spectral_matrix(NT)
    first_local = lax.axis_index("inst") * local_count
    own_rows = lax.dynamic_slice_in_dim(spectral, first_local, local_count, 0)
    shard_block = jax.tree.map(lambda a: lax.all_gather(a, "inst", axis=0, tiled=True), state)
    columns = lax.slice_in_dim(own_rows, 0, shard_block.shape[0], axis=1)
    time_term = jnp.zeros_like(state) + jnp.einsum(
        "nm,mvil->nvil", columns, shard_block, precision=lax.Precision.HIGHEST
    )
    padded = extended(state, (("cell", 2),), 2)
    codes_lines = jnp.repeat(face_codes, LINES_DEV, axis=1)
    lower_ghost = boundary_cells(state[:, :, 0:2, :], codes_lines[0], True)
    upper_ghost = boundary_cells(state[:, :, -2:, :], codes_lines[1], False)
    lower_rim = jnp.where(cell_index == 0, lower_ghost, padded[:, :, :2, :])
    upper_rim = jnp.where(cell_index == cell_count - 1, upper_ghost, padded[:, :, -2:, :])
    padded = jnp.concatenate([lower_rim, padded[:, :, 2:-2, :], upper_rim], axis=2)
    line_part, radius = line_residual(padded)
    prev_lines = (
        jnp.zeros_like(line_next).at[line_next].set(jnp.arange(line_next.shape[0], dtype=jnp.int32))
    )
    residual = line_part + pitch_residual(state, line_next, prev_lines) + time_term
    right_side = -residual
    centre_radius = radius[:, 2:-2, :]
    diagonal_term = pseudo_rate * centre_radius
    positions = cell_index * tile_cells + jnp.arange(-1, tile_cells + 1, dtype=jnp.int32)
    inside = (positions >= 0) & (positions < total_cells)
    radius_ext = jnp.where(inside[:, None], radius[:, 1:-1, :], 0.0)
    coefficients = line_coefficients(radius_ext, diagonal_term, positions[1:-1], total_cells)
    stacked = jnp.stack(coefficients, axis=1)
    line_source = lax.all_to_all(right_side, "cell", split_axis=3, concat_axis=2, tiled=True)
    line_coef = lax.all_to_all(stacked, "cell", split_axis=3, concat_axis=2, tiled=True)
    update = return_tiles(solve_in_lanes(tuple((line_coef[:, k] for k in range(5))), line_source))
    return state + update


LANES = 128
ROWS = 8
PAIRS = 3
CELL_ROWS = PAIRS * ROWS
RATE_ROW = 2 * CELL_ROWS
VMEM_BYTES = 8 * 2**20
BLOCK_ROWS = RATE_ROW + ROWS

MIDDLE_CELLS = 3
CORRECTION_ROW = 2 * CELL_ROWS
SIDE_ROWS = CORRECTION_ROW + 2 * ROWS


def spectral_offsets():
    table = np.zeros(NT)
    for offset in range(1, NT):
        angle = np.pi * offset / NT
        parity = -1.0 if offset % 2 == 0 else 1.0
        table[offset] = 0.5 * OMEGA_BLADE * parity * np.cos(angle) / np.sin(angle)
    return [float(np.float32(value)) for value in table]


def plane_masks():
    row_index = lax.broadcasted_iota(jnp.int32, (ROWS, LANES), 0)
    return row_index < 4, (row_index & 2) == 0, row_index & 1


def both(first_var, plane):
    turned = pltpu.roll(plane, 4, 0)
    return jnp.where(first_var, plane, turned), jnp.where(first_var, turned, plane)


def primitives(first_var, planes):
    density, moment_x = both(first_var, planes[0])
    moment_y, moment_z = both(first_var, planes[1])
    energy = jnp.where(first_var, planes[2], pltpu.roll(planes[2], 4, 0))
    inverse = 1.0 / density
    velocity_x = moment_x * inverse
    velocity_y = moment_y * inverse
    velocity_z = moment_z * inverse
    kinetic = moment_x * velocity_x + moment_y * velocity_y + moment_z * velocity_z
    pressure = (GAMMA_GAS - 1.0) * (energy - 0.5 * kinetic)
    sound = jnp.sqrt(GAMMA_GAS * pressure * inverse)
    return velocity_x, velocity_y, pressure, sound


def rows_of(var, inst, half):
    return (var // 2) * ROWS + (var % 2) * 4 + inst * 2 + half


def pack_kernel(
    held_state_ref, held_rate_ref, held_next_ref, held_codes_ref, out_ref, next_ref, codes_ref,
    state_ref, rate_ref, sems,
):
    copies = [
        pltpu.make_async_copy(source, target, sems.at[k])
        for k, (source, target) in enumerate(
            (
                (held_state_ref, state_ref),
                (held_rate_ref, rate_ref),
                (held_next_ref, next_ref),
                (held_codes_ref, codes_ref),
            )
        )
    ]
    for copy in copies:
        copy.start()
    for copy in copies:
        copy.wait()
    mirrored = lax.axis_index("cell") // (lax.axis_size("cell") // 2)
    for cell in range(2):
        place = pl.multiple_of(jnp.bitwise_xor(cell, mirrored) * CELL_ROWS, ROWS)
        for k in range(PAIRS):
            rows = [
                state_ref[inst, 2 * k + var, pl.ds(cell, 1), pl.ds(half * LANES, LANES)]
                for var in range(2)
                for inst in range(2)
                for half in range(2)
            ]
            for row, values in enumerate(rows):
                out_ref[0, pl.ds(place + (k * ROWS + row), 1), :] = values
    rates = [
        rate_ref[pl.ds(cell, 1), pl.ds(half * LANES, LANES)]
        for cell in range(2)
        for half in range(2)
    ]
    for row in range(4):
        out_ref[0, pl.ds(RATE_ROW + row, 1), :] = jnp.where(
            mirrored == 0, rates[row], rates[row ^ 2]
        )
    out_ref[0, pl.ds(RATE_ROW + 4, 4), :] = jnp.zeros((4, LANES), jnp.float32)
    for row in range(0, BLOCK_ROWS, ROWS):
        values = out_ref[0, pl.ds(row, ROWS), :]
        for copy in range(1, out_ref.shape[0]):
            out_ref[copy, pl.ds(row, ROWS), :] = values


def turn_insts(first_inst, plane):
    return jnp.where(first_inst, pltpu.roll(plane, 6, 0), pltpu.roll(plane, 2, 0))


def time_weights(first_inst, shift):
    offsets = spectral_offsets()
    other = jnp.where(
        first_inst, offsets[(2 * shift + 1) % NT], offsets[(2 * shift - 1) % NT]
    )
    return offsets[(2 * shift) % NT], other


def cell_rows(cell, k):
    return pl.ds((cell % 2) * CELL_ROWS + k * ROWS, ROWS)


def partner_kernel(all_ref, out_ref, middle_ref):
    own_inst = lax.axis_index("inst")
    own_y, core = own_inst >> 1, own_inst & 1
    _, first_inst, _ = plane_masks()
    one, three = time_weights(first_inst, 1), time_weights(first_inst, 3)
    near = [jnp.where(core == 0, a, b) for a, b in zip(one, three)]
    away = [jnp.where(core == 0, b, a) for a, b in zip(one, three)]
    cells = 2 * all_ref.shape[1]
    for cell in range(cells - MIDDLE_CELLS, cells):
        for k in range(PAIRS):
            row = (cell - (cells - MIDDLE_CELLS)) * CELL_ROWS + k * ROWS
            middle_ref[pl.ds(row, ROWS), :] = all_ref[own_y, cell // 2, cell_rows(cell, k), :]
    for cell in range(cells):
        for k in range(PAIRS):
            here = all_ref[own_y, cell // 2, cell_rows(cell, k), :]
            there = all_ref[1 - own_y, cell // 2, cell_rows(cell, k), :]
            out_ref[pl.ds(cell * CELL_ROWS + k * ROWS, ROWS), :] = (
                near[0] * here
                + away[0] * there
                + turn_insts(first_inst, near[1] * here + away[1] * there)
            )


def two_by_two(first, second):
    def entry(a, b, c, d):
        terms = [x * y for x, y in ((a, b), (c, d)) if x is not None and y is not None]
        return None if not terms else terms[0] if len(terms) == 1 else terms[0] + terms[1]

    return (
        entry(first[0], second[0], first[1], second[2]),
        entry(first[0], second[1], first[1], second[3]),
        entry(first[2], second[0], first[3], second[2]),
        entry(first[2], second[1], first[3], second[3]),
    )


def inverse_of(matrix):
    reciprocal = 1.0 / (matrix[0] * matrix[3] - matrix[1] * matrix[2])
    return (
        matrix[3] * reciprocal,
        -(matrix[1] * reciprocal),
        -(matrix[2] * reciprocal),
        matrix[0] * reciprocal,
    )


def less(first, second):
    return tuple(a if b is None else a - b for a, b in zip(first, second))


def minus(members):
    return tuple(None if a is None else -a for a in members)


def matrix_vector(matrix, low, high):
    def row(a, b):
        terms = [x * y for x, y in ((a, low), (b, high)) if x is not None]
        return terms[0] if len(terms) == 1 else terms[0] + terms[1]

    return row(matrix[0], matrix[1]), row(matrix[2], matrix[3])


def apply_matrix(matrix, side):
    parts = [matrix_vector(matrix, side[k], side[PAIRS + k]) for k in range(PAIRS)]
    return [low for low, _ in parts] + [high for _, high in parts]


def difference(first, second):
    return [a - b for a, b in zip(first, second)]


def flux_along(first_var, planes, velocity, pressure, sign):
    normal = sign * velocity
    return [
        planes[0] * normal + jnp.where(first_var, 0.0, sign * pressure),
        planes[1] * normal,
        planes[2] * normal + jnp.where(first_var, pressure * normal, 0.0),
    ]


class LineCells:
    def __init__(self, first_var, sign):
        self.first_var, self.sign = first_var, sign
        self.state, self.pressure, self.radius = {}, {}, {}
        self.flux, self.step, self.sensor = {}, {}, {}

    def add(self, cell, planes, velocity, pressure, sound):
        self.state[cell], self.pressure[cell] = planes, pressure
        self.radius[cell] = jnp.abs(velocity) + sound
        self.flux[cell] = flux_along(self.first_var, planes, velocity, pressure, self.sign)
        if cell - 1 in self.state:
            self.step[cell - 1] = difference(planes, self.state[cell - 1])
        if cell - 2 in self.state:
            twice = 2.0 * self.pressure[cell - 1]
            outer = pressure + self.pressure[cell - 2]
            self.sensor[cell - 1] = jnp.abs(outer - twice) / (outer + twice)

    def face(self, cell):
        second = SENSOR_GAIN * jnp.maximum(self.sensor[cell], self.sensor[cell + 1])
        fourth = jnp.maximum(0.0, FOURTH_GAIN - second)
        face_radius = 0.5 * (self.radius[cell] + self.radius[cell + 1])
        near_weight = face_radius * (second + 2.0 * fourth)
        far_weight = face_radius * fourth
        return [
            0.5 * (self.flux[cell][k] + self.flux[cell + 1][k])
            - (
                near_weight * self.step[cell][k]
                - far_weight * (self.step[cell + 1][k] + self.step[cell - 1][k])
            )
            for k in range(PAIRS)
        ]

    def near(self, cell):
        scale = SECOND_IMPL * 0.5 + 2.0 * FOURTH_IMPL
        return -scale * (self.radius[cell] + self.radius[cell + 1])

    def far(self, cell):
        return FOURTH_IMPL * self.radius[cell]

    def middle(self, cell, rate):
        centre, above = self.radius[cell], self.radius[cell + 1]
        if cell == 0:
            total, weighted = centre + (centre + above), 4.0 * centre + above
        else:
            below = self.radius[cell - 1]
            total = (below + centre) + (centre + above)
            weighted = below + 4.0 * centre + above
        result = SECOND_IMPL * (0.5 * total) + FOURTH_IMPL * weighted
        return result if rate is None else rate * centre + result

    def diagonal(self, cell, rates):
        across = self.near(cell)
        return (self.middle(cell, rates[0]), across, across, self.middle(cell + 1, rates[1]))

    def below(self, cell):
        return (self.far(cell - 1), self.near(cell - 1), None, self.far(cell))

    def above(self, cell):
        return (self.far(cell + 1), None, self.near(cell + 1), self.far(cell + 2))


def rates_at(ref, index, start, first_half):
    rows = [ref[index + (pl.ds(start + k, 1), slice(None))] for k in range(4)]
    return [jnp.where(first_half, rows[2 * k], rows[2 * k + 1]) for k in range(2)]


def half_kernel(
    all_ref, next_ref, codes_ref, partial_ref, factor_ref, blocks_ref, correction_ref,
    line_ref,
):
    own_y = lax.axis_index("inst") >> 1
    blocks = all_ref.shape[1]
    cells = 2 * blocks
    mirrored = lax.axis_index("cell") // blocks
    sign = (1 - 2 * mirrored).astype(jnp.float32)
    shape = (ROWS, LANES)
    lane_index = lax.broadcasted_iota(jnp.int32, shape, 1)
    first_var, first_inst, half_index = plane_masks()
    first_half = half_index == 0
    zero = jnp.zeros(shape, jnp.float32)

    next_rows = [
        next_ref[pl.ds(half * LANES, LANES)].reshape(1, LANES) for half in range(2)
    ]
    next_line = jnp.where(first_half, next_rows[0], next_rows[1])
    column = lax.broadcasted_iota(jnp.int32, (LANES, LANES), 0)
    prev_halves = []
    for target in range(2):
        total = None
        for source in range(2):
            hits = jnp.where(column + target * LANES == next_rows[source], 1.0, 0.0)
            names = (lane_index + source * LANES).astype(jnp.float32)
            part = lax.dot_general(
                names, hits, (((1,), (1,)), ((), ())), preferred_element_type=jnp.float32
            )
            total = part if total is None else total + part
        prev_halves.append(total)
    prev_line = jnp.where(first_half, prev_halves[0], prev_halves[1]).astype(jnp.int32)

    def picker(lines):
        lane = lines & (LANES - 1)
        same = (lines >> 7) == half_index

        def pick(plane):
            swapped = jnp.where(first_half, pltpu.roll(plane, 7, 0), pltpu.roll(plane, 1, 0))
            here = jnp.take_along_axis(plane, lane, axis=1, mode="promise_in_bounds")
            there = jnp.take_along_axis(swapped, lane, axis=1, mode="promise_in_bounds")
            return jnp.where(same, here, there)

        return pick

    pick_next = picker(next_line)
    pick_prev = picker(prev_line)

    def loaded(cell, place=own_y):
        return [all_ref[place, cell // 2, cell_rows(cell, k), :] for k in range(PAIRS)]

    own_weights, away_weights = time_weights(first_inst, 0), time_weights(first_inst, 2)

    def own_time_parts(planes, cell):
        return [
            away_weights[0] * away
            + turn_insts(first_inst, own_weights[1] * own + away_weights[1] * away)
            for own, away in zip(planes, loaded(cell, 1 - own_y))
        ]

    def flux_across(planes, velocity, pressure):
        return [
            planes[0] * velocity,
            planes[1] * velocity + jnp.where(first_var, pressure, 0.0),
            planes[2] * velocity + jnp.where(first_var, pressure * velocity, 0.0),
        ]

    def pitch_flux(planes, velocity_y, pressure, sound):
        nearby = [pick_next(plane) for plane in planes]
        _, next_velocity, next_pressure, next_sound = primitives(first_var, nearby)
        own_flux = flux_across(planes, velocity_y, pressure)
        next_flux = flux_across(nearby, next_velocity, next_pressure)
        weight = (PITCH_GAIN * 0.5) * (
            jnp.abs(velocity_y) + sound + (jnp.abs(next_velocity) + next_sound)
        )
        return [
            0.5 * (a + b) - weight * (n - o)
            for a, b, n, o in zip(own_flux, next_flux, nearby, planes)
        ]

    for cell in range(cells):
        planes = loaded(cell)
        velocity_x, velocity_y, pressure, sound = primitives(first_var, planes)
        line_ref[cell, 0], line_ref[cell, 1], line_ref[cell, 2] = velocity_x, pressure, sound
        faces_across = pitch_flux(planes, velocity_y, pressure, sound)
        times = own_time_parts(planes, cell)
        for k in range(PAIRS):
            partial_ref[cell, k] = -(times[k] + (faces_across[k] - pick_prev(faces_across[k])))

    tile = half_index * (LANES // LINES_DEV) + lane_index // LINES_DEV
    end_codes = jnp.where(mirrored == 0, codes_ref[pl.ds(0, 1), :], codes_ref[pl.ds(1, 1), :])
    codes = jnp.zeros(shape, jnp.int32)
    for k in range(2 * LANES // LINES_DEV):
        codes = jnp.where(tile == k, jnp.broadcast_to(end_codes[:, k : k + 1], shape), codes)

    def ghost(cell):
        planes = loaded(-1 - cell)
        copied = loaded(0)
        result = []
        for k in range(PAIRS):
            reflected = planes[k] if k else jnp.where(first_var, planes[k], -planes[k])
            inflow = jnp.where(first_var, FREE_STATE[2 * k], FREE_STATE[2 * k + 1])
            result.append(
                jnp.where(codes == 0, reflected, jnp.where(codes == 1, inflow, copied[k]))
            )
        return result

    line = LineCells(first_var, sign)
    faces, inverses, aboves = {}, [], []
    for cell in range(-2, cells):
        if cell < 0:
            planes = ghost(cell)
            velocity_x, _, pressure, sound = primitives(first_var, planes)
        else:
            planes = loaded(cell)
            velocity_x, pressure, sound = [line_ref[cell, k] for k in range(3)]
        line.add(cell, planes, velocity_x, pressure, sound)
        if cell >= 1:
            faces[cell - 2] = line.face(cell - 2)
        if cell >= 2:
            at = cell - 2
            for k in range(PAIRS):
                partial_ref[at, k] = partial_ref[at, k] + (faces[at - 1][k] - faces[at][k])
        if cell >= 3 and cell % 2 == 1:
            at = cell - 3
            block = at // 2
            rates = rates_at(all_ref, (own_y, block), RATE_ROW, first_half)
            diag = line.diagonal(at, rates)
            if block > 0:
                factor = two_by_two(line.below(at), inverses[-1])
                diag = less(diag, two_by_two(factor, aboves[-1]))
                for n in range(4):
                    factor_ref[block - 1, n] = factor[n]
            inverses.append(inverse_of(diag))
            aboves.append(line.above(at))
            kept = [*inverses[-1], aboves[-1][0], *aboves[-1][2:]]
            for n, plane in enumerate(kept):
                blocks_ref[block, n] = plane

    last = cells - 2
    for k in range(PAIRS):
        partial_ref[last, k] = partial_ref[last, k] + faces[last - 1][k]
    factor = two_by_two(line.below(last), inverses[-1])
    for n in range(4):
        factor_ref[blocks - 2, n] = factor[n]
    correction = list(two_by_two(factor, aboves[-1]))
    rates = rates_at(all_ref, (own_y, blocks - 1), RATE_ROW, first_half)
    for member in range(2):
        centre = line.radius[last + member]
        correction[3 * member] = correction[3 * member] - rates[member] * centre
    for n in range(2):
        correction_ref[pl.ds(n * ROWS, ROWS), :] = jnp.where(
            first_var, correction[2 * n], correction[2 * n + 1]
        )


def reduce_kernel(partial_ref, time_ref, factor_ref, correction_ref, middle_ref, sides_ref):
    for row in range(0, 2 * ROWS, ROWS):
        middle_ref[pl.ds(CORRECTION_ROW + row, ROWS), :] = correction_ref[pl.ds(row, ROWS), :]
    blocks = partial_ref.shape[0] // 2
    side = None
    for block in range(blocks):
        own = []
        for cell in (2 * block, 2 * block + 1):
            for k in range(PAIRS):
                time = time_ref[pl.ds(cell * CELL_ROWS + k * ROWS, ROWS), :]
                own.append(partial_ref[cell, k] - time)
        if block > 0:
            factor = [factor_ref[block - 1, n] for n in range(4)]
            own = difference(own, apply_matrix(factor, side))
        side = own
        for n, plane in enumerate(side):
            if block < blocks - 1:
                sides_ref[block, n] = plane
            else:
                middle_ref[pl.ds(n * ROWS, ROWS), :] = plane


def spread_kernel(all_ref, blocks_ref, sides_ref, known_ref, spread_ref, table_ref):
    own_y = lax.axis_index("inst") >> 1
    blocks = all_ref.shape[1]
    own_cell = lax.axis_index("cell")
    own_block = jnp.where(own_cell < blocks, own_cell, 2 * blocks - 1 - own_cell)
    zero = jnp.zeros((ROWS, LANES), jnp.float32)
    known, spread = [zero] * (2 * PAIRS), (zero + 1.0, zero, zero, zero + 1.0)
    for block in range(blocks - 1, -1, -1):
        if block < blocks - 1:
            kept = [blocks_ref[block, n] for n in range(7)]
            inverse, above = kept[:4], (kept[4], None, kept[5], kept[6])
            side = [sides_ref[block, n] for n in range(2 * PAIRS)]
            step = two_by_two(inverse, above)
            own = apply_matrix(inverse, side)
            if block < blocks - 2:
                known = difference(own, apply_matrix(step, known))
                spread = minus(two_by_two(step, spread))
            else:
                known, spread = own, minus(step)
        for n, plane in enumerate(known + list(spread)):
            table_ref[block, n] = plane
    for n in range(2 * PAIRS):
        base = all_ref[own_y, own_block, pl.ds(n * ROWS, ROWS), :]
        known_ref[n] = base + table_ref[own_block, n]
    for n in range(4):
        spread_ref[n] = table_ref[own_block, 2 * PAIRS + n]


def plane_of(ref, row):
    return ref[pl.ds(row, ROWS), :]


def correction_of(first_var, ref):
    pairs = [both(first_var, plane_of(ref, CORRECTION_ROW + n * ROWS)) for n in range(2)]
    return [pairs[0][0], pairs[0][1], pairs[1][0], pairs[1][1]]


def middle_kernel(here_ref, there_ref, here_side_ref, side_ref, other_ref, matrix_ref):
    mirrored = lax.axis_index("cell") // (lax.axis_size("cell") // 2)
    sign = (1 - 2 * mirrored).astype(jnp.float32)
    first_var, _, _ = plane_masks()
    line = LineCells(first_var, sign)
    for cell in range(6):
        ref, at = (here_ref, cell) if cell < 3 else (there_ref, 5 - cell)
        planes = [plane_of(ref, at * CELL_ROWS + k * ROWS) for k in range(PAIRS)]
        velocity_x, _, pressure, sound = primitives(first_var, planes)
        line.add(cell, planes, velocity_x, pressure, sound)
    faces = {cell: line.face(cell) for cell in (1, 2, 3)}
    for k in range(PAIRS):
        side_ref[k] = plane_of(here_side_ref, k * ROWS) - faces[1][k]
        side_ref[PAIRS + k] = plane_of(here_side_ref, (PAIRS + k) * ROWS) + (
            faces[1][k] - faces[2][k]
        )
        other_ref[k] = faces[2][k] - faces[3][k]
        other_ref[PAIRS + k] = faces[3][k]
    no_rates = (None, None)
    diag = difference(line.diagonal(1, no_rates), correction_of(first_var, here_side_ref))
    above, below = line.above(1), line.below(3)
    kept = [*diag, *line.diagonal(3, no_rates), above[0], *above[2:], *below[:2], below[3]]
    for n, plane in enumerate(kept):
        matrix_ref[n] = plane


def join_kernel(
    side_ref, other_ref, matrix_ref, there_side_ref, known_ref, spread_ref, out_ref
):
    mirrored = lax.axis_index("cell") // (lax.axis_size("cell") // 2)
    first_var, _, _ = plane_masks()
    kept = [matrix_ref[n] for n in range(14)]
    diag, other_diag = kept[:4], kept[4:8]
    above, below = (kept[8], None, kept[9], kept[10]), (kept[11], kept[12], None, kept[13])
    other_diag = difference(other_diag, correction_of(first_var, there_side_ref)[::-1])
    other = []
    for member in range(2):
        for k in range(PAIRS):
            there = plane_of(there_side_ref, ((1 - member) * PAIRS + k) * ROWS)
            other.append(there + other_ref[member * PAIRS + k])
    factor = two_by_two(above, inverse_of(other_diag))
    diag = less(diag, two_by_two(factor, below))
    side = [side_ref[n] for n in range(2 * PAIRS)]
    middle = apply_matrix(inverse_of(diag), difference(side, apply_matrix(factor, other)))
    moved = apply_matrix([spread_ref[n] for n in range(4)], middle)
    results = [known_ref[n] + moved[n] for n in range(2 * PAIRS)]
    for cell in range(2):
        for k in range(PAIRS):
            first, second = results[cell * PAIRS + k], results[(1 - cell) * PAIRS + k]
            result = jnp.where(mirrored == 0, first, second)
            for var in range(2):
                for inst in range(2):
                    for half in range(2):
                        row = rows_of(var, inst, half)
                        out_ref[
                            inst, 2 * k + var, pl.ds(cell, 1), pl.ds(half * LANES, LANES)
                        ] = result[row : row + 1]


def share_half(copies):
    insts, count = lax.axis_size("inst"), lax.axis_size("cell")
    halves = [range(count // 2), range(count - 1, count // 2 - 1, -1)]
    groups = [
        [inst * count + cell for inst in range(core, insts, 2) for cell in half]
        for core in range(2)
        for half in halves
    ]
    return lax.all_to_all(
        copies, ("inst", "cell"), split_axis=0, concat_axis=0, tiled=True,
        axis_index_groups=groups,
    )


def swap_cores(block):
    pairs = [(inst, inst ^ 1) for inst in range(lax.axis_size("inst"))]
    return lax.ppermute(block, "inst", pairs)


def swap_halves(block):
    count = lax.axis_size("cell")
    return lax.ppermute(block, "cell", [(i, (i + count // 2) % count) for i in range(count)])


def float_shape(*sizes):
    return jax.ShapeDtypeStruct(sizes, jnp.float32)


def local_by_halves(state, pseudo_rate, line_next, face_codes):
    blocks = lax.axis_size("cell") // 2
    cells = 2 * blocks
    vmem = pl.BlockSpec(memory_space=pltpu.VMEM)
    plane = (ROWS, LANES)
    params = pltpu.CompilerParams(vmem_limit_bytes=VMEM_BYTES)
    places = lax.axis_size("inst") // 2
    held = [
        pltpu.with_memory_space_constraint(array, pltpu.HBM)
        for array in (state, pseudo_rate, line_next, face_codes)
    ]
    packed, next_here, codes_here = pl.pallas_call(
        pack_kernel,
        out_shape=(
            float_shape(places * blocks, BLOCK_ROWS, LANES),
            jax.ShapeDtypeStruct(line_next.shape, jnp.int32),
            jax.ShapeDtypeStruct(face_codes.shape, jnp.int32),
        ),
        in_specs=[pl.BlockSpec(memory_space=pltpu.HBM)] * 4,
        out_specs=(vmem, vmem, vmem),
        scratch_shapes=[
            pltpu.VMEM(state.shape, jnp.float32),
            pltpu.VMEM(pseudo_rate.shape, jnp.float32),
            pltpu.SemaphoreType.DMA((4,)),
        ],
        compiler_params=params,
    )(*held)
    shared = share_half(packed).reshape(places, blocks, BLOCK_ROWS, LANES)
    for_partner, here = pl.pallas_call(
        partner_kernel,
        out_shape=(
            float_shape(cells * CELL_ROWS, LANES),
            float_shape(MIDDLE_CELLS * CELL_ROWS, LANES),
        ),
        in_specs=[vmem],
        out_specs=(vmem, vmem),
        compiler_params=params,
    )(shared)
    from_partner = swap_cores(for_partner)
    there = swap_halves(here)
    beside = pl.CostEstimate(flops=10**6, bytes_accessed=10**6, transcendentals=0)
    partial, factors, eliminated, correction = pl.pallas_call(
        half_kernel,
        out_shape=(
            float_shape(cells, PAIRS, *plane),
            float_shape(blocks - 1, 4, *plane),
            float_shape(blocks - 1, 7, *plane),
            float_shape(2 * ROWS, LANES),
        ),
        in_specs=[vmem] * 3,
        out_specs=(vmem,) * 4,
        scratch_shapes=[pltpu.VMEM((cells, 3) + plane, jnp.float32)],
        compiler_params=params,
        cost_estimate=beside,
    )(shared, next_here, codes_here)
    here_side, sides = pl.pallas_call(
        reduce_kernel,
        out_shape=(
            float_shape(SIDE_ROWS, LANES),
            float_shape(blocks - 1, 2 * PAIRS, *plane),
        ),
        in_specs=[vmem] * 4,
        out_specs=(vmem, vmem),
        compiler_params=params,
    )(partial, from_partner, factors, correction)
    there_side = swap_halves(here_side)
    known, spread = pl.pallas_call(
        spread_kernel,
        out_shape=(float_shape(2 * PAIRS, *plane), float_shape(4, *plane)),
        in_specs=[vmem] * 3,
        out_specs=(vmem, vmem),
        scratch_shapes=[pltpu.VMEM((blocks, 2 * PAIRS + 4) + plane, jnp.float32)],
        compiler_params=params,
        cost_estimate=beside,
    )(shared, eliminated, sides)
    side, other, matrices = pl.pallas_call(
        middle_kernel,
        out_shape=(
            float_shape(2 * PAIRS, *plane),
            float_shape(2 * PAIRS, *plane),
            float_shape(14, *plane),
        ),
        in_specs=[vmem] * 3,
        out_specs=(vmem,) * 3,
        compiler_params=params,
        cost_estimate=beside,
    )(here, there, here_side)
    return pl.pallas_call(
        join_kernel,
        out_shape=float_shape(*state.shape),
        in_specs=[vmem] * 6,
        out_specs=vmem,
        compiler_params=params,
    )(side, other, matrices, there_side, known, spread)


def solution(mesh):
    placed = (P("inst", None, "cell", None), P("cell", None), P(), P())
    inst_count, cell_count = mesh.shape["inst"], mesh.shape["cell"]

    def local(state, pseudo_rate, line_next, face_codes):
        small = (
            state.shape == (2, 6, 2, 2 * LANES)
            and inst_count * 2 == NT
            and cell_count == 8
            and face_codes.shape[1] * LINES_DEV == state.shape[3]
        )
        chosen = local_by_halves if small else local_by_lines
        return chosen(state, pseudo_rate, line_next, face_codes)

    return jax.shard_map(
        local, mesh=mesh, in_specs=placed, out_specs=P("inst", None, "cell", None), check_vma=False
    )
```

```python
import functools

import jax
import jax.numpy as jnp
import numpy as np
from jax import lax
from jax.experimental import pallas as pl
from jax.experimental.pallas import tpu as pltpu
from jax.sharding import PartitionSpec as P

NT = 8
LINES_DEV = 32


GAMMA_GAS = 1.4
OMEGA_BLADE = 1.0
SENSOR_GAIN = 0.25
FOURTH_GAIN = 0.03125
PITCH_GAIN = 0.5
SECOND_IMPL = 1.0
FOURTH_IMPL = 0.25
FREE_STATE = (1.0, 0.5, 0.0, 0.0, 2.625, 0.2)
MIRROR_SIGNS = (1.0, -1.0, 1.0, 1.0, 1.0, 1.0)
ZERO_BLOCK = (0.0, 0.0, 0.0, 0.0)
UNIT_BLOCK = (1.0, 0.0, 0.0, 1.0)
ZERO_PAIR = (0.0, 0.0)


def extended(block, sides, width):
    for axis, dim in sides:
        count = lax.axis_size(axis)
        forward = [(i, i + 1) for i in range(count - 1)]
        backward = [(target, source) for source, target in forward]
        low = lax.ppermute(
            lax.slice_in_dim(block, block.shape[dim] - width, None, axis=dim), axis, forward
        )
        high = lax.ppermute(lax.slice_in_dim(block, 0, width, axis=dim), axis, backward)
        block = jnp.concatenate([low, block, high], axis=dim)
    return block


def spectral_matrix(instances):
    offsets = np.arange(instances)[:, None] - np.arange(instances)[None, :]
    angles = np.pi * offsets / instances
    safe_sin = np.where(offsets == 0, 1.0, np.sin(angles))
    parity = np.where(np.mod(offsets, 2) == 0, -1.0, 1.0)
    matrix_table = np.where(
        offsets == 0, 0.0, 0.5 * OMEGA_BLADE * parity * np.cos(angles) / safe_sin
    )
    return jnp.asarray(matrix_table, jnp.float32)


def primitive_parts(cells_state):
    density = cells_state[..., 0, :, :]
    inverse = 1.0 / density
    velocity_x = cells_state[..., 1, :, :] * inverse
    velocity_y = cells_state[..., 2, :, :] * inverse
    velocity_z = cells_state[..., 3, :, :] * inverse
    energy = cells_state[..., 4, :, :]
    pressure = (GAMMA_GAS - 1.0) * (
        energy
        - 0.5
        * density
        * (velocity_x * velocity_x + velocity_y * velocity_y + velocity_z * velocity_z)
    )
    sound_speed = jnp.sqrt(GAMMA_GAS * pressure * inverse)
    return (velocity_x, velocity_y, pressure, sound_speed)


def directed_flux(cells_state, normal_velocity, pressure, component):
    zero_plane = jnp.zeros_like(pressure)
    pressure_rows = [
        zero_plane,
        zero_plane,
        zero_plane,
        zero_plane,
        pressure * normal_velocity,
        zero_plane,
    ]
    pressure_rows[component] = pressure
    return cells_state * normal_velocity[..., None, :, :] + jnp.stack(pressure_rows, axis=-3)


def line_residual(padded):
    velocity_x, velocity_y, pressure, sound_speed = primitive_parts(padded)
    flux_line = directed_flux(padded, velocity_x, pressure, 1)
    radius = jnp.abs(velocity_x) + sound_speed
    sensor = jnp.abs(
        pressure[..., 2:, :] - 2.0 * pressure[..., 1:-1, :] + pressure[..., :-2, :]
    ) / (pressure[..., 2:, :] + 2.0 * pressure[..., 1:-1, :] + pressure[..., :-2, :])
    second = SENSOR_GAIN * jnp.maximum(sensor[..., :-1, :], sensor[..., 1:, :])
    fourth = jnp.maximum(0.0, FOURTH_GAIN - second)
    face_radius = 0.5 * (radius[..., 1:-2, :] + radius[..., 2:-1, :])
    left_far = padded[..., :-3, :]
    left_near = padded[..., 1:-2, :]
    right_near = padded[..., 2:-1, :]
    right_far = padded[..., 3:, :]
    damping = face_radius[..., None, :, :] * (
        second[..., None, :, :] * (right_near - left_near)
        - fourth[..., None, :, :] * (right_far - 3.0 * right_near + 3.0 * left_near - left_far)
    )
    face_flux = 0.5 * (flux_line[..., 1:-2, :] + flux_line[..., 2:-1, :]) - damping
    return (face_flux[..., 1:, :] - face_flux[..., :-1, :], radius)


def pitch_parts(cells_state):
    velocity_x, velocity_y, pressure, sound_speed = primitive_parts(cells_state)
    return (directed_flux(cells_state, velocity_y, pressure, 2), jnp.abs(velocity_y) + sound_speed)


def pitch_residual(cells_state, next_lines, prev_lines):
    pitch_flux, radius = pitch_parts(cells_state)
    state_next = jnp.take(cells_state, next_lines, axis=-1)
    flux_next, radius_next = pitch_parts(state_next)
    face_flux = 0.5 * (pitch_flux + flux_next) - PITCH_GAIN * (0.5 * (radius + radius_next))[
        ..., None, :, :
    ] * (state_next - cells_state)
    return face_flux - jnp.take(face_flux, prev_lines, axis=-1)


def boundary_cells(edge_pair, line_codes, lower_end):
    reflected = edge_pair[..., ::-1, :] * jnp.asarray(MIRROR_SIGNS, jnp.float32)[:, None, None]
    if lower_end:
        copied = jnp.concatenate([edge_pair[..., :1, :], edge_pair[..., :1, :]], axis=-2)
    else:
        copied = jnp.concatenate([edge_pair[..., 1:, :], edge_pair[..., 1:, :]], axis=-2)
    inflow = jnp.asarray(FREE_STATE, jnp.float32)[:, None, None] + jnp.zeros_like(edge_pair)
    return jnp.where(line_codes == 0, reflected, jnp.where(line_codes == 1, inflow, copied))


def line_coefficients(radius_ext, diagonal_term, positions, total_cells):
    radius_below = radius_ext[..., :-2, :]
    radius_centre = radius_ext[..., 1:-1, :]
    radius_above = radius_ext[..., 2:, :]
    face_below = 0.5 * (radius_below + radius_centre)
    face_above = 0.5 * (radius_centre + radius_above)
    far_low = FOURTH_IMPL * radius_below
    near_low = -SECOND_IMPL * face_below - 2.0 * FOURTH_IMPL * (radius_below + radius_centre)
    middle = (
        diagonal_term
        + SECOND_IMPL * (face_below + face_above)
        + FOURTH_IMPL * (radius_below + 4.0 * radius_centre + radius_above)
    )
    near_high = -SECOND_IMPL * face_above - 2.0 * FOURTH_IMPL * (radius_centre + radius_above)
    far_high = FOURTH_IMPL * radius_above
    column = positions[:, None]
    far_low = jnp.where(column >= 2, far_low, 0.0)
    near_low = jnp.where(column >= 1, near_low, 0.0)
    near_high = jnp.where(column <= total_cells - 2, near_high, 0.0)
    far_high = jnp.where(column <= total_cells - 3, far_high, 0.0)
    return (far_low, near_low, middle, near_high, far_high)


def block_product(first_matrix, second_matrix):
    return (
        first_matrix[0] * second_matrix[0] + first_matrix[1] * second_matrix[2],
        first_matrix[0] * second_matrix[1] + first_matrix[1] * second_matrix[3],
        first_matrix[2] * second_matrix[0] + first_matrix[3] * second_matrix[2],
        first_matrix[2] * second_matrix[1] + first_matrix[3] * second_matrix[3],
    )


def block_inverse(matrix):
    determinant = matrix[0] * matrix[3] - matrix[1] * matrix[2]
    reciprocal = 1.0 / determinant
    return (
        matrix[3] * reciprocal,
        -matrix[1] * reciprocal,
        -matrix[2] * reciprocal,
        matrix[0] * reciprocal,
    )


def block_apply(matrix, vector):
    return (
        matrix[0] * vector[0] + matrix[1] * vector[1],
        matrix[2] * vector[0] + matrix[3] * vector[1],
    )


def add_blocks(first_members, second_members):
    return tuple((a + b for a, b in zip(first_members, second_members)))


def negate(members):
    return tuple((-a for a in members))


def extend_blocks(members, fill_values):
    return tuple(
        (
            jnp.concatenate([m, jnp.full_like(m[..., :1, :], f)], axis=-2)
            for m, f in zip(members, fill_values)
        )
    )


def shift_next(members, fill_values):
    return tuple(
        (
            jnp.concatenate([m[..., 1:, :], jnp.full_like(m[..., :1, :], f)], axis=-2)
            for m, f in zip(members, fill_values)
        )
    )


def shift_prev(members):
    return tuple(
        (jnp.concatenate([jnp.zeros_like(m[..., :1, :]), m[..., :-1, :]], axis=-2) for m in members)
    )


def pair_split(member):
    shaped = member.reshape(member.shape[:-2] + (member.shape[-2] // 2, 2, member.shape[-1]))
    return (shaped[..., 0, :], shaped[..., 1, :])


def split_parity(members):
    halves = [pair_split(m) for m in members]
    return (tuple((h[0] for h in halves)), tuple((h[1] for h in halves)))


def alternate(first_member, second_member):
    stacked = jnp.stack((first_member, second_member), axis=-2)
    return stacked.reshape(
        first_member.shape[:-2] + (2 * first_member.shape[-2], first_member.shape[-1])
    )


def reduce_blocks(sub_blocks, diag_blocks, super_blocks, right_side):
    block_count = diag_blocks[0].shape[-2]
    if block_count == 1:
        return block_apply(block_inverse(diag_blocks), right_side)
    if block_count % 2 == 1:
        sub_blocks = extend_blocks(sub_blocks, ZERO_BLOCK)
        diag_blocks = extend_blocks(diag_blocks, UNIT_BLOCK)
        super_blocks = extend_blocks(super_blocks, ZERO_BLOCK)
        right_side = extend_blocks(right_side, ZERO_PAIR)
    sub_even, sub_odd = split_parity(sub_blocks)
    diag_even, diag_odd = split_parity(diag_blocks)
    super_even, super_odd = split_parity(super_blocks)
    side_even, side_odd = split_parity(right_side)
    inverse_even = block_inverse(diag_even)
    inverse_next = shift_next(inverse_even, UNIT_BLOCK)
    sub_next = shift_next(sub_even, ZERO_BLOCK)
    super_next = shift_next(super_even, ZERO_BLOCK)
    side_next = shift_next(side_even, ZERO_PAIR)
    left_factor = negate(block_product(sub_odd, inverse_even))
    right_factor = negate(block_product(super_odd, inverse_next))
    reduced_sub = block_product(left_factor, sub_even)
    reduced_diag = add_blocks(
        diag_odd,
        add_blocks(block_product(left_factor, super_even), block_product(right_factor, sub_next)),
    )
    reduced_super = block_product(right_factor, super_next)
    reduced_side = add_blocks(
        side_odd,
        add_blocks(block_apply(left_factor, side_even), block_apply(right_factor, side_next)),
    )
    odd_values = reduce_blocks(reduced_sub, reduced_diag, reduced_super, reduced_side)
    before_values = shift_prev(odd_values)
    remainder = add_blocks(
        side_even,
        negate(
            add_blocks(block_apply(sub_even, before_values), block_apply(super_even, odd_values))
        ),
    )
    even_values = block_apply(inverse_even, remainder)
    merged = tuple((alternate(e, o) for e, o in zip(even_values, odd_values)))
    return tuple((m[..., :block_count, :] for m in merged))


def cells_leading(block):
    moved = jnp.transpose(block, (2, 0, 1, 3))
    return moved.reshape(block.shape[2], block.shape[0] * block.shape[1] * block.shape[3])


def solve_in_lanes(coefficients, line_source):
    source_shape = line_source.shape
    lane_coef = [cells_leading(jnp.broadcast_to(c[:, None], source_shape)) for c in coefficients]
    pairs_list = [pair_split(m) for m in lane_coef]
    zero_plane = jnp.zeros_like(pairs_list[2][0])
    sub_blocks = (pairs_list[0][0], pairs_list[1][0], zero_plane, pairs_list[0][1])
    diag_blocks = (pairs_list[2][0], pairs_list[3][0], pairs_list[1][1], pairs_list[2][1])
    super_blocks = (pairs_list[4][0], zero_plane, pairs_list[3][1], pairs_list[4][1])
    values = reduce_blocks(
        sub_blocks, diag_blocks, super_blocks, pair_split(cells_leading(line_source))
    )
    flat = alternate(values[0], values[1])
    shaped = flat.reshape(source_shape[2], source_shape[0], source_shape[1], source_shape[3])
    return jnp.transpose(shaped, (1, 2, 0, 3))


def return_tiles(line_values):
    return lax.all_to_all(line_values, "cell", split_axis=2, concat_axis=3, tiled=True)


def local_by_lines(state, pseudo_rate, line_next, face_codes):
    local_count = state.shape[0]
    tile_cells = state.shape[2]
    cell_index = lax.axis_index("cell")
    cell_count = lax.axis_size("cell")
    total_cells = tile_cells * cell_count
    spectral = spectral_matrix(NT)
    first_local = lax.axis_index("inst") * local_count
    own_rows = lax.dynamic_slice_in_dim(spectral, first_local, local_count, 0)
    shard_block = jax.tree.map(lambda a: lax.all_gather(a, "inst", axis=0, tiled=True), state)
    columns = lax.slice_in_dim(own_rows, 0, shard_block.shape[0], axis=1)
    time_term = jnp.zeros_like(state) + jnp.einsum(
        "nm,mvil->nvil", columns, shard_block, precision=lax.Precision.HIGHEST
    )
    padded = extended(state, (("cell", 2),), 2)
    codes_lines = jnp.repeat(face_codes, LINES_DEV, axis=1)
    lower_ghost = boundary_cells(state[:, :, 0:2, :], codes_lines[0], True)
    upper_ghost = boundary_cells(state[:, :, -2:, :], codes_lines[1], False)
    lower_rim = jnp.where(cell_index == 0, lower_ghost, padded[:, :, :2, :])
    upper_rim = jnp.where(cell_index == cell_count - 1, upper_ghost, padded[:, :, -2:, :])
    padded = jnp.concatenate([lower_rim, padded[:, :, 2:-2, :], upper_rim], axis=2)
    line_part, radius = line_residual(padded)
    prev_lines = (
        jnp.zeros_like(line_next).at[line_next].set(jnp.arange(line_next.shape[0], dtype=jnp.int32))
    )
    residual = line_part + pitch_residual(state, line_next, prev_lines) + time_term
    right_side = -residual
    centre_radius = radius[:, 2:-2, :]
    diagonal_term = pseudo_rate * centre_radius
    positions = cell_index * tile_cells + jnp.arange(-1, tile_cells + 1, dtype=jnp.int32)
    inside = (positions >= 0) & (positions < total_cells)
    radius_ext = jnp.where(inside[:, None], radius[:, 1:-1, :], 0.0)
    coefficients = line_coefficients(radius_ext, diagonal_term, positions[1:-1], total_cells)
    stacked = jnp.stack(coefficients, axis=1)
    line_source = lax.all_to_all(right_side, "cell", split_axis=3, concat_axis=2, tiled=True)
    line_coef = lax.all_to_all(stacked, "cell", split_axis=3, concat_axis=2, tiled=True)
    update = return_tiles(solve_in_lanes(tuple((line_coef[:, k] for k in range(5))), line_source))
    return state + update


LANES = 128
ROWS = 8
PAIRS = 3
CELL_ROWS = PAIRS * ROWS
TILE = 4
STATE_TILES = 2 * CELL_ROWS // TILE
BLOCK_TILES = STATE_TILES + 1
VMEM_BYTES = 8 * 2**20

MIDDLE_CELLS = 3
CORRECTION_ROW = 2 * CELL_ROWS
SIDE_ROWS = CORRECTION_ROW + 2 * ROWS


def spectral_offsets():
    table = np.zeros(NT)
    for offset in range(1, NT):
        angle = np.pi * offset / NT
        parity = -1.0 if offset % 2 == 0 else 1.0
        table[offset] = 0.5 * OMEGA_BLADE * parity * np.cos(angle) / np.sin(angle)
    return [float(np.float32(value)) for value in table]


def plane_masks():
    row_index = lax.broadcasted_iota(jnp.int32, (ROWS, LANES), 0)
    return row_index < 4, (row_index & 2) == 0, row_index & 1


def both(first_var, plane):
    turned = pltpu.roll(plane, 4, 0)
    return jnp.where(first_var, plane, turned), jnp.where(first_var, turned, plane)


def primitives(first_var, planes):
    density, moment_x = both(first_var, planes[0])
    moment_y, moment_z = both(first_var, planes[1])
    energy = jnp.where(first_var, planes[2], pltpu.roll(planes[2], 4, 0))
    inverse = 1.0 / density
    velocity_x = moment_x * inverse
    velocity_y = moment_y * inverse
    velocity_z = moment_z * inverse
    kinetic = moment_x * velocity_x + moment_y * velocity_y + moment_z * velocity_z
    pressure = (GAMMA_GAS - 1.0) * (energy - 0.5 * kinetic)
    sound = jnp.sqrt(GAMMA_GAS * pressure * inverse)
    return velocity_x, velocity_y, pressure, sound


def rows_of(var, inst, half):
    return (var // 2) * ROWS + (var % 2) * 4 + inst * 2 + half


def pack_kernel(
    held_state_ref, held_rate_ref, held_next_ref, held_codes_ref, out_ref, next_ref, codes_ref,
    state_ref, rate_ref, sems,
):
    copies = [
        pltpu.make_async_copy(source, target, sems.at[k])
        for k, (source, target) in enumerate(
            (
                (held_state_ref, state_ref),
                (held_rate_ref, rate_ref),
                (held_next_ref, next_ref),
                (held_codes_ref, codes_ref),
            )
        )
    ]
    for copy in copies:
        copy.start()
    for copy in copies:
        copy.wait()
    mirrored = lax.axis_index("cell") // (lax.axis_size("cell") // 2)
    for cell in range(2):
        place = jnp.bitwise_xor(cell, mirrored) * (CELL_ROWS // TILE)
        for var in range(6):
            for inst in range(2):
                for half in range(2):
                    row = rows_of(var, inst, half)
                    out_ref[0, place + row // TILE, pl.ds(row % TILE, 1), :] = state_ref[
                        inst, var, pl.ds(cell, 1), pl.ds(half * LANES, LANES)
                    ]
    rates = [
        rate_ref[pl.ds(cell, 1), pl.ds(half * LANES, LANES)]
        for cell in range(2)
        for half in range(2)
    ]
    for row in range(4):
        out_ref[0, STATE_TILES, pl.ds(row, 1), :] = jnp.where(
            mirrored == 0, rates[row], rates[row ^ 2]
        )
    for tile in range(BLOCK_TILES):
        values = out_ref[0, tile]
        for copy in range(1, out_ref.shape[0]):
            out_ref[copy, tile] = values


def turn_insts(first_inst, plane):
    return jnp.where(first_inst, pltpu.roll(plane, 6, 0), pltpu.roll(plane, 2, 0))


def time_weights(first_inst, shift):
    offsets = spectral_offsets()
    other = jnp.where(
        first_inst, offsets[(2 * shift + 1) % NT], offsets[(2 * shift - 1) % NT]
    )
    return offsets[(2 * shift) % NT], other


def block_plane(ref, place, block, n):
    tiles = ref[place, block, pl.ds(2 * n, 2), :, :]
    return tiles.reshape(ROWS, LANES)


def cell_plane(ref, place, cell, k):
    return block_plane(ref, place, cell // 2, (cell % 2) * PAIRS + k)


def partner_kernel(all_ref, out_ref, middle_ref):
    own_inst = lax.axis_index("inst")
    own_y, core = own_inst >> 1, own_inst & 1
    _, first_inst, _ = plane_masks()
    one, three = time_weights(first_inst, 1), time_weights(first_inst, 3)
    near = [jnp.where(core == 0, a, b) for a, b in zip(one, three)]
    away = [jnp.where(core == 0, b, a) for a, b in zip(one, three)]
    cells = 2 * all_ref.shape[1]
    for cell in range(cells - MIDDLE_CELLS, cells):
        for k in range(PAIRS):
            row = (cell - (cells - MIDDLE_CELLS)) * CELL_ROWS + k * ROWS
            middle_ref[pl.ds(row, ROWS), :] = cell_plane(all_ref, own_y, cell, k)
    for cell in range(cells):
        for k in range(PAIRS):
            here = cell_plane(all_ref, own_y, cell, k)
            there = cell_plane(all_ref, 1 - own_y, cell, k)
            out_ref[pl.ds(cell * CELL_ROWS + k * ROWS, ROWS), :] = (
                near[0] * here
                + away[0] * there
                + turn_insts(first_inst, near[1] * here + away[1] * there)
            )


def two_by_two(first, second):
    def entry(a, b, c, d):
        terms = [x * y for x, y in ((a, b), (c, d)) if x is not None and y is not None]
        return None if not terms else terms[0] if len(terms) == 1 else terms[0] + terms[1]

    return (
        entry(first[0], second[0], first[1], second[2]),
        entry(first[0], second[1], first[1], second[3]),
        entry(first[2], second[0], first[3], second[2]),
        entry(first[2], second[1], first[3], second[3]),
    )


def inverse_of(matrix):
    reciprocal = 1.0 / (matrix[0] * matrix[3] - matrix[1] * matrix[2])
    return (
        matrix[3] * reciprocal,
        -(matrix[1] * reciprocal),
        -(matrix[2] * reciprocal),
        matrix[0] * reciprocal,
    )


def less(first, second):
    return tuple(a if b is None else a - b for a, b in zip(first, second))


def minus(members):
    return tuple(None if a is None else -a for a in members)


def matrix_vector(matrix, low, high):
    def row(a, b):
        terms = [x * y for x, y in ((a, low), (b, high)) if x is not None]
        return terms[0] if len(terms) == 1 else terms[0] + terms[1]

    return row(matrix[0], matrix[1]), row(matrix[2], matrix[3])


def apply_matrix(matrix, side):
    parts = [matrix_vector(matrix, side[k], side[PAIRS + k]) for k in range(PAIRS)]
    return [low for low, _ in parts] + [high for _, high in parts]


def difference(first, second):
    return [a - b for a, b in zip(first, second)]


def flux_along(first_var, planes, velocity, pressure, sign):
    normal = sign * velocity
    return [
        planes[0] * normal + jnp.where(first_var, 0.0, sign * pressure),
        planes[1] * normal,
        planes[2] * normal + jnp.where(first_var, pressure * normal, 0.0),
    ]


class LineCells:
    def __init__(self, first_var, sign):
        self.first_var, self.sign = first_var, sign
        self.state, self.pressure, self.radius = {}, {}, {}
        self.flux, self.step, self.sensor = {}, {}, {}

    def add(self, cell, planes, velocity, pressure, sound):
        self.state[cell], self.pressure[cell] = planes, pressure
        self.radius[cell] = jnp.abs(velocity) + sound
        self.flux[cell] = flux_along(self.first_var, planes, velocity, pressure, self.sign)
        if cell - 1 in self.state:
            self.step[cell - 1] = difference(planes, self.state[cell - 1])
        if cell - 2 in self.state:
            twice = 2.0 * self.pressure[cell - 1]
            outer = pressure + self.pressure[cell - 2]
            self.sensor[cell - 1] = jnp.abs(outer - twice) / (outer + twice)

    def face(self, cell):
        second = SENSOR_GAIN * jnp.maximum(self.sensor[cell], self.sensor[cell + 1])
        fourth = jnp.maximum(0.0, FOURTH_GAIN - second)
        face_radius = 0.5 * (self.radius[cell] + self.radius[cell + 1])
        near_weight = face_radius * (second + 2.0 * fourth)
        far_weight = face_radius * fourth
        return [
            0.5 * (self.flux[cell][k] + self.flux[cell + 1][k])
            - (
                near_weight * self.step[cell][k]
                - far_weight * (self.step[cell + 1][k] + self.step[cell - 1][k])
            )
            for k in range(PAIRS)
        ]

    def near(self, cell):
        scale = SECOND_IMPL * 0.5 + 2.0 * FOURTH_IMPL
        return -scale * (self.radius[cell] + self.radius[cell + 1])

    def far(self, cell):
        return FOURTH_IMPL * self.radius[cell]

    def middle(self, cell, rate):
        centre, above = self.radius[cell], self.radius[cell + 1]
        if cell == 0:
            total, weighted = centre + (centre + above), 4.0 * centre + above
        else:
            below = self.radius[cell - 1]
            total = (below + centre) + (centre + above)
            weighted = below + 4.0 * centre + above
        result = SECOND_IMPL * (0.5 * total) + FOURTH_IMPL * weighted
        return result if rate is None else rate * centre + result

    def diagonal(self, cell, rates):
        across = self.near(cell)
        return (self.middle(cell, rates[0]), across, across, self.middle(cell + 1, rates[1]))

    def below(self, cell):
        return (self.far(cell - 1), self.near(cell - 1), None, self.far(cell))

    def above(self, cell):
        return (self.far(cell + 1), None, self.near(cell + 1), self.far(cell + 2))


def rates_at(ref, place, block, first_half):
    rows = [ref[place, block, STATE_TILES, pl.ds(k, 1), :] for k in range(4)]
    return [jnp.where(first_half, rows[2 * k], rows[2 * k + 1]) for k in range(2)]


def half_kernel(
    all_ref, next_ref, codes_ref, partial_ref, factor_ref, blocks_ref, correction_ref,
    line_ref,
):
    own_y = lax.axis_index("inst") >> 1
    blocks = all_ref.shape[1]
    cells = 2 * blocks
    mirrored = lax.axis_index("cell") // blocks
    sign = (1 - 2 * mirrored).astype(jnp.float32)
    shape = (ROWS, LANES)
    lane_index = lax.broadcasted_iota(jnp.int32, shape, 1)
    first_var, first_inst, half_index = plane_masks()
    first_half = half_index == 0
    zero = jnp.zeros(shape, jnp.float32)

    next_rows = [
        next_ref[pl.ds(half * LANES, LANES)].reshape(1, LANES) for half in range(2)
    ]
    next_line = jnp.where(first_half, next_rows[0], next_rows[1])
    column = lax.broadcasted_iota(jnp.int32, (LANES, LANES), 0)
    prev_halves = []
    for target in range(2):
        total = None
        for source in range(2):
            hits = jnp.where(column + target * LANES == next_rows[source], 1.0, 0.0)
            names = (lane_index + source * LANES).astype(jnp.float32)
            part = lax.dot_general(
                names, hits, (((1,), (1,)), ((), ())), preferred_element_type=jnp.float32
            )
            total = part if total is None else total + part
        prev_halves.append(total)
    prev_line = jnp.where(first_half, prev_halves[0], prev_halves[1]).astype(jnp.int32)

    def picker(lines):
        lane = lines & (LANES - 1)
        same = (lines >> 7) == half_index

        def pick(plane):
            swapped = jnp.where(first_half, pltpu.roll(plane, 7, 0), pltpu.roll(plane, 1, 0))
            here = jnp.take_along_axis(plane, lane, axis=1, mode="promise_in_bounds")
            there = jnp.take_along_axis(swapped, lane, axis=1, mode="promise_in_bounds")
            return jnp.where(same, here, there)

        return pick

    pick_next = picker(next_line)
    pick_prev = picker(prev_line)

    def loaded(cell, place=own_y):
        return [cell_plane(all_ref, place, cell, k) for k in range(PAIRS)]

    own_weights, away_weights = time_weights(first_inst, 0), time_weights(first_inst, 2)

    def own_time_parts(planes, cell):
        return [
            away_weights[0] * away
            + turn_insts(first_inst, own_weights[1] * own + away_weights[1] * away)
            for own, away in zip(planes, loaded(cell, 1 - own_y))
        ]

    def flux_across(planes, velocity, pressure):
        return [
            planes[0] * velocity,
            planes[1] * velocity + jnp.where(first_var, pressure, 0.0),
            planes[2] * velocity + jnp.where(first_var, pressure * velocity, 0.0),
        ]

    def pitch_flux(planes, velocity_y, pressure, sound):
        nearby = [pick_next(plane) for plane in planes]
        _, next_velocity, next_pressure, next_sound = primitives(first_var, nearby)
        own_flux = flux_across(planes, velocity_y, pressure)
        next_flux = flux_across(nearby, next_velocity, next_pressure)
        weight = (PITCH_GAIN * 0.5) * (
            jnp.abs(velocity_y) + sound + (jnp.abs(next_velocity) + next_sound)
        )
        return [
            0.5 * (a + b) - weight * (n - o)
            for a, b, n, o in zip(own_flux, next_flux, nearby, planes)
        ]

    for cell in range(cells):
        planes = loaded(cell)
        velocity_x, velocity_y, pressure, sound = primitives(first_var, planes)
        line_ref[cell, 0], line_ref[cell, 1], line_ref[cell, 2] = velocity_x, pressure, sound
        faces_across = pitch_flux(planes, velocity_y, pressure, sound)
        times = own_time_parts(planes, cell)
        for k in range(PAIRS):
            partial_ref[cell, k] = -(times[k] + (faces_across[k] - pick_prev(faces_across[k])))

    tile = half_index * (LANES // LINES_DEV) + lane_index // LINES_DEV
    end_codes = jnp.where(mirrored == 0, codes_ref[pl.ds(0, 1), :], codes_ref[pl.ds(1, 1), :])
    codes = jnp.zeros(shape, jnp.int32)
    for k in range(2 * LANES // LINES_DEV):
        codes = jnp.where(tile == k, jnp.broadcast_to(end_codes[:, k : k + 1], shape), codes)

    def ghost(cell):
        planes = loaded(-1 - cell)
        copied = loaded(0)
        result = []
        for k in range(PAIRS):
            reflected = planes[k] if k else jnp.where(first_var, planes[k], -planes[k])
            inflow = jnp.where(first_var, FREE_STATE[2 * k], FREE_STATE[2 * k + 1])
            result.append(
                jnp.where(codes == 0, reflected, jnp.where(codes == 1, inflow, copied[k]))
            )
        return result

    line = LineCells(first_var, sign)
    faces, inverses, aboves = {}, [], []
    for cell in range(-2, cells):
        if cell < 0:
            planes = ghost(cell)
            velocity_x, _, pressure, sound = primitives(first_var, planes)
        else:
            planes = loaded(cell)
            velocity_x, pressure, sound = [line_ref[cell, k] for k in range(3)]
        line.add(cell, planes, velocity_x, pressure, sound)
        if cell >= 1:
            faces[cell - 2] = line.face(cell - 2)
        if cell >= 2:
            at = cell - 2
            for k in range(PAIRS):
                partial_ref[at, k] = partial_ref[at, k] + (faces[at - 1][k] - faces[at][k])
        if cell >= 3 and cell % 2 == 1:
            at = cell - 3
            block = at // 2
            rates = rates_at(all_ref, own_y, block, first_half)
            diag = line.diagonal(at, rates)
            if block > 0:
                factor = two_by_two(line.below(at), inverses[-1])
                diag = less(diag, two_by_two(factor, aboves[-1]))
                for n in range(4):
                    factor_ref[block - 1, n] = factor[n]
            inverses.append(inverse_of(diag))
            aboves.append(line.above(at))
            kept = [*inverses[-1], aboves[-1][0], *aboves[-1][2:]]
            for n, plane in enumerate(kept):
                blocks_ref[block, n] = plane

    last = cells - 2
    for k in range(PAIRS):
        partial_ref[last, k] = partial_ref[last, k] + faces[last - 1][k]
    factor = two_by_two(line.below(last), inverses[-1])
    for n in range(4):
        factor_ref[blocks - 2, n] = factor[n]
    correction = list(two_by_two(factor, aboves[-1]))
    rates = rates_at(all_ref, own_y, blocks - 1, first_half)
    for member in range(2):
        centre = line.radius[last + member]
        correction[3 * member] = correction[3 * member] - rates[member] * centre
    for n in range(2):
        correction_ref[pl.ds(n * ROWS, ROWS), :] = jnp.where(
            first_var, correction[2 * n], correction[2 * n + 1]
        )


def reduce_kernel(partial_ref, time_ref, factor_ref, correction_ref, middle_ref, sides_ref):
    for row in range(0, 2 * ROWS, ROWS):
        middle_ref[pl.ds(CORRECTION_ROW + row, ROWS), :] = correction_ref[pl.ds(row, ROWS), :]
    blocks = partial_ref.shape[0] // 2
    side = None
    for block in range(blocks):
        own = []
        for cell in (2 * block, 2 * block + 1):
            for k in range(PAIRS):
                time = time_ref[pl.ds(cell * CELL_ROWS + k * ROWS, ROWS), :]
                own.append(partial_ref[cell, k] - time)
        if block > 0:
            factor = [factor_ref[block - 1, n] for n in range(4)]
            own = difference(own, apply_matrix(factor, side))
        side = own
        for n, plane in enumerate(side):
            if block < blocks - 1:
                sides_ref[block, n] = plane
            else:
                middle_ref[pl.ds(n * ROWS, ROWS), :] = plane


def spread_kernel(all_ref, blocks_ref, sides_ref, known_ref, spread_ref, table_ref):
    own_y = lax.axis_index("inst") >> 1
    blocks = all_ref.shape[1]
    own_cell = lax.axis_index("cell")
    own_block = jnp.where(own_cell < blocks, own_cell, 2 * blocks - 1 - own_cell)
    zero = jnp.zeros((ROWS, LANES), jnp.float32)
    known, spread = [zero] * (2 * PAIRS), (zero + 1.0, zero, zero, zero + 1.0)
    for block in range(blocks - 1, -1, -1):
        if block < blocks - 1:
            kept = [blocks_ref[block, n] for n in range(7)]
            inverse, above = kept[:4], (kept[4], None, kept[5], kept[6])
            side = [sides_ref[block, n] for n in range(2 * PAIRS)]
            step = two_by_two(inverse, above)
            own = apply_matrix(inverse, side)
            if block < blocks - 2:
                known = difference(own, apply_matrix(step, known))
                spread = minus(two_by_two(step, spread))
            else:
                known, spread = own, minus(step)
        for n, plane in enumerate(known + list(spread)):
            table_ref[block, n] = plane
    for n in range(2 * PAIRS):
        base = block_plane(all_ref, own_y, own_block, n)
        known_ref[n] = base + table_ref[own_block, n]
    for n in range(4):
        spread_ref[n] = table_ref[own_block, 2 * PAIRS + n]


def plane_of(ref, row):
    return ref[pl.ds(row, ROWS), :]


def correction_of(first_var, ref):
    pairs = [both(first_var, plane_of(ref, CORRECTION_ROW + n * ROWS)) for n in range(2)]
    return [pairs[0][0], pairs[0][1], pairs[1][0], pairs[1][1]]


def middle_kernel(here_ref, there_ref, here_side_ref, side_ref, other_ref, matrix_ref):
    mirrored = lax.axis_index("cell") // (lax.axis_size("cell") // 2)
    sign = (1 - 2 * mirrored).astype(jnp.float32)
    first_var, _, _ = plane_masks()
    line = LineCells(first_var, sign)
    for cell in range(6):
        ref, at = (here_ref, cell) if cell < 3 else (there_ref, 5 - cell)
        planes = [plane_of(ref, at * CELL_ROWS + k * ROWS) for k in range(PAIRS)]
        velocity_x, _, pressure, sound = primitives(first_var, planes)
        line.add(cell, planes, velocity_x, pressure, sound)
    faces = {cell: line.face(cell) for cell in (1, 2, 3)}
    for k in range(PAIRS):
        side_ref[k] = plane_of(here_side_ref, k * ROWS) - faces[1][k]
        side_ref[PAIRS + k] = plane_of(here_side_ref, (PAIRS + k) * ROWS) + (
            faces[1][k] - faces[2][k]
        )
        other_ref[k] = faces[2][k] - faces[3][k]
        other_ref[PAIRS + k] = faces[3][k]
    no_rates = (None, None)
    diag = difference(line.diagonal(1, no_rates), correction_of(first_var, here_side_ref))
    above, below = line.above(1), line.below(3)
    kept = [*diag, *line.diagonal(3, no_rates), above[0], *above[2:], *below[:2], below[3]]
    for n, plane in enumerate(kept):
        matrix_ref[n] = plane


def join_kernel(
    side_ref, other_ref, matrix_ref, there_side_ref, known_ref, spread_ref, out_ref
):
    mirrored = lax.axis_index("cell") // (lax.axis_size("cell") // 2)
    first_var, _, _ = plane_masks()
    kept = [matrix_ref[n] for n in range(14)]
    diag, other_diag = kept[:4], kept[4:8]
    above, below = (kept[8], None, kept[9], kept[10]), (kept[11], kept[12], None, kept[13])
    other_diag = difference(other_diag, correction_of(first_var, there_side_ref)[::-1])
    other = []
    for member in range(2):
        for k in range(PAIRS):
            there = plane_of(there_side_ref, ((1 - member) * PAIRS + k) * ROWS)
            other.append(there + other_ref[member * PAIRS + k])
    factor = two_by_two(above, inverse_of(other_diag))
    diag = less(diag, two_by_two(factor, below))
    side = [side_ref[n] for n in range(2 * PAIRS)]
    middle = apply_matrix(inverse_of(diag), difference(side, apply_matrix(factor, other)))
    moved = apply_matrix([spread_ref[n] for n in range(4)], middle)
    results = [known_ref[n] + moved[n] for n in range(2 * PAIRS)]
    for cell in range(2):
        for k in range(PAIRS):
            first, second = results[cell * PAIRS + k], results[(1 - cell) * PAIRS + k]
            result = jnp.where(mirrored == 0, first, second)
            for var in range(2):
                for inst in range(2):
                    for half in range(2):
                        row = rows_of(var, inst, half)
                        out_ref[
                            inst, 2 * k + var, pl.ds(cell, 1), pl.ds(half * LANES, LANES)
                        ] = result[row : row + 1]


def share_half(copies):
    insts, count = lax.axis_size("inst"), lax.axis_size("cell")
    halves = [range(count // 2), range(count - 1, count // 2 - 1, -1)]
    groups = [
        [inst * count + cell for inst in range(core, insts, 2) for cell in half]
        for core in range(2)
        for half in halves
    ]
    return lax.all_to_all(
        copies, ("inst", "cell"), split_axis=0, concat_axis=0, tiled=True,
        axis_index_groups=groups,
    )


def swap_cores(block):
    pairs = [(inst, inst ^ 1) for inst in range(lax.axis_size("inst"))]
    return lax.ppermute(block, "inst", pairs)


def swap_halves(block):
    count = lax.axis_size("cell")
    return lax.ppermute(block, "cell", [(i, (i + count // 2) % count) for i in range(count)])


def float_shape(*sizes):
    return jax.ShapeDtypeStruct(sizes, jnp.float32)


def local_by_halves(state, pseudo_rate, line_next, face_codes):
    blocks = lax.axis_size("cell") // 2
    cells = 2 * blocks
    vmem = pl.BlockSpec(memory_space=pltpu.VMEM)
    plane = (ROWS, LANES)
    params = pltpu.CompilerParams(vmem_limit_bytes=VMEM_BYTES)
    places = lax.axis_size("inst") // 2
    held = [
        pltpu.with_memory_space_constraint(array, pltpu.HBM)
        for array in (state, pseudo_rate, line_next, face_codes)
    ]
    packed, next_here, codes_here = pl.pallas_call(
        pack_kernel,
        out_shape=(
            float_shape(places * blocks, BLOCK_TILES, TILE, LANES),
            jax.ShapeDtypeStruct(line_next.shape, jnp.int32),
            jax.ShapeDtypeStruct(face_codes.shape, jnp.int32),
        ),
        in_specs=[pl.BlockSpec(memory_space=pltpu.HBM)] * 4,
        out_specs=(vmem, vmem, vmem),
        scratch_shapes=[
            pltpu.VMEM(state.shape, jnp.float32),
            pltpu.VMEM(pseudo_rate.shape, jnp.float32),
            pltpu.SemaphoreType.DMA((4,)),
        ],
        compiler_params=params,
    )(*held)
    shared = share_half(packed).reshape(places, blocks, BLOCK_TILES, TILE, LANES)
    for_partner, here = pl.pallas_call(
        partner_kernel,
        out_shape=(
            float_shape(cells * CELL_ROWS, LANES),
            float_shape(MIDDLE_CELLS * CELL_ROWS, LANES),
        ),
        in_specs=[vmem],
        out_specs=(vmem, vmem),
        compiler_params=params,
    )(shared)
    from_partner = swap_cores(for_partner)
    there = swap_halves(here)
    beside = pl.CostEstimate(flops=10**6, bytes_accessed=10**6, transcendentals=0)
    partial, factors, eliminated, correction = pl.pallas_call(
        half_kernel,
        out_shape=(
            float_shape(cells, PAIRS, *plane),
            float_shape(blocks - 1, 4, *plane),
            float_shape(blocks - 1, 7, *plane),
            float_shape(2 * ROWS, LANES),
        ),
        in_specs=[vmem] * 3,
        out_specs=(vmem,) * 4,
        scratch_shapes=[pltpu.VMEM((cells, 3) + plane, jnp.float32)],
        compiler_params=params,
        cost_estimate=beside,
    )(shared, next_here, codes_here)
    here_side, sides = pl.pallas_call(
        reduce_kernel,
        out_shape=(
            float_shape(SIDE_ROWS, LANES),
            float_shape(blocks - 1, 2 * PAIRS, *plane),
        ),
        in_specs=[vmem] * 4,
        out_specs=(vmem, vmem),
        compiler_params=params,
    )(partial, from_partner, factors, correction)
    there_side = swap_halves(here_side)
    known, spread = pl.pallas_call(
        spread_kernel,
        out_shape=(float_shape(2 * PAIRS, *plane), float_shape(4, *plane)),
        in_specs=[vmem] * 3,
        out_specs=(vmem, vmem),
        scratch_shapes=[pltpu.VMEM((blocks, 2 * PAIRS + 4) + plane, jnp.float32)],
        compiler_params=params,
        cost_estimate=beside,
    )(shared, eliminated, sides)
    side, other, matrices = pl.pallas_call(
        middle_kernel,
        out_shape=(
            float_shape(2 * PAIRS, *plane),
            float_shape(2 * PAIRS, *plane),
            float_shape(14, *plane),
        ),
        in_specs=[vmem] * 3,
        out_specs=(vmem,) * 3,
        compiler_params=params,
        cost_estimate=beside,
    )(here, there, here_side)
    return pl.pallas_call(
        join_kernel,
        out_shape=float_shape(*state.shape),
        in_specs=[vmem] * 6,
        out_specs=vmem,
        compiler_params=params,
    )(side, other, matrices, there_side, known, spread)


def solution(mesh):
    placed = (P("inst", None, "cell", None), P("cell", None), P(), P())
    inst_count, cell_count = mesh.shape["inst"], mesh.shape["cell"]

    def local(state, pseudo_rate, line_next, face_codes):
        small = (
            state.shape == (2, 6, 2, 2 * LANES)
            and inst_count * 2 == NT
            and cell_count == 8
            and face_codes.shape[1] * LINES_DEV == state.shape[3]
        )
        chosen = local_by_halves if small else local_by_lines
        return chosen(state, pseudo_rate, line_next, face_codes)

    return jax.shard_map(
        local, mesh=mesh, in_specs=placed, out_specs=P("inst", None, "cell", None), check_vma=False
    )
```

```python
import functools

import jax
import jax.numpy as jnp
import numpy as np
from jax import lax
from jax.experimental import pallas as pl
from jax.experimental.pallas import tpu as pltpu
from jax.sharding import PartitionSpec as P

NT = 8
LINES_DEV = 32


GAMMA_GAS = 1.4
OMEGA_BLADE = 1.0
SENSOR_GAIN = 0.25
FOURTH_GAIN = 0.03125
PITCH_GAIN = 0.5
SECOND_IMPL = 1.0
FOURTH_IMPL = 0.25
FREE_STATE = (1.0, 0.5, 0.0, 0.0, 2.625, 0.2)
MIRROR_SIGNS = (1.0, -1.0, 1.0, 1.0, 1.0, 1.0)
ZERO_BLOCK = (0.0, 0.0, 0.0, 0.0)
UNIT_BLOCK = (1.0, 0.0, 0.0, 1.0)
ZERO_PAIR = (0.0, 0.0)


def extended(block, sides, width):
    for axis, dim in sides:
        count = lax.axis_size(axis)
        forward = [(i, i + 1) for i in range(count - 1)]
        backward = [(target, source) for source, target in forward]
        low = lax.ppermute(
            lax.slice_in_dim(block, block.shape[dim] - width, None, axis=dim), axis, forward
        )
        high = lax.ppermute(lax.slice_in_dim(block, 0, width, axis=dim), axis, backward)
        block = jnp.concatenate([low, block, high], axis=dim)
    return block


def spectral_matrix(instances):
    offsets = np.arange(instances)[:, None] - np.arange(instances)[None, :]
    angles = np.pi * offsets / instances
    safe_sin = np.where(offsets == 0, 1.0, np.sin(angles))
    parity = np.where(np.mod(offsets, 2) == 0, -1.0, 1.0)
    matrix_table = np.where(
        offsets == 0, 0.0, 0.5 * OMEGA_BLADE * parity * np.cos(angles) / safe_sin
    )
    return jnp.asarray(matrix_table, jnp.float32)


def primitive_parts(cells_state):
    density = cells_state[..., 0, :, :]
    inverse = 1.0 / density
    velocity_x = cells_state[..., 1, :, :] * inverse
    velocity_y = cells_state[..., 2, :, :] * inverse
    velocity_z = cells_state[..., 3, :, :] * inverse
    energy = cells_state[..., 4, :, :]
    pressure = (GAMMA_GAS - 1.0) * (
        energy
        - 0.5
        * density
        * (velocity_x * velocity_x + velocity_y * velocity_y + velocity_z * velocity_z)
    )
    sound_speed = jnp.sqrt(GAMMA_GAS * pressure * inverse)
    return (velocity_x, velocity_y, pressure, sound_speed)


def directed_flux(cells_state, normal_velocity, pressure, component):
    zero_plane = jnp.zeros_like(pressure)
    pressure_rows = [
        zero_plane,
        zero_plane,
        zero_plane,
        zero_plane,
        pressure * normal_velocity,
        zero_plane,
    ]
    pressure_rows[component] = pressure
    return cells_state * normal_velocity[..., None, :, :] + jnp.stack(pressure_rows, axis=-3)


def line_residual(padded):
    velocity_x, velocity_y, pressure, sound_speed = primitive_parts(padded)
    flux_line = directed_flux(padded, velocity_x, pressure, 1)
    radius = jnp.abs(velocity_x) + sound_speed
    sensor = jnp.abs(
        pressure[..., 2:, :] - 2.0 * pressure[..., 1:-1, :] + pressure[..., :-2, :]
    ) / (pressure[..., 2:, :] + 2.0 * pressure[..., 1:-1, :] + pressure[..., :-2, :])
    second = SENSOR_GAIN * jnp.maximum(sensor[..., :-1, :], sensor[..., 1:, :])
    fourth = jnp.maximum(0.0, FOURTH_GAIN - second)
    face_radius = 0.5 * (radius[..., 1:-2, :] + radius[..., 2:-1, :])
    left_far = padded[..., :-3, :]
    left_near = padded[..., 1:-2, :]
    right_near = padded[..., 2:-1, :]
    right_far = padded[..., 3:, :]
    damping = face_radius[..., None, :, :] * (
        second[..., None, :, :] * (right_near - left_near)
        - fourth[..., None, :, :] * (right_far - 3.0 * right_near + 3.0 * left_near - left_far)
    )
    face_flux = 0.5 * (flux_line[..., 1:-2, :] + flux_line[..., 2:-1, :]) - damping
    return (face_flux[..., 1:, :] - face_flux[..., :-1, :], radius)


def pitch_parts(cells_state):
    velocity_x, velocity_y, pressure, sound_speed = primitive_parts(cells_state)
    return (directed_flux(cells_state, velocity_y, pressure, 2), jnp.abs(velocity_y) + sound_speed)


def pitch_residual(cells_state, next_lines, prev_lines):
    pitch_flux, radius = pitch_parts(cells_state)
    state_next = jnp.take(cells_state, next_lines, axis=-1)
    flux_next, radius_next = pitch_parts(state_next)
    face_flux = 0.5 * (pitch_flux + flux_next) - PITCH_GAIN * (0.5 * (radius + radius_next))[
        ..., None, :, :
    ] * (state_next - cells_state)
    return face_flux - jnp.take(face_flux, prev_lines, axis=-1)


def boundary_cells(edge_pair, line_codes, lower_end):
    reflected = edge_pair[..., ::-1, :] * jnp.asarray(MIRROR_SIGNS, jnp.float32)[:, None, None]
    if lower_end:
        copied = jnp.concatenate([edge_pair[..., :1, :], edge_pair[..., :1, :]], axis=-2)
    else:
        copied = jnp.concatenate([edge_pair[..., 1:, :], edge_pair[..., 1:, :]], axis=-2)
    inflow = jnp.asarray(FREE_STATE, jnp.float32)[:, None, None] + jnp.zeros_like(edge_pair)
    return jnp.where(line_codes == 0, reflected, jnp.where(line_codes == 1, inflow, copied))


def line_coefficients(radius_ext, diagonal_term, positions, total_cells):
    radius_below = radius_ext[..., :-2, :]
    radius_centre = radius_ext[..., 1:-1, :]
    radius_above = radius_ext[..., 2:, :]
    face_below = 0.5 * (radius_below + radius_centre)
    face_above = 0.5 * (radius_centre + radius_above)
    far_low = FOURTH_IMPL * radius_below
    near_low = -SECOND_IMPL * face_below - 2.0 * FOURTH_IMPL * (radius_below + radius_centre)
    middle = (
        diagonal_term
        + SECOND_IMPL * (face_below + face_above)
        + FOURTH_IMPL * (radius_below + 4.0 * radius_centre + radius_above)
    )
    near_high = -SECOND_IMPL * face_above - 2.0 * FOURTH_IMPL * (radius_centre + radius_above)
    far_high = FOURTH_IMPL * radius_above
    column = positions[:, None]
    far_low = jnp.where(column >= 2, far_low, 0.0)
    near_low = jnp.where(column >= 1, near_low, 0.0)
    near_high = jnp.where(column <= total_cells - 2, near_high, 0.0)
    far_high = jnp.where(column <= total_cells - 3, far_high, 0.0)
    return (far_low, near_low, middle, near_high, far_high)


def block_product(first_matrix, second_matrix):
    return (
        first_matrix[0] * second_matrix[0] + first_matrix[1] * second_matrix[2],
        first_matrix[0] * second_matrix[1] + first_matrix[1] * second_matrix[3],
        first_matrix[2] * second_matrix[0] + first_matrix[3] * second_matrix[2],
        first_matrix[2] * second_matrix[1] + first_matrix[3] * second_matrix[3],
    )


def block_inverse(matrix):
    determinant = matrix[0] * matrix[3] - matrix[1] * matrix[2]
    reciprocal = 1.0 / determinant
    return (
        matrix[3] * reciprocal,
        -matrix[1] * reciprocal,
        -matrix[2] * reciprocal,
        matrix[0] * reciprocal,
    )


def block_apply(matrix, vector):
    return (
        matrix[0] * vector[0] + matrix[1] * vector[1],
        matrix[2] * vector[0] + matrix[3] * vector[1],
    )


def add_blocks(first_members, second_members):
    return tuple((a + b for a, b in zip(first_members, second_members)))


def negate(members):
    return tuple((-a for a in members))


def extend_blocks(members, fill_values):
    return tuple(
        (
            jnp.concatenate([m, jnp.full_like(m[..., :1, :], f)], axis=-2)
            for m, f in zip(members, fill_values)
        )
    )


def shift_next(members, fill_values):
    return tuple(
        (
            jnp.concatenate([m[..., 1:, :], jnp.full_like(m[..., :1, :], f)], axis=-2)
            for m, f in zip(members, fill_values)
        )
    )


def shift_prev(members):
    return tuple(
        (jnp.concatenate([jnp.zeros_like(m[..., :1, :]), m[..., :-1, :]], axis=-2) for m in members)
    )


def pair_split(member):
    shaped = member.reshape(member.shape[:-2] + (member.shape[-2] // 2, 2, member.shape[-1]))
    return (shaped[..., 0, :], shaped[..., 1, :])


def split_parity(members):
    halves = [pair_split(m) for m in members]
    return (tuple((h[0] for h in halves)), tuple((h[1] for h in halves)))


def alternate(first_member, second_member):
    stacked = jnp.stack((first_member, second_member), axis=-2)
    return stacked.reshape(
        first_member.shape[:-2] + (2 * first_member.shape[-2], first_member.shape[-1])
    )


def reduce_blocks(sub_blocks, diag_blocks, super_blocks, right_side):
    block_count = diag_blocks[0].shape[-2]
    if block_count == 1:
        return block_apply(block_inverse(diag_blocks), right_side)
    if block_count % 2 == 1:
        sub_blocks = extend_blocks(sub_blocks, ZERO_BLOCK)
        diag_blocks = extend_blocks(diag_blocks, UNIT_BLOCK)
        super_blocks = extend_blocks(super_blocks, ZERO_BLOCK)
        right_side = extend_blocks(right_side, ZERO_PAIR)
    sub_even, sub_odd = split_parity(sub_blocks)
    diag_even, diag_odd = split_parity(diag_blocks)
    super_even, super_odd = split_parity(super_blocks)
    side_even, side_odd = split_parity(right_side)
    inverse_even = block_inverse(diag_even)
    inverse_next = shift_next(inverse_even, UNIT_BLOCK)
    sub_next = shift_next(sub_even, ZERO_BLOCK)
    super_next = shift_next(super_even, ZERO_BLOCK)
    side_next = shift_next(side_even, ZERO_PAIR)
    left_factor = negate(block_product(sub_odd, inverse_even))
    right_factor = negate(block_product(super_odd, inverse_next))
    reduced_sub = block_product(left_factor, sub_even)
    reduced_diag = add_blocks(
        diag_odd,
        add_blocks(block_product(left_factor, super_even), block_product(right_factor, sub_next)),
    )
    reduced_super = block_product(right_factor, super_next)
    reduced_side = add_blocks(
        side_odd,
        add_blocks(block_apply(left_factor, side_even), block_apply(right_factor, side_next)),
    )
    odd_values = reduce_blocks(reduced_sub, reduced_diag, reduced_super, reduced_side)
    before_values = shift_prev(odd_values)
    remainder = add_blocks(
        side_even,
        negate(
            add_blocks(block_apply(sub_even, before_values), block_apply(super_even, odd_values))
        ),
    )
    even_values = block_apply(inverse_even, remainder)
    merged = tuple((alternate(e, o) for e, o in zip(even_values, odd_values)))
    return tuple((m[..., :block_count, :] for m in merged))


def cells_leading(block):
    moved = jnp.transpose(block, (2, 0, 1, 3))
    return moved.reshape(block.shape[2], block.shape[0] * block.shape[1] * block.shape[3])


def solve_in_lanes(coefficients, line_source):
    source_shape = line_source.shape
    lane_coef = [cells_leading(jnp.broadcast_to(c[:, None], source_shape)) for c in coefficients]
    pairs_list = [pair_split(m) for m in lane_coef]
    zero_plane = jnp.zeros_like(pairs_list[2][0])
    sub_blocks = (pairs_list[0][0], pairs_list[1][0], zero_plane, pairs_list[0][1])
    diag_blocks = (pairs_list[2][0], pairs_list[3][0], pairs_list[1][1], pairs_list[2][1])
    super_blocks = (pairs_list[4][0], zero_plane, pairs_list[3][1], pairs_list[4][1])
    values = reduce_blocks(
        sub_blocks, diag_blocks, super_blocks, pair_split(cells_leading(line_source))
    )
    flat = alternate(values[0], values[1])
    shaped = flat.reshape(source_shape[2], source_shape[0], source_shape[1], source_shape[3])
    return jnp.transpose(shaped, (1, 2, 0, 3))


def return_tiles(line_values):
    return lax.all_to_all(line_values, "cell", split_axis=2, concat_axis=3, tiled=True)


def local_by_lines(state, pseudo_rate, line_next, face_codes):
    local_count = state.shape[0]
    tile_cells = state.shape[2]
    cell_index = lax.axis_index("cell")
    cell_count = lax.axis_size("cell")
    total_cells = tile_cells * cell_count
    spectral = spectral_matrix(NT)
    first_local = lax.axis_index("inst") * local_count
    own_rows = lax.dynamic_slice_in_dim(spectral, first_local, local_count, 0)
    shard_block = jax.tree.map(lambda a: lax.all_gather(a, "inst", axis=0, tiled=True), state)
    columns = lax.slice_in_dim(own_rows, 0, shard_block.shape[0], axis=1)
    time_term = jnp.zeros_like(state) + jnp.einsum(
        "nm,mvil->nvil", columns, shard_block, precision=lax.Precision.HIGHEST
    )
    padded = extended(state, (("cell", 2),), 2)
    codes_lines = jnp.repeat(face_codes, LINES_DEV, axis=1)
    lower_ghost = boundary_cells(state[:, :, 0:2, :], codes_lines[0], True)
    upper_ghost = boundary_cells(state[:, :, -2:, :], codes_lines[1], False)
    lower_rim = jnp.where(cell_index == 0, lower_ghost, padded[:, :, :2, :])
    upper_rim = jnp.where(cell_index == cell_count - 1, upper_ghost, padded[:, :, -2:, :])
    padded = jnp.concatenate([lower_rim, padded[:, :, 2:-2, :], upper_rim], axis=2)
    line_part, radius = line_residual(padded)
    prev_lines = (
        jnp.zeros_like(line_next).at[line_next].set(jnp.arange(line_next.shape[0], dtype=jnp.int32))
    )
    residual = line_part + pitch_residual(state, line_next, prev_lines) + time_term
    right_side = -residual
    centre_radius = radius[:, 2:-2, :]
    diagonal_term = pseudo_rate * centre_radius
    positions = cell_index * tile_cells + jnp.arange(-1, tile_cells + 1, dtype=jnp.int32)
    inside = (positions >= 0) & (positions < total_cells)
    radius_ext = jnp.where(inside[:, None], radius[:, 1:-1, :], 0.0)
    coefficients = line_coefficients(radius_ext, diagonal_term, positions[1:-1], total_cells)
    stacked = jnp.stack(coefficients, axis=1)
    line_source = lax.all_to_all(right_side, "cell", split_axis=3, concat_axis=2, tiled=True)
    line_coef = lax.all_to_all(stacked, "cell", split_axis=3, concat_axis=2, tiled=True)
    update = return_tiles(solve_in_lanes(tuple((line_coef[:, k] for k in range(5))), line_source))
    return state + update


LANES = 128
ROWS = 8
PAIRS = 3
CELL_ROWS = PAIRS * ROWS
RATE_ROW = 2 * CELL_ROWS
VMEM_BYTES = 8 * 2**20
BLOCK_ROWS = RATE_ROW + ROWS

MIDDLE_CELLS = 3
CORRECTION_ROW = 2 * CELL_ROWS
SIDE_ROWS = CORRECTION_ROW + 2 * ROWS


def spectral_offsets():
    table = np.zeros(NT)
    for offset in range(1, NT):
        angle = np.pi * offset / NT
        parity = -1.0 if offset % 2 == 0 else 1.0
        table[offset] = 0.5 * OMEGA_BLADE * parity * np.cos(angle) / np.sin(angle)
    return [float(np.float32(value)) for value in table]


def plane_masks():
    row_index = lax.broadcasted_iota(jnp.int32, (ROWS, LANES), 0)
    return row_index < 4, (row_index & 2) == 0, row_index & 1


def both(first_var, plane):
    turned = pltpu.roll(plane, 4, 0)
    return jnp.where(first_var, plane, turned), jnp.where(first_var, turned, plane)


def primitives(first_var, planes):
    density, moment_x = both(first_var, planes[0])
    moment_y, moment_z = both(first_var, planes[1])
    energy = jnp.where(first_var, planes[2], pltpu.roll(planes[2], 4, 0))
    inverse = 1.0 / density
    velocity_x = moment_x * inverse
    velocity_y = moment_y * inverse
    velocity_z = moment_z * inverse
    kinetic = moment_x * velocity_x + moment_y * velocity_y + moment_z * velocity_z
    pressure = (GAMMA_GAS - 1.0) * (energy - 0.5 * kinetic)
    sound = jnp.sqrt(GAMMA_GAS * pressure * inverse)
    return velocity_x, velocity_y, pressure, sound


def rows_of(var, inst, half):
    return (var // 2) * ROWS + (var % 2) * 4 + inst * 2 + half


def pack_kernel(
    held_state_ref, held_rate_ref, held_next_ref, held_codes_ref, out_ref, next_ref, codes_ref,
    state_ref, rate_ref, sems,
):
    copies = [
        pltpu.make_async_copy(source, target, sems.at[k])
        for k, (source, target) in enumerate(
            (
                (held_state_ref, state_ref),
                (held_rate_ref, rate_ref),
                (held_next_ref, next_ref),
                (held_codes_ref, codes_ref),
            )
        )
    ]
    for copy in copies:
        copy.start()
    for copy in copies:
        copy.wait()
    mirrored = lax.axis_index("cell") // (lax.axis_size("cell") // 2)
    for cell in range(2):
        place = pl.multiple_of(jnp.bitwise_xor(cell, mirrored) * CELL_ROWS, ROWS)
        for k in range(PAIRS):
            rows = [
                state_ref[inst, 2 * k + var, pl.ds(cell, 1), pl.ds(half * LANES, LANES)]
                for var in range(2)
                for inst in range(2)
                for half in range(2)
            ]
            for row, values in enumerate(rows):
                out_ref[0, pl.ds(place + (k * ROWS + row), 1), :] = values
    rates = [
        rate_ref[pl.ds(cell, 1), pl.ds(half * LANES, LANES)]
        for cell in range(2)
        for half in range(2)
    ]
    for row in range(4):
        out_ref[0, pl.ds(RATE_ROW + row, 1), :] = jnp.where(
            mirrored == 0, rates[row], rates[row ^ 2]
        )
    out_ref[0, pl.ds(RATE_ROW + 4, 4), :] = jnp.zeros((4, LANES), jnp.float32)
    for row in range(0, BLOCK_ROWS, ROWS):
        values = out_ref[0, pl.ds(row, ROWS), :]
        for copy in range(1, out_ref.shape[0]):
            out_ref[copy, pl.ds(row, ROWS), :] = values


def turn_insts(first_inst, plane):
    return jnp.where(first_inst, pltpu.roll(plane, 6, 0), pltpu.roll(plane, 2, 0))


def time_weights(first_inst, shift):
    offsets = spectral_offsets()
    other = jnp.where(
        first_inst, offsets[(2 * shift + 1) % NT], offsets[(2 * shift - 1) % NT]
    )
    return offsets[(2 * shift) % NT], other


def at_block(ref, y, block):
    return ref.at[ref.shape[0] - 1 - y, ref.shape[1] - 1 - block]


def cell_plane(ref, y, cell, k):
    return at_block(ref, y, cell // 2)[pl.ds((cell % 2) * CELL_ROWS + k * ROWS, ROWS), :]


def partner_kernel(all_ref, out_ref, middle_ref):
    own_inst = lax.axis_index("inst")
    own_y, core = own_inst >> 1, own_inst & 1
    _, first_inst, _ = plane_masks()
    one, three = time_weights(first_inst, 1), time_weights(first_inst, 3)
    near = [jnp.where(core == 0, a, b) for a, b in zip(one, three)]
    away = [jnp.where(core == 0, b, a) for a, b in zip(one, three)]
    cells = 2 * all_ref.shape[1]
    for cell in range(cells - MIDDLE_CELLS, cells):
        for k in range(PAIRS):
            row = (cell - (cells - MIDDLE_CELLS)) * CELL_ROWS + k * ROWS
            middle_ref[pl.ds(row, ROWS), :] = cell_plane(all_ref, own_y, cell, k)
    for cell in range(cells):
        for k in range(PAIRS):
            here = cell_plane(all_ref, own_y, cell, k)
            there = cell_plane(all_ref, 1 - own_y, cell, k)
            out_ref[pl.ds(cell * CELL_ROWS + k * ROWS, ROWS), :] = (
                near[0] * here
                + away[0] * there
                + turn_insts(first_inst, near[1] * here + away[1] * there)
            )


def two_by_two(first, second):
    def entry(a, b, c, d):
        terms = [x * y for x, y in ((a, b), (c, d)) if x is not None and y is not None]
        return None if not terms else terms[0] if len(terms) == 1 else terms[0] + terms[1]

    return (
        entry(first[0], second[0], first[1], second[2]),
        entry(first[0], second[1], first[1], second[3]),
        entry(first[2], second[0], first[3], second[2]),
        entry(first[2], second[1], first[3], second[3]),
    )


def inverse_of(matrix):
    reciprocal = 1.0 / (matrix[0] * matrix[3] - matrix[1] * matrix[2])
    return (
        matrix[3] * reciprocal,
        -(matrix[1] * reciprocal),
        -(matrix[2] * reciprocal),
        matrix[0] * reciprocal,
    )


def less(first, second):
    return tuple(a if b is None else a - b for a, b in zip(first, second))


def minus(members):
    return tuple(None if a is None else -a for a in members)


def matrix_vector(matrix, low, high):
    def row(a, b):
        terms = [x * y for x, y in ((a, low), (b, high)) if x is not None]
        return terms[0] if len(terms) == 1 else terms[0] + terms[1]

    return row(matrix[0], matrix[1]), row(matrix[2], matrix[3])


def apply_matrix(matrix, side):
    parts = [matrix_vector(matrix, side[k], side[PAIRS + k]) for k in range(PAIRS)]
    return [low for low, _ in parts] + [high for _, high in parts]


def difference(first, second):
    return [a - b for a, b in zip(first, second)]


def flux_along(first_var, planes, velocity, pressure, sign):
    normal = sign * velocity
    return [
        planes[0] * normal + jnp.where(first_var, 0.0, sign * pressure),
        planes[1] * normal,
        planes[2] * normal + jnp.where(first_var, pressure * normal, 0.0),
    ]


class LineCells:
    def __init__(self, first_var, sign):
        self.first_var, self.sign = first_var, sign
        self.state, self.pressure, self.radius = {}, {}, {}
        self.flux, self.step, self.sensor = {}, {}, {}

    def add(self, cell, planes, velocity, pressure, sound):
        self.state[cell], self.pressure[cell] = planes, pressure
        self.radius[cell] = jnp.abs(velocity) + sound
        self.flux[cell] = flux_along(self.first_var, planes, velocity, pressure, self.sign)
        if cell - 1 in self.state:
            self.step[cell - 1] = difference(planes, self.state[cell - 1])
        if cell - 2 in self.state:
            twice = 2.0 * self.pressure[cell - 1]
            outer = pressure + self.pressure[cell - 2]
            self.sensor[cell - 1] = jnp.abs(outer - twice) / (outer + twice)

    def face(self, cell):
        second = SENSOR_GAIN * jnp.maximum(self.sensor[cell], self.sensor[cell + 1])
        fourth = jnp.maximum(0.0, FOURTH_GAIN - second)
        face_radius = 0.5 * (self.radius[cell] + self.radius[cell + 1])
        near_weight = face_radius * (second + 2.0 * fourth)
        far_weight = face_radius * fourth
        return [
            0.5 * (self.flux[cell][k] + self.flux[cell + 1][k])
            - (
                near_weight * self.step[cell][k]
                - far_weight * (self.step[cell + 1][k] + self.step[cell - 1][k])
            )
            for k in range(PAIRS)
        ]

    def near(self, cell):
        scale = SECOND_IMPL * 0.5 + 2.0 * FOURTH_IMPL
        return -scale * (self.radius[cell] + self.radius[cell + 1])

    def far(self, cell):
        return FOURTH_IMPL * self.radius[cell]

    def middle(self, cell, rate):
        centre, above = self.radius[cell], self.radius[cell + 1]
        if cell == 0:
            total, weighted = centre + (centre + above), 4.0 * centre + above
        else:
            below = self.radius[cell - 1]
            total = (below + centre) + (centre + above)
            weighted = below + 4.0 * centre + above
        result = SECOND_IMPL * (0.5 * total) + FOURTH_IMPL * weighted
        return result if rate is None else rate * centre + result

    def diagonal(self, cell, rates):
        across = self.near(cell)
        return (self.middle(cell, rates[0]), across, across, self.middle(cell + 1, rates[1]))

    def below(self, cell):
        return (self.far(cell - 1), self.near(cell - 1), None, self.far(cell))

    def above(self, cell):
        return (self.far(cell + 1), None, self.near(cell + 1), self.far(cell + 2))


def rates_at(ref, y, block, first_half):
    rows = [at_block(ref, y, block)[pl.ds(RATE_ROW + k, 1), :] for k in range(4)]
    return [jnp.where(first_half, rows[2 * k], rows[2 * k + 1]) for k in range(2)]


def half_kernel(
    all_ref, next_ref, codes_ref, partial_ref, factor_ref, blocks_ref, correction_ref,
    line_ref,
):
    own_y = lax.axis_index("inst") >> 1
    blocks = all_ref.shape[1]
    cells = 2 * blocks
    mirrored = lax.axis_index("cell") // blocks
    sign = (1 - 2 * mirrored).astype(jnp.float32)
    shape = (ROWS, LANES)
    lane_index = lax.broadcasted_iota(jnp.int32, shape, 1)
    first_var, first_inst, half_index = plane_masks()
    first_half = half_index == 0
    zero = jnp.zeros(shape, jnp.float32)

    next_rows = [
        next_ref[pl.ds(half * LANES, LANES)].reshape(1, LANES) for half in range(2)
    ]
    next_line = jnp.where(first_half, next_rows[0], next_rows[1])
    column = lax.broadcasted_iota(jnp.int32, (LANES, LANES), 0)
    prev_halves = []
    for target in range(2):
        total = None
        for source in range(2):
            hits = jnp.where(column + target * LANES == next_rows[source], 1.0, 0.0)
            names = (lane_index + source * LANES).astype(jnp.float32)
            part = lax.dot_general(
                names, hits, (((1,), (1,)), ((), ())), preferred_element_type=jnp.float32
            )
            total = part if total is None else total + part
        prev_halves.append(total)
    prev_line = jnp.where(first_half, prev_halves[0], prev_halves[1]).astype(jnp.int32)

    def picker(lines):
        lane = lines & (LANES - 1)
        same = (lines >> 7) == half_index

        def pick(plane):
            swapped = jnp.where(first_half, pltpu.roll(plane, 7, 0), pltpu.roll(plane, 1, 0))
            here = jnp.take_along_axis(plane, lane, axis=1, mode="promise_in_bounds")
            there = jnp.take_along_axis(swapped, lane, axis=1, mode="promise_in_bounds")
            return jnp.where(same, here, there)

        return pick

    pick_next = picker(next_line)
    pick_prev = picker(prev_line)

    def loaded(cell, y=own_y):
        return [cell_plane(all_ref, y, cell, k) for k in range(PAIRS)]

    own_weights, away_weights = time_weights(first_inst, 0), time_weights(first_inst, 2)

    def own_time_parts(planes, cell):
        return [
            away_weights[0] * away
            + turn_insts(first_inst, own_weights[1] * own + away_weights[1] * away)
            for own, away in zip(planes, loaded(cell, 1 - own_y))
        ]

    def flux_across(planes, velocity, pressure):
        return [
            planes[0] * velocity,
            planes[1] * velocity + jnp.where(first_var, pressure, 0.0),
            planes[2] * velocity + jnp.where(first_var, pressure * velocity, 0.0),
        ]

    def pitch_flux(planes, velocity_y, pressure, sound):
        nearby = [pick_next(plane) for plane in planes]
        _, next_velocity, next_pressure, next_sound = primitives(first_var, nearby)
        own_flux = flux_across(planes, velocity_y, pressure)
        next_flux = flux_across(nearby, next_velocity, next_pressure)
        weight = (PITCH_GAIN * 0.5) * (
            jnp.abs(velocity_y) + sound + (jnp.abs(next_velocity) + next_sound)
        )
        return [
            0.5 * (a + b) - weight * (n - o)
            for a, b, n, o in zip(own_flux, next_flux, nearby, planes)
        ]

    for cell in range(cells):
        planes = loaded(cell)
        velocity_x, velocity_y, pressure, sound = primitives(first_var, planes)
        line_ref[cell, 0], line_ref[cell, 1], line_ref[cell, 2] = velocity_x, pressure, sound
        faces_across = pitch_flux(planes, velocity_y, pressure, sound)
        times = own_time_parts(planes, cell)
        for k in range(PAIRS):
            partial_ref[cell, k] = -(times[k] + (faces_across[k] - pick_prev(faces_across[k])))

    tile = half_index * (LANES // LINES_DEV) + lane_index // LINES_DEV
    end_codes = jnp.where(mirrored == 0, codes_ref[pl.ds(0, 1), :], codes_ref[pl.ds(1, 1), :])
    codes = jnp.zeros(shape, jnp.int32)
    for k in range(2 * LANES // LINES_DEV):
        codes = jnp.where(tile == k, jnp.broadcast_to(end_codes[:, k : k + 1], shape), codes)

    def ghost(cell):
        planes = loaded(-1 - cell)
        copied = loaded(0)
        result = []
        for k in range(PAIRS):
            reflected = planes[k] if k else jnp.where(first_var, planes[k], -planes[k])
            inflow = jnp.where(first_var, FREE_STATE[2 * k], FREE_STATE[2 * k + 1])
            result.append(
                jnp.where(codes == 0, reflected, jnp.where(codes == 1, inflow, copied[k]))
            )
        return result

    line = LineCells(first_var, sign)
    faces, inverses, aboves = {}, [], []
    for cell in range(-2, cells):
        if cell < 0:
            planes = ghost(cell)
            velocity_x, _, pressure, sound = primitives(first_var, planes)
        else:
            planes = loaded(cell)
            velocity_x, pressure, sound = [line_ref[cell, k] for k in range(3)]
        line.add(cell, planes, velocity_x, pressure, sound)
        if cell >= 1:
            faces[cell - 2] = line.face(cell - 2)
        if cell >= 2:
            at = cell - 2
            for k in range(PAIRS):
                partial_ref[at, k] = partial_ref[at, k] + (faces[at - 1][k] - faces[at][k])
        if cell >= 3 and cell % 2 == 1:
            at = cell - 3
            block = at // 2
            rates = rates_at(all_ref, own_y, block, first_half)
            diag = line.diagonal(at, rates)
            if block > 0:
                factor = two_by_two(line.below(at), inverses[-1])
                diag = less(diag, two_by_two(factor, aboves[-1]))
                for n in range(4):
                    factor_ref[block - 1, n] = factor[n]
            inverses.append(inverse_of(diag))
            aboves.append(line.above(at))
            kept = [*inverses[-1], aboves[-1][0], *aboves[-1][2:]]
            for n, plane in enumerate(kept):
                blocks_ref[block, n] = plane

    last = cells - 2
    for k in range(PAIRS):
        partial_ref[last, k] = partial_ref[last, k] + faces[last - 1][k]
    factor = two_by_two(line.below(last), inverses[-1])
    for n in range(4):
        factor_ref[blocks - 2, n] = factor[n]
    correction = list(two_by_two(factor, aboves[-1]))
    rates = rates_at(all_ref, own_y, blocks - 1, first_half)
    for member in range(2):
        centre = line.radius[last + member]
        correction[3 * member] = correction[3 * member] - rates[member] * centre
    for n in range(2):
        correction_ref[pl.ds(n * ROWS, ROWS), :] = jnp.where(
            first_var, correction[2 * n], correction[2 * n + 1]
        )


def reduce_kernel(partial_ref, time_ref, factor_ref, correction_ref, middle_ref, sides_ref):
    for row in range(0, 2 * ROWS, ROWS):
        middle_ref[pl.ds(CORRECTION_ROW + row, ROWS), :] = correction_ref[pl.ds(row, ROWS), :]
    blocks = partial_ref.shape[0] // 2
    side = None
    for block in range(blocks):
        own = []
        for cell in (2 * block, 2 * block + 1):
            for k in range(PAIRS):
                time = time_ref[pl.ds(cell * CELL_ROWS + k * ROWS, ROWS), :]
                own.append(partial_ref[cell, k] - time)
        if block > 0:
            factor = [factor_ref[block - 1, n] for n in range(4)]
            own = difference(own, apply_matrix(factor, side))
        side = own
        for n, plane in enumerate(side):
            if block < blocks - 1:
                sides_ref[block, n] = plane
            else:
                middle_ref[pl.ds(n * ROWS, ROWS), :] = plane


def spread_kernel(all_ref, blocks_ref, sides_ref, known_ref, spread_ref, table_ref):
    own_y = lax.axis_index("inst") >> 1
    blocks = all_ref.shape[1]
    own_cell = lax.axis_index("cell")
    own_block = jnp.where(own_cell < blocks, own_cell, 2 * blocks - 1 - own_cell)
    zero = jnp.zeros((ROWS, LANES), jnp.float32)
    known, spread = [zero] * (2 * PAIRS), (zero + 1.0, zero, zero, zero + 1.0)
    for block in range(blocks - 1, -1, -1):
        if block < blocks - 1:
            kept = [blocks_ref[block, n] for n in range(7)]
            inverse, above = kept[:4], (kept[4], None, kept[5], kept[6])
            side = [sides_ref[block, n] for n in range(2 * PAIRS)]
            step = two_by_two(inverse, above)
            own = apply_matrix(inverse, side)
            if block < blocks - 2:
                known = difference(own, apply_matrix(step, known))
                spread = minus(two_by_two(step, spread))
            else:
                known, spread = own, minus(step)
        for n, plane in enumerate(known + list(spread)):
            table_ref[block, n] = plane
    for n in range(2 * PAIRS):
        base = at_block(all_ref, own_y, own_block)[pl.ds(n * ROWS, ROWS), :]
        known_ref[n] = base + table_ref[own_block, n]
    for n in range(4):
        spread_ref[n] = table_ref[own_block, 2 * PAIRS + n]


def plane_of(ref, row):
    return ref[pl.ds(row, ROWS), :]


def correction_of(first_var, ref):
    pairs = [both(first_var, plane_of(ref, CORRECTION_ROW + n * ROWS)) for n in range(2)]
    return [pairs[0][0], pairs[0][1], pairs[1][0], pairs[1][1]]


def middle_kernel(here_ref, there_ref, here_side_ref, side_ref, other_ref, matrix_ref):
    mirrored = lax.axis_index("cell") // (lax.axis_size("cell") // 2)
    sign = (1 - 2 * mirrored).astype(jnp.float32)
    first_var, _, _ = plane_masks()
    line = LineCells(first_var, sign)
    for cell in range(6):
        ref, at = (here_ref, cell) if cell < 3 else (there_ref, 5 - cell)
        planes = [plane_of(ref, at * CELL_ROWS + k * ROWS) for k in range(PAIRS)]
        velocity_x, _, pressure, sound = primitives(first_var, planes)
        line.add(cell, planes, velocity_x, pressure, sound)
    faces = {cell: line.face(cell) for cell in (1, 2, 3)}
    for k in range(PAIRS):
        side_ref[k] = plane_of(here_side_ref, k * ROWS) - faces[1][k]
        side_ref[PAIRS + k] = plane_of(here_side_ref, (PAIRS + k) * ROWS) + (
            faces[1][k] - faces[2][k]
        )
        other_ref[k] = faces[2][k] - faces[3][k]
        other_ref[PAIRS + k] = faces[3][k]
    no_rates = (None, None)
    diag = difference(line.diagonal(1, no_rates), correction_of(first_var, here_side_ref))
    above, below = line.above(1), line.below(3)
    kept = [*diag, *line.diagonal(3, no_rates), above[0], *above[2:], *below[:2], below[3]]
    for n, plane in enumerate(kept):
        matrix_ref[n] = plane


def join_kernel(
    side_ref, other_ref, matrix_ref, there_side_ref, known_ref, spread_ref, out_ref
):
    mirrored = lax.axis_index("cell") // (lax.axis_size("cell") // 2)
    first_var, _, _ = plane_masks()
    kept = [matrix_ref[n] for n in range(14)]
    diag, other_diag = kept[:4], kept[4:8]
    above, below = (kept[8], None, kept[9], kept[10]), (kept[11], kept[12], None, kept[13])
    other_diag = difference(other_diag, correction_of(first_var, there_side_ref)[::-1])
    other = []
    for member in range(2):
        for k in range(PAIRS):
            there = plane_of(there_side_ref, ((1 - member) * PAIRS + k) * ROWS)
            other.append(there + other_ref[member * PAIRS + k])
    factor = two_by_two(above, inverse_of(other_diag))
    diag = less(diag, two_by_two(factor, below))
    side = [side_ref[n] for n in range(2 * PAIRS)]
    middle = apply_matrix(inverse_of(diag), difference(side, apply_matrix(factor, other)))
    moved = apply_matrix([spread_ref[n] for n in range(4)], middle)
    results = [known_ref[n] + moved[n] for n in range(2 * PAIRS)]
    for cell in range(2):
        for k in range(PAIRS):
            first, second = results[cell * PAIRS + k], results[(1 - cell) * PAIRS + k]
            result = jnp.where(mirrored == 0, first, second)
            for var in range(2):
                for inst in range(2):
                    for half in range(2):
                        row = rows_of(var, inst, half)
                        out_ref[
                            inst, 2 * k + var, pl.ds(cell, 1), pl.ds(half * LANES, LANES)
                        ] = result[row : row + 1]


def share_half(copies):
    insts, count = lax.axis_size("inst"), lax.axis_size("cell")
    halves = [range(count // 2 - 1, -1, -1), range(count // 2, count)]
    groups = [
        [inst * count + cell for inst in range(insts - 2 + core, -1, -2) for cell in half]
        for core in range(2)
        for half in halves
    ]
    return lax.all_to_all(
        copies, ("inst", "cell"), split_axis=0, concat_axis=0, tiled=True,
        axis_index_groups=groups,
    )


def swap_cores(block):
    pairs = [(inst, inst ^ 1) for inst in range(lax.axis_size("inst"))]
    return lax.ppermute(block, "inst", pairs)


def swap_halves(block):
    count = lax.axis_size("cell")
    return lax.ppermute(block, "cell", [(i, (i + count // 2) % count) for i in range(count)])


def float_shape(*sizes):
    return jax.ShapeDtypeStruct(sizes, jnp.float32)


def local_by_halves(state, pseudo_rate, line_next, face_codes):
    blocks = lax.axis_size("cell") // 2
    cells = 2 * blocks
    vmem = pl.BlockSpec(memory_space=pltpu.VMEM)
    plane = (ROWS, LANES)
    params = pltpu.CompilerParams(vmem_limit_bytes=VMEM_BYTES)
    places = lax.axis_size("inst") // 2
    held = [
        pltpu.with_memory_space_constraint(array, pltpu.HBM)
        for array in (state, pseudo_rate, line_next, face_codes)
    ]
    packed, next_here, codes_here = pl.pallas_call(
        pack_kernel,
        out_shape=(
            float_shape(places * blocks, BLOCK_ROWS, LANES),
            jax.ShapeDtypeStruct(line_next.shape, jnp.int32),
            jax.ShapeDtypeStruct(face_codes.shape, jnp.int32),
        ),
        in_specs=[pl.BlockSpec(memory_space=pltpu.HBM)] * 4,
        out_specs=(vmem, vmem, vmem),
        scratch_shapes=[
            pltpu.VMEM(state.shape, jnp.float32),
            pltpu.VMEM(pseudo_rate.shape, jnp.float32),
            pltpu.SemaphoreType.DMA((4,)),
        ],
        compiler_params=params,
    )(*held)
    shared = share_half(packed).reshape(places, blocks, BLOCK_ROWS, LANES)
    for_partner, here = pl.pallas_call(
        partner_kernel,
        out_shape=(
            float_shape(cells * CELL_ROWS, LANES),
            float_shape(MIDDLE_CELLS * CELL_ROWS, LANES),
        ),
        in_specs=[vmem],
        out_specs=(vmem, vmem),
        compiler_params=params,
    )(shared)
    from_partner = swap_cores(for_partner)
    there = swap_halves(here)
    beside = pl.CostEstimate(flops=10**6, bytes_accessed=10**6, transcendentals=0)
    partial, factors, eliminated, correction = pl.pallas_call(
        half_kernel,
        out_shape=(
            float_shape(cells, PAIRS, *plane),
            float_shape(blocks - 1, 4, *plane),
            float_shape(blocks - 1, 7, *plane),
            float_shape(2 * ROWS, LANES),
        ),
        in_specs=[vmem] * 3,
        out_specs=(vmem,) * 4,
        scratch_shapes=[pltpu.VMEM((cells, 3) + plane, jnp.float32)],
        compiler_params=params,
        cost_estimate=beside,
    )(shared, next_here, codes_here)
    here_side, sides = pl.pallas_call(
        reduce_kernel,
        out_shape=(
            float_shape(SIDE_ROWS, LANES),
            float_shape(blocks - 1, 2 * PAIRS, *plane),
        ),
        in_specs=[vmem] * 4,
        out_specs=(vmem, vmem),
        compiler_params=params,
    )(partial, from_partner, factors, correction)
    there_side = swap_halves(here_side)
    known, spread = pl.pallas_call(
        spread_kernel,
        out_shape=(float_shape(2 * PAIRS, *plane), float_shape(4, *plane)),
        in_specs=[vmem] * 3,
        out_specs=(vmem, vmem),
        scratch_shapes=[pltpu.VMEM((blocks, 2 * PAIRS + 4) + plane, jnp.float32)],
        compiler_params=params,
        cost_estimate=beside,
    )(shared, eliminated, sides)
    side, other, matrices = pl.pallas_call(
        middle_kernel,
        out_shape=(
            float_shape(2 * PAIRS, *plane),
            float_shape(2 * PAIRS, *plane),
            float_shape(14, *plane),
        ),
        in_specs=[vmem] * 3,
        out_specs=(vmem,) * 3,
        compiler_params=params,
        cost_estimate=beside,
    )(here, there, here_side)
    return pl.pallas_call(
        join_kernel,
        out_shape=float_shape(*state.shape),
        in_specs=[vmem] * 6,
        out_specs=vmem,
        compiler_params=params,
    )(side, other, matrices, there_side, known, spread)


def solution(mesh):
    placed = (P("inst", None, "cell", None), P("cell", None), P(), P())
    inst_count, cell_count = mesh.shape["inst"], mesh.shape["cell"]

    def local(state, pseudo_rate, line_next, face_codes):
        small = (
            state.shape == (2, 6, 2, 2 * LANES)
            and inst_count * 2 == NT
            and cell_count == 8
            and face_codes.shape[1] * LINES_DEV == state.shape[3]
        )
        chosen = local_by_halves if small else local_by_lines
        return chosen(state, pseudo_rate, line_next, face_codes)

    return jax.shard_map(
        local, mesh=mesh, in_specs=placed, out_specs=P("inst", None, "cell", None), check_vma=False
    )
```

```python
import functools

import jax
import jax.numpy as jnp
import numpy as np
from jax import lax
from jax.experimental import pallas as pl
from jax.experimental.pallas import tpu as pltpu
from jax.sharding import PartitionSpec as P

NT = 8
LINES_DEV = 32


GAMMA_GAS = 1.4
OMEGA_BLADE = 1.0
SENSOR_GAIN = 0.25
FOURTH_GAIN = 0.03125
PITCH_GAIN = 0.5
SECOND_IMPL = 1.0
FOURTH_IMPL = 0.25
FREE_STATE = (1.0, 0.5, 0.0, 0.0, 2.625, 0.2)
MIRROR_SIGNS = (1.0, -1.0, 1.0, 1.0, 1.0, 1.0)
ZERO_BLOCK = (0.0, 0.0, 0.0, 0.0)
UNIT_BLOCK = (1.0, 0.0, 0.0, 1.0)
ZERO_PAIR = (0.0, 0.0)


def extended(block, sides, width):
    for axis, dim in sides:
        count = lax.axis_size(axis)
        forward = [(i, i + 1) for i in range(count - 1)]
        backward = [(target, source) for source, target in forward]
        low = lax.ppermute(
            lax.slice_in_dim(block, block.shape[dim] - width, None, axis=dim), axis, forward
        )
        high = lax.ppermute(lax.slice_in_dim(block, 0, width, axis=dim), axis, backward)
        block = jnp.concatenate([low, block, high], axis=dim)
    return block


def spectral_matrix(instances):
    offsets = np.arange(instances)[:, None] - np.arange(instances)[None, :]
    angles = np.pi * offsets / instances
    safe_sin = np.where(offsets == 0, 1.0, np.sin(angles))
    parity = np.where(np.mod(offsets, 2) == 0, -1.0, 1.0)
    matrix_table = np.where(
        offsets == 0, 0.0, 0.5 * OMEGA_BLADE * parity * np.cos(angles) / safe_sin
    )
    return jnp.asarray(matrix_table, jnp.float32)


def primitive_parts(cells_state):
    density = cells_state[..., 0, :, :]
    inverse = 1.0 / density
    velocity_x = cells_state[..., 1, :, :] * inverse
    velocity_y = cells_state[..., 2, :, :] * inverse
    velocity_z = cells_state[..., 3, :, :] * inverse
    energy = cells_state[..., 4, :, :]
    pressure = (GAMMA_GAS - 1.0) * (
        energy
        - 0.5
        * density
        * (velocity_x * velocity_x + velocity_y * velocity_y + velocity_z * velocity_z)
    )
    sound_speed = jnp.sqrt(GAMMA_GAS * pressure * inverse)
    return (velocity_x, velocity_y, pressure, sound_speed)


def directed_flux(cells_state, normal_velocity, pressure, component):
    zero_plane = jnp.zeros_like(pressure)
    pressure_rows = [
        zero_plane,
        zero_plane,
        zero_plane,
        zero_plane,
        pressure * normal_velocity,
        zero_plane,
    ]
    pressure_rows[component] = pressure
    return cells_state * normal_velocity[..., None, :, :] + jnp.stack(pressure_rows, axis=-3)


def line_residual(padded):
    velocity_x, velocity_y, pressure, sound_speed = primitive_parts(padded)
    flux_line = directed_flux(padded, velocity_x, pressure, 1)
    radius = jnp.abs(velocity_x) + sound_speed
    sensor = jnp.abs(
        pressure[..., 2:, :] - 2.0 * pressure[..., 1:-1, :] + pressure[..., :-2, :]
    ) / (pressure[..., 2:, :] + 2.0 * pressure[..., 1:-1, :] + pressure[..., :-2, :])
    second = SENSOR_GAIN * jnp.maximum(sensor[..., :-1, :], sensor[..., 1:, :])
    fourth = jnp.maximum(0.0, FOURTH_GAIN - second)
    face_radius = 0.5 * (radius[..., 1:-2, :] + radius[..., 2:-1, :])
    left_far = padded[..., :-3, :]
    left_near = padded[..., 1:-2, :]
    right_near = padded[..., 2:-1, :]
    right_far = padded[..., 3:, :]
    damping = face_radius[..., None, :, :] * (
        second[..., None, :, :] * (right_near - left_near)
        - fourth[..., None, :, :] * (right_far - 3.0 * right_near + 3.0 * left_near - left_far)
    )
    face_flux = 0.5 * (flux_line[..., 1:-2, :] + flux_line[..., 2:-1, :]) - damping
    return (face_flux[..., 1:, :] - face_flux[..., :-1, :], radius)


def pitch_parts(cells_state):
    velocity_x, velocity_y, pressure, sound_speed = primitive_parts(cells_state)
    return (directed_flux(cells_state, velocity_y, pressure, 2), jnp.abs(velocity_y) + sound_speed)


def pitch_residual(cells_state, next_lines, prev_lines):
    pitch_flux, radius = pitch_parts(cells_state)
    state_next = jnp.take(cells_state, next_lines, axis=-1)
    flux_next, radius_next = pitch_parts(state_next)
    face_flux = 0.5 * (pitch_flux + flux_next) - PITCH_GAIN * (0.5 * (radius + radius_next))[
        ..., None, :, :
    ] * (state_next - cells_state)
    return face_flux - jnp.take(face_flux, prev_lines, axis=-1)


def boundary_cells(edge_pair, line_codes, lower_end):
    reflected = edge_pair[..., ::-1, :] * jnp.asarray(MIRROR_SIGNS, jnp.float32)[:, None, None]
    if lower_end:
        copied = jnp.concatenate([edge_pair[..., :1, :], edge_pair[..., :1, :]], axis=-2)
    else:
        copied = jnp.concatenate([edge_pair[..., 1:, :], edge_pair[..., 1:, :]], axis=-2)
    inflow = jnp.asarray(FREE_STATE, jnp.float32)[:, None, None] + jnp.zeros_like(edge_pair)
    return jnp.where(line_codes == 0, reflected, jnp.where(line_codes == 1, inflow, copied))


def line_coefficients(radius_ext, diagonal_term, positions, total_cells):
    radius_below = radius_ext[..., :-2, :]
    radius_centre = radius_ext[..., 1:-1, :]
    radius_above = radius_ext[..., 2:, :]
    face_below = 0.5 * (radius_below + radius_centre)
    face_above = 0.5 * (radius_centre + radius_above)
    far_low = FOURTH_IMPL * radius_below
    near_low = -SECOND_IMPL * face_below - 2.0 * FOURTH_IMPL * (radius_below + radius_centre)
    middle = (
        diagonal_term
        + SECOND_IMPL * (face_below + face_above)
        + FOURTH_IMPL * (radius_below + 4.0 * radius_centre + radius_above)
    )
    near_high = -SECOND_IMPL * face_above - 2.0 * FOURTH_IMPL * (radius_centre + radius_above)
    far_high = FOURTH_IMPL * radius_above
    column = positions[:, None]
    far_low = jnp.where(column >= 2, far_low, 0.0)
    near_low = jnp.where(column >= 1, near_low, 0.0)
    near_high = jnp.where(column <= total_cells - 2, near_high, 0.0)
    far_high = jnp.where(column <= total_cells - 3, far_high, 0.0)
    return (far_low, near_low, middle, near_high, far_high)


def block_product(first_matrix, second_matrix):
    return (
        first_matrix[0] * second_matrix[0] + first_matrix[1] * second_matrix[2],
        first_matrix[0] * second_matrix[1] + first_matrix[1] * second_matrix[3],
        first_matrix[2] * second_matrix[0] + first_matrix[3] * second_matrix[2],
        first_matrix[2] * second_matrix[1] + first_matrix[3] * second_matrix[3],
    )


def block_inverse(matrix):
    determinant = matrix[0] * matrix[3] - matrix[1] * matrix[2]
    reciprocal = 1.0 / determinant
    return (
        matrix[3] * reciprocal,
        -matrix[1] * reciprocal,
        -matrix[2] * reciprocal,
        matrix[0] * reciprocal,
    )


def block_apply(matrix, vector):
    return (
        matrix[0] * vector[0] + matrix[1] * vector[1],
        matrix[2] * vector[0] + matrix[3] * vector[1],
    )


def add_blocks(first_members, second_members):
    return tuple((a + b for a, b in zip(first_members, second_members)))


def negate(members):
    return tuple((-a for a in members))


def extend_blocks(members, fill_values):
    return tuple(
        (
            jnp.concatenate([m, jnp.full_like(m[..., :1, :], f)], axis=-2)
            for m, f in zip(members, fill_values)
        )
    )


def shift_next(members, fill_values):
    return tuple(
        (
            jnp.concatenate([m[..., 1:, :], jnp.full_like(m[..., :1, :], f)], axis=-2)
            for m, f in zip(members, fill_values)
        )
    )


def shift_prev(members):
    return tuple(
        (jnp.concatenate([jnp.zeros_like(m[..., :1, :]), m[..., :-1, :]], axis=-2) for m in members)
    )


def pair_split(member):
    shaped = member.reshape(member.shape[:-2] + (member.shape[-2] // 2, 2, member.shape[-1]))
    return (shaped[..., 0, :], shaped[..., 1, :])


def split_parity(members):
    halves = [pair_split(m) for m in members]
    return (tuple((h[0] for h in halves)), tuple((h[1] for h in halves)))


def alternate(first_member, second_member):
    stacked = jnp.stack((first_member, second_member), axis=-2)
    return stacked.reshape(
        first_member.shape[:-2] + (2 * first_member.shape[-2], first_member.shape[-1])
    )


def reduce_blocks(sub_blocks, diag_blocks, super_blocks, right_side):
    block_count = diag_blocks[0].shape[-2]
    if block_count == 1:
        return block_apply(block_inverse(diag_blocks), right_side)
    if block_count % 2 == 1:
        sub_blocks = extend_blocks(sub_blocks, ZERO_BLOCK)
        diag_blocks = extend_blocks(diag_blocks, UNIT_BLOCK)
        super_blocks = extend_blocks(super_blocks, ZERO_BLOCK)
        right_side = extend_blocks(right_side, ZERO_PAIR)
    sub_even, sub_odd = split_parity(sub_blocks)
    diag_even, diag_odd = split_parity(diag_blocks)
    super_even, super_odd = split_parity(super_blocks)
    side_even, side_odd = split_parity(right_side)
    inverse_even = block_inverse(diag_even)
    inverse_next = shift_next(inverse_even, UNIT_BLOCK)
    sub_next = shift_next(sub_even, ZERO_BLOCK)
    super_next = shift_next(super_even, ZERO_BLOCK)
    side_next = shift_next(side_even, ZERO_PAIR)
    left_factor = negate(block_product(sub_odd, inverse_even))
    right_factor = negate(block_product(super_odd, inverse_next))
    reduced_sub = block_product(left_factor, sub_even)
    reduced_diag = add_blocks(
        diag_odd,
        add_blocks(block_product(left_factor, super_even), block_product(right_factor, sub_next)),
    )
    reduced_super = block_product(right_factor, super_next)
    reduced_side = add_blocks(
        side_odd,
        add_blocks(block_apply(left_factor, side_even), block_apply(right_factor, side_next)),
    )
    odd_values = reduce_blocks(reduced_sub, reduced_diag, reduced_super, reduced_side)
    before_values = shift_prev(odd_values)
    remainder = add_blocks(
        side_even,
        negate(
            add_blocks(block_apply(sub_even, before_values), block_apply(super_even, odd_values))
        ),
    )
    even_values = block_apply(inverse_even, remainder)
    merged = tuple((alternate(e, o) for e, o in zip(even_values, odd_values)))
    return tuple((m[..., :block_count, :] for m in merged))


def cells_leading(block):
    moved = jnp.transpose(block, (2, 0, 1, 3))
    return moved.reshape(block.shape[2], block.shape[0] * block.shape[1] * block.shape[3])


def solve_in_lanes(coefficients, line_source):
    source_shape = line_source.shape
    lane_coef = [cells_leading(jnp.broadcast_to(c[:, None], source_shape)) for c in coefficients]
    pairs_list = [pair_split(m) for m in lane_coef]
    zero_plane = jnp.zeros_like(pairs_list[2][0])
    sub_blocks = (pairs_list[0][0], pairs_list[1][0], zero_plane, pairs_list[0][1])
    diag_blocks = (pairs_list[2][0], pairs_list[3][0], pairs_list[1][1], pairs_list[2][1])
    super_blocks = (pairs_list[4][0], zero_plane, pairs_list[3][1], pairs_list[4][1])
    values = reduce_blocks(
        sub_blocks, diag_blocks, super_blocks, pair_split(cells_leading(line_source))
    )
    flat = alternate(values[0], values[1])
    shaped = flat.reshape(source_shape[2], source_shape[0], source_shape[1], source_shape[3])
    return jnp.transpose(shaped, (1, 2, 0, 3))


def return_tiles(line_values):
    return lax.all_to_all(line_values, "cell", split_axis=2, concat_axis=3, tiled=True)


def local_by_lines(state, pseudo_rate, line_next, face_codes):
    local_count = state.shape[0]
    tile_cells = state.shape[2]
    cell_index = lax.axis_index("cell")
    cell_count = lax.axis_size("cell")
    total_cells = tile_cells * cell_count
    spectral = spectral_matrix(NT)
    first_local = lax.axis_index("inst") * local_count
    own_rows = lax.dynamic_slice_in_dim(spectral, first_local, local_count, 0)
    shard_block = jax.tree.map(lambda a: lax.all_gather(a, "inst", axis=0, tiled=True), state)
    columns = lax.slice_in_dim(own_rows, 0, shard_block.shape[0], axis=1)
    time_term = jnp.zeros_like(state) + jnp.einsum(
        "nm,mvil->nvil", columns, shard_block, precision=lax.Precision.HIGHEST
    )
    padded = extended(state, (("cell", 2),), 2)
    codes_lines = jnp.repeat(face_codes, LINES_DEV, axis=1)
    lower_ghost = boundary_cells(state[:, :, 0:2, :], codes_lines[0], True)
    upper_ghost = boundary_cells(state[:, :, -2:, :], codes_lines[1], False)
    lower_rim = jnp.where(cell_index == 0, lower_ghost, padded[:, :, :2, :])
    upper_rim = jnp.where(cell_index == cell_count - 1, upper_ghost, padded[:, :, -2:, :])
    padded = jnp.concatenate([lower_rim, padded[:, :, 2:-2, :], upper_rim], axis=2)
    line_part, radius = line_residual(padded)
    prev_lines = (
        jnp.zeros_like(line_next).at[line_next].set(jnp.arange(line_next.shape[0], dtype=jnp.int32))
    )
    residual = line_part + pitch_residual(state, line_next, prev_lines) + time_term
    right_side = -residual
    centre_radius = radius[:, 2:-2, :]
    diagonal_term = pseudo_rate * centre_radius
    positions = cell_index * tile_cells + jnp.arange(-1, tile_cells + 1, dtype=jnp.int32)
    inside = (positions >= 0) & (positions < total_cells)
    radius_ext = jnp.where(inside[:, None], radius[:, 1:-1, :], 0.0)
    coefficients = line_coefficients(radius_ext, diagonal_term, positions[1:-1], total_cells)
    stacked = jnp.stack(coefficients, axis=1)
    line_source = lax.all_to_all(right_side, "cell", split_axis=3, concat_axis=2, tiled=True)
    line_coef = lax.all_to_all(stacked, "cell", split_axis=3, concat_axis=2, tiled=True)
    update = return_tiles(solve_in_lanes(tuple((line_coef[:, k] for k in range(5))), line_source))
    return state + update


LANES = 128
ROWS = 8
PAIRS = 3
CELL_ROWS = PAIRS * ROWS
RATE_ROW = 2 * CELL_ROWS
VMEM_BYTES = 8 * 2**20
BLOCK_ROWS = RATE_ROW + ROWS

MIDDLE_CELLS = 3
CORRECTION_ROW = 2 * CELL_ROWS
SIDE_ROWS = CORRECTION_ROW + 2 * ROWS


def spectral_offsets():
    table = np.zeros(NT)
    for offset in range(1, NT):
        angle = np.pi * offset / NT
        parity = -1.0 if offset % 2 == 0 else 1.0
        table[offset] = 0.5 * OMEGA_BLADE * parity * np.cos(angle) / np.sin(angle)
    return [float(np.float32(value)) for value in table]


def plane_masks():
    row_index = lax.broadcasted_iota(jnp.int32, (ROWS, LANES), 0)
    return row_index < 4, (row_index & 2) == 0, row_index & 1


def both(first_var, plane):
    turned = pltpu.roll(plane, 4, 0)
    return jnp.where(first_var, plane, turned), jnp.where(first_var, turned, plane)


def primitives(first_var, planes):
    density, moment_x = both(first_var, planes[0])
    moment_y, moment_z = both(first_var, planes[1])
    energy = jnp.where(first_var, planes[2], pltpu.roll(planes[2], 4, 0))
    inverse = 1.0 / density
    velocity_x = moment_x * inverse
    velocity_y = moment_y * inverse
    velocity_z = moment_z * inverse
    kinetic = moment_x * velocity_x + moment_y * velocity_y + moment_z * velocity_z
    pressure = (GAMMA_GAS - 1.0) * (energy - 0.5 * kinetic)
    sound = jnp.sqrt(GAMMA_GAS * pressure * inverse)
    return velocity_x, velocity_y, pressure, sound


def rows_of(var, inst, half):
    return (var // 2) * ROWS + (var % 2) * 4 + inst * 2 + half


def pack_kernel(
    held_state_ref, held_rate_ref, held_next_ref, held_codes_ref, out_ref, next_ref, codes_ref,
    state_ref, rate_ref, sems,
):
    copies = [
        pltpu.make_async_copy(source, target, sems.at[k])
        for k, (source, target) in enumerate(
            (
                (held_state_ref, state_ref),
                (held_rate_ref, rate_ref),
                (held_next_ref, next_ref),
                (held_codes_ref, codes_ref),
            )
        )
    ]
    for copy in copies:
        copy.start()
    for copy in copies:
        copy.wait()
    mirrored = lax.axis_index("cell") // (lax.axis_size("cell") // 2)
    for cell in range(2):
        place = pl.multiple_of(jnp.bitwise_xor(cell, mirrored) * CELL_ROWS, ROWS)
        for k in range(PAIRS):
            rows = [
                state_ref[inst, 2 * k + var, pl.ds(cell, 1), pl.ds(half * LANES, LANES)]
                for var in range(2)
                for inst in range(2)
                for half in range(2)
            ]
            for row, values in enumerate(rows):
                out_ref[0, pl.ds(place + (k * ROWS + row), 1), :] = values
    rates = [
        rate_ref[pl.ds(cell, 1), pl.ds(half * LANES, LANES)]
        for cell in range(2)
        for half in range(2)
    ]
    for row in range(4):
        out_ref[0, pl.ds(RATE_ROW + row, 1), :] = jnp.where(
            mirrored == 0, rates[row], rates[row ^ 2]
        )
    out_ref[0, pl.ds(RATE_ROW + 4, 4), :] = jnp.zeros((4, LANES), jnp.float32)
    for row in range(0, BLOCK_ROWS, ROWS):
        values = out_ref[0, pl.ds(row, ROWS), :]
        for copy in range(1, out_ref.shape[0]):
            out_ref[copy, pl.ds(row, ROWS), :] = values


def turn_insts(first_inst, plane):
    return jnp.where(first_inst, pltpu.roll(plane, 6, 0), pltpu.roll(plane, 2, 0))


def time_weights(first_inst, shift):
    offsets = spectral_offsets()
    other = jnp.where(
        first_inst, offsets[(2 * shift + 1) % NT], offsets[(2 * shift - 1) % NT]
    )
    return offsets[(2 * shift) % NT], other


def at_block(ref, y, block):
    blocks = ref.shape[1]
    mirrored = lax.axis_index("cell") // blocks
    place = mirrored * block + (1 - mirrored) * (blocks - 1 - block)
    return ref.at[ref.shape[0] - 1 - y, place]


def cell_plane(ref, y, cell, k):
    return at_block(ref, y, cell // 2)[pl.ds((cell % 2) * CELL_ROWS + k * ROWS, ROWS), :]


def partner_kernel(all_ref, out_ref, middle_ref):
    own_inst = lax.axis_index("inst")
    own_y, core = own_inst >> 1, own_inst & 1
    _, first_inst, _ = plane_masks()
    one, three = time_weights(first_inst, 1), time_weights(first_inst, 3)
    near = [jnp.where(core == 0, a, b) for a, b in zip(one, three)]
    away = [jnp.where(core == 0, b, a) for a, b in zip(one, three)]
    cells = 2 * all_ref.shape[1]
    for cell in range(cells - MIDDLE_CELLS, cells):
        for k in range(PAIRS):
            row = (cell - (cells - MIDDLE_CELLS)) * CELL_ROWS + k * ROWS
            middle_ref[pl.ds(row, ROWS), :] = cell_plane(all_ref, own_y, cell, k)
    for cell in range(cells):
        for k in range(PAIRS):
            here = cell_plane(all_ref, own_y, cell, k)
            there = cell_plane(all_ref, 1 - own_y, cell, k)
            out_ref[pl.ds(cell * CELL_ROWS + k * ROWS, ROWS), :] = (
                near[0] * here
                + away[0] * there
                + turn_insts(first_inst, near[1] * here + away[1] * there)
            )


def two_by_two(first, second):
    def entry(a, b, c, d):
        terms = [x * y for x, y in ((a, b), (c, d)) if x is not None and y is not None]
        return None if not terms else terms[0] if len(terms) == 1 else terms[0] + terms[1]

    return (
        entry(first[0], second[0], first[1], second[2]),
        entry(first[0], second[1], first[1], second[3]),
        entry(first[2], second[0], first[3], second[2]),
        entry(first[2], second[1], first[3], second[3]),
    )


def inverse_of(matrix):
    reciprocal = 1.0 / (matrix[0] * matrix[3] - matrix[1] * matrix[2])
    return (
        matrix[3] * reciprocal,
        -(matrix[1] * reciprocal),
        -(matrix[2] * reciprocal),
        matrix[0] * reciprocal,
    )


def less(first, second):
    return tuple(a if b is None else a - b for a, b in zip(first, second))


def minus(members):
    return tuple(None if a is None else -a for a in members)


def matrix_vector(matrix, low, high):
    def row(a, b):
        terms = [x * y for x, y in ((a, low), (b, high)) if x is not None]
        return terms[0] if len(terms) == 1 else terms[0] + terms[1]

    return row(matrix[0], matrix[1]), row(matrix[2], matrix[3])


def apply_matrix(matrix, side):
    parts = [matrix_vector(matrix, side[k], side[PAIRS + k]) for k in range(PAIRS)]
    return [low for low, _ in parts] + [high for _, high in parts]


def difference(first, second):
    return [a - b for a, b in zip(first, second)]


def flux_along(first_var, planes, velocity, pressure, sign):
    normal = sign * velocity
    return [
        planes[0] * normal + jnp.where(first_var, 0.0, sign * pressure),
        planes[1] * normal,
        planes[2] * normal + jnp.where(first_var, pressure * normal, 0.0),
    ]


class LineCells:
    def __init__(self, first_var, sign):
        self.first_var, self.sign = first_var, sign
        self.state, self.pressure, self.radius = {}, {}, {}
        self.flux, self.step, self.sensor = {}, {}, {}

    def add(self, cell, planes, velocity, pressure, sound):
        self.state[cell], self.pressure[cell] = planes, pressure
        self.radius[cell] = jnp.abs(velocity) + sound
        self.flux[cell] = flux_along(self.first_var, planes, velocity, pressure, self.sign)
        if cell - 1 in self.state:
            self.step[cell - 1] = difference(planes, self.state[cell - 1])
        if cell - 2 in self.state:
            twice = 2.0 * self.pressure[cell - 1]
            outer = pressure + self.pressure[cell - 2]
            self.sensor[cell - 1] = jnp.abs(outer - twice) / (outer + twice)

    def face(self, cell):
        second = SENSOR_GAIN * jnp.maximum(self.sensor[cell], self.sensor[cell + 1])
        fourth = jnp.maximum(0.0, FOURTH_GAIN - second)
        face_radius = 0.5 * (self.radius[cell] + self.radius[cell + 1])
        near_weight = face_radius * (second + 2.0 * fourth)
        far_weight = face_radius * fourth
        return [
            0.5 * (self.flux[cell][k] + self.flux[cell + 1][k])
            - (
                near_weight * self.step[cell][k]
                - far_weight * (self.step[cell + 1][k] + self.step[cell - 1][k])
            )
            for k in range(PAIRS)
        ]

    def near(self, cell):
        scale = SECOND_IMPL * 0.5 + 2.0 * FOURTH_IMPL
        return -scale * (self.radius[cell] + self.radius[cell + 1])

    def far(self, cell):
        return FOURTH_IMPL * self.radius[cell]

    def middle(self, cell, rate):
        centre, above = self.radius[cell], self.radius[cell + 1]
        if cell == 0:
            total, weighted = centre + (centre + above), 4.0 * centre + above
        else:
            below = self.radius[cell - 1]
            total = (below + centre) + (centre + above)
            weighted = below + 4.0 * centre + above
        result = SECOND_IMPL * (0.5 * total) + FOURTH_IMPL * weighted
        return result if rate is None else rate * centre + result

    def diagonal(self, cell, rates):
        across = self.near(cell)
        return (self.middle(cell, rates[0]), across, across, self.middle(cell + 1, rates[1]))

    def below(self, cell):
        return (self.far(cell - 1), self.near(cell - 1), None, self.far(cell))

    def above(self, cell):
        return (self.far(cell + 1), None, self.near(cell + 1), self.far(cell + 2))


def rates_at(ref, y, block, first_half):
    rows = [at_block(ref, y, block)[pl.ds(RATE_ROW + k, 1), :] for k in range(4)]
    return [jnp.where(first_half, rows[2 * k], rows[2 * k + 1]) for k in range(2)]


def half_kernel(
    all_ref, next_ref, codes_ref, partial_ref, factor_ref, blocks_ref, correction_ref,
    line_ref,
):
    own_y = lax.axis_index("inst") >> 1
    blocks = all_ref.shape[1]
    cells = 2 * blocks
    mirrored = lax.axis_index("cell") // blocks
    sign = (1 - 2 * mirrored).astype(jnp.float32)
    shape = (ROWS, LANES)
    lane_index = lax.broadcasted_iota(jnp.int32, shape, 1)
    first_var, first_inst, half_index = plane_masks()
    first_half = half_index == 0
    zero = jnp.zeros(shape, jnp.float32)

    next_rows = [
        next_ref[pl.ds(half * LANES, LANES)].reshape(1, LANES) for half in range(2)
    ]
    next_line = jnp.where(first_half, next_rows[0], next_rows[1])
    column = lax.broadcasted_iota(jnp.int32, (LANES, LANES), 0)
    prev_halves = []
    for target in range(2):
        total = None
        for source in range(2):
            hits = jnp.where(column + target * LANES == next_rows[source], 1.0, 0.0)
            names = (lane_index + source * LANES).astype(jnp.float32)
            part = lax.dot_general(
                names, hits, (((1,), (1,)), ((), ())), preferred_element_type=jnp.float32
            )
            total = part if total is None else total + part
        prev_halves.append(total)
    prev_line = jnp.where(first_half, prev_halves[0], prev_halves[1]).astype(jnp.int32)

    def picker(lines):
        lane = lines & (LANES - 1)
        same = (lines >> 7) == half_index

        def pick(plane):
            swapped = jnp.where(first_half, pltpu.roll(plane, 7, 0), pltpu.roll(plane, 1, 0))
            here = jnp.take_along_axis(plane, lane, axis=1, mode="promise_in_bounds")
            there = jnp.take_along_axis(swapped, lane, axis=1, mode="promise_in_bounds")
            return jnp.where(same, here, there)

        return pick

    pick_next = picker(next_line)
    pick_prev = picker(prev_line)

    def loaded(cell, y=own_y):
        return [cell_plane(all_ref, y, cell, k) for k in range(PAIRS)]

    own_weights, away_weights = time_weights(first_inst, 0), time_weights(first_inst, 2)

    def own_time_parts(planes, cell):
        return [
            away_weights[0] * away
            + turn_insts(first_inst, own_weights[1] * own + away_weights[1] * away)
            for own, away in zip(planes, loaded(cell, 1 - own_y))
        ]

    def flux_across(planes, velocity, pressure):
        return [
            planes[0] * velocity,
            planes[1] * velocity + jnp.where(first_var, pressure, 0.0),
            planes[2] * velocity + jnp.where(first_var, pressure * velocity, 0.0),
        ]

    def pitch_flux(planes, velocity_y, pressure, sound):
        nearby = [pick_next(plane) for plane in planes]
        _, next_velocity, next_pressure, next_sound = primitives(first_var, nearby)
        own_flux = flux_across(planes, velocity_y, pressure)
        next_flux = flux_across(nearby, next_velocity, next_pressure)
        weight = (PITCH_GAIN * 0.5) * (
            jnp.abs(velocity_y) + sound + (jnp.abs(next_velocity) + next_sound)
        )
        return [
            0.5 * (a + b) - weight * (n - o)
            for a, b, n, o in zip(own_flux, next_flux, nearby, planes)
        ]

    for cell in range(cells):
        planes = loaded(cell)
        velocity_x, velocity_y, pressure, sound = primitives(first_var, planes)
        line_ref[cell, 0], line_ref[cell, 1], line_ref[cell, 2] = velocity_x, pressure, sound
        faces_across = pitch_flux(planes, velocity_y, pressure, sound)
        times = own_time_parts(planes, cell)
        for k in range(PAIRS):
            partial_ref[cell, k] = -(times[k] + (faces_across[k] - pick_prev(faces_across[k])))

    tile = half_index * (LANES // LINES_DEV) + lane_index // LINES_DEV
    end_codes = jnp.where(mirrored == 0, codes_ref[pl.ds(0, 1), :], codes_ref[pl.ds(1, 1), :])
    codes = jnp.zeros(shape, jnp.int32)
    for k in range(2 * LANES // LINES_DEV):
        codes = jnp.where(tile == k, jnp.broadcast_to(end_codes[:, k : k + 1], shape), codes)

    def ghost(cell):
        planes = loaded(-1 - cell)
        copied = loaded(0)
        result = []
        for k in range(PAIRS):
            reflected = planes[k] if k else jnp.where(first_var, planes[k], -planes[k])
            inflow = jnp.where(first_var, FREE_STATE[2 * k], FREE_STATE[2 * k + 1])
            result.append(
                jnp.where(codes == 0, reflected, jnp.where(codes == 1, inflow, copied[k]))
            )
        return result

    line = LineCells(first_var, sign)
    faces, inverses, aboves = {}, [], []
    for cell in range(-2, cells):
        if cell < 0:
            planes = ghost(cell)
            velocity_x, _, pressure, sound = primitives(first_var, planes)
        else:
            planes = loaded(cell)
            velocity_x, pressure, sound = [line_ref[cell, k] for k in range(3)]
        line.add(cell, planes, velocity_x, pressure, sound)
        if cell >= 1:
            faces[cell - 2] = line.face(cell - 2)
        if cell >= 2:
            at = cell - 2
            for k in range(PAIRS):
                partial_ref[at, k] = partial_ref[at, k] + (faces[at - 1][k] - faces[at][k])
        if cell >= 3 and cell % 2 == 1:
            at = cell - 3
            block = at // 2
            rates = rates_at(all_ref, own_y, block, first_half)
            diag = line.diagonal(at, rates)
            if block > 0:
                factor = two_by_two(line.below(at), inverses[-1])
                diag = less(diag, two_by_two(factor, aboves[-1]))
                for n in range(4):
                    factor_ref[block - 1, n] = factor[n]
            inverses.append(inverse_of(diag))
            aboves.append(line.above(at))
            kept = [*inverses[-1], aboves[-1][0], *aboves[-1][2:]]
            for n, plane in enumerate(kept):
                blocks_ref[block, n] = plane

    last = cells - 2
    for k in range(PAIRS):
        partial_ref[last, k] = partial_ref[last, k] + faces[last - 1][k]
    factor = two_by_two(line.below(last), inverses[-1])
    for n in range(4):
        factor_ref[blocks - 2, n] = factor[n]
    correction = list(two_by_two(factor, aboves[-1]))
    rates = rates_at(all_ref, own_y, blocks - 1, first_half)
    for member in range(2):
        centre = line.radius[last + member]
        correction[3 * member] = correction[3 * member] - rates[member] * centre
    for n in range(2):
        correction_ref[pl.ds(n * ROWS, ROWS), :] = jnp.where(
            first_var, correction[2 * n], correction[2 * n + 1]
        )


def reduce_kernel(partial_ref, time_ref, factor_ref, correction_ref, middle_ref, sides_ref):
    for row in range(0, 2 * ROWS, ROWS):
        middle_ref[pl.ds(CORRECTION_ROW + row, ROWS), :] = correction_ref[pl.ds(row, ROWS), :]
    blocks = partial_ref.shape[0] // 2
    side = None
    for block in range(blocks):
        own = []
        for cell in (2 * block, 2 * block + 1):
            for k in range(PAIRS):
                time = time_ref[pl.ds(cell * CELL_ROWS + k * ROWS, ROWS), :]
                own.append(partial_ref[cell, k] - time)
        if block > 0:
            factor = [factor_ref[block - 1, n] for n in range(4)]
            own = difference(own, apply_matrix(factor, side))
        side = own
        for n, plane in enumerate(side):
            if block < blocks - 1:
                sides_ref[block, n] = plane
            else:
                middle_ref[pl.ds(n * ROWS, ROWS), :] = plane


def spread_kernel(all_ref, blocks_ref, sides_ref, known_ref, spread_ref, table_ref):
    own_y = lax.axis_index("inst") >> 1
    blocks = all_ref.shape[1]
    own_cell = lax.axis_index("cell")
    own_block = jnp.where(own_cell < blocks, own_cell, 2 * blocks - 1 - own_cell)
    zero = jnp.zeros((ROWS, LANES), jnp.float32)
    known, spread = [zero] * (2 * PAIRS), (zero + 1.0, zero, zero, zero + 1.0)
    for block in range(blocks - 1, -1, -1):
        if block < blocks - 1:
            kept = [blocks_ref[block, n] for n in range(7)]
            inverse, above = kept[:4], (kept[4], None, kept[5], kept[6])
            side = [sides_ref[block, n] for n in range(2 * PAIRS)]
            step = two_by_two(inverse, above)
            own = apply_matrix(inverse, side)
            if block < blocks - 2:
                known = difference(own, apply_matrix(step, known))
                spread = minus(two_by_two(step, spread))
            else:
                known, spread = own, minus(step)
        for n, plane in enumerate(known + list(spread)):
            table_ref[block, n] = plane
    for n in range(2 * PAIRS):
        base = at_block(all_ref, own_y, own_block)[pl.ds(n * ROWS, ROWS), :]
        known_ref[n] = base + table_ref[own_block, n]
    for n in range(4):
        spread_ref[n] = table_ref[own_block, 2 * PAIRS + n]


def plane_of(ref, row):
    return ref[pl.ds(row, ROWS), :]


def correction_of(first_var, ref):
    pairs = [both(first_var, plane_of(ref, CORRECTION_ROW + n * ROWS)) for n in range(2)]
    return [pairs[0][0], pairs[0][1], pairs[1][0], pairs[1][1]]


def middle_kernel(here_ref, there_ref, here_side_ref, side_ref, other_ref, matrix_ref):
    mirrored = lax.axis_index("cell") // (lax.axis_size("cell") // 2)
    sign = (1 - 2 * mirrored).astype(jnp.float32)
    first_var, _, _ = plane_masks()
    line = LineCells(first_var, sign)
    for cell in range(6):
        ref, at = (here_ref, cell) if cell < 3 else (there_ref, 5 - cell)
        planes = [plane_of(ref, at * CELL_ROWS + k * ROWS) for k in range(PAIRS)]
        velocity_x, _, pressure, sound = primitives(first_var, planes)
        line.add(cell, planes, velocity_x, pressure, sound)
    faces = {cell: line.face(cell) for cell in (1, 2, 3)}
    for k in range(PAIRS):
        side_ref[k] = plane_of(here_side_ref, k * ROWS) - faces[1][k]
        side_ref[PAIRS + k] = plane_of(here_side_ref, (PAIRS + k) * ROWS) + (
            faces[1][k] - faces[2][k]
        )
        other_ref[k] = faces[2][k] - faces[3][k]
        other_ref[PAIRS + k] = faces[3][k]
    no_rates = (None, None)
    diag = difference(line.diagonal(1, no_rates), correction_of(first_var, here_side_ref))
    above, below = line.above(1), line.below(3)
    kept = [*diag, *line.diagonal(3, no_rates), above[0], *above[2:], *below[:2], below[3]]
    for n, plane in enumerate(kept):
        matrix_ref[n] = plane


def join_kernel(
    side_ref, other_ref, matrix_ref, there_side_ref, known_ref, spread_ref, out_ref
):
    mirrored = lax.axis_index("cell") // (lax.axis_size("cell") // 2)
    first_var, _, _ = plane_masks()
    kept = [matrix_ref[n] for n in range(14)]
    diag, other_diag = kept[:4], kept[4:8]
    above, below = (kept[8], None, kept[9], kept[10]), (kept[11], kept[12], None, kept[13])
    other_diag = difference(other_diag, correction_of(first_var, there_side_ref)[::-1])
    other = []
    for member in range(2):
        for k in range(PAIRS):
            there = plane_of(there_side_ref, ((1 - member) * PAIRS + k) * ROWS)
            other.append(there + other_ref[member * PAIRS + k])
    factor = two_by_two(above, inverse_of(other_diag))
    diag = less(diag, two_by_two(factor, below))
    side = [side_ref[n] for n in range(2 * PAIRS)]
    middle = apply_matrix(inverse_of(diag), difference(side, apply_matrix(factor, other)))
    moved = apply_matrix([spread_ref[n] for n in range(4)], middle)
    results = [known_ref[n] + moved[n] for n in range(2 * PAIRS)]
    for cell in range(2):
        for k in range(PAIRS):
            first, second = results[cell * PAIRS + k], results[(1 - cell) * PAIRS + k]
            result = jnp.where(mirrored == 0, first, second)
            for var in range(2):
                for inst in range(2):
                    for half in range(2):
                        row = rows_of(var, inst, half)
                        out_ref[
                            inst, 2 * k + var, pl.ds(cell, 1), pl.ds(half * LANES, LANES)
                        ] = result[row : row + 1]


def share_half(copies):
    insts, count = lax.axis_size("inst"), lax.axis_size("cell")
    halves = [range(count // 2 - 1, -1, -1), range(count - 1, count // 2 - 1, -1)]
    groups = [
        [inst * count + cell for inst in range(insts - 2 + core, -1, -2) for cell in half]
        for core in range(2)
        for half in halves
    ]
    return lax.all_to_all(
        copies, ("inst", "cell"), split_axis=0, concat_axis=0, tiled=True,
        axis_index_groups=groups,
    )


def swap_cores(block):
    pairs = [(inst, inst ^ 1) for inst in range(lax.axis_size("inst"))]
    return lax.ppermute(block, "inst", pairs)


def swap_halves(block):
    count = lax.axis_size("cell")
    return lax.ppermute(block, "cell", [(i, (i + count // 2) % count) for i in range(count)])


def float_shape(*sizes):
    return jax.ShapeDtypeStruct(sizes, jnp.float32)


def local_by_halves(state, pseudo_rate, line_next, face_codes):
    blocks = lax.axis_size("cell") // 2
    cells = 2 * blocks
    vmem = pl.BlockSpec(memory_space=pltpu.VMEM)
    plane = (ROWS, LANES)
    params = pltpu.CompilerParams(vmem_limit_bytes=VMEM_BYTES)
    places = lax.axis_size("inst") // 2
    held = [
        pltpu.with_memory_space_constraint(array, pltpu.HBM)
        for array in (state, pseudo_rate, line_next, face_codes)
    ]
    packed, next_here, codes_here = pl.pallas_call(
        pack_kernel,
        out_shape=(
            float_shape(places * blocks, BLOCK_ROWS, LANES),
            jax.ShapeDtypeStruct(line_next.shape, jnp.int32),
            jax.ShapeDtypeStruct(face_codes.shape, jnp.int32),
        ),
        in_specs=[pl.BlockSpec(memory_space=pltpu.HBM)] * 4,
        out_specs=(vmem, vmem, vmem),
        scratch_shapes=[
            pltpu.VMEM(state.shape, jnp.float32),
            pltpu.VMEM(pseudo_rate.shape, jnp.float32),
            pltpu.SemaphoreType.DMA((4,)),
        ],
        compiler_params=params,
    )(*held)
    shared = share_half(packed).reshape(places, blocks, BLOCK_ROWS, LANES)
    for_partner, here = pl.pallas_call(
        partner_kernel,
        out_shape=(
            float_shape(cells * CELL_ROWS, LANES),
            float_shape(MIDDLE_CELLS * CELL_ROWS, LANES),
        ),
        in_specs=[vmem],
        out_specs=(vmem, vmem),
        compiler_params=params,
    )(shared)
    from_partner = swap_cores(for_partner)
    there = swap_halves(here)
    beside = pl.CostEstimate(flops=10**6, bytes_accessed=10**6, transcendentals=0)
    partial, factors, eliminated, correction = pl.pallas_call(
        half_kernel,
        out_shape=(
            float_shape(cells, PAIRS, *plane),
            float_shape(blocks - 1, 4, *plane),
            float_shape(blocks - 1, 7, *plane),
            float_shape(2 * ROWS, LANES),
        ),
        in_specs=[vmem] * 3,
        out_specs=(vmem,) * 4,
        scratch_shapes=[pltpu.VMEM((cells, 3) + plane, jnp.float32)],
        compiler_params=params,
        cost_estimate=beside,
    )(shared, next_here, codes_here)
    here_side, sides = pl.pallas_call(
        reduce_kernel,
        out_shape=(
            float_shape(SIDE_ROWS, LANES),
            float_shape(blocks - 1, 2 * PAIRS, *plane),
        ),
        in_specs=[vmem] * 4,
        out_specs=(vmem, vmem),
        compiler_params=params,
    )(partial, from_partner, factors, correction)
    there_side = swap_halves(here_side)
    known, spread = pl.pallas_call(
        spread_kernel,
        out_shape=(float_shape(2 * PAIRS, *plane), float_shape(4, *plane)),
        in_specs=[vmem] * 3,
        out_specs=(vmem, vmem),
        scratch_shapes=[pltpu.VMEM((blocks, 2 * PAIRS + 4) + plane, jnp.float32)],
        compiler_params=params,
        cost_estimate=beside,
    )(shared, eliminated, sides)
    side, other, matrices = pl.pallas_call(
        middle_kernel,
        out_shape=(
            float_shape(2 * PAIRS, *plane),
            float_shape(2 * PAIRS, *plane),
            float_shape(14, *plane),
        ),
        in_specs=[vmem] * 3,
        out_specs=(vmem,) * 3,
        compiler_params=params,
        cost_estimate=beside,
    )(here, there, here_side)
    return pl.pallas_call(
        join_kernel,
        out_shape=float_shape(*state.shape),
        in_specs=[vmem] * 6,
        out_specs=vmem,
        compiler_params=params,
    )(side, other, matrices, there_side, known, spread)


def solution(mesh):
    placed = (P("inst", None, "cell", None), P("cell", None), P(), P())
    inst_count, cell_count = mesh.shape["inst"], mesh.shape["cell"]

    def local(state, pseudo_rate, line_next, face_codes):
        small = (
            state.shape == (2, 6, 2, 2 * LANES)
            and inst_count * 2 == NT
            and cell_count == 8
            and face_codes.shape[1] * LINES_DEV == state.shape[3]
        )
        chosen = local_by_halves if small else local_by_lines
        return chosen(state, pseudo_rate, line_next, face_codes)

    return jax.shard_map(
        local, mesh=mesh, in_specs=placed, out_specs=P("inst", None, "cell", None), check_vma=False
    )
```

```python
import functools

import jax
import jax.numpy as jnp
import numpy as np
from jax import lax
from jax.experimental import pallas as pl
from jax.experimental.pallas import tpu as pltpu
from jax.sharding import PartitionSpec as P

NT = 8
LINES_DEV = 32


GAMMA_GAS = 1.4
OMEGA_BLADE = 1.0
SENSOR_GAIN = 0.25
FOURTH_GAIN = 0.03125
PITCH_GAIN = 0.5
SECOND_IMPL = 1.0
FOURTH_IMPL = 0.25
FREE_STATE = (1.0, 0.5, 0.0, 0.0, 2.625, 0.2)
MIRROR_SIGNS = (1.0, -1.0, 1.0, 1.0, 1.0, 1.0)
ZERO_BLOCK = (0.0, 0.0, 0.0, 0.0)
UNIT_BLOCK = (1.0, 0.0, 0.0, 1.0)
ZERO_PAIR = (0.0, 0.0)


def extended(block, sides, width):
    for axis, dim in sides:
        count = lax.axis_size(axis)
        forward = [(i, i + 1) for i in range(count - 1)]
        backward = [(target, source) for source, target in forward]
        low = lax.ppermute(
            lax.slice_in_dim(block, block.shape[dim] - width, None, axis=dim), axis, forward
        )
        high = lax.ppermute(lax.slice_in_dim(block, 0, width, axis=dim), axis, backward)
        block = jnp.concatenate([low, block, high], axis=dim)
    return block


def spectral_matrix(instances):
    offsets = np.arange(instances)[:, None] - np.arange(instances)[None, :]
    angles = np.pi * offsets / instances
    safe_sin = np.where(offsets == 0, 1.0, np.sin(angles))
    parity = np.where(np.mod(offsets, 2) == 0, -1.0, 1.0)
    matrix_table = np.where(
        offsets == 0, 0.0, 0.5 * OMEGA_BLADE * parity * np.cos(angles) / safe_sin
    )
    return jnp.asarray(matrix_table, jnp.float32)


def primitive_parts(cells_state):
    density = cells_state[..., 0, :, :]
    inverse = 1.0 / density
    velocity_x = cells_state[..., 1, :, :] * inverse
    velocity_y = cells_state[..., 2, :, :] * inverse
    velocity_z = cells_state[..., 3, :, :] * inverse
    energy = cells_state[..., 4, :, :]
    pressure = (GAMMA_GAS - 1.0) * (
        energy
        - 0.5
        * density
        * (velocity_x * velocity_x + velocity_y * velocity_y + velocity_z * velocity_z)
    )
    sound_speed = jnp.sqrt(GAMMA_GAS * pressure * inverse)
    return (velocity_x, velocity_y, pressure, sound_speed)


def directed_flux(cells_state, normal_velocity, pressure, component):
    zero_plane = jnp.zeros_like(pressure)
    pressure_rows = [
        zero_plane,
        zero_plane,
        zero_plane,
        zero_plane,
        pressure * normal_velocity,
        zero_plane,
    ]
    pressure_rows[component] = pressure
    return cells_state * normal_velocity[..., None, :, :] + jnp.stack(pressure_rows, axis=-3)


def line_residual(padded):
    velocity_x, velocity_y, pressure, sound_speed = primitive_parts(padded)
    flux_line = directed_flux(padded, velocity_x, pressure, 1)
    radius = jnp.abs(velocity_x) + sound_speed
    sensor = jnp.abs(
        pressure[..., 2:, :] - 2.0 * pressure[..., 1:-1, :] + pressure[..., :-2, :]
    ) / (pressure[..., 2:, :] + 2.0 * pressure[..., 1:-1, :] + pressure[..., :-2, :])
    second = SENSOR_GAIN * jnp.maximum(sensor[..., :-1, :], sensor[..., 1:, :])
    fourth = jnp.maximum(0.0, FOURTH_GAIN - second)
    face_radius = 0.5 * (radius[..., 1:-2, :] + radius[..., 2:-1, :])
    left_far = padded[..., :-3, :]
    left_near = padded[..., 1:-2, :]
    right_near = padded[..., 2:-1, :]
    right_far = padded[..., 3:, :]
    damping = face_radius[..., None, :, :] * (
        second[..., None, :, :] * (right_near - left_near)
        - fourth[..., None, :, :] * (right_far - 3.0 * right_near + 3.0 * left_near - left_far)
    )
    face_flux = 0.5 * (flux_line[..., 1:-2, :] + flux_line[..., 2:-1, :]) - damping
    return (face_flux[..., 1:, :] - face_flux[..., :-1, :], radius)


def pitch_parts(cells_state):
    velocity_x, velocity_y, pressure, sound_speed = primitive_parts(cells_state)
    return (directed_flux(cells_state, velocity_y, pressure, 2), jnp.abs(velocity_y) + sound_speed)


def pitch_residual(cells_state, next_lines, prev_lines):
    pitch_flux, radius = pitch_parts(cells_state)
    state_next = jnp.take(cells_state, next_lines, axis=-1)
    flux_next, radius_next = pitch_parts(state_next)
    face_flux = 0.5 * (pitch_flux + flux_next) - PITCH_GAIN * (0.5 * (radius + radius_next))[
        ..., None, :, :
    ] * (state_next - cells_state)
    return face_flux - jnp.take(face_flux, prev_lines, axis=-1)


def boundary_cells(edge_pair, line_codes, lower_end):
    reflected = edge_pair[..., ::-1, :] * jnp.asarray(MIRROR_SIGNS, jnp.float32)[:, None, None]
    if lower_end:
        copied = jnp.concatenate([edge_pair[..., :1, :], edge_pair[..., :1, :]], axis=-2)
    else:
        copied = jnp.concatenate([edge_pair[..., 1:, :], edge_pair[..., 1:, :]], axis=-2)
    inflow = jnp.asarray(FREE_STATE, jnp.float32)[:, None, None] + jnp.zeros_like(edge_pair)
    return jnp.where(line_codes == 0, reflected, jnp.where(line_codes == 1, inflow, copied))


def line_coefficients(radius_ext, diagonal_term, positions, total_cells):
    radius_below = radius_ext[..., :-2, :]
    radius_centre = radius_ext[..., 1:-1, :]
    radius_above = radius_ext[..., 2:, :]
    face_below = 0.5 * (radius_below + radius_centre)
    face_above = 0.5 * (radius_centre + radius_above)
    far_low = FOURTH_IMPL * radius_below
    near_low = -SECOND_IMPL * face_below - 2.0 * FOURTH_IMPL * (radius_below + radius_centre)
    middle = (
        diagonal_term
        + SECOND_IMPL * (face_below + face_above)
        + FOURTH_IMPL * (radius_below + 4.0 * radius_centre + radius_above)
    )
    near_high = -SECOND_IMPL * face_above - 2.0 * FOURTH_IMPL * (radius_centre + radius_above)
    far_high = FOURTH_IMPL * radius_above
    column = positions[:, None]
    far_low = jnp.where(column >= 2, far_low, 0.0)
    near_low = jnp.where(column >= 1, near_low, 0.0)
    near_high = jnp.where(column <= total_cells - 2, near_high, 0.0)
    far_high = jnp.where(column <= total_cells - 3, far_high, 0.0)
    return (far_low, near_low, middle, near_high, far_high)


def block_product(first_matrix, second_matrix):
    return (
        first_matrix[0] * second_matrix[0] + first_matrix[1] * second_matrix[2],
        first_matrix[0] * second_matrix[1] + first_matrix[1] * second_matrix[3],
        first_matrix[2] * second_matrix[0] + first_matrix[3] * second_matrix[2],
        first_matrix[2] * second_matrix[1] + first_matrix[3] * second_matrix[3],
    )


def block_inverse(matrix):
    determinant = matrix[0] * matrix[3] - matrix[1] * matrix[2]
    reciprocal = 1.0 / determinant
    return (
        matrix[3] * reciprocal,
        -matrix[1] * reciprocal,
        -matrix[2] * reciprocal,
        matrix[0] * reciprocal,
    )


def block_apply(matrix, vector):
    return (
        matrix[0] * vector[0] + matrix[1] * vector[1],
        matrix[2] * vector[0] + matrix[3] * vector[1],
    )


def add_blocks(first_members, second_members):
    return tuple((a + b for a, b in zip(first_members, second_members)))


def negate(members):
    return tuple((-a for a in members))


def extend_blocks(members, fill_values):
    return tuple(
        (
            jnp.concatenate([m, jnp.full_like(m[..., :1, :], f)], axis=-2)
            for m, f in zip(members, fill_values)
        )
    )


def shift_next(members, fill_values):
    return tuple(
        (
            jnp.concatenate([m[..., 1:, :], jnp.full_like(m[..., :1, :], f)], axis=-2)
            for m, f in zip(members, fill_values)
        )
    )


def shift_prev(members):
    return tuple(
        (jnp.concatenate([jnp.zeros_like(m[..., :1, :]), m[..., :-1, :]], axis=-2) for m in members)
    )


def pair_split(member):
    shaped = member.reshape(member.shape[:-2] + (member.shape[-2] // 2, 2, member.shape[-1]))
    return (shaped[..., 0, :], shaped[..., 1, :])


def split_parity(members):
    halves = [pair_split(m) for m in members]
    return (tuple((h[0] for h in halves)), tuple((h[1] for h in halves)))


def alternate(first_member, second_member):
    stacked = jnp.stack((first_member, second_member), axis=-2)
    return stacked.reshape(
        first_member.shape[:-2] + (2 * first_member.shape[-2], first_member.shape[-1])
    )


def reduce_blocks(sub_blocks, diag_blocks, super_blocks, right_side):
    block_count = diag_blocks[0].shape[-2]
    if block_count == 1:
        return block_apply(block_inverse(diag_blocks), right_side)
    if block_count % 2 == 1:
        sub_blocks = extend_blocks(sub_blocks, ZERO_BLOCK)
        diag_blocks = extend_blocks(diag_blocks, UNIT_BLOCK)
        super_blocks = extend_blocks(super_blocks, ZERO_BLOCK)
        right_side = extend_blocks(right_side, ZERO_PAIR)
    sub_even, sub_odd = split_parity(sub_blocks)
    diag_even, diag_odd = split_parity(diag_blocks)
    super_even, super_odd = split_parity(super_blocks)
    side_even, side_odd = split_parity(right_side)
    inverse_even = block_inverse(diag_even)
    inverse_next = shift_next(inverse_even, UNIT_BLOCK)
    sub_next = shift_next(sub_even, ZERO_BLOCK)
    super_next = shift_next(super_even, ZERO_BLOCK)
    side_next = shift_next(side_even, ZERO_PAIR)
    left_factor = negate(block_product(sub_odd, inverse_even))
    right_factor = negate(block_product(super_odd, inverse_next))
    reduced_sub = block_product(left_factor, sub_even)
    reduced_diag = add_blocks(
        diag_odd,
        add_blocks(block_product(left_factor, super_even), block_product(right_factor, sub_next)),
    )
    reduced_super = block_product(right_factor, super_next)
    reduced_side = add_blocks(
        side_odd,
        add_blocks(block_apply(left_factor, side_even), block_apply(right_factor, side_next)),
    )
    odd_values = reduce_blocks(reduced_sub, reduced_diag, reduced_super, reduced_side)
    before_values = shift_prev(odd_values)
    remainder = add_blocks(
        side_even,
        negate(
            add_blocks(block_apply(sub_even, before_values), block_apply(super_even, odd_values))
        ),
    )
    even_values = block_apply(inverse_even, remainder)
    merged = tuple((alternate(e, o) for e, o in zip(even_values, odd_values)))
    return tuple((m[..., :block_count, :] for m in merged))


def cells_leading(block):
    moved = jnp.transpose(block, (2, 0, 1, 3))
    return moved.reshape(block.shape[2], block.shape[0] * block.shape[1] * block.shape[3])


def solve_in_lanes(coefficients, line_source):
    source_shape = line_source.shape
    lane_coef = [cells_leading(jnp.broadcast_to(c[:, None], source_shape)) for c in coefficients]
    pairs_list = [pair_split(m) for m in lane_coef]
    zero_plane = jnp.zeros_like(pairs_list[2][0])
    sub_blocks = (pairs_list[0][0], pairs_list[1][0], zero_plane, pairs_list[0][1])
    diag_blocks = (pairs_list[2][0], pairs_list[3][0], pairs_list[1][1], pairs_list[2][1])
    super_blocks = (pairs_list[4][0], zero_plane, pairs_list[3][1], pairs_list[4][1])
    values = reduce_blocks(
        sub_blocks, diag_blocks, super_blocks, pair_split(cells_leading(line_source))
    )
    flat = alternate(values[0], values[1])
    shaped = flat.reshape(source_shape[2], source_shape[0], source_shape[1], source_shape[3])
    return jnp.transpose(shaped, (1, 2, 0, 3))


def return_tiles(line_values):
    return lax.all_to_all(line_values, "cell", split_axis=2, concat_axis=3, tiled=True)


def local_by_lines(state, pseudo_rate, line_next, face_codes):
    local_count = state.shape[0]
    tile_cells = state.shape[2]
    cell_index = lax.axis_index("cell")
    cell_count = lax.axis_size("cell")
    total_cells = tile_cells * cell_count
    spectral = spectral_matrix(NT)
    first_local = lax.axis_index("inst") * local_count
    own_rows = lax.dynamic_slice_in_dim(spectral, first_local, local_count, 0)
    shard_block = jax.tree.map(lambda a: lax.all_gather(a, "inst", axis=0, tiled=True), state)
    columns = lax.slice_in_dim(own_rows, 0, shard_block.shape[0], axis=1)
    time_term = jnp.zeros_like(state) + jnp.einsum(
        "nm,mvil->nvil", columns, shard_block, precision=lax.Precision.HIGHEST
    )
    padded = extended(state, (("cell", 2),), 2)
    codes_lines = jnp.repeat(face_codes, LINES_DEV, axis=1)
    lower_ghost = boundary_cells(state[:, :, 0:2, :], codes_lines[0], True)
    upper_ghost = boundary_cells(state[:, :, -2:, :], codes_lines[1], False)
    lower_rim = jnp.where(cell_index == 0, lower_ghost, padded[:, :, :2, :])
    upper_rim = jnp.where(cell_index == cell_count - 1, upper_ghost, padded[:, :, -2:, :])
    padded = jnp.concatenate([lower_rim, padded[:, :, 2:-2, :], upper_rim], axis=2)
    line_part, radius = line_residual(padded)
    prev_lines = (
        jnp.zeros_like(line_next).at[line_next].set(jnp.arange(line_next.shape[0], dtype=jnp.int32))
    )
    residual = line_part + pitch_residual(state, line_next, prev_lines) + time_term
    right_side = -residual
    centre_radius = radius[:, 2:-2, :]
    diagonal_term = pseudo_rate * centre_radius
    positions = cell_index * tile_cells + jnp.arange(-1, tile_cells + 1, dtype=jnp.int32)
    inside = (positions >= 0) & (positions < total_cells)
    radius_ext = jnp.where(inside[:, None], radius[:, 1:-1, :], 0.0)
    coefficients = line_coefficients(radius_ext, diagonal_term, positions[1:-1], total_cells)
    stacked = jnp.stack(coefficients, axis=1)
    line_source = lax.all_to_all(right_side, "cell", split_axis=3, concat_axis=2, tiled=True)
    line_coef = lax.all_to_all(stacked, "cell", split_axis=3, concat_axis=2, tiled=True)
    update = return_tiles(solve_in_lanes(tuple((line_coef[:, k] for k in range(5))), line_source))
    return state + update


LANES = 128
ROWS = 8
PAIRS = 3
CELL_ROWS = PAIRS * ROWS
RATE_ROW = 2 * CELL_ROWS
VMEM_BYTES = 8 * 2**20
BLOCK_ROWS = RATE_ROW + ROWS

SIDE_ROW = 3 * CELL_ROWS
CORRECTION_ROW = SIDE_ROW + 2 * CELL_ROWS
MIDDLE_ROWS = CORRECTION_ROW + 2 * ROWS
FIXED_ROWS = 3 * CELL_ROWS + 2 * ROWS


def spectral_offsets():
    table = np.zeros(NT)
    for offset in range(1, NT):
        angle = np.pi * offset / NT
        parity = -1.0 if offset % 2 == 0 else 1.0
        table[offset] = 0.5 * OMEGA_BLADE * parity * np.cos(angle) / np.sin(angle)
    return [float(np.float32(value)) for value in table]


def plane_masks():
    row_index = lax.broadcasted_iota(jnp.int32, (ROWS, LANES), 0)
    return row_index < 4, (row_index & 2) == 0, row_index & 1


def both(first_var, plane):
    turned = pltpu.roll(plane, 4, 0)
    return jnp.where(first_var, plane, turned), jnp.where(first_var, turned, plane)


def primitives(first_var, planes):
    density, moment_x = both(first_var, planes[0])
    moment_y, moment_z = both(first_var, planes[1])
    energy = jnp.where(first_var, planes[2], pltpu.roll(planes[2], 4, 0))
    inverse = 1.0 / density
    velocity_x = moment_x * inverse
    velocity_y = moment_y * inverse
    velocity_z = moment_z * inverse
    kinetic = moment_x * velocity_x + moment_y * velocity_y + moment_z * velocity_z
    pressure = (GAMMA_GAS - 1.0) * (energy - 0.5 * kinetic)
    sound = jnp.sqrt(GAMMA_GAS * pressure * inverse)
    return velocity_x, velocity_y, pressure, sound


def rows_of(var, inst, half):
    return (var // 2) * ROWS + (var % 2) * 4 + inst * 2 + half


def pack_kernel(
    held_state_ref, held_rate_ref, held_next_ref, held_codes_ref, out_ref, next_ref, codes_ref,
    state_ref, rate_ref, sems,
):
    copies = [
        pltpu.make_async_copy(source, target, sems.at[k])
        for k, (source, target) in enumerate(
            (
                (held_state_ref, state_ref),
                (held_rate_ref, rate_ref),
                (held_next_ref, next_ref),
                (held_codes_ref, codes_ref),
            )
        )
    ]
    for copy in copies:
        copy.start()
    for copy in copies:
        copy.wait()
    mirrored = lax.axis_index("cell") // (lax.axis_size("cell") // 2)
    for cell in range(2):
        place = pl.multiple_of(jnp.bitwise_xor(cell, mirrored) * CELL_ROWS, ROWS)
        for k in range(PAIRS):
            rows = [
                state_ref[inst, 2 * k + var, pl.ds(cell, 1), pl.ds(half * LANES, LANES)]
                for var in range(2)
                for inst in range(2)
                for half in range(2)
            ]
            for row, values in enumerate(rows):
                out_ref[0, pl.ds(place + (k * ROWS + row), 1), :] = values
    rates = [
        rate_ref[pl.ds(cell, 1), pl.ds(half * LANES, LANES)]
        for cell in range(2)
        for half in range(2)
    ]
    for row in range(4):
        out_ref[0, pl.ds(RATE_ROW + row, 1), :] = jnp.where(
            mirrored == 0, rates[row], rates[row ^ 2]
        )
    out_ref[0, pl.ds(RATE_ROW + 4, 4), :] = jnp.zeros((4, LANES), jnp.float32)
    for row in range(0, BLOCK_ROWS, ROWS):
        values = out_ref[0, pl.ds(row, ROWS), :]
        for copy in range(1, out_ref.shape[0]):
            out_ref[copy, pl.ds(row, ROWS), :] = values


def turn_insts(first_inst, plane):
    return jnp.where(first_inst, pltpu.roll(plane, 6, 0), pltpu.roll(plane, 2, 0))


def time_weights(first_inst, shift):
    offsets = spectral_offsets()
    other = jnp.where(
        first_inst, offsets[(2 * shift + 1) % NT], offsets[(2 * shift - 1) % NT]
    )
    return offsets[(2 * shift) % NT], other


def at_block(ref, y, block):
    blocks = ref.shape[1]
    mirrored = lax.axis_index("cell") // blocks
    place = mirrored * block + (1 - mirrored) * (blocks - 1 - block)
    return ref.at[ref.shape[0] - 1 - y, place]


def cell_plane(ref, y, cell, k):
    return at_block(ref, y, cell // 2)[pl.ds((cell % 2) * CELL_ROWS + k * ROWS, ROWS), :]


def partner_kernel(all_ref, out_ref):
    own_inst = lax.axis_index("inst")
    own_y, core = own_inst >> 1, own_inst & 1
    _, first_inst, _ = plane_masks()
    one, three = time_weights(first_inst, 1), time_weights(first_inst, 3)
    near = [jnp.where(core == 0, a, b) for a, b in zip(one, three)]
    away = [jnp.where(core == 0, b, a) for a, b in zip(one, three)]
    for cell in range(2 * all_ref.shape[1]):
        for k in range(PAIRS):
            here = cell_plane(all_ref, own_y, cell, k)
            there = cell_plane(all_ref, 1 - own_y, cell, k)
            out_ref[pl.ds(cell * CELL_ROWS + k * ROWS, ROWS), :] = (
                near[0] * here
                + away[0] * there
                + turn_insts(first_inst, near[1] * here + away[1] * there)
            )


def two_by_two(first, second):
    def entry(a, b, c, d):
        terms = [x * y for x, y in ((a, b), (c, d)) if x is not None and y is not None]
        return None if not terms else terms[0] if len(terms) == 1 else terms[0] + terms[1]

    return (
        entry(first[0], second[0], first[1], second[2]),
        entry(first[0], second[1], first[1], second[3]),
        entry(first[2], second[0], first[3], second[2]),
        entry(first[2], second[1], first[3], second[3]),
    )


def inverse_of(matrix):
    reciprocal = 1.0 / (matrix[0] * matrix[3] - matrix[1] * matrix[2])
    return (
        matrix[3] * reciprocal,
        -(matrix[1] * reciprocal),
        -(matrix[2] * reciprocal),
        matrix[0] * reciprocal,
    )


def less(first, second):
    return tuple(a if b is None else a - b for a, b in zip(first, second))


def minus(members):
    return tuple(None if a is None else -a for a in members)


def matrix_vector(matrix, low, high):
    def row(a, b):
        terms = [x * y for x, y in ((a, low), (b, high)) if x is not None]
        return terms[0] if len(terms) == 1 else terms[0] + terms[1]

    return row(matrix[0], matrix[1]), row(matrix[2], matrix[3])


def apply_matrix(matrix, side):
    parts = [matrix_vector(matrix, side[k], side[PAIRS + k]) for k in range(PAIRS)]
    return [low for low, _ in parts] + [high for _, high in parts]


def difference(first, second):
    return [a - b for a, b in zip(first, second)]


def flux_along(first_var, planes, velocity, pressure, sign):
    normal = sign * velocity
    return [
        planes[0] * normal + jnp.where(first_var, 0.0, sign * pressure),
        planes[1] * normal,
        planes[2] * normal + jnp.where(first_var, pressure * normal, 0.0),
    ]


class LineCells:
    def __init__(self, first_var, sign):
        self.first_var, self.sign = first_var, sign
        self.state, self.pressure, self.radius = {}, {}, {}
        self.flux, self.step, self.sensor = {}, {}, {}

    def add(self, cell, planes, velocity, pressure, sound):
        self.state[cell], self.pressure[cell] = planes, pressure
        self.radius[cell] = jnp.abs(velocity) + sound
        self.flux[cell] = flux_along(self.first_var, planes, velocity, pressure, self.sign)
        if cell - 1 in self.state:
            self.step[cell - 1] = difference(planes, self.state[cell - 1])
        if cell - 2 in self.state:
            twice = 2.0 * self.pressure[cell - 1]
            outer = pressure + self.pressure[cell - 2]
            self.sensor[cell - 1] = jnp.abs(outer - twice) / (outer + twice)

    def face(self, cell):
        second = SENSOR_GAIN * jnp.maximum(self.sensor[cell], self.sensor[cell + 1])
        fourth = jnp.maximum(0.0, FOURTH_GAIN - second)
        face_radius = 0.5 * (self.radius[cell] + self.radius[cell + 1])
        near_weight = face_radius * (second + 2.0 * fourth)
        far_weight = face_radius * fourth
        return [
            0.5 * (self.flux[cell][k] + self.flux[cell + 1][k])
            - (
                near_weight * self.step[cell][k]
                - far_weight * (self.step[cell + 1][k] + self.step[cell - 1][k])
            )
            for k in range(PAIRS)
        ]

    def near(self, cell):
        scale = SECOND_IMPL * 0.5 + 2.0 * FOURTH_IMPL
        return -scale * (self.radius[cell] + self.radius[cell + 1])

    def far(self, cell):
        return FOURTH_IMPL * self.radius[cell]

    def middle(self, cell, rate):
        centre, above = self.radius[cell], self.radius[cell + 1]
        if cell == 0:
            total, weighted = centre + (centre + above), 4.0 * centre + above
        else:
            below = self.radius[cell - 1]
            total = (below + centre) + (centre + above)
            weighted = below + 4.0 * centre + above
        result = SECOND_IMPL * (0.5 * total) + FOURTH_IMPL * weighted
        return result if rate is None else rate * centre + result

    def diagonal(self, cell, rates):
        across = self.near(cell)
        return (self.middle(cell, rates[0]), across, across, self.middle(cell + 1, rates[1]))

    def below(self, cell):
        return (self.far(cell - 1), self.near(cell - 1), None, self.far(cell))

    def above(self, cell):
        return (self.far(cell + 1), None, self.near(cell + 1), self.far(cell + 2))


def rates_at(ref, y, block, first_half):
    rows = [at_block(ref, y, block)[pl.ds(RATE_ROW + k, 1), :] for k in range(4)]
    return [jnp.where(first_half, rows[2 * k], rows[2 * k + 1]) for k in range(2)]


def half_kernel(
    all_ref, next_ref, codes_ref, partial_ref, factor_ref, blocks_ref, fixed_ref, line_ref,
):
    own_y = lax.axis_index("inst") >> 1
    blocks = all_ref.shape[1]
    cells = 2 * blocks
    mirrored = lax.axis_index("cell") // blocks
    sign = (1 - 2 * mirrored).astype(jnp.float32)
    shape = (ROWS, LANES)
    lane_index = lax.broadcasted_iota(jnp.int32, shape, 1)
    first_var, first_inst, half_index = plane_masks()
    first_half = half_index == 0
    zero = jnp.zeros(shape, jnp.float32)

    next_rows = [
        next_ref[pl.ds(half * LANES, LANES)].reshape(1, LANES) for half in range(2)
    ]
    next_line = jnp.where(first_half, next_rows[0], next_rows[1])
    column = lax.broadcasted_iota(jnp.int32, (LANES, LANES), 0)
    prev_halves = []
    for target in range(2):
        total = None
        for source in range(2):
            hits = jnp.where(column + target * LANES == next_rows[source], 1.0, 0.0)
            names = (lane_index + source * LANES).astype(jnp.float32)
            part = lax.dot_general(
                names, hits, (((1,), (1,)), ((), ())), preferred_element_type=jnp.float32
            )
            total = part if total is None else total + part
        prev_halves.append(total)
    prev_line = jnp.where(first_half, prev_halves[0], prev_halves[1]).astype(jnp.int32)

    def picker(lines):
        lane = lines & (LANES - 1)
        same = (lines >> 7) == half_index

        def pick(plane):
            swapped = jnp.where(first_half, pltpu.roll(plane, 7, 0), pltpu.roll(plane, 1, 0))
            here = jnp.take_along_axis(plane, lane, axis=1, mode="promise_in_bounds")
            there = jnp.take_along_axis(swapped, lane, axis=1, mode="promise_in_bounds")
            return jnp.where(same, here, there)

        return pick

    pick_next = picker(next_line)
    pick_prev = picker(prev_line)

    def loaded(cell, y=own_y):
        return [cell_plane(all_ref, y, cell, k) for k in range(PAIRS)]

    own_weights, away_weights = time_weights(first_inst, 0), time_weights(first_inst, 2)

    def own_time_parts(planes, cell):
        return [
            away_weights[0] * away
            + turn_insts(first_inst, own_weights[1] * own + away_weights[1] * away)
            for own, away in zip(planes, loaded(cell, 1 - own_y))
        ]

    def flux_across(planes, velocity, pressure):
        return [
            planes[0] * velocity,
            planes[1] * velocity + jnp.where(first_var, pressure, 0.0),
            planes[2] * velocity + jnp.where(first_var, pressure * velocity, 0.0),
        ]

    def pitch_flux(planes, velocity_y, pressure, sound):
        nearby = [pick_next(plane) for plane in planes]
        _, next_velocity, next_pressure, next_sound = primitives(first_var, nearby)
        own_flux = flux_across(planes, velocity_y, pressure)
        next_flux = flux_across(nearby, next_velocity, next_pressure)
        weight = (PITCH_GAIN * 0.5) * (
            jnp.abs(velocity_y) + sound + (jnp.abs(next_velocity) + next_sound)
        )
        return [
            0.5 * (a + b) - weight * (n - o)
            for a, b, n, o in zip(own_flux, next_flux, nearby, planes)
        ]

    for cell in range(cells):
        planes = loaded(cell)
        velocity_x, velocity_y, pressure, sound = primitives(first_var, planes)
        line_ref[cell, 0], line_ref[cell, 1], line_ref[cell, 2] = velocity_x, pressure, sound
        faces_across = pitch_flux(planes, velocity_y, pressure, sound)
        times = own_time_parts(planes, cell)
        for k in range(PAIRS):
            partial_ref[cell, k] = -(times[k] + (faces_across[k] - pick_prev(faces_across[k])))

    tile = half_index * (LANES // LINES_DEV) + lane_index // LINES_DEV
    end_codes = jnp.where(mirrored == 0, codes_ref[pl.ds(0, 1), :], codes_ref[pl.ds(1, 1), :])
    codes = jnp.zeros(shape, jnp.int32)
    for k in range(2 * LANES // LINES_DEV):
        codes = jnp.where(tile == k, jnp.broadcast_to(end_codes[:, k : k + 1], shape), codes)

    def ghost(cell):
        planes = loaded(-1 - cell)
        copied = loaded(0)
        result = []
        for k in range(PAIRS):
            reflected = planes[k] if k else jnp.where(first_var, planes[k], -planes[k])
            inflow = jnp.where(first_var, FREE_STATE[2 * k], FREE_STATE[2 * k + 1])
            result.append(
                jnp.where(codes == 0, reflected, jnp.where(codes == 1, inflow, copied[k]))
            )
        return result

    line = LineCells(first_var, sign)
    faces, inverses, aboves = {}, [], []
    for cell in range(-2, cells):
        if cell < 0:
            planes = ghost(cell)
            velocity_x, _, pressure, sound = primitives(first_var, planes)
        else:
            planes = loaded(cell)
            velocity_x, pressure, sound = [line_ref[cell, k] for k in range(3)]
        line.add(cell, planes, velocity_x, pressure, sound)
        if cell >= 1:
            faces[cell - 2] = line.face(cell - 2)
        if cell >= 2:
            at = cell - 2
            for k in range(PAIRS):
                partial_ref[at, k] = partial_ref[at, k] + (faces[at - 1][k] - faces[at][k])
        if cell >= 3 and cell % 2 == 1:
            at = cell - 3
            block = at // 2
            rates = rates_at(all_ref, own_y, block, first_half)
            diag = line.diagonal(at, rates)
            if block > 0:
                factor = two_by_two(line.below(at), inverses[-1])
                diag = less(diag, two_by_two(factor, aboves[-1]))
                for n in range(4):
                    factor_ref[block - 1, n] = factor[n]
            inverses.append(inverse_of(diag))
            aboves.append(line.above(at))
            kept = [*inverses[-1], aboves[-1][0], *aboves[-1][2:]]
            for n, plane in enumerate(kept):
                blocks_ref[block, n] = plane

    last = cells - 2
    for k in range(PAIRS):
        partial_ref[last, k] = partial_ref[last, k] + faces[last - 1][k]
    factor = two_by_two(line.below(last), inverses[-1])
    for n in range(4):
        factor_ref[blocks - 2, n] = factor[n]
    correction = list(two_by_two(factor, aboves[-1]))
    rates = rates_at(all_ref, own_y, blocks - 1, first_half)
    for member in range(2):
        centre = line.radius[last + member]
        correction[3 * member] = correction[3 * member] - rates[member] * centre
    for n in range(3):
        for k, plane in enumerate(line.state[cells - 3 + n]):
            fixed_ref[pl.ds(n * CELL_ROWS + k * ROWS, ROWS), :] = plane
    for n in range(2):
        fixed_ref[pl.ds(SIDE_ROW + n * ROWS, ROWS), :] = jnp.where(
            first_var, correction[2 * n], correction[2 * n + 1]
        )


def reduce_kernel(partial_ref, time_ref, factor_ref, fixed_ref, middle_ref, sides_ref):
    blocks = partial_ref.shape[0] // 2
    side = None
    for block in range(blocks):
        own = []
        for cell in (2 * block, 2 * block + 1):
            for k in range(PAIRS):
                time = time_ref[pl.ds(cell * CELL_ROWS + k * ROWS, ROWS), :]
                own.append(partial_ref[cell, k] - time)
        if block > 0:
            factor = [factor_ref[block - 1, n] for n in range(4)]
            own = difference(own, apply_matrix(factor, side))
        side = own
        for n, plane in enumerate(side):
            if block < blocks - 1:
                sides_ref[block, n] = plane
            else:
                middle_ref[pl.ds(SIDE_ROW + n * ROWS, ROWS), :] = plane
    for row in range(0, SIDE_ROW, ROWS):
        middle_ref[pl.ds(row, ROWS), :] = fixed_ref[pl.ds(row, ROWS), :]
    for n in range(2):
        rows = fixed_ref[pl.ds(SIDE_ROW + n * ROWS, ROWS), :]
        middle_ref[pl.ds(CORRECTION_ROW + n * ROWS, ROWS), :] = rows


def spread_kernel(all_ref, blocks_ref, sides_ref, known_ref, spread_ref, table_ref):
    own_y = lax.axis_index("inst") >> 1
    blocks = all_ref.shape[1]
    own_cell = lax.axis_index("cell")
    own_block = jnp.where(own_cell < blocks, own_cell, 2 * blocks - 1 - own_cell)
    zero = jnp.zeros((ROWS, LANES), jnp.float32)
    known, spread = [zero] * (2 * PAIRS), (zero + 1.0, zero, zero, zero + 1.0)
    for block in range(blocks - 1, -1, -1):
        if block < blocks - 1:
            kept = [blocks_ref[block, n] for n in range(7)]
            inverse, above = kept[:4], (kept[4], None, kept[5], kept[6])
            side = [sides_ref[block, n] for n in range(2 * PAIRS)]
            step = two_by_two(inverse, above)
            own = apply_matrix(inverse, side)
            if block < blocks - 2:
                known = difference(own, apply_matrix(step, known))
                spread = minus(two_by_two(step, spread))
            else:
                known, spread = own, minus(step)
        for n, plane in enumerate(known + list(spread)):
            table_ref[block, n] = plane
    for n in range(2 * PAIRS):
        base = at_block(all_ref, own_y, own_block)[pl.ds(n * ROWS, ROWS), :]
        known_ref[n] = base + table_ref[own_block, n]
    for n in range(4):
        spread_ref[n] = table_ref[own_block, 2 * PAIRS + n]


def join_kernel(here_ref, there_ref, known_ref, spread_ref, out_ref):
    mirrored = lax.axis_index("cell") // (lax.axis_size("cell") // 2)
    sign = (1 - 2 * mirrored).astype(jnp.float32)
    first_var, _, _ = plane_masks()

    def plane_of(ref, row):
        return ref[pl.ds(row, ROWS), :]

    line = LineCells(first_var, sign)
    for cell in range(6):
        ref, at = (here_ref, cell) if cell < 3 else (there_ref, 5 - cell)
        planes = [plane_of(ref, at * CELL_ROWS + k * ROWS) for k in range(PAIRS)]
        velocity_x, _, pressure, sound = primitives(first_var, planes)
        line.add(cell, planes, velocity_x, pressure, sound)
    faces = {cell: line.face(cell) for cell in (1, 2, 3)}

    def correction_of(ref):
        pairs = [both(first_var, plane_of(ref, CORRECTION_ROW + n * ROWS)) for n in range(2)]
        return [pairs[0][0], pairs[0][1], pairs[1][0], pairs[1][1]]

    here_side = [plane_of(here_ref, SIDE_ROW + n * ROWS) for n in range(2 * PAIRS)]
    there_side = [plane_of(there_ref, SIDE_ROW + n * ROWS) for n in range(2 * PAIRS)]
    side = [here_side[k] - faces[1][k] for k in range(PAIRS)]
    side += [here_side[PAIRS + k] + (faces[1][k] - faces[2][k]) for k in range(PAIRS)]
    other = [there_side[PAIRS + k] + (faces[2][k] - faces[3][k]) for k in range(PAIRS)]
    other += [there_side[k] + faces[3][k] for k in range(PAIRS)]
    no_rates = (None, None)
    diag = difference(line.diagonal(1, no_rates), correction_of(here_ref))
    other_diag = difference(line.diagonal(3, no_rates), correction_of(there_ref)[::-1])
    factor = two_by_two(line.above(1), inverse_of(other_diag))
    diag = less(diag, two_by_two(factor, line.below(3)))
    middle = apply_matrix(inverse_of(diag), difference(side, apply_matrix(factor, other)))
    moved = apply_matrix([spread_ref[n] for n in range(4)], middle)
    results = [known_ref[n] + moved[n] for n in range(2 * PAIRS)]
    for cell in range(2):
        for k in range(PAIRS):
            first, second = results[cell * PAIRS + k], results[(1 - cell) * PAIRS + k]
            result = jnp.where(mirrored == 0, first, second)
            for var in range(2):
                for inst in range(2):
                    for half in range(2):
                        row = rows_of(var, inst, half)
                        out_ref[
                            inst, 2 * k + var, pl.ds(cell, 1), pl.ds(half * LANES, LANES)
                        ] = result[row : row + 1]


def share_half(copies):
    insts, count = lax.axis_size("inst"), lax.axis_size("cell")
    halves = [range(count // 2 - 1, -1, -1), range(count - 1, count // 2 - 1, -1)]
    groups = [
        [inst * count + cell for inst in range(insts - 2 + core, -1, -2) for cell in half]
        for core in range(2)
        for half in halves
    ]
    return lax.all_to_all(
        copies, ("inst", "cell"), split_axis=0, concat_axis=0, tiled=True,
        axis_index_groups=groups,
    )


def swap_cores(block):
    pairs = [(inst, inst ^ 1) for inst in range(lax.axis_size("inst"))]
    return lax.ppermute(block, "inst", pairs)


def swap_halves(block):
    count = lax.axis_size("cell")
    return lax.ppermute(block, "cell", [(i, (i + count // 2) % count) for i in range(count)])


def float_shape(*sizes):
    return jax.ShapeDtypeStruct(sizes, jnp.float32)


def local_by_halves(state, pseudo_rate, line_next, face_codes):
    blocks = lax.axis_size("cell") // 2
    cells = 2 * blocks
    vmem = pl.BlockSpec(memory_space=pltpu.VMEM)
    plane = (ROWS, LANES)
    params = pltpu.CompilerParams(vmem_limit_bytes=VMEM_BYTES)
    places = lax.axis_size("inst") // 2
    held = [
        pltpu.with_memory_space_constraint(array, pltpu.HBM)
        for array in (state, pseudo_rate, line_next, face_codes)
    ]
    packed, next_here, codes_here = pl.pallas_call(
        pack_kernel,
        out_shape=(
            float_shape(places * blocks, BLOCK_ROWS, LANES),
            jax.ShapeDtypeStruct(line_next.shape, jnp.int32),
            jax.ShapeDtypeStruct(face_codes.shape, jnp.int32),
        ),
        in_specs=[pl.BlockSpec(memory_space=pltpu.HBM)] * 4,
        out_specs=(vmem, vmem, vmem),
        scratch_shapes=[
            pltpu.VMEM(state.shape, jnp.float32),
            pltpu.VMEM(pseudo_rate.shape, jnp.float32),
            pltpu.SemaphoreType.DMA((4,)),
        ],
        compiler_params=params,
    )(*held)
    shared = share_half(packed).reshape(places, blocks, BLOCK_ROWS, LANES)
    for_partner = pl.pallas_call(
        partner_kernel,
        out_shape=float_shape(cells * CELL_ROWS, LANES),
        in_specs=[vmem],
        out_specs=vmem,
        compiler_params=params,
    )(shared)
    from_partner = swap_cores(for_partner)
    beside = pl.CostEstimate(flops=10**6, bytes_accessed=10**6, transcendentals=0)
    partial, factors, eliminated, fixed = pl.pallas_call(
        half_kernel,
        out_shape=(
            float_shape(cells, PAIRS, *plane),
            float_shape(blocks - 1, 4, *plane),
            float_shape(blocks - 1, 7, *plane),
            float_shape(FIXED_ROWS, LANES),
        ),
        in_specs=[vmem] * 3,
        out_specs=(vmem,) * 4,
        scratch_shapes=[pltpu.VMEM((cells, 3) + plane, jnp.float32)],
        compiler_params=params,
        cost_estimate=beside,
    )(shared, next_here, codes_here)
    here, sides = pl.pallas_call(
        reduce_kernel,
        out_shape=(
            float_shape(MIDDLE_ROWS, LANES),
            float_shape(blocks - 1, 2 * PAIRS, *plane),
        ),
        in_specs=[vmem] * 4,
        out_specs=(vmem, vmem),
        compiler_params=params,
    )(partial, from_partner, factors, fixed)
    there = swap_halves(here)
    known, spread = pl.pallas_call(
        spread_kernel,
        out_shape=(float_shape(2 * PAIRS, *plane), float_shape(4, *plane)),
        in_specs=[vmem] * 3,
        out_specs=(vmem, vmem),
        scratch_shapes=[pltpu.VMEM((blocks, 2 * PAIRS + 4) + plane, jnp.float32)],
        compiler_params=params,
        cost_estimate=beside,
    )(shared, eliminated, sides)
    return pl.pallas_call(
        join_kernel,
        out_shape=float_shape(*state.shape),
        in_specs=[vmem] * 4,
        out_specs=vmem,
        compiler_params=params,
    )(here, there, known, spread)


def solution(mesh):
    placed = (P("inst", None, "cell", None), P("cell", None), P(), P())
    inst_count, cell_count = mesh.shape["inst"], mesh.shape["cell"]

    def local(state, pseudo_rate, line_next, face_codes):
        small = (
            state.shape == (2, 6, 2, 2 * LANES)
            and inst_count * 2 == NT
            and cell_count == 8
            and face_codes.shape[1] * LINES_DEV == state.shape[3]
        )
        chosen = local_by_halves if small else local_by_lines
        return chosen(state, pseudo_rate, line_next, face_codes)

    return jax.shard_map(
        local, mesh=mesh, in_specs=placed, out_specs=P("inst", None, "cell", None), check_vma=False
    )
```

```python
import functools

import jax
import jax.numpy as jnp
import numpy as np
from jax import lax
from jax.experimental import pallas as pl
from jax.experimental.pallas import tpu as pltpu
from jax.sharding import PartitionSpec as P

NT = 8
LINES_DEV = 32


GAMMA_GAS = 1.4
OMEGA_BLADE = 1.0
SENSOR_GAIN = 0.25
FOURTH_GAIN = 0.03125
PITCH_GAIN = 0.5
SECOND_IMPL = 1.0
FOURTH_IMPL = 0.25
FREE_STATE = (1.0, 0.5, 0.0, 0.0, 2.625, 0.2)
MIRROR_SIGNS = (1.0, -1.0, 1.0, 1.0, 1.0, 1.0)
ZERO_BLOCK = (0.0, 0.0, 0.0, 0.0)
UNIT_BLOCK = (1.0, 0.0, 0.0, 1.0)
ZERO_PAIR = (0.0, 0.0)


def extended(block, sides, width):
    for axis, dim in sides:
        count = lax.axis_size(axis)
        forward = [(i, i + 1) for i in range(count - 1)]
        backward = [(target, source) for source, target in forward]
        low = lax.ppermute(
            lax.slice_in_dim(block, block.shape[dim] - width, None, axis=dim), axis, forward
        )
        high = lax.ppermute(lax.slice_in_dim(block, 0, width, axis=dim), axis, backward)
        block = jnp.concatenate([low, block, high], axis=dim)
    return block


def spectral_matrix(instances):
    offsets = np.arange(instances)[:, None] - np.arange(instances)[None, :]
    angles = np.pi * offsets / instances
    safe_sin = np.where(offsets == 0, 1.0, np.sin(angles))
    parity = np.where(np.mod(offsets, 2) == 0, -1.0, 1.0)
    matrix_table = np.where(
        offsets == 0, 0.0, 0.5 * OMEGA_BLADE * parity * np.cos(angles) / safe_sin
    )
    return jnp.asarray(matrix_table, jnp.float32)


def primitive_parts(cells_state):
    density = cells_state[..., 0, :, :]
    inverse = 1.0 / density
    velocity_x = cells_state[..., 1, :, :] * inverse
    velocity_y = cells_state[..., 2, :, :] * inverse
    velocity_z = cells_state[..., 3, :, :] * inverse
    energy = cells_state[..., 4, :, :]
    pressure = (GAMMA_GAS - 1.0) * (
        energy
        - 0.5
        * density
        * (velocity_x * velocity_x + velocity_y * velocity_y + velocity_z * velocity_z)
    )
    sound_speed = jnp.sqrt(GAMMA_GAS * pressure * inverse)
    return (velocity_x, velocity_y, pressure, sound_speed)


def directed_flux(cells_state, normal_velocity, pressure, component):
    zero_plane = jnp.zeros_like(pressure)
    pressure_rows = [
        zero_plane,
        zero_plane,
        zero_plane,
        zero_plane,
        pressure * normal_velocity,
        zero_plane,
    ]
    pressure_rows[component] = pressure
    return cells_state * normal_velocity[..., None, :, :] + jnp.stack(pressure_rows, axis=-3)


def line_residual(padded):
    velocity_x, velocity_y, pressure, sound_speed = primitive_parts(padded)
    flux_line = directed_flux(padded, velocity_x, pressure, 1)
    radius = jnp.abs(velocity_x) + sound_speed
    sensor = jnp.abs(
        pressure[..., 2:, :] - 2.0 * pressure[..., 1:-1, :] + pressure[..., :-2, :]
    ) / (pressure[..., 2:, :] + 2.0 * pressure[..., 1:-1, :] + pressure[..., :-2, :])
    second = SENSOR_GAIN * jnp.maximum(sensor[..., :-1, :], sensor[..., 1:, :])
    fourth = jnp.maximum(0.0, FOURTH_GAIN - second)
    face_radius = 0.5 * (radius[..., 1:-2, :] + radius[..., 2:-1, :])
    left_far = padded[..., :-3, :]
    left_near = padded[..., 1:-2, :]
    right_near = padded[..., 2:-1, :]
    right_far = padded[..., 3:, :]
    damping = face_radius[..., None, :, :] * (
        second[..., None, :, :] * (right_near - left_near)
        - fourth[..., None, :, :] * (right_far - 3.0 * right_near + 3.0 * left_near - left_far)
    )
    face_flux = 0.5 * (flux_line[..., 1:-2, :] + flux_line[..., 2:-1, :]) - damping
    return (face_flux[..., 1:, :] - face_flux[..., :-1, :], radius)


def pitch_parts(cells_state):
    velocity_x, velocity_y, pressure, sound_speed = primitive_parts(cells_state)
    return (directed_flux(cells_state, velocity_y, pressure, 2), jnp.abs(velocity_y) + sound_speed)


def pitch_residual(cells_state, next_lines, prev_lines):
    pitch_flux, radius = pitch_parts(cells_state)
    state_next = jnp.take(cells_state, next_lines, axis=-1)
    flux_next, radius_next = pitch_parts(state_next)
    face_flux = 0.5 * (pitch_flux + flux_next) - PITCH_GAIN * (0.5 * (radius + radius_next))[
        ..., None, :, :
    ] * (state_next - cells_state)
    return face_flux - jnp.take(face_flux, prev_lines, axis=-1)


def boundary_cells(edge_pair, line_codes, lower_end):
    reflected = edge_pair[..., ::-1, :] * jnp.asarray(MIRROR_SIGNS, jnp.float32)[:, None, None]
    if lower_end:
        copied = jnp.concatenate([edge_pair[..., :1, :], edge_pair[..., :1, :]], axis=-2)
    else:
        copied = jnp.concatenate([edge_pair[..., 1:, :], edge_pair[..., 1:, :]], axis=-2)
    inflow = jnp.asarray(FREE_STATE, jnp.float32)[:, None, None] + jnp.zeros_like(edge_pair)
    return jnp.where(line_codes == 0, reflected, jnp.where(line_codes == 1, inflow, copied))


def line_coefficients(radius_ext, diagonal_term, positions, total_cells):
    radius_below = radius_ext[..., :-2, :]
    radius_centre = radius_ext[..., 1:-1, :]
    radius_above = radius_ext[..., 2:, :]
    face_below = 0.5 * (radius_below + radius_centre)
    face_above = 0.5 * (radius_centre + radius_above)
    far_low = FOURTH_IMPL * radius_below
    near_low = -SECOND_IMPL * face_below - 2.0 * FOURTH_IMPL * (radius_below + radius_centre)
    middle = (
        diagonal_term
        + SECOND_IMPL * (face_below + face_above)
        + FOURTH_IMPL * (radius_below + 4.0 * radius_centre + radius_above)
    )
    near_high = -SECOND_IMPL * face_above - 2.0 * FOURTH_IMPL * (radius_centre + radius_above)
    far_high = FOURTH_IMPL * radius_above
    column = positions[:, None]
    far_low = jnp.where(column >= 2, far_low, 0.0)
    near_low = jnp.where(column >= 1, near_low, 0.0)
    near_high = jnp.where(column <= total_cells - 2, near_high, 0.0)
    far_high = jnp.where(column <= total_cells - 3, far_high, 0.0)
    return (far_low, near_low, middle, near_high, far_high)


def block_product(first_matrix, second_matrix):
    return (
        first_matrix[0] * second_matrix[0] + first_matrix[1] * second_matrix[2],
        first_matrix[0] * second_matrix[1] + first_matrix[1] * second_matrix[3],
        first_matrix[2] * second_matrix[0] + first_matrix[3] * second_matrix[2],
        first_matrix[2] * second_matrix[1] + first_matrix[3] * second_matrix[3],
    )


def block_inverse(matrix):
    determinant = matrix[0] * matrix[3] - matrix[1] * matrix[2]
    reciprocal = 1.0 / determinant
    return (
        matrix[3] * reciprocal,
        -matrix[1] * reciprocal,
        -matrix[2] * reciprocal,
        matrix[0] * reciprocal,
    )


def block_apply(matrix, vector):
    return (
        matrix[0] * vector[0] + matrix[1] * vector[1],
        matrix[2] * vector[0] + matrix[3] * vector[1],
    )


def add_blocks(first_members, second_members):
    return tuple((a + b for a, b in zip(first_members, second_members)))


def negate(members):
    return tuple((-a for a in members))


def extend_blocks(members, fill_values):
    return tuple(
        (
            jnp.concatenate([m, jnp.full_like(m[..., :1, :], f)], axis=-2)
            for m, f in zip(members, fill_values)
        )
    )


def shift_next(members, fill_values):
    return tuple(
        (
            jnp.concatenate([m[..., 1:, :], jnp.full_like(m[..., :1, :], f)], axis=-2)
            for m, f in zip(members, fill_values)
        )
    )


def shift_prev(members):
    return tuple(
        (jnp.concatenate([jnp.zeros_like(m[..., :1, :]), m[..., :-1, :]], axis=-2) for m in members)
    )


def pair_split(member):
    shaped = member.reshape(member.shape[:-2] + (member.shape[-2] // 2, 2, member.shape[-1]))
    return (shaped[..., 0, :], shaped[..., 1, :])


def split_parity(members):
    halves = [pair_split(m) for m in members]
    return (tuple((h[0] for h in halves)), tuple((h[1] for h in halves)))


def alternate(first_member, second_member):
    stacked = jnp.stack((first_member, second_member), axis=-2)
    return stacked.reshape(
        first_member.shape[:-2] + (2 * first_member.shape[-2], first_member.shape[-1])
    )


def reduce_blocks(sub_blocks, diag_blocks, super_blocks, right_side):
    block_count = diag_blocks[0].shape[-2]
    if block_count == 1:
        return block_apply(block_inverse(diag_blocks), right_side)
    if block_count % 2 == 1:
        sub_blocks = extend_blocks(sub_blocks, ZERO_BLOCK)
        diag_blocks = extend_blocks(diag_blocks, UNIT_BLOCK)
        super_blocks = extend_blocks(super_blocks, ZERO_BLOCK)
        right_side = extend_blocks(right_side, ZERO_PAIR)
    sub_even, sub_odd = split_parity(sub_blocks)
    diag_even, diag_odd = split_parity(diag_blocks)
    super_even, super_odd = split_parity(super_blocks)
    side_even, side_odd = split_parity(right_side)
    inverse_even = block_inverse(diag_even)
    inverse_next = shift_next(inverse_even, UNIT_BLOCK)
    sub_next = shift_next(sub_even, ZERO_BLOCK)
    super_next = shift_next(super_even, ZERO_BLOCK)
    side_next = shift_next(side_even, ZERO_PAIR)
    left_factor = negate(block_product(sub_odd, inverse_even))
    right_factor = negate(block_product(super_odd, inverse_next))
    reduced_sub = block_product(left_factor, sub_even)
    reduced_diag = add_blocks(
        diag_odd,
        add_blocks(block_product(left_factor, super_even), block_product(right_factor, sub_next)),
    )
    reduced_super = block_product(right_factor, super_next)
    reduced_side = add_blocks(
        side_odd,
        add_blocks(block_apply(left_factor, side_even), block_apply(right_factor, side_next)),
    )
    odd_values = reduce_blocks(reduced_sub, reduced_diag, reduced_super, reduced_side)
    before_values = shift_prev(odd_values)
    remainder = add_blocks(
        side_even,
        negate(
            add_blocks(block_apply(sub_even, before_values), block_apply(super_even, odd_values))
        ),
    )
    even_values = block_apply(inverse_even, remainder)
    merged = tuple((alternate(e, o) for e, o in zip(even_values, odd_values)))
    return tuple((m[..., :block_count, :] for m in merged))


def cells_leading(block):
    moved = jnp.transpose(block, (2, 0, 1, 3))
    return moved.reshape(block.shape[2], block.shape[0] * block.shape[1] * block.shape[3])


def solve_in_lanes(coefficients, line_source):
    source_shape = line_source.shape
    lane_coef = [cells_leading(jnp.broadcast_to(c[:, None], source_shape)) for c in coefficients]
    pairs_list = [pair_split(m) for m in lane_coef]
    zero_plane = jnp.zeros_like(pairs_list[2][0])
    sub_blocks = (pairs_list[0][0], pairs_list[1][0], zero_plane, pairs_list[0][1])
    diag_blocks = (pairs_list[2][0], pairs_list[3][0], pairs_list[1][1], pairs_list[2][1])
    super_blocks = (pairs_list[4][0], zero_plane, pairs_list[3][1], pairs_list[4][1])
    values = reduce_blocks(
        sub_blocks, diag_blocks, super_blocks, pair_split(cells_leading(line_source))
    )
    flat = alternate(values[0], values[1])
    shaped = flat.reshape(source_shape[2], source_shape[0], source_shape[1], source_shape[3])
    return jnp.transpose(shaped, (1, 2, 0, 3))


def return_tiles(line_values):
    return lax.all_to_all(line_values, "cell", split_axis=2, concat_axis=3, tiled=True)


def local_by_lines(state, pseudo_rate, line_next, face_codes):
    local_count = state.shape[0]
    tile_cells = state.shape[2]
    cell_index = lax.axis_index("cell")
    cell_count = lax.axis_size("cell")
    total_cells = tile_cells * cell_count
    spectral = spectral_matrix(NT)
    first_local = lax.axis_index("inst") * local_count
    own_rows = lax.dynamic_slice_in_dim(spectral, first_local, local_count, 0)
    shard_block = jax.tree.map(lambda a: lax.all_gather(a, "inst", axis=0, tiled=True), state)
    columns = lax.slice_in_dim(own_rows, 0, shard_block.shape[0], axis=1)
    time_term = jnp.zeros_like(state) + jnp.einsum(
        "nm,mvil->nvil", columns, shard_block, precision=lax.Precision.HIGHEST
    )
    padded = extended(state, (("cell", 2),), 2)
    codes_lines = jnp.repeat(face_codes, LINES_DEV, axis=1)
    lower_ghost = boundary_cells(state[:, :, 0:2, :], codes_lines[0], True)
    upper_ghost = boundary_cells(state[:, :, -2:, :], codes_lines[1], False)
    lower_rim = jnp.where(cell_index == 0, lower_ghost, padded[:, :, :2, :])
    upper_rim = jnp.where(cell_index == cell_count - 1, upper_ghost, padded[:, :, -2:, :])
    padded = jnp.concatenate([lower_rim, padded[:, :, 2:-2, :], upper_rim], axis=2)
    line_part, radius = line_residual(padded)
    prev_lines = (
        jnp.zeros_like(line_next).at[line_next].set(jnp.arange(line_next.shape[0], dtype=jnp.int32))
    )
    residual = line_part + pitch_residual(state, line_next, prev_lines) + time_term
    right_side = -residual
    centre_radius = radius[:, 2:-2, :]
    diagonal_term = pseudo_rate * centre_radius
    positions = cell_index * tile_cells + jnp.arange(-1, tile_cells + 1, dtype=jnp.int32)
    inside = (positions >= 0) & (positions < total_cells)
    radius_ext = jnp.where(inside[:, None], radius[:, 1:-1, :], 0.0)
    coefficients = line_coefficients(radius_ext, diagonal_term, positions[1:-1], total_cells)
    stacked = jnp.stack(coefficients, axis=1)
    line_source = lax.all_to_all(right_side, "cell", split_axis=3, concat_axis=2, tiled=True)
    line_coef = lax.all_to_all(stacked, "cell", split_axis=3, concat_axis=2, tiled=True)
    update = return_tiles(solve_in_lanes(tuple((line_coef[:, k] for k in range(5))), line_source))
    return state + update


LANES = 128
ROWS = 8
PAIRS = 3
CELL_ROWS = PAIRS * ROWS
RATE_ROW = 2 * CELL_ROWS
VMEM_BYTES = 8 * 2**20
BLOCK_ROWS = RATE_ROW + ROWS

MIDDLE_CELLS = 3
CORRECTION_ROW = 2 * CELL_ROWS
SIDE_ROWS = CORRECTION_ROW + 2 * ROWS


def spectral_offsets():
    table = np.zeros(NT)
    for offset in range(1, NT):
        angle = np.pi * offset / NT
        parity = -1.0 if offset % 2 == 0 else 1.0
        table[offset] = 0.5 * OMEGA_BLADE * parity * np.cos(angle) / np.sin(angle)
    return [float(np.float32(value)) for value in table]


def plane_masks():
    row_index = lax.broadcasted_iota(jnp.int32, (ROWS, LANES), 0)
    return row_index < 4, (row_index & 2) == 0, row_index & 1


def both(first_var, plane):
    turned = pltpu.roll(plane, 4, 0)
    return jnp.where(first_var, plane, turned), jnp.where(first_var, turned, plane)


def primitives(first_var, planes):
    density, moment_x = both(first_var, planes[0])
    moment_y, moment_z = both(first_var, planes[1])
    energy = jnp.where(first_var, planes[2], pltpu.roll(planes[2], 4, 0))
    inverse = 1.0 / density
    velocity_x = moment_x * inverse
    velocity_y = moment_y * inverse
    velocity_z = moment_z * inverse
    kinetic = moment_x * velocity_x + moment_y * velocity_y + moment_z * velocity_z
    pressure = (GAMMA_GAS - 1.0) * (energy - 0.5 * kinetic)
    sound = jnp.sqrt(GAMMA_GAS * pressure * inverse)
    return velocity_x, velocity_y, pressure, sound


def rows_of(var, inst, half):
    return (var // 2) * ROWS + (var % 2) * 4 + inst * 2 + half


def pack_kernel(
    held_state_ref, held_rate_ref, held_next_ref, held_codes_ref, out_ref, next_ref, codes_ref,
    state_ref, rate_ref, sems,
):
    copies = [
        pltpu.make_async_copy(source, target, sems.at[k])
        for k, (source, target) in enumerate(
            (
                (held_state_ref, state_ref),
                (held_rate_ref, rate_ref),
                (held_next_ref, next_ref),
                (held_codes_ref, codes_ref),
            )
        )
    ]
    for copy in copies:
        copy.start()
    for copy in copies:
        copy.wait()
    mirrored = lax.axis_index("cell") // (lax.axis_size("cell") // 2)
    for cell in range(2):
        place = pl.multiple_of(jnp.bitwise_xor(cell, mirrored) * CELL_ROWS, ROWS)
        for k in range(PAIRS):
            rows = [
                state_ref[inst, 2 * k + var, pl.ds(cell, 1), pl.ds(half * LANES, LANES)]
                for var in range(2)
                for inst in range(2)
                for half in range(2)
            ]
            for row, values in enumerate(rows):
                out_ref[0, pl.ds(place + (k * ROWS + row), 1), :] = values
    rates = [
        rate_ref[pl.ds(cell, 1), pl.ds(half * LANES, LANES)]
        for cell in range(2)
        for half in range(2)
    ]
    for row in range(4):
        out_ref[0, pl.ds(RATE_ROW + row, 1), :] = jnp.where(
            mirrored == 0, rates[row], rates[row ^ 2]
        )
    out_ref[0, pl.ds(RATE_ROW + 4, 4), :] = jnp.zeros((4, LANES), jnp.float32)
    for row in range(0, BLOCK_ROWS, ROWS):
        values = out_ref[0, pl.ds(row, ROWS), :]
        for copy in range(1, out_ref.shape[0]):
            out_ref[copy, pl.ds(row, ROWS), :] = values


def turn_insts(first_inst, plane):
    return jnp.where(first_inst, pltpu.roll(plane, 6, 0), pltpu.roll(plane, 2, 0))


def time_weights(first_inst, shift):
    offsets = spectral_offsets()
    other = jnp.where(
        first_inst, offsets[(2 * shift + 1) % NT], offsets[(2 * shift - 1) % NT]
    )
    return offsets[(2 * shift) % NT], other


def at_block(ref, y, block):
    blocks = ref.shape[1]
    mirrored = lax.axis_index("cell") // blocks
    place = mirrored * block + (1 - mirrored) * (blocks - 1 - block)
    return ref.at[ref.shape[0] - 1 - y, place]


def cell_plane(ref, y, cell, k):
    return at_block(ref, y, cell // 2)[pl.ds((cell % 2) * CELL_ROWS + k * ROWS, ROWS), :]


def partner_kernel(all_ref, out_ref):
    own_inst = lax.axis_index("inst")
    own_y, core = own_inst >> 1, own_inst & 1
    _, first_inst, _ = plane_masks()
    one, three = time_weights(first_inst, 1), time_weights(first_inst, 3)
    near = [jnp.where(core == 0, a, b) for a, b in zip(one, three)]
    away = [jnp.where(core == 0, b, a) for a, b in zip(one, three)]
    cells = 2 * all_ref.shape[1]
    for cell in range(cells):
        for k in range(PAIRS):
            here = cell_plane(all_ref, own_y, cell, k)
            there = cell_plane(all_ref, 1 - own_y, cell, k)
            out_ref[pl.ds(cell * CELL_ROWS + k * ROWS, ROWS), :] = (
                near[0] * here
                + away[0] * there
                + turn_insts(first_inst, near[1] * here + away[1] * there)
            )


def two_by_two(first, second):
    def entry(a, b, c, d):
        terms = [x * y for x, y in ((a, b), (c, d)) if x is not None and y is not None]
        return None if not terms else terms[0] if len(terms) == 1 else terms[0] + terms[1]

    return (
        entry(first[0], second[0], first[1], second[2]),
        entry(first[0], second[1], first[1], second[3]),
        entry(first[2], second[0], first[3], second[2]),
        entry(first[2], second[1], first[3], second[3]),
    )


def inverse_of(matrix):
    reciprocal = 1.0 / (matrix[0] * matrix[3] - matrix[1] * matrix[2])
    return (
        matrix[3] * reciprocal,
        -(matrix[1] * reciprocal),
        -(matrix[2] * reciprocal),
        matrix[0] * reciprocal,
    )


def less(first, second):
    return tuple(a if b is None else a - b for a, b in zip(first, second))


def minus(members):
    return tuple(None if a is None else -a for a in members)


def matrix_vector(matrix, low, high):
    def row(a, b):
        terms = [x * y for x, y in ((a, low), (b, high)) if x is not None]
        return terms[0] if len(terms) == 1 else terms[0] + terms[1]

    return row(matrix[0], matrix[1]), row(matrix[2], matrix[3])


def apply_matrix(matrix, side):
    parts = [matrix_vector(matrix, side[k], side[PAIRS + k]) for k in range(PAIRS)]
    return [low for low, _ in parts] + [high for _, high in parts]


def difference(first, second):
    return [a - b for a, b in zip(first, second)]


def flux_along(first_var, planes, velocity, pressure, sign):
    normal = sign * velocity
    return [
        planes[0] * normal + jnp.where(first_var, 0.0, sign * pressure),
        planes[1] * normal,
        planes[2] * normal + jnp.where(first_var, pressure * normal, 0.0),
    ]


class LineCells:
    def __init__(self, first_var, sign):
        self.first_var, self.sign = first_var, sign
        self.state, self.pressure, self.radius = {}, {}, {}
        self.flux, self.step, self.sensor = {}, {}, {}

    def add(self, cell, planes, velocity, pressure, sound):
        self.state[cell], self.pressure[cell] = planes, pressure
        self.radius[cell] = jnp.abs(velocity) + sound
        self.flux[cell] = flux_along(self.first_var, planes, velocity, pressure, self.sign)
        if cell - 1 in self.state:
            self.step[cell - 1] = difference(planes, self.state[cell - 1])
        if cell - 2 in self.state:
            twice = 2.0 * self.pressure[cell - 1]
            outer = pressure + self.pressure[cell - 2]
            self.sensor[cell - 1] = jnp.abs(outer - twice) / (outer + twice)

    def face(self, cell):
        second = SENSOR_GAIN * jnp.maximum(self.sensor[cell], self.sensor[cell + 1])
        fourth = jnp.maximum(0.0, FOURTH_GAIN - second)
        face_radius = 0.5 * (self.radius[cell] + self.radius[cell + 1])
        near_weight = face_radius * (second + 2.0 * fourth)
        far_weight = face_radius * fourth
        return [
            0.5 * (self.flux[cell][k] + self.flux[cell + 1][k])
            - (
                near_weight * self.step[cell][k]
                - far_weight * (self.step[cell + 1][k] + self.step[cell - 1][k])
            )
            for k in range(PAIRS)
        ]

    def near(self, cell):
        scale = SECOND_IMPL * 0.5 + 2.0 * FOURTH_IMPL
        return -scale * (self.radius[cell] + self.radius[cell + 1])

    def far(self, cell):
        return FOURTH_IMPL * self.radius[cell]

    def middle(self, cell, rate):
        centre, above = self.radius[cell], self.radius[cell + 1]
        if cell == 0:
            total, weighted = centre + (centre + above), 4.0 * centre + above
        else:
            below = self.radius[cell - 1]
            total = (below + centre) + (centre + above)
            weighted = below + 4.0 * centre + above
        result = SECOND_IMPL * (0.5 * total) + FOURTH_IMPL * weighted
        return result if rate is None else rate * centre + result

    def diagonal(self, cell, rates):
        across = self.near(cell)
        return (self.middle(cell, rates[0]), across, across, self.middle(cell + 1, rates[1]))

    def below(self, cell):
        return (self.far(cell - 1), self.near(cell - 1), None, self.far(cell))

    def above(self, cell):
        return (self.far(cell + 1), None, self.near(cell + 1), self.far(cell + 2))


def rates_at(ref, y, block, first_half):
    rows = [at_block(ref, y, block)[pl.ds(RATE_ROW + k, 1), :] for k in range(4)]
    return [jnp.where(first_half, rows[2 * k], rows[2 * k + 1]) for k in range(2)]


def near_half_kernel(all_ref, next_ref, codes_ref, *refs):
    *results, middle_ref, line_ref = refs
    own_y = lax.axis_index("inst") >> 1
    cells = 2 * all_ref.shape[1]
    for cell in range(cells - MIDDLE_CELLS, cells):
        for k in range(PAIRS):
            row = (cell - (cells - MIDDLE_CELLS)) * CELL_ROWS + k * ROWS
            middle_ref[pl.ds(row, ROWS), :] = cell_plane(all_ref, own_y, cell, k)

    @pl.when(lax.axis_index("cell") < all_ref.shape[1])
    def _():
        half_kernel(all_ref, next_ref, codes_ref, *results, line_ref)


def far_half_kernel(all_ref, next_ref, codes_ref, *refs):
    *refs, line_ref = refs
    given, results = refs[: len(refs) // 2], refs[len(refs) // 2 :]
    far = lax.axis_index("cell") >= all_ref.shape[1]

    @pl.when(far)
    def _():
        half_kernel(all_ref, next_ref, codes_ref, *results, line_ref)

    @pl.when(jnp.logical_not(far))
    def _():
        for source, target in zip(given, results):
            target[...] = source[...]


def half_kernel(
    all_ref, next_ref, codes_ref, partial_ref, factor_ref, blocks_ref, correction_ref,
    line_ref,
):
    own_y = lax.axis_index("inst") >> 1
    blocks = all_ref.shape[1]
    cells = 2 * blocks
    mirrored = lax.axis_index("cell") // blocks
    sign = (1 - 2 * mirrored).astype(jnp.float32)
    shape = (ROWS, LANES)
    lane_index = lax.broadcasted_iota(jnp.int32, shape, 1)
    first_var, first_inst, half_index = plane_masks()
    first_half = half_index == 0
    zero = jnp.zeros(shape, jnp.float32)

    next_rows = [
        next_ref[pl.ds(half * LANES, LANES)].reshape(1, LANES) for half in range(2)
    ]
    next_line = jnp.where(first_half, next_rows[0], next_rows[1])
    column = lax.broadcasted_iota(jnp.int32, (LANES, LANES), 0)
    prev_halves = []
    for target in range(2):
        total = None
        for source in range(2):
            hits = jnp.where(column + target * LANES == next_rows[source], 1.0, 0.0)
            names = (lane_index + source * LANES).astype(jnp.float32)
            part = lax.dot_general(
                names, hits, (((1,), (1,)), ((), ())), preferred_element_type=jnp.float32
            )
            total = part if total is None else total + part
        prev_halves.append(total)
    prev_line = jnp.where(first_half, prev_halves[0], prev_halves[1]).astype(jnp.int32)

    def picker(lines):
        lane = lines & (LANES - 1)
        same = (lines >> 7) == half_index

        def pick(plane):
            swapped = jnp.where(first_half, pltpu.roll(plane, 7, 0), pltpu.roll(plane, 1, 0))
            here = jnp.take_along_axis(plane, lane, axis=1, mode="promise_in_bounds")
            there = jnp.take_along_axis(swapped, lane, axis=1, mode="promise_in_bounds")
            return jnp.where(same, here, there)

        return pick

    pick_next = picker(next_line)
    pick_prev = picker(prev_line)

    def loaded(cell, y=own_y):
        return [cell_plane(all_ref, y, cell, k) for k in range(PAIRS)]

    own_weights, away_weights = time_weights(first_inst, 0), time_weights(first_inst, 2)

    def own_time_parts(planes, cell):
        return [
            away_weights[0] * away
            + turn_insts(first_inst, own_weights[1] * own + away_weights[1] * away)
            for own, away in zip(planes, loaded(cell, 1 - own_y))
        ]

    def flux_across(planes, velocity, pressure):
        return [
            planes[0] * velocity,
            planes[1] * velocity + jnp.where(first_var, pressure, 0.0),
            planes[2] * velocity + jnp.where(first_var, pressure * velocity, 0.0),
        ]

    def pitch_flux(planes, velocity_y, pressure, sound):
        nearby = [pick_next(plane) for plane in planes]
        _, next_velocity, next_pressure, next_sound = primitives(first_var, nearby)
        own_flux = flux_across(planes, velocity_y, pressure)
        next_flux = flux_across(nearby, next_velocity, next_pressure)
        weight = (PITCH_GAIN * 0.5) * (
            jnp.abs(velocity_y) + sound + (jnp.abs(next_velocity) + next_sound)
        )
        return [
            0.5 * (a + b) - weight * (n - o)
            for a, b, n, o in zip(own_flux, next_flux, nearby, planes)
        ]

    for cell in range(cells):
        planes = loaded(cell)
        velocity_x, velocity_y, pressure, sound = primitives(first_var, planes)
        line_ref[cell, 0], line_ref[cell, 1], line_ref[cell, 2] = velocity_x, pressure, sound
        faces_across = pitch_flux(planes, velocity_y, pressure, sound)
        times = own_time_parts(planes, cell)
        for k in range(PAIRS):
            partial_ref[cell, k] = -(times[k] + (faces_across[k] - pick_prev(faces_across[k])))

    tile = half_index * (LANES // LINES_DEV) + lane_index // LINES_DEV
    end_codes = jnp.where(mirrored == 0, codes_ref[pl.ds(0, 1), :], codes_ref[pl.ds(1, 1), :])
    codes = jnp.zeros(shape, jnp.int32)
    for k in range(2 * LANES // LINES_DEV):
        codes = jnp.where(tile == k, jnp.broadcast_to(end_codes[:, k : k + 1], shape), codes)

    def ghost(cell):
        planes = loaded(-1 - cell)
        copied = loaded(0)
        result = []
        for k in range(PAIRS):
            reflected = planes[k] if k else jnp.where(first_var, planes[k], -planes[k])
            inflow = jnp.where(first_var, FREE_STATE[2 * k], FREE_STATE[2 * k + 1])
            result.append(
                jnp.where(codes == 0, reflected, jnp.where(codes == 1, inflow, copied[k]))
            )
        return result

    line = LineCells(first_var, sign)
    faces, inverses, aboves = {}, [], []
    for cell in range(-2, cells):
        if cell < 0:
            planes = ghost(cell)
            velocity_x, _, pressure, sound = primitives(first_var, planes)
        else:
            planes = loaded(cell)
            velocity_x, pressure, sound = [line_ref[cell, k] for k in range(3)]
        line.add(cell, planes, velocity_x, pressure, sound)
        if cell >= 1:
            faces[cell - 2] = line.face(cell - 2)
        if cell >= 2:
            at = cell - 2
            for k in range(PAIRS):
                partial_ref[at, k] = partial_ref[at, k] + (faces[at - 1][k] - faces[at][k])
        if cell >= 3 and cell % 2 == 1:
            at = cell - 3
            block = at // 2
            rates = rates_at(all_ref, own_y, block, first_half)
            diag = line.diagonal(at, rates)
            if block > 0:
                factor = two_by_two(line.below(at), inverses[-1])
                diag = less(diag, two_by_two(factor, aboves[-1]))
                for n in range(4):
                    factor_ref[block - 1, n] = factor[n]
            inverses.append(inverse_of(diag))
            aboves.append(line.above(at))
            kept = [*inverses[-1], aboves[-1][0], *aboves[-1][2:]]
            for n, plane in enumerate(kept):
                blocks_ref[block, n] = plane

    last = cells - 2
    for k in range(PAIRS):
        partial_ref[last, k] = partial_ref[last, k] + faces[last - 1][k]
    factor = two_by_two(line.below(last), inverses[-1])
    for n in range(4):
        factor_ref[blocks - 2, n] = factor[n]
    correction = list(two_by_two(factor, aboves[-1]))
    rates = rates_at(all_ref, own_y, blocks - 1, first_half)
    for member in range(2):
        centre = line.radius[last + member]
        correction[3 * member] = correction[3 * member] - rates[member] * centre
    for n in range(2):
        correction_ref[pl.ds(n * ROWS, ROWS), :] = jnp.where(
            first_var, correction[2 * n], correction[2 * n + 1]
        )


def reduce_kernel(partial_ref, time_ref, factor_ref, correction_ref, middle_ref, sides_ref):
    for row in range(0, 2 * ROWS, ROWS):
        middle_ref[pl.ds(CORRECTION_ROW + row, ROWS), :] = correction_ref[pl.ds(row, ROWS), :]
    blocks = partial_ref.shape[0] // 2
    side = None
    for block in range(blocks):
        own = []
        for cell in (2 * block, 2 * block + 1):
            for k in range(PAIRS):
                time = time_ref[pl.ds(cell * CELL_ROWS + k * ROWS, ROWS), :]
                own.append(partial_ref[cell, k] - time)
        if block > 0:
            factor = [factor_ref[block - 1, n] for n in range(4)]
            own = difference(own, apply_matrix(factor, side))
        side = own
        for n, plane in enumerate(side):
            if block < blocks - 1:
                sides_ref[block, n] = plane
            else:
                middle_ref[pl.ds(n * ROWS, ROWS), :] = plane


def spread_kernel(all_ref, blocks_ref, sides_ref, known_ref, spread_ref, table_ref):
    own_y = lax.axis_index("inst") >> 1
    blocks = all_ref.shape[1]
    own_cell = lax.axis_index("cell")
    own_block = jnp.where(own_cell < blocks, own_cell, 2 * blocks - 1 - own_cell)
    zero = jnp.zeros((ROWS, LANES), jnp.float32)
    known, spread = [zero] * (2 * PAIRS), (zero + 1.0, zero, zero, zero + 1.0)
    for block in range(blocks - 1, -1, -1):
        if block < blocks - 1:
            kept = [blocks_ref[block, n] for n in range(7)]
            inverse, above = kept[:4], (kept[4], None, kept[5], kept[6])
            side = [sides_ref[block, n] for n in range(2 * PAIRS)]
            step = two_by_two(inverse, above)
            own = apply_matrix(inverse, side)
            if block < blocks - 2:
                known = difference(own, apply_matrix(step, known))
                spread = minus(two_by_two(step, spread))
            else:
                known, spread = own, minus(step)
        for n, plane in enumerate(known + list(spread)):
            table_ref[block, n] = plane
    for n in range(2 * PAIRS):
        base = at_block(all_ref, own_y, own_block)[pl.ds(n * ROWS, ROWS), :]
        known_ref[n] = base + table_ref[own_block, n]
    for n in range(4):
        spread_ref[n] = table_ref[own_block, 2 * PAIRS + n]


def plane_of(ref, row):
    return ref[pl.ds(row, ROWS), :]


def correction_of(first_var, ref):
    pairs = [both(first_var, plane_of(ref, CORRECTION_ROW + n * ROWS)) for n in range(2)]
    return [pairs[0][0], pairs[0][1], pairs[1][0], pairs[1][1]]


def middle_kernel(here_ref, there_ref, here_side_ref, side_ref, other_ref, matrix_ref):
    mirrored = lax.axis_index("cell") // (lax.axis_size("cell") // 2)
    sign = (1 - 2 * mirrored).astype(jnp.float32)
    first_var, _, _ = plane_masks()
    line = LineCells(first_var, sign)
    for cell in range(6):
        ref, at = (here_ref, cell) if cell < 3 else (there_ref, 5 - cell)
        planes = [plane_of(ref, at * CELL_ROWS + k * ROWS) for k in range(PAIRS)]
        velocity_x, _, pressure, sound = primitives(first_var, planes)
        line.add(cell, planes, velocity_x, pressure, sound)
    faces = {cell: line.face(cell) for cell in (1, 2, 3)}
    for k in range(PAIRS):
        side_ref[k] = plane_of(here_side_ref, k * ROWS) - faces[1][k]
        side_ref[PAIRS + k] = plane_of(here_side_ref, (PAIRS + k) * ROWS) + (
            faces[1][k] - faces[2][k]
        )
        other_ref[k] = faces[2][k] - faces[3][k]
        other_ref[PAIRS + k] = faces[3][k]
    no_rates = (None, None)
    diag = difference(line.diagonal(1, no_rates), correction_of(first_var, here_side_ref))
    above, below = line.above(1), line.below(3)
    kept = [*diag, *line.diagonal(3, no_rates), above[0], *above[2:], *below[:2], below[3]]
    for n, plane in enumerate(kept):
        matrix_ref[n] = plane


def join_kernel(
    side_ref, other_ref, matrix_ref, there_side_ref, known_ref, spread_ref, out_ref
):
    mirrored = lax.axis_index("cell") // (lax.axis_size("cell") // 2)
    first_var, _, _ = plane_masks()
    kept = [matrix_ref[n] for n in range(14)]
    diag, other_diag = kept[:4], kept[4:8]
    above, below = (kept[8], None, kept[9], kept[10]), (kept[11], kept[12], None, kept[13])
    other_diag = difference(other_diag, correction_of(first_var, there_side_ref)[::-1])
    other = []
    for member in range(2):
        for k in range(PAIRS):
            there = plane_of(there_side_ref, ((1 - member) * PAIRS + k) * ROWS)
            other.append(there + other_ref[member * PAIRS + k])
    factor = two_by_two(above, inverse_of(other_diag))
    diag = less(diag, two_by_two(factor, below))
    side = [side_ref[n] for n in range(2 * PAIRS)]
    middle = apply_matrix(inverse_of(diag), difference(side, apply_matrix(factor, other)))
    moved = apply_matrix([spread_ref[n] for n in range(4)], middle)
    results = [known_ref[n] + moved[n] for n in range(2 * PAIRS)]
    for cell in range(2):
        for k in range(PAIRS):
            first, second = results[cell * PAIRS + k], results[(1 - cell) * PAIRS + k]
            result = jnp.where(mirrored == 0, first, second)
            for var in range(2):
                for inst in range(2):
                    for half in range(2):
                        row = rows_of(var, inst, half)
                        out_ref[
                            inst, 2 * k + var, pl.ds(cell, 1), pl.ds(half * LANES, LANES)
                        ] = result[row : row + 1]


def share_half(copies):
    insts, count = lax.axis_size("inst"), lax.axis_size("cell")
    halves = [range(count // 2 - 1, -1, -1), range(count - 1, count // 2 - 1, -1)]
    groups = [
        [inst * count + cell for inst in range(insts - 2 + core, -1, -2) for cell in half]
        for core in range(2)
        for half in halves
    ]
    return lax.all_to_all(
        copies, ("inst", "cell"), split_axis=0, concat_axis=0, tiled=True,
        axis_index_groups=groups,
    )


def swap_cores(block):
    pairs = [(inst, inst ^ 1) for inst in range(lax.axis_size("inst"))]
    return lax.ppermute(block, "inst", pairs)


def swap_halves(block):
    count = lax.axis_size("cell")
    return lax.ppermute(block, "cell", [(i, (i + count // 2) % count) for i in range(count)])


def float_shape(*sizes):
    return jax.ShapeDtypeStruct(sizes, jnp.float32)


def local_by_halves(state, pseudo_rate, line_next, face_codes):
    blocks = lax.axis_size("cell") // 2
    cells = 2 * blocks
    vmem = pl.BlockSpec(memory_space=pltpu.VMEM)
    plane = (ROWS, LANES)
    params = pltpu.CompilerParams(vmem_limit_bytes=VMEM_BYTES)
    places = lax.axis_size("inst") // 2
    held = [
        pltpu.with_memory_space_constraint(array, pltpu.HBM)
        for array in (state, pseudo_rate, line_next, face_codes)
    ]
    packed, next_here, codes_here = pl.pallas_call(
        pack_kernel,
        out_shape=(
            float_shape(places * blocks, BLOCK_ROWS, LANES),
            jax.ShapeDtypeStruct(line_next.shape, jnp.int32),
            jax.ShapeDtypeStruct(face_codes.shape, jnp.int32),
        ),
        in_specs=[pl.BlockSpec(memory_space=pltpu.HBM)] * 4,
        out_specs=(vmem, vmem, vmem),
        scratch_shapes=[
            pltpu.VMEM(state.shape, jnp.float32),
            pltpu.VMEM(pseudo_rate.shape, jnp.float32),
            pltpu.SemaphoreType.DMA((4,)),
        ],
        compiler_params=params,
    )(*held)
    shared = share_half(packed).reshape(places, blocks, BLOCK_ROWS, LANES)
    for_partner = pl.pallas_call(
        partner_kernel,
        out_shape=float_shape(cells * CELL_ROWS, LANES),
        in_specs=[vmem],
        out_specs=vmem,
        compiler_params=params,
    )(shared)
    from_partner = swap_cores(for_partner)
    beside = pl.CostEstimate(flops=10**6, bytes_accessed=10**6, transcendentals=0)
    kinds = (
        float_shape(cells, PAIRS, *plane),
        float_shape(blocks - 1, 4, *plane),
        float_shape(blocks - 1, 7, *plane),
        float_shape(2 * ROWS, LANES),
    )
    line_scratch = [pltpu.VMEM((cells, 3) + plane, jnp.float32)]
    arguments = (shared, next_here, codes_here)
    *near, here = pl.pallas_call(
        near_half_kernel,
        out_shape=kinds + (float_shape(MIDDLE_CELLS * CELL_ROWS, LANES),),
        in_specs=[vmem] * 3,
        out_specs=(vmem,) * 5,
        scratch_shapes=line_scratch,
        compiler_params=params,
    )(*arguments)
    there = swap_halves(here)
    partial, factors, eliminated, correction = pl.pallas_call(
        far_half_kernel,
        out_shape=kinds,
        in_specs=[vmem] * 7,
        out_specs=(vmem,) * 4,
        scratch_shapes=line_scratch,
        input_output_aliases={3 + n: n for n in range(4)},
        compiler_params=params,
        cost_estimate=beside,
    )(*arguments, *near)
    here_side, sides = pl.pallas_call(
        reduce_kernel,
        out_shape=(
            float_shape(SIDE_ROWS, LANES),
            float_shape(blocks - 1, 2 * PAIRS, *plane),
        ),
        in_specs=[vmem] * 4,
        out_specs=(vmem, vmem),
        compiler_params=params,
    )(partial, from_partner, factors, correction)
    there_side = swap_halves(here_side)
    known, spread = pl.pallas_call(
        spread_kernel,
        out_shape=(float_shape(2 * PAIRS, *plane), float_shape(4, *plane)),
        in_specs=[vmem] * 3,
        out_specs=(vmem, vmem),
        scratch_shapes=[pltpu.VMEM((blocks, 2 * PAIRS + 4) + plane, jnp.float32)],
        compiler_params=params,
        cost_estimate=beside,
    )(shared, eliminated, sides)
    side, other, matrices = pl.pallas_call(
        middle_kernel,
        out_shape=(
            float_shape(2 * PAIRS, *plane),
            float_shape(2 * PAIRS, *plane),
            float_shape(14, *plane),
        ),
        in_specs=[vmem] * 3,
        out_specs=(vmem,) * 3,
        compiler_params=params,
        cost_estimate=beside,
    )(here, there, here_side)
    return pl.pallas_call(
        join_kernel,
        out_shape=float_shape(*state.shape),
        in_specs=[vmem] * 6,
        out_specs=vmem,
        compiler_params=params,
    )(side, other, matrices, there_side, known, spread)


def solution(mesh):
    placed = (P("inst", None, "cell", None), P("cell", None), P(), P())
    inst_count, cell_count = mesh.shape["inst"], mesh.shape["cell"]

    def local(state, pseudo_rate, line_next, face_codes):
        small = (
            state.shape == (2, 6, 2, 2 * LANES)
            and inst_count * 2 == NT
            and cell_count == 8
            and face_codes.shape[1] * LINES_DEV == state.shape[3]
        )
        chosen = local_by_halves if small else local_by_lines
        return chosen(state, pseudo_rate, line_next, face_codes)

    return jax.shard_map(
        local, mesh=mesh, in_specs=placed, out_specs=P("inst", None, "cell", None), check_vma=False
    )
```

```python
import functools

import jax
import jax.numpy as jnp
import numpy as np
from jax import lax
from jax.experimental import pallas as pl
from jax.experimental.pallas import tpu as pltpu
from jax.sharding import PartitionSpec as P

NT = 8
LINES_DEV = 32


GAMMA_GAS = 1.4
OMEGA_BLADE = 1.0
SENSOR_GAIN = 0.25
FOURTH_GAIN = 0.03125
PITCH_GAIN = 0.5
SECOND_IMPL = 1.0
FOURTH_IMPL = 0.25
FREE_STATE = (1.0, 0.5, 0.0, 0.0, 2.625, 0.2)
MIRROR_SIGNS = (1.0, -1.0, 1.0, 1.0, 1.0, 1.0)
ZERO_BLOCK = (0.0, 0.0, 0.0, 0.0)
UNIT_BLOCK = (1.0, 0.0, 0.0, 1.0)
ZERO_PAIR = (0.0, 0.0)


def extended(block, sides, width):
    for axis, dim in sides:
        count = lax.axis_size(axis)
        forward = [(i, i + 1) for i in range(count - 1)]
        backward = [(target, source) for source, target in forward]
        low = lax.ppermute(
            lax.slice_in_dim(block, block.shape[dim] - width, None, axis=dim), axis, forward
        )
        high = lax.ppermute(lax.slice_in_dim(block, 0, width, axis=dim), axis, backward)
        block = jnp.concatenate([low, block, high], axis=dim)
    return block


def spectral_matrix(instances):
    offsets = np.arange(instances)[:, None] - np.arange(instances)[None, :]
    angles = np.pi * offsets / instances
    safe_sin = np.where(offsets == 0, 1.0, np.sin(angles))
    parity = np.where(np.mod(offsets, 2) == 0, -1.0, 1.0)
    matrix_table = np.where(
        offsets == 0, 0.0, 0.5 * OMEGA_BLADE * parity * np.cos(angles) / safe_sin
    )
    return jnp.asarray(matrix_table, jnp.float32)


def primitive_parts(cells_state):
    density = cells_state[..., 0, :, :]
    inverse = 1.0 / density
    velocity_x = cells_state[..., 1, :, :] * inverse
    velocity_y = cells_state[..., 2, :, :] * inverse
    velocity_z = cells_state[..., 3, :, :] * inverse
    energy = cells_state[..., 4, :, :]
    pressure = (GAMMA_GAS - 1.0) * (
        energy
        - 0.5
        * density
        * (velocity_x * velocity_x + velocity_y * velocity_y + velocity_z * velocity_z)
    )
    sound_speed = jnp.sqrt(GAMMA_GAS * pressure * inverse)
    return (velocity_x, velocity_y, pressure, sound_speed)


def directed_flux(cells_state, normal_velocity, pressure, component):
    zero_plane = jnp.zeros_like(pressure)
    pressure_rows = [
        zero_plane,
        zero_plane,
        zero_plane,
        zero_plane,
        pressure * normal_velocity,
        zero_plane,
    ]
    pressure_rows[component] = pressure
    return cells_state * normal_velocity[..., None, :, :] + jnp.stack(pressure_rows, axis=-3)


def line_residual(padded):
    velocity_x, velocity_y, pressure, sound_speed = primitive_parts(padded)
    flux_line = directed_flux(padded, velocity_x, pressure, 1)
    radius = jnp.abs(velocity_x) + sound_speed
    sensor = jnp.abs(
        pressure[..., 2:, :] - 2.0 * pressure[..., 1:-1, :] + pressure[..., :-2, :]
    ) / (pressure[..., 2:, :] + 2.0 * pressure[..., 1:-1, :] + pressure[..., :-2, :])
    second = SENSOR_GAIN * jnp.maximum(sensor[..., :-1, :], sensor[..., 1:, :])
    fourth = jnp.maximum(0.0, FOURTH_GAIN - second)
    face_radius = 0.5 * (radius[..., 1:-2, :] + radius[..., 2:-1, :])
    left_far = padded[..., :-3, :]
    left_near = padded[..., 1:-2, :]
    right_near = padded[..., 2:-1, :]
    right_far = padded[..., 3:, :]
    damping = face_radius[..., None, :, :] * (
        second[..., None, :, :] * (right_near - left_near)
        - fourth[..., None, :, :] * (right_far - 3.0 * right_near + 3.0 * left_near - left_far)
    )
    face_flux = 0.5 * (flux_line[..., 1:-2, :] + flux_line[..., 2:-1, :]) - damping
    return (face_flux[..., 1:, :] - face_flux[..., :-1, :], radius)


def pitch_parts(cells_state):
    velocity_x, velocity_y, pressure, sound_speed = primitive_parts(cells_state)
    return (directed_flux(cells_state, velocity_y, pressure, 2), jnp.abs(velocity_y) + sound_speed)


def pitch_residual(cells_state, next_lines, prev_lines):
    pitch_flux, radius = pitch_parts(cells_state)
    state_next = jnp.take(cells_state, next_lines, axis=-1)
    flux_next, radius_next = pitch_parts(state_next)
    face_flux = 0.5 * (pitch_flux + flux_next) - PITCH_GAIN * (0.5 * (radius + radius_next))[
        ..., None, :, :
    ] * (state_next - cells_state)
    return face_flux - jnp.take(face_flux, prev_lines, axis=-1)


def boundary_cells(edge_pair, line_codes, lower_end):
    reflected = edge_pair[..., ::-1, :] * jnp.asarray(MIRROR_SIGNS, jnp.float32)[:, None, None]
    if lower_end:
        copied = jnp.concatenate([edge_pair[..., :1, :], edge_pair[..., :1, :]], axis=-2)
    else:
        copied = jnp.concatenate([edge_pair[..., 1:, :], edge_pair[..., 1:, :]], axis=-2)
    inflow = jnp.asarray(FREE_STATE, jnp.float32)[:, None, None] + jnp.zeros_like(edge_pair)
    return jnp.where(line_codes == 0, reflected, jnp.where(line_codes == 1, inflow, copied))


def line_coefficients(radius_ext, diagonal_term, positions, total_cells):
    radius_below = radius_ext[..., :-2, :]
    radius_centre = radius_ext[..., 1:-1, :]
    radius_above = radius_ext[..., 2:, :]
    face_below = 0.5 * (radius_below + radius_centre)
    face_above = 0.5 * (radius_centre + radius_above)
    far_low = FOURTH_IMPL * radius_below
    near_low = -SECOND_IMPL * face_below - 2.0 * FOURTH_IMPL * (radius_below + radius_centre)
    middle = (
        diagonal_term
        + SECOND_IMPL * (face_below + face_above)
        + FOURTH_IMPL * (radius_below + 4.0 * radius_centre + radius_above)
    )
    near_high = -SECOND_IMPL * face_above - 2.0 * FOURTH_IMPL * (radius_centre + radius_above)
    far_high = FOURTH_IMPL * radius_above
    column = positions[:, None]
    far_low = jnp.where(column >= 2, far_low, 0.0)
    near_low = jnp.where(column >= 1, near_low, 0.0)
    near_high = jnp.where(column <= total_cells - 2, near_high, 0.0)
    far_high = jnp.where(column <= total_cells - 3, far_high, 0.0)
    return (far_low, near_low, middle, near_high, far_high)


def block_product(first_matrix, second_matrix):
    return (
        first_matrix[0] * second_matrix[0] + first_matrix[1] * second_matrix[2],
        first_matrix[0] * second_matrix[1] + first_matrix[1] * second_matrix[3],
        first_matrix[2] * second_matrix[0] + first_matrix[3] * second_matrix[2],
        first_matrix[2] * second_matrix[1] + first_matrix[3] * second_matrix[3],
    )


def block_inverse(matrix):
    determinant = matrix[0] * matrix[3] - matrix[1] * matrix[2]
    reciprocal = 1.0 / determinant
    return (
        matrix[3] * reciprocal,
        -matrix[1] * reciprocal,
        -matrix[2] * reciprocal,
        matrix[0] * reciprocal,
    )


def block_apply(matrix, vector):
    return (
        matrix[0] * vector[0] + matrix[1] * vector[1],
        matrix[2] * vector[0] + matrix[3] * vector[1],
    )


def add_blocks(first_members, second_members):
    return tuple((a + b for a, b in zip(first_members, second_members)))


def negate(members):
    return tuple((-a for a in members))


def extend_blocks(members, fill_values):
    return tuple(
        (
            jnp.concatenate([m, jnp.full_like(m[..., :1, :], f)], axis=-2)
            for m, f in zip(members, fill_values)
        )
    )


def shift_next(members, fill_values):
    return tuple(
        (
            jnp.concatenate([m[..., 1:, :], jnp.full_like(m[..., :1, :], f)], axis=-2)
            for m, f in zip(members, fill_values)
        )
    )


def shift_prev(members):
    return tuple(
        (jnp.concatenate([jnp.zeros_like(m[..., :1, :]), m[..., :-1, :]], axis=-2) for m in members)
    )


def pair_split(member):
    shaped = member.reshape(member.shape[:-2] + (member.shape[-2] // 2, 2, member.shape[-1]))
    return (shaped[..., 0, :], shaped[..., 1, :])


def split_parity(members):
    halves = [pair_split(m) for m in members]
    return (tuple((h[0] for h in halves)), tuple((h[1] for h in halves)))


def alternate(first_member, second_member):
    stacked = jnp.stack((first_member, second_member), axis=-2)
    return stacked.reshape(
        first_member.shape[:-2] + (2 * first_member.shape[-2], first_member.shape[-1])
    )


def reduce_blocks(sub_blocks, diag_blocks, super_blocks, right_side):
    block_count = diag_blocks[0].shape[-2]
    if block_count == 1:
        return block_apply(block_inverse(diag_blocks), right_side)
    if block_count % 2 == 1:
        sub_blocks = extend_blocks(sub_blocks, ZERO_BLOCK)
        diag_blocks = extend_blocks(diag_blocks, UNIT_BLOCK)
        super_blocks = extend_blocks(super_blocks, ZERO_BLOCK)
        right_side = extend_blocks(right_side, ZERO_PAIR)
    sub_even, sub_odd = split_parity(sub_blocks)
    diag_even, diag_odd = split_parity(diag_blocks)
    super_even, super_odd = split_parity(super_blocks)
    side_even, side_odd = split_parity(right_side)
    inverse_even = block_inverse(diag_even)
    inverse_next = shift_next(inverse_even, UNIT_BLOCK)
    sub_next = shift_next(sub_even, ZERO_BLOCK)
    super_next = shift_next(super_even, ZERO_BLOCK)
    side_next = shift_next(side_even, ZERO_PAIR)
    left_factor = negate(block_product(sub_odd, inverse_even))
    right_factor = negate(block_product(super_odd, inverse_next))
    reduced_sub = block_product(left_factor, sub_even)
    reduced_diag = add_blocks(
        diag_odd,
        add_blocks(block_product(left_factor, super_even), block_product(right_factor, sub_next)),
    )
    reduced_super = block_product(right_factor, super_next)
    reduced_side = add_blocks(
        side_odd,
        add_blocks(block_apply(left_factor, side_even), block_apply(right_factor, side_next)),
    )
    odd_values = reduce_blocks(reduced_sub, reduced_diag, reduced_super, reduced_side)
    before_values = shift_prev(odd_values)
    remainder = add_blocks(
        side_even,
        negate(
            add_blocks(block_apply(sub_even, before_values), block_apply(super_even, odd_values))
        ),
    )
    even_values = block_apply(inverse_even, remainder)
    merged = tuple((alternate(e, o) for e, o in zip(even_values, odd_values)))
    return tuple((m[..., :block_count, :] for m in merged))


def cells_leading(block):
    moved = jnp.transpose(block, (2, 0, 1, 3))
    return moved.reshape(block.shape[2], block.shape[0] * block.shape[1] * block.shape[3])


def solve_in_lanes(coefficients, line_source):
    source_shape = line_source.shape
    lane_coef = [cells_leading(jnp.broadcast_to(c[:, None], source_shape)) for c in coefficients]
    pairs_list = [pair_split(m) for m in lane_coef]
    zero_plane = jnp.zeros_like(pairs_list[2][0])
    sub_blocks = (pairs_list[0][0], pairs_list[1][0], zero_plane, pairs_list[0][1])
    diag_blocks = (pairs_list[2][0], pairs_list[3][0], pairs_list[1][1], pairs_list[2][1])
    super_blocks = (pairs_list[4][0], zero_plane, pairs_list[3][1], pairs_list[4][1])
    values = reduce_blocks(
        sub_blocks, diag_blocks, super_blocks, pair_split(cells_leading(line_source))
    )
    flat = alternate(values[0], values[1])
    shaped = flat.reshape(source_shape[2], source_shape[0], source_shape[1], source_shape[3])
    return jnp.transpose(shaped, (1, 2, 0, 3))


def return_tiles(line_values):
    return lax.all_to_all(line_values, "cell", split_axis=2, concat_axis=3, tiled=True)


def local_by_lines(state, pseudo_rate, line_next, face_codes):
    local_count = state.shape[0]
    tile_cells = state.shape[2]
    cell_index = lax.axis_index("cell")
    cell_count = lax.axis_size("cell")
    total_cells = tile_cells * cell_count
    spectral = spectral_matrix(NT)
    first_local = lax.axis_index("inst") * local_count
    own_rows = lax.dynamic_slice_in_dim(spectral, first_local, local_count, 0)
    shard_block = jax.tree.map(lambda a: lax.all_gather(a, "inst", axis=0, tiled=True), state)
    columns = lax.slice_in_dim(own_rows, 0, shard_block.shape[0], axis=1)
    time_term = jnp.zeros_like(state) + jnp.einsum(
        "nm,mvil->nvil", columns, shard_block, precision=lax.Precision.HIGHEST
    )
    padded = extended(state, (("cell", 2),), 2)
    codes_lines = jnp.repeat(face_codes, LINES_DEV, axis=1)
    lower_ghost = boundary_cells(state[:, :, 0:2, :], codes_lines[0], True)
    upper_ghost = boundary_cells(state[:, :, -2:, :], codes_lines[1], False)
    lower_rim = jnp.where(cell_index == 0, lower_ghost, padded[:, :, :2, :])
    upper_rim = jnp.where(cell_index == cell_count - 1, upper_ghost, padded[:, :, -2:, :])
    padded = jnp.concatenate([lower_rim, padded[:, :, 2:-2, :], upper_rim], axis=2)
    line_part, radius = line_residual(padded)
    prev_lines = (
        jnp.zeros_like(line_next).at[line_next].set(jnp.arange(line_next.shape[0], dtype=jnp.int32))
    )
    residual = line_part + pitch_residual(state, line_next, prev_lines) + time_term
    right_side = -residual
    centre_radius = radius[:, 2:-2, :]
    diagonal_term = pseudo_rate * centre_radius
    positions = cell_index * tile_cells + jnp.arange(-1, tile_cells + 1, dtype=jnp.int32)
    inside = (positions >= 0) & (positions < total_cells)
    radius_ext = jnp.where(inside[:, None], radius[:, 1:-1, :], 0.0)
    coefficients = line_coefficients(radius_ext, diagonal_term, positions[1:-1], total_cells)
    stacked = jnp.stack(coefficients, axis=1)
    line_source = lax.all_to_all(right_side, "cell", split_axis=3, concat_axis=2, tiled=True)
    line_coef = lax.all_to_all(stacked, "cell", split_axis=3, concat_axis=2, tiled=True)
    update = return_tiles(solve_in_lanes(tuple((line_coef[:, k] for k in range(5))), line_source))
    return state + update


LANES = 128
ROWS = 8
PAIRS = 3
CELL_ROWS = PAIRS * ROWS
RATE_ROW = 2 * CELL_ROWS
VMEM_BYTES = 8 * 2**20
BLOCK_ROWS = RATE_ROW + ROWS

MIDDLE_CELLS = 3
CORRECTION_ROW = 2 * CELL_ROWS
SIDE_ROWS = CORRECTION_ROW + 2 * ROWS


def spectral_offsets():
    table = np.zeros(NT)
    for offset in range(1, NT):
        angle = np.pi * offset / NT
        parity = -1.0 if offset % 2 == 0 else 1.0
        table[offset] = 0.5 * OMEGA_BLADE * parity * np.cos(angle) / np.sin(angle)
    return [float(np.float32(value)) for value in table]


def plane_masks():
    row_index = lax.broadcasted_iota(jnp.int32, (ROWS, LANES), 0)
    return row_index < 4, (row_index & 2) == 0, row_index & 1


def both(first_var, plane):
    turned = pltpu.roll(plane, 4, 0)
    return jnp.where(first_var, plane, turned), jnp.where(first_var, turned, plane)


def primitives(first_var, planes):
    density, moment_x = both(first_var, planes[0])
    moment_y, moment_z = both(first_var, planes[1])
    energy = jnp.where(first_var, planes[2], pltpu.roll(planes[2], 4, 0))
    inverse = 1.0 / density
    velocity_x = moment_x * inverse
    velocity_y = moment_y * inverse
    velocity_z = moment_z * inverse
    kinetic = moment_x * velocity_x + moment_y * velocity_y + moment_z * velocity_z
    pressure = (GAMMA_GAS - 1.0) * (energy - 0.5 * kinetic)
    sound = jnp.sqrt(GAMMA_GAS * pressure * inverse)
    return velocity_x, velocity_y, pressure, sound


def rows_of(var, inst, half):
    return (var // 2) * ROWS + (var % 2) * 4 + inst * 2 + half


def pack_kernel(
    held_state_ref, held_rate_ref, held_next_ref, held_codes_ref, out_ref, next_ref, codes_ref,
    state_ref, rate_ref, sems,
):
    copies = [
        pltpu.make_async_copy(source, target, sems.at[k])
        for k, (source, target) in enumerate(
            (
                (held_state_ref, state_ref),
                (held_rate_ref, rate_ref),
                (held_next_ref, next_ref),
                (held_codes_ref, codes_ref),
            )
        )
    ]
    for copy in copies:
        copy.start()
    for copy in copies:
        copy.wait()
    mirrored = lax.axis_index("cell") // (lax.axis_size("cell") // 2)
    for cell in range(2):
        place = pl.multiple_of(jnp.bitwise_xor(cell, mirrored) * CELL_ROWS, ROWS)
        for k in range(PAIRS):
            rows = [
                state_ref[inst, 2 * k + var, pl.ds(cell, 1), pl.ds(half * LANES, LANES)]
                for var in range(2)
                for inst in range(2)
                for half in range(2)
            ]
            for row, values in enumerate(rows):
                out_ref[0, pl.ds(place + (k * ROWS + row), 1), :] = values
    rates = [
        rate_ref[pl.ds(cell, 1), pl.ds(half * LANES, LANES)]
        for cell in range(2)
        for half in range(2)
    ]
    for row in range(4):
        out_ref[0, pl.ds(RATE_ROW + row, 1), :] = jnp.where(
            mirrored == 0, rates[row], rates[row ^ 2]
        )
    out_ref[0, pl.ds(RATE_ROW + 4, 4), :] = jnp.zeros((4, LANES), jnp.float32)
    for row in range(0, BLOCK_ROWS, ROWS):
        values = out_ref[0, pl.ds(row, ROWS), :]
        for copy in range(1, out_ref.shape[0]):
            out_ref[copy, pl.ds(row, ROWS), :] = values


def turn_insts(first_inst, plane):
    return jnp.where(first_inst, pltpu.roll(plane, 6, 0), pltpu.roll(plane, 2, 0))


def time_weights(first_inst, shift):
    offsets = spectral_offsets()
    other = jnp.where(
        first_inst, offsets[(2 * shift + 1) % NT], offsets[(2 * shift - 1) % NT]
    )
    return offsets[(2 * shift) % NT], other


def select_weights(core, first_inst, first_shift, second_shift):
    first, second = time_weights(first_inst, first_shift), time_weights(first_inst, second_shift)
    return [jnp.where(core == 0, a, b) for a, b in zip(first, second)]


def at_block(ref, core, block):
    blocks = ref.shape[1]
    mirrored = lax.axis_index("cell") // blocks
    place = mirrored * block + (1 - mirrored) * (blocks - 1 - block)
    return ref.at[ref.shape[0] - 1 - core, place]


def cell_plane(ref, core, cell, k):
    return at_block(ref, core, cell // 2)[pl.ds((cell % 2) * CELL_ROWS + k * ROWS, ROWS), :]


def partner_kernel(all_ref, out_ref):
    core = lax.axis_index("inst") & 1
    _, first_inst, _ = plane_masks()
    own_weights = time_weights(first_inst, 2)
    other_weights = select_weights(core, first_inst, 1, 3)
    cells = 2 * all_ref.shape[1]
    for cell in range(cells):
        for k in range(PAIRS):
            own = cell_plane(all_ref, core, cell, k)
            other = cell_plane(all_ref, 1 - core, cell, k)
            out_ref[pl.ds(cell * CELL_ROWS + k * ROWS, ROWS), :] = (
                own_weights[0] * own
                + other_weights[0] * other
                + turn_insts(first_inst, own_weights[1] * own + other_weights[1] * other)
            )


def two_by_two(first, second):
    def entry(a, b, c, d):
        terms = [x * y for x, y in ((a, b), (c, d)) if x is not None and y is not None]
        return None if not terms else terms[0] if len(terms) == 1 else terms[0] + terms[1]

    return (
        entry(first[0], second[0], first[1], second[2]),
        entry(first[0], second[1], first[1], second[3]),
        entry(first[2], second[0], first[3], second[2]),
        entry(first[2], second[1], first[3], second[3]),
    )


def inverse_of(matrix):
    reciprocal = 1.0 / (matrix[0] * matrix[3] - matrix[1] * matrix[2])
    return (
        matrix[3] * reciprocal,
        -(matrix[1] * reciprocal),
        -(matrix[2] * reciprocal),
        matrix[0] * reciprocal,
    )


def less(first, second):
    return tuple(a if b is None else a - b for a, b in zip(first, second))


def minus(members):
    return tuple(None if a is None else -a for a in members)


def matrix_vector(matrix, low, high):
    def row(a, b):
        terms = [x * y for x, y in ((a, low), (b, high)) if x is not None]
        return terms[0] if len(terms) == 1 else terms[0] + terms[1]

    return row(matrix[0], matrix[1]), row(matrix[2], matrix[3])


def apply_matrix(matrix, side):
    parts = [matrix_vector(matrix, side[k], side[PAIRS + k]) for k in range(PAIRS)]
    return [low for low, _ in parts] + [high for _, high in parts]


def difference(first, second):
    return [a - b for a, b in zip(first, second)]


def flux_along(first_var, planes, velocity, pressure, sign):
    normal = sign * velocity
    return [
        planes[0] * normal + jnp.where(first_var, 0.0, sign * pressure),
        planes[1] * normal,
        planes[2] * normal + jnp.where(first_var, pressure * normal, 0.0),
    ]


class LineCells:
    def __init__(self, first_var, sign):
        self.first_var, self.sign = first_var, sign
        self.state, self.pressure, self.radius = {}, {}, {}
        self.flux, self.step, self.sensor = {}, {}, {}

    def add(self, cell, planes, velocity, pressure, sound):
        self.state[cell], self.pressure[cell] = planes, pressure
        self.radius[cell] = jnp.abs(velocity) + sound
        self.flux[cell] = flux_along(self.first_var, planes, velocity, pressure, self.sign)
        if cell - 1 in self.state:
            self.step[cell - 1] = difference(planes, self.state[cell - 1])
        if cell - 2 in self.state:
            twice = 2.0 * self.pressure[cell - 1]
            outer = pressure + self.pressure[cell - 2]
            self.sensor[cell - 1] = jnp.abs(outer - twice) / (outer + twice)

    def face(self, cell):
        second = SENSOR_GAIN * jnp.maximum(self.sensor[cell], self.sensor[cell + 1])
        fourth = jnp.maximum(0.0, FOURTH_GAIN - second)
        face_radius = 0.5 * (self.radius[cell] + self.radius[cell + 1])
        near_weight = face_radius * (second + 2.0 * fourth)
        far_weight = face_radius * fourth
        return [
            0.5 * (self.flux[cell][k] + self.flux[cell + 1][k])
            - (
                near_weight * self.step[cell][k]
                - far_weight * (self.step[cell + 1][k] + self.step[cell - 1][k])
            )
            for k in range(PAIRS)
        ]

    def near(self, cell):
        scale = SECOND_IMPL * 0.5 + 2.0 * FOURTH_IMPL
        return -scale * (self.radius[cell] + self.radius[cell + 1])

    def far(self, cell):
        return FOURTH_IMPL * self.radius[cell]

    def middle(self, cell, rate):
        centre, above = self.radius[cell], self.radius[cell + 1]
        if cell == 0:
            total, weighted = centre + (centre + above), 4.0 * centre + above
        else:
            below = self.radius[cell - 1]
            total = (below + centre) + (centre + above)
            weighted = below + 4.0 * centre + above
        result = SECOND_IMPL * (0.5 * total) + FOURTH_IMPL * weighted
        return result if rate is None else rate * centre + result

    def diagonal(self, cell, rates):
        across = self.near(cell)
        return (self.middle(cell, rates[0]), across, across, self.middle(cell + 1, rates[1]))

    def below(self, cell):
        return (self.far(cell - 1), self.near(cell - 1), None, self.far(cell))

    def above(self, cell):
        return (self.far(cell + 1), None, self.near(cell + 1), self.far(cell + 2))


def rates_at(ref, core, block, first_half):
    rows = [at_block(ref, core, block)[pl.ds(RATE_ROW + k, 1), :] for k in range(4)]
    return [jnp.where(first_half, rows[2 * k], rows[2 * k + 1]) for k in range(2)]


def near_half_kernel(all_ref, next_ref, codes_ref, *refs):
    *results, middle_ref, line_ref = refs
    core = lax.axis_index("inst") & 1
    cells = 2 * all_ref.shape[1]
    for cell in range(cells - MIDDLE_CELLS, cells):
        for k in range(PAIRS):
            row = (cell - (cells - MIDDLE_CELLS)) * CELL_ROWS + k * ROWS
            middle_ref[pl.ds(row, ROWS), :] = cell_plane(all_ref, core, cell, k)

    @pl.when(lax.axis_index("cell") < all_ref.shape[1])
    def _():
        half_kernel(all_ref, next_ref, codes_ref, *results, line_ref)


def far_half_kernel(all_ref, next_ref, codes_ref, *refs):
    *refs, line_ref = refs
    given, results = refs[: len(refs) // 2], refs[len(refs) // 2 :]
    far = lax.axis_index("cell") >= all_ref.shape[1]

    @pl.when(far)
    def _():
        half_kernel(all_ref, next_ref, codes_ref, *results, line_ref)

    @pl.when(jnp.logical_not(far))
    def _():
        for source, target in zip(given, results):
            target[...] = source[...]


def half_kernel(
    all_ref, next_ref, codes_ref, partial_ref, factor_ref, blocks_ref, correction_ref,
    line_ref,
):
    core = lax.axis_index("inst") & 1
    blocks = all_ref.shape[1]
    cells = 2 * blocks
    mirrored = lax.axis_index("cell") // blocks
    sign = (1 - 2 * mirrored).astype(jnp.float32)
    shape = (ROWS, LANES)
    lane_index = lax.broadcasted_iota(jnp.int32, shape, 1)
    first_var, first_inst, half_index = plane_masks()
    first_half = half_index == 0
    zero = jnp.zeros(shape, jnp.float32)

    next_rows = [
        next_ref[pl.ds(half * LANES, LANES)].reshape(1, LANES) for half in range(2)
    ]
    next_line = jnp.where(first_half, next_rows[0], next_rows[1])
    column = lax.broadcasted_iota(jnp.int32, (LANES, LANES), 0)
    prev_halves = []
    for target in range(2):
        total = None
        for source in range(2):
            hits = jnp.where(column + target * LANES == next_rows[source], 1.0, 0.0)
            names = (lane_index + source * LANES).astype(jnp.float32)
            part = lax.dot_general(
                names, hits, (((1,), (1,)), ((), ())), preferred_element_type=jnp.float32
            )
            total = part if total is None else total + part
        prev_halves.append(total)
    prev_line = jnp.where(first_half, prev_halves[0], prev_halves[1]).astype(jnp.int32)

    def picker(lines):
        lane = lines & (LANES - 1)
        same = (lines >> 7) == half_index

        def pick(plane):
            swapped = jnp.where(first_half, pltpu.roll(plane, 7, 0), pltpu.roll(plane, 1, 0))
            here = jnp.take_along_axis(plane, lane, axis=1, mode="promise_in_bounds")
            there = jnp.take_along_axis(swapped, lane, axis=1, mode="promise_in_bounds")
            return jnp.where(same, here, there)

        return pick

    pick_next = picker(next_line)
    pick_prev = picker(prev_line)

    def loaded(cell, of_core=core):
        return [cell_plane(all_ref, of_core, cell, k) for k in range(PAIRS)]

    own_weights = time_weights(first_inst, 0)
    other_weights = select_weights(core, first_inst, 3, 1)

    def chip_time_parts(planes, cell):
        return [
            other_weights[0] * other
            + turn_insts(first_inst, own_weights[1] * own + other_weights[1] * other)
            for own, other in zip(planes, loaded(cell, 1 - core))
        ]

    def flux_across(planes, velocity, pressure):
        return [
            planes[0] * velocity,
            planes[1] * velocity + jnp.where(first_var, pressure, 0.0),
            planes[2] * velocity + jnp.where(first_var, pressure * velocity, 0.0),
        ]

    def pitch_flux(planes, velocity_y, pressure, sound):
        nearby = [pick_next(plane) for plane in planes]
        _, next_velocity, next_pressure, next_sound = primitives(first_var, nearby)
        own_flux = flux_across(planes, velocity_y, pressure)
        next_flux = flux_across(nearby, next_velocity, next_pressure)
        weight = (PITCH_GAIN * 0.5) * (
            jnp.abs(velocity_y) + sound + (jnp.abs(next_velocity) + next_sound)
        )
        return [
            0.5 * (a + b) - weight * (n - o)
            for a, b, n, o in zip(own_flux, next_flux, nearby, planes)
        ]

    for cell in range(cells):
        planes = loaded(cell)
        velocity_x, velocity_y, pressure, sound = primitives(first_var, planes)
        line_ref[cell, 0], line_ref[cell, 1], line_ref[cell, 2] = velocity_x, pressure, sound
        faces_across = pitch_flux(planes, velocity_y, pressure, sound)
        times = chip_time_parts(planes, cell)
        for k in range(PAIRS):
            partial_ref[cell, k] = -(times[k] + (faces_across[k] - pick_prev(faces_across[k])))

    tile = half_index * (LANES // LINES_DEV) + lane_index // LINES_DEV
    end_codes = jnp.where(mirrored == 0, codes_ref[pl.ds(0, 1), :], codes_ref[pl.ds(1, 1), :])
    codes = jnp.zeros(shape, jnp.int32)
    for k in range(2 * LANES // LINES_DEV):
        codes = jnp.where(tile == k, jnp.broadcast_to(end_codes[:, k : k + 1], shape), codes)

    def ghost(cell):
        planes = loaded(-1 - cell)
        copied = loaded(0)
        result = []
        for k in range(PAIRS):
            reflected = planes[k] if k else jnp.where(first_var, planes[k], -planes[k])
            inflow = jnp.where(first_var, FREE_STATE[2 * k], FREE_STATE[2 * k + 1])
            result.append(
                jnp.where(codes == 0, reflected, jnp.where(codes == 1, inflow, copied[k]))
            )
        return result

    line = LineCells(first_var, sign)
    faces, inverses, aboves = {}, [], []
    for cell in range(-2, cells):
        if cell < 0:
            planes = ghost(cell)
            velocity_x, _, pressure, sound = primitives(first_var, planes)
        else:
            planes = loaded(cell)
            velocity_x, pressure, sound = [line_ref[cell, k] for k in range(3)]
        line.add(cell, planes, velocity_x, pressure, sound)
        if cell >= 1:
            faces[cell - 2] = line.face(cell - 2)
        if cell >= 2:
            at = cell - 2
            for k in range(PAIRS):
                partial_ref[at, k] = partial_ref[at, k] + (faces[at - 1][k] - faces[at][k])
        if cell >= 3 and cell % 2 == 1:
            at = cell - 3
            block = at // 2
            rates = rates_at(all_ref, core, block, first_half)
            diag = line.diagonal(at, rates)
            if block > 0:
                factor = two_by_two(line.below(at), inverses[-1])
                diag = less(diag, two_by_two(factor, aboves[-1]))
                for n in range(4):
                    factor_ref[block - 1, n] = factor[n]
            inverses.append(inverse_of(diag))
            aboves.append(line.above(at))
            kept = [*inverses[-1], aboves[-1][0], *aboves[-1][2:]]
            for n, plane in enumerate(kept):
                blocks_ref[block, n] = plane

    last = cells - 2
    for k in range(PAIRS):
        partial_ref[last, k] = partial_ref[last, k] + faces[last - 1][k]
    factor = two_by_two(line.below(last), inverses[-1])
    for n in range(4):
        factor_ref[blocks - 2, n] = factor[n]
    correction = list(two_by_two(factor, aboves[-1]))
    rates = rates_at(all_ref, core, blocks - 1, first_half)
    for member in range(2):
        centre = line.radius[last + member]
        correction[3 * member] = correction[3 * member] - rates[member] * centre
    for n in range(2):
        correction_ref[pl.ds(n * ROWS, ROWS), :] = jnp.where(
            first_var, correction[2 * n], correction[2 * n + 1]
        )


def reduce_kernel(partial_ref, time_ref, factor_ref, correction_ref, middle_ref, sides_ref):
    for row in range(0, 2 * ROWS, ROWS):
        middle_ref[pl.ds(CORRECTION_ROW + row, ROWS), :] = correction_ref[pl.ds(row, ROWS), :]
    blocks = partial_ref.shape[0] // 2
    side = None
    for block in range(blocks):
        own = []
        for cell in (2 * block, 2 * block + 1):
            for k in range(PAIRS):
                time = time_ref[pl.ds(cell * CELL_ROWS + k * ROWS, ROWS), :]
                own.append(partial_ref[cell, k] - time)
        if block > 0:
            factor = [factor_ref[block - 1, n] for n in range(4)]
            own = difference(own, apply_matrix(factor, side))
        side = own
        for n, plane in enumerate(side):
            if block < blocks - 1:
                sides_ref[block, n] = plane
            else:
                middle_ref[pl.ds(n * ROWS, ROWS), :] = plane


def spread_kernel(all_ref, blocks_ref, sides_ref, known_ref, spread_ref, table_ref):
    core = lax.axis_index("inst") & 1
    blocks = all_ref.shape[1]
    own_cell = lax.axis_index("cell")
    own_block = jnp.where(own_cell < blocks, own_cell, 2 * blocks - 1 - own_cell)
    zero = jnp.zeros((ROWS, LANES), jnp.float32)
    known, spread = [zero] * (2 * PAIRS), (zero + 1.0, zero, zero, zero + 1.0)
    for block in range(blocks - 1, -1, -1):
        if block < blocks - 1:
            kept = [blocks_ref[block, n] for n in range(7)]
            inverse, above = kept[:4], (kept[4], None, kept[5], kept[6])
            side = [sides_ref[block, n] for n in range(2 * PAIRS)]
            step = two_by_two(inverse, above)
            own = apply_matrix(inverse, side)
            if block < blocks - 2:
                known = difference(own, apply_matrix(step, known))
                spread = minus(two_by_two(step, spread))
            else:
                known, spread = own, minus(step)
        for n, plane in enumerate(known + list(spread)):
            table_ref[block, n] = plane
    for n in range(2 * PAIRS):
        base = at_block(all_ref, core, own_block)[pl.ds(n * ROWS, ROWS), :]
        known_ref[n] = base + table_ref[own_block, n]
    for n in range(4):
        spread_ref[n] = table_ref[own_block, 2 * PAIRS + n]


def plane_of(ref, row):
    return ref[pl.ds(row, ROWS), :]


def correction_of(first_var, ref):
    pairs = [both(first_var, plane_of(ref, CORRECTION_ROW + n * ROWS)) for n in range(2)]
    return [pairs[0][0], pairs[0][1], pairs[1][0], pairs[1][1]]


def middle_kernel(here_ref, there_ref, here_side_ref, side_ref, other_ref, matrix_ref):
    mirrored = lax.axis_index("cell") // (lax.axis_size("cell") // 2)
    sign = (1 - 2 * mirrored).astype(jnp.float32)
    first_var, _, _ = plane_masks()
    line = LineCells(first_var, sign)
    for cell in range(6):
        ref, at = (here_ref, cell) if cell < 3 else (there_ref, 5 - cell)
        planes = [plane_of(ref, at * CELL_ROWS + k * ROWS) for k in range(PAIRS)]
        velocity_x, _, pressure, sound = primitives(first_var, planes)
        line.add(cell, planes, velocity_x, pressure, sound)
    faces = {cell: line.face(cell) for cell in (1, 2, 3)}
    for k in range(PAIRS):
        side_ref[k] = plane_of(here_side_ref, k * ROWS) - faces[1][k]
        side_ref[PAIRS + k] = plane_of(here_side_ref, (PAIRS + k) * ROWS) + (
            faces[1][k] - faces[2][k]
        )
        other_ref[k] = faces[2][k] - faces[3][k]
        other_ref[PAIRS + k] = faces[3][k]
    no_rates = (None, None)
    diag = difference(line.diagonal(1, no_rates), correction_of(first_var, here_side_ref))
    above, below = line.above(1), line.below(3)
    kept = [*diag, *line.diagonal(3, no_rates), above[0], *above[2:], *below[:2], below[3]]
    for n, plane in enumerate(kept):
        matrix_ref[n] = plane


def join_kernel(
    side_ref, other_ref, matrix_ref, there_side_ref, known_ref, spread_ref, out_ref
):
    mirrored = lax.axis_index("cell") // (lax.axis_size("cell") // 2)
    first_var, _, _ = plane_masks()
    kept = [matrix_ref[n] for n in range(14)]
    diag, other_diag = kept[:4], kept[4:8]
    above, below = (kept[8], None, kept[9], kept[10]), (kept[11], kept[12], None, kept[13])
    other_diag = difference(other_diag, correction_of(first_var, there_side_ref)[::-1])
    other = []
    for member in range(2):
        for k in range(PAIRS):
            there = plane_of(there_side_ref, ((1 - member) * PAIRS + k) * ROWS)
            other.append(there + other_ref[member * PAIRS + k])
    factor = two_by_two(above, inverse_of(other_diag))
    diag = less(diag, two_by_two(factor, below))
    side = [side_ref[n] for n in range(2 * PAIRS)]
    middle = apply_matrix(inverse_of(diag), difference(side, apply_matrix(factor, other)))
    moved = apply_matrix([spread_ref[n] for n in range(4)], middle)
    results = [known_ref[n] + moved[n] for n in range(2 * PAIRS)]
    for cell in range(2):
        for k in range(PAIRS):
            first, second = results[cell * PAIRS + k], results[(1 - cell) * PAIRS + k]
            result = jnp.where(mirrored == 0, first, second)
            for var in range(2):
                for inst in range(2):
                    for half in range(2):
                        row = rows_of(var, inst, half)
                        out_ref[
                            inst, 2 * k + var, pl.ds(cell, 1), pl.ds(half * LANES, LANES)
                        ] = result[row : row + 1]


def share_half(copies):
    insts, count = lax.axis_size("inst"), lax.axis_size("cell")
    halves = [range(count // 2 - 1, -1, -1), range(count - 1, count // 2 - 1, -1)]
    groups = [
        [inst * count + cell for inst in (first + 1, first) for cell in half]
        for first in range(0, insts, 2)
        for half in halves
    ]
    return lax.all_to_all(
        copies, ("inst", "cell"), split_axis=0, concat_axis=0, tiled=True,
        axis_index_groups=groups,
    )


def swap_sides(block):
    pairs = [(inst, inst ^ 2) for inst in range(lax.axis_size("inst"))]
    return lax.ppermute(block, "inst", pairs)


def swap_halves(block):
    count = lax.axis_size("cell")
    return lax.ppermute(block, "cell", [(i, (i + count // 2) % count) for i in range(count)])


def float_shape(*sizes):
    return jax.ShapeDtypeStruct(sizes, jnp.float32)


def local_by_halves(state, pseudo_rate, line_next, face_codes):
    blocks = lax.axis_size("cell") // 2
    cells = 2 * blocks
    vmem = pl.BlockSpec(memory_space=pltpu.VMEM)
    plane = (ROWS, LANES)
    params = pltpu.CompilerParams(vmem_limit_bytes=VMEM_BYTES)
    places = lax.axis_size("inst") // 2
    held = [
        pltpu.with_memory_space_constraint(array, pltpu.HBM)
        for array in (state, pseudo_rate, line_next, face_codes)
    ]
    packed, next_here, codes_here = pl.pallas_call(
        pack_kernel,
        out_shape=(
            float_shape(places * blocks, BLOCK_ROWS, LANES),
            jax.ShapeDtypeStruct(line_next.shape, jnp.int32),
            jax.ShapeDtypeStruct(face_codes.shape, jnp.int32),
        ),
        in_specs=[pl.BlockSpec(memory_space=pltpu.HBM)] * 4,
        out_specs=(vmem, vmem, vmem),
        scratch_shapes=[
            pltpu.VMEM(state.shape, jnp.float32),
            pltpu.VMEM(pseudo_rate.shape, jnp.float32),
            pltpu.SemaphoreType.DMA((4,)),
        ],
        compiler_params=params,
    )(*held)
    shared = share_half(packed).reshape(places, blocks, BLOCK_ROWS, LANES)
    for_partner = pl.pallas_call(
        partner_kernel,
        out_shape=float_shape(cells * CELL_ROWS, LANES),
        in_specs=[vmem],
        out_specs=vmem,
        compiler_params=params,
    )(shared)
    from_partner = swap_sides(for_partner)
    beside = pl.CostEstimate(flops=10**6, bytes_accessed=10**6, transcendentals=0)
    kinds = (
        float_shape(cells, PAIRS, *plane),
        float_shape(blocks - 1, 4, *plane),
        float_shape(blocks - 1, 7, *plane),
        float_shape(2 * ROWS, LANES),
    )
    line_scratch = [pltpu.VMEM((cells, 3) + plane, jnp.float32)]
    arguments = (shared, next_here, codes_here)
    *near, here = pl.pallas_call(
        near_half_kernel,
        out_shape=kinds + (float_shape(MIDDLE_CELLS * CELL_ROWS, LANES),),
        in_specs=[vmem] * 3,
        out_specs=(vmem,) * 5,
        scratch_shapes=line_scratch,
        compiler_params=params,
    )(*arguments)
    there = swap_halves(here)
    partial, factors, eliminated, correction = pl.pallas_call(
        far_half_kernel,
        out_shape=kinds,
        in_specs=[vmem] * 7,
        out_specs=(vmem,) * 4,
        scratch_shapes=line_scratch,
        input_output_aliases={3 + n: n for n in range(4)},
        compiler_params=params,
        cost_estimate=beside,
    )(*arguments, *near)
    here_side, sides = pl.pallas_call(
        reduce_kernel,
        out_shape=(
            float_shape(SIDE_ROWS, LANES),
            float_shape(blocks - 1, 2 * PAIRS, *plane),
        ),
        in_specs=[vmem] * 4,
        out_specs=(vmem, vmem),
        compiler_params=params,
    )(partial, from_partner, factors, correction)
    there_side = swap_halves(here_side)
    known, spread = pl.pallas_call(
        spread_kernel,
        out_shape=(float_shape(2 * PAIRS, *plane), float_shape(4, *plane)),
        in_specs=[vmem] * 3,
        out_specs=(vmem, vmem),
        scratch_shapes=[pltpu.VMEM((blocks, 2 * PAIRS + 4) + plane, jnp.float32)],
        compiler_params=params,
        cost_estimate=beside,
    )(shared, eliminated, sides)
    side, other, matrices = pl.pallas_call(
        middle_kernel,
        out_shape=(
            float_shape(2 * PAIRS, *plane),
            float_shape(2 * PAIRS, *plane),
            float_shape(14, *plane),
        ),
        in_specs=[vmem] * 3,
        out_specs=(vmem,) * 3,
        compiler_params=params,
        cost_estimate=beside,
    )(here, there, here_side)
    return pl.pallas_call(
        join_kernel,
        out_shape=float_shape(*state.shape),
        in_specs=[vmem] * 6,
        out_specs=vmem,
        compiler_params=params,
    )(side, other, matrices, there_side, known, spread)


def solution(mesh):
    placed = (P("inst", None, "cell", None), P("cell", None), P(), P())
    inst_count, cell_count = mesh.shape["inst"], mesh.shape["cell"]

    def local(state, pseudo_rate, line_next, face_codes):
        small = (
            state.shape == (2, 6, 2, 2 * LANES)
            and inst_count * 2 == NT
            and cell_count == 8
            and face_codes.shape[1] * LINES_DEV == state.shape[3]
        )
        chosen = local_by_halves if small else local_by_lines
        return chosen(state, pseudo_rate, line_next, face_codes)

    return jax.shard_map(
        local, mesh=mesh, in_specs=placed, out_specs=P("inst", None, "cell", None), check_vma=False
    )
```

```python
import functools

import jax
import jax.numpy as jnp
import numpy as np
from jax import lax
from jax.experimental import pallas as pl
from jax.experimental.pallas import tpu as pltpu
from jax.sharding import PartitionSpec as P

NT = 8
LINES_DEV = 32


GAMMA_GAS = 1.4
OMEGA_BLADE = 1.0
SENSOR_GAIN = 0.25
FOURTH_GAIN = 0.03125
PITCH_GAIN = 0.5
SECOND_IMPL = 1.0
FOURTH_IMPL = 0.25
FREE_STATE = (1.0, 0.5, 0.0, 0.0, 2.625, 0.2)
MIRROR_SIGNS = (1.0, -1.0, 1.0, 1.0, 1.0, 1.0)
ZERO_BLOCK = (0.0, 0.0, 0.0, 0.0)
UNIT_BLOCK = (1.0, 0.0, 0.0, 1.0)
ZERO_PAIR = (0.0, 0.0)


def extended(block, sides, width):
    for axis, dim in sides:
        count = lax.axis_size(axis)
        forward = [(i, i + 1) for i in range(count - 1)]
        backward = [(target, source) for source, target in forward]
        low = lax.ppermute(
            lax.slice_in_dim(block, block.shape[dim] - width, None, axis=dim), axis, forward
        )
        high = lax.ppermute(lax.slice_in_dim(block, 0, width, axis=dim), axis, backward)
        block = jnp.concatenate([low, block, high], axis=dim)
    return block


def spectral_matrix(instances):
    offsets = np.arange(instances)[:, None] - np.arange(instances)[None, :]
    angles = np.pi * offsets / instances
    safe_sin = np.where(offsets == 0, 1.0, np.sin(angles))
    parity = np.where(np.mod(offsets, 2) == 0, -1.0, 1.0)
    matrix_table = np.where(
        offsets == 0, 0.0, 0.5 * OMEGA_BLADE * parity * np.cos(angles) / safe_sin
    )
    return jnp.asarray(matrix_table, jnp.float32)


def primitive_parts(cells_state):
    density = cells_state[..., 0, :, :]
    inverse = 1.0 / density
    velocity_x = cells_state[..., 1, :, :] * inverse
    velocity_y = cells_state[..., 2, :, :] * inverse
    velocity_z = cells_state[..., 3, :, :] * inverse
    energy = cells_state[..., 4, :, :]
    pressure = (GAMMA_GAS - 1.0) * (
        energy
        - 0.5
        * density
        * (velocity_x * velocity_x + velocity_y * velocity_y + velocity_z * velocity_z)
    )
    sound_speed = jnp.sqrt(GAMMA_GAS * pressure * inverse)
    return (velocity_x, velocity_y, pressure, sound_speed)


def directed_flux(cells_state, normal_velocity, pressure, component):
    zero_plane = jnp.zeros_like(pressure)
    pressure_rows = [
        zero_plane,
        zero_plane,
        zero_plane,
        zero_plane,
        pressure * normal_velocity,
        zero_plane,
    ]
    pressure_rows[component] = pressure
    return cells_state * normal_velocity[..., None, :, :] + jnp.stack(pressure_rows, axis=-3)


def line_residual(padded):
    velocity_x, velocity_y, pressure, sound_speed = primitive_parts(padded)
    flux_line = directed_flux(padded, velocity_x, pressure, 1)
    radius = jnp.abs(velocity_x) + sound_speed
    sensor = jnp.abs(
        pressure[..., 2:, :] - 2.0 * pressure[..., 1:-1, :] + pressure[..., :-2, :]
    ) / (pressure[..., 2:, :] + 2.0 * pressure[..., 1:-1, :] + pressure[..., :-2, :])
    second = SENSOR_GAIN * jnp.maximum(sensor[..., :-1, :], sensor[..., 1:, :])
    fourth = jnp.maximum(0.0, FOURTH_GAIN - second)
    face_radius = 0.5 * (radius[..., 1:-2, :] + radius[..., 2:-1, :])
    left_far = padded[..., :-3, :]
    left_near = padded[..., 1:-2, :]
    right_near = padded[..., 2:-1, :]
    right_far = padded[..., 3:, :]
    damping = face_radius[..., None, :, :] * (
        second[..., None, :, :] * (right_near - left_near)
        - fourth[..., None, :, :] * (right_far - 3.0 * right_near + 3.0 * left_near - left_far)
    )
    face_flux = 0.5 * (flux_line[..., 1:-2, :] + flux_line[..., 2:-1, :]) - damping
    return (face_flux[..., 1:, :] - face_flux[..., :-1, :], radius)


def pitch_parts(cells_state):
    velocity_x, velocity_y, pressure, sound_speed = primitive_parts(cells_state)
    return (directed_flux(cells_state, velocity_y, pressure, 2), jnp.abs(velocity_y) + sound_speed)


def pitch_residual(cells_state, next_lines, prev_lines):
    pitch_flux, radius = pitch_parts(cells_state)
    state_next = jnp.take(cells_state, next_lines, axis=-1)
    flux_next, radius_next = pitch_parts(state_next)
    face_flux = 0.5 * (pitch_flux + flux_next) - PITCH_GAIN * (0.5 * (radius + radius_next))[
        ..., None, :, :
    ] * (state_next - cells_state)
    return face_flux - jnp.take(face_flux, prev_lines, axis=-1)


def boundary_cells(edge_pair, line_codes, lower_end):
    reflected = edge_pair[..., ::-1, :] * jnp.asarray(MIRROR_SIGNS, jnp.float32)[:, None, None]
    if lower_end:
        copied = jnp.concatenate([edge_pair[..., :1, :], edge_pair[..., :1, :]], axis=-2)
    else:
        copied = jnp.concatenate([edge_pair[..., 1:, :], edge_pair[..., 1:, :]], axis=-2)
    inflow = jnp.asarray(FREE_STATE, jnp.float32)[:, None, None] + jnp.zeros_like(edge_pair)
    return jnp.where(line_codes == 0, reflected, jnp.where(line_codes == 1, inflow, copied))


def line_coefficients(radius_ext, diagonal_term, positions, total_cells):
    radius_below = radius_ext[..., :-2, :]
    radius_centre = radius_ext[..., 1:-1, :]
    radius_above = radius_ext[..., 2:, :]
    face_below = 0.5 * (radius_below + radius_centre)
    face_above = 0.5 * (radius_centre + radius_above)
    far_low = FOURTH_IMPL * radius_below
    near_low = -SECOND_IMPL * face_below - 2.0 * FOURTH_IMPL * (radius_below + radius_centre)
    middle = (
        diagonal_term
        + SECOND_IMPL * (face_below + face_above)
        + FOURTH_IMPL * (radius_below + 4.0 * radius_centre + radius_above)
    )
    near_high = -SECOND_IMPL * face_above - 2.0 * FOURTH_IMPL * (radius_centre + radius_above)
    far_high = FOURTH_IMPL * radius_above
    column = positions[:, None]
    far_low = jnp.where(column >= 2, far_low, 0.0)
    near_low = jnp.where(column >= 1, near_low, 0.0)
    near_high = jnp.where(column <= total_cells - 2, near_high, 0.0)
    far_high = jnp.where(column <= total_cells - 3, far_high, 0.0)
    return (far_low, near_low, middle, near_high, far_high)


def block_product(first_matrix, second_matrix):
    return (
        first_matrix[0] * second_matrix[0] + first_matrix[1] * second_matrix[2],
        first_matrix[0] * second_matrix[1] + first_matrix[1] * second_matrix[3],
        first_matrix[2] * second_matrix[0] + first_matrix[3] * second_matrix[2],
        first_matrix[2] * second_matrix[1] + first_matrix[3] * second_matrix[3],
    )


def block_inverse(matrix):
    determinant = matrix[0] * matrix[3] - matrix[1] * matrix[2]
    reciprocal = 1.0 / determinant
    return (
        matrix[3] * reciprocal,
        -matrix[1] * reciprocal,
        -matrix[2] * reciprocal,
        matrix[0] * reciprocal,
    )


def block_apply(matrix, vector):
    return (
        matrix[0] * vector[0] + matrix[1] * vector[1],
        matrix[2] * vector[0] + matrix[3] * vector[1],
    )


def add_blocks(first_members, second_members):
    return tuple((a + b for a, b in zip(first_members, second_members)))


def negate(members):
    return tuple((-a for a in members))


def extend_blocks(members, fill_values):
    return tuple(
        (
            jnp.concatenate([m, jnp.full_like(m[..., :1, :], f)], axis=-2)
            for m, f in zip(members, fill_values)
        )
    )


def shift_next(members, fill_values):
    return tuple(
        (
            jnp.concatenate([m[..., 1:, :], jnp.full_like(m[..., :1, :], f)], axis=-2)
            for m, f in zip(members, fill_values)
        )
    )


def shift_prev(members):
    return tuple(
        (jnp.concatenate([jnp.zeros_like(m[..., :1, :]), m[..., :-1, :]], axis=-2) for m in members)
    )


def pair_split(member):
    shaped = member.reshape(member.shape[:-2] + (member.shape[-2] // 2, 2, member.shape[-1]))
    return (shaped[..., 0, :], shaped[..., 1, :])


def split_parity(members):
    halves = [pair_split(m) for m in members]
    return (tuple((h[0] for h in halves)), tuple((h[1] for h in halves)))


def alternate(first_member, second_member):
    stacked = jnp.stack((first_member, second_member), axis=-2)
    return stacked.reshape(
        first_member.shape[:-2] + (2 * first_member.shape[-2], first_member.shape[-1])
    )


def reduce_blocks(sub_blocks, diag_blocks, super_blocks, right_side):
    block_count = diag_blocks[0].shape[-2]
    if block_count == 1:
        return block_apply(block_inverse(diag_blocks), right_side)
    if block_count % 2 == 1:
        sub_blocks = extend_blocks(sub_blocks, ZERO_BLOCK)
        diag_blocks = extend_blocks(diag_blocks, UNIT_BLOCK)
        super_blocks = extend_blocks(super_blocks, ZERO_BLOCK)
        right_side = extend_blocks(right_side, ZERO_PAIR)
    sub_even, sub_odd = split_parity(sub_blocks)
    diag_even, diag_odd = split_parity(diag_blocks)
    super_even, super_odd = split_parity(super_blocks)
    side_even, side_odd = split_parity(right_side)
    inverse_even = block_inverse(diag_even)
    inverse_next = shift_next(inverse_even, UNIT_BLOCK)
    sub_next = shift_next(sub_even, ZERO_BLOCK)
    super_next = shift_next(super_even, ZERO_BLOCK)
    side_next = shift_next(side_even, ZERO_PAIR)
    left_factor = negate(block_product(sub_odd, inverse_even))
    right_factor = negate(block_product(super_odd, inverse_next))
    reduced_sub = block_product(left_factor, sub_even)
    reduced_diag = add_blocks(
        diag_odd,
        add_blocks(block_product(left_factor, super_even), block_product(right_factor, sub_next)),
    )
    reduced_super = block_product(right_factor, super_next)
    reduced_side = add_blocks(
        side_odd,
        add_blocks(block_apply(left_factor, side_even), block_apply(right_factor, side_next)),
    )
    odd_values = reduce_blocks(reduced_sub, reduced_diag, reduced_super, reduced_side)
    before_values = shift_prev(odd_values)
    remainder = add_blocks(
        side_even,
        negate(
            add_blocks(block_apply(sub_even, before_values), block_apply(super_even, odd_values))
        ),
    )
    even_values = block_apply(inverse_even, remainder)
    merged = tuple((alternate(e, o) for e, o in zip(even_values, odd_values)))
    return tuple((m[..., :block_count, :] for m in merged))


def cells_leading(block):
    moved = jnp.transpose(block, (2, 0, 1, 3))
    return moved.reshape(block.shape[2], block.shape[0] * block.shape[1] * block.shape[3])


def solve_in_lanes(coefficients, line_source):
    source_shape = line_source.shape
    lane_coef = [cells_leading(jnp.broadcast_to(c[:, None], source_shape)) for c in coefficients]
    pairs_list = [pair_split(m) for m in lane_coef]
    zero_plane = jnp.zeros_like(pairs_list[2][0])
    sub_blocks = (pairs_list[0][0], pairs_list[1][0], zero_plane, pairs_list[0][1])
    diag_blocks = (pairs_list[2][0], pairs_list[3][0], pairs_list[1][1], pairs_list[2][1])
    super_blocks = (pairs_list[4][0], zero_plane, pairs_list[3][1], pairs_list[4][1])
    values = reduce_blocks(
        sub_blocks, diag_blocks, super_blocks, pair_split(cells_leading(line_source))
    )
    flat = alternate(values[0], values[1])
    shaped = flat.reshape(source_shape[2], source_shape[0], source_shape[1], source_shape[3])
    return jnp.transpose(shaped, (1, 2, 0, 3))


def return_tiles(line_values):
    return lax.all_to_all(line_values, "cell", split_axis=2, concat_axis=3, tiled=True)


def local_by_lines(state, pseudo_rate, line_next, face_codes):
    local_count = state.shape[0]
    tile_cells = state.shape[2]
    cell_index = lax.axis_index("cell")
    cell_count = lax.axis_size("cell")
    total_cells = tile_cells * cell_count
    spectral = spectral_matrix(NT)
    first_local = lax.axis_index("inst") * local_count
    own_rows = lax.dynamic_slice_in_dim(spectral, first_local, local_count, 0)
    shard_block = jax.tree.map(lambda a: lax.all_gather(a, "inst", axis=0, tiled=True), state)
    columns = lax.slice_in_dim(own_rows, 0, shard_block.shape[0], axis=1)
    time_term = jnp.zeros_like(state) + jnp.einsum(
        "nm,mvil->nvil", columns, shard_block, precision=lax.Precision.HIGHEST
    )
    padded = extended(state, (("cell", 2),), 2)
    codes_lines = jnp.repeat(face_codes, LINES_DEV, axis=1)
    lower_ghost = boundary_cells(state[:, :, 0:2, :], codes_lines[0], True)
    upper_ghost = boundary_cells(state[:, :, -2:, :], codes_lines[1], False)
    lower_rim = jnp.where(cell_index == 0, lower_ghost, padded[:, :, :2, :])
    upper_rim = jnp.where(cell_index == cell_count - 1, upper_ghost, padded[:, :, -2:, :])
    padded = jnp.concatenate([lower_rim, padded[:, :, 2:-2, :], upper_rim], axis=2)
    line_part, radius = line_residual(padded)
    prev_lines = (
        jnp.zeros_like(line_next).at[line_next].set(jnp.arange(line_next.shape[0], dtype=jnp.int32))
    )
    residual = line_part + pitch_residual(state, line_next, prev_lines) + time_term
    right_side = -residual
    centre_radius = radius[:, 2:-2, :]
    diagonal_term = pseudo_rate * centre_radius
    positions = cell_index * tile_cells + jnp.arange(-1, tile_cells + 1, dtype=jnp.int32)
    inside = (positions >= 0) & (positions < total_cells)
    radius_ext = jnp.where(inside[:, None], radius[:, 1:-1, :], 0.0)
    coefficients = line_coefficients(radius_ext, diagonal_term, positions[1:-1], total_cells)
    stacked = jnp.stack(coefficients, axis=1)
    line_source = lax.all_to_all(right_side, "cell", split_axis=3, concat_axis=2, tiled=True)
    line_coef = lax.all_to_all(stacked, "cell", split_axis=3, concat_axis=2, tiled=True)
    update = return_tiles(solve_in_lanes(tuple((line_coef[:, k] for k in range(5))), line_source))
    return state + update


LANES = 128
ROWS = 8
PAIRS = 3
CELL_ROWS = PAIRS * ROWS
RATE_ROW = 2 * CELL_ROWS
VMEM_BYTES = 8 * 2**20
BLOCK_ROWS = RATE_ROW + ROWS

MIDDLE_CELLS = 2
ROUND_CELLS = 4
CORRECTION_ROW = 2 * CELL_ROWS
THIRD_ROW = CORRECTION_ROW + 2 * ROWS
SIDE_ROWS = THIRD_ROW + CELL_ROWS


def spectral_offsets():
    table = np.zeros(NT)
    for offset in range(1, NT):
        angle = np.pi * offset / NT
        parity = -1.0 if offset % 2 == 0 else 1.0
        table[offset] = 0.5 * OMEGA_BLADE * parity * np.cos(angle) / np.sin(angle)
    return [float(np.float32(value)) for value in table]


def plane_masks():
    row_index = lax.broadcasted_iota(jnp.int32, (ROWS, LANES), 0)
    return row_index < 4, (row_index & 2) == 0, row_index & 1


def both(first_var, plane):
    turned = pltpu.roll(plane, 4, 0)
    return jnp.where(first_var, plane, turned), jnp.where(first_var, turned, plane)


def primitives(first_var, planes):
    density, moment_x = both(first_var, planes[0])
    moment_y, moment_z = both(first_var, planes[1])
    energy = jnp.where(first_var, planes[2], pltpu.roll(planes[2], 4, 0))
    inverse = 1.0 / density
    velocity_x = moment_x * inverse
    velocity_y = moment_y * inverse
    velocity_z = moment_z * inverse
    kinetic = moment_x * velocity_x + moment_y * velocity_y + moment_z * velocity_z
    pressure = (GAMMA_GAS - 1.0) * (energy - 0.5 * kinetic)
    sound = jnp.sqrt(GAMMA_GAS * pressure * inverse)
    return velocity_x, velocity_y, pressure, sound


def rows_of(var, inst, half):
    return (var // 2) * ROWS + (var % 2) * 4 + inst * 2 + half


def pack_kernel(
    held_state_ref, held_rate_ref, held_next_ref, held_codes_ref, out_ref, next_ref, codes_ref,
    state_ref, rate_ref, sems,
):
    copies = [
        pltpu.make_async_copy(source, target, sems.at[k])
        for k, (source, target) in enumerate(
            (
                (held_state_ref, state_ref),
                (held_rate_ref, rate_ref),
                (held_next_ref, next_ref),
                (held_codes_ref, codes_ref),
            )
        )
    ]
    for copy in copies:
        copy.start()
    for copy in copies:
        copy.wait()
    mirrored = lax.axis_index("cell") // (lax.axis_size("cell") // 2)
    for cell in range(2):
        place = pl.multiple_of(jnp.bitwise_xor(cell, mirrored) * CELL_ROWS, ROWS)
        for k in range(PAIRS):
            rows = [
                state_ref[inst, 2 * k + var, pl.ds(cell, 1), pl.ds(half * LANES, LANES)]
                for var in range(2)
                for inst in range(2)
                for half in range(2)
            ]
            for row, values in enumerate(rows):
                out_ref[0, pl.ds(place + (k * ROWS + row), 1), :] = values
    rates = [
        rate_ref[pl.ds(cell, 1), pl.ds(half * LANES, LANES)]
        for cell in range(2)
        for half in range(2)
    ]
    for row in range(4):
        out_ref[0, pl.ds(RATE_ROW + row, 1), :] = jnp.where(
            mirrored == 0, rates[row], rates[row ^ 2]
        )
    out_ref[0, pl.ds(RATE_ROW + 4, 4), :] = jnp.zeros((4, LANES), jnp.float32)
    for row in range(0, BLOCK_ROWS, ROWS):
        values = out_ref[0, pl.ds(row, ROWS), :]
        for copy in range(1, out_ref.shape[0]):
            out_ref[copy, pl.ds(row, ROWS), :] = values


def turn_insts(first_inst, plane):
    return jnp.where(first_inst, pltpu.roll(plane, 6, 0), pltpu.roll(plane, 2, 0))


def time_weights(first_inst, shift):
    offsets = spectral_offsets()
    other = jnp.where(
        first_inst, offsets[(2 * shift + 1) % NT], offsets[(2 * shift - 1) % NT]
    )
    return offsets[(2 * shift) % NT], other


def at_block(ref, y, block):
    blocks = ref.shape[1]
    mirrored = lax.axis_index("cell") // blocks
    place = mirrored * block + (1 - mirrored) * (blocks - 1 - block)
    return ref.at[ref.shape[0] - 1 - y, place]


def cell_plane(ref, y, cell, k):
    return at_block(ref, y, cell // 2)[pl.ds((cell % 2) * CELL_ROWS + k * ROWS, ROWS), :]


def partner_kernel(all_ref, out_ref):
    own_inst = lax.axis_index("inst")
    own_y, core = own_inst >> 1, own_inst & 1
    _, first_inst, _ = plane_masks()
    one, three = time_weights(first_inst, 1), time_weights(first_inst, 3)
    near = [jnp.where(core == 0, a, b) for a, b in zip(one, three)]
    away = [jnp.where(core == 0, b, a) for a, b in zip(one, three)]
    cells = 2 * all_ref.shape[1]
    for cell in range(cells):
        for k in range(PAIRS):
            here = cell_plane(all_ref, own_y, cell, k)
            there = cell_plane(all_ref, 1 - own_y, cell, k)
            out_ref[pl.ds(cell * CELL_ROWS + k * ROWS, ROWS), :] = (
                near[0] * here
                + away[0] * there
                + turn_insts(first_inst, near[1] * here + away[1] * there)
            )


def two_by_two(first, second):
    def entry(a, b, c, d):
        terms = [x * y for x, y in ((a, b), (c, d)) if x is not None and y is not None]
        return None if not terms else terms[0] if len(terms) == 1 else terms[0] + terms[1]

    return (
        entry(first[0], second[0], first[1], second[2]),
        entry(first[0], second[1], first[1], second[3]),
        entry(first[2], second[0], first[3], second[2]),
        entry(first[2], second[1], first[3], second[3]),
    )


def inverse_of(matrix):
    reciprocal = 1.0 / (matrix[0] * matrix[3] - matrix[1] * matrix[2])
    return (
        matrix[3] * reciprocal,
        -(matrix[1] * reciprocal),
        -(matrix[2] * reciprocal),
        matrix[0] * reciprocal,
    )


def less(first, second):
    return tuple(a if b is None else a - b for a, b in zip(first, second))


def minus(members):
    return tuple(None if a is None else -a for a in members)


def matrix_vector(matrix, low, high):
    def row(a, b):
        terms = [x * y for x, y in ((a, low), (b, high)) if x is not None]
        return terms[0] if len(terms) == 1 else terms[0] + terms[1]

    return row(matrix[0], matrix[1]), row(matrix[2], matrix[3])


def apply_matrix(matrix, side):
    parts = [matrix_vector(matrix, side[k], side[PAIRS + k]) for k in range(PAIRS)]
    return [low for low, _ in parts] + [high for _, high in parts]


def difference(first, second):
    return [a - b for a, b in zip(first, second)]


def flux_along(first_var, planes, velocity, pressure, sign):
    normal = sign * velocity
    return [
        planes[0] * normal + jnp.where(first_var, 0.0, sign * pressure),
        planes[1] * normal,
        planes[2] * normal + jnp.where(first_var, pressure * normal, 0.0),
    ]


class LineCells:
    def __init__(self, first_var, sign):
        self.first_var, self.sign = first_var, sign
        self.state, self.pressure, self.radius = {}, {}, {}
        self.flux, self.step, self.sensor = {}, {}, {}

    def add(self, cell, planes, velocity, pressure, sound):
        self.state[cell], self.pressure[cell] = planes, pressure
        self.radius[cell] = jnp.abs(velocity) + sound
        self.flux[cell] = flux_along(self.first_var, planes, velocity, pressure, self.sign)
        if cell - 1 in self.state:
            self.step[cell - 1] = difference(planes, self.state[cell - 1])
        if cell - 2 in self.state:
            twice = 2.0 * self.pressure[cell - 1]
            outer = pressure + self.pressure[cell - 2]
            self.sensor[cell - 1] = jnp.abs(outer - twice) / (outer + twice)

    def face(self, cell):
        second = SENSOR_GAIN * jnp.maximum(self.sensor[cell], self.sensor[cell + 1])
        fourth = jnp.maximum(0.0, FOURTH_GAIN - second)
        face_radius = 0.5 * (self.radius[cell] + self.radius[cell + 1])
        near_weight = face_radius * (second + 2.0 * fourth)
        far_weight = face_radius * fourth
        return [
            0.5 * (self.flux[cell][k] + self.flux[cell + 1][k])
            - (
                near_weight * self.step[cell][k]
                - far_weight * (self.step[cell + 1][k] + self.step[cell - 1][k])
            )
            for k in range(PAIRS)
        ]

    def near(self, cell):
        scale = SECOND_IMPL * 0.5 + 2.0 * FOURTH_IMPL
        return -scale * (self.radius[cell] + self.radius[cell + 1])

    def far(self, cell):
        return FOURTH_IMPL * self.radius[cell]

    def middle(self, cell, rate):
        centre, above = self.radius[cell], self.radius[cell + 1]
        if cell == 0:
            total, weighted = centre + (centre + above), 4.0 * centre + above
        else:
            below = self.radius[cell - 1]
            total = (below + centre) + (centre + above)
            weighted = below + 4.0 * centre + above
        result = SECOND_IMPL * (0.5 * total) + FOURTH_IMPL * weighted
        return result if rate is None else rate * centre + result

    def diagonal(self, cell, rates):
        across = self.near(cell)
        return (self.middle(cell, rates[0]), across, across, self.middle(cell + 1, rates[1]))

    def below(self, cell):
        return (self.far(cell - 1), self.near(cell - 1), None, self.far(cell))

    def above(self, cell):
        return (self.far(cell + 1), None, self.near(cell + 1), self.far(cell + 2))


def rates_at(ref, y, block, first_half):
    rows = [at_block(ref, y, block)[pl.ds(RATE_ROW + k, 1), :] for k in range(4)]
    return [jnp.where(first_half, rows[2 * k], rows[2 * k + 1]) for k in range(2)]


def near_half_kernel(all_ref, next_ref, codes_ref, *refs):
    *results, middle_ref, round_ref, third_ref, line_ref = refs
    own_y = lax.axis_index("inst") >> 1
    cells = 2 * all_ref.shape[1]
    for cell in range(cells - MIDDLE_CELLS, cells):
        for k in range(PAIRS):
            row = (cell - (cells - MIDDLE_CELLS)) * CELL_ROWS + k * ROWS
            middle_ref[pl.ds(row, ROWS), :] = cell_plane(all_ref, own_y, cell, k)
    for cell in range(ROUND_CELLS):
        for k in range(PAIRS):
            plane = cell_plane(all_ref, own_y, cells - 1 - cell, k)
            round_ref[pl.ds(cell * CELL_ROWS + k * ROWS, ROWS), :] = plane
    for k in range(PAIRS):
        third = cell_plane(all_ref, own_y, cells - MIDDLE_CELLS - 1, k)
        third_ref[pl.ds(k * ROWS, ROWS), :] = third

    @pl.when(lax.axis_index("cell") < all_ref.shape[1])
    def _():
        half_kernel(all_ref, next_ref, codes_ref, *results, line_ref)


def far_half_kernel(all_ref, next_ref, codes_ref, *refs):
    *refs, line_ref = refs
    given, results = refs[: len(refs) // 2], refs[len(refs) // 2 :]
    far = lax.axis_index("cell") >= all_ref.shape[1]

    @pl.when(far)
    def _():
        half_kernel(all_ref, next_ref, codes_ref, *results, line_ref)

    @pl.when(jnp.logical_not(far))
    def _():
        for source, target in zip(given, results):
            target[...] = source[...]


def half_kernel(
    all_ref, next_ref, codes_ref, partial_ref, factor_ref, blocks_ref, correction_ref,
    line_ref,
):
    own_y = lax.axis_index("inst") >> 1
    blocks = all_ref.shape[1]
    cells = 2 * blocks
    mirrored = lax.axis_index("cell") // blocks
    sign = (1 - 2 * mirrored).astype(jnp.float32)
    shape = (ROWS, LANES)
    lane_index = lax.broadcasted_iota(jnp.int32, shape, 1)
    first_var, first_inst, half_index = plane_masks()
    first_half = half_index == 0
    zero = jnp.zeros(shape, jnp.float32)

    next_rows = [
        next_ref[pl.ds(half * LANES, LANES)].reshape(1, LANES) for half in range(2)
    ]
    next_line = jnp.where(first_half, next_rows[0], next_rows[1])
    column = lax.broadcasted_iota(jnp.int32, (LANES, LANES), 0)
    prev_halves = []
    for target in range(2):
        total = None
        for source in range(2):
            hits = jnp.where(column + target * LANES == next_rows[source], 1.0, 0.0)
            names = (lane_index + source * LANES).astype(jnp.float32)
            part = lax.dot_general(
                names, hits, (((1,), (1,)), ((), ())), preferred_element_type=jnp.float32
            )
            total = part if total is None else total + part
        prev_halves.append(total)
    prev_line = jnp.where(first_half, prev_halves[0], prev_halves[1]).astype(jnp.int32)

    def picker(lines):
        lane = lines & (LANES - 1)
        same = (lines >> 7) == half_index

        def pick(plane):
            swapped = jnp.where(first_half, pltpu.roll(plane, 7, 0), pltpu.roll(plane, 1, 0))
            here = jnp.take_along_axis(plane, lane, axis=1, mode="promise_in_bounds")
            there = jnp.take_along_axis(swapped, lane, axis=1, mode="promise_in_bounds")
            return jnp.where(same, here, there)

        return pick

    pick_next = picker(next_line)
    pick_prev = picker(prev_line)

    def loaded(cell, y=own_y):
        return [cell_plane(all_ref, y, cell, k) for k in range(PAIRS)]

    own_weights, away_weights = time_weights(first_inst, 0), time_weights(first_inst, 2)

    def own_time_parts(planes, cell):
        return [
            away_weights[0] * away
            + turn_insts(first_inst, own_weights[1] * own + away_weights[1] * away)
            for own, away in zip(planes, loaded(cell, 1 - own_y))
        ]

    def flux_across(planes, velocity, pressure):
        return [
            planes[0] * velocity,
            planes[1] * velocity + jnp.where(first_var, pressure, 0.0),
            planes[2] * velocity + jnp.where(first_var, pressure * velocity, 0.0),
        ]

    def pitch_flux(planes, velocity_y, pressure, sound):
        nearby = [pick_next(plane) for plane in planes]
        _, next_velocity, next_pressure, next_sound = primitives(first_var, nearby)
        own_flux = flux_across(planes, velocity_y, pressure)
        next_flux = flux_across(nearby, next_velocity, next_pressure)
        weight = (PITCH_GAIN * 0.5) * (
            jnp.abs(velocity_y) + sound + (jnp.abs(next_velocity) + next_sound)
        )
        return [
            0.5 * (a + b) - weight * (n - o)
            for a, b, n, o in zip(own_flux, next_flux, nearby, planes)
        ]

    for cell in range(cells):
        planes = loaded(cell)
        velocity_x, velocity_y, pressure, sound = primitives(first_var, planes)
        line_ref[cell, 0], line_ref[cell, 1], line_ref[cell, 2] = velocity_x, pressure, sound
        faces_across = pitch_flux(planes, velocity_y, pressure, sound)
        times = own_time_parts(planes, cell)
        for k in range(PAIRS):
            partial_ref[cell, k] = -(times[k] + (faces_across[k] - pick_prev(faces_across[k])))

    tile = half_index * (LANES // LINES_DEV) + lane_index // LINES_DEV
    end_codes = jnp.where(mirrored == 0, codes_ref[pl.ds(0, 1), :], codes_ref[pl.ds(1, 1), :])
    codes = jnp.zeros(shape, jnp.int32)
    for k in range(2 * LANES // LINES_DEV):
        codes = jnp.where(tile == k, jnp.broadcast_to(end_codes[:, k : k + 1], shape), codes)

    def ghost(cell):
        planes = loaded(-1 - cell)
        copied = loaded(0)
        result = []
        for k in range(PAIRS):
            reflected = planes[k] if k else jnp.where(first_var, planes[k], -planes[k])
            inflow = jnp.where(first_var, FREE_STATE[2 * k], FREE_STATE[2 * k + 1])
            result.append(
                jnp.where(codes == 0, reflected, jnp.where(codes == 1, inflow, copied[k]))
            )
        return result

    line = LineCells(first_var, sign)
    faces, inverses, aboves = {}, [], []
    for cell in range(-2, cells):
        if cell < 0:
            planes = ghost(cell)
            velocity_x, _, pressure, sound = primitives(first_var, planes)
        else:
            planes = loaded(cell)
            velocity_x, pressure, sound = [line_ref[cell, k] for k in range(3)]
        line.add(cell, planes, velocity_x, pressure, sound)
        if cell >= 1:
            faces[cell - 2] = line.face(cell - 2)
        if cell >= 2:
            at = cell - 2
            for k in range(PAIRS):
                partial_ref[at, k] = partial_ref[at, k] + (faces[at - 1][k] - faces[at][k])
        if cell >= 3 and cell % 2 == 1:
            at = cell - 3
            block = at // 2
            rates = rates_at(all_ref, own_y, block, first_half)
            diag = line.diagonal(at, rates)
            if block > 0:
                factor = two_by_two(line.below(at), inverses[-1])
                diag = less(diag, two_by_two(factor, aboves[-1]))
                for n in range(4):
                    factor_ref[block - 1, n] = factor[n]
            inverses.append(inverse_of(diag))
            aboves.append(line.above(at))
            kept = [*inverses[-1], aboves[-1][0], *aboves[-1][2:]]
            for n, plane in enumerate(kept):
                blocks_ref[block, n] = plane

    last = cells - 2
    for k in range(PAIRS):
        partial_ref[last, k] = partial_ref[last, k] + faces[last - 1][k]
    factor = two_by_two(line.below(last), inverses[-1])
    for n in range(4):
        factor_ref[blocks - 2, n] = factor[n]
    correction = list(two_by_two(factor, aboves[-1]))
    rates = rates_at(all_ref, own_y, blocks - 1, first_half)
    for member in range(2):
        centre = line.radius[last + member]
        correction[3 * member] = correction[3 * member] - rates[member] * centre
    for n in range(2):
        correction_ref[pl.ds(n * ROWS, ROWS), :] = jnp.where(
            first_var, correction[2 * n], correction[2 * n + 1]
        )


def reduce_kernel(
    partial_ref, time_ref, factor_ref, correction_ref, here_ref, third_ref, middle_ref, sides_ref,
    again_ref,
):
    again_ref[...] = here_ref[...]
    middle_ref[pl.ds(THIRD_ROW, CELL_ROWS), :] = third_ref[...]
    for row in range(0, 2 * ROWS, ROWS):
        middle_ref[pl.ds(CORRECTION_ROW + row, ROWS), :] = correction_ref[pl.ds(row, ROWS), :]
    blocks = partial_ref.shape[0] // 2
    side = None
    for block in range(blocks):
        own = []
        for cell in (2 * block, 2 * block + 1):
            for k in range(PAIRS):
                time = time_ref[pl.ds(cell * CELL_ROWS + k * ROWS, ROWS), :]
                own.append(partial_ref[cell, k] - time)
        if block > 0:
            factor = [factor_ref[block - 1, n] for n in range(4)]
            own = difference(own, apply_matrix(factor, side))
        side = own
        for n, plane in enumerate(side):
            if block < blocks - 1:
                sides_ref[block, n] = plane
            else:
                middle_ref[pl.ds(n * ROWS, ROWS), :] = plane


def spread_kernel(all_ref, blocks_ref, sides_ref, known_ref, spread_ref, table_ref):
    own_y = lax.axis_index("inst") >> 1
    blocks = all_ref.shape[1]
    own_cell = lax.axis_index("cell")
    own_block = jnp.where(own_cell < blocks, own_cell, 2 * blocks - 1 - own_cell)
    zero = jnp.zeros((ROWS, LANES), jnp.float32)
    known, spread = [zero] * (2 * PAIRS), (zero + 1.0, zero, zero, zero + 1.0)
    for block in range(blocks - 1, -1, -1):
        if block < blocks - 1:
            kept = [blocks_ref[block, n] for n in range(7)]
            inverse, above = kept[:4], (kept[4], None, kept[5], kept[6])
            side = [sides_ref[block, n] for n in range(2 * PAIRS)]
            step = two_by_two(inverse, above)
            own = apply_matrix(inverse, side)
            if block < blocks - 2:
                known = difference(own, apply_matrix(step, known))
                spread = minus(two_by_two(step, spread))
            else:
                known, spread = own, minus(step)
        for n, plane in enumerate(known + list(spread)):
            table_ref[block, n] = plane
    for n in range(2 * PAIRS):
        base = at_block(all_ref, own_y, own_block)[pl.ds(n * ROWS, ROWS), :]
        known_ref[n] = base + table_ref[own_block, n]
    for n in range(4):
        spread_ref[n] = table_ref[own_block, 2 * PAIRS + n]


def plane_of(ref, row):
    return ref[pl.ds(row, ROWS), :]


def correction_of(first_var, ref):
    pairs = [both(first_var, plane_of(ref, CORRECTION_ROW + n * ROWS)) for n in range(2)]
    return [pairs[0][0], pairs[0][1], pairs[1][0], pairs[1][1]]


def middle_kernel(
    here_ref, first_ref, second_ref, here_side_ref, there_side_ref, side_ref, other_ref, matrix_ref
):
    own_cell, count = lax.axis_index("cell"), lax.axis_size("cell")
    mirrored = own_cell // (count // 2)
    outer = jnp.logical_or(own_cell < count // 4, own_cell >= count - count // 4)
    sign = (1 - 2 * mirrored).astype(jnp.float32)
    first_var, _, _ = plane_masks()
    line = LineCells(first_var, sign)
    for cell in range(6):
        at = cell if cell < 3 else 5 - cell
        rows = [(at - 1) * CELL_ROWS + k * ROWS for k in range(PAIRS)]
        if at == 0:
            ref = here_side_ref if cell < 3 else there_side_ref
            planes = [plane_of(ref, THIRD_ROW + k * ROWS) for k in range(PAIRS)]
        elif cell < 3:
            planes = [plane_of(here_ref, row) for row in rows]
        else:
            planes = [
                jnp.where(
                    outer,
                    plane_of(first_ref, (2 - at) * CELL_ROWS + k * ROWS),
                    plane_of(second_ref, row),
                )
                for k, row in enumerate(rows)
            ]
        velocity_x, _, pressure, sound = primitives(first_var, planes)
        line.add(cell, planes, velocity_x, pressure, sound)
    faces = {cell: line.face(cell) for cell in (1, 2, 3)}
    for k in range(PAIRS):
        side_ref[k] = plane_of(here_side_ref, k * ROWS) - faces[1][k]
        side_ref[PAIRS + k] = plane_of(here_side_ref, (PAIRS + k) * ROWS) + (
            faces[1][k] - faces[2][k]
        )
        other_ref[k] = plane_of(there_side_ref, (PAIRS + k) * ROWS) + (
            faces[2][k] - faces[3][k]
        )
        other_ref[PAIRS + k] = plane_of(there_side_ref, k * ROWS) + faces[3][k]
    no_rates = (None, None)
    diag = difference(line.diagonal(1, no_rates), correction_of(first_var, here_side_ref))
    above, below = line.above(1), line.below(3)
    kept = [*diag, *line.diagonal(3, no_rates), above[0], *above[2:], *below[:2], below[3]]
    for n, plane in enumerate(kept):
        matrix_ref[n] = plane


def join_kernel(
    side_ref, other_ref, matrix_ref, there_side_ref, known_ref, spread_ref, out_ref
):
    mirrored = lax.axis_index("cell") // (lax.axis_size("cell") // 2)
    first_var, _, _ = plane_masks()
    kept = [matrix_ref[n] for n in range(14)]
    diag, other_diag = kept[:4], kept[4:8]
    above, below = (kept[8], None, kept[9], kept[10]), (kept[11], kept[12], None, kept[13])
    other_diag = difference(other_diag, correction_of(first_var, there_side_ref)[::-1])
    other = [other_ref[n] for n in range(2 * PAIRS)]
    factor = two_by_two(above, inverse_of(other_diag))
    diag = less(diag, two_by_two(factor, below))
    side = [side_ref[n] for n in range(2 * PAIRS)]
    middle = apply_matrix(inverse_of(diag), difference(side, apply_matrix(factor, other)))
    moved = apply_matrix([spread_ref[n] for n in range(4)], middle)
    results = [known_ref[n] + moved[n] for n in range(2 * PAIRS)]
    for cell in range(2):
        for k in range(PAIRS):
            first, second = results[cell * PAIRS + k], results[(1 - cell) * PAIRS + k]
            result = jnp.where(mirrored == 0, first, second)
            for var in range(2):
                for inst in range(2):
                    for half in range(2):
                        row = rows_of(var, inst, half)
                        out_ref[
                            inst, 2 * k + var, pl.ds(cell, 1), pl.ds(half * LANES, LANES)
                        ] = result[row : row + 1]


def share_half(copies):
    insts, count = lax.axis_size("inst"), lax.axis_size("cell")
    halves = [range(count // 2 - 1, -1, -1), range(count - 1, count // 2 - 1, -1)]
    groups = [
        [inst * count + cell for inst in range(insts - 2 + core, -1, -2) for cell in half]
        for core in range(2)
        for half in halves
    ]
    return lax.all_to_all(
        copies, ("inst", "cell"), split_axis=0, concat_axis=0, tiled=True,
        axis_index_groups=groups,
    )


def swap_cores(block):
    pairs = [(inst, inst ^ 1) for inst in range(lax.axis_size("inst"))]
    return lax.ppermute(block, "inst", pairs)


def swap_halves(block):
    count = lax.axis_size("cell")
    return lax.ppermute(block, "cell", [(i, (i + count // 2) % count) for i in range(count)])


def pass_round(block, back):
    width = lax.axis_size("cell") // 4
    steps = [(2, 0), (0, 1), (1, 3), (3, 2)]
    pairs = [
        (source * width + i, target * width + i) for source, target in steps for i in range(width)
    ]
    pairs = [(target, source) for source, target in pairs] if back else pairs
    return lax.ppermute(block, "cell", pairs)


def float_shape(*sizes):
    return jax.ShapeDtypeStruct(sizes, jnp.float32)


def local_by_halves(state, pseudo_rate, line_next, face_codes):
    blocks = lax.axis_size("cell") // 2
    cells = 2 * blocks
    vmem = pl.BlockSpec(memory_space=pltpu.VMEM)
    plane = (ROWS, LANES)
    params = pltpu.CompilerParams(vmem_limit_bytes=VMEM_BYTES)
    places = lax.axis_size("inst") // 2
    held = [
        pltpu.with_memory_space_constraint(array, pltpu.HBM)
        for array in (state, pseudo_rate, line_next, face_codes)
    ]
    packed, next_here, codes_here = pl.pallas_call(
        pack_kernel,
        out_shape=(
            float_shape(places * blocks, BLOCK_ROWS, LANES),
            jax.ShapeDtypeStruct(line_next.shape, jnp.int32),
            jax.ShapeDtypeStruct(face_codes.shape, jnp.int32),
        ),
        in_specs=[pl.BlockSpec(memory_space=pltpu.HBM)] * 4,
        out_specs=(vmem, vmem, vmem),
        scratch_shapes=[
            pltpu.VMEM(state.shape, jnp.float32),
            pltpu.VMEM(pseudo_rate.shape, jnp.float32),
            pltpu.SemaphoreType.DMA((4,)),
        ],
        compiler_params=params,
    )(*held)
    shared = share_half(packed).reshape(places, blocks, BLOCK_ROWS, LANES)
    for_partner = pl.pallas_call(
        partner_kernel,
        out_shape=float_shape(cells * CELL_ROWS, LANES),
        in_specs=[vmem],
        out_specs=vmem,
        compiler_params=params,
    )(shared)
    from_partner = swap_cores(for_partner)
    beside = pl.CostEstimate(flops=10**6, bytes_accessed=10**6, transcendentals=0)
    kinds = (
        float_shape(cells, PAIRS, *plane),
        float_shape(blocks - 1, 4, *plane),
        float_shape(blocks - 1, 7, *plane),
        float_shape(2 * ROWS, LANES),
    )
    line_scratch = [pltpu.VMEM((cells, 3) + plane, jnp.float32)]
    arguments = (shared, next_here, codes_here)
    *near, here, for_round, third = pl.pallas_call(
        near_half_kernel,
        out_shape=kinds
        + (
            float_shape(MIDDLE_CELLS * CELL_ROWS, LANES),
            float_shape(ROUND_CELLS * CELL_ROWS, LANES),
            float_shape(CELL_ROWS, LANES),
        ),
        in_specs=[vmem] * 3,
        out_specs=(vmem,) * 7,
        scratch_shapes=line_scratch,
        compiler_params=params,
    )(*arguments)
    there_first = pass_round(for_round, False)
    partial, factors, eliminated, correction = pl.pallas_call(
        far_half_kernel,
        out_shape=kinds,
        in_specs=[vmem] * 7,
        out_specs=(vmem,) * 4,
        scratch_shapes=line_scratch,
        input_output_aliases={3 + n: n for n in range(4)},
        compiler_params=params,
        cost_estimate=beside,
    )(*arguments, *near)
    here_side, sides, here_again = pl.pallas_call(
        reduce_kernel,
        out_shape=(
            float_shape(SIDE_ROWS, LANES),
            float_shape(blocks - 1, 2 * PAIRS, *plane),
            float_shape(MIDDLE_CELLS * CELL_ROWS, LANES),
        ),
        in_specs=[vmem] * 6,
        out_specs=(vmem,) * 3,
        compiler_params=params,
    )(partial, from_partner, factors, correction, here, third)
    there_side = swap_halves(here_side)
    there_second = pass_round(here_again, True)
    known, spread = pl.pallas_call(
        spread_kernel,
        out_shape=(float_shape(2 * PAIRS, *plane), float_shape(4, *plane)),
        in_specs=[vmem] * 3,
        out_specs=(vmem, vmem),
        scratch_shapes=[pltpu.VMEM((blocks, 2 * PAIRS + 4) + plane, jnp.float32)],
        compiler_params=params,
        cost_estimate=beside,
    )(shared, eliminated, sides)
    side, other, matrices = pl.pallas_call(
        middle_kernel,
        out_shape=(
            float_shape(2 * PAIRS, *plane),
            float_shape(2 * PAIRS, *plane),
            float_shape(14, *plane),
        ),
        in_specs=[vmem] * 5,
        out_specs=(vmem,) * 3,
        compiler_params=params,
    )(here, there_first, there_second, here_side, there_side)
    return pl.pallas_call(
        join_kernel,
        out_shape=float_shape(*state.shape),
        in_specs=[vmem] * 6,
        out_specs=vmem,
        compiler_params=params,
    )(side, other, matrices, there_side, known, spread)


def solution(mesh):
    placed = (P("inst", None, "cell", None), P("cell", None), P(), P())
    inst_count, cell_count = mesh.shape["inst"], mesh.shape["cell"]

    def local(state, pseudo_rate, line_next, face_codes):
        small = (
            state.shape == (2, 6, 2, 2 * LANES)
            and inst_count * 2 == NT
            and cell_count == 8
            and face_codes.shape[1] * LINES_DEV == state.shape[3]
        )
        chosen = local_by_halves if small else local_by_lines
        return chosen(state, pseudo_rate, line_next, face_codes)

    return jax.shard_map(
        local, mesh=mesh, in_specs=placed, out_specs=P("inst", None, "cell", None), check_vma=False
    )
```

```python
import functools

import jax
import jax.numpy as jnp
import numpy as np
from jax import lax
from jax.experimental import pallas as pl
from jax.experimental.pallas import tpu as pltpu
from jax.sharding import PartitionSpec as P

NT = 8
LINES_DEV = 32


GAMMA_GAS = 1.4
OMEGA_BLADE = 1.0
SENSOR_GAIN = 0.25
FOURTH_GAIN = 0.03125
PITCH_GAIN = 0.5
SECOND_IMPL = 1.0
FOURTH_IMPL = 0.25
FREE_STATE = (1.0, 0.5, 0.0, 0.0, 2.625, 0.2)
MIRROR_SIGNS = (1.0, -1.0, 1.0, 1.0, 1.0, 1.0)
ZERO_BLOCK = (0.0, 0.0, 0.0, 0.0)
UNIT_BLOCK = (1.0, 0.0, 0.0, 1.0)
ZERO_PAIR = (0.0, 0.0)


def extended(block, sides, width):
    for axis, dim in sides:
        count = lax.axis_size(axis)
        forward = [(i, i + 1) for i in range(count - 1)]
        backward = [(target, source) for source, target in forward]
        low = lax.ppermute(
            lax.slice_in_dim(block, block.shape[dim] - width, None, axis=dim), axis, forward
        )
        high = lax.ppermute(lax.slice_in_dim(block, 0, width, axis=dim), axis, backward)
        block = jnp.concatenate([low, block, high], axis=dim)
    return block


def spectral_matrix(instances):
    offsets = np.arange(instances)[:, None] - np.arange(instances)[None, :]
    angles = np.pi * offsets / instances
    safe_sin = np.where(offsets == 0, 1.0, np.sin(angles))
    parity = np.where(np.mod(offsets, 2) == 0, -1.0, 1.0)
    matrix_table = np.where(
        offsets == 0, 0.0, 0.5 * OMEGA_BLADE * parity * np.cos(angles) / safe_sin
    )
    return jnp.asarray(matrix_table, jnp.float32)


def primitive_parts(cells_state):
    density = cells_state[..., 0, :, :]
    inverse = 1.0 / density
    velocity_x = cells_state[..., 1, :, :] * inverse
    velocity_y = cells_state[..., 2, :, :] * inverse
    velocity_z = cells_state[..., 3, :, :] * inverse
    energy = cells_state[..., 4, :, :]
    pressure = (GAMMA_GAS - 1.0) * (
        energy
        - 0.5
        * density
        * (velocity_x * velocity_x + velocity_y * velocity_y + velocity_z * velocity_z)
    )
    sound_speed = jnp.sqrt(GAMMA_GAS * pressure * inverse)
    return (velocity_x, velocity_y, pressure, sound_speed)


def directed_flux(cells_state, normal_velocity, pressure, component):
    zero_plane = jnp.zeros_like(pressure)
    pressure_rows = [
        zero_plane,
        zero_plane,
        zero_plane,
        zero_plane,
        pressure * normal_velocity,
        zero_plane,
    ]
    pressure_rows[component] = pressure
    return cells_state * normal_velocity[..., None, :, :] + jnp.stack(pressure_rows, axis=-3)


def line_residual(padded):
    velocity_x, velocity_y, pressure, sound_speed = primitive_parts(padded)
    flux_line = directed_flux(padded, velocity_x, pressure, 1)
    radius = jnp.abs(velocity_x) + sound_speed
    sensor = jnp.abs(
        pressure[..., 2:, :] - 2.0 * pressure[..., 1:-1, :] + pressure[..., :-2, :]
    ) / (pressure[..., 2:, :] + 2.0 * pressure[..., 1:-1, :] + pressure[..., :-2, :])
    second = SENSOR_GAIN * jnp.maximum(sensor[..., :-1, :], sensor[..., 1:, :])
    fourth = jnp.maximum(0.0, FOURTH_GAIN - second)
    face_radius = 0.5 * (radius[..., 1:-2, :] + radius[..., 2:-1, :])
    left_far = padded[..., :-3, :]
    left_near = padded[..., 1:-2, :]
    right_near = padded[..., 2:-1, :]
    right_far = padded[..., 3:, :]
    damping = face_radius[..., None, :, :] * (
        second[..., None, :, :] * (right_near - left_near)
        - fourth[..., None, :, :] * (right_far - 3.0 * right_near + 3.0 * left_near - left_far)
    )
    face_flux = 0.5 * (flux_line[..., 1:-2, :] + flux_line[..., 2:-1, :]) - damping
    return (face_flux[..., 1:, :] - face_flux[..., :-1, :], radius)


def pitch_parts(cells_state):
    velocity_x, velocity_y, pressure, sound_speed = primitive_parts(cells_state)
    return (directed_flux(cells_state, velocity_y, pressure, 2), jnp.abs(velocity_y) + sound_speed)


def pitch_residual(cells_state, next_lines, prev_lines):
    pitch_flux, radius = pitch_parts(cells_state)
    state_next = jnp.take(cells_state, next_lines, axis=-1)
    flux_next, radius_next = pitch_parts(state_next)
    face_flux = 0.5 * (pitch_flux + flux_next) - PITCH_GAIN * (0.5 * (radius + radius_next))[
        ..., None, :, :
    ] * (state_next - cells_state)
    return face_flux - jnp.take(face_flux, prev_lines, axis=-1)


def boundary_cells(edge_pair, line_codes, lower_end):
    reflected = edge_pair[..., ::-1, :] * jnp.asarray(MIRROR_SIGNS, jnp.float32)[:, None, None]
    if lower_end:
        copied = jnp.concatenate([edge_pair[..., :1, :], edge_pair[..., :1, :]], axis=-2)
    else:
        copied = jnp.concatenate([edge_pair[..., 1:, :], edge_pair[..., 1:, :]], axis=-2)
    inflow = jnp.asarray(FREE_STATE, jnp.float32)[:, None, None] + jnp.zeros_like(edge_pair)
    return jnp.where(line_codes == 0, reflected, jnp.where(line_codes == 1, inflow, copied))


def line_coefficients(radius_ext, diagonal_term, positions, total_cells):
    radius_below = radius_ext[..., :-2, :]
    radius_centre = radius_ext[..., 1:-1, :]
    radius_above = radius_ext[..., 2:, :]
    face_below = 0.5 * (radius_below + radius_centre)
    face_above = 0.5 * (radius_centre + radius_above)
    far_low = FOURTH_IMPL * radius_below
    near_low = -SECOND_IMPL * face_below - 2.0 * FOURTH_IMPL * (radius_below + radius_centre)
    middle = (
        diagonal_term
        + SECOND_IMPL * (face_below + face_above)
        + FOURTH_IMPL * (radius_below + 4.0 * radius_centre + radius_above)
    )
    near_high = -SECOND_IMPL * face_above - 2.0 * FOURTH_IMPL * (radius_centre + radius_above)
    far_high = FOURTH_IMPL * radius_above
    column = positions[:, None]
    far_low = jnp.where(column >= 2, far_low, 0.0)
    near_low = jnp.where(column >= 1, near_low, 0.0)
    near_high = jnp.where(column <= total_cells - 2, near_high, 0.0)
    far_high = jnp.where(column <= total_cells - 3, far_high, 0.0)
    return (far_low, near_low, middle, near_high, far_high)


def block_product(first_matrix, second_matrix):
    return (
        first_matrix[0] * second_matrix[0] + first_matrix[1] * second_matrix[2],
        first_matrix[0] * second_matrix[1] + first_matrix[1] * second_matrix[3],
        first_matrix[2] * second_matrix[0] + first_matrix[3] * second_matrix[2],
        first_matrix[2] * second_matrix[1] + first_matrix[3] * second_matrix[3],
    )


def block_inverse(matrix):
    determinant = matrix[0] * matrix[3] - matrix[1] * matrix[2]
    reciprocal = 1.0 / determinant
    return (
        matrix[3] * reciprocal,
        -matrix[1] * reciprocal,
        -matrix[2] * reciprocal,
        matrix[0] * reciprocal,
    )


def block_apply(matrix, vector):
    return (
        matrix[0] * vector[0] + matrix[1] * vector[1],
        matrix[2] * vector[0] + matrix[3] * vector[1],
    )


def add_blocks(first_members, second_members):
    return tuple((a + b for a, b in zip(first_members, second_members)))


def negate(members):
    return tuple((-a for a in members))


def extend_blocks(members, fill_values):
    return tuple(
        (
            jnp.concatenate([m, jnp.full_like(m[..., :1, :], f)], axis=-2)
            for m, f in zip(members, fill_values)
        )
    )


def shift_next(members, fill_values):
    return tuple(
        (
            jnp.concatenate([m[..., 1:, :], jnp.full_like(m[..., :1, :], f)], axis=-2)
            for m, f in zip(members, fill_values)
        )
    )


def shift_prev(members):
    return tuple(
        (jnp.concatenate([jnp.zeros_like(m[..., :1, :]), m[..., :-1, :]], axis=-2) for m in members)
    )


def pair_split(member):
    shaped = member.reshape(member.shape[:-2] + (member.shape[-2] // 2, 2, member.shape[-1]))
    return (shaped[..., 0, :], shaped[..., 1, :])


def split_parity(members):
    halves = [pair_split(m) for m in members]
    return (tuple((h[0] for h in halves)), tuple((h[1] for h in halves)))


def alternate(first_member, second_member):
    stacked = jnp.stack((first_member, second_member), axis=-2)
    return stacked.reshape(
        first_member.shape[:-2] + (2 * first_member.shape[-2], first_member.shape[-1])
    )


def reduce_blocks(sub_blocks, diag_blocks, super_blocks, right_side):
    block_count = diag_blocks[0].shape[-2]
    if block_count == 1:
        return block_apply(block_inverse(diag_blocks), right_side)
    if block_count % 2 == 1:
        sub_blocks = extend_blocks(sub_blocks, ZERO_BLOCK)
        diag_blocks = extend_blocks(diag_blocks, UNIT_BLOCK)
        super_blocks = extend_blocks(super_blocks, ZERO_BLOCK)
        right_side = extend_blocks(right_side, ZERO_PAIR)
    sub_even, sub_odd = split_parity(sub_blocks)
    diag_even, diag_odd = split_parity(diag_blocks)
    super_even, super_odd = split_parity(super_blocks)
    side_even, side_odd = split_parity(right_side)
    inverse_even = block_inverse(diag_even)
    inverse_next = shift_next(inverse_even, UNIT_BLOCK)
    sub_next = shift_next(sub_even, ZERO_BLOCK)
    super_next = shift_next(super_even, ZERO_BLOCK)
    side_next = shift_next(side_even, ZERO_PAIR)
    left_factor = negate(block_product(sub_odd, inverse_even))
    right_factor = negate(block_product(super_odd, inverse_next))
    reduced_sub = block_product(left_factor, sub_even)
    reduced_diag = add_blocks(
        diag_odd,
        add_blocks(block_product(left_factor, super_even), block_product(right_factor, sub_next)),
    )
    reduced_super = block_product(right_factor, super_next)
    reduced_side = add_blocks(
        side_odd,
        add_blocks(block_apply(left_factor, side_even), block_apply(right_factor, side_next)),
    )
    odd_values = reduce_blocks(reduced_sub, reduced_diag, reduced_super, reduced_side)
    before_values = shift_prev(odd_values)
    remainder = add_blocks(
        side_even,
        negate(
            add_blocks(block_apply(sub_even, before_values), block_apply(super_even, odd_values))
        ),
    )
    even_values = block_apply(inverse_even, remainder)
    merged = tuple((alternate(e, o) for e, o in zip(even_values, odd_values)))
    return tuple((m[..., :block_count, :] for m in merged))


def cells_leading(block):
    moved = jnp.transpose(block, (2, 0, 1, 3))
    return moved.reshape(block.shape[2], block.shape[0] * block.shape[1] * block.shape[3])


def solve_in_lanes(coefficients, line_source):
    source_shape = line_source.shape
    lane_coef = [cells_leading(jnp.broadcast_to(c[:, None], source_shape)) for c in coefficients]
    pairs_list = [pair_split(m) for m in lane_coef]
    zero_plane = jnp.zeros_like(pairs_list[2][0])
    sub_blocks = (pairs_list[0][0], pairs_list[1][0], zero_plane, pairs_list[0][1])
    diag_blocks = (pairs_list[2][0], pairs_list[3][0], pairs_list[1][1], pairs_list[2][1])
    super_blocks = (pairs_list[4][0], zero_plane, pairs_list[3][1], pairs_list[4][1])
    values = reduce_blocks(
        sub_blocks, diag_blocks, super_blocks, pair_split(cells_leading(line_source))
    )
    flat = alternate(values[0], values[1])
    shaped = flat.reshape(source_shape[2], source_shape[0], source_shape[1], source_shape[3])
    return jnp.transpose(shaped, (1, 2, 0, 3))


def return_tiles(line_values):
    return lax.all_to_all(line_values, "cell", split_axis=2, concat_axis=3, tiled=True)


def local_by_lines(state, pseudo_rate, line_next, face_codes):
    local_count = state.shape[0]
    tile_cells = state.shape[2]
    cell_index = lax.axis_index("cell")
    cell_count = lax.axis_size("cell")
    total_cells = tile_cells * cell_count
    spectral = spectral_matrix(NT)
    first_local = lax.axis_index("inst") * local_count
    own_rows = lax.dynamic_slice_in_dim(spectral, first_local, local_count, 0)
    shard_block = jax.tree.map(lambda a: lax.all_gather(a, "inst", axis=0, tiled=True), state)
    columns = lax.slice_in_dim(own_rows, 0, shard_block.shape[0], axis=1)
    time_term = jnp.zeros_like(state) + jnp.einsum(
        "nm,mvil->nvil", columns, shard_block, precision=lax.Precision.HIGHEST
    )
    padded = extended(state, (("cell", 2),), 2)
    codes_lines = jnp.repeat(face_codes, LINES_DEV, axis=1)
    lower_ghost = boundary_cells(state[:, :, 0:2, :], codes_lines[0], True)
    upper_ghost = boundary_cells(state[:, :, -2:, :], codes_lines[1], False)
    lower_rim = jnp.where(cell_index == 0, lower_ghost, padded[:, :, :2, :])
    upper_rim = jnp.where(cell_index == cell_count - 1, upper_ghost, padded[:, :, -2:, :])
    padded = jnp.concatenate([lower_rim, padded[:, :, 2:-2, :], upper_rim], axis=2)
    line_part, radius = line_residual(padded)
    prev_lines = (
        jnp.zeros_like(line_next).at[line_next].set(jnp.arange(line_next.shape[0], dtype=jnp.int32))
    )
    residual = line_part + pitch_residual(state, line_next, prev_lines) + time_term
    right_side = -residual
    centre_radius = radius[:, 2:-2, :]
    diagonal_term = pseudo_rate * centre_radius
    positions = cell_index * tile_cells + jnp.arange(-1, tile_cells + 1, dtype=jnp.int32)
    inside = (positions >= 0) & (positions < total_cells)
    radius_ext = jnp.where(inside[:, None], radius[:, 1:-1, :], 0.0)
    coefficients = line_coefficients(radius_ext, diagonal_term, positions[1:-1], total_cells)
    stacked = jnp.stack(coefficients, axis=1)
    line_source = lax.all_to_all(right_side, "cell", split_axis=3, concat_axis=2, tiled=True)
    line_coef = lax.all_to_all(stacked, "cell", split_axis=3, concat_axis=2, tiled=True)
    update = return_tiles(solve_in_lanes(tuple((line_coef[:, k] for k in range(5))), line_source))
    return state + update


LANES = 128
ROWS = 8
PAIRS = 3
CELL_ROWS = PAIRS * ROWS
RATE_ROW = 2 * CELL_ROWS
VMEM_BYTES = 8 * 2**20
BLOCK_ROWS = RATE_ROW + ROWS

MIDDLE_CELLS = 2
ROUND_CELLS = 4
CORRECTION_ROW = 2 * CELL_ROWS
THIRD_ROW = CORRECTION_ROW + 2 * ROWS
SIDE_ROWS = THIRD_ROW + CELL_ROWS


def spectral_offsets():
    table = np.zeros(NT)
    for offset in range(1, NT):
        angle = np.pi * offset / NT
        parity = -1.0 if offset % 2 == 0 else 1.0
        table[offset] = 0.5 * OMEGA_BLADE * parity * np.cos(angle) / np.sin(angle)
    return [float(np.float32(value)) for value in table]


def plane_masks():
    row_index = lax.broadcasted_iota(jnp.int32, (ROWS, LANES), 0)
    return row_index < 4, (row_index & 2) == 0, row_index & 1


def both(first_var, plane):
    turned = pltpu.roll(plane, 4, 0)
    return jnp.where(first_var, plane, turned), jnp.where(first_var, turned, plane)


def primitives(first_var, planes):
    density, moment_x = both(first_var, planes[0])
    moment_y, moment_z = both(first_var, planes[1])
    energy = jnp.where(first_var, planes[2], pltpu.roll(planes[2], 4, 0))
    inverse = 1.0 / density
    velocity_x = moment_x * inverse
    velocity_y = moment_y * inverse
    velocity_z = moment_z * inverse
    kinetic = moment_x * velocity_x + moment_y * velocity_y + moment_z * velocity_z
    pressure = (GAMMA_GAS - 1.0) * (energy - 0.5 * kinetic)
    sound = jnp.sqrt(GAMMA_GAS * pressure * inverse)
    return velocity_x, velocity_y, pressure, sound


def rows_of(var, inst, half):
    return (var // 2) * ROWS + (var % 2) * 4 + inst * 2 + half


def pack_kernel(
    held_state_ref, held_rate_ref, held_next_ref, held_codes_ref, out_ref, next_ref, codes_ref,
    state_ref, rate_ref, sems,
):
    copies = [
        pltpu.make_async_copy(source, target, sems.at[k])
        for k, (source, target) in enumerate(
            (
                (held_state_ref, state_ref),
                (held_rate_ref, rate_ref),
                (held_next_ref, next_ref),
                (held_codes_ref, codes_ref),
            )
        )
    ]
    for copy in copies:
        copy.start()
    for copy in copies:
        copy.wait()
    mirrored = lax.axis_index("cell") // (lax.axis_size("cell") // 2)
    for cell in range(2):
        place = pl.multiple_of(jnp.bitwise_xor(cell, mirrored) * CELL_ROWS, ROWS)
        for k in range(PAIRS):
            rows = [
                state_ref[inst, 2 * k + var, pl.ds(cell, 1), pl.ds(half * LANES, LANES)]
                for var in range(2)
                for inst in range(2)
                for half in range(2)
            ]
            for row, values in enumerate(rows):
                out_ref[0, pl.ds(place + (k * ROWS + row), 1), :] = values
    rates = [
        rate_ref[pl.ds(cell, 1), pl.ds(half * LANES, LANES)]
        for cell in range(2)
        for half in range(2)
    ]
    for row in range(4):
        out_ref[0, pl.ds(RATE_ROW + row, 1), :] = jnp.where(
            mirrored == 0, rates[row], rates[row ^ 2]
        )
    out_ref[0, pl.ds(RATE_ROW + 4, 4), :] = jnp.zeros((4, LANES), jnp.float32)
    for row in range(0, BLOCK_ROWS, ROWS):
        values = out_ref[0, pl.ds(row, ROWS), :]
        for copy in range(1, out_ref.shape[0]):
            out_ref[copy, pl.ds(row, ROWS), :] = values


def turn_insts(first_inst, plane):
    return jnp.where(first_inst, pltpu.roll(plane, 6, 0), pltpu.roll(plane, 2, 0))


def time_weights(first_inst, shift):
    offsets = spectral_offsets()
    other = jnp.where(
        first_inst, offsets[(2 * shift + 1) % NT], offsets[(2 * shift - 1) % NT]
    )
    return offsets[(2 * shift) % NT], other


def at_block(ref, y, block):
    blocks = ref.shape[1]
    mirrored = lax.axis_index("cell") // blocks
    place = mirrored * block + (1 - mirrored) * (blocks - 1 - block)
    return ref.at[ref.shape[0] - 1 - y, place]


def cell_plane(ref, y, cell, k):
    return at_block(ref, y, cell // 2)[pl.ds((cell % 2) * CELL_ROWS + k * ROWS, ROWS), :]


def partner_kernel(all_ref, out_ref):
    own_inst = lax.axis_index("inst")
    own_y, core = own_inst >> 1, own_inst & 1
    _, first_inst, _ = plane_masks()
    one, three = time_weights(first_inst, 1), time_weights(first_inst, 3)
    near = [jnp.where(core == 0, a, b) for a, b in zip(one, three)]
    away = [jnp.where(core == 0, b, a) for a, b in zip(one, three)]
    cells = 2 * all_ref.shape[1]
    for cell in range(cells):
        for k in range(PAIRS):
            here = cell_plane(all_ref, own_y, cell, k)
            there = cell_plane(all_ref, 1 - own_y, cell, k)
            out_ref[pl.ds(cell * CELL_ROWS + k * ROWS, ROWS), :] = (
                near[0] * here
                + away[0] * there
                + turn_insts(first_inst, near[1] * here + away[1] * there)
            )


def two_by_two(first, second):
    def entry(a, b, c, d):
        terms = [x * y for x, y in ((a, b), (c, d)) if x is not None and y is not None]
        return None if not terms else terms[0] if len(terms) == 1 else terms[0] + terms[1]

    return (
        entry(first[0], second[0], first[1], second[2]),
        entry(first[0], second[1], first[1], second[3]),
        entry(first[2], second[0], first[3], second[2]),
        entry(first[2], second[1], first[3], second[3]),
    )


def inverse_of(matrix):
    reciprocal = 1.0 / (matrix[0] * matrix[3] - matrix[1] * matrix[2])
    return (
        matrix[3] * reciprocal,
        -(matrix[1] * reciprocal),
        -(matrix[2] * reciprocal),
        matrix[0] * reciprocal,
    )


def less(first, second):
    return tuple(a if b is None else a - b for a, b in zip(first, second))


def minus(members):
    return tuple(None if a is None else -a for a in members)


def matrix_vector(matrix, low, high):
    def row(a, b):
        terms = [x * y for x, y in ((a, low), (b, high)) if x is not None]
        return terms[0] if len(terms) == 1 else terms[0] + terms[1]

    return row(matrix[0], matrix[1]), row(matrix[2], matrix[3])


def apply_matrix(matrix, side):
    parts = [matrix_vector(matrix, side[k], side[PAIRS + k]) for k in range(PAIRS)]
    return [low for low, _ in parts] + [high for _, high in parts]


def difference(first, second):
    return [a - b for a, b in zip(first, second)]


def flux_along(first_var, planes, velocity, pressure, sign):
    normal = sign * velocity
    return [
        planes[0] * normal + jnp.where(first_var, 0.0, sign * pressure),
        planes[1] * normal,
        planes[2] * normal + jnp.where(first_var, pressure * normal, 0.0),
    ]


class LineCells:
    def __init__(self, first_var, sign):
        self.first_var, self.sign = first_var, sign
        self.state, self.pressure, self.radius = {}, {}, {}
        self.flux, self.step, self.sensor = {}, {}, {}

    def add(self, cell, planes, velocity, pressure, sound):
        self.state[cell], self.pressure[cell] = planes, pressure
        self.radius[cell] = jnp.abs(velocity) + sound
        self.flux[cell] = flux_along(self.first_var, planes, velocity, pressure, self.sign)
        if cell - 1 in self.state:
            self.step[cell - 1] = difference(planes, self.state[cell - 1])
        if cell - 2 in self.state:
            twice = 2.0 * self.pressure[cell - 1]
            outer = pressure + self.pressure[cell - 2]
            self.sensor[cell - 1] = jnp.abs(outer - twice) / (outer + twice)

    def face(self, cell):
        second = SENSOR_GAIN * jnp.maximum(self.sensor[cell], self.sensor[cell + 1])
        fourth = jnp.maximum(0.0, FOURTH_GAIN - second)
        face_radius = 0.5 * (self.radius[cell] + self.radius[cell + 1])
        near_weight = face_radius * (second + 2.0 * fourth)
        far_weight = face_radius * fourth
        return [
            0.5 * (self.flux[cell][k] + self.flux[cell + 1][k])
            - (
                near_weight * self.step[cell][k]
                - far_weight * (self.step[cell + 1][k] + self.step[cell - 1][k])
            )
            for k in range(PAIRS)
        ]

    def near(self, cell):
        scale = SECOND_IMPL * 0.5 + 2.0 * FOURTH_IMPL
        return -scale * (self.radius[cell] + self.radius[cell + 1])

    def far(self, cell):
        return FOURTH_IMPL * self.radius[cell]

    def middle(self, cell, rate):
        centre, above = self.radius[cell], self.radius[cell + 1]
        if cell == 0:
            total, weighted = centre + (centre + above), 4.0 * centre + above
        else:
            below = self.radius[cell - 1]
            total = (below + centre) + (centre + above)
            weighted = below + 4.0 * centre + above
        result = SECOND_IMPL * (0.5 * total) + FOURTH_IMPL * weighted
        return result if rate is None else rate * centre + result

    def diagonal(self, cell, rates):
        across = self.near(cell)
        return (self.middle(cell, rates[0]), across, across, self.middle(cell + 1, rates[1]))

    def below(self, cell):
        return (self.far(cell - 1), self.near(cell - 1), None, self.far(cell))

    def above(self, cell):
        return (self.far(cell + 1), None, self.near(cell + 1), self.far(cell + 2))


def rates_at(ref, y, block, first_half):
    rows = [at_block(ref, y, block)[pl.ds(RATE_ROW + k, 1), :] for k in range(4)]
    return [jnp.where(first_half, rows[2 * k], rows[2 * k + 1]) for k in range(2)]


def near_half_kernel(all_ref, next_ref, codes_ref, *refs):
    *results, middle_ref, round_ref, third_ref, line_ref = refs
    own_y = lax.axis_index("inst") >> 1
    cells = 2 * all_ref.shape[1]
    for cell in range(cells - MIDDLE_CELLS, cells):
        for k in range(PAIRS):
            row = (cell - (cells - MIDDLE_CELLS)) * CELL_ROWS + k * ROWS
            middle_ref[pl.ds(row, ROWS), :] = cell_plane(all_ref, own_y, cell, k)
    for cell in range(ROUND_CELLS):
        for k in range(PAIRS):
            plane = cell_plane(all_ref, own_y, cells - 1 - cell, k)
            round_ref[pl.ds(cell * CELL_ROWS + k * ROWS, ROWS), :] = plane
    for k in range(PAIRS):
        third = cell_plane(all_ref, own_y, cells - MIDDLE_CELLS - 1, k)
        third_ref[pl.ds(k * ROWS, ROWS), :] = third

    @pl.when(lax.axis_index("cell") < all_ref.shape[1])
    def _():
        half_kernel(all_ref, next_ref, codes_ref, *results, line_ref)


def far_half_kernel(all_ref, next_ref, codes_ref, *refs):
    *refs, line_ref = refs
    given, results = refs[: len(refs) // 2], refs[len(refs) // 2 :]
    far = lax.axis_index("cell") >= all_ref.shape[1]

    @pl.when(far)
    def _():
        half_kernel(all_ref, next_ref, codes_ref, *results, line_ref)

    @pl.when(jnp.logical_not(far))
    def _():
        for source, target in zip(given, results):
            target[...] = source[...]


def half_kernel(
    all_ref, next_ref, codes_ref, partial_ref, factor_ref, blocks_ref, correction_ref,
    line_ref,
):
    own_y = lax.axis_index("inst") >> 1
    blocks = all_ref.shape[1]
    cells = 2 * blocks
    mirrored = lax.axis_index("cell") // blocks
    sign = (1 - 2 * mirrored).astype(jnp.float32)
    shape = (ROWS, LANES)
    lane_index = lax.broadcasted_iota(jnp.int32, shape, 1)
    first_var, first_inst, half_index = plane_masks()
    first_half = half_index == 0
    zero = jnp.zeros(shape, jnp.float32)

    next_rows = [
        next_ref[pl.ds(half * LANES, LANES)].reshape(1, LANES) for half in range(2)
    ]
    next_line = jnp.where(first_half, next_rows[0], next_rows[1])
    column = lax.broadcasted_iota(jnp.int32, (LANES, LANES), 0)
    prev_halves = []
    for target in range(2):
        total = None
        for source in range(2):
            hits = jnp.where(column + target * LANES == next_rows[source], 1.0, 0.0)
            names = (lane_index + source * LANES).astype(jnp.float32)
            part = lax.dot_general(
                names, hits, (((1,), (1,)), ((), ())), preferred_element_type=jnp.float32
            )
            total = part if total is None else total + part
        prev_halves.append(total)
    prev_line = jnp.where(first_half, prev_halves[0], prev_halves[1]).astype(jnp.int32)

    def picker(lines):
        lane = lines & (LANES - 1)
        same = (lines >> 7) == half_index

        def pick(plane):
            swapped = jnp.where(first_half, pltpu.roll(plane, 7, 0), pltpu.roll(plane, 1, 0))
            here = jnp.take_along_axis(plane, lane, axis=1, mode="promise_in_bounds")
            there = jnp.take_along_axis(swapped, lane, axis=1, mode="promise_in_bounds")
            return jnp.where(same, here, there)

        return pick

    pick_next = picker(next_line)
    pick_prev = picker(prev_line)

    def loaded(cell, y=own_y):
        return [cell_plane(all_ref, y, cell, k) for k in range(PAIRS)]

    own_weights, away_weights = time_weights(first_inst, 0), time_weights(first_inst, 2)

    def own_time_parts(planes, cell):
        return [
            away_weights[0] * away
            + turn_insts(first_inst, own_weights[1] * own + away_weights[1] * away)
            for own, away in zip(planes, loaded(cell, 1 - own_y))
        ]

    def flux_across(planes, velocity, pressure):
        return [
            planes[0] * velocity,
            planes[1] * velocity + jnp.where(first_var, pressure, 0.0),
            planes[2] * velocity + jnp.where(first_var, pressure * velocity, 0.0),
        ]

    def pitch_flux(planes, velocity_y, pressure, sound):
        nearby = [pick_next(plane) for plane in planes]
        _, next_velocity, next_pressure, next_sound = primitives(first_var, nearby)
        own_flux = flux_across(planes, velocity_y, pressure)
        next_flux = flux_across(nearby, next_velocity, next_pressure)
        weight = (PITCH_GAIN * 0.5) * (
            jnp.abs(velocity_y) + sound + (jnp.abs(next_velocity) + next_sound)
        )
        return [
            0.5 * (a + b) - weight * (n - o)
            for a, b, n, o in zip(own_flux, next_flux, nearby, planes)
        ]

    for cell in range(cells):
        planes = loaded(cell)
        velocity_x, velocity_y, pressure, sound = primitives(first_var, planes)
        line_ref[cell, 0], line_ref[cell, 1], line_ref[cell, 2] = velocity_x, pressure, sound
        faces_across = pitch_flux(planes, velocity_y, pressure, sound)
        times = own_time_parts(planes, cell)
        for k in range(PAIRS):
            partial_ref[cell, k] = -(times[k] + (faces_across[k] - pick_prev(faces_across[k])))

    tile = half_index * (LANES // LINES_DEV) + lane_index // LINES_DEV
    end_codes = jnp.where(mirrored == 0, codes_ref[pl.ds(0, 1), :], codes_ref[pl.ds(1, 1), :])
    codes = jnp.zeros(shape, jnp.int32)
    for k in range(2 * LANES // LINES_DEV):
        codes = jnp.where(tile == k, jnp.broadcast_to(end_codes[:, k : k + 1], shape), codes)

    def ghost(cell):
        planes = loaded(-1 - cell)
        copied = loaded(0)
        result = []
        for k in range(PAIRS):
            reflected = planes[k] if k else jnp.where(first_var, planes[k], -planes[k])
            inflow = jnp.where(first_var, FREE_STATE[2 * k], FREE_STATE[2 * k + 1])
            result.append(
                jnp.where(codes == 0, reflected, jnp.where(codes == 1, inflow, copied[k]))
            )
        return result

    line = LineCells(first_var, sign)
    faces, inverses, aboves = {}, [], []
    for cell in range(-2, cells):
        if cell < 0:
            planes = ghost(cell)
            velocity_x, _, pressure, sound = primitives(first_var, planes)
        else:
            planes = loaded(cell)
            velocity_x, pressure, sound = [line_ref[cell, k] for k in range(3)]
        line.add(cell, planes, velocity_x, pressure, sound)
        if cell >= 1:
            faces[cell - 2] = line.face(cell - 2)
        if cell >= 2:
            at = cell - 2
            for k in range(PAIRS):
                partial_ref[at, k] = partial_ref[at, k] + (faces[at - 1][k] - faces[at][k])
        if cell >= 3 and cell % 2 == 1:
            at = cell - 3
            block = at // 2
            rates = rates_at(all_ref, own_y, block, first_half)
            diag = line.diagonal(at, rates)
            if block > 0:
                factor = two_by_two(line.below(at), inverses[-1])
                diag = less(diag, two_by_two(factor, aboves[-1]))
                for n in range(4):
                    factor_ref[block - 1, n] = factor[n]
            inverses.append(inverse_of(diag))
            aboves.append(line.above(at))
            kept = [*inverses[-1], aboves[-1][0], *aboves[-1][2:]]
            for n, plane in enumerate(kept):
                blocks_ref[block, n] = plane

    last = cells - 2
    for k in range(PAIRS):
        partial_ref[last, k] = partial_ref[last, k] + faces[last - 1][k]
    factor = two_by_two(line.below(last), inverses[-1])
    for n in range(4):
        factor_ref[blocks - 2, n] = factor[n]
    correction = list(two_by_two(factor, aboves[-1]))
    rates = rates_at(all_ref, own_y, blocks - 1, first_half)
    for member in range(2):
        centre = line.radius[last + member]
        correction[3 * member] = correction[3 * member] - rates[member] * centre
    for n in range(2):
        correction_ref[pl.ds(n * ROWS, ROWS), :] = jnp.where(
            first_var, correction[2 * n], correction[2 * n + 1]
        )


def reduce_kernel(
    partial_ref, time_ref, factor_ref, correction_ref, here_ref, third_ref, middle_ref, sides_ref,
    again_ref,
):
    again_ref[...] = here_ref[...]
    middle_ref[pl.ds(THIRD_ROW, CELL_ROWS), :] = third_ref[...]
    for row in range(0, 2 * ROWS, ROWS):
        middle_ref[pl.ds(CORRECTION_ROW + row, ROWS), :] = correction_ref[pl.ds(row, ROWS), :]
    blocks = partial_ref.shape[0] // 2
    side = None
    for block in range(blocks):
        own = []
        for cell in (2 * block, 2 * block + 1):
            for k in range(PAIRS):
                time = time_ref[pl.ds(cell * CELL_ROWS + k * ROWS, ROWS), :]
                own.append(partial_ref[cell, k] - time)
        if block > 0:
            factor = [factor_ref[block - 1, n] for n in range(4)]
            own = difference(own, apply_matrix(factor, side))
        side = own
        for n, plane in enumerate(side):
            if block < blocks - 1:
                sides_ref[block, n] = plane
            else:
                middle_ref[pl.ds(n * ROWS, ROWS), :] = plane


def spread_kernel(all_ref, blocks_ref, sides_ref, known_ref, spread_ref, table_ref):
    own_y = lax.axis_index("inst") >> 1
    blocks = all_ref.shape[1]
    own_cell = lax.axis_index("cell")
    own_block = jnp.where(own_cell < blocks, own_cell, 2 * blocks - 1 - own_cell)
    zero = jnp.zeros((ROWS, LANES), jnp.float32)
    known, spread = [zero] * (2 * PAIRS), (zero + 1.0, zero, zero, zero + 1.0)
    for block in range(blocks - 1, -1, -1):
        if block < blocks - 1:
            kept = [blocks_ref[block, n] for n in range(7)]
            inverse, above = kept[:4], (kept[4], None, kept[5], kept[6])
            side = [sides_ref[block, n] for n in range(2 * PAIRS)]
            step = two_by_two(inverse, above)
            own = apply_matrix(inverse, side)
            if block < blocks - 2:
                known = difference(own, apply_matrix(step, known))
                spread = minus(two_by_two(step, spread))
            else:
                known, spread = own, minus(step)
        for n, plane in enumerate(known + list(spread)):
            table_ref[block, n] = plane
    for n in range(2 * PAIRS):
        base = at_block(all_ref, own_y, own_block)[pl.ds(n * ROWS, ROWS), :]
        known_ref[n] = base + table_ref[own_block, n]
    for n in range(4):
        spread_ref[n] = table_ref[own_block, 2 * PAIRS + n]


def plane_of(ref, row):
    return ref[pl.ds(row, ROWS), :]


def correction_of(first_var, ref):
    pairs = [both(first_var, plane_of(ref, CORRECTION_ROW + n * ROWS)) for n in range(2)]
    return [pairs[0][0], pairs[0][1], pairs[1][0], pairs[1][1]]


def middle_kernel(
    here_ref, first_ref, second_ref, here_side_ref, there_side_ref, side_ref, other_ref, matrix_ref
):
    own_cell, count = lax.axis_index("cell"), lax.axis_size("cell")
    mirrored = own_cell // (count // 2)
    outer = jnp.logical_or(own_cell < count // 4, own_cell >= count - count // 4)
    sign = (1 - 2 * mirrored).astype(jnp.float32)
    first_var, _, _ = plane_masks()
    line = LineCells(first_var, sign)
    for cell in range(6):
        at = cell if cell < 3 else 5 - cell
        rows = [(at - 1) * CELL_ROWS + k * ROWS for k in range(PAIRS)]
        if at == 0:
            ref = here_side_ref if cell < 3 else there_side_ref
            planes = [plane_of(ref, THIRD_ROW + k * ROWS) for k in range(PAIRS)]
        elif cell < 3:
            planes = [plane_of(here_ref, row) for row in rows]
        else:
            planes = [
                jnp.where(
                    outer,
                    plane_of(first_ref, (2 - at) * CELL_ROWS + k * ROWS),
                    plane_of(second_ref, row),
                )
                for k, row in enumerate(rows)
            ]
        velocity_x, _, pressure, sound = primitives(first_var, planes)
        line.add(cell, planes, velocity_x, pressure, sound)
    faces = {cell: line.face(cell) for cell in (1, 2, 3)}
    for k in range(PAIRS):
        side_ref[k] = plane_of(here_side_ref, k * ROWS) - faces[1][k]
        side_ref[PAIRS + k] = plane_of(here_side_ref, (PAIRS + k) * ROWS) + (
            faces[1][k] - faces[2][k]
        )
        other_ref[k] = plane_of(there_side_ref, (PAIRS + k) * ROWS) + (
            faces[2][k] - faces[3][k]
        )
        other_ref[PAIRS + k] = plane_of(there_side_ref, k * ROWS) + faces[3][k]
    no_rates = (None, None)
    diag = difference(line.diagonal(1, no_rates), correction_of(first_var, here_side_ref))
    above, below = line.above(1), line.below(3)
    kept = [*diag, *line.diagonal(3, no_rates), above[0], *above[2:], *below[:2], below[3]]
    for n, plane in enumerate(kept):
        matrix_ref[n] = plane


def join_kernel(
    side_ref, other_ref, matrix_ref, there_side_ref, known_ref, spread_ref, out_ref
):
    mirrored = lax.axis_index("cell") // (lax.axis_size("cell") // 2)
    first_var, _, _ = plane_masks()
    kept = [matrix_ref[n] for n in range(14)]
    diag, other_diag = kept[:4], kept[4:8]
    above, below = (kept[8], None, kept[9], kept[10]), (kept[11], kept[12], None, kept[13])
    other_diag = difference(other_diag, correction_of(first_var, there_side_ref)[::-1])
    other = [other_ref[n] for n in range(2 * PAIRS)]
    factor = two_by_two(above, inverse_of(other_diag))
    diag = less(diag, two_by_two(factor, below))
    side = [side_ref[n] for n in range(2 * PAIRS)]
    middle = apply_matrix(inverse_of(diag), difference(side, apply_matrix(factor, other)))
    moved = apply_matrix([spread_ref[n] for n in range(4)], middle)
    results = [known_ref[n] + moved[n] for n in range(2 * PAIRS)]
    for cell in range(2):
        for k in range(PAIRS):
            first, second = results[cell * PAIRS + k], results[(1 - cell) * PAIRS + k]
            result = jnp.where(mirrored == 0, first, second)
            for var in range(2):
                for inst in range(2):
                    for half in range(2):
                        row = rows_of(var, inst, half)
                        out_ref[
                            inst, 2 * k + var, pl.ds(cell, 1), pl.ds(half * LANES, LANES)
                        ] = result[row : row + 1]


def share_half(copies):
    insts, count = lax.axis_size("inst"), lax.axis_size("cell")
    halves = [range(count // 2 - 1, -1, -1), range(count - 1, count // 2 - 1, -1)]
    groups = [
        [inst * count + cell for inst in range(insts - 2 + core, -1, -2) for cell in half]
        for core in range(2)
        for half in halves
    ]
    return lax.all_to_all(
        copies, ("inst", "cell"), split_axis=0, concat_axis=0, tiled=True,
        axis_index_groups=groups,
    )


def swap_cores(block):
    pairs = [(inst, inst ^ 1) for inst in range(lax.axis_size("inst"))]
    return lax.ppermute(block, "inst", pairs)


def swap_halves(block):
    count = lax.axis_size("cell")
    return lax.ppermute(block, "cell", [(i, (i + count // 2) % count) for i in range(count)])


def pass_round(block, steps):
    width = lax.axis_size("cell") // 4
    pairs = [
        (source * width + i, target * width + i) for source, target in steps for i in range(width)
    ]
    return lax.ppermute(block, "cell", pairs)


FIRST_ROUND = ((2, 0), (0, 1), (1, 3), (3, 2))
SECOND_ROUND = ((3, 1), (1, 2), (2, 3), (0, 0))


def float_shape(*sizes):
    return jax.ShapeDtypeStruct(sizes, jnp.float32)


def local_by_halves(state, pseudo_rate, line_next, face_codes):
    blocks = lax.axis_size("cell") // 2
    cells = 2 * blocks
    vmem = pl.BlockSpec(memory_space=pltpu.VMEM)
    plane = (ROWS, LANES)
    params = pltpu.CompilerParams(vmem_limit_bytes=VMEM_BYTES)
    places = lax.axis_size("inst") // 2
    held = [
        pltpu.with_memory_space_constraint(array, pltpu.HBM)
        for array in (state, pseudo_rate, line_next, face_codes)
    ]
    packed, next_here, codes_here = pl.pallas_call(
        pack_kernel,
        out_shape=(
            float_shape(places * blocks, BLOCK_ROWS, LANES),
            jax.ShapeDtypeStruct(line_next.shape, jnp.int32),
            jax.ShapeDtypeStruct(face_codes.shape, jnp.int32),
        ),
        in_specs=[pl.BlockSpec(memory_space=pltpu.HBM)] * 4,
        out_specs=(vmem, vmem, vmem),
        scratch_shapes=[
            pltpu.VMEM(state.shape, jnp.float32),
            pltpu.VMEM(pseudo_rate.shape, jnp.float32),
            pltpu.SemaphoreType.DMA((4,)),
        ],
        compiler_params=params,
    )(*held)
    shared = share_half(packed).reshape(places, blocks, BLOCK_ROWS, LANES)
    for_partner = pl.pallas_call(
        partner_kernel,
        out_shape=float_shape(cells * CELL_ROWS, LANES),
        in_specs=[vmem],
        out_specs=vmem,
        compiler_params=params,
    )(shared)
    from_partner = swap_cores(for_partner)
    beside = pl.CostEstimate(flops=10**6, bytes_accessed=10**6, transcendentals=0)
    kinds = (
        float_shape(cells, PAIRS, *plane),
        float_shape(blocks - 1, 4, *plane),
        float_shape(blocks - 1, 7, *plane),
        float_shape(2 * ROWS, LANES),
    )
    line_scratch = [pltpu.VMEM((cells, 3) + plane, jnp.float32)]
    arguments = (shared, next_here, codes_here)
    *near, here, for_round, third = pl.pallas_call(
        near_half_kernel,
        out_shape=kinds
        + (
            float_shape(MIDDLE_CELLS * CELL_ROWS, LANES),
            float_shape(ROUND_CELLS * CELL_ROWS, LANES),
            float_shape(CELL_ROWS, LANES),
        ),
        in_specs=[vmem] * 3,
        out_specs=(vmem,) * 7,
        scratch_shapes=line_scratch,
        compiler_params=params,
    )(*arguments)
    there_first = pass_round(for_round, FIRST_ROUND)
    partial, factors, eliminated, correction = pl.pallas_call(
        far_half_kernel,
        out_shape=kinds,
        in_specs=[vmem] * 7,
        out_specs=(vmem,) * 4,
        scratch_shapes=line_scratch,
        input_output_aliases={3 + n: n for n in range(4)},
        compiler_params=params,
        cost_estimate=beside,
    )(*arguments, *near)
    here_side, sides, here_again = pl.pallas_call(
        reduce_kernel,
        out_shape=(
            float_shape(SIDE_ROWS, LANES),
            float_shape(blocks - 1, 2 * PAIRS, *plane),
            float_shape(MIDDLE_CELLS * CELL_ROWS, LANES),
        ),
        in_specs=[vmem] * 6,
        out_specs=(vmem,) * 3,
        compiler_params=params,
    )(partial, from_partner, factors, correction, here, third)
    there_side = swap_halves(here_side)
    there_second = pass_round(here_again, SECOND_ROUND)
    known, spread = pl.pallas_call(
        spread_kernel,
        out_shape=(float_shape(2 * PAIRS, *plane), float_shape(4, *plane)),
        in_specs=[vmem] * 3,
        out_specs=(vmem, vmem),
        scratch_shapes=[pltpu.VMEM((blocks, 2 * PAIRS + 4) + plane, jnp.float32)],
        compiler_params=params,
        cost_estimate=beside,
    )(shared, eliminated, sides)
    side, other, matrices = pl.pallas_call(
        middle_kernel,
        out_shape=(
            float_shape(2 * PAIRS, *plane),
            float_shape(2 * PAIRS, *plane),
            float_shape(14, *plane),
        ),
        in_specs=[vmem] * 5,
        out_specs=(vmem,) * 3,
        compiler_params=params,
    )(here, there_first, there_second, here_side, there_side)
    return pl.pallas_call(
        join_kernel,
        out_shape=float_shape(*state.shape),
        in_specs=[vmem] * 6,
        out_specs=vmem,
        compiler_params=params,
    )(side, other, matrices, there_side, known, spread)


def solution(mesh):
    placed = (P("inst", None, "cell", None), P("cell", None), P(), P())
    inst_count, cell_count = mesh.shape["inst"], mesh.shape["cell"]

    def local(state, pseudo_rate, line_next, face_codes):
        small = (
            state.shape == (2, 6, 2, 2 * LANES)
            and inst_count * 2 == NT
            and cell_count == 8
            and face_codes.shape[1] * LINES_DEV == state.shape[3]
        )
        chosen = local_by_halves if small else local_by_lines
        return chosen(state, pseudo_rate, line_next, face_codes)

    return jax.shard_map(
        local, mesh=mesh, in_specs=placed, out_specs=P("inst", None, "cell", None), check_vma=False
    )
```

```python
import functools

import jax
import jax.numpy as jnp
import numpy as np
from jax import lax
from jax.experimental import pallas as pl
from jax.experimental.pallas import tpu as pltpu
from jax.sharding import PartitionSpec as P

NT = 8
LINES_DEV = 32


GAMMA_GAS = 1.4
OMEGA_BLADE = 1.0
SENSOR_GAIN = 0.25
FOURTH_GAIN = 0.03125
PITCH_GAIN = 0.5
SECOND_IMPL = 1.0
FOURTH_IMPL = 0.25
FREE_STATE = (1.0, 0.5, 0.0, 0.0, 2.625, 0.2)
MIRROR_SIGNS = (1.0, -1.0, 1.0, 1.0, 1.0, 1.0)
ZERO_BLOCK = (0.0, 0.0, 0.0, 0.0)
UNIT_BLOCK = (1.0, 0.0, 0.0, 1.0)
ZERO_PAIR = (0.0, 0.0)


def extended(block, sides, width):
    for axis, dim in sides:
        count = lax.axis_size(axis)
        forward = [(i, i + 1) for i in range(count - 1)]
        backward = [(target, source) for source, target in forward]
        low = lax.ppermute(
            lax.slice_in_dim(block, block.shape[dim] - width, None, axis=dim), axis, forward
        )
        high = lax.ppermute(lax.slice_in_dim(block, 0, width, axis=dim), axis, backward)
        block = jnp.concatenate([low, block, high], axis=dim)
    return block


def spectral_matrix(instances):
    offsets = np.arange(instances)[:, None] - np.arange(instances)[None, :]
    angles = np.pi * offsets / instances
    safe_sin = np.where(offsets == 0, 1.0, np.sin(angles))
    parity = np.where(np.mod(offsets, 2) == 0, -1.0, 1.0)
    matrix_table = np.where(
        offsets == 0, 0.0, 0.5 * OMEGA_BLADE * parity * np.cos(angles) / safe_sin
    )
    return jnp.asarray(matrix_table, jnp.float32)


def primitive_parts(cells_state):
    density = cells_state[..., 0, :, :]
    inverse = 1.0 / density
    velocity_x = cells_state[..., 1, :, :] * inverse
    velocity_y = cells_state[..., 2, :, :] * inverse
    velocity_z = cells_state[..., 3, :, :] * inverse
    energy = cells_state[..., 4, :, :]
    pressure = (GAMMA_GAS - 1.0) * (
        energy
        - 0.5
        * density
        * (velocity_x * velocity_x + velocity_y * velocity_y + velocity_z * velocity_z)
    )
    sound_speed = jnp.sqrt(GAMMA_GAS * pressure * inverse)
    return (velocity_x, velocity_y, pressure, sound_speed)


def directed_flux(cells_state, normal_velocity, pressure, component):
    zero_plane = jnp.zeros_like(pressure)
    pressure_rows = [
        zero_plane,
        zero_plane,
        zero_plane,
        zero_plane,
        pressure * normal_velocity,
        zero_plane,
    ]
    pressure_rows[component] = pressure
    return cells_state * normal_velocity[..., None, :, :] + jnp.stack(pressure_rows, axis=-3)


def line_residual(padded):
    velocity_x, velocity_y, pressure, sound_speed = primitive_parts(padded)
    flux_line = directed_flux(padded, velocity_x, pressure, 1)
    radius = jnp.abs(velocity_x) + sound_speed
    sensor = jnp.abs(
        pressure[..., 2:, :] - 2.0 * pressure[..., 1:-1, :] + pressure[..., :-2, :]
    ) / (pressure[..., 2:, :] + 2.0 * pressure[..., 1:-1, :] + pressure[..., :-2, :])
    second = SENSOR_GAIN * jnp.maximum(sensor[..., :-1, :], sensor[..., 1:, :])
    fourth = jnp.maximum(0.0, FOURTH_GAIN - second)
    face_radius = 0.5 * (radius[..., 1:-2, :] + radius[..., 2:-1, :])
    left_far = padded[..., :-3, :]
    left_near = padded[..., 1:-2, :]
    right_near = padded[..., 2:-1, :]
    right_far = padded[..., 3:, :]
    damping = face_radius[..., None, :, :] * (
        second[..., None, :, :] * (right_near - left_near)
        - fourth[..., None, :, :] * (right_far - 3.0 * right_near + 3.0 * left_near - left_far)
    )
    face_flux = 0.5 * (flux_line[..., 1:-2, :] + flux_line[..., 2:-1, :]) - damping
    return (face_flux[..., 1:, :] - face_flux[..., :-1, :], radius)


def pitch_parts(cells_state):
    velocity_x, velocity_y, pressure, sound_speed = primitive_parts(cells_state)
    return (directed_flux(cells_state, velocity_y, pressure, 2), jnp.abs(velocity_y) + sound_speed)


def pitch_residual(cells_state, next_lines, prev_lines):
    pitch_flux, radius = pitch_parts(cells_state)
    state_next = jnp.take(cells_state, next_lines, axis=-1)
    flux_next, radius_next = pitch_parts(state_next)
    face_flux = 0.5 * (pitch_flux + flux_next) - PITCH_GAIN * (0.5 * (radius + radius_next))[
        ..., None, :, :
    ] * (state_next - cells_state)
    return face_flux - jnp.take(face_flux, prev_lines, axis=-1)


def boundary_cells(edge_pair, line_codes, lower_end):
    reflected = edge_pair[..., ::-1, :] * jnp.asarray(MIRROR_SIGNS, jnp.float32)[:, None, None]
    if lower_end:
        copied = jnp.concatenate([edge_pair[..., :1, :], edge_pair[..., :1, :]], axis=-2)
    else:
        copied = jnp.concatenate([edge_pair[..., 1:, :], edge_pair[..., 1:, :]], axis=-2)
    inflow = jnp.asarray(FREE_STATE, jnp.float32)[:, None, None] + jnp.zeros_like(edge_pair)
    return jnp.where(line_codes == 0, reflected, jnp.where(line_codes == 1, inflow, copied))


def line_coefficients(radius_ext, diagonal_term, positions, total_cells):
    radius_below = radius_ext[..., :-2, :]
    radius_centre = radius_ext[..., 1:-1, :]
    radius_above = radius_ext[..., 2:, :]
    face_below = 0.5 * (radius_below + radius_centre)
    face_above = 0.5 * (radius_centre + radius_above)
    far_low = FOURTH_IMPL * radius_below
    near_low = -SECOND_IMPL * face_below - 2.0 * FOURTH_IMPL * (radius_below + radius_centre)
    middle = (
        diagonal_term
        + SECOND_IMPL * (face_below + face_above)
        + FOURTH_IMPL * (radius_below + 4.0 * radius_centre + radius_above)
    )
    near_high = -SECOND_IMPL * face_above - 2.0 * FOURTH_IMPL * (radius_centre + radius_above)
    far_high = FOURTH_IMPL * radius_above
    column = positions[:, None]
    far_low = jnp.where(column >= 2, far_low, 0.0)
    near_low = jnp.where(column >= 1, near_low, 0.0)
    near_high = jnp.where(column <= total_cells - 2, near_high, 0.0)
    far_high = jnp.where(column <= total_cells - 3, far_high, 0.0)
    return (far_low, near_low, middle, near_high, far_high)


def block_product(first_matrix, second_matrix):
    return (
        first_matrix[0] * second_matrix[0] + first_matrix[1] * second_matrix[2],
        first_matrix[0] * second_matrix[1] + first_matrix[1] * second_matrix[3],
        first_matrix[2] * second_matrix[0] + first_matrix[3] * second_matrix[2],
        first_matrix[2] * second_matrix[1] + first_matrix[3] * second_matrix[3],
    )


def block_inverse(matrix):
    determinant = matrix[0] * matrix[3] - matrix[1] * matrix[2]
    reciprocal = 1.0 / determinant
    return (
        matrix[3] * reciprocal,
        -matrix[1] * reciprocal,
        -matrix[2] * reciprocal,
        matrix[0] * reciprocal,
    )


def block_apply(matrix, vector):
    return (
        matrix[0] * vector[0] + matrix[1] * vector[1],
        matrix[2] * vector[0] + matrix[3] * vector[1],
    )


def add_blocks(first_members, second_members):
    return tuple((a + b for a, b in zip(first_members, second_members)))


def negate(members):
    return tuple((-a for a in members))


def extend_blocks(members, fill_values):
    return tuple(
        (
            jnp.concatenate([m, jnp.full_like(m[..., :1, :], f)], axis=-2)
            for m, f in zip(members, fill_values)
        )
    )


def shift_next(members, fill_values):
    return tuple(
        (
            jnp.concatenate([m[..., 1:, :], jnp.full_like(m[..., :1, :], f)], axis=-2)
            for m, f in zip(members, fill_values)
        )
    )


def shift_prev(members):
    return tuple(
        (jnp.concatenate([jnp.zeros_like(m[..., :1, :]), m[..., :-1, :]], axis=-2) for m in members)
    )


def pair_split(member):
    shaped = member.reshape(member.shape[:-2] + (member.shape[-2] // 2, 2, member.shape[-1]))
    return (shaped[..., 0, :], shaped[..., 1, :])


def split_parity(members):
    halves = [pair_split(m) for m in members]
    return (tuple((h[0] for h in halves)), tuple((h[1] for h in halves)))


def alternate(first_member, second_member):
    stacked = jnp.stack((first_member, second_member), axis=-2)
    return stacked.reshape(
        first_member.shape[:-2] + (2 * first_member.shape[-2], first_member.shape[-1])
    )


def reduce_blocks(sub_blocks, diag_blocks, super_blocks, right_side):
    block_count = diag_blocks[0].shape[-2]
    if block_count == 1:
        return block_apply(block_inverse(diag_blocks), right_side)
    if block_count % 2 == 1:
        sub_blocks = extend_blocks(sub_blocks, ZERO_BLOCK)
        diag_blocks = extend_blocks(diag_blocks, UNIT_BLOCK)
        super_blocks = extend_blocks(super_blocks, ZERO_BLOCK)
        right_side = extend_blocks(right_side, ZERO_PAIR)
    sub_even, sub_odd = split_parity(sub_blocks)
    diag_even, diag_odd = split_parity(diag_blocks)
    super_even, super_odd = split_parity(super_blocks)
    side_even, side_odd = split_parity(right_side)
    inverse_even = block_inverse(diag_even)
    inverse_next = shift_next(inverse_even, UNIT_BLOCK)
    sub_next = shift_next(sub_even, ZERO_BLOCK)
    super_next = shift_next(super_even, ZERO_BLOCK)
    side_next = shift_next(side_even, ZERO_PAIR)
    left_factor = negate(block_product(sub_odd, inverse_even))
    right_factor = negate(block_product(super_odd, inverse_next))
    reduced_sub = block_product(left_factor, sub_even)
    reduced_diag = add_blocks(
        diag_odd,
        add_blocks(block_product(left_factor, super_even), block_product(right_factor, sub_next)),
    )
    reduced_super = block_product(right_factor, super_next)
    reduced_side = add_blocks(
        side_odd,
        add_blocks(block_apply(left_factor, side_even), block_apply(right_factor, side_next)),
    )
    odd_values = reduce_blocks(reduced_sub, reduced_diag, reduced_super, reduced_side)
    before_values = shift_prev(odd_values)
    remainder = add_blocks(
        side_even,
        negate(
            add_blocks(block_apply(sub_even, before_values), block_apply(super_even, odd_values))
        ),
    )
    even_values = block_apply(inverse_even, remainder)
    merged = tuple((alternate(e, o) for e, o in zip(even_values, odd_values)))
    return tuple((m[..., :block_count, :] for m in merged))


def cells_leading(block):
    moved = jnp.transpose(block, (2, 0, 1, 3))
    return moved.reshape(block.shape[2], block.shape[0] * block.shape[1] * block.shape[3])


def solve_in_lanes(coefficients, line_source):
    source_shape = line_source.shape
    lane_coef = [cells_leading(jnp.broadcast_to(c[:, None], source_shape)) for c in coefficients]
    pairs_list = [pair_split(m) for m in lane_coef]
    zero_plane = jnp.zeros_like(pairs_list[2][0])
    sub_blocks = (pairs_list[0][0], pairs_list[1][0], zero_plane, pairs_list[0][1])
    diag_blocks = (pairs_list[2][0], pairs_list[3][0], pairs_list[1][1], pairs_list[2][1])
    super_blocks = (pairs_list[4][0], zero_plane, pairs_list[3][1], pairs_list[4][1])
    values = reduce_blocks(
        sub_blocks, diag_blocks, super_blocks, pair_split(cells_leading(line_source))
    )
    flat = alternate(values[0], values[1])
    shaped = flat.reshape(source_shape[2], source_shape[0], source_shape[1], source_shape[3])
    return jnp.transpose(shaped, (1, 2, 0, 3))


def return_tiles(line_values):
    return lax.all_to_all(line_values, "cell", split_axis=2, concat_axis=3, tiled=True)


def local_by_lines(state, pseudo_rate, line_next, face_codes):
    local_count = state.shape[0]
    tile_cells = state.shape[2]
    cell_index = lax.axis_index("cell")
    cell_count = lax.axis_size("cell")
    total_cells = tile_cells * cell_count
    spectral = spectral_matrix(NT)
    first_local = lax.axis_index("inst") * local_count
    own_rows = lax.dynamic_slice_in_dim(spectral, first_local, local_count, 0)
    shard_block = jax.tree.map(lambda a: lax.all_gather(a, "inst", axis=0, tiled=True), state)
    columns = lax.slice_in_dim(own_rows, 0, shard_block.shape[0], axis=1)
    time_term = jnp.zeros_like(state) + jnp.einsum(
        "nm,mvil->nvil", columns, shard_block, precision=lax.Precision.HIGHEST
    )
    padded = extended(state, (("cell", 2),), 2)
    codes_lines = jnp.repeat(face_codes, LINES_DEV, axis=1)
    lower_ghost = boundary_cells(state[:, :, 0:2, :], codes_lines[0], True)
    upper_ghost = boundary_cells(state[:, :, -2:, :], codes_lines[1], False)
    lower_rim = jnp.where(cell_index == 0, lower_ghost, padded[:, :, :2, :])
    upper_rim = jnp.where(cell_index == cell_count - 1, upper_ghost, padded[:, :, -2:, :])
    padded = jnp.concatenate([lower_rim, padded[:, :, 2:-2, :], upper_rim], axis=2)
    line_part, radius = line_residual(padded)
    prev_lines = (
        jnp.zeros_like(line_next).at[line_next].set(jnp.arange(line_next.shape[0], dtype=jnp.int32))
    )
    residual = line_part + pitch_residual(state, line_next, prev_lines) + time_term
    right_side = -residual
    centre_radius = radius[:, 2:-2, :]
    diagonal_term = pseudo_rate * centre_radius
    positions = cell_index * tile_cells + jnp.arange(-1, tile_cells + 1, dtype=jnp.int32)
    inside = (positions >= 0) & (positions < total_cells)
    radius_ext = jnp.where(inside[:, None], radius[:, 1:-1, :], 0.0)
    coefficients = line_coefficients(radius_ext, diagonal_term, positions[1:-1], total_cells)
    stacked = jnp.stack(coefficients, axis=1)
    line_source = lax.all_to_all(right_side, "cell", split_axis=3, concat_axis=2, tiled=True)
    line_coef = lax.all_to_all(stacked, "cell", split_axis=3, concat_axis=2, tiled=True)
    update = return_tiles(solve_in_lanes(tuple((line_coef[:, k] for k in range(5))), line_source))
    return state + update


LANES = 128
ROWS = 8
PAIRS = 3
CELL_ROWS = PAIRS * ROWS
RATE_ROW = 2 * CELL_ROWS
VMEM_BYTES = 8 * 2**20
BLOCK_ROWS = RATE_ROW + ROWS

MIDDLE_CELLS = 2
ROUND_CELLS = 4
CORRECTION_ROW = 2 * CELL_ROWS
THIRD_ROW = CORRECTION_ROW + 2 * ROWS
SIDE_ROWS = THIRD_ROW + CELL_ROWS


def spectral_offsets():
    table = np.zeros(NT)
    for offset in range(1, NT):
        angle = np.pi * offset / NT
        parity = -1.0 if offset % 2 == 0 else 1.0
        table[offset] = 0.5 * OMEGA_BLADE * parity * np.cos(angle) / np.sin(angle)
    return [float(np.float32(value)) for value in table]


def plane_masks():
    row_index = lax.broadcasted_iota(jnp.int32, (ROWS, LANES), 0)
    return row_index < 4, (row_index & 2) == 0, row_index & 1


def both(first_var, plane):
    turned = pltpu.roll(plane, 4, 0)
    return jnp.where(first_var, plane, turned), jnp.where(first_var, turned, plane)


def primitives(first_var, planes):
    density, moment_x = both(first_var, planes[0])
    moment_y, moment_z = both(first_var, planes[1])
    energy = jnp.where(first_var, planes[2], pltpu.roll(planes[2], 4, 0))
    inverse = 1.0 / density
    velocity_x = moment_x * inverse
    velocity_y = moment_y * inverse
    velocity_z = moment_z * inverse
    kinetic = moment_x * velocity_x + moment_y * velocity_y + moment_z * velocity_z
    pressure = (GAMMA_GAS - 1.0) * (energy - 0.5 * kinetic)
    sound = jnp.sqrt(GAMMA_GAS * pressure * inverse)
    return velocity_x, velocity_y, pressure, sound


def rows_of(var, inst, half):
    return (var // 2) * ROWS + (var % 2) * 4 + inst * 2 + half


def pack_kernel(
    held_state_ref, held_rate_ref, held_next_ref, held_codes_ref, out_ref, next_ref, codes_ref,
    state_ref, rate_ref, sems,
):
    copies = [
        pltpu.make_async_copy(source, target, sems.at[k])
        for k, (source, target) in enumerate(
            (
                (held_state_ref, state_ref),
                (held_rate_ref, rate_ref),
                (held_next_ref, next_ref),
                (held_codes_ref, codes_ref),
            )
        )
    ]
    for copy in copies:
        copy.start()
    for copy in copies:
        copy.wait()
    mirrored = lax.axis_index("cell") // (lax.axis_size("cell") // 2)
    for cell in range(2):
        place = pl.multiple_of(jnp.bitwise_xor(cell, mirrored) * CELL_ROWS, ROWS)
        for k in range(PAIRS):
            rows = [
                state_ref[inst, 2 * k + var, pl.ds(cell, 1), pl.ds(half * LANES, LANES)]
                for var in range(2)
                for inst in range(2)
                for half in range(2)
            ]
            for row, values in enumerate(rows):
                out_ref[0, pl.ds(place + (k * ROWS + row), 1), :] = values
    rates = [
        rate_ref[pl.ds(cell, 1), pl.ds(half * LANES, LANES)]
        for cell in range(2)
        for half in range(2)
    ]
    for row in range(4):
        out_ref[0, pl.ds(RATE_ROW + row, 1), :] = jnp.where(
            mirrored == 0, rates[row], rates[row ^ 2]
        )
    out_ref[0, pl.ds(RATE_ROW + 4, 4), :] = jnp.zeros((4, LANES), jnp.float32)
    for row in range(0, BLOCK_ROWS, ROWS):
        values = out_ref[0, pl.ds(row, ROWS), :]
        for copy in range(1, out_ref.shape[0]):
            out_ref[copy, pl.ds(row, ROWS), :] = values


def turn_insts(first_inst, plane):
    return jnp.where(first_inst, pltpu.roll(plane, 6, 0), pltpu.roll(plane, 2, 0))


def time_weights(first_inst, shift):
    offsets = spectral_offsets()
    other = jnp.where(
        first_inst, offsets[(2 * shift + 1) % NT], offsets[(2 * shift - 1) % NT]
    )
    return offsets[(2 * shift) % NT], other


def at_block(ref, y, block):
    blocks = ref.shape[1]
    mirrored = lax.axis_index("cell") // blocks
    place = mirrored * block + (1 - mirrored) * (blocks - 1 - block)
    return ref.at[ref.shape[0] - 1 - y, place]


def cell_plane(ref, y, cell, k):
    return at_block(ref, y, cell // 2)[pl.ds((cell % 2) * CELL_ROWS + k * ROWS, ROWS), :]


def partner_kernel(all_ref, out_ref):
    own_inst = lax.axis_index("inst")
    own_y, core = own_inst >> 1, own_inst & 1
    _, first_inst, _ = plane_masks()
    one, three = time_weights(first_inst, 1), time_weights(first_inst, 3)
    near = [jnp.where(core == 0, a, b) for a, b in zip(one, three)]
    away = [jnp.where(core == 0, b, a) for a, b in zip(one, three)]
    cells = 2 * all_ref.shape[1]
    for cell in range(cells):
        for k in range(PAIRS):
            here = cell_plane(all_ref, own_y, cell, k)
            there = cell_plane(all_ref, 1 - own_y, cell, k)
            out_ref[pl.ds(cell * CELL_ROWS + k * ROWS, ROWS), :] = (
                near[0] * here
                + away[0] * there
                + turn_insts(first_inst, near[1] * here + away[1] * there)
            )


def two_by_two(first, second):
    def entry(a, b, c, d):
        terms = [x * y for x, y in ((a, b), (c, d)) if x is not None and y is not None]
        return None if not terms else terms[0] if len(terms) == 1 else terms[0] + terms[1]

    return (
        entry(first[0], second[0], first[1], second[2]),
        entry(first[0], second[1], first[1], second[3]),
        entry(first[2], second[0], first[3], second[2]),
        entry(first[2], second[1], first[3], second[3]),
    )


def inverse_of(matrix):
    reciprocal = 1.0 / (matrix[0] * matrix[3] - matrix[1] * matrix[2])
    return (
        matrix[3] * reciprocal,
        -(matrix[1] * reciprocal),
        -(matrix[2] * reciprocal),
        matrix[0] * reciprocal,
    )


def less(first, second):
    return tuple(a if b is None else a - b for a, b in zip(first, second))


def minus(members):
    return tuple(None if a is None else -a for a in members)


def matrix_vector(matrix, low, high):
    def row(a, b):
        terms = [x * y for x, y in ((a, low), (b, high)) if x is not None]
        return terms[0] if len(terms) == 1 else terms[0] + terms[1]

    return row(matrix[0], matrix[1]), row(matrix[2], matrix[3])


def apply_matrix(matrix, side):
    parts = [matrix_vector(matrix, side[k], side[PAIRS + k]) for k in range(PAIRS)]
    return [low for low, _ in parts] + [high for _, high in parts]


def difference(first, second):
    return [a - b for a, b in zip(first, second)]


def flux_along(first_var, planes, velocity, pressure, sign):
    normal = sign * velocity
    return [
        planes[0] * normal + jnp.where(first_var, 0.0, sign * pressure),
        planes[1] * normal,
        planes[2] * normal + jnp.where(first_var, pressure * normal, 0.0),
    ]


class LineCells:
    def __init__(self, first_var, sign):
        self.first_var, self.sign = first_var, sign
        self.state, self.pressure, self.radius = {}, {}, {}
        self.flux, self.step, self.sensor = {}, {}, {}

    def add(self, cell, planes, velocity, pressure, sound):
        self.state[cell], self.pressure[cell] = planes, pressure
        self.radius[cell] = jnp.abs(velocity) + sound
        self.flux[cell] = flux_along(self.first_var, planes, velocity, pressure, self.sign)
        if cell - 1 in self.state:
            self.step[cell - 1] = difference(planes, self.state[cell - 1])
        if cell - 2 in self.state:
            twice = 2.0 * self.pressure[cell - 1]
            outer = pressure + self.pressure[cell - 2]
            self.sensor[cell - 1] = jnp.abs(outer - twice) / (outer + twice)

    def face(self, cell):
        second = SENSOR_GAIN * jnp.maximum(self.sensor[cell], self.sensor[cell + 1])
        fourth = jnp.maximum(0.0, FOURTH_GAIN - second)
        face_radius = 0.5 * (self.radius[cell] + self.radius[cell + 1])
        near_weight = face_radius * (second + 2.0 * fourth)
        far_weight = face_radius * fourth
        return [
            0.5 * (self.flux[cell][k] + self.flux[cell + 1][k])
            - (
                near_weight * self.step[cell][k]
                - far_weight * (self.step[cell + 1][k] + self.step[cell - 1][k])
            )
            for k in range(PAIRS)
        ]

    def near(self, cell):
        scale = SECOND_IMPL * 0.5 + 2.0 * FOURTH_IMPL
        return -scale * (self.radius[cell] + self.radius[cell + 1])

    def far(self, cell):
        return FOURTH_IMPL * self.radius[cell]

    def middle(self, cell, rate):
        centre, above = self.radius[cell], self.radius[cell + 1]
        if cell == 0:
            total, weighted = centre + (centre + above), 4.0 * centre + above
        else:
            below = self.radius[cell - 1]
            total = (below + centre) + (centre + above)
            weighted = below + 4.0 * centre + above
        result = SECOND_IMPL * (0.5 * total) + FOURTH_IMPL * weighted
        return result if rate is None else rate * centre + result

    def diagonal(self, cell, rates):
        across = self.near(cell)
        return (self.middle(cell, rates[0]), across, across, self.middle(cell + 1, rates[1]))

    def below(self, cell):
        return (self.far(cell - 1), self.near(cell - 1), None, self.far(cell))

    def above(self, cell):
        return (self.far(cell + 1), None, self.near(cell + 1), self.far(cell + 2))


def rates_at(ref, y, block, first_half):
    rows = [at_block(ref, y, block)[pl.ds(RATE_ROW + k, 1), :] for k in range(4)]
    return [jnp.where(first_half, rows[2 * k], rows[2 * k + 1]) for k in range(2)]


def near_half_kernel(all_ref, next_ref, codes_ref, *refs):
    *results, middle_ref, round_ref, third_ref, line_ref = refs
    own_y = lax.axis_index("inst") >> 1
    cells = 2 * all_ref.shape[1]
    for cell in range(cells - MIDDLE_CELLS, cells):
        for k in range(PAIRS):
            row = (cell - (cells - MIDDLE_CELLS)) * CELL_ROWS + k * ROWS
            middle_ref[pl.ds(row, ROWS), :] = cell_plane(all_ref, own_y, cell, k)
    for cell in range(ROUND_CELLS):
        for k in range(PAIRS):
            plane = cell_plane(all_ref, own_y, cells - 1 - cell, k)
            round_ref[pl.ds(cell * CELL_ROWS + k * ROWS, ROWS), :] = plane
    for k in range(PAIRS):
        third = cell_plane(all_ref, own_y, cells - MIDDLE_CELLS - 1, k)
        third_ref[pl.ds(k * ROWS, ROWS), :] = third

    @pl.when(lax.axis_index("cell") < all_ref.shape[1])
    def _():
        half_kernel(all_ref, next_ref, codes_ref, *results, line_ref)


def far_half_kernel(all_ref, next_ref, codes_ref, *refs):
    *refs, line_ref = refs
    given, results = refs[: len(refs) // 2], refs[len(refs) // 2 :]
    far = lax.axis_index("cell") >= all_ref.shape[1]

    @pl.when(far)
    def _():
        half_kernel(all_ref, next_ref, codes_ref, *results, line_ref)

    @pl.when(jnp.logical_not(far))
    def _():
        for source, target in zip(given, results):
            target[...] = source[...]


def half_kernel(
    all_ref, next_ref, codes_ref, partial_ref, factor_ref, blocks_ref, correction_ref,
    line_ref,
):
    own_y = lax.axis_index("inst") >> 1
    blocks = all_ref.shape[1]
    cells = 2 * blocks
    mirrored = lax.axis_index("cell") // blocks
    sign = (1 - 2 * mirrored).astype(jnp.float32)
    shape = (ROWS, LANES)
    lane_index = lax.broadcasted_iota(jnp.int32, shape, 1)
    first_var, first_inst, half_index = plane_masks()
    first_half = half_index == 0
    zero = jnp.zeros(shape, jnp.float32)

    next_rows = [
        next_ref[pl.ds(half * LANES, LANES)].reshape(1, LANES) for half in range(2)
    ]
    next_line = jnp.where(first_half, next_rows[0], next_rows[1])
    column = lax.broadcasted_iota(jnp.int32, (LANES, LANES), 0)
    prev_halves = []
    for target in range(2):
        total = None
        for source in range(2):
            hits = jnp.where(column + target * LANES == next_rows[source], 1.0, 0.0)
            names = (lane_index + source * LANES).astype(jnp.float32)
            part = lax.dot_general(
                names, hits, (((1,), (1,)), ((), ())), preferred_element_type=jnp.float32
            )
            total = part if total is None else total + part
        prev_halves.append(total)
    prev_line = jnp.where(first_half, prev_halves[0], prev_halves[1]).astype(jnp.int32)

    def picker(lines):
        lane = lines & (LANES - 1)
        same = (lines >> 7) == half_index

        def pick(plane):
            swapped = jnp.where(first_half, pltpu.roll(plane, 7, 0), pltpu.roll(plane, 1, 0))
            here = jnp.take_along_axis(plane, lane, axis=1, mode="promise_in_bounds")
            there = jnp.take_along_axis(swapped, lane, axis=1, mode="promise_in_bounds")
            return jnp.where(same, here, there)

        return pick

    pick_next = picker(next_line)
    pick_prev = picker(prev_line)

    def loaded(cell, y=own_y):
        return [cell_plane(all_ref, y, cell, k) for k in range(PAIRS)]

    own_weights, away_weights = time_weights(first_inst, 0), time_weights(first_inst, 2)

    def own_time_parts(planes, cell):
        return [
            away_weights[0] * away
            + turn_insts(first_inst, own_weights[1] * own + away_weights[1] * away)
            for own, away in zip(planes, loaded(cell, 1 - own_y))
        ]

    def flux_across(planes, velocity, pressure):
        return [
            planes[0] * velocity,
            planes[1] * velocity + jnp.where(first_var, pressure, 0.0),
            planes[2] * velocity + jnp.where(first_var, pressure * velocity, 0.0),
        ]

    def pitch_flux(planes, velocity_y, pressure, sound):
        nearby = [pick_next(plane) for plane in planes]
        _, next_velocity, next_pressure, next_sound = primitives(first_var, nearby)
        own_flux = flux_across(planes, velocity_y, pressure)
        next_flux = flux_across(nearby, next_velocity, next_pressure)
        weight = (PITCH_GAIN * 0.5) * (
            jnp.abs(velocity_y) + sound + (jnp.abs(next_velocity) + next_sound)
        )
        return [
            0.5 * (a + b) - weight * (n - o)
            for a, b, n, o in zip(own_flux, next_flux, nearby, planes)
        ]

    for cell in range(cells):
        planes = loaded(cell)
        velocity_x, velocity_y, pressure, sound = primitives(first_var, planes)
        line_ref[cell, 0], line_ref[cell, 1], line_ref[cell, 2] = velocity_x, pressure, sound
        faces_across = pitch_flux(planes, velocity_y, pressure, sound)
        times = own_time_parts(planes, cell)
        for k in range(PAIRS):
            partial_ref[cell, k] = -(times[k] + (faces_across[k] - pick_prev(faces_across[k])))

    tile = half_index * (LANES // LINES_DEV) + lane_index // LINES_DEV
    end_codes = jnp.where(mirrored == 0, codes_ref[pl.ds(0, 1), :], codes_ref[pl.ds(1, 1), :])
    codes = jnp.zeros(shape, jnp.int32)
    for k in range(2 * LANES // LINES_DEV):
        codes = jnp.where(tile == k, jnp.broadcast_to(end_codes[:, k : k + 1], shape), codes)

    def ghost(cell):
        planes = loaded(-1 - cell)
        copied = loaded(0)
        result = []
        for k in range(PAIRS):
            reflected = planes[k] if k else jnp.where(first_var, planes[k], -planes[k])
            inflow = jnp.where(first_var, FREE_STATE[2 * k], FREE_STATE[2 * k + 1])
            result.append(
                jnp.where(codes == 0, reflected, jnp.where(codes == 1, inflow, copied[k]))
            )
        return result

    line = LineCells(first_var, sign)
    faces, inverses, aboves = {}, [], []
    for cell in range(-2, cells):
        if cell < 0:
            planes = ghost(cell)
            velocity_x, _, pressure, sound = primitives(first_var, planes)
        else:
            planes = loaded(cell)
            velocity_x, pressure, sound = [line_ref[cell, k] for k in range(3)]
        line.add(cell, planes, velocity_x, pressure, sound)
        if cell >= 1:
            faces[cell - 2] = line.face(cell - 2)
        if cell >= 2:
            at = cell - 2
            for k in range(PAIRS):
                partial_ref[at, k] = partial_ref[at, k] + (faces[at - 1][k] - faces[at][k])
        if cell >= 3 and cell % 2 == 1:
            at = cell - 3
            block = at // 2
            rates = rates_at(all_ref, own_y, block, first_half)
            diag = line.diagonal(at, rates)
            if block > 0:
                factor = two_by_two(line.below(at), inverses[-1])
                diag = less(diag, two_by_two(factor, aboves[-1]))
                for n in range(4):
                    factor_ref[block - 1, n] = factor[n]
            inverses.append(inverse_of(diag))
            aboves.append(line.above(at))
            kept = [*inverses[-1], aboves[-1][0], *aboves[-1][2:]]
            for n, plane in enumerate(kept):
                blocks_ref[block, n] = plane

    last = cells - 2
    for k in range(PAIRS):
        partial_ref[last, k] = partial_ref[last, k] + faces[last - 1][k]
    factor = two_by_two(line.below(last), inverses[-1])
    for n in range(4):
        factor_ref[blocks - 2, n] = factor[n]
    correction = list(two_by_two(factor, aboves[-1]))
    rates = rates_at(all_ref, own_y, blocks - 1, first_half)
    for member in range(2):
        centre = line.radius[last + member]
        correction[3 * member] = correction[3 * member] - rates[member] * centre
    for n in range(2):
        correction_ref[pl.ds(n * ROWS, ROWS), :] = jnp.where(
            first_var, correction[2 * n], correction[2 * n + 1]
        )


def reduce_kernel(
    partial_ref, time_ref, factor_ref, correction_ref, here_ref, third_ref, middle_ref, sides_ref,
    again_ref,
):
    again_ref[...] = here_ref[...]
    middle_ref[pl.ds(THIRD_ROW, CELL_ROWS), :] = third_ref[...]
    for row in range(0, 2 * ROWS, ROWS):
        middle_ref[pl.ds(CORRECTION_ROW + row, ROWS), :] = correction_ref[pl.ds(row, ROWS), :]
    blocks = partial_ref.shape[0] // 2
    side = None
    for block in range(blocks):
        own = []
        for cell in (2 * block, 2 * block + 1):
            for k in range(PAIRS):
                time = time_ref[pl.ds(cell * CELL_ROWS + k * ROWS, ROWS), :]
                own.append(partial_ref[cell, k] - time)
        if block > 0:
            factor = [factor_ref[block - 1, n] for n in range(4)]
            own = difference(own, apply_matrix(factor, side))
        side = own
        for n, plane in enumerate(side):
            if block < blocks - 1:
                sides_ref[block, n] = plane
            else:
                middle_ref[pl.ds(n * ROWS, ROWS), :] = plane


def spread_kernel(all_ref, blocks_ref, sides_ref, known_ref, spread_ref, table_ref):
    own_y = lax.axis_index("inst") >> 1
    blocks = all_ref.shape[1]
    own_cell = lax.axis_index("cell")
    own_block = jnp.where(own_cell < blocks, own_cell, 2 * blocks - 1 - own_cell)
    zero = jnp.zeros((ROWS, LANES), jnp.float32)
    known, spread = [zero] * (2 * PAIRS), (zero + 1.0, zero, zero, zero + 1.0)
    for block in range(blocks - 1, -1, -1):
        if block < blocks - 1:
            kept = [blocks_ref[block, n] for n in range(7)]
            inverse, above = kept[:4], (kept[4], None, kept[5], kept[6])
            side = [sides_ref[block, n] for n in range(2 * PAIRS)]
            step = two_by_two(inverse, above)
            own = apply_matrix(inverse, side)
            if block < blocks - 2:
                known = difference(own, apply_matrix(step, known))
                spread = minus(two_by_two(step, spread))
            else:
                known, spread = own, minus(step)
        for n, plane in enumerate(known + list(spread)):
            table_ref[block, n] = plane
    for n in range(2 * PAIRS):
        base = at_block(all_ref, own_y, own_block)[pl.ds(n * ROWS, ROWS), :]
        known_ref[n] = base + table_ref[own_block, n]
    for n in range(4):
        spread_ref[n] = table_ref[own_block, 2 * PAIRS + n]


def plane_of(ref, row):
    return ref[pl.ds(row, ROWS), :]


def correction_of(first_var, ref):
    pairs = [both(first_var, plane_of(ref, CORRECTION_ROW + n * ROWS)) for n in range(2)]
    return [pairs[0][0], pairs[0][1], pairs[1][0], pairs[1][1]]


def middle_kernel(
    here_ref, first_ref, second_ref, here_side_ref, there_side_ref, side_ref, other_ref, matrix_ref
):
    own_cell, count = lax.axis_index("cell"), lax.axis_size("cell")
    mirrored = own_cell // (count // 2)
    outer = jnp.logical_or(own_cell < count // 4, own_cell >= count - count // 4)
    sign = (1 - 2 * mirrored).astype(jnp.float32)
    first_var, _, _ = plane_masks()
    line = LineCells(first_var, sign)
    for cell in range(6):
        at = cell if cell < 3 else 5 - cell
        rows = [(at - 1) * CELL_ROWS + k * ROWS for k in range(PAIRS)]
        if at == 0:
            ref = here_side_ref if cell < 3 else there_side_ref
            planes = [plane_of(ref, THIRD_ROW + k * ROWS) for k in range(PAIRS)]
        elif cell < 3:
            planes = [plane_of(here_ref, row) for row in rows]
        else:
            planes = [
                jnp.where(
                    outer,
                    plane_of(first_ref, (2 - at) * CELL_ROWS + k * ROWS),
                    plane_of(second_ref, row),
                )
                for k, row in enumerate(rows)
            ]
        velocity_x, _, pressure, sound = primitives(first_var, planes)
        line.add(cell, planes, velocity_x, pressure, sound)
    faces = {cell: line.face(cell) for cell in (1, 2, 3)}
    for k in range(PAIRS):
        side_ref[k] = plane_of(here_side_ref, k * ROWS) - faces[1][k]
        side_ref[PAIRS + k] = plane_of(here_side_ref, (PAIRS + k) * ROWS) + (
            faces[1][k] - faces[2][k]
        )
        other_ref[k] = plane_of(there_side_ref, (PAIRS + k) * ROWS) + (
            faces[2][k] - faces[3][k]
        )
        other_ref[PAIRS + k] = plane_of(there_side_ref, k * ROWS) + faces[3][k]
    no_rates = (None, None)
    diag = difference(line.diagonal(1, no_rates), correction_of(first_var, here_side_ref))
    above, below = line.above(1), line.below(3)
    kept = [*diag, *line.diagonal(3, no_rates), above[0], *above[2:], *below[:2], below[3]]
    for n, plane in enumerate(kept):
        matrix_ref[n] = plane


def join_kernel(
    side_ref, other_ref, matrix_ref, there_side_ref, known_ref, spread_ref, out_ref
):
    mirrored = lax.axis_index("cell") // (lax.axis_size("cell") // 2)
    first_var, _, _ = plane_masks()
    kept = [matrix_ref[n] for n in range(14)]
    diag, other_diag = kept[:4], kept[4:8]
    above, below = (kept[8], None, kept[9], kept[10]), (kept[11], kept[12], None, kept[13])
    other_diag = difference(other_diag, correction_of(first_var, there_side_ref)[::-1])
    other = [other_ref[n] for n in range(2 * PAIRS)]
    factor = two_by_two(above, inverse_of(other_diag))
    diag = less(diag, two_by_two(factor, below))
    side = [side_ref[n] for n in range(2 * PAIRS)]
    middle = apply_matrix(inverse_of(diag), difference(side, apply_matrix(factor, other)))
    moved = apply_matrix([spread_ref[n] for n in range(4)], middle)
    results = [known_ref[n] + moved[n] for n in range(2 * PAIRS)]
    for cell in range(2):
        for k in range(PAIRS):
            first, second = results[cell * PAIRS + k], results[(1 - cell) * PAIRS + k]
            result = jnp.where(mirrored == 0, first, second)
            for var in range(2):
                for inst in range(2):
                    for half in range(2):
                        row = rows_of(var, inst, half)
                        out_ref[
                            inst, 2 * k + var, pl.ds(cell, 1), pl.ds(half * LANES, LANES)
                        ] = result[row : row + 1]


def share_half(copies):
    insts, count = lax.axis_size("inst"), lax.axis_size("cell")
    halves = [range(count // 2 - 1, -1, -1), range(count - 1, count // 2 - 1, -1)]
    groups = [
        [inst * count + cell for inst in range(insts - 2 + core, -1, -2) for cell in half]
        for core in range(2)
        for half in halves
    ]
    return lax.all_to_all(
        copies, ("inst", "cell"), split_axis=0, concat_axis=0, tiled=True,
        axis_index_groups=groups,
    )


def swap_cores(block):
    pairs = [(inst, inst ^ 1) for inst in range(lax.axis_size("inst"))]
    return lax.ppermute(block, "inst", pairs)


def swap_halves(block):
    count = lax.axis_size("cell")
    return lax.ppermute(block, "cell", [(i, (i + count // 2) % count) for i in range(count)])


def pass_round(block, steps):
    width = lax.axis_size("cell") // 4
    pairs = [
        (source * width + i, target * width + (i + (source == target)) % width)
        for source, target in steps
        for i in range(width)
    ]
    return lax.ppermute(block, "cell", pairs)


FIRST_ROUND = ((2, 0), (0, 1), (1, 3), (3, 2))
SECOND_ROUND = ((3, 1), (1, 2), (2, 3), (0, 0))


def float_shape(*sizes):
    return jax.ShapeDtypeStruct(sizes, jnp.float32)


def local_by_halves(state, pseudo_rate, line_next, face_codes):
    blocks = lax.axis_size("cell") // 2
    cells = 2 * blocks
    vmem = pl.BlockSpec(memory_space=pltpu.VMEM)
    plane = (ROWS, LANES)
    params = pltpu.CompilerParams(vmem_limit_bytes=VMEM_BYTES)
    places = lax.axis_size("inst") // 2
    held = [
        pltpu.with_memory_space_constraint(array, pltpu.HBM)
        for array in (state, pseudo_rate, line_next, face_codes)
    ]
    packed, next_here, codes_here = pl.pallas_call(
        pack_kernel,
        out_shape=(
            float_shape(places * blocks, BLOCK_ROWS, LANES),
            jax.ShapeDtypeStruct(line_next.shape, jnp.int32),
            jax.ShapeDtypeStruct(face_codes.shape, jnp.int32),
        ),
        in_specs=[pl.BlockSpec(memory_space=pltpu.HBM)] * 4,
        out_specs=(vmem, vmem, vmem),
        scratch_shapes=[
            pltpu.VMEM(state.shape, jnp.float32),
            pltpu.VMEM(pseudo_rate.shape, jnp.float32),
            pltpu.SemaphoreType.DMA((4,)),
        ],
        compiler_params=params,
    )(*held)
    shared = share_half(packed).reshape(places, blocks, BLOCK_ROWS, LANES)
    for_partner = pl.pallas_call(
        partner_kernel,
        out_shape=float_shape(cells * CELL_ROWS, LANES),
        in_specs=[vmem],
        out_specs=vmem,
        compiler_params=params,
    )(shared)
    from_partner = swap_cores(for_partner)
    beside = pl.CostEstimate(flops=10**6, bytes_accessed=10**6, transcendentals=0)
    kinds = (
        float_shape(cells, PAIRS, *plane),
        float_shape(blocks - 1, 4, *plane),
        float_shape(blocks - 1, 7, *plane),
        float_shape(2 * ROWS, LANES),
    )
    line_scratch = [pltpu.VMEM((cells, 3) + plane, jnp.float32)]
    arguments = (shared, next_here, codes_here)
    *near, here, for_round, third = pl.pallas_call(
        near_half_kernel,
        out_shape=kinds
        + (
            float_shape(MIDDLE_CELLS * CELL_ROWS, LANES),
            float_shape(ROUND_CELLS * CELL_ROWS, LANES),
            float_shape(CELL_ROWS, LANES),
        ),
        in_specs=[vmem] * 3,
        out_specs=(vmem,) * 7,
        scratch_shapes=line_scratch,
        compiler_params=params,
    )(*arguments)
    there_first = pass_round(for_round, FIRST_ROUND)
    partial, factors, eliminated, correction = pl.pallas_call(
        far_half_kernel,
        out_shape=kinds,
        in_specs=[vmem] * 7,
        out_specs=(vmem,) * 4,
        scratch_shapes=line_scratch,
        input_output_aliases={3 + n: n for n in range(4)},
        compiler_params=params,
        cost_estimate=beside,
    )(*arguments, *near)
    here_side, sides, here_again = pl.pallas_call(
        reduce_kernel,
        out_shape=(
            float_shape(SIDE_ROWS, LANES),
            float_shape(blocks - 1, 2 * PAIRS, *plane),
            float_shape(MIDDLE_CELLS * CELL_ROWS, LANES),
        ),
        in_specs=[vmem] * 6,
        out_specs=(vmem,) * 3,
        compiler_params=params,
    )(partial, from_partner, factors, correction, here, third)
    there_side = swap_halves(here_side)
    there_second = pass_round(here_again, SECOND_ROUND)
    known, spread = pl.pallas_call(
        spread_kernel,
        out_shape=(float_shape(2 * PAIRS, *plane), float_shape(4, *plane)),
        in_specs=[vmem] * 3,
        out_specs=(vmem, vmem),
        scratch_shapes=[pltpu.VMEM((blocks, 2 * PAIRS + 4) + plane, jnp.float32)],
        compiler_params=params,
        cost_estimate=beside,
    )(shared, eliminated, sides)
    side, other, matrices = pl.pallas_call(
        middle_kernel,
        out_shape=(
            float_shape(2 * PAIRS, *plane),
            float_shape(2 * PAIRS, *plane),
            float_shape(14, *plane),
        ),
        in_specs=[vmem] * 5,
        out_specs=(vmem,) * 3,
        compiler_params=params,
    )(here, there_first, there_second, here_side, there_side)
    return pl.pallas_call(
        join_kernel,
        out_shape=float_shape(*state.shape),
        in_specs=[vmem] * 6,
        out_specs=vmem,
        compiler_params=params,
    )(side, other, matrices, there_side, known, spread)


def solution(mesh):
    placed = (P("inst", None, "cell", None), P("cell", None), P(), P())
    inst_count, cell_count = mesh.shape["inst"], mesh.shape["cell"]

    def local(state, pseudo_rate, line_next, face_codes):
        small = (
            state.shape == (2, 6, 2, 2 * LANES)
            and inst_count * 2 == NT
            and cell_count == 8
            and face_codes.shape[1] * LINES_DEV == state.shape[3]
        )
        chosen = local_by_halves if small else local_by_lines
        return chosen(state, pseudo_rate, line_next, face_codes)

    return jax.shard_map(
        local, mesh=mesh, in_specs=placed, out_specs=P("inst", None, "cell", None), check_vma=False
    )
```

```python
import functools

import jax
import jax.numpy as jnp
import numpy as np
from jax import lax
from jax.experimental import pallas as pl
from jax.experimental.pallas import tpu as pltpu
from jax.sharding import PartitionSpec as P

NT = 8
LINES_DEV = 32


GAMMA_GAS = 1.4
OMEGA_BLADE = 1.0
SENSOR_GAIN = 0.25
FOURTH_GAIN = 0.03125
PITCH_GAIN = 0.5
SECOND_IMPL = 1.0
FOURTH_IMPL = 0.25
FREE_STATE = (1.0, 0.5, 0.0, 0.0, 2.625, 0.2)
MIRROR_SIGNS = (1.0, -1.0, 1.0, 1.0, 1.0, 1.0)
ZERO_BLOCK = (0.0, 0.0, 0.0, 0.0)
UNIT_BLOCK = (1.0, 0.0, 0.0, 1.0)
ZERO_PAIR = (0.0, 0.0)


def extended(block, sides, width):
    for axis, dim in sides:
        count = lax.axis_size(axis)
        forward = [(i, i + 1) for i in range(count - 1)]
        backward = [(target, source) for source, target in forward]
        low = lax.ppermute(
            lax.slice_in_dim(block, block.shape[dim] - width, None, axis=dim), axis, forward
        )
        high = lax.ppermute(lax.slice_in_dim(block, 0, width, axis=dim), axis, backward)
        block = jnp.concatenate([low, block, high], axis=dim)
    return block


def spectral_matrix(instances):
    offsets = np.arange(instances)[:, None] - np.arange(instances)[None, :]
    angles = np.pi * offsets / instances
    safe_sin = np.where(offsets == 0, 1.0, np.sin(angles))
    parity = np.where(np.mod(offsets, 2) == 0, -1.0, 1.0)
    matrix_table = np.where(
        offsets == 0, 0.0, 0.5 * OMEGA_BLADE * parity * np.cos(angles) / safe_sin
    )
    return jnp.asarray(matrix_table, jnp.float32)


def primitive_parts(cells_state):
    density = cells_state[..., 0, :, :]
    inverse = 1.0 / density
    velocity_x = cells_state[..., 1, :, :] * inverse
    velocity_y = cells_state[..., 2, :, :] * inverse
    velocity_z = cells_state[..., 3, :, :] * inverse
    energy = cells_state[..., 4, :, :]
    pressure = (GAMMA_GAS - 1.0) * (
        energy
        - 0.5
        * density
        * (velocity_x * velocity_x + velocity_y * velocity_y + velocity_z * velocity_z)
    )
    sound_speed = jnp.sqrt(GAMMA_GAS * pressure * inverse)
    return (velocity_x, velocity_y, pressure, sound_speed)


def directed_flux(cells_state, normal_velocity, pressure, component):
    zero_plane = jnp.zeros_like(pressure)
    pressure_rows = [
        zero_plane,
        zero_plane,
        zero_plane,
        zero_plane,
        pressure * normal_velocity,
        zero_plane,
    ]
    pressure_rows[component] = pressure
    return cells_state * normal_velocity[..., None, :, :] + jnp.stack(pressure_rows, axis=-3)


def line_residual(padded):
    velocity_x, velocity_y, pressure, sound_speed = primitive_parts(padded)
    flux_line = directed_flux(padded, velocity_x, pressure, 1)
    radius = jnp.abs(velocity_x) + sound_speed
    sensor = jnp.abs(
        pressure[..., 2:, :] - 2.0 * pressure[..., 1:-1, :] + pressure[..., :-2, :]
    ) / (pressure[..., 2:, :] + 2.0 * pressure[..., 1:-1, :] + pressure[..., :-2, :])
    second = SENSOR_GAIN * jnp.maximum(sensor[..., :-1, :], sensor[..., 1:, :])
    fourth = jnp.maximum(0.0, FOURTH_GAIN - second)
    face_radius = 0.5 * (radius[..., 1:-2, :] + radius[..., 2:-1, :])
    left_far = padded[..., :-3, :]
    left_near = padded[..., 1:-2, :]
    right_near = padded[..., 2:-1, :]
    right_far = padded[..., 3:, :]
    damping = face_radius[..., None, :, :] * (
        second[..., None, :, :] * (right_near - left_near)
        - fourth[..., None, :, :] * (right_far - 3.0 * right_near + 3.0 * left_near - left_far)
    )
    face_flux = 0.5 * (flux_line[..., 1:-2, :] + flux_line[..., 2:-1, :]) - damping
    return (face_flux[..., 1:, :] - face_flux[..., :-1, :], radius)


def pitch_parts(cells_state):
    velocity_x, velocity_y, pressure, sound_speed = primitive_parts(cells_state)
    return (directed_flux(cells_state, velocity_y, pressure, 2), jnp.abs(velocity_y) + sound_speed)


def pitch_residual(cells_state, next_lines, prev_lines):
    pitch_flux, radius = pitch_parts(cells_state)
    state_next = jnp.take(cells_state, next_lines, axis=-1)
    flux_next, radius_next = pitch_parts(state_next)
    face_flux = 0.5 * (pitch_flux + flux_next) - PITCH_GAIN * (0.5 * (radius + radius_next))[
        ..., None, :, :
    ] * (state_next - cells_state)
    return face_flux - jnp.take(face_flux, prev_lines, axis=-1)


def boundary_cells(edge_pair, line_codes, lower_end):
    reflected = edge_pair[..., ::-1, :] * jnp.asarray(MIRROR_SIGNS, jnp.float32)[:, None, None]
    if lower_end:
        copied = jnp.concatenate([edge_pair[..., :1, :], edge_pair[..., :1, :]], axis=-2)
    else:
        copied = jnp.concatenate([edge_pair[..., 1:, :], edge_pair[..., 1:, :]], axis=-2)
    inflow = jnp.asarray(FREE_STATE, jnp.float32)[:, None, None] + jnp.zeros_like(edge_pair)
    return jnp.where(line_codes == 0, reflected, jnp.where(line_codes == 1, inflow, copied))


def line_coefficients(radius_ext, diagonal_term, positions, total_cells):
    radius_below = radius_ext[..., :-2, :]
    radius_centre = radius_ext[..., 1:-1, :]
    radius_above = radius_ext[..., 2:, :]
    face_below = 0.5 * (radius_below + radius_centre)
    face_above = 0.5 * (radius_centre + radius_above)
    far_low = FOURTH_IMPL * radius_below
    near_low = -SECOND_IMPL * face_below - 2.0 * FOURTH_IMPL * (radius_below + radius_centre)
    middle = (
        diagonal_term
        + SECOND_IMPL * (face_below + face_above)
        + FOURTH_IMPL * (radius_below + 4.0 * radius_centre + radius_above)
    )
    near_high = -SECOND_IMPL * face_above - 2.0 * FOURTH_IMPL * (radius_centre + radius_above)
    far_high = FOURTH_IMPL * radius_above
    column = positions[:, None]
    far_low = jnp.where(column >= 2, far_low, 0.0)
    near_low = jnp.where(column >= 1, near_low, 0.0)
    near_high = jnp.where(column <= total_cells - 2, near_high, 0.0)
    far_high = jnp.where(column <= total_cells - 3, far_high, 0.0)
    return (far_low, near_low, middle, near_high, far_high)


def block_product(first_matrix, second_matrix):
    return (
        first_matrix[0] * second_matrix[0] + first_matrix[1] * second_matrix[2],
        first_matrix[0] * second_matrix[1] + first_matrix[1] * second_matrix[3],
        first_matrix[2] * second_matrix[0] + first_matrix[3] * second_matrix[2],
        first_matrix[2] * second_matrix[1] + first_matrix[3] * second_matrix[3],
    )


def block_inverse(matrix):
    determinant = matrix[0] * matrix[3] - matrix[1] * matrix[2]
    reciprocal = 1.0 / determinant
    return (
        matrix[3] * reciprocal,
        -matrix[1] * reciprocal,
        -matrix[2] * reciprocal,
        matrix[0] * reciprocal,
    )


def block_apply(matrix, vector):
    return (
        matrix[0] * vector[0] + matrix[1] * vector[1],
        matrix[2] * vector[0] + matrix[3] * vector[1],
    )


def add_blocks(first_members, second_members):
    return tuple((a + b for a, b in zip(first_members, second_members)))


def negate(members):
    return tuple((-a for a in members))


def extend_blocks(members, fill_values):
    return tuple(
        (
            jnp.concatenate([m, jnp.full_like(m[..., :1, :], f)], axis=-2)
            for m, f in zip(members, fill_values)
        )
    )


def shift_next(members, fill_values):
    return tuple(
        (
            jnp.concatenate([m[..., 1:, :], jnp.full_like(m[..., :1, :], f)], axis=-2)
            for m, f in zip(members, fill_values)
        )
    )


def shift_prev(members):
    return tuple(
        (jnp.concatenate([jnp.zeros_like(m[..., :1, :]), m[..., :-1, :]], axis=-2) for m in members)
    )


def pair_split(member):
    shaped = member.reshape(member.shape[:-2] + (member.shape[-2] // 2, 2, member.shape[-1]))
    return (shaped[..., 0, :], shaped[..., 1, :])


def split_parity(members):
    halves = [pair_split(m) for m in members]
    return (tuple((h[0] for h in halves)), tuple((h[1] for h in halves)))


def alternate(first_member, second_member):
    stacked = jnp.stack((first_member, second_member), axis=-2)
    return stacked.reshape(
        first_member.shape[:-2] + (2 * first_member.shape[-2], first_member.shape[-1])
    )


def reduce_blocks(sub_blocks, diag_blocks, super_blocks, right_side):
    block_count = diag_blocks[0].shape[-2]
    if block_count == 1:
        return block_apply(block_inverse(diag_blocks), right_side)
    if block_count % 2 == 1:
        sub_blocks = extend_blocks(sub_blocks, ZERO_BLOCK)
        diag_blocks = extend_blocks(diag_blocks, UNIT_BLOCK)
        super_blocks = extend_blocks(super_blocks, ZERO_BLOCK)
        right_side = extend_blocks(right_side, ZERO_PAIR)
    sub_even, sub_odd = split_parity(sub_blocks)
    diag_even, diag_odd = split_parity(diag_blocks)
    super_even, super_odd = split_parity(super_blocks)
    side_even, side_odd = split_parity(right_side)
    inverse_even = block_inverse(diag_even)
    inverse_next = shift_next(inverse_even, UNIT_BLOCK)
    sub_next = shift_next(sub_even, ZERO_BLOCK)
    super_next = shift_next(super_even, ZERO_BLOCK)
    side_next = shift_next(side_even, ZERO_PAIR)
    left_factor = negate(block_product(sub_odd, inverse_even))
    right_factor = negate(block_product(super_odd, inverse_next))
    reduced_sub = block_product(left_factor, sub_even)
    reduced_diag = add_blocks(
        diag_odd,
        add_blocks(block_product(left_factor, super_even), block_product(right_factor, sub_next)),
    )
    reduced_super = block_product(right_factor, super_next)
    reduced_side = add_blocks(
        side_odd,
        add_blocks(block_apply(left_factor, side_even), block_apply(right_factor, side_next)),
    )
    odd_values = reduce_blocks(reduced_sub, reduced_diag, reduced_super, reduced_side)
    before_values = shift_prev(odd_values)
    remainder = add_blocks(
        side_even,
        negate(
            add_blocks(block_apply(sub_even, before_values), block_apply(super_even, odd_values))
        ),
    )
    even_values = block_apply(inverse_even, remainder)
    merged = tuple((alternate(e, o) for e, o in zip(even_values, odd_values)))
    return tuple((m[..., :block_count, :] for m in merged))


def cells_leading(block):
    moved = jnp.transpose(block, (2, 0, 1, 3))
    return moved.reshape(block.shape[2], block.shape[0] * block.shape[1] * block.shape[3])


def solve_in_lanes(coefficients, line_source):
    source_shape = line_source.shape
    lane_coef = [cells_leading(jnp.broadcast_to(c[:, None], source_shape)) for c in coefficients]
    pairs_list = [pair_split(m) for m in lane_coef]
    zero_plane = jnp.zeros_like(pairs_list[2][0])
    sub_blocks = (pairs_list[0][0], pairs_list[1][0], zero_plane, pairs_list[0][1])
    diag_blocks = (pairs_list[2][0], pairs_list[3][0], pairs_list[1][1], pairs_list[2][1])
    super_blocks = (pairs_list[4][0], zero_plane, pairs_list[3][1], pairs_list[4][1])
    values = reduce_blocks(
        sub_blocks, diag_blocks, super_blocks, pair_split(cells_leading(line_source))
    )
    flat = alternate(values[0], values[1])
    shaped = flat.reshape(source_shape[2], source_shape[0], source_shape[1], source_shape[3])
    return jnp.transpose(shaped, (1, 2, 0, 3))


def return_tiles(line_values):
    return lax.all_to_all(line_values, "cell", split_axis=2, concat_axis=3, tiled=True)


def local_by_lines(state, pseudo_rate, line_next, face_codes):
    local_count = state.shape[0]
    tile_cells = state.shape[2]
    cell_index = lax.axis_index("cell")
    cell_count = lax.axis_size("cell")
    total_cells = tile_cells * cell_count
    spectral = spectral_matrix(NT)
    first_local = lax.axis_index("inst") * local_count
    own_rows = lax.dynamic_slice_in_dim(spectral, first_local, local_count, 0)
    shard_block = jax.tree.map(lambda a: lax.all_gather(a, "inst", axis=0, tiled=True), state)
    columns = lax.slice_in_dim(own_rows, 0, shard_block.shape[0], axis=1)
    time_term = jnp.zeros_like(state) + jnp.einsum(
        "nm,mvil->nvil", columns, shard_block, precision=lax.Precision.HIGHEST
    )
    padded = extended(state, (("cell", 2),), 2)
    codes_lines = jnp.repeat(face_codes, LINES_DEV, axis=1)
    lower_ghost = boundary_cells(state[:, :, 0:2, :], codes_lines[0], True)
    upper_ghost = boundary_cells(state[:, :, -2:, :], codes_lines[1], False)
    lower_rim = jnp.where(cell_index == 0, lower_ghost, padded[:, :, :2, :])
    upper_rim = jnp.where(cell_index == cell_count - 1, upper_ghost, padded[:, :, -2:, :])
    padded = jnp.concatenate([lower_rim, padded[:, :, 2:-2, :], upper_rim], axis=2)
    line_part, radius = line_residual(padded)
    prev_lines = (
        jnp.zeros_like(line_next).at[line_next].set(jnp.arange(line_next.shape[0], dtype=jnp.int32))
    )
    residual = line_part + pitch_residual(state, line_next, prev_lines) + time_term
    right_side = -residual
    centre_radius = radius[:, 2:-2, :]
    diagonal_term = pseudo_rate * centre_radius
    positions = cell_index * tile_cells + jnp.arange(-1, tile_cells + 1, dtype=jnp.int32)
    inside = (positions >= 0) & (positions < total_cells)
    radius_ext = jnp.where(inside[:, None], radius[:, 1:-1, :], 0.0)
    coefficients = line_coefficients(radius_ext, diagonal_term, positions[1:-1], total_cells)
    stacked = jnp.stack(coefficients, axis=1)
    line_source = lax.all_to_all(right_side, "cell", split_axis=3, concat_axis=2, tiled=True)
    line_coef = lax.all_to_all(stacked, "cell", split_axis=3, concat_axis=2, tiled=True)
    update = return_tiles(solve_in_lanes(tuple((line_coef[:, k] for k in range(5))), line_source))
    return state + update


LANES = 128
ROWS = 8
PAIRS = 3
CELL_ROWS = PAIRS * ROWS
RATE_ROW = 2 * CELL_ROWS
VMEM_BYTES = 8 * 2**20
BLOCK_ROWS = RATE_ROW + ROWS

MIDDLE_CELLS = 2
ROUND_CELLS = 4
CORRECTION_ROW = 2 * CELL_ROWS
THIRD_ROW = CORRECTION_ROW + 2 * ROWS
SIDE_ROWS = THIRD_ROW + CELL_ROWS


def spectral_offsets():
    table = np.zeros(NT)
    for offset in range(1, NT):
        angle = np.pi * offset / NT
        parity = -1.0 if offset % 2 == 0 else 1.0
        table[offset] = 0.5 * OMEGA_BLADE * parity * np.cos(angle) / np.sin(angle)
    return [float(np.float32(value)) for value in table]


def plane_masks():
    row_index = lax.broadcasted_iota(jnp.int32, (ROWS, LANES), 0)
    return row_index < 4, (row_index & 2) == 0, row_index & 1


def both(first_var, plane):
    turned = pltpu.roll(plane, 4, 0)
    return jnp.where(first_var, plane, turned), jnp.where(first_var, turned, plane)


def primitives(first_var, planes):
    density, moment_x = both(first_var, planes[0])
    moment_y, moment_z = both(first_var, planes[1])
    energy = jnp.where(first_var, planes[2], pltpu.roll(planes[2], 4, 0))
    inverse = 1.0 / density
    velocity_x = moment_x * inverse
    velocity_y = moment_y * inverse
    velocity_z = moment_z * inverse
    kinetic = moment_x * velocity_x + moment_y * velocity_y + moment_z * velocity_z
    pressure = (GAMMA_GAS - 1.0) * (energy - 0.5 * kinetic)
    sound = jnp.sqrt(GAMMA_GAS * pressure * inverse)
    return velocity_x, velocity_y, pressure, sound


def rows_of(var, inst, half):
    return (var // 2) * ROWS + (var % 2) * 4 + inst * 2 + half


def pack_kernel(
    held_state_ref, held_rate_ref, held_next_ref, held_codes_ref, out_ref, next_ref, codes_ref,
    state_ref, rate_ref, sems,
):
    copies = [
        pltpu.make_async_copy(source, target, sems.at[k])
        for k, (source, target) in enumerate(
            (
                (held_state_ref, state_ref),
                (held_rate_ref, rate_ref),
                (held_next_ref, next_ref),
                (held_codes_ref, codes_ref),
            )
        )
    ]
    for copy in copies:
        copy.start()
    for copy in copies:
        copy.wait()
    mirrored = lax.axis_index("cell") // (lax.axis_size("cell") // 2)
    for cell in range(2):
        place = pl.multiple_of(jnp.bitwise_xor(cell, mirrored) * CELL_ROWS, ROWS)
        for k in range(PAIRS):
            rows = [
                state_ref[inst, 2 * k + var, pl.ds(cell, 1), pl.ds(half * LANES, LANES)]
                for var in range(2)
                for inst in range(2)
                for half in range(2)
            ]
            for row, values in enumerate(rows):
                out_ref[0, pl.ds(place + (k * ROWS + row), 1), :] = values
    rates = [
        rate_ref[pl.ds(cell, 1), pl.ds(half * LANES, LANES)]
        for cell in range(2)
        for half in range(2)
    ]
    for row in range(4):
        out_ref[0, pl.ds(RATE_ROW + row, 1), :] = jnp.where(
            mirrored == 0, rates[row], rates[row ^ 2]
        )
    out_ref[0, pl.ds(RATE_ROW + 4, 4), :] = jnp.zeros((4, LANES), jnp.float32)
    for row in range(0, BLOCK_ROWS, ROWS):
        values = out_ref[0, pl.ds(row, ROWS), :]
        for copy in range(1, out_ref.shape[0]):
            out_ref[copy, pl.ds(row, ROWS), :] = values


def turn_insts(first_inst, plane):
    return jnp.where(first_inst, pltpu.roll(plane, 6, 0), pltpu.roll(plane, 2, 0))


def time_weights(first_inst, shift):
    offsets = spectral_offsets()
    other = jnp.where(
        first_inst, offsets[(2 * shift + 1) % NT], offsets[(2 * shift - 1) % NT]
    )
    return offsets[(2 * shift) % NT], other


def at_block(ref, y, block):
    blocks = ref.shape[1]
    mirrored = lax.axis_index("cell") // blocks
    place = mirrored * block + (1 - mirrored) * (blocks - 1 - block)
    return ref.at[ref.shape[0] - 1 - y, place]


def cell_plane(ref, y, cell, k):
    return at_block(ref, y, cell // 2)[pl.ds((cell % 2) * CELL_ROWS + k * ROWS, ROWS), :]


def partner_kernel(all_ref, out_ref):
    own_inst = lax.axis_index("inst")
    own_y, core = own_inst >> 1, own_inst & 1
    _, first_inst, _ = plane_masks()
    one, three = time_weights(first_inst, 1), time_weights(first_inst, 3)
    near = [jnp.where(core == 0, a, b) for a, b in zip(one, three)]
    away = [jnp.where(core == 0, b, a) for a, b in zip(one, three)]
    cells = 2 * all_ref.shape[1]
    for cell in range(cells):
        for k in range(PAIRS):
            here = cell_plane(all_ref, own_y, cell, k)
            there = cell_plane(all_ref, 1 - own_y, cell, k)
            out_ref[pl.ds(cell * CELL_ROWS + k * ROWS, ROWS), :] = (
                near[0] * here
                + away[0] * there
                + turn_insts(first_inst, near[1] * here + away[1] * there)
            )


def two_by_two(first, second):
    def entry(a, b, c, d):
        terms = [x * y for x, y in ((a, b), (c, d)) if x is not None and y is not None]
        return None if not terms else terms[0] if len(terms) == 1 else terms[0] + terms[1]

    return (
        entry(first[0], second[0], first[1], second[2]),
        entry(first[0], second[1], first[1], second[3]),
        entry(first[2], second[0], first[3], second[2]),
        entry(first[2], second[1], first[3], second[3]),
    )


def inverse_of(matrix):
    reciprocal = 1.0 / (matrix[0] * matrix[3] - matrix[1] * matrix[2])
    return (
        matrix[3] * reciprocal,
        -(matrix[1] * reciprocal),
        -(matrix[2] * reciprocal),
        matrix[0] * reciprocal,
    )


def less(first, second):
    return tuple(a if b is None else a - b for a, b in zip(first, second))


def minus(members):
    return tuple(None if a is None else -a for a in members)


def matrix_vector(matrix, low, high):
    def row(a, b):
        terms = [x * y for x, y in ((a, low), (b, high)) if x is not None]
        return terms[0] if len(terms) == 1 else terms[0] + terms[1]

    return row(matrix[0], matrix[1]), row(matrix[2], matrix[3])


def apply_matrix(matrix, side):
    parts = [matrix_vector(matrix, side[k], side[PAIRS + k]) for k in range(PAIRS)]
    return [low for low, _ in parts] + [high for _, high in parts]


def difference(first, second):
    return [a - b for a, b in zip(first, second)]


def flux_along(first_var, planes, velocity, pressure, sign):
    normal = sign * velocity
    return [
        planes[0] * normal + jnp.where(first_var, 0.0, sign * pressure),
        planes[1] * normal,
        planes[2] * normal + jnp.where(first_var, pressure * normal, 0.0),
    ]


class LineCells:
    def __init__(self, first_var, sign):
        self.first_var, self.sign = first_var, sign
        self.state, self.pressure, self.radius = {}, {}, {}
        self.flux, self.step, self.sensor = {}, {}, {}

    def add(self, cell, planes, velocity, pressure, sound):
        self.state[cell], self.pressure[cell] = planes, pressure
        self.radius[cell] = jnp.abs(velocity) + sound
        self.flux[cell] = flux_along(self.first_var, planes, velocity, pressure, self.sign)
        if cell - 1 in self.state:
            self.step[cell - 1] = difference(planes, self.state[cell - 1])
        if cell - 2 in self.state:
            twice = 2.0 * self.pressure[cell - 1]
            outer = pressure + self.pressure[cell - 2]
            self.sensor[cell - 1] = jnp.abs(outer - twice) / (outer + twice)

    def face(self, cell):
        second = SENSOR_GAIN * jnp.maximum(self.sensor[cell], self.sensor[cell + 1])
        fourth = jnp.maximum(0.0, FOURTH_GAIN - second)
        face_radius = 0.5 * (self.radius[cell] + self.radius[cell + 1])
        near_weight = face_radius * (second + 2.0 * fourth)
        far_weight = face_radius * fourth
        return [
            0.5 * (self.flux[cell][k] + self.flux[cell + 1][k])
            - (
                near_weight * self.step[cell][k]
                - far_weight * (self.step[cell + 1][k] + self.step[cell - 1][k])
            )
            for k in range(PAIRS)
        ]

    def near(self, cell):
        scale = SECOND_IMPL * 0.5 + 2.0 * FOURTH_IMPL
        return -scale * (self.radius[cell] + self.radius[cell + 1])

    def far(self, cell):
        return FOURTH_IMPL * self.radius[cell]

    def middle(self, cell, rate):
        centre, above = self.radius[cell], self.radius[cell + 1]
        if cell == 0:
            total, weighted = centre + (centre + above), 4.0 * centre + above
        else:
            below = self.radius[cell - 1]
            total = (below + centre) + (centre + above)
            weighted = below + 4.0 * centre + above
        result = SECOND_IMPL * (0.5 * total) + FOURTH_IMPL * weighted
        return result if rate is None else rate * centre + result

    def diagonal(self, cell, rates):
        across = self.near(cell)
        return (self.middle(cell, rates[0]), across, across, self.middle(cell + 1, rates[1]))

    def below(self, cell):
        return (self.far(cell - 1), self.near(cell - 1), None, self.far(cell))

    def above(self, cell):
        return (self.far(cell + 1), None, self.near(cell + 1), self.far(cell + 2))


def rates_at(ref, y, block, first_half):
    rows = [at_block(ref, y, block)[pl.ds(RATE_ROW + k, 1), :] for k in range(4)]
    return [jnp.where(first_half, rows[2 * k], rows[2 * k + 1]) for k in range(2)]


def near_half_kernel(all_ref, next_ref, codes_ref, *refs):
    *results, middle_ref, round_ref, third_ref, line_ref = refs
    own_y = lax.axis_index("inst") >> 1
    cells = 2 * all_ref.shape[1]
    for cell in range(cells - MIDDLE_CELLS, cells):
        for k in range(PAIRS):
            row = (cell - (cells - MIDDLE_CELLS)) * CELL_ROWS + k * ROWS
            middle_ref[pl.ds(row, ROWS), :] = cell_plane(all_ref, own_y, cell, k)
    for cell in range(ROUND_CELLS):
        for k in range(PAIRS):
            plane = cell_plane(all_ref, own_y, cells - 1 - cell, k)
            round_ref[pl.ds(cell * CELL_ROWS + k * ROWS, ROWS), :] = plane
    for k in range(PAIRS):
        third = cell_plane(all_ref, own_y, cells - MIDDLE_CELLS - 1, k)
        third_ref[pl.ds(k * ROWS, ROWS), :] = third

    @pl.when(lax.axis_index("cell") < all_ref.shape[1])
    def _():
        half_kernel(all_ref, next_ref, codes_ref, *results, line_ref)


def far_half_kernel(all_ref, next_ref, codes_ref, *refs):
    *refs, line_ref = refs
    given, results = refs[: len(refs) // 2], refs[len(refs) // 2 :]
    far = lax.axis_index("cell") >= all_ref.shape[1]

    @pl.when(far)
    def _():
        half_kernel(all_ref, next_ref, codes_ref, *results, line_ref)

    @pl.when(jnp.logical_not(far))
    def _():
        for source, target in zip(given, results):
            target[...] = source[...]


def half_kernel(
    all_ref, next_ref, codes_ref, partial_ref, factor_ref, blocks_ref, correction_ref,
    line_ref,
):
    own_y = lax.axis_index("inst") >> 1
    blocks = all_ref.shape[1]
    cells = 2 * blocks
    mirrored = lax.axis_index("cell") // blocks
    sign = (1 - 2 * mirrored).astype(jnp.float32)
    shape = (ROWS, LANES)
    lane_index = lax.broadcasted_iota(jnp.int32, shape, 1)
    first_var, first_inst, half_index = plane_masks()
    first_half = half_index == 0
    zero = jnp.zeros(shape, jnp.float32)

    next_rows = [
        next_ref[pl.ds(half * LANES, LANES)].reshape(1, LANES) for half in range(2)
    ]
    next_line = jnp.where(first_half, next_rows[0], next_rows[1])
    column = lax.broadcasted_iota(jnp.int32, (LANES, LANES), 0)
    prev_halves = []
    for target in range(2):
        total = None
        for source in range(2):
            hits = jnp.where(column + target * LANES == next_rows[source], 1.0, 0.0)
            names = (lane_index + source * LANES).astype(jnp.float32)
            part = lax.dot_general(
                names, hits, (((1,), (1,)), ((), ())), preferred_element_type=jnp.float32
            )
            total = part if total is None else total + part
        prev_halves.append(total)
    prev_line = jnp.where(first_half, prev_halves[0], prev_halves[1]).astype(jnp.int32)

    def picker(lines):
        lane = lines & (LANES - 1)
        same = (lines >> 7) == half_index

        def pick(plane):
            swapped = jnp.where(first_half, pltpu.roll(plane, 7, 0), pltpu.roll(plane, 1, 0))
            here = jnp.take_along_axis(plane, lane, axis=1, mode="promise_in_bounds")
            there = jnp.take_along_axis(swapped, lane, axis=1, mode="promise_in_bounds")
            return jnp.where(same, here, there)

        return pick

    pick_next = picker(next_line)
    pick_prev = picker(prev_line)

    def loaded(cell, y=own_y):
        return [cell_plane(all_ref, y, cell, k) for k in range(PAIRS)]

    own_weights, away_weights = time_weights(first_inst, 0), time_weights(first_inst, 2)

    def own_time_parts(planes, cell):
        return [
            away_weights[0] * away
            + turn_insts(first_inst, own_weights[1] * own + away_weights[1] * away)
            for own, away in zip(planes, loaded(cell, 1 - own_y))
        ]

    def flux_across(planes, velocity, pressure):
        return [
            planes[0] * velocity,
            planes[1] * velocity + jnp.where(first_var, pressure, 0.0),
            planes[2] * velocity + jnp.where(first_var, pressure * velocity, 0.0),
        ]

    def pitch_flux(planes, velocity_y, pressure, sound):
        nearby = [pick_next(plane) for plane in planes]
        _, next_velocity, next_pressure, next_sound = primitives(first_var, nearby)
        own_flux = flux_across(planes, velocity_y, pressure)
        next_flux = flux_across(nearby, next_velocity, next_pressure)
        weight = (PITCH_GAIN * 0.5) * (
            jnp.abs(velocity_y) + sound + (jnp.abs(next_velocity) + next_sound)
        )
        return [
            0.5 * (a + b) - weight * (n - o)
            for a, b, n, o in zip(own_flux, next_flux, nearby, planes)
        ]

    for cell in range(cells):
        planes = loaded(cell)
        velocity_x, velocity_y, pressure, sound = primitives(first_var, planes)
        line_ref[cell, 0], line_ref[cell, 1], line_ref[cell, 2] = velocity_x, pressure, sound
        faces_across = pitch_flux(planes, velocity_y, pressure, sound)
        times = own_time_parts(planes, cell)
        for k in range(PAIRS):
            partial_ref[cell, k] = -(times[k] + (faces_across[k] - pick_prev(faces_across[k])))

    tile = half_index * (LANES // LINES_DEV) + lane_index // LINES_DEV
    end_codes = jnp.where(mirrored == 0, codes_ref[pl.ds(0, 1), :], codes_ref[pl.ds(1, 1), :])
    codes = jnp.zeros(shape, jnp.int32)
    for k in range(2 * LANES // LINES_DEV):
        codes = jnp.where(tile == k, jnp.broadcast_to(end_codes[:, k : k + 1], shape), codes)

    def ghost(cell):
        planes = loaded(-1 - cell)
        copied = loaded(0)
        result = []
        for k in range(PAIRS):
            reflected = planes[k] if k else jnp.where(first_var, planes[k], -planes[k])
            inflow = jnp.where(first_var, FREE_STATE[2 * k], FREE_STATE[2 * k + 1])
            result.append(
                jnp.where(codes == 0, reflected, jnp.where(codes == 1, inflow, copied[k]))
            )
        return result

    line = LineCells(first_var, sign)
    faces, inverses, aboves = {}, [], []
    for cell in range(-2, cells):
        if cell < 0:
            planes = ghost(cell)
            velocity_x, _, pressure, sound = primitives(first_var, planes)
        else:
            planes = loaded(cell)
            velocity_x, pressure, sound = [line_ref[cell, k] for k in range(3)]
        line.add(cell, planes, velocity_x, pressure, sound)
        if cell >= 1:
            faces[cell - 2] = line.face(cell - 2)
        if cell >= 2:
            at = cell - 2
            for k in range(PAIRS):
                partial_ref[at, k] = partial_ref[at, k] + (faces[at - 1][k] - faces[at][k])
        if cell >= 3 and cell % 2 == 1:
            at = cell - 3
            block = at // 2
            rates = rates_at(all_ref, own_y, block, first_half)
            diag = line.diagonal(at, rates)
            if block > 0:
                factor = two_by_two(line.below(at), inverses[-1])
                diag = less(diag, two_by_two(factor, aboves[-1]))
                for n in range(4):
                    factor_ref[block - 1, n] = factor[n]
            inverses.append(inverse_of(diag))
            aboves.append(line.above(at))
            kept = [*inverses[-1], aboves[-1][0], *aboves[-1][2:]]
            for n, plane in enumerate(kept):
                blocks_ref[block, n] = plane

    last = cells - 2
    for k in range(PAIRS):
        partial_ref[last, k] = partial_ref[last, k] + faces[last - 1][k]
    factor = two_by_two(line.below(last), inverses[-1])
    for n in range(4):
        factor_ref[blocks - 2, n] = factor[n]
    correction = list(two_by_two(factor, aboves[-1]))
    rates = rates_at(all_ref, own_y, blocks - 1, first_half)
    for member in range(2):
        centre = line.radius[last + member]
        correction[3 * member] = correction[3 * member] - rates[member] * centre
    for n in range(2):
        correction_ref[pl.ds(n * ROWS, ROWS), :] = jnp.where(
            first_var, correction[2 * n], correction[2 * n + 1]
        )


def reduce_kernel(
    partial_ref, time_ref, factor_ref, correction_ref, here_ref, third_ref, middle_ref, sides_ref,
    again_ref,
):
    again_ref[...] = here_ref[...]
    middle_ref[pl.ds(THIRD_ROW, CELL_ROWS), :] = third_ref[...]
    for row in range(0, 2 * ROWS, ROWS):
        middle_ref[pl.ds(CORRECTION_ROW + row, ROWS), :] = correction_ref[pl.ds(row, ROWS), :]
    blocks = partial_ref.shape[0] // 2
    side = None
    for block in range(blocks):
        own = []
        for cell in (2 * block, 2 * block + 1):
            for k in range(PAIRS):
                time = time_ref[pl.ds(cell * CELL_ROWS + k * ROWS, ROWS), :]
                own.append(partial_ref[cell, k] - time)
        if block > 0:
            factor = [factor_ref[block - 1, n] for n in range(4)]
            own = difference(own, apply_matrix(factor, side))
        side = own
        for n, plane in enumerate(side):
            if block < blocks - 1:
                sides_ref[block, n] = plane
            else:
                middle_ref[pl.ds(n * ROWS, ROWS), :] = plane


def spread_kernel(all_ref, blocks_ref, sides_ref, known_ref, spread_ref, table_ref):
    own_y = lax.axis_index("inst") >> 1
    blocks = all_ref.shape[1]
    own_cell = lax.axis_index("cell")
    own_block = jnp.where(own_cell < blocks, own_cell, 2 * blocks - 1 - own_cell)
    zero = jnp.zeros((ROWS, LANES), jnp.float32)
    known, spread = [zero] * (2 * PAIRS), (zero + 1.0, zero, zero, zero + 1.0)
    for block in range(blocks - 1, -1, -1):
        if block < blocks - 1:
            kept = [blocks_ref[block, n] for n in range(7)]
            inverse, above = kept[:4], (kept[4], None, kept[5], kept[6])
            side = [sides_ref[block, n] for n in range(2 * PAIRS)]
            step = two_by_two(inverse, above)
            own = apply_matrix(inverse, side)
            if block < blocks - 2:
                known = difference(own, apply_matrix(step, known))
                spread = minus(two_by_two(step, spread))
            else:
                known, spread = own, minus(step)
        for n, plane in enumerate(known + list(spread)):
            table_ref[block, n] = plane
    for n in range(2 * PAIRS):
        base = at_block(all_ref, own_y, own_block)[pl.ds(n * ROWS, ROWS), :]
        known_ref[n] = base + table_ref[own_block, n]
    for n in range(4):
        spread_ref[n] = table_ref[own_block, 2 * PAIRS + n]


def plane_of(ref, row):
    return ref[pl.ds(row, ROWS), :]


def correction_of(first_var, ref):
    pairs = [both(first_var, plane_of(ref, CORRECTION_ROW + n * ROWS)) for n in range(2)]
    return [pairs[0][0], pairs[0][1], pairs[1][0], pairs[1][1]]


def middle_kernel(
    here_ref, first_ref, second_ref, here_side_ref, there_side_ref, side_ref, other_ref, matrix_ref
):
    own_cell, count = lax.axis_index("cell"), lax.axis_size("cell")
    mirrored = own_cell // (count // 2)
    outer = jnp.logical_or(own_cell < count // 4, own_cell >= count - count // 4)
    sign = (1 - 2 * mirrored).astype(jnp.float32)
    first_var, _, _ = plane_masks()
    line = LineCells(first_var, sign)
    for cell in range(6):
        at = cell if cell < 3 else 5 - cell
        rows = [(at - 1) * CELL_ROWS + k * ROWS for k in range(PAIRS)]
        if at == 0:
            ref = here_side_ref if cell < 3 else there_side_ref
            planes = [plane_of(ref, THIRD_ROW + k * ROWS) for k in range(PAIRS)]
        elif cell < 3:
            planes = [plane_of(here_ref, row) for row in rows]
        else:
            planes = [
                jnp.where(
                    outer,
                    plane_of(first_ref, (2 - at) * CELL_ROWS + k * ROWS),
                    plane_of(second_ref, row),
                )
                for k, row in enumerate(rows)
            ]
        velocity_x, _, pressure, sound = primitives(first_var, planes)
        line.add(cell, planes, velocity_x, pressure, sound)
    faces = {cell: line.face(cell) for cell in (1, 2, 3)}
    for k in range(PAIRS):
        side_ref[k] = plane_of(here_side_ref, k * ROWS) - faces[1][k]
        side_ref[PAIRS + k] = plane_of(here_side_ref, (PAIRS + k) * ROWS) + (
            faces[1][k] - faces[2][k]
        )
        other_ref[k] = plane_of(there_side_ref, (PAIRS + k) * ROWS) + (
            faces[2][k] - faces[3][k]
        )
        other_ref[PAIRS + k] = plane_of(there_side_ref, k * ROWS) + faces[3][k]
    no_rates = (None, None)
    diag = difference(line.diagonal(1, no_rates), correction_of(first_var, here_side_ref))
    above, below = line.above(1), line.below(3)
    kept = [*diag, *line.diagonal(3, no_rates), above[0], *above[2:], *below[:2], below[3]]
    for n, plane in enumerate(kept):
        matrix_ref[n] = plane


def join_kernel(
    side_ref, other_ref, matrix_ref, there_side_ref, known_ref, spread_ref, out_ref
):
    mirrored = lax.axis_index("cell") // (lax.axis_size("cell") // 2)
    first_var, _, _ = plane_masks()
    kept = [matrix_ref[n] for n in range(14)]
    diag, other_diag = kept[:4], kept[4:8]
    above, below = (kept[8], None, kept[9], kept[10]), (kept[11], kept[12], None, kept[13])
    other_diag = difference(other_diag, correction_of(first_var, there_side_ref)[::-1])
    other = [other_ref[n] for n in range(2 * PAIRS)]
    factor = two_by_two(above, inverse_of(other_diag))
    diag = less(diag, two_by_two(factor, below))
    side = [side_ref[n] for n in range(2 * PAIRS)]
    middle = apply_matrix(inverse_of(diag), difference(side, apply_matrix(factor, other)))
    moved = apply_matrix([spread_ref[n] for n in range(4)], middle)
    results = [known_ref[n] + moved[n] for n in range(2 * PAIRS)]
    for cell in range(2):
        for k in range(PAIRS):
            first, second = results[cell * PAIRS + k], results[(1 - cell) * PAIRS + k]
            result = jnp.where(mirrored == 0, first, second)
            for var in range(2):
                for inst in range(2):
                    for half in range(2):
                        row = rows_of(var, inst, half)
                        out_ref[
                            inst, 2 * k + var, pl.ds(cell, 1), pl.ds(half * LANES, LANES)
                        ] = result[row : row + 1]


def share_half(copies):
    insts, count = lax.axis_size("inst"), lax.axis_size("cell")
    halves = [range(count // 2 - 1, -1, -1), range(count - 1, count // 2 - 1, -1)]
    groups = [
        [inst * count + cell for inst in range(insts - 2 + core, -1, -2) for cell in half]
        for core in range(2)
        for half in halves
    ]
    return lax.all_to_all(
        copies, ("inst", "cell"), split_axis=0, concat_axis=0, tiled=True,
        axis_index_groups=groups,
    )


def swap_cores(block):
    pairs = [(inst, inst ^ 1) for inst in range(lax.axis_size("inst"))]
    return lax.ppermute(block, "inst", pairs)


def swap_halves(block):
    count = lax.axis_size("cell")
    return lax.ppermute(block, "cell", [(i, (i + count // 2) % count) for i in range(count)])


def pass_round(block, steps):
    insts, count = lax.axis_size("inst"), lax.axis_size("cell")
    width = count // 4
    pairs = [
        (
            inst * count + source * width + i,
            (inst ^ (source == target)) * count + target * width + i,
        )
        for inst in range(insts)
        for source, target in steps
        for i in range(width)
    ]
    return lax.ppermute(block, ("inst", "cell"), pairs)


FIRST_ROUND = ((2, 0), (0, 1), (1, 3), (3, 2))
SECOND_ROUND = ((3, 1), (1, 2), (2, 3), (0, 0))


def float_shape(*sizes):
    return jax.ShapeDtypeStruct(sizes, jnp.float32)


def local_by_halves(state, pseudo_rate, line_next, face_codes):
    blocks = lax.axis_size("cell") // 2
    cells = 2 * blocks
    vmem = pl.BlockSpec(memory_space=pltpu.VMEM)
    plane = (ROWS, LANES)
    params = pltpu.CompilerParams(vmem_limit_bytes=VMEM_BYTES)
    places = lax.axis_size("inst") // 2
    held = [
        pltpu.with_memory_space_constraint(array, pltpu.HBM)
        for array in (state, pseudo_rate, line_next, face_codes)
    ]
    packed, next_here, codes_here = pl.pallas_call(
        pack_kernel,
        out_shape=(
            float_shape(places * blocks, BLOCK_ROWS, LANES),
            jax.ShapeDtypeStruct(line_next.shape, jnp.int32),
            jax.ShapeDtypeStruct(face_codes.shape, jnp.int32),
        ),
        in_specs=[pl.BlockSpec(memory_space=pltpu.HBM)] * 4,
        out_specs=(vmem, vmem, vmem),
        scratch_shapes=[
            pltpu.VMEM(state.shape, jnp.float32),
            pltpu.VMEM(pseudo_rate.shape, jnp.float32),
            pltpu.SemaphoreType.DMA((4,)),
        ],
        compiler_params=params,
    )(*held)
    shared = share_half(packed).reshape(places, blocks, BLOCK_ROWS, LANES)
    for_partner = pl.pallas_call(
        partner_kernel,
        out_shape=float_shape(cells * CELL_ROWS, LANES),
        in_specs=[vmem],
        out_specs=vmem,
        compiler_params=params,
    )(shared)
    from_partner = swap_cores(for_partner)
    beside = pl.CostEstimate(flops=10**6, bytes_accessed=10**6, transcendentals=0)
    kinds = (
        float_shape(cells, PAIRS, *plane),
        float_shape(blocks - 1, 4, *plane),
        float_shape(blocks - 1, 7, *plane),
        float_shape(2 * ROWS, LANES),
    )
    line_scratch = [pltpu.VMEM((cells, 3) + plane, jnp.float32)]
    arguments = (shared, next_here, codes_here)
    *near, here, for_round, third = pl.pallas_call(
        near_half_kernel,
        out_shape=kinds
        + (
            float_shape(MIDDLE_CELLS * CELL_ROWS, LANES),
            float_shape(ROUND_CELLS * CELL_ROWS, LANES),
            float_shape(CELL_ROWS, LANES),
        ),
        in_specs=[vmem] * 3,
        out_specs=(vmem,) * 7,
        scratch_shapes=line_scratch,
        compiler_params=params,
    )(*arguments)
    there_first = pass_round(for_round, FIRST_ROUND)
    partial, factors, eliminated, correction = pl.pallas_call(
        far_half_kernel,
        out_shape=kinds,
        in_specs=[vmem] * 7,
        out_specs=(vmem,) * 4,
        scratch_shapes=line_scratch,
        input_output_aliases={3 + n: n for n in range(4)},
        compiler_params=params,
        cost_estimate=beside,
    )(*arguments, *near)
    here_side, sides, here_again = pl.pallas_call(
        reduce_kernel,
        out_shape=(
            float_shape(SIDE_ROWS, LANES),
            float_shape(blocks - 1, 2 * PAIRS, *plane),
            float_shape(MIDDLE_CELLS * CELL_ROWS, LANES),
        ),
        in_specs=[vmem] * 6,
        out_specs=(vmem,) * 3,
        compiler_params=params,
    )(partial, from_partner, factors, correction, here, third)
    there_side = swap_halves(here_side)
    there_second = pass_round(here_again, SECOND_ROUND)
    known, spread = pl.pallas_call(
        spread_kernel,
        out_shape=(float_shape(2 * PAIRS, *plane), float_shape(4, *plane)),
        in_specs=[vmem] * 3,
        out_specs=(vmem, vmem),
        scratch_shapes=[pltpu.VMEM((blocks, 2 * PAIRS + 4) + plane, jnp.float32)],
        compiler_params=params,
        cost_estimate=beside,
    )(shared, eliminated, sides)
    side, other, matrices = pl.pallas_call(
        middle_kernel,
        out_shape=(
            float_shape(2 * PAIRS, *plane),
            float_shape(2 * PAIRS, *plane),
            float_shape(14, *plane),
        ),
        in_specs=[vmem] * 5,
        out_specs=(vmem,) * 3,
        compiler_params=params,
    )(here, there_first, there_second, here_side, there_side)
    return pl.pallas_call(
        join_kernel,
        out_shape=float_shape(*state.shape),
        in_specs=[vmem] * 6,
        out_specs=vmem,
        compiler_params=params,
    )(side, other, matrices, there_side, known, spread)


def solution(mesh):
    placed = (P("inst", None, "cell", None), P("cell", None), P(), P())
    inst_count, cell_count = mesh.shape["inst"], mesh.shape["cell"]

    def local(state, pseudo_rate, line_next, face_codes):
        small = (
            state.shape == (2, 6, 2, 2 * LANES)
            and inst_count * 2 == NT
            and cell_count == 8
            and face_codes.shape[1] * LINES_DEV == state.shape[3]
        )
        chosen = local_by_halves if small else local_by_lines
        return chosen(state, pseudo_rate, line_next, face_codes)

    return jax.shard_map(
        local, mesh=mesh, in_specs=placed, out_specs=P("inst", None, "cell", None), check_vma=False
    )
```

```python
import functools

import jax
import jax.numpy as jnp
import numpy as np
from jax import lax
from jax.experimental import pallas as pl
from jax.experimental.pallas import tpu as pltpu
from jax.sharding import PartitionSpec as P

NT = 8
LINES_DEV = 32


GAMMA_GAS = 1.4
OMEGA_BLADE = 1.0
SENSOR_GAIN = 0.25
FOURTH_GAIN = 0.03125
PITCH_GAIN = 0.5
SECOND_IMPL = 1.0
FOURTH_IMPL = 0.25
FREE_STATE = (1.0, 0.5, 0.0, 0.0, 2.625, 0.2)
MIRROR_SIGNS = (1.0, -1.0, 1.0, 1.0, 1.0, 1.0)
ZERO_BLOCK = (0.0, 0.0, 0.0, 0.0)
UNIT_BLOCK = (1.0, 0.0, 0.0, 1.0)
ZERO_PAIR = (0.0, 0.0)


def extended(block, sides, width):
    for axis, dim in sides:
        count = lax.axis_size(axis)
        forward = [(i, i + 1) for i in range(count - 1)]
        backward = [(target, source) for source, target in forward]
        low = lax.ppermute(
            lax.slice_in_dim(block, block.shape[dim] - width, None, axis=dim), axis, forward
        )
        high = lax.ppermute(lax.slice_in_dim(block, 0, width, axis=dim), axis, backward)
        block = jnp.concatenate([low, block, high], axis=dim)
    return block


def spectral_matrix(instances):
    offsets = np.arange(instances)[:, None] - np.arange(instances)[None, :]
    angles = np.pi * offsets / instances
    safe_sin = np.where(offsets == 0, 1.0, np.sin(angles))
    parity = np.where(np.mod(offsets, 2) == 0, -1.0, 1.0)
    matrix_table = np.where(
        offsets == 0, 0.0, 0.5 * OMEGA_BLADE * parity * np.cos(angles) / safe_sin
    )
    return jnp.asarray(matrix_table, jnp.float32)


def primitive_parts(cells_state):
    density = cells_state[..., 0, :, :]
    inverse = 1.0 / density
    velocity_x = cells_state[..., 1, :, :] * inverse
    velocity_y = cells_state[..., 2, :, :] * inverse
    velocity_z = cells_state[..., 3, :, :] * inverse
    energy = cells_state[..., 4, :, :]
    pressure = (GAMMA_GAS - 1.0) * (
        energy
        - 0.5
        * density
        * (velocity_x * velocity_x + velocity_y * velocity_y + velocity_z * velocity_z)
    )
    sound_speed = jnp.sqrt(GAMMA_GAS * pressure * inverse)
    return (velocity_x, velocity_y, pressure, sound_speed)


def directed_flux(cells_state, normal_velocity, pressure, component):
    zero_plane = jnp.zeros_like(pressure)
    pressure_rows = [
        zero_plane,
        zero_plane,
        zero_plane,
        zero_plane,
        pressure * normal_velocity,
        zero_plane,
    ]
    pressure_rows[component] = pressure
    return cells_state * normal_velocity[..., None, :, :] + jnp.stack(pressure_rows, axis=-3)


def line_residual(padded):
    velocity_x, velocity_y, pressure, sound_speed = primitive_parts(padded)
    flux_line = directed_flux(padded, velocity_x, pressure, 1)
    radius = jnp.abs(velocity_x) + sound_speed
    sensor = jnp.abs(
        pressure[..., 2:, :] - 2.0 * pressure[..., 1:-1, :] + pressure[..., :-2, :]
    ) / (pressure[..., 2:, :] + 2.0 * pressure[..., 1:-1, :] + pressure[..., :-2, :])
    second = SENSOR_GAIN * jnp.maximum(sensor[..., :-1, :], sensor[..., 1:, :])
    fourth = jnp.maximum(0.0, FOURTH_GAIN - second)
    face_radius = 0.5 * (radius[..., 1:-2, :] + radius[..., 2:-1, :])
    left_far = padded[..., :-3, :]
    left_near = padded[..., 1:-2, :]
    right_near = padded[..., 2:-1, :]
    right_far = padded[..., 3:, :]
    damping = face_radius[..., None, :, :] * (
        second[..., None, :, :] * (right_near - left_near)
        - fourth[..., None, :, :] * (right_far - 3.0 * right_near + 3.0 * left_near - left_far)
    )
    face_flux = 0.5 * (flux_line[..., 1:-2, :] + flux_line[..., 2:-1, :]) - damping
    return (face_flux[..., 1:, :] - face_flux[..., :-1, :], radius)


def pitch_parts(cells_state):
    velocity_x, velocity_y, pressure, sound_speed = primitive_parts(cells_state)
    return (directed_flux(cells_state, velocity_y, pressure, 2), jnp.abs(velocity_y) + sound_speed)


def pitch_residual(cells_state, next_lines, prev_lines):
    pitch_flux, radius = pitch_parts(cells_state)
    state_next = jnp.take(cells_state, next_lines, axis=-1)
    flux_next, radius_next = pitch_parts(state_next)
    face_flux = 0.5 * (pitch_flux + flux_next) - PITCH_GAIN * (0.5 * (radius + radius_next))[
        ..., None, :, :
    ] * (state_next - cells_state)
    return face_flux - jnp.take(face_flux, prev_lines, axis=-1)


def boundary_cells(edge_pair, line_codes, lower_end):
    reflected = edge_pair[..., ::-1, :] * jnp.asarray(MIRROR_SIGNS, jnp.float32)[:, None, None]
    if lower_end:
        copied = jnp.concatenate([edge_pair[..., :1, :], edge_pair[..., :1, :]], axis=-2)
    else:
        copied = jnp.concatenate([edge_pair[..., 1:, :], edge_pair[..., 1:, :]], axis=-2)
    inflow = jnp.asarray(FREE_STATE, jnp.float32)[:, None, None] + jnp.zeros_like(edge_pair)
    return jnp.where(line_codes == 0, reflected, jnp.where(line_codes == 1, inflow, copied))


def line_coefficients(radius_ext, diagonal_term, positions, total_cells):
    radius_below = radius_ext[..., :-2, :]
    radius_centre = radius_ext[..., 1:-1, :]
    radius_above = radius_ext[..., 2:, :]
    face_below = 0.5 * (radius_below + radius_centre)
    face_above = 0.5 * (radius_centre + radius_above)
    far_low = FOURTH_IMPL * radius_below
    near_low = -SECOND_IMPL * face_below - 2.0 * FOURTH_IMPL * (radius_below + radius_centre)
    middle = (
        diagonal_term
        + SECOND_IMPL * (face_below + face_above)
        + FOURTH_IMPL * (radius_below + 4.0 * radius_centre + radius_above)
    )
    near_high = -SECOND_IMPL * face_above - 2.0 * FOURTH_IMPL * (radius_centre + radius_above)
    far_high = FOURTH_IMPL * radius_above
    column = positions[:, None]
    far_low = jnp.where(column >= 2, far_low, 0.0)
    near_low = jnp.where(column >= 1, near_low, 0.0)
    near_high = jnp.where(column <= total_cells - 2, near_high, 0.0)
    far_high = jnp.where(column <= total_cells - 3, far_high, 0.0)
    return (far_low, near_low, middle, near_high, far_high)


def block_product(first_matrix, second_matrix):
    return (
        first_matrix[0] * second_matrix[0] + first_matrix[1] * second_matrix[2],
        first_matrix[0] * second_matrix[1] + first_matrix[1] * second_matrix[3],
        first_matrix[2] * second_matrix[0] + first_matrix[3] * second_matrix[2],
        first_matrix[2] * second_matrix[1] + first_matrix[3] * second_matrix[3],
    )


def block_inverse(matrix):
    determinant = matrix[0] * matrix[3] - matrix[1] * matrix[2]
    reciprocal = 1.0 / determinant
    return (
        matrix[3] * reciprocal,
        -matrix[1] * reciprocal,
        -matrix[2] * reciprocal,
        matrix[0] * reciprocal,
    )


def block_apply(matrix, vector):
    return (
        matrix[0] * vector[0] + matrix[1] * vector[1],
        matrix[2] * vector[0] + matrix[3] * vector[1],
    )


def add_blocks(first_members, second_members):
    return tuple((a + b for a, b in zip(first_members, second_members)))


def negate(members):
    return tuple((-a for a in members))


def extend_blocks(members, fill_values):
    return tuple(
        (
            jnp.concatenate([m, jnp.full_like(m[..., :1, :], f)], axis=-2)
            for m, f in zip(members, fill_values)
        )
    )


def shift_next(members, fill_values):
    return tuple(
        (
            jnp.concatenate([m[..., 1:, :], jnp.full_like(m[..., :1, :], f)], axis=-2)
            for m, f in zip(members, fill_values)
        )
    )


def shift_prev(members):
    return tuple(
        (jnp.concatenate([jnp.zeros_like(m[..., :1, :]), m[..., :-1, :]], axis=-2) for m in members)
    )


def pair_split(member):
    shaped = member.reshape(member.shape[:-2] + (member.shape[-2] // 2, 2, member.shape[-1]))
    return (shaped[..., 0, :], shaped[..., 1, :])


def split_parity(members):
    halves = [pair_split(m) for m in members]
    return (tuple((h[0] for h in halves)), tuple((h[1] for h in halves)))


def alternate(first_member, second_member):
    stacked = jnp.stack((first_member, second_member), axis=-2)
    return stacked.reshape(
        first_member.shape[:-2] + (2 * first_member.shape[-2], first_member.shape[-1])
    )


def reduce_blocks(sub_blocks, diag_blocks, super_blocks, right_side):
    block_count = diag_blocks[0].shape[-2]
    if block_count == 1:
        return block_apply(block_inverse(diag_blocks), right_side)
    if block_count % 2 == 1:
        sub_blocks = extend_blocks(sub_blocks, ZERO_BLOCK)
        diag_blocks = extend_blocks(diag_blocks, UNIT_BLOCK)
        super_blocks = extend_blocks(super_blocks, ZERO_BLOCK)
        right_side = extend_blocks(right_side, ZERO_PAIR)
    sub_even, sub_odd = split_parity(sub_blocks)
    diag_even, diag_odd = split_parity(diag_blocks)
    super_even, super_odd = split_parity(super_blocks)
    side_even, side_odd = split_parity(right_side)
    inverse_even = block_inverse(diag_even)
    inverse_next = shift_next(inverse_even, UNIT_BLOCK)
    sub_next = shift_next(sub_even, ZERO_BLOCK)
    super_next = shift_next(super_even, ZERO_BLOCK)
    side_next = shift_next(side_even, ZERO_PAIR)
    left_factor = negate(block_product(sub_odd, inverse_even))
    right_factor = negate(block_product(super_odd, inverse_next))
    reduced_sub = block_product(left_factor, sub_even)
    reduced_diag = add_blocks(
        diag_odd,
        add_blocks(block_product(left_factor, super_even), block_product(right_factor, sub_next)),
    )
    reduced_super = block_product(right_factor, super_next)
    reduced_side = add_blocks(
        side_odd,
        add_blocks(block_apply(left_factor, side_even), block_apply(right_factor, side_next)),
    )
    odd_values = reduce_blocks(reduced_sub, reduced_diag, reduced_super, reduced_side)
    before_values = shift_prev(odd_values)
    remainder = add_blocks(
        side_even,
        negate(
            add_blocks(block_apply(sub_even, before_values), block_apply(super_even, odd_values))
        ),
    )
    even_values = block_apply(inverse_even, remainder)
    merged = tuple((alternate(e, o) for e, o in zip(even_values, odd_values)))
    return tuple((m[..., :block_count, :] for m in merged))


def cells_leading(block):
    moved = jnp.transpose(block, (2, 0, 1, 3))
    return moved.reshape(block.shape[2], block.shape[0] * block.shape[1] * block.shape[3])


def solve_in_lanes(coefficients, line_source):
    source_shape = line_source.shape
    lane_coef = [cells_leading(jnp.broadcast_to(c[:, None], source_shape)) for c in coefficients]
    pairs_list = [pair_split(m) for m in lane_coef]
    zero_plane = jnp.zeros_like(pairs_list[2][0])
    sub_blocks = (pairs_list[0][0], pairs_list[1][0], zero_plane, pairs_list[0][1])
    diag_blocks = (pairs_list[2][0], pairs_list[3][0], pairs_list[1][1], pairs_list[2][1])
    super_blocks = (pairs_list[4][0], zero_plane, pairs_list[3][1], pairs_list[4][1])
    values = reduce_blocks(
        sub_blocks, diag_blocks, super_blocks, pair_split(cells_leading(line_source))
    )
    flat = alternate(values[0], values[1])
    shaped = flat.reshape(source_shape[2], source_shape[0], source_shape[1], source_shape[3])
    return jnp.transpose(shaped, (1, 2, 0, 3))


def return_tiles(line_values):
    return lax.all_to_all(line_values, "cell", split_axis=2, concat_axis=3, tiled=True)


def local_by_lines(state, pseudo_rate, line_next, face_codes):
    local_count = state.shape[0]
    tile_cells = state.shape[2]
    cell_index = lax.axis_index("cell")
    cell_count = lax.axis_size("cell")
    total_cells = tile_cells * cell_count
    spectral = spectral_matrix(NT)
    first_local = lax.axis_index("inst") * local_count
    own_rows = lax.dynamic_slice_in_dim(spectral, first_local, local_count, 0)
    shard_block = jax.tree.map(lambda a: lax.all_gather(a, "inst", axis=0, tiled=True), state)
    columns = lax.slice_in_dim(own_rows, 0, shard_block.shape[0], axis=1)
    time_term = jnp.zeros_like(state) + jnp.einsum(
        "nm,mvil->nvil", columns, shard_block, precision=lax.Precision.HIGHEST
    )
    padded = extended(state, (("cell", 2),), 2)
    codes_lines = jnp.repeat(face_codes, LINES_DEV, axis=1)
    lower_ghost = boundary_cells(state[:, :, 0:2, :], codes_lines[0], True)
    upper_ghost = boundary_cells(state[:, :, -2:, :], codes_lines[1], False)
    lower_rim = jnp.where(cell_index == 0, lower_ghost, padded[:, :, :2, :])
    upper_rim = jnp.where(cell_index == cell_count - 1, upper_ghost, padded[:, :, -2:, :])
    padded = jnp.concatenate([lower_rim, padded[:, :, 2:-2, :], upper_rim], axis=2)
    line_part, radius = line_residual(padded)
    prev_lines = (
        jnp.zeros_like(line_next).at[line_next].set(jnp.arange(line_next.shape[0], dtype=jnp.int32))
    )
    residual = line_part + pitch_residual(state, line_next, prev_lines) + time_term
    right_side = -residual
    centre_radius = radius[:, 2:-2, :]
    diagonal_term = pseudo_rate * centre_radius
    positions = cell_index * tile_cells + jnp.arange(-1, tile_cells + 1, dtype=jnp.int32)
    inside = (positions >= 0) & (positions < total_cells)
    radius_ext = jnp.where(inside[:, None], radius[:, 1:-1, :], 0.0)
    coefficients = line_coefficients(radius_ext, diagonal_term, positions[1:-1], total_cells)
    stacked = jnp.stack(coefficients, axis=1)
    line_source = lax.all_to_all(right_side, "cell", split_axis=3, concat_axis=2, tiled=True)
    line_coef = lax.all_to_all(stacked, "cell", split_axis=3, concat_axis=2, tiled=True)
    update = return_tiles(solve_in_lanes(tuple((line_coef[:, k] for k in range(5))), line_source))
    return state + update


LANES = 128
ROWS = 8
PAIRS = 3
CELL_ROWS = PAIRS * ROWS
RATE_ROW = 2 * CELL_ROWS
VMEM_BYTES = 8 * 2**20
BLOCK_ROWS = RATE_ROW + ROWS

MIDDLE_CELLS = (1, 0, 2)
MIDDLE_ROWS = 3 * CELL_ROWS
SECOND_ROWS = MIDDLE_ROWS - ROWS
CORRECTION_ROW = 2 * CELL_ROWS
SIDE_ROWS = CORRECTION_ROW + 3 * ROWS


def spectral_offsets():
    table = np.zeros(NT)
    for offset in range(1, NT):
        angle = np.pi * offset / NT
        parity = -1.0 if offset % 2 == 0 else 1.0
        table[offset] = 0.5 * OMEGA_BLADE * parity * np.cos(angle) / np.sin(angle)
    return [float(np.float32(value)) for value in table]


def plane_masks():
    row_index = lax.broadcasted_iota(jnp.int32, (ROWS, LANES), 0)
    return row_index < 4, (row_index & 2) == 0, row_index & 1


def both(first_var, plane):
    turned = pltpu.roll(plane, 4, 0)
    return jnp.where(first_var, plane, turned), jnp.where(first_var, turned, plane)


def primitives(first_var, planes):
    density, moment_x = both(first_var, planes[0])
    moment_y, moment_z = both(first_var, planes[1])
    energy = jnp.where(first_var, planes[2], pltpu.roll(planes[2], 4, 0))
    inverse = 1.0 / density
    velocity_x = moment_x * inverse
    velocity_y = moment_y * inverse
    velocity_z = moment_z * inverse
    kinetic = moment_x * velocity_x + moment_y * velocity_y + moment_z * velocity_z
    pressure = (GAMMA_GAS - 1.0) * (energy - 0.5 * kinetic)
    sound = jnp.sqrt(GAMMA_GAS * pressure * inverse)
    return velocity_x, velocity_y, pressure, sound


def rows_of(var, inst, half):
    return (var // 2) * ROWS + (var % 2) * 4 + inst * 2 + half


def pack_kernel(
    held_state_ref, held_rate_ref, held_next_ref, held_codes_ref, out_ref, next_ref, codes_ref,
    state_ref, rate_ref, sems,
):
    copies = [
        pltpu.make_async_copy(source, target, sems.at[k])
        for k, (source, target) in enumerate(
            (
                (held_state_ref, state_ref),
                (held_rate_ref, rate_ref),
                (held_next_ref, next_ref),
                (held_codes_ref, codes_ref),
            )
        )
    ]
    for copy in copies:
        copy.start()
    for copy in copies:
        copy.wait()
    mirrored = lax.axis_index("cell") // (lax.axis_size("cell") // 2)
    for cell in range(2):
        place = pl.multiple_of(jnp.bitwise_xor(cell, mirrored) * CELL_ROWS, ROWS)
        for k in range(PAIRS):
            rows = [
                state_ref[inst, 2 * k + var, pl.ds(cell, 1), pl.ds(half * LANES, LANES)]
                for var in range(2)
                for inst in range(2)
                for half in range(2)
            ]
            for row, values in enumerate(rows):
                out_ref[0, pl.ds(place + (k * ROWS + row), 1), :] = values
    rates = [
        rate_ref[pl.ds(cell, 1), pl.ds(half * LANES, LANES)]
        for cell in range(2)
        for half in range(2)
    ]
    for row in range(4):
        out_ref[0, pl.ds(RATE_ROW + row, 1), :] = jnp.where(
            mirrored == 0, rates[row], rates[row ^ 2]
        )
    out_ref[0, pl.ds(RATE_ROW + 4, 4), :] = jnp.zeros((4, LANES), jnp.float32)
    for row in range(0, BLOCK_ROWS, ROWS):
        values = out_ref[0, pl.ds(row, ROWS), :]
        for copy in range(1, out_ref.shape[0]):
            out_ref[copy, pl.ds(row, ROWS), :] = values


def turn_insts(first_inst, plane):
    return jnp.where(first_inst, pltpu.roll(plane, 6, 0), pltpu.roll(plane, 2, 0))


def time_weights(first_inst, shift):
    offsets = spectral_offsets()
    other = jnp.where(
        first_inst, offsets[(2 * shift + 1) % NT], offsets[(2 * shift - 1) % NT]
    )
    return offsets[(2 * shift) % NT], other


def at_block(ref, y, block):
    blocks = ref.shape[1]
    mirrored = lax.axis_index("cell") // blocks
    place = mirrored * block + (1 - mirrored) * (blocks - 1 - block)
    return ref.at[ref.shape[0] - 1 - y, place]


def cell_plane(ref, y, cell, k):
    return at_block(ref, y, cell // 2)[pl.ds((cell % 2) * CELL_ROWS + k * ROWS, ROWS), :]


def partner_kernel(all_ref, out_ref):
    own_inst = lax.axis_index("inst")
    own_y, core = own_inst >> 1, own_inst & 1
    _, first_inst, _ = plane_masks()
    one, three = time_weights(first_inst, 1), time_weights(first_inst, 3)
    near = [jnp.where(core == 0, a, b) for a, b in zip(one, three)]
    away = [jnp.where(core == 0, b, a) for a, b in zip(one, three)]
    cells = 2 * all_ref.shape[1]
    for cell in range(cells):
        for k in range(PAIRS):
            here = cell_plane(all_ref, own_y, cell, k)
            there = cell_plane(all_ref, 1 - own_y, cell, k)
            out_ref[pl.ds(cell * CELL_ROWS + k * ROWS, ROWS), :] = (
                near[0] * here
                + away[0] * there
                + turn_insts(first_inst, near[1] * here + away[1] * there)
            )


def two_by_two(first, second):
    def entry(a, b, c, d):
        terms = [x * y for x, y in ((a, b), (c, d)) if x is not None and y is not None]
        return None if not terms else terms[0] if len(terms) == 1 else terms[0] + terms[1]

    return (
        entry(first[0], second[0], first[1], second[2]),
        entry(first[0], second[1], first[1], second[3]),
        entry(first[2], second[0], first[3], second[2]),
        entry(first[2], second[1], first[3], second[3]),
    )


def inverse_of(matrix):
    reciprocal = 1.0 / (matrix[0] * matrix[3] - matrix[1] * matrix[2])
    return (
        matrix[3] * reciprocal,
        -(matrix[1] * reciprocal),
        -(matrix[2] * reciprocal),
        matrix[0] * reciprocal,
    )


def less(first, second):
    return tuple(a if b is None else a - b for a, b in zip(first, second))


def minus(members):
    return tuple(None if a is None else -a for a in members)


def matrix_vector(matrix, low, high):
    def row(a, b):
        terms = [x * y for x, y in ((a, low), (b, high)) if x is not None]
        return terms[0] if len(terms) == 1 else terms[0] + terms[1]

    return row(matrix[0], matrix[1]), row(matrix[2], matrix[3])


def apply_matrix(matrix, side):
    parts = [matrix_vector(matrix, side[k], side[PAIRS + k]) for k in range(PAIRS)]
    return [low for low, _ in parts] + [high for _, high in parts]


def difference(first, second):
    return [a - b for a, b in zip(first, second)]


def flux_along(first_var, planes, velocity, pressure, sign):
    normal = sign * velocity
    return [
        planes[0] * normal + jnp.where(first_var, 0.0, sign * pressure),
        planes[1] * normal,
        planes[2] * normal + jnp.where(first_var, pressure * normal, 0.0),
    ]


class LineCells:
    def __init__(self, first_var, sign):
        self.first_var, self.sign = first_var, sign
        self.state, self.pressure, self.radius = {}, {}, {}
        self.flux, self.step, self.sensor = {}, {}, {}

    def add(self, cell, planes, velocity, pressure, sound):
        self.state[cell], self.pressure[cell] = planes, pressure
        self.radius[cell] = jnp.abs(velocity) + sound
        self.flux[cell] = flux_along(self.first_var, planes, velocity, pressure, self.sign)
        if cell - 1 in self.state:
            self.step[cell - 1] = difference(planes, self.state[cell - 1])
        if cell - 2 in self.state:
            twice = 2.0 * self.pressure[cell - 1]
            outer = pressure + self.pressure[cell - 2]
            self.sensor[cell - 1] = jnp.abs(outer - twice) / (outer + twice)

    def face(self, cell):
        second = SENSOR_GAIN * jnp.maximum(self.sensor[cell], self.sensor[cell + 1])
        fourth = jnp.maximum(0.0, FOURTH_GAIN - second)
        face_radius = 0.5 * (self.radius[cell] + self.radius[cell + 1])
        near_weight = face_radius * (second + 2.0 * fourth)
        far_weight = face_radius * fourth
        return [
            0.5 * (self.flux[cell][k] + self.flux[cell + 1][k])
            - (
                near_weight * self.step[cell][k]
                - far_weight * (self.step[cell + 1][k] + self.step[cell - 1][k])
            )
            for k in range(PAIRS)
        ]

    def near(self, cell):
        scale = SECOND_IMPL * 0.5 + 2.0 * FOURTH_IMPL
        return -scale * (self.radius[cell] + self.radius[cell + 1])

    def far(self, cell):
        return FOURTH_IMPL * self.radius[cell]

    def middle(self, cell, rate):
        centre, above = self.radius[cell], self.radius[cell + 1]
        if cell == 0:
            total, weighted = centre + (centre + above), 4.0 * centre + above
        else:
            below = self.radius[cell - 1]
            total = (below + centre) + (centre + above)
            weighted = below + 4.0 * centre + above
        result = SECOND_IMPL * (0.5 * total) + FOURTH_IMPL * weighted
        return result if rate is None else rate * centre + result

    def diagonal(self, cell, rates):
        across = self.near(cell)
        return (self.middle(cell, rates[0]), across, across, self.middle(cell + 1, rates[1]))

    def below(self, cell):
        return (self.far(cell - 1), self.near(cell - 1), None, self.far(cell))

    def above(self, cell):
        return (self.far(cell + 1), None, self.near(cell + 1), self.far(cell + 2))


def rates_at(ref, y, block, first_half):
    rows = [at_block(ref, y, block)[pl.ds(RATE_ROW + k, 1), :] for k in range(4)]
    return [jnp.where(first_half, rows[2 * k], rows[2 * k + 1]) for k in range(2)]


def near_half_kernel(all_ref, next_ref, codes_ref, *refs):
    *results, middle_ref, line_ref = refs
    own_y = lax.axis_index("inst") >> 1
    cells = 2 * all_ref.shape[1]
    for n, back in enumerate(MIDDLE_CELLS):
        for k in range(PAIRS):
            plane = cell_plane(all_ref, own_y, cells - 1 - back, k)
            middle_ref[pl.ds(n * CELL_ROWS + k * ROWS, ROWS), :] = plane

    @pl.when(lax.axis_index("cell") < all_ref.shape[1])
    def _():
        half_kernel(all_ref, next_ref, codes_ref, *results, line_ref)


def far_half_kernel(all_ref, next_ref, codes_ref, *refs):
    *refs, line_ref = refs
    given, results = refs[: len(refs) // 2], refs[len(refs) // 2 :]
    far = lax.axis_index("cell") >= all_ref.shape[1]

    @pl.when(far)
    def _():
        half_kernel(all_ref, next_ref, codes_ref, *results, line_ref)

    @pl.when(jnp.logical_not(far))
    def _():
        for source, target in zip(given, results):
            target[...] = source[...]


def half_kernel(
    all_ref, next_ref, codes_ref, partial_ref, factor_ref, blocks_ref, correction_ref,
    line_ref,
):
    own_y = lax.axis_index("inst") >> 1
    blocks = all_ref.shape[1]
    cells = 2 * blocks
    mirrored = lax.axis_index("cell") // blocks
    sign = (1 - 2 * mirrored).astype(jnp.float32)
    shape = (ROWS, LANES)
    lane_index = lax.broadcasted_iota(jnp.int32, shape, 1)
    first_var, first_inst, half_index = plane_masks()
    first_half = half_index == 0
    zero = jnp.zeros(shape, jnp.float32)

    next_rows = [
        next_ref[pl.ds(half * LANES, LANES)].reshape(1, LANES) for half in range(2)
    ]
    next_line = jnp.where(first_half, next_rows[0], next_rows[1])
    column = lax.broadcasted_iota(jnp.int32, (LANES, LANES), 0)
    prev_halves = []
    for target in range(2):
        total = None
        for source in range(2):
            hits = jnp.where(column + target * LANES == next_rows[source], 1.0, 0.0)
            names = (lane_index + source * LANES).astype(jnp.float32)
            part = lax.dot_general(
                names, hits, (((1,), (1,)), ((), ())), preferred_element_type=jnp.float32
            )
            total = part if total is None else total + part
        prev_halves.append(total)
    prev_line = jnp.where(first_half, prev_halves[0], prev_halves[1]).astype(jnp.int32)

    def picker(lines):
        lane = lines & (LANES - 1)
        same = (lines >> 7) == half_index

        def pick(plane):
            swapped = jnp.where(first_half, pltpu.roll(plane, 7, 0), pltpu.roll(plane, 1, 0))
            here = jnp.take_along_axis(plane, lane, axis=1, mode="promise_in_bounds")
            there = jnp.take_along_axis(swapped, lane, axis=1, mode="promise_in_bounds")
            return jnp.where(same, here, there)

        return pick

    pick_next = picker(next_line)
    pick_prev = picker(prev_line)

    def loaded(cell, y=own_y):
        return [cell_plane(all_ref, y, cell, k) for k in range(PAIRS)]

    own_weights, away_weights = time_weights(first_inst, 0), time_weights(first_inst, 2)

    def own_time_parts(planes, cell):
        return [
            away_weights[0] * away
            + turn_insts(first_inst, own_weights[1] * own + away_weights[1] * away)
            for own, away in zip(planes, loaded(cell, 1 - own_y))
        ]

    def flux_across(planes, velocity, pressure):
        return [
            planes[0] * velocity,
            planes[1] * velocity + jnp.where(first_var, pressure, 0.0),
            planes[2] * velocity + jnp.where(first_var, pressure * velocity, 0.0),
        ]

    def pitch_flux(planes, velocity_y, pressure, sound):
        nearby = [pick_next(plane) for plane in planes]
        _, next_velocity, next_pressure, next_sound = primitives(first_var, nearby)
        own_flux = flux_across(planes, velocity_y, pressure)
        next_flux = flux_across(nearby, next_velocity, next_pressure)
        weight = (PITCH_GAIN * 0.5) * (
            jnp.abs(velocity_y) + sound + (jnp.abs(next_velocity) + next_sound)
        )
        return [
            0.5 * (a + b) - weight * (n - o)
            for a, b, n, o in zip(own_flux, next_flux, nearby, planes)
        ]

    for cell in range(cells):
        planes = loaded(cell)
        velocity_x, velocity_y, pressure, sound = primitives(first_var, planes)
        line_ref[cell, 0], line_ref[cell, 1], line_ref[cell, 2] = velocity_x, pressure, sound
        faces_across = pitch_flux(planes, velocity_y, pressure, sound)
        times = own_time_parts(planes, cell)
        for k in range(PAIRS):
            partial_ref[cell, k] = -(times[k] + (faces_across[k] - pick_prev(faces_across[k])))

    tile = half_index * (LANES // LINES_DEV) + lane_index // LINES_DEV
    end_codes = jnp.where(mirrored == 0, codes_ref[pl.ds(0, 1), :], codes_ref[pl.ds(1, 1), :])
    codes = jnp.zeros(shape, jnp.int32)
    for k in range(2 * LANES // LINES_DEV):
        codes = jnp.where(tile == k, jnp.broadcast_to(end_codes[:, k : k + 1], shape), codes)

    def ghost(cell):
        planes = loaded(-1 - cell)
        copied = loaded(0)
        result = []
        for k in range(PAIRS):
            reflected = planes[k] if k else jnp.where(first_var, planes[k], -planes[k])
            inflow = jnp.where(first_var, FREE_STATE[2 * k], FREE_STATE[2 * k + 1])
            result.append(
                jnp.where(codes == 0, reflected, jnp.where(codes == 1, inflow, copied[k]))
            )
        return result

    line = LineCells(first_var, sign)
    faces, inverses, aboves = {}, [], []
    for cell in range(-2, cells):
        if cell < 0:
            planes = ghost(cell)
            velocity_x, _, pressure, sound = primitives(first_var, planes)
        else:
            planes = loaded(cell)
            velocity_x, pressure, sound = [line_ref[cell, k] for k in range(3)]
        line.add(cell, planes, velocity_x, pressure, sound)
        if cell >= 1:
            faces[cell - 2] = line.face(cell - 2)
        if cell >= 2:
            at = cell - 2
            for k in range(PAIRS):
                partial_ref[at, k] = partial_ref[at, k] + (faces[at - 1][k] - faces[at][k])
        if cell >= 3 and cell % 2 == 1:
            at = cell - 3
            block = at // 2
            rates = rates_at(all_ref, own_y, block, first_half)
            diag = line.diagonal(at, rates)
            if block > 0:
                factor = two_by_two(line.below(at), inverses[-1])
                diag = less(diag, two_by_two(factor, aboves[-1]))
                for n in range(4):
                    factor_ref[block - 1, n] = factor[n]
            inverses.append(inverse_of(diag))
            aboves.append(line.above(at))
            kept = [*inverses[-1], aboves[-1][0], *aboves[-1][2:]]
            for n, plane in enumerate(kept):
                blocks_ref[block, n] = plane

    last = cells - 2
    for k in range(PAIRS):
        partial_ref[last, k] = partial_ref[last, k] + faces[last - 1][k]
    factor = two_by_two(line.below(last), inverses[-1])
    for n in range(4):
        factor_ref[blocks - 2, n] = factor[n]
    correction = list(two_by_two(factor, aboves[-1]))
    rates = rates_at(all_ref, own_y, blocks - 1, first_half)
    for member in range(2):
        centre = line.radius[last + member]
        correction[3 * member] = correction[3 * member] - rates[member] * centre
    for n in range(2):
        correction_ref[pl.ds(n * ROWS, ROWS), :] = jnp.where(
            first_var, correction[2 * n], correction[2 * n + 1]
        )


def reduce_kernel(
    partial_ref, time_ref, factor_ref, correction_ref, here_ref, middle_ref, sides_ref, again_ref
):
    again_ref[...] = here_ref[pl.ds(0, SECOND_ROWS), :]
    middle_ref[pl.ds(SIDE_ROWS - ROWS, ROWS), :] = here_ref[pl.ds(SECOND_ROWS, ROWS), :]
    for row in range(0, 2 * ROWS, ROWS):
        middle_ref[pl.ds(CORRECTION_ROW + row, ROWS), :] = correction_ref[pl.ds(row, ROWS), :]
    blocks = partial_ref.shape[0] // 2
    side = None
    for block in range(blocks):
        own = []
        for cell in (2 * block, 2 * block + 1):
            for k in range(PAIRS):
                time = time_ref[pl.ds(cell * CELL_ROWS + k * ROWS, ROWS), :]
                own.append(partial_ref[cell, k] - time)
        if block > 0:
            factor = [factor_ref[block - 1, n] for n in range(4)]
            own = difference(own, apply_matrix(factor, side))
        side = own
        for n, plane in enumerate(side):
            if block < blocks - 1:
                sides_ref[block, n] = plane
            else:
                middle_ref[pl.ds(n * ROWS, ROWS), :] = plane


def spread_kernel(all_ref, blocks_ref, sides_ref, known_ref, spread_ref, table_ref):
    own_y = lax.axis_index("inst") >> 1
    blocks = all_ref.shape[1]
    own_cell = lax.axis_index("cell")
    own_block = jnp.where(own_cell < blocks, own_cell, 2 * blocks - 1 - own_cell)
    zero = jnp.zeros((ROWS, LANES), jnp.float32)
    known, spread = [zero] * (2 * PAIRS), (zero + 1.0, zero, zero, zero + 1.0)
    for block in range(blocks - 1, -1, -1):
        if block < blocks - 1:
            kept = [blocks_ref[block, n] for n in range(7)]
            inverse, above = kept[:4], (kept[4], None, kept[5], kept[6])
            side = [sides_ref[block, n] for n in range(2 * PAIRS)]
            step = two_by_two(inverse, above)
            own = apply_matrix(inverse, side)
            if block < blocks - 2:
                known = difference(own, apply_matrix(step, known))
                spread = minus(two_by_two(step, spread))
            else:
                known, spread = own, minus(step)
        for n, plane in enumerate(known + list(spread)):
            table_ref[block, n] = plane
    for n in range(2 * PAIRS):
        base = at_block(all_ref, own_y, own_block)[pl.ds(n * ROWS, ROWS), :]
        known_ref[n] = base + table_ref[own_block, n]
    for n in range(4):
        spread_ref[n] = table_ref[own_block, 2 * PAIRS + n]


def plane_of(ref, row):
    return ref[pl.ds(row, ROWS), :]


def correction_of(first_var, ref):
    pairs = [both(first_var, plane_of(ref, CORRECTION_ROW + n * ROWS)) for n in range(2)]
    return [pairs[0][0], pairs[0][1], pairs[1][0], pairs[1][1]]


def middle_kernel(
    here_ref, first_ref, second_ref, here_side_ref, there_side_ref, side_ref, other_ref, matrix_ref
):
    own_cell, count = lax.axis_index("cell"), lax.axis_size("cell")
    mirrored = own_cell // (count // 2)
    outer = jnp.logical_or(own_cell < count // 4, own_cell >= count - count // 4)
    sign = (1 - 2 * mirrored).astype(jnp.float32)
    first_var, _, _ = plane_masks()
    line = LineCells(first_var, sign)
    for cell in range(6):
        at = (2, 0, 1)[cell if cell < 3 else 5 - cell]
        planes = []
        for k in range(PAIRS):
            row = at * CELL_ROWS + k * ROWS
            if cell < 3:
                planes.append(plane_of(here_ref, row))
            elif row < SECOND_ROWS:
                first, second = plane_of(first_ref, row), plane_of(second_ref, row)
                planes.append(jnp.where(outer, first, second))
            else:
                planes.append(plane_of(there_side_ref, SIDE_ROWS - ROWS))
        velocity_x, _, pressure, sound = primitives(first_var, planes)
        line.add(cell, planes, velocity_x, pressure, sound)
    faces = {cell: line.face(cell) for cell in (1, 2, 3)}
    for k in range(PAIRS):
        side_ref[k] = plane_of(here_side_ref, k * ROWS) - faces[1][k]
        side_ref[PAIRS + k] = plane_of(here_side_ref, (PAIRS + k) * ROWS) + (
            faces[1][k] - faces[2][k]
        )
        other_ref[k] = plane_of(there_side_ref, (PAIRS + k) * ROWS) + (
            faces[2][k] - faces[3][k]
        )
        other_ref[PAIRS + k] = plane_of(there_side_ref, k * ROWS) + faces[3][k]
    no_rates = (None, None)
    diag = difference(line.diagonal(1, no_rates), correction_of(first_var, here_side_ref))
    above, below = line.above(1), line.below(3)
    kept = [*diag, *line.diagonal(3, no_rates), above[0], *above[2:], *below[:2], below[3]]
    for n, plane in enumerate(kept):
        matrix_ref[n] = plane


def join_kernel(
    side_ref, other_ref, matrix_ref, there_side_ref, known_ref, spread_ref, out_ref
):
    mirrored = lax.axis_index("cell") // (lax.axis_size("cell") // 2)
    first_var, _, _ = plane_masks()
    kept = [matrix_ref[n] for n in range(14)]
    diag, other_diag = kept[:4], kept[4:8]
    above, below = (kept[8], None, kept[9], kept[10]), (kept[11], kept[12], None, kept[13])
    other_diag = difference(other_diag, correction_of(first_var, there_side_ref)[::-1])
    other = [other_ref[n] for n in range(2 * PAIRS)]
    factor = two_by_two(above, inverse_of(other_diag))
    diag = less(diag, two_by_two(factor, below))
    side = [side_ref[n] for n in range(2 * PAIRS)]
    middle = apply_matrix(inverse_of(diag), difference(side, apply_matrix(factor, other)))
    moved = apply_matrix([spread_ref[n] for n in range(4)], middle)
    results = [known_ref[n] + moved[n] for n in range(2 * PAIRS)]
    for cell in range(2):
        for k in range(PAIRS):
            first, second = results[cell * PAIRS + k], results[(1 - cell) * PAIRS + k]
            result = jnp.where(mirrored == 0, first, second)
            for var in range(2):
                for inst in range(2):
                    for half in range(2):
                        row = rows_of(var, inst, half)
                        out_ref[
                            inst, 2 * k + var, pl.ds(cell, 1), pl.ds(half * LANES, LANES)
                        ] = result[row : row + 1]


def share_half(copies):
    insts, count = lax.axis_size("inst"), lax.axis_size("cell")
    halves = [range(count // 2 - 1, -1, -1), range(count - 1, count // 2 - 1, -1)]
    groups = [
        [inst * count + cell for inst in range(insts - 2 + core, -1, -2) for cell in half]
        for core in range(2)
        for half in halves
    ]
    return lax.all_to_all(
        copies, ("inst", "cell"), split_axis=0, concat_axis=0, tiled=True,
        axis_index_groups=groups,
    )


def swap_cores(block):
    pairs = [(inst, inst ^ 1) for inst in range(lax.axis_size("inst"))]
    return lax.ppermute(block, "inst", pairs)


def swap_halves(block):
    count = lax.axis_size("cell")
    return lax.ppermute(block, "cell", [(i, (i + count // 2) % count) for i in range(count)])


def pass_round(block, steps):
    insts, count = lax.axis_size("inst"), lax.axis_size("cell")
    width = count // 4
    pairs = [
        (
            inst * count + source * width + i,
            (inst ^ (source == target)) * count + target * width + i,
        )
        for inst in range(insts)
        for source, target in steps
        for i in range(width)
    ]
    return lax.ppermute(block, ("inst", "cell"), pairs)


FIRST_ROUND = ((2, 0), (0, 1), (1, 3), (3, 2))
SECOND_ROUND = ((3, 1), (1, 2), (2, 3), (0, 0))


def float_shape(*sizes):
    return jax.ShapeDtypeStruct(sizes, jnp.float32)


def local_by_halves(state, pseudo_rate, line_next, face_codes):
    blocks = lax.axis_size("cell") // 2
    cells = 2 * blocks
    vmem = pl.BlockSpec(memory_space=pltpu.VMEM)
    plane = (ROWS, LANES)
    params = pltpu.CompilerParams(vmem_limit_bytes=VMEM_BYTES)
    places = lax.axis_size("inst") // 2
    held = [
        pltpu.with_memory_space_constraint(array, pltpu.HBM)
        for array in (state, pseudo_rate, line_next, face_codes)
    ]
    packed, next_here, codes_here = pl.pallas_call(
        pack_kernel,
        out_shape=(
            float_shape(places * blocks, BLOCK_ROWS, LANES),
            jax.ShapeDtypeStruct(line_next.shape, jnp.int32),
            jax.ShapeDtypeStruct(face_codes.shape, jnp.int32),
        ),
        in_specs=[pl.BlockSpec(memory_space=pltpu.HBM)] * 4,
        out_specs=(vmem, vmem, vmem),
        scratch_shapes=[
            pltpu.VMEM(state.shape, jnp.float32),
            pltpu.VMEM(pseudo_rate.shape, jnp.float32),
            pltpu.SemaphoreType.DMA((4,)),
        ],
        compiler_params=params,
    )(*held)
    shared = share_half(packed).reshape(places, blocks, BLOCK_ROWS, LANES)
    for_partner = pl.pallas_call(
        partner_kernel,
        out_shape=float_shape(cells * CELL_ROWS, LANES),
        in_specs=[vmem],
        out_specs=vmem,
        compiler_params=params,
    )(shared)
    from_partner = swap_cores(for_partner)
    beside = pl.CostEstimate(flops=10**6, bytes_accessed=10**6, transcendentals=0)
    kinds = (
        float_shape(cells, PAIRS, *plane),
        float_shape(blocks - 1, 4, *plane),
        float_shape(blocks - 1, 7, *plane),
        float_shape(2 * ROWS, LANES),
    )
    line_scratch = [pltpu.VMEM((cells, 3) + plane, jnp.float32)]
    arguments = (shared, next_here, codes_here)
    *near, here = pl.pallas_call(
        near_half_kernel,
        out_shape=kinds
        + (float_shape(MIDDLE_ROWS, LANES),),
        in_specs=[vmem] * 3,
        out_specs=(vmem,) * 5,
        scratch_shapes=line_scratch,
        compiler_params=params,
    )(*arguments)
    there_first = pass_round(here, FIRST_ROUND)
    partial, factors, eliminated, correction = pl.pallas_call(
        far_half_kernel,
        out_shape=kinds,
        in_specs=[vmem] * 7,
        out_specs=(vmem,) * 4,
        scratch_shapes=line_scratch,
        input_output_aliases={3 + n: n for n in range(4)},
        compiler_params=params,
        cost_estimate=beside,
    )(*arguments, *near)
    here_side, sides, here_again = pl.pallas_call(
        reduce_kernel,
        out_shape=(
            float_shape(SIDE_ROWS, LANES),
            float_shape(blocks - 1, 2 * PAIRS, *plane),
            float_shape(SECOND_ROWS, LANES),
        ),
        in_specs=[vmem] * 5,
        out_specs=(vmem,) * 3,
        compiler_params=params,
    )(partial, from_partner, factors, correction, here)
    there_side = swap_halves(here_side)
    there_second = pass_round(here_again, SECOND_ROUND)
    known, spread = pl.pallas_call(
        spread_kernel,
        out_shape=(float_shape(2 * PAIRS, *plane), float_shape(4, *plane)),
        in_specs=[vmem] * 3,
        out_specs=(vmem, vmem),
        scratch_shapes=[pltpu.VMEM((blocks, 2 * PAIRS + 4) + plane, jnp.float32)],
        compiler_params=params,
        cost_estimate=beside,
    )(shared, eliminated, sides)
    side, other, matrices = pl.pallas_call(
        middle_kernel,
        out_shape=(
            float_shape(2 * PAIRS, *plane),
            float_shape(2 * PAIRS, *plane),
            float_shape(14, *plane),
        ),
        in_specs=[vmem] * 5,
        out_specs=(vmem,) * 3,
        compiler_params=params,
    )(here, there_first, there_second, here_side, there_side)
    return pl.pallas_call(
        join_kernel,
        out_shape=float_shape(*state.shape),
        in_specs=[vmem] * 6,
        out_specs=vmem,
        compiler_params=params,
    )(side, other, matrices, there_side, known, spread)


def solution(mesh):
    placed = (P("inst", None, "cell", None), P("cell", None), P(), P())
    inst_count, cell_count = mesh.shape["inst"], mesh.shape["cell"]

    def local(state, pseudo_rate, line_next, face_codes):
        small = (
            state.shape == (2, 6, 2, 2 * LANES)
            and inst_count * 2 == NT
            and cell_count == 8
            and face_codes.shape[1] * LINES_DEV == state.shape[3]
        )
        chosen = local_by_halves if small else local_by_lines
        return chosen(state, pseudo_rate, line_next, face_codes)

    return jax.shard_map(
        local, mesh=mesh, in_specs=placed, out_specs=P("inst", None, "cell", None), check_vma=False
    )
```

```python
import functools

import jax
import jax.numpy as jnp
import numpy as np
from jax import lax
from jax.experimental import pallas as pl
from jax.experimental.pallas import tpu as pltpu
from jax.sharding import PartitionSpec as P

NT = 8
LINES_DEV = 32


GAMMA_GAS = 1.4
OMEGA_BLADE = 1.0
SENSOR_GAIN = 0.25
FOURTH_GAIN = 0.03125
PITCH_GAIN = 0.5
SECOND_IMPL = 1.0
FOURTH_IMPL = 0.25
FREE_STATE = (1.0, 0.5, 0.0, 0.0, 2.625, 0.2)
MIRROR_SIGNS = (1.0, -1.0, 1.0, 1.0, 1.0, 1.0)
ZERO_BLOCK = (0.0, 0.0, 0.0, 0.0)
UNIT_BLOCK = (1.0, 0.0, 0.0, 1.0)
ZERO_PAIR = (0.0, 0.0)


def extended(block, sides, width):
    for axis, dim in sides:
        count = lax.axis_size(axis)
        forward = [(i, i + 1) for i in range(count - 1)]
        backward = [(target, source) for source, target in forward]
        low = lax.ppermute(
            lax.slice_in_dim(block, block.shape[dim] - width, None, axis=dim), axis, forward
        )
        high = lax.ppermute(lax.slice_in_dim(block, 0, width, axis=dim), axis, backward)
        block = jnp.concatenate([low, block, high], axis=dim)
    return block


def spectral_matrix(instances):
    offsets = np.arange(instances)[:, None] - np.arange(instances)[None, :]
    angles = np.pi * offsets / instances
    safe_sin = np.where(offsets == 0, 1.0, np.sin(angles))
    parity = np.where(np.mod(offsets, 2) == 0, -1.0, 1.0)
    matrix_table = np.where(
        offsets == 0, 0.0, 0.5 * OMEGA_BLADE * parity * np.cos(angles) / safe_sin
    )
    return jnp.asarray(matrix_table, jnp.float32)


def primitive_parts(cells_state):
    density = cells_state[..., 0, :, :]
    inverse = 1.0 / density
    velocity_x = cells_state[..., 1, :, :] * inverse
    velocity_y = cells_state[..., 2, :, :] * inverse
    velocity_z = cells_state[..., 3, :, :] * inverse
    energy = cells_state[..., 4, :, :]
    pressure = (GAMMA_GAS - 1.0) * (
        energy
        - 0.5
        * density
        * (velocity_x * velocity_x + velocity_y * velocity_y + velocity_z * velocity_z)
    )
    sound_speed = jnp.sqrt(GAMMA_GAS * pressure * inverse)
    return (velocity_x, velocity_y, pressure, sound_speed)


def directed_flux(cells_state, normal_velocity, pressure, component):
    zero_plane = jnp.zeros_like(pressure)
    pressure_rows = [
        zero_plane,
        zero_plane,
        zero_plane,
        zero_plane,
        pressure * normal_velocity,
        zero_plane,
    ]
    pressure_rows[component] = pressure
    return cells_state * normal_velocity[..., None, :, :] + jnp.stack(pressure_rows, axis=-3)


def line_residual(padded):
    velocity_x, velocity_y, pressure, sound_speed = primitive_parts(padded)
    flux_line = directed_flux(padded, velocity_x, pressure, 1)
    radius = jnp.abs(velocity_x) + sound_speed
    sensor = jnp.abs(
        pressure[..., 2:, :] - 2.0 * pressure[..., 1:-1, :] + pressure[..., :-2, :]
    ) / (pressure[..., 2:, :] + 2.0 * pressure[..., 1:-1, :] + pressure[..., :-2, :])
    second = SENSOR_GAIN * jnp.maximum(sensor[..., :-1, :], sensor[..., 1:, :])
    fourth = jnp.maximum(0.0, FOURTH_GAIN - second)
    face_radius = 0.5 * (radius[..., 1:-2, :] + radius[..., 2:-1, :])
    left_far = padded[..., :-3, :]
    left_near = padded[..., 1:-2, :]
    right_near = padded[..., 2:-1, :]
    right_far = padded[..., 3:, :]
    damping = face_radius[..., None, :, :] * (
        second[..., None, :, :] * (right_near - left_near)
        - fourth[..., None, :, :] * (right_far - 3.0 * right_near + 3.0 * left_near - left_far)
    )
    face_flux = 0.5 * (flux_line[..., 1:-2, :] + flux_line[..., 2:-1, :]) - damping
    return (face_flux[..., 1:, :] - face_flux[..., :-1, :], radius)


def pitch_parts(cells_state):
    velocity_x, velocity_y, pressure, sound_speed = primitive_parts(cells_state)
    return (directed_flux(cells_state, velocity_y, pressure, 2), jnp.abs(velocity_y) + sound_speed)


def pitch_residual(cells_state, next_lines, prev_lines):
    pitch_flux, radius = pitch_parts(cells_state)
    state_next = jnp.take(cells_state, next_lines, axis=-1)
    flux_next, radius_next = pitch_parts(state_next)
    face_flux = 0.5 * (pitch_flux + flux_next) - PITCH_GAIN * (0.5 * (radius + radius_next))[
        ..., None, :, :
    ] * (state_next - cells_state)
    return face_flux - jnp.take(face_flux, prev_lines, axis=-1)


def boundary_cells(edge_pair, line_codes, lower_end):
    reflected = edge_pair[..., ::-1, :] * jnp.asarray(MIRROR_SIGNS, jnp.float32)[:, None, None]
    if lower_end:
        copied = jnp.concatenate([edge_pair[..., :1, :], edge_pair[..., :1, :]], axis=-2)
    else:
        copied = jnp.concatenate([edge_pair[..., 1:, :], edge_pair[..., 1:, :]], axis=-2)
    inflow = jnp.asarray(FREE_STATE, jnp.float32)[:, None, None] + jnp.zeros_like(edge_pair)
    return jnp.where(line_codes == 0, reflected, jnp.where(line_codes == 1, inflow, copied))


def line_coefficients(radius_ext, diagonal_term, positions, total_cells):
    radius_below = radius_ext[..., :-2, :]
    radius_centre = radius_ext[..., 1:-1, :]
    radius_above = radius_ext[..., 2:, :]
    face_below = 0.5 * (radius_below + radius_centre)
    face_above = 0.5 * (radius_centre + radius_above)
    far_low = FOURTH_IMPL * radius_below
    near_low = -SECOND_IMPL * face_below - 2.0 * FOURTH_IMPL * (radius_below + radius_centre)
    middle = (
        diagonal_term
        + SECOND_IMPL * (face_below + face_above)
        + FOURTH_IMPL * (radius_below + 4.0 * radius_centre + radius_above)
    )
    near_high = -SECOND_IMPL * face_above - 2.0 * FOURTH_IMPL * (radius_centre + radius_above)
    far_high = FOURTH_IMPL * radius_above
    column = positions[:, None]
    far_low = jnp.where(column >= 2, far_low, 0.0)
    near_low = jnp.where(column >= 1, near_low, 0.0)
    near_high = jnp.where(column <= total_cells - 2, near_high, 0.0)
    far_high = jnp.where(column <= total_cells - 3, far_high, 0.0)
    return (far_low, near_low, middle, near_high, far_high)


def block_product(first_matrix, second_matrix):
    return (
        first_matrix[0] * second_matrix[0] + first_matrix[1] * second_matrix[2],
        first_matrix[0] * second_matrix[1] + first_matrix[1] * second_matrix[3],
        first_matrix[2] * second_matrix[0] + first_matrix[3] * second_matrix[2],
        first_matrix[2] * second_matrix[1] + first_matrix[3] * second_matrix[3],
    )


def block_inverse(matrix):
    determinant = matrix[0] * matrix[3] - matrix[1] * matrix[2]
    reciprocal = 1.0 / determinant
    return (
        matrix[3] * reciprocal,
        -matrix[1] * reciprocal,
        -matrix[2] * reciprocal,
        matrix[0] * reciprocal,
    )


def block_apply(matrix, vector):
    return (
        matrix[0] * vector[0] + matrix[1] * vector[1],
        matrix[2] * vector[0] + matrix[3] * vector[1],
    )


def add_blocks(first_members, second_members):
    return tuple((a + b for a, b in zip(first_members, second_members)))


def negate(members):
    return tuple((-a for a in members))


def extend_blocks(members, fill_values):
    return tuple(
        (
            jnp.concatenate([m, jnp.full_like(m[..., :1, :], f)], axis=-2)
            for m, f in zip(members, fill_values)
        )
    )


def shift_next(members, fill_values):
    return tuple(
        (
            jnp.concatenate([m[..., 1:, :], jnp.full_like(m[..., :1, :], f)], axis=-2)
            for m, f in zip(members, fill_values)
        )
    )


def shift_prev(members):
    return tuple(
        (jnp.concatenate([jnp.zeros_like(m[..., :1, :]), m[..., :-1, :]], axis=-2) for m in members)
    )


def pair_split(member):
    shaped = member.reshape(member.shape[:-2] + (member.shape[-2] // 2, 2, member.shape[-1]))
    return (shaped[..., 0, :], shaped[..., 1, :])


def split_parity(members):
    halves = [pair_split(m) for m in members]
    return (tuple((h[0] for h in halves)), tuple((h[1] for h in halves)))


def alternate(first_member, second_member):
    stacked = jnp.stack((first_member, second_member), axis=-2)
    return stacked.reshape(
        first_member.shape[:-2] + (2 * first_member.shape[-2], first_member.shape[-1])
    )


def reduce_blocks(sub_blocks, diag_blocks, super_blocks, right_side):
    block_count = diag_blocks[0].shape[-2]
    if block_count == 1:
        return block_apply(block_inverse(diag_blocks), right_side)
    if block_count % 2 == 1:
        sub_blocks = extend_blocks(sub_blocks, ZERO_BLOCK)
        diag_blocks = extend_blocks(diag_blocks, UNIT_BLOCK)
        super_blocks = extend_blocks(super_blocks, ZERO_BLOCK)
        right_side = extend_blocks(right_side, ZERO_PAIR)
    sub_even, sub_odd = split_parity(sub_blocks)
    diag_even, diag_odd = split_parity(diag_blocks)
    super_even, super_odd = split_parity(super_blocks)
    side_even, side_odd = split_parity(right_side)
    inverse_even = block_inverse(diag_even)
    inverse_next = shift_next(inverse_even, UNIT_BLOCK)
    sub_next = shift_next(sub_even, ZERO_BLOCK)
    super_next = shift_next(super_even, ZERO_BLOCK)
    side_next = shift_next(side_even, ZERO_PAIR)
    left_factor = negate(block_product(sub_odd, inverse_even))
    right_factor = negate(block_product(super_odd, inverse_next))
    reduced_sub = block_product(left_factor, sub_even)
    reduced_diag = add_blocks(
        diag_odd,
        add_blocks(block_product(left_factor, super_even), block_product(right_factor, sub_next)),
    )
    reduced_super = block_product(right_factor, super_next)
    reduced_side = add_blocks(
        side_odd,
        add_blocks(block_apply(left_factor, side_even), block_apply(right_factor, side_next)),
    )
    odd_values = reduce_blocks(reduced_sub, reduced_diag, reduced_super, reduced_side)
    before_values = shift_prev(odd_values)
    remainder = add_blocks(
        side_even,
        negate(
            add_blocks(block_apply(sub_even, before_values), block_apply(super_even, odd_values))
        ),
    )
    even_values = block_apply(inverse_even, remainder)
    merged = tuple((alternate(e, o) for e, o in zip(even_values, odd_values)))
    return tuple((m[..., :block_count, :] for m in merged))


def cells_leading(block):
    moved = jnp.transpose(block, (2, 0, 1, 3))
    return moved.reshape(block.shape[2], block.shape[0] * block.shape[1] * block.shape[3])


def solve_in_lanes(coefficients, line_source):
    source_shape = line_source.shape
    lane_coef = [cells_leading(jnp.broadcast_to(c[:, None], source_shape)) for c in coefficients]
    pairs_list = [pair_split(m) for m in lane_coef]
    zero_plane = jnp.zeros_like(pairs_list[2][0])
    sub_blocks = (pairs_list[0][0], pairs_list[1][0], zero_plane, pairs_list[0][1])
    diag_blocks = (pairs_list[2][0], pairs_list[3][0], pairs_list[1][1], pairs_list[2][1])
    super_blocks = (pairs_list[4][0], zero_plane, pairs_list[3][1], pairs_list[4][1])
    values = reduce_blocks(
        sub_blocks, diag_blocks, super_blocks, pair_split(cells_leading(line_source))
    )
    flat = alternate(values[0], values[1])
    shaped = flat.reshape(source_shape[2], source_shape[0], source_shape[1], source_shape[3])
    return jnp.transpose(shaped, (1, 2, 0, 3))


def return_tiles(line_values):
    return lax.all_to_all(line_values, "cell", split_axis=2, concat_axis=3, tiled=True)


def local_by_lines(state, pseudo_rate, line_next, face_codes):
    local_count = state.shape[0]
    tile_cells = state.shape[2]
    cell_index = lax.axis_index("cell")
    cell_count = lax.axis_size("cell")
    total_cells = tile_cells * cell_count
    spectral = spectral_matrix(NT)
    first_local = lax.axis_index("inst") * local_count
    own_rows = lax.dynamic_slice_in_dim(spectral, first_local, local_count, 0)
    shard_block = jax.tree.map(lambda a: lax.all_gather(a, "inst", axis=0, tiled=True), state)
    columns = lax.slice_in_dim(own_rows, 0, shard_block.shape[0], axis=1)
    time_term = jnp.zeros_like(state) + jnp.einsum(
        "nm,mvil->nvil", columns, shard_block, precision=lax.Precision.HIGHEST
    )
    padded = extended(state, (("cell", 2),), 2)
    codes_lines = jnp.repeat(face_codes, LINES_DEV, axis=1)
    lower_ghost = boundary_cells(state[:, :, 0:2, :], codes_lines[0], True)
    upper_ghost = boundary_cells(state[:, :, -2:, :], codes_lines[1], False)
    lower_rim = jnp.where(cell_index == 0, lower_ghost, padded[:, :, :2, :])
    upper_rim = jnp.where(cell_index == cell_count - 1, upper_ghost, padded[:, :, -2:, :])
    padded = jnp.concatenate([lower_rim, padded[:, :, 2:-2, :], upper_rim], axis=2)
    line_part, radius = line_residual(padded)
    prev_lines = (
        jnp.zeros_like(line_next).at[line_next].set(jnp.arange(line_next.shape[0], dtype=jnp.int32))
    )
    residual = line_part + pitch_residual(state, line_next, prev_lines) + time_term
    right_side = -residual
    centre_radius = radius[:, 2:-2, :]
    diagonal_term = pseudo_rate * centre_radius
    positions = cell_index * tile_cells + jnp.arange(-1, tile_cells + 1, dtype=jnp.int32)
    inside = (positions >= 0) & (positions < total_cells)
    radius_ext = jnp.where(inside[:, None], radius[:, 1:-1, :], 0.0)
    coefficients = line_coefficients(radius_ext, diagonal_term, positions[1:-1], total_cells)
    stacked = jnp.stack(coefficients, axis=1)
    line_source = lax.all_to_all(right_side, "cell", split_axis=3, concat_axis=2, tiled=True)
    line_coef = lax.all_to_all(stacked, "cell", split_axis=3, concat_axis=2, tiled=True)
    update = return_tiles(solve_in_lanes(tuple((line_coef[:, k] for k in range(5))), line_source))
    return state + update


LANES = 128
ROWS = 8
PAIRS = 3
CELL_ROWS = PAIRS * ROWS
RATE_ROW = 2 * CELL_ROWS
VMEM_BYTES = 8 * 2**20
BLOCK_ROWS = RATE_ROW + ROWS

MIDDLE_CELLS = (1, 0, 2)
MIDDLE_ROWS = 3 * CELL_ROWS
SECOND_ROWS = MIDDLE_ROWS - ROWS
CORRECTION_ROW = 2 * CELL_ROWS
SIDE_ROWS = CORRECTION_ROW + 3 * ROWS


def spectral_offsets():
    table = np.zeros(NT)
    for offset in range(1, NT):
        angle = np.pi * offset / NT
        parity = -1.0 if offset % 2 == 0 else 1.0
        table[offset] = 0.5 * OMEGA_BLADE * parity * np.cos(angle) / np.sin(angle)
    return [float(np.float32(value)) for value in table]


def plane_masks():
    row_index = lax.broadcasted_iota(jnp.int32, (ROWS, LANES), 0)
    return row_index < 4, (row_index & 2) == 0, row_index & 1


def both(first_var, plane):
    turned = pltpu.roll(plane, 4, 0)
    return jnp.where(first_var, plane, turned), jnp.where(first_var, turned, plane)


def primitives(first_var, planes):
    density, moment_x = both(first_var, planes[0])
    moment_y, moment_z = both(first_var, planes[1])
    energy = jnp.where(first_var, planes[2], pltpu.roll(planes[2], 4, 0))
    inverse = 1.0 / density
    velocity_x = moment_x * inverse
    velocity_y = moment_y * inverse
    velocity_z = moment_z * inverse
    kinetic = moment_x * velocity_x + moment_y * velocity_y + moment_z * velocity_z
    pressure = (GAMMA_GAS - 1.0) * (energy - 0.5 * kinetic)
    sound = jnp.sqrt(GAMMA_GAS * pressure * inverse)
    return velocity_x, velocity_y, pressure, sound


def rows_of(var, inst, half):
    return (var // 2) * ROWS + (var % 2) * 4 + inst * 2 + half


def pack_kernel(
    held_state_ref, held_rate_ref, held_next_ref, held_codes_ref, out_ref, next_ref, codes_ref,
    state_ref, rate_ref, sems,
):
    copies = [
        pltpu.make_async_copy(source, target, sems.at[k])
        for k, (source, target) in enumerate(
            (
                (held_state_ref, state_ref),
                (held_rate_ref, rate_ref),
                (held_next_ref, next_ref),
                (held_codes_ref, codes_ref),
            )
        )
    ]
    for copy in copies:
        copy.start()
    for copy in copies:
        copy.wait()
    mirrored = lax.axis_index("cell") // (lax.axis_size("cell") // 2)
    for cell in range(2):
        place = pl.multiple_of(jnp.bitwise_xor(cell, mirrored) * CELL_ROWS, ROWS)
        for k in range(PAIRS):
            rows = [
                state_ref[inst, 2 * k + var, pl.ds(cell, 1), pl.ds(half * LANES, LANES)]
                for var in range(2)
                for inst in range(2)
                for half in range(2)
            ]
            for row, values in enumerate(rows):
                out_ref[0, pl.ds(place + (k * ROWS + row), 1), :] = values
    rates = [
        rate_ref[pl.ds(cell, 1), pl.ds(half * LANES, LANES)]
        for cell in range(2)
        for half in range(2)
    ]
    for row in range(4):
        out_ref[0, pl.ds(RATE_ROW + row, 1), :] = jnp.where(
            mirrored == 0, rates[row], rates[row ^ 2]
        )
    out_ref[0, pl.ds(RATE_ROW + 4, 4), :] = jnp.zeros((4, LANES), jnp.float32)
    for row in range(0, BLOCK_ROWS, ROWS):
        values = out_ref[0, pl.ds(row, ROWS), :]
        for copy in range(1, out_ref.shape[0]):
            out_ref[copy, pl.ds(row, ROWS), :] = values


def turn_insts(first_inst, plane):
    return jnp.where(first_inst, pltpu.roll(plane, 6, 0), pltpu.roll(plane, 2, 0))


def time_weights(first_inst, shift):
    offsets = spectral_offsets()
    other = jnp.where(
        first_inst, offsets[(2 * shift + 1) % NT], offsets[(2 * shift - 1) % NT]
    )
    return offsets[(2 * shift) % NT], other


def at_block(ref, y, block):
    blocks = ref.shape[1]
    mirrored = lax.axis_index("cell") // blocks
    place = mirrored * block + (1 - mirrored) * (blocks - 1 - block)
    return ref.at[ref.shape[0] - 1 - y, place]


def cell_plane(ref, y, cell, k):
    return at_block(ref, y, cell // 2)[pl.ds((cell % 2) * CELL_ROWS + k * ROWS, ROWS), :]


def partner_kernel(all_ref, out_ref):
    own_inst = lax.axis_index("inst")
    own_y, core = own_inst >> 1, own_inst & 1
    _, first_inst, _ = plane_masks()
    one, three = time_weights(first_inst, 1), time_weights(first_inst, 3)
    near = [jnp.where(core == 0, a, b) for a, b in zip(one, three)]
    away = [jnp.where(core == 0, b, a) for a, b in zip(one, three)]
    cells = 2 * all_ref.shape[1]
    for cell in range(cells):
        for k in range(PAIRS):
            here = cell_plane(all_ref, own_y, cell, k)
            there = cell_plane(all_ref, 1 - own_y, cell, k)
            out_ref[pl.ds(cell * CELL_ROWS + k * ROWS, ROWS), :] = (
                near[0] * here
                + away[0] * there
                + turn_insts(first_inst, near[1] * here + away[1] * there)
            )


def two_by_two(first, second):
    def entry(a, b, c, d):
        terms = [x * y for x, y in ((a, b), (c, d)) if x is not None and y is not None]
        return None if not terms else terms[0] if len(terms) == 1 else terms[0] + terms[1]

    return (
        entry(first[0], second[0], first[1], second[2]),
        entry(first[0], second[1], first[1], second[3]),
        entry(first[2], second[0], first[3], second[2]),
        entry(first[2], second[1], first[3], second[3]),
    )


def inverse_of(matrix):
    reciprocal = 1.0 / (matrix[0] * matrix[3] - matrix[1] * matrix[2])
    return (
        matrix[3] * reciprocal,
        -(matrix[1] * reciprocal),
        -(matrix[2] * reciprocal),
        matrix[0] * reciprocal,
    )


def less(first, second):
    return tuple(a if b is None else a - b for a, b in zip(first, second))


def minus(members):
    return tuple(None if a is None else -a for a in members)


def matrix_vector(matrix, low, high):
    def row(a, b):
        terms = [x * y for x, y in ((a, low), (b, high)) if x is not None]
        return terms[0] if len(terms) == 1 else terms[0] + terms[1]

    return row(matrix[0], matrix[1]), row(matrix[2], matrix[3])


def apply_matrix(matrix, side):
    parts = [matrix_vector(matrix, side[k], side[PAIRS + k]) for k in range(PAIRS)]
    return [low for low, _ in parts] + [high for _, high in parts]


def difference(first, second):
    return [a - b for a, b in zip(first, second)]


def flux_along(first_var, planes, velocity, pressure, sign):
    normal = sign * velocity
    return [
        planes[0] * normal + jnp.where(first_var, 0.0, sign * pressure),
        planes[1] * normal,
        planes[2] * normal + jnp.where(first_var, pressure * normal, 0.0),
    ]


class LineCells:
    def __init__(self, first_var, sign):
        self.first_var, self.sign = first_var, sign
        self.state, self.pressure, self.radius = {}, {}, {}
        self.flux, self.step, self.sensor = {}, {}, {}

    def add(self, cell, planes, velocity, pressure, sound):
        self.state[cell], self.pressure[cell] = planes, pressure
        self.radius[cell] = jnp.abs(velocity) + sound
        self.flux[cell] = flux_along(self.first_var, planes, velocity, pressure, self.sign)
        if cell - 1 in self.state:
            self.step[cell - 1] = difference(planes, self.state[cell - 1])
        if cell - 2 in self.state:
            twice = 2.0 * self.pressure[cell - 1]
            outer = pressure + self.pressure[cell - 2]
            self.sensor[cell - 1] = jnp.abs(outer - twice) / (outer + twice)

    def face(self, cell):
        second = SENSOR_GAIN * jnp.maximum(self.sensor[cell], self.sensor[cell + 1])
        fourth = jnp.maximum(0.0, FOURTH_GAIN - second)
        face_radius = 0.5 * (self.radius[cell] + self.radius[cell + 1])
        near_weight = face_radius * (second + 2.0 * fourth)
        far_weight = face_radius * fourth
        return [
            0.5 * (self.flux[cell][k] + self.flux[cell + 1][k])
            - (
                near_weight * self.step[cell][k]
                - far_weight * (self.step[cell + 1][k] + self.step[cell - 1][k])
            )
            for k in range(PAIRS)
        ]

    def near(self, cell):
        scale = SECOND_IMPL * 0.5 + 2.0 * FOURTH_IMPL
        return -scale * (self.radius[cell] + self.radius[cell + 1])

    def far(self, cell):
        return FOURTH_IMPL * self.radius[cell]

    def middle(self, cell, rate):
        centre, above = self.radius[cell], self.radius[cell + 1]
        if cell == 0:
            total, weighted = centre + (centre + above), 4.0 * centre + above
        else:
            below = self.radius[cell - 1]
            total = (below + centre) + (centre + above)
            weighted = below + 4.0 * centre + above
        result = SECOND_IMPL * (0.5 * total) + FOURTH_IMPL * weighted
        return result if rate is None else rate * centre + result

    def diagonal(self, cell, rates):
        across = self.near(cell)
        return (self.middle(cell, rates[0]), across, across, self.middle(cell + 1, rates[1]))

    def below(self, cell):
        return (self.far(cell - 1), self.near(cell - 1), None, self.far(cell))

    def above(self, cell):
        return (self.far(cell + 1), None, self.near(cell + 1), self.far(cell + 2))


def rates_at(ref, y, block, first_half):
    rows = [at_block(ref, y, block)[pl.ds(RATE_ROW + k, 1), :] for k in range(4)]
    return [jnp.where(first_half, rows[2 * k], rows[2 * k + 1]) for k in range(2)]


def near_half_kernel(all_ref, next_ref, codes_ref, *refs):
    *results, middle_ref, line_ref = refs
    own_y = lax.axis_index("inst") >> 1
    cells = 2 * all_ref.shape[1]
    for n, back in enumerate(MIDDLE_CELLS):
        for k in range(PAIRS):
            plane = cell_plane(all_ref, own_y, cells - 1 - back, k)
            middle_ref[pl.ds(n * CELL_ROWS + k * ROWS, ROWS), :] = plane

    @pl.when(lax.axis_index("cell") < all_ref.shape[1])
    def _():
        half_kernel(all_ref, next_ref, codes_ref, *results, line_ref)


def far_half_kernel(all_ref, next_ref, codes_ref, *refs):
    *refs, line_ref = refs
    given, results = refs[: len(refs) // 2], refs[len(refs) // 2 :]
    far = lax.axis_index("cell") >= all_ref.shape[1]

    @pl.when(far)
    def _():
        half_kernel(all_ref, next_ref, codes_ref, *results, line_ref)

    @pl.when(jnp.logical_not(far))
    def _():
        for source, target in zip(given, results):
            target[...] = source[...]


def half_kernel(
    all_ref, next_ref, codes_ref, partial_ref, factor_ref, blocks_ref, correction_ref,
    line_ref,
):
    own_y = lax.axis_index("inst") >> 1
    blocks = all_ref.shape[1]
    cells = 2 * blocks
    mirrored = lax.axis_index("cell") // blocks
    sign = (1 - 2 * mirrored).astype(jnp.float32)
    shape = (ROWS, LANES)
    lane_index = lax.broadcasted_iota(jnp.int32, shape, 1)
    first_var, first_inst, half_index = plane_masks()
    first_half = half_index == 0
    zero = jnp.zeros(shape, jnp.float32)

    next_rows = [
        next_ref[pl.ds(half * LANES, LANES)].reshape(1, LANES) for half in range(2)
    ]
    next_line = jnp.where(first_half, next_rows[0], next_rows[1])
    column = lax.broadcasted_iota(jnp.int32, (LANES, LANES), 0)
    prev_halves = []
    for target in range(2):
        total = None
        for source in range(2):
            hits = jnp.where(column + target * LANES == next_rows[source], 1.0, 0.0)
            names = (lane_index + source * LANES).astype(jnp.float32)
            part = lax.dot_general(
                names, hits, (((1,), (1,)), ((), ())), preferred_element_type=jnp.float32
            )
            total = part if total is None else total + part
        prev_halves.append(total)
    prev_line = jnp.where(first_half, prev_halves[0], prev_halves[1]).astype(jnp.int32)

    def picker(lines):
        lane = lines & (LANES - 1)
        same = (lines >> 7) == half_index

        def pick(plane):
            swapped = jnp.where(first_half, pltpu.roll(plane, 7, 0), pltpu.roll(plane, 1, 0))
            here = jnp.take_along_axis(plane, lane, axis=1, mode="promise_in_bounds")
            there = jnp.take_along_axis(swapped, lane, axis=1, mode="promise_in_bounds")
            return jnp.where(same, here, there)

        return pick

    pick_next = picker(next_line)
    pick_prev = picker(prev_line)

    def loaded(cell, y=own_y):
        return [cell_plane(all_ref, y, cell, k) for k in range(PAIRS)]

    own_weights, away_weights = time_weights(first_inst, 0), time_weights(first_inst, 2)

    def own_time_parts(planes, cell):
        return [
            away_weights[0] * away
            + turn_insts(first_inst, own_weights[1] * own + away_weights[1] * away)
            for own, away in zip(planes, loaded(cell, 1 - own_y))
        ]

    def flux_across(planes, velocity, pressure):
        return [
            planes[0] * velocity,
            planes[1] * velocity + jnp.where(first_var, pressure, 0.0),
            planes[2] * velocity + jnp.where(first_var, pressure * velocity, 0.0),
        ]

    def pitch_flux(planes, velocity_y, pressure, sound):
        nearby = [pick_next(plane) for plane in planes]
        _, next_velocity, next_pressure, next_sound = primitives(first_var, nearby)
        own_flux = flux_across(planes, velocity_y, pressure)
        next_flux = flux_across(nearby, next_velocity, next_pressure)
        weight = (PITCH_GAIN * 0.5) * (
            jnp.abs(velocity_y) + sound + (jnp.abs(next_velocity) + next_sound)
        )
        return [
            0.5 * (a + b) - weight * (n - o)
            for a, b, n, o in zip(own_flux, next_flux, nearby, planes)
        ]

    for cell in range(cells):
        planes = loaded(cell)
        velocity_x, velocity_y, pressure, sound = primitives(first_var, planes)
        line_ref[cell, 0], line_ref[cell, 1], line_ref[cell, 2] = velocity_x, pressure, sound
        faces_across = pitch_flux(planes, velocity_y, pressure, sound)
        times = own_time_parts(planes, cell)
        for k in range(PAIRS):
            partial_ref[cell, k] = -(times[k] + (faces_across[k] - pick_prev(faces_across[k])))

    tile = half_index * (LANES // LINES_DEV) + lane_index // LINES_DEV
    end_codes = jnp.where(mirrored == 0, codes_ref[pl.ds(0, 1), :], codes_ref[pl.ds(1, 1), :])
    codes = jnp.zeros(shape, jnp.int32)
    for k in range(2 * LANES // LINES_DEV):
        codes = jnp.where(tile == k, jnp.broadcast_to(end_codes[:, k : k + 1], shape), codes)

    def ghost(cell):
        planes = loaded(-1 - cell)
        copied = loaded(0)
        result = []
        for k in range(PAIRS):
            reflected = planes[k] if k else jnp.where(first_var, planes[k], -planes[k])
            inflow = jnp.where(first_var, FREE_STATE[2 * k], FREE_STATE[2 * k + 1])
            result.append(
                jnp.where(codes == 0, reflected, jnp.where(codes == 1, inflow, copied[k]))
            )
        return result

    line = LineCells(first_var, sign)
    faces, inverses, aboves = {}, [], []
    for cell in range(-2, cells):
        if cell < 0:
            planes = ghost(cell)
            velocity_x, _, pressure, sound = primitives(first_var, planes)
        else:
            planes = loaded(cell)
            velocity_x, pressure, sound = [line_ref[cell, k] for k in range(3)]
        line.add(cell, planes, velocity_x, pressure, sound)
        if cell >= 1:
            faces[cell - 2] = line.face(cell - 2)
        if cell >= 2:
            at = cell - 2
            for k in range(PAIRS):
                partial_ref[at, k] = partial_ref[at, k] + (faces[at - 1][k] - faces[at][k])
        if cell >= 3 and cell % 2 == 1:
            at = cell - 3
            block = at // 2
            rates = rates_at(all_ref, own_y, block, first_half)
            diag = line.diagonal(at, rates)
            if block > 0:
                factor = two_by_two(line.below(at), inverses[-1])
                diag = less(diag, two_by_two(factor, aboves[-1]))
                for n in range(4):
                    factor_ref[block - 1, n] = factor[n]
            inverses.append(inverse_of(diag))
            aboves.append(line.above(at))
            kept = [*inverses[-1], aboves[-1][0], *aboves[-1][2:]]
            for n, plane in enumerate(kept):
                blocks_ref[block, n] = plane

    last = cells - 2
    for k in range(PAIRS):
        partial_ref[last, k] = partial_ref[last, k] + faces[last - 1][k]
    factor = two_by_two(line.below(last), inverses[-1])
    for n in range(4):
        factor_ref[blocks - 2, n] = factor[n]
    correction = list(two_by_two(factor, aboves[-1]))
    rates = rates_at(all_ref, own_y, blocks - 1, first_half)
    for member in range(2):
        centre = line.radius[last + member]
        correction[3 * member] = correction[3 * member] - rates[member] * centre
    for n in range(2):
        correction_ref[pl.ds(n * ROWS, ROWS), :] = jnp.where(
            first_var, correction[2 * n], correction[2 * n + 1]
        )


def reduce_kernel(
    partial_ref, time_ref, factor_ref, correction_ref, here_ref, middle_ref, sides_ref, again_ref
):
    again_ref[...] = here_ref[pl.ds(0, SECOND_ROWS), :]
    middle_ref[pl.ds(SIDE_ROWS - ROWS, ROWS), :] = here_ref[pl.ds(SECOND_ROWS, ROWS), :]
    for row in range(0, 2 * ROWS, ROWS):
        middle_ref[pl.ds(CORRECTION_ROW + row, ROWS), :] = correction_ref[pl.ds(row, ROWS), :]
    blocks = partial_ref.shape[0] // 2
    side = None
    for block in range(blocks):
        own = []
        for cell in (2 * block, 2 * block + 1):
            for k in range(PAIRS):
                time = time_ref[pl.ds(cell * CELL_ROWS + k * ROWS, ROWS), :]
                own.append(partial_ref[cell, k] - time)
        if block > 0:
            factor = [factor_ref[block - 1, n] for n in range(4)]
            own = difference(own, apply_matrix(factor, side))
        side = own
        for n, plane in enumerate(side):
            if block < blocks - 1:
                sides_ref[block, n] = plane
            else:
                middle_ref[pl.ds(n * ROWS, ROWS), :] = plane


def spread_kernel(all_ref, blocks_ref, sides_ref, known_ref, spread_ref, table_ref):
    own_y = lax.axis_index("inst") >> 1
    blocks = all_ref.shape[1]
    own_cell = lax.axis_index("cell")
    own_block = jnp.where(own_cell < blocks, own_cell, 2 * blocks - 1 - own_cell)
    zero = jnp.zeros((ROWS, LANES), jnp.float32)
    known, spread = [zero] * (2 * PAIRS), (zero + 1.0, zero, zero, zero + 1.0)
    for block in range(blocks - 1, -1, -1):
        if block < blocks - 1:
            kept = [blocks_ref[block, n] for n in range(7)]
            inverse, above = kept[:4], (kept[4], None, kept[5], kept[6])
            side = [sides_ref[block, n] for n in range(2 * PAIRS)]
            step = two_by_two(inverse, above)
            own = apply_matrix(inverse, side)
            if block < blocks - 2:
                known = difference(own, apply_matrix(step, known))
                spread = minus(two_by_two(step, spread))
            else:
                known, spread = own, minus(step)
        for n, plane in enumerate(known + list(spread)):
            table_ref[block, n] = plane
    for n in range(2 * PAIRS):
        base = at_block(all_ref, own_y, own_block)[pl.ds(n * ROWS, ROWS), :]
        known_ref[n] = base + table_ref[own_block, n]
    for n in range(4):
        spread_ref[n] = table_ref[own_block, 2 * PAIRS + n]


def plane_of(ref, row):
    return ref[pl.ds(row, ROWS), :]


def correction_of(first_var, ref):
    pairs = [both(first_var, plane_of(ref, CORRECTION_ROW + n * ROWS)) for n in range(2)]
    return [pairs[0][0], pairs[0][1], pairs[1][0], pairs[1][1]]


def middle_kernel(
    here_ref, first_ref, second_ref, here_side_ref, there_side_ref, side_ref, other_ref, matrix_ref
):
    own_cell, count = lax.axis_index("cell"), lax.axis_size("cell")
    mirrored = own_cell // (count // 2)
    early = (own_cell // (count // 4)) % 2 == 0
    sign = (1 - 2 * mirrored).astype(jnp.float32)
    first_var, _, _ = plane_masks()
    line = LineCells(first_var, sign)
    for cell in range(6):
        at = (2, 0, 1)[cell if cell < 3 else 5 - cell]
        planes = []
        for k in range(PAIRS):
            row = at * CELL_ROWS + k * ROWS
            if cell < 3:
                planes.append(plane_of(here_ref, row))
            elif row < SECOND_ROWS:
                first, second = plane_of(first_ref, row), plane_of(second_ref, row)
                planes.append(jnp.where(early, first, second))
            else:
                planes.append(plane_of(there_side_ref, SIDE_ROWS - ROWS))
        velocity_x, _, pressure, sound = primitives(first_var, planes)
        line.add(cell, planes, velocity_x, pressure, sound)
    faces = {cell: line.face(cell) for cell in (1, 2, 3)}
    for k in range(PAIRS):
        side_ref[k] = plane_of(here_side_ref, k * ROWS) - faces[1][k]
        side_ref[PAIRS + k] = plane_of(here_side_ref, (PAIRS + k) * ROWS) + (
            faces[1][k] - faces[2][k]
        )
        other_ref[k] = plane_of(there_side_ref, (PAIRS + k) * ROWS) + (
            faces[2][k] - faces[3][k]
        )
        other_ref[PAIRS + k] = plane_of(there_side_ref, k * ROWS) + faces[3][k]
    no_rates = (None, None)
    diag = difference(line.diagonal(1, no_rates), correction_of(first_var, here_side_ref))
    above, below = line.above(1), line.below(3)
    kept = [*diag, *line.diagonal(3, no_rates), above[0], *above[2:], *below[:2], below[3]]
    for n, plane in enumerate(kept):
        matrix_ref[n] = plane


def join_kernel(
    side_ref, other_ref, matrix_ref, there_side_ref, known_ref, spread_ref, out_ref
):
    mirrored = lax.axis_index("cell") // (lax.axis_size("cell") // 2)
    first_var, _, _ = plane_masks()
    kept = [matrix_ref[n] for n in range(14)]
    diag, other_diag = kept[:4], kept[4:8]
    above, below = (kept[8], None, kept[9], kept[10]), (kept[11], kept[12], None, kept[13])
    other_diag = difference(other_diag, correction_of(first_var, there_side_ref)[::-1])
    other = [other_ref[n] for n in range(2 * PAIRS)]
    factor = two_by_two(above, inverse_of(other_diag))
    diag = less(diag, two_by_two(factor, below))
    side = [side_ref[n] for n in range(2 * PAIRS)]
    middle = apply_matrix(inverse_of(diag), difference(side, apply_matrix(factor, other)))
    moved = apply_matrix([spread_ref[n] for n in range(4)], middle)
    results = [known_ref[n] + moved[n] for n in range(2 * PAIRS)]
    for cell in range(2):
        for k in range(PAIRS):
            first, second = results[cell * PAIRS + k], results[(1 - cell) * PAIRS + k]
            result = jnp.where(mirrored == 0, first, second)
            for var in range(2):
                for inst in range(2):
                    for half in range(2):
                        row = rows_of(var, inst, half)
                        out_ref[
                            inst, 2 * k + var, pl.ds(cell, 1), pl.ds(half * LANES, LANES)
                        ] = result[row : row + 1]


def share_half(copies):
    insts, count = lax.axis_size("inst"), lax.axis_size("cell")
    halves = [range(count // 2 - 1, -1, -1), range(count - 1, count // 2 - 1, -1)]
    groups = [
        [inst * count + cell for inst in range(insts - 2 + core, -1, -2) for cell in half]
        for core in range(2)
        for half in halves
    ]
    return lax.all_to_all(
        copies, ("inst", "cell"), split_axis=0, concat_axis=0, tiled=True,
        axis_index_groups=groups,
    )


def swap_cores(block):
    pairs = [(inst, inst ^ 1) for inst in range(lax.axis_size("inst"))]
    return lax.ppermute(block, "inst", pairs)


def swap_halves(block):
    count = lax.axis_size("cell")
    return lax.ppermute(block, "cell", [(i, (i + count // 2) % count) for i in range(count)])


def pass_round(block, steps):
    insts, count = lax.axis_size("inst"), lax.axis_size("cell")
    width = count // 4
    pairs = [
        (
            inst * count + source * width + i,
            (inst ^ (source == target)) * count + target * width + i,
        )
        for inst in range(insts)
        for source, target in steps
        for i in range(width)
    ]
    return lax.ppermute(block, ("inst", "cell"), pairs)


FIRST_ROUND = ((2, 0), (0, 1), (1, 2), (3, 3))
SECOND_ROUND = ((3, 1), (1, 3), (0, 0), (2, 2))


def float_shape(*sizes):
    return jax.ShapeDtypeStruct(sizes, jnp.float32)


def local_by_halves(state, pseudo_rate, line_next, face_codes):
    blocks = lax.axis_size("cell") // 2
    cells = 2 * blocks
    vmem = pl.BlockSpec(memory_space=pltpu.VMEM)
    plane = (ROWS, LANES)
    params = pltpu.CompilerParams(vmem_limit_bytes=VMEM_BYTES)
    places = lax.axis_size("inst") // 2
    held = [
        pltpu.with_memory_space_constraint(array, pltpu.HBM)
        for array in (state, pseudo_rate, line_next, face_codes)
    ]
    packed, next_here, codes_here = pl.pallas_call(
        pack_kernel,
        out_shape=(
            float_shape(places * blocks, BLOCK_ROWS, LANES),
            jax.ShapeDtypeStruct(line_next.shape, jnp.int32),
            jax.ShapeDtypeStruct(face_codes.shape, jnp.int32),
        ),
        in_specs=[pl.BlockSpec(memory_space=pltpu.HBM)] * 4,
        out_specs=(vmem, vmem, vmem),
        scratch_shapes=[
            pltpu.VMEM(state.shape, jnp.float32),
            pltpu.VMEM(pseudo_rate.shape, jnp.float32),
            pltpu.SemaphoreType.DMA((4,)),
        ],
        compiler_params=params,
    )(*held)
    shared = share_half(packed).reshape(places, blocks, BLOCK_ROWS, LANES)
    for_partner = pl.pallas_call(
        partner_kernel,
        out_shape=float_shape(cells * CELL_ROWS, LANES),
        in_specs=[vmem],
        out_specs=vmem,
        compiler_params=params,
    )(shared)
    from_partner = swap_cores(for_partner)
    beside = pl.CostEstimate(flops=10**6, bytes_accessed=10**6, transcendentals=0)
    kinds = (
        float_shape(cells, PAIRS, *plane),
        float_shape(blocks - 1, 4, *plane),
        float_shape(blocks - 1, 7, *plane),
        float_shape(2 * ROWS, LANES),
    )
    line_scratch = [pltpu.VMEM((cells, 3) + plane, jnp.float32)]
    arguments = (shared, next_here, codes_here)
    *near, here = pl.pallas_call(
        near_half_kernel,
        out_shape=kinds
        + (float_shape(MIDDLE_ROWS, LANES),),
        in_specs=[vmem] * 3,
        out_specs=(vmem,) * 5,
        scratch_shapes=line_scratch,
        compiler_params=params,
    )(*arguments)
    there_first = pass_round(here, FIRST_ROUND)
    partial, factors, eliminated, correction = pl.pallas_call(
        far_half_kernel,
        out_shape=kinds,
        in_specs=[vmem] * 7,
        out_specs=(vmem,) * 4,
        scratch_shapes=line_scratch,
        input_output_aliases={3 + n: n for n in range(4)},
        compiler_params=params,
        cost_estimate=beside,
    )(*arguments, *near)
    here_side, sides, here_again = pl.pallas_call(
        reduce_kernel,
        out_shape=(
            float_shape(SIDE_ROWS, LANES),
            float_shape(blocks - 1, 2 * PAIRS, *plane),
            float_shape(SECOND_ROWS, LANES),
        ),
        in_specs=[vmem] * 5,
        out_specs=(vmem,) * 3,
        compiler_params=params,
    )(partial, from_partner, factors, correction, here)
    there_side = swap_halves(here_side)
    there_second = pass_round(here_again, SECOND_ROUND)
    known, spread = pl.pallas_call(
        spread_kernel,
        out_shape=(float_shape(2 * PAIRS, *plane), float_shape(4, *plane)),
        in_specs=[vmem] * 3,
        out_specs=(vmem, vmem),
        scratch_shapes=[pltpu.VMEM((blocks, 2 * PAIRS + 4) + plane, jnp.float32)],
        compiler_params=params,
        cost_estimate=beside,
    )(shared, eliminated, sides)
    side, other, matrices = pl.pallas_call(
        middle_kernel,
        out_shape=(
            float_shape(2 * PAIRS, *plane),
            float_shape(2 * PAIRS, *plane),
            float_shape(14, *plane),
        ),
        in_specs=[vmem] * 5,
        out_specs=(vmem,) * 3,
        compiler_params=params,
    )(here, there_first, there_second, here_side, there_side)
    return pl.pallas_call(
        join_kernel,
        out_shape=float_shape(*state.shape),
        in_specs=[vmem] * 6,
        out_specs=vmem,
        compiler_params=params,
    )(side, other, matrices, there_side, known, spread)


def solution(mesh):
    placed = (P("inst", None, "cell", None), P("cell", None), P(), P())
    inst_count, cell_count = mesh.shape["inst"], mesh.shape["cell"]

    def local(state, pseudo_rate, line_next, face_codes):
        small = (
            state.shape == (2, 6, 2, 2 * LANES)
            and inst_count * 2 == NT
            and cell_count == 8
            and face_codes.shape[1] * LINES_DEV == state.shape[3]
        )
        chosen = local_by_halves if small else local_by_lines
        return chosen(state, pseudo_rate, line_next, face_codes)

    return jax.shard_map(
        local, mesh=mesh, in_specs=placed, out_specs=P("inst", None, "cell", None), check_vma=False
    )
```

```python
import functools

import jax
import jax.numpy as jnp
import numpy as np
from jax import lax
from jax.experimental import pallas as pl
from jax.experimental.pallas import tpu as pltpu
from jax.sharding import PartitionSpec as P

NT = 8
LINES_DEV = 32


GAMMA_GAS = 1.4
OMEGA_BLADE = 1.0
SENSOR_GAIN = 0.25
FOURTH_GAIN = 0.03125
PITCH_GAIN = 0.5
SECOND_IMPL = 1.0
FOURTH_IMPL = 0.25
FREE_STATE = (1.0, 0.5, 0.0, 0.0, 2.625, 0.2)
MIRROR_SIGNS = (1.0, -1.0, 1.0, 1.0, 1.0, 1.0)
ZERO_BLOCK = (0.0, 0.0, 0.0, 0.0)
UNIT_BLOCK = (1.0, 0.0, 0.0, 1.0)
ZERO_PAIR = (0.0, 0.0)


def extended(block, sides, width):
    for axis, dim in sides:
        count = lax.axis_size(axis)
        forward = [(i, i + 1) for i in range(count - 1)]
        backward = [(target, source) for source, target in forward]
        low = lax.ppermute(
            lax.slice_in_dim(block, block.shape[dim] - width, None, axis=dim), axis, forward
        )
        high = lax.ppermute(lax.slice_in_dim(block, 0, width, axis=dim), axis, backward)
        block = jnp.concatenate([low, block, high], axis=dim)
    return block


def spectral_matrix(instances):
    offsets = np.arange(instances)[:, None] - np.arange(instances)[None, :]
    angles = np.pi * offsets / instances
    safe_sin = np.where(offsets == 0, 1.0, np.sin(angles))
    parity = np.where(np.mod(offsets, 2) == 0, -1.0, 1.0)
    matrix_table = np.where(
        offsets == 0, 0.0, 0.5 * OMEGA_BLADE * parity * np.cos(angles) / safe_sin
    )
    return jnp.asarray(matrix_table, jnp.float32)


def primitive_parts(cells_state):
    density = cells_state[..., 0, :, :]
    inverse = 1.0 / density
    velocity_x = cells_state[..., 1, :, :] * inverse
    velocity_y = cells_state[..., 2, :, :] * inverse
    velocity_z = cells_state[..., 3, :, :] * inverse
    energy = cells_state[..., 4, :, :]
    pressure = (GAMMA_GAS - 1.0) * (
        energy
        - 0.5
        * density
        * (velocity_x * velocity_x + velocity_y * velocity_y + velocity_z * velocity_z)
    )
    sound_speed = jnp.sqrt(GAMMA_GAS * pressure * inverse)
    return (velocity_x, velocity_y, pressure, sound_speed)


def directed_flux(cells_state, normal_velocity, pressure, component):
    zero_plane = jnp.zeros_like(pressure)
    pressure_rows = [
        zero_plane,
        zero_plane,
        zero_plane,
        zero_plane,
        pressure * normal_velocity,
        zero_plane,
    ]
    pressure_rows[component] = pressure
    return cells_state * normal_velocity[..., None, :, :] + jnp.stack(pressure_rows, axis=-3)


def line_residual(padded):
    velocity_x, velocity_y, pressure, sound_speed = primitive_parts(padded)
    flux_line = directed_flux(padded, velocity_x, pressure, 1)
    radius = jnp.abs(velocity_x) + sound_speed
    sensor = jnp.abs(
        pressure[..., 2:, :] - 2.0 * pressure[..., 1:-1, :] + pressure[..., :-2, :]
    ) / (pressure[..., 2:, :] + 2.0 * pressure[..., 1:-1, :] + pressure[..., :-2, :])
    second = SENSOR_GAIN * jnp.maximum(sensor[..., :-1, :], sensor[..., 1:, :])
    fourth = jnp.maximum(0.0, FOURTH_GAIN - second)
    face_radius = 0.5 * (radius[..., 1:-2, :] + radius[..., 2:-1, :])
    left_far = padded[..., :-3, :]
    left_near = padded[..., 1:-2, :]
    right_near = padded[..., 2:-1, :]
    right_far = padded[..., 3:, :]
    damping = face_radius[..., None, :, :] * (
        second[..., None, :, :] * (right_near - left_near)
        - fourth[..., None, :, :] * (right_far - 3.0 * right_near + 3.0 * left_near - left_far)
    )
    face_flux = 0.5 * (flux_line[..., 1:-2, :] + flux_line[..., 2:-1, :]) - damping
    return (face_flux[..., 1:, :] - face_flux[..., :-1, :], radius)


def pitch_parts(cells_state):
    velocity_x, velocity_y, pressure, sound_speed = primitive_parts(cells_state)
    return (directed_flux(cells_state, velocity_y, pressure, 2), jnp.abs(velocity_y) + sound_speed)


def pitch_residual(cells_state, next_lines, prev_lines):
    pitch_flux, radius = pitch_parts(cells_state)
    state_next = jnp.take(cells_state, next_lines, axis=-1)
    flux_next, radius_next = pitch_parts(state_next)
    face_flux = 0.5 * (pitch_flux + flux_next) - PITCH_GAIN * (0.5 * (radius + radius_next))[
        ..., None, :, :
    ] * (state_next - cells_state)
    return face_flux - jnp.take(face_flux, prev_lines, axis=-1)


def boundary_cells(edge_pair, line_codes, lower_end):
    reflected = edge_pair[..., ::-1, :] * jnp.asarray(MIRROR_SIGNS, jnp.float32)[:, None, None]
    if lower_end:
        copied = jnp.concatenate([edge_pair[..., :1, :], edge_pair[..., :1, :]], axis=-2)
    else:
        copied = jnp.concatenate([edge_pair[..., 1:, :], edge_pair[..., 1:, :]], axis=-2)
    inflow = jnp.asarray(FREE_STATE, jnp.float32)[:, None, None] + jnp.zeros_like(edge_pair)
    return jnp.where(line_codes == 0, reflected, jnp.where(line_codes == 1, inflow, copied))


def line_coefficients(radius_ext, diagonal_term, positions, total_cells):
    radius_below = radius_ext[..., :-2, :]
    radius_centre = radius_ext[..., 1:-1, :]
    radius_above = radius_ext[..., 2:, :]
    face_below = 0.5 * (radius_below + radius_centre)
    face_above = 0.5 * (radius_centre + radius_above)
    far_low = FOURTH_IMPL * radius_below
    near_low = -SECOND_IMPL * face_below - 2.0 * FOURTH_IMPL * (radius_below + radius_centre)
    middle = (
        diagonal_term
        + SECOND_IMPL * (face_below + face_above)
        + FOURTH_IMPL * (radius_below + 4.0 * radius_centre + radius_above)
    )
    near_high = -SECOND_IMPL * face_above - 2.0 * FOURTH_IMPL * (radius_centre + radius_above)
    far_high = FOURTH_IMPL * radius_above
    column = positions[:, None]
    far_low = jnp.where(column >= 2, far_low, 0.0)
    near_low = jnp.where(column >= 1, near_low, 0.0)
    near_high = jnp.where(column <= total_cells - 2, near_high, 0.0)
    far_high = jnp.where(column <= total_cells - 3, far_high, 0.0)
    return (far_low, near_low, middle, near_high, far_high)


def block_product(first_matrix, second_matrix):
    return (
        first_matrix[0] * second_matrix[0] + first_matrix[1] * second_matrix[2],
        first_matrix[0] * second_matrix[1] + first_matrix[1] * second_matrix[3],
        first_matrix[2] * second_matrix[0] + first_matrix[3] * second_matrix[2],
        first_matrix[2] * second_matrix[1] + first_matrix[3] * second_matrix[3],
    )


def block_inverse(matrix):
    determinant = matrix[0] * matrix[3] - matrix[1] * matrix[2]
    reciprocal = 1.0 / determinant
    return (
        matrix[3] * reciprocal,
        -matrix[1] * reciprocal,
        -matrix[2] * reciprocal,
        matrix[0] * reciprocal,
    )


def block_apply(matrix, vector):
    return (
        matrix[0] * vector[0] + matrix[1] * vector[1],
        matrix[2] * vector[0] + matrix[3] * vector[1],
    )


def add_blocks(first_members, second_members):
    return tuple((a + b for a, b in zip(first_members, second_members)))


def negate(members):
    return tuple((-a for a in members))


def extend_blocks(members, fill_values):
    return tuple(
        (
            jnp.concatenate([m, jnp.full_like(m[..., :1, :], f)], axis=-2)
            for m, f in zip(members, fill_values)
        )
    )


def shift_next(members, fill_values):
    return tuple(
        (
            jnp.concatenate([m[..., 1:, :], jnp.full_like(m[..., :1, :], f)], axis=-2)
            for m, f in zip(members, fill_values)
        )
    )


def shift_prev(members):
    return tuple(
        (jnp.concatenate([jnp.zeros_like(m[..., :1, :]), m[..., :-1, :]], axis=-2) for m in members)
    )


def pair_split(member):
    shaped = member.reshape(member.shape[:-2] + (member.shape[-2] // 2, 2, member.shape[-1]))
    return (shaped[..., 0, :], shaped[..., 1, :])


def split_parity(members):
    halves = [pair_split(m) for m in members]
    return (tuple((h[0] for h in halves)), tuple((h[1] for h in halves)))


def alternate(first_member, second_member):
    stacked = jnp.stack((first_member, second_member), axis=-2)
    return stacked.reshape(
        first_member.shape[:-2] + (2 * first_member.shape[-2], first_member.shape[-1])
    )


def reduce_blocks(sub_blocks, diag_blocks, super_blocks, right_side):
    block_count = diag_blocks[0].shape[-2]
    if block_count == 1:
        return block_apply(block_inverse(diag_blocks), right_side)
    if block_count % 2 == 1:
        sub_blocks = extend_blocks(sub_blocks, ZERO_BLOCK)
        diag_blocks = extend_blocks(diag_blocks, UNIT_BLOCK)
        super_blocks = extend_blocks(super_blocks, ZERO_BLOCK)
        right_side = extend_blocks(right_side, ZERO_PAIR)
    sub_even, sub_odd = split_parity(sub_blocks)
    diag_even, diag_odd = split_parity(diag_blocks)
    super_even, super_odd = split_parity(super_blocks)
    side_even, side_odd = split_parity(right_side)
    inverse_even = block_inverse(diag_even)
    inverse_next = shift_next(inverse_even, UNIT_BLOCK)
    sub_next = shift_next(sub_even, ZERO_BLOCK)
    super_next = shift_next(super_even, ZERO_BLOCK)
    side_next = shift_next(side_even, ZERO_PAIR)
    left_factor = negate(block_product(sub_odd, inverse_even))
    right_factor = negate(block_product(super_odd, inverse_next))
    reduced_sub = block_product(left_factor, sub_even)
    reduced_diag = add_blocks(
        diag_odd,
        add_blocks(block_product(left_factor, super_even), block_product(right_factor, sub_next)),
    )
    reduced_super = block_product(right_factor, super_next)
    reduced_side = add_blocks(
        side_odd,
        add_blocks(block_apply(left_factor, side_even), block_apply(right_factor, side_next)),
    )
    odd_values = reduce_blocks(reduced_sub, reduced_diag, reduced_super, reduced_side)
    before_values = shift_prev(odd_values)
    remainder = add_blocks(
        side_even,
        negate(
            add_blocks(block_apply(sub_even, before_values), block_apply(super_even, odd_values))
        ),
    )
    even_values = block_apply(inverse_even, remainder)
    merged = tuple((alternate(e, o) for e, o in zip(even_values, odd_values)))
    return tuple((m[..., :block_count, :] for m in merged))


def cells_leading(block):
    moved = jnp.transpose(block, (2, 0, 1, 3))
    return moved.reshape(block.shape[2], block.shape[0] * block.shape[1] * block.shape[3])


def solve_in_lanes(coefficients, line_source):
    source_shape = line_source.shape
    lane_coef = [cells_leading(jnp.broadcast_to(c[:, None], source_shape)) for c in coefficients]
    pairs_list = [pair_split(m) for m in lane_coef]
    zero_plane = jnp.zeros_like(pairs_list[2][0])
    sub_blocks = (pairs_list[0][0], pairs_list[1][0], zero_plane, pairs_list[0][1])
    diag_blocks = (pairs_list[2][0], pairs_list[3][0], pairs_list[1][1], pairs_list[2][1])
    super_blocks = (pairs_list[4][0], zero_plane, pairs_list[3][1], pairs_list[4][1])
    values = reduce_blocks(
        sub_blocks, diag_blocks, super_blocks, pair_split(cells_leading(line_source))
    )
    flat = alternate(values[0], values[1])
    shaped = flat.reshape(source_shape[2], source_shape[0], source_shape[1], source_shape[3])
    return jnp.transpose(shaped, (1, 2, 0, 3))


def return_tiles(line_values):
    return lax.all_to_all(line_values, "cell", split_axis=2, concat_axis=3, tiled=True)


def local_by_lines(state, pseudo_rate, line_next, face_codes):
    local_count = state.shape[0]
    tile_cells = state.shape[2]
    cell_index = lax.axis_index("cell")
    cell_count = lax.axis_size("cell")
    total_cells = tile_cells * cell_count
    spectral = spectral_matrix(NT)
    first_local = lax.axis_index("inst") * local_count
    own_rows = lax.dynamic_slice_in_dim(spectral, first_local, local_count, 0)
    shard_block = jax.tree.map(lambda a: lax.all_gather(a, "inst", axis=0, tiled=True), state)
    columns = lax.slice_in_dim(own_rows, 0, shard_block.shape[0], axis=1)
    time_term = jnp.zeros_like(state) + jnp.einsum(
        "nm,mvil->nvil", columns, shard_block, precision=lax.Precision.HIGHEST
    )
    padded = extended(state, (("cell", 2),), 2)
    codes_lines = jnp.repeat(face_codes, LINES_DEV, axis=1)
    lower_ghost = boundary_cells(state[:, :, 0:2, :], codes_lines[0], True)
    upper_ghost = boundary_cells(state[:, :, -2:, :], codes_lines[1], False)
    lower_rim = jnp.where(cell_index == 0, lower_ghost, padded[:, :, :2, :])
    upper_rim = jnp.where(cell_index == cell_count - 1, upper_ghost, padded[:, :, -2:, :])
    padded = jnp.concatenate([lower_rim, padded[:, :, 2:-2, :], upper_rim], axis=2)
    line_part, radius = line_residual(padded)
    prev_lines = (
        jnp.zeros_like(line_next).at[line_next].set(jnp.arange(line_next.shape[0], dtype=jnp.int32))
    )
    residual = line_part + pitch_residual(state, line_next, prev_lines) + time_term
    right_side = -residual
    centre_radius = radius[:, 2:-2, :]
    diagonal_term = pseudo_rate * centre_radius
    positions = cell_index * tile_cells + jnp.arange(-1, tile_cells + 1, dtype=jnp.int32)
    inside = (positions >= 0) & (positions < total_cells)
    radius_ext = jnp.where(inside[:, None], radius[:, 1:-1, :], 0.0)
    coefficients = line_coefficients(radius_ext, diagonal_term, positions[1:-1], total_cells)
    stacked = jnp.stack(coefficients, axis=1)
    line_source = lax.all_to_all(right_side, "cell", split_axis=3, concat_axis=2, tiled=True)
    line_coef = lax.all_to_all(stacked, "cell", split_axis=3, concat_axis=2, tiled=True)
    update = return_tiles(solve_in_lanes(tuple((line_coef[:, k] for k in range(5))), line_source))
    return state + update


LANES = 128
ROWS = 8
PAIRS = 3
CELL_ROWS = PAIRS * ROWS
RATE_ROW = 2 * CELL_ROWS
VMEM_BYTES = 8 * 2**20
BLOCK_ROWS = RATE_ROW + ROWS

MIDDLE_CELLS = 2
ROUND_CELLS = 4
CORRECTION_ROW = 2 * CELL_ROWS
THIRD_ROW = CORRECTION_ROW + 2 * ROWS
SIDE_ROWS = THIRD_ROW + CELL_ROWS


def spectral_offsets():
    table = np.zeros(NT)
    for offset in range(1, NT):
        angle = np.pi * offset / NT
        parity = -1.0 if offset % 2 == 0 else 1.0
        table[offset] = 0.5 * OMEGA_BLADE * parity * np.cos(angle) / np.sin(angle)
    return [float(np.float32(value)) for value in table]


def plane_masks():
    row_index = lax.broadcasted_iota(jnp.int32, (ROWS, LANES), 0)
    return row_index < 4, (row_index & 2) == 0, row_index & 1


def both(first_var, plane):
    turned = pltpu.roll(plane, 4, 0)
    return jnp.where(first_var, plane, turned), jnp.where(first_var, turned, plane)


def primitives(first_var, planes):
    density, moment_x = both(first_var, planes[0])
    moment_y, moment_z = both(first_var, planes[1])
    energy = jnp.where(first_var, planes[2], pltpu.roll(planes[2], 4, 0))
    inverse = 1.0 / density
    velocity_x = moment_x * inverse
    velocity_y = moment_y * inverse
    velocity_z = moment_z * inverse
    kinetic = moment_x * velocity_x + moment_y * velocity_y + moment_z * velocity_z
    pressure = (GAMMA_GAS - 1.0) * (energy - 0.5 * kinetic)
    sound = jnp.sqrt(GAMMA_GAS * pressure * inverse)
    return velocity_x, velocity_y, pressure, sound


def rows_of(var, inst, half):
    return (var // 2) * ROWS + (var % 2) * 4 + inst * 2 + half


def pack_kernel(
    held_state_ref, held_rate_ref, held_next_ref, held_codes_ref, out_ref, next_ref, codes_ref,
    state_ref, rate_ref, sems,
):
    copies = [
        pltpu.make_async_copy(source, target, sems.at[k])
        for k, (source, target) in enumerate(
            (
                (held_state_ref, state_ref),
                (held_rate_ref, rate_ref),
                (held_next_ref, next_ref),
                (held_codes_ref, codes_ref),
            )
        )
    ]
    for copy in copies:
        copy.start()
    for copy in copies:
        copy.wait()
    mirrored = lax.axis_index("cell") // (lax.axis_size("cell") // 2)
    for cell in range(2):
        place = pl.multiple_of(jnp.bitwise_xor(cell, mirrored) * CELL_ROWS, ROWS)
        for k in range(PAIRS):
            rows = [
                state_ref[inst, 2 * k + var, pl.ds(cell, 1), pl.ds(half * LANES, LANES)]
                for var in range(2)
                for inst in range(2)
                for half in range(2)
            ]
            for row, values in enumerate(rows):
                out_ref[0, pl.ds(place + (k * ROWS + row), 1), :] = values
    rates = [
        rate_ref[pl.ds(cell, 1), pl.ds(half * LANES, LANES)]
        for cell in range(2)
        for half in range(2)
    ]
    for row in range(4):
        out_ref[0, pl.ds(RATE_ROW + row, 1), :] = jnp.where(
            mirrored == 0, rates[row], rates[row ^ 2]
        )
    out_ref[0, pl.ds(RATE_ROW + 4, 4), :] = jnp.zeros((4, LANES), jnp.float32)
    for row in range(0, BLOCK_ROWS, ROWS):
        values = out_ref[0, pl.ds(row, ROWS), :]
        for copy in range(1, out_ref.shape[0]):
            out_ref[copy, pl.ds(row, ROWS), :] = values


def turn_insts(first_inst, plane):
    return jnp.where(first_inst, pltpu.roll(plane, 6, 0), pltpu.roll(plane, 2, 0))


def time_weights(first_inst, shift):
    offsets = spectral_offsets()
    other = jnp.where(
        first_inst, offsets[(2 * shift + 1) % NT], offsets[(2 * shift - 1) % NT]
    )
    return offsets[(2 * shift) % NT], other


NEAR_ORDER = ((1, 3), (1, 2), (1, 1), (1, 0), (0, 3), (0, 2), (0, 1), (0, 0))
FAR_ORDER = ((1, 3), (1, 2), (1, 0), (1, 1), (0, 2), (0, 0), (0, 1), (0, 3))


def at_block(ref, y, block):
    blocks = ref.shape[0] // 2
    near = lax.axis_index("cell") < blocks
    place = 0
    for n, (near_at, far_at) in enumerate(zip(NEAR_ORDER, FAR_ORDER)):
        for at, in_half in ((near_at, near), (far_at, jnp.logical_not(near))):
            if isinstance(block, int) and at[1] != block:
                continue
            here = jnp.logical_and(in_half, jnp.logical_and(y == at[0], block == at[1]))
            place = place + n * here.astype(jnp.int32)
    return ref.at[place]


def cell_plane(ref, y, cell, k):
    return at_block(ref, y, cell // 2)[pl.ds((cell % 2) * CELL_ROWS + k * ROWS, ROWS), :]


def partner_kernel(all_ref, out_ref):
    own_inst = lax.axis_index("inst")
    own_y, core = own_inst >> 1, own_inst & 1
    _, first_inst, _ = plane_masks()
    one, three = time_weights(first_inst, 1), time_weights(first_inst, 3)
    near = [jnp.where(core == 0, a, b) for a, b in zip(one, three)]
    away = [jnp.where(core == 0, b, a) for a, b in zip(one, three)]
    cells = 2 * (all_ref.shape[0] // 2)
    for cell in range(cells):
        for k in range(PAIRS):
            here = cell_plane(all_ref, own_y, cell, k)
            there = cell_plane(all_ref, 1 - own_y, cell, k)
            out_ref[pl.ds(cell * CELL_ROWS + k * ROWS, ROWS), :] = (
                near[0] * here
                + away[0] * there
                + turn_insts(first_inst, near[1] * here + away[1] * there)
            )


def two_by_two(first, second):
    def entry(a, b, c, d):
        terms = [x * y for x, y in ((a, b), (c, d)) if x is not None and y is not None]
        return None if not terms else terms[0] if len(terms) == 1 else terms[0] + terms[1]

    return (
        entry(first[0], second[0], first[1], second[2]),
        entry(first[0], second[1], first[1], second[3]),
        entry(first[2], second[0], first[3], second[2]),
        entry(first[2], second[1], first[3], second[3]),
    )


def inverse_of(matrix):
    reciprocal = 1.0 / (matrix[0] * matrix[3] - matrix[1] * matrix[2])
    return (
        matrix[3] * reciprocal,
        -(matrix[1] * reciprocal),
        -(matrix[2] * reciprocal),
        matrix[0] * reciprocal,
    )


def less(first, second):
    return tuple(a if b is None else a - b for a, b in zip(first, second))


def minus(members):
    return tuple(None if a is None else -a for a in members)


def matrix_vector(matrix, low, high):
    def row(a, b):
        terms = [x * y for x, y in ((a, low), (b, high)) if x is not None]
        return terms[0] if len(terms) == 1 else terms[0] + terms[1]

    return row(matrix[0], matrix[1]), row(matrix[2], matrix[3])


def apply_matrix(matrix, side):
    parts = [matrix_vector(matrix, side[k], side[PAIRS + k]) for k in range(PAIRS)]
    return [low for low, _ in parts] + [high for _, high in parts]


def difference(first, second):
    return [a - b for a, b in zip(first, second)]


def flux_along(first_var, planes, velocity, pressure, sign):
    normal = sign * velocity
    return [
        planes[0] * normal + jnp.where(first_var, 0.0, sign * pressure),
        planes[1] * normal,
        planes[2] * normal + jnp.where(first_var, pressure * normal, 0.0),
    ]


class LineCells:
    def __init__(self, first_var, sign):
        self.first_var, self.sign = first_var, sign
        self.state, self.pressure, self.radius = {}, {}, {}
        self.flux, self.step, self.sensor = {}, {}, {}

    def add(self, cell, planes, velocity, pressure, sound):
        self.state[cell], self.pressure[cell] = planes, pressure
        self.radius[cell] = jnp.abs(velocity) + sound
        self.flux[cell] = flux_along(self.first_var, planes, velocity, pressure, self.sign)
        if cell - 1 in self.state:
            self.step[cell - 1] = difference(planes, self.state[cell - 1])
        if cell - 2 in self.state:
            twice = 2.0 * self.pressure[cell - 1]
            outer = pressure + self.pressure[cell - 2]
            self.sensor[cell - 1] = jnp.abs(outer - twice) / (outer + twice)

    def face(self, cell):
        second = SENSOR_GAIN * jnp.maximum(self.sensor[cell], self.sensor[cell + 1])
        fourth = jnp.maximum(0.0, FOURTH_GAIN - second)
        face_radius = 0.5 * (self.radius[cell] + self.radius[cell + 1])
        near_weight = face_radius * (second + 2.0 * fourth)
        far_weight = face_radius * fourth
        return [
            0.5 * (self.flux[cell][k] + self.flux[cell + 1][k])
            - (
                near_weight * self.step[cell][k]
                - far_weight * (self.step[cell + 1][k] + self.step[cell - 1][k])
            )
            for k in range(PAIRS)
        ]

    def near(self, cell):
        scale = SECOND_IMPL * 0.5 + 2.0 * FOURTH_IMPL
        return -scale * (self.radius[cell] + self.radius[cell + 1])

    def far(self, cell):
        return FOURTH_IMPL * self.radius[cell]

    def middle(self, cell, rate):
        centre, above = self.radius[cell], self.radius[cell + 1]
        if cell == 0:
            total, weighted = centre + (centre + above), 4.0 * centre + above
        else:
            below = self.radius[cell - 1]
            total = (below + centre) + (centre + above)
            weighted = below + 4.0 * centre + above
        result = SECOND_IMPL * (0.5 * total) + FOURTH_IMPL * weighted
        return result if rate is None else rate * centre + result

    def diagonal(self, cell, rates):
        across = self.near(cell)
        return (self.middle(cell, rates[0]), across, across, self.middle(cell + 1, rates[1]))

    def below(self, cell):
        return (self.far(cell - 1), self.near(cell - 1), None, self.far(cell))

    def above(self, cell):
        return (self.far(cell + 1), None, self.near(cell + 1), self.far(cell + 2))


def rates_at(ref, y, block, first_half):
    rows = [at_block(ref, y, block)[pl.ds(RATE_ROW + k, 1), :] for k in range(4)]
    return [jnp.where(first_half, rows[2 * k], rows[2 * k + 1]) for k in range(2)]


def near_half_kernel(all_ref, next_ref, codes_ref, *refs):
    *results, middle_ref, round_ref, third_ref, line_ref = refs
    own_y = lax.axis_index("inst") >> 1
    cells = 2 * (all_ref.shape[0] // 2)
    for cell in range(cells - MIDDLE_CELLS, cells):
        for k in range(PAIRS):
            row = (cell - (cells - MIDDLE_CELLS)) * CELL_ROWS + k * ROWS
            middle_ref[pl.ds(row, ROWS), :] = cell_plane(all_ref, own_y, cell, k)
    for cell in range(ROUND_CELLS):
        for k in range(PAIRS):
            plane = cell_plane(all_ref, own_y, cells - 1 - cell, k)
            round_ref[pl.ds(cell * CELL_ROWS + k * ROWS, ROWS), :] = plane
    for k in range(PAIRS):
        third = cell_plane(all_ref, own_y, cells - MIDDLE_CELLS - 1, k)
        third_ref[pl.ds(k * ROWS, ROWS), :] = third

    @pl.when(lax.axis_index("cell") < (all_ref.shape[0] // 2))
    def _():
        half_kernel(all_ref, next_ref, codes_ref, *results, line_ref)


def far_half_kernel(all_ref, next_ref, codes_ref, *refs):
    *refs, line_ref = refs
    given, results = refs[: len(refs) // 2], refs[len(refs) // 2 :]
    far = lax.axis_index("cell") >= (all_ref.shape[0] // 2)

    @pl.when(far)
    def _():
        half_kernel(all_ref, next_ref, codes_ref, *results, line_ref)

    @pl.when(jnp.logical_not(far))
    def _():
        for source, target in zip(given, results):
            target[...] = source[...]


def half_kernel(
    all_ref, next_ref, codes_ref, partial_ref, factor_ref, blocks_ref, correction_ref,
    line_ref,
):
    own_y = lax.axis_index("inst") >> 1
    blocks = (all_ref.shape[0] // 2)
    cells = 2 * blocks
    mirrored = lax.axis_index("cell") // blocks
    sign = (1 - 2 * mirrored).astype(jnp.float32)
    shape = (ROWS, LANES)
    lane_index = lax.broadcasted_iota(jnp.int32, shape, 1)
    first_var, first_inst, half_index = plane_masks()
    first_half = half_index == 0
    zero = jnp.zeros(shape, jnp.float32)

    next_rows = [
        next_ref[pl.ds(half * LANES, LANES)].reshape(1, LANES) for half in range(2)
    ]
    next_line = jnp.where(first_half, next_rows[0], next_rows[1])
    column = lax.broadcasted_iota(jnp.int32, (LANES, LANES), 0)
    prev_halves = []
    for target in range(2):
        total = None
        for source in range(2):
            hits = jnp.where(column + target * LANES == next_rows[source], 1.0, 0.0)
            names = (lane_index + source * LANES).astype(jnp.float32)
            part = lax.dot_general(
                names, hits, (((1,), (1,)), ((), ())), preferred_element_type=jnp.float32
            )
            total = part if total is None else total + part
        prev_halves.append(total)
    prev_line = jnp.where(first_half, prev_halves[0], prev_halves[1]).astype(jnp.int32)

    def picker(lines):
        lane = lines & (LANES - 1)
        same = (lines >> 7) == half_index

        def pick(plane):
            swapped = jnp.where(first_half, pltpu.roll(plane, 7, 0), pltpu.roll(plane, 1, 0))
            here = jnp.take_along_axis(plane, lane, axis=1, mode="promise_in_bounds")
            there = jnp.take_along_axis(swapped, lane, axis=1, mode="promise_in_bounds")
            return jnp.where(same, here, there)

        return pick

    pick_next = picker(next_line)
    pick_prev = picker(prev_line)

    def loaded(cell, y=own_y):
        return [cell_plane(all_ref, y, cell, k) for k in range(PAIRS)]

    own_weights, away_weights = time_weights(first_inst, 0), time_weights(first_inst, 2)

    def own_time_parts(planes, cell):
        return [
            away_weights[0] * away
            + turn_insts(first_inst, own_weights[1] * own + away_weights[1] * away)
            for own, away in zip(planes, loaded(cell, 1 - own_y))
        ]

    def flux_across(planes, velocity, pressure):
        return [
            planes[0] * velocity,
            planes[1] * velocity + jnp.where(first_var, pressure, 0.0),
            planes[2] * velocity + jnp.where(first_var, pressure * velocity, 0.0),
        ]

    def pitch_flux(planes, velocity_y, pressure, sound):
        nearby = [pick_next(plane) for plane in planes]
        _, next_velocity, next_pressure, next_sound = primitives(first_var, nearby)
        own_flux = flux_across(planes, velocity_y, pressure)
        next_flux = flux_across(nearby, next_velocity, next_pressure)
        weight = (PITCH_GAIN * 0.5) * (
            jnp.abs(velocity_y) + sound + (jnp.abs(next_velocity) + next_sound)
        )
        return [
            0.5 * (a + b) - weight * (n - o)
            for a, b, n, o in zip(own_flux, next_flux, nearby, planes)
        ]

    for cell in range(cells):
        planes = loaded(cell)
        velocity_x, velocity_y, pressure, sound = primitives(first_var, planes)
        line_ref[cell, 0], line_ref[cell, 1], line_ref[cell, 2] = velocity_x, pressure, sound
        faces_across = pitch_flux(planes, velocity_y, pressure, sound)
        times = own_time_parts(planes, cell)
        for k in range(PAIRS):
            partial_ref[cell, k] = -(times[k] + (faces_across[k] - pick_prev(faces_across[k])))

    tile = half_index * (LANES // LINES_DEV) + lane_index // LINES_DEV
    end_codes = jnp.where(mirrored == 0, codes_ref[pl.ds(0, 1), :], codes_ref[pl.ds(1, 1), :])
    codes = jnp.zeros(shape, jnp.int32)
    for k in range(2 * LANES // LINES_DEV):
        codes = jnp.where(tile == k, jnp.broadcast_to(end_codes[:, k : k + 1], shape), codes)

    def ghost(cell):
        planes = loaded(-1 - cell)
        copied = loaded(0)
        result = []
        for k in range(PAIRS):
            reflected = planes[k] if k else jnp.where(first_var, planes[k], -planes[k])
            inflow = jnp.where(first_var, FREE_STATE[2 * k], FREE_STATE[2 * k + 1])
            result.append(
                jnp.where(codes == 0, reflected, jnp.where(codes == 1, inflow, copied[k]))
            )
        return result

    line = LineCells(first_var, sign)
    faces, inverses, aboves = {}, [], []
    for cell in range(-2, cells):
        if cell < 0:
            planes = ghost(cell)
            velocity_x, _, pressure, sound = primitives(first_var, planes)
        else:
            planes = loaded(cell)
            velocity_x, pressure, sound = [line_ref[cell, k] for k in range(3)]
        line.add(cell, planes, velocity_x, pressure, sound)
        if cell >= 1:
            faces[cell - 2] = line.face(cell - 2)
        if cell >= 2:
            at = cell - 2
            for k in range(PAIRS):
                partial_ref[at, k] = partial_ref[at, k] + (faces[at - 1][k] - faces[at][k])
        if cell >= 3 and cell % 2 == 1:
            at = cell - 3
            block = at // 2
            rates = rates_at(all_ref, own_y, block, first_half)
            diag = line.diagonal(at, rates)
            if block > 0:
                factor = two_by_two(line.below(at), inverses[-1])
                diag = less(diag, two_by_two(factor, aboves[-1]))
                for n in range(4):
                    factor_ref[block - 1, n] = factor[n]
            inverses.append(inverse_of(diag))
            aboves.append(line.above(at))
            kept = [*inverses[-1], aboves[-1][0], *aboves[-1][2:]]
            for n, plane in enumerate(kept):
                blocks_ref[block, n] = plane

    last = cells - 2
    for k in range(PAIRS):
        partial_ref[last, k] = partial_ref[last, k] + faces[last - 1][k]
    factor = two_by_two(line.below(last), inverses[-1])
    for n in range(4):
        factor_ref[blocks - 2, n] = factor[n]
    correction = list(two_by_two(factor, aboves[-1]))
    rates = rates_at(all_ref, own_y, blocks - 1, first_half)
    for member in range(2):
        centre = line.radius[last + member]
        correction[3 * member] = correction[3 * member] - rates[member] * centre
    for n in range(2):
        correction_ref[pl.ds(n * ROWS, ROWS), :] = jnp.where(
            first_var, correction[2 * n], correction[2 * n + 1]
        )


def reduce_kernel(
    partial_ref, time_ref, factor_ref, correction_ref, here_ref, third_ref, middle_ref, sides_ref,
    again_ref,
):
    again_ref[...] = here_ref[...]
    middle_ref[pl.ds(THIRD_ROW, CELL_ROWS), :] = third_ref[...]
    for row in range(0, 2 * ROWS, ROWS):
        middle_ref[pl.ds(CORRECTION_ROW + row, ROWS), :] = correction_ref[pl.ds(row, ROWS), :]
    blocks = partial_ref.shape[0] // 2
    side = None
    for block in range(blocks):
        own = []
        for cell in (2 * block, 2 * block + 1):
            for k in range(PAIRS):
                time = time_ref[pl.ds(cell * CELL_ROWS + k * ROWS, ROWS), :]
                own.append(partial_ref[cell, k] - time)
        if block > 0:
            factor = [factor_ref[block - 1, n] for n in range(4)]
            own = difference(own, apply_matrix(factor, side))
        side = own
        for n, plane in enumerate(side):
            if block < blocks - 1:
                sides_ref[block, n] = plane
            else:
                middle_ref[pl.ds(n * ROWS, ROWS), :] = plane


def spread_kernel(all_ref, blocks_ref, sides_ref, known_ref, spread_ref, table_ref):
    own_y = lax.axis_index("inst") >> 1
    blocks = (all_ref.shape[0] // 2)
    own_cell = lax.axis_index("cell")
    own_block = jnp.where(own_cell < blocks, own_cell, 2 * blocks - 1 - own_cell)
    zero = jnp.zeros((ROWS, LANES), jnp.float32)
    known, spread = [zero] * (2 * PAIRS), (zero + 1.0, zero, zero, zero + 1.0)
    for block in range(blocks - 1, -1, -1):
        if block < blocks - 1:
            kept = [blocks_ref[block, n] for n in range(7)]
            inverse, above = kept[:4], (kept[4], None, kept[5], kept[6])
            side = [sides_ref[block, n] for n in range(2 * PAIRS)]
            step = two_by_two(inverse, above)
            own = apply_matrix(inverse, side)
            if block < blocks - 2:
                known = difference(own, apply_matrix(step, known))
                spread = minus(two_by_two(step, spread))
            else:
                known, spread = own, minus(step)
        for n, plane in enumerate(known + list(spread)):
            table_ref[block, n] = plane
    for n in range(2 * PAIRS):
        base = at_block(all_ref, own_y, own_block)[pl.ds(n * ROWS, ROWS), :]
        known_ref[n] = base + table_ref[own_block, n]
    for n in range(4):
        spread_ref[n] = table_ref[own_block, 2 * PAIRS + n]


def plane_of(ref, row):
    return ref[pl.ds(row, ROWS), :]


def correction_of(first_var, ref):
    pairs = [both(first_var, plane_of(ref, CORRECTION_ROW + n * ROWS)) for n in range(2)]
    return [pairs[0][0], pairs[0][1], pairs[1][0], pairs[1][1]]


def middle_kernel(
    here_ref, first_ref, second_ref, here_side_ref, there_side_ref, side_ref, other_ref, matrix_ref
):
    own_cell, count = lax.axis_index("cell"), lax.axis_size("cell")
    mirrored = own_cell // (count // 2)
    outer = jnp.logical_or(own_cell < count // 4, own_cell >= count - count // 4)
    sign = (1 - 2 * mirrored).astype(jnp.float32)
    first_var, _, _ = plane_masks()
    line = LineCells(first_var, sign)
    for cell in range(6):
        at = cell if cell < 3 else 5 - cell
        rows = [(at - 1) * CELL_ROWS + k * ROWS for k in range(PAIRS)]
        if at == 0:
            ref = here_side_ref if cell < 3 else there_side_ref
            planes = [plane_of(ref, THIRD_ROW + k * ROWS) for k in range(PAIRS)]
        elif cell < 3:
            planes = [plane_of(here_ref, row) for row in rows]
        else:
            planes = [
                jnp.where(
                    outer,
                    plane_of(first_ref, (2 - at) * CELL_ROWS + k * ROWS),
                    plane_of(second_ref, row),
                )
                for k, row in enumerate(rows)
            ]
        velocity_x, _, pressure, sound = primitives(first_var, planes)
        line.add(cell, planes, velocity_x, pressure, sound)
    faces = {cell: line.face(cell) for cell in (1, 2, 3)}
    for k in range(PAIRS):
        side_ref[k] = plane_of(here_side_ref, k * ROWS) - faces[1][k]
        side_ref[PAIRS + k] = plane_of(here_side_ref, (PAIRS + k) * ROWS) + (
            faces[1][k] - faces[2][k]
        )
        other_ref[k] = plane_of(there_side_ref, (PAIRS + k) * ROWS) + (
            faces[2][k] - faces[3][k]
        )
        other_ref[PAIRS + k] = plane_of(there_side_ref, k * ROWS) + faces[3][k]
    no_rates = (None, None)
    diag = difference(line.diagonal(1, no_rates), correction_of(first_var, here_side_ref))
    above, below = line.above(1), line.below(3)
    kept = [*diag, *line.diagonal(3, no_rates), above[0], *above[2:], *below[:2], below[3]]
    for n, plane in enumerate(kept):
        matrix_ref[n] = plane


def join_kernel(
    side_ref, other_ref, matrix_ref, there_side_ref, known_ref, spread_ref, out_ref
):
    mirrored = lax.axis_index("cell") // (lax.axis_size("cell") // 2)
    first_var, _, _ = plane_masks()
    kept = [matrix_ref[n] for n in range(14)]
    diag, other_diag = kept[:4], kept[4:8]
    above, below = (kept[8], None, kept[9], kept[10]), (kept[11], kept[12], None, kept[13])
    other_diag = difference(other_diag, correction_of(first_var, there_side_ref)[::-1])
    other = [other_ref[n] for n in range(2 * PAIRS)]
    factor = two_by_two(above, inverse_of(other_diag))
    diag = less(diag, two_by_two(factor, below))
    side = [side_ref[n] for n in range(2 * PAIRS)]
    middle = apply_matrix(inverse_of(diag), difference(side, apply_matrix(factor, other)))
    moved = apply_matrix([spread_ref[n] for n in range(4)], middle)
    results = [known_ref[n] + moved[n] for n in range(2 * PAIRS)]
    for cell in range(2):
        for k in range(PAIRS):
            first, second = results[cell * PAIRS + k], results[(1 - cell) * PAIRS + k]
            result = jnp.where(mirrored == 0, first, second)
            for var in range(2):
                for inst in range(2):
                    for half in range(2):
                        row = rows_of(var, inst, half)
                        out_ref[
                            inst, 2 * k + var, pl.ds(cell, 1), pl.ds(half * LANES, LANES)
                        ] = result[row : row + 1]


def share_half(copies):
    count = lax.axis_size("cell")
    groups = [
        [(2 * y + core) * count + (count - 1 - block if far else block) for y, block in order]
        for core in range(2)
        for far, order in enumerate((NEAR_ORDER, FAR_ORDER))
    ]
    return lax.all_to_all(
        copies, ("inst", "cell"), split_axis=0, concat_axis=0, tiled=True,
        axis_index_groups=groups,
    )


def swap_cores(block):
    pairs = [(inst, inst ^ 1) for inst in range(lax.axis_size("inst"))]
    return lax.ppermute(block, "inst", pairs)


def swap_halves(block):
    count = lax.axis_size("cell")
    return lax.ppermute(block, "cell", [(i, (i + count // 2) % count) for i in range(count)])


def pass_round(block, steps):
    insts, count = lax.axis_size("inst"), lax.axis_size("cell")
    width = count // 4
    pairs = [
        (
            inst * count + source * width + i,
            (inst ^ (source == target)) * count + target * width + i,
        )
        for inst in range(insts)
        for source, target in steps
        for i in range(width)
    ]
    return lax.ppermute(block, ("inst", "cell"), pairs)


FIRST_ROUND = ((2, 0), (0, 1), (1, 3), (3, 2))
SECOND_ROUND = ((3, 1), (1, 2), (2, 3), (0, 0))


def float_shape(*sizes):
    return jax.ShapeDtypeStruct(sizes, jnp.float32)


def local_by_halves(state, pseudo_rate, line_next, face_codes):
    blocks = lax.axis_size("cell") // 2
    cells = 2 * blocks
    vmem = pl.BlockSpec(memory_space=pltpu.VMEM)
    plane = (ROWS, LANES)
    params = pltpu.CompilerParams(vmem_limit_bytes=VMEM_BYTES)
    places = lax.axis_size("inst") // 2
    held = [
        pltpu.with_memory_space_constraint(array, pltpu.HBM)
        for array in (state, pseudo_rate, line_next, face_codes)
    ]
    packed, next_here, codes_here = pl.pallas_call(
        pack_kernel,
        out_shape=(
            float_shape(places * blocks, BLOCK_ROWS, LANES),
            jax.ShapeDtypeStruct(line_next.shape, jnp.int32),
            jax.ShapeDtypeStruct(face_codes.shape, jnp.int32),
        ),
        in_specs=[pl.BlockSpec(memory_space=pltpu.HBM)] * 4,
        out_specs=(vmem, vmem, vmem),
        scratch_shapes=[
            pltpu.VMEM(state.shape, jnp.float32),
            pltpu.VMEM(pseudo_rate.shape, jnp.float32),
            pltpu.SemaphoreType.DMA((4,)),
        ],
        compiler_params=params,
    )(*held)
    shared = share_half(packed)
    for_partner = pl.pallas_call(
        partner_kernel,
        out_shape=float_shape(cells * CELL_ROWS, LANES),
        in_specs=[vmem],
        out_specs=vmem,
        compiler_params=params,
    )(shared)
    from_partner = swap_cores(for_partner)
    beside = pl.CostEstimate(flops=10**6, bytes_accessed=10**6, transcendentals=0)
    kinds = (
        float_shape(cells, PAIRS, *plane),
        float_shape(blocks - 1, 4, *plane),
        float_shape(blocks - 1, 7, *plane),
        float_shape(2 * ROWS, LANES),
    )
    line_scratch = [pltpu.VMEM((cells, 3) + plane, jnp.float32)]
    arguments = (shared, next_here, codes_here)
    *near, here, for_round, third = pl.pallas_call(
        near_half_kernel,
        out_shape=kinds
        + (
            float_shape(MIDDLE_CELLS * CELL_ROWS, LANES),
            float_shape(ROUND_CELLS * CELL_ROWS, LANES),
            float_shape(CELL_ROWS, LANES),
        ),
        in_specs=[vmem] * 3,
        out_specs=(vmem,) * 7,
        scratch_shapes=line_scratch,
        compiler_params=params,
    )(*arguments)
    there_first = pass_round(for_round, FIRST_ROUND)
    partial, factors, eliminated, correction = pl.pallas_call(
        far_half_kernel,
        out_shape=kinds,
        in_specs=[vmem] * 7,
        out_specs=(vmem,) * 4,
        scratch_shapes=line_scratch,
        input_output_aliases={3 + n: n for n in range(4)},
        compiler_params=params,
        cost_estimate=beside,
    )(*arguments, *near)
    here_side, sides, here_again = pl.pallas_call(
        reduce_kernel,
        out_shape=(
            float_shape(SIDE_ROWS, LANES),
            float_shape(blocks - 1, 2 * PAIRS, *plane),
            float_shape(MIDDLE_CELLS * CELL_ROWS, LANES),
        ),
        in_specs=[vmem] * 6,
        out_specs=(vmem,) * 3,
        compiler_params=params,
    )(partial, from_partner, factors, correction, here, third)
    there_side = swap_halves(here_side)
    there_second = pass_round(here_again, SECOND_ROUND)
    known, spread = pl.pallas_call(
        spread_kernel,
        out_shape=(float_shape(2 * PAIRS, *plane), float_shape(4, *plane)),
        in_specs=[vmem] * 3,
        out_specs=(vmem, vmem),
        scratch_shapes=[pltpu.VMEM((blocks, 2 * PAIRS + 4) + plane, jnp.float32)],
        compiler_params=params,
        cost_estimate=beside,
    )(shared, eliminated, sides)
    side, other, matrices = pl.pallas_call(
        middle_kernel,
        out_shape=(
            float_shape(2 * PAIRS, *plane),
            float_shape(2 * PAIRS, *plane),
            float_shape(14, *plane),
        ),
        in_specs=[vmem] * 5,
        out_specs=(vmem,) * 3,
        compiler_params=params,
    )(here, there_first, there_second, here_side, there_side)
    return pl.pallas_call(
        join_kernel,
        out_shape=float_shape(*state.shape),
        in_specs=[vmem] * 6,
        out_specs=vmem,
        compiler_params=params,
    )(side, other, matrices, there_side, known, spread)


def solution(mesh):
    placed = (P("inst", None, "cell", None), P("cell", None), P(), P())
    inst_count, cell_count = mesh.shape["inst"], mesh.shape["cell"]

    def local(state, pseudo_rate, line_next, face_codes):
        small = (
            state.shape == (2, 6, 2, 2 * LANES)
            and inst_count * 2 == NT
            and cell_count == 8
            and face_codes.shape[1] * LINES_DEV == state.shape[3]
        )
        chosen = local_by_halves if small else local_by_lines
        return chosen(state, pseudo_rate, line_next, face_codes)

    return jax.shard_map(
        local, mesh=mesh, in_specs=placed, out_specs=P("inst", None, "cell", None), check_vma=False
    )
```

```python
import functools

import jax
import jax.numpy as jnp
import numpy as np
from jax import lax
from jax.experimental import pallas as pl
from jax.experimental.pallas import tpu as pltpu
from jax.sharding import PartitionSpec as P

NT = 8
LINES_DEV = 32


GAMMA_GAS = 1.4
OMEGA_BLADE = 1.0
SENSOR_GAIN = 0.25
FOURTH_GAIN = 0.03125
PITCH_GAIN = 0.5
SECOND_IMPL = 1.0
FOURTH_IMPL = 0.25
FREE_STATE = (1.0, 0.5, 0.0, 0.0, 2.625, 0.2)
MIRROR_SIGNS = (1.0, -1.0, 1.0, 1.0, 1.0, 1.0)
ZERO_BLOCK = (0.0, 0.0, 0.0, 0.0)
UNIT_BLOCK = (1.0, 0.0, 0.0, 1.0)
ZERO_PAIR = (0.0, 0.0)


def extended(block, sides, width):
    for axis, dim in sides:
        count = lax.axis_size(axis)
        forward = [(i, i + 1) for i in range(count - 1)]
        backward = [(target, source) for source, target in forward]
        low = lax.ppermute(
            lax.slice_in_dim(block, block.shape[dim] - width, None, axis=dim), axis, forward
        )
        high = lax.ppermute(lax.slice_in_dim(block, 0, width, axis=dim), axis, backward)
        block = jnp.concatenate([low, block, high], axis=dim)
    return block


def spectral_matrix(instances):
    offsets = np.arange(instances)[:, None] - np.arange(instances)[None, :]
    angles = np.pi * offsets / instances
    safe_sin = np.where(offsets == 0, 1.0, np.sin(angles))
    parity = np.where(np.mod(offsets, 2) == 0, -1.0, 1.0)
    matrix_table = np.where(
        offsets == 0, 0.0, 0.5 * OMEGA_BLADE * parity * np.cos(angles) / safe_sin
    )
    return jnp.asarray(matrix_table, jnp.float32)


def primitive_parts(cells_state):
    density = cells_state[..., 0, :, :]
    inverse = 1.0 / density
    velocity_x = cells_state[..., 1, :, :] * inverse
    velocity_y = cells_state[..., 2, :, :] * inverse
    velocity_z = cells_state[..., 3, :, :] * inverse
    energy = cells_state[..., 4, :, :]
    pressure = (GAMMA_GAS - 1.0) * (
        energy
        - 0.5
        * density
        * (velocity_x * velocity_x + velocity_y * velocity_y + velocity_z * velocity_z)
    )
    sound_speed = jnp.sqrt(GAMMA_GAS * pressure * inverse)
    return (velocity_x, velocity_y, pressure, sound_speed)


def directed_flux(cells_state, normal_velocity, pressure, component):
    zero_plane = jnp.zeros_like(pressure)
    pressure_rows = [
        zero_plane,
        zero_plane,
        zero_plane,
        zero_plane,
        pressure * normal_velocity,
        zero_plane,
    ]
    pressure_rows[component] = pressure
    return cells_state * normal_velocity[..., None, :, :] + jnp.stack(pressure_rows, axis=-3)


def line_residual(padded):
    velocity_x, velocity_y, pressure, sound_speed = primitive_parts(padded)
    flux_line = directed_flux(padded, velocity_x, pressure, 1)
    radius = jnp.abs(velocity_x) + sound_speed
    sensor = jnp.abs(
        pressure[..., 2:, :] - 2.0 * pressure[..., 1:-1, :] + pressure[..., :-2, :]
    ) / (pressure[..., 2:, :] + 2.0 * pressure[..., 1:-1, :] + pressure[..., :-2, :])
    second = SENSOR_GAIN * jnp.maximum(sensor[..., :-1, :], sensor[..., 1:, :])
    fourth = jnp.maximum(0.0, FOURTH_GAIN - second)
    face_radius = 0.5 * (radius[..., 1:-2, :] + radius[..., 2:-1, :])
    left_far = padded[..., :-3, :]
    left_near = padded[..., 1:-2, :]
    right_near = padded[..., 2:-1, :]
    right_far = padded[..., 3:, :]
    damping = face_radius[..., None, :, :] * (
        second[..., None, :, :] * (right_near - left_near)
        - fourth[..., None, :, :] * (right_far - 3.0 * right_near + 3.0 * left_near - left_far)
    )
    face_flux = 0.5 * (flux_line[..., 1:-2, :] + flux_line[..., 2:-1, :]) - damping
    return (face_flux[..., 1:, :] - face_flux[..., :-1, :], radius)


def pitch_parts(cells_state):
    velocity_x, velocity_y, pressure, sound_speed = primitive_parts(cells_state)
    return (directed_flux(cells_state, velocity_y, pressure, 2), jnp.abs(velocity_y) + sound_speed)


def pitch_residual(cells_state, next_lines, prev_lines):
    pitch_flux, radius = pitch_parts(cells_state)
    state_next = jnp.take(cells_state, next_lines, axis=-1)
    flux_next, radius_next = pitch_parts(state_next)
    face_flux = 0.5 * (pitch_flux + flux_next) - PITCH_GAIN * (0.5 * (radius + radius_next))[
        ..., None, :, :
    ] * (state_next - cells_state)
    return face_flux - jnp.take(face_flux, prev_lines, axis=-1)


def boundary_cells(edge_pair, line_codes, lower_end):
    reflected = edge_pair[..., ::-1, :] * jnp.asarray(MIRROR_SIGNS, jnp.float32)[:, None, None]
    if lower_end:
        copied = jnp.concatenate([edge_pair[..., :1, :], edge_pair[..., :1, :]], axis=-2)
    else:
        copied = jnp.concatenate([edge_pair[..., 1:, :], edge_pair[..., 1:, :]], axis=-2)
    inflow = jnp.asarray(FREE_STATE, jnp.float32)[:, None, None] + jnp.zeros_like(edge_pair)
    return jnp.where(line_codes == 0, reflected, jnp.where(line_codes == 1, inflow, copied))


def line_coefficients(radius_ext, diagonal_term, positions, total_cells):
    radius_below = radius_ext[..., :-2, :]
    radius_centre = radius_ext[..., 1:-1, :]
    radius_above = radius_ext[..., 2:, :]
    face_below = 0.5 * (radius_below + radius_centre)
    face_above = 0.5 * (radius_centre + radius_above)
    far_low = FOURTH_IMPL * radius_below
    near_low = -SECOND_IMPL * face_below - 2.0 * FOURTH_IMPL * (radius_below + radius_centre)
    middle = (
        diagonal_term
        + SECOND_IMPL * (face_below + face_above)
        + FOURTH_IMPL * (radius_below + 4.0 * radius_centre + radius_above)
    )
    near_high = -SECOND_IMPL * face_above - 2.0 * FOURTH_IMPL * (radius_centre + radius_above)
    far_high = FOURTH_IMPL * radius_above
    column = positions[:, None]
    far_low = jnp.where(column >= 2, far_low, 0.0)
    near_low = jnp.where(column >= 1, near_low, 0.0)
    near_high = jnp.where(column <= total_cells - 2, near_high, 0.0)
    far_high = jnp.where(column <= total_cells - 3, far_high, 0.0)
    return (far_low, near_low, middle, near_high, far_high)


def block_product(first_matrix, second_matrix):
    return (
        first_matrix[0] * second_matrix[0] + first_matrix[1] * second_matrix[2],
        first_matrix[0] * second_matrix[1] + first_matrix[1] * second_matrix[3],
        first_matrix[2] * second_matrix[0] + first_matrix[3] * second_matrix[2],
        first_matrix[2] * second_matrix[1] + first_matrix[3] * second_matrix[3],
    )


def block_inverse(matrix):
    determinant = matrix[0] * matrix[3] - matrix[1] * matrix[2]
    reciprocal = 1.0 / determinant
    return (
        matrix[3] * reciprocal,
        -matrix[1] * reciprocal,
        -matrix[2] * reciprocal,
        matrix[0] * reciprocal,
    )


def block_apply(matrix, vector):
    return (
        matrix[0] * vector[0] + matrix[1] * vector[1],
        matrix[2] * vector[0] + matrix[3] * vector[1],
    )


def add_blocks(first_members, second_members):
    return tuple((a + b for a, b in zip(first_members, second_members)))


def negate(members):
    return tuple((-a for a in members))


def extend_blocks(members, fill_values):
    return tuple(
        (
            jnp.concatenate([m, jnp.full_like(m[..., :1, :], f)], axis=-2)
            for m, f in zip(members, fill_values)
        )
    )


def shift_next(members, fill_values):
    return tuple(
        (
            jnp.concatenate([m[..., 1:, :], jnp.full_like(m[..., :1, :], f)], axis=-2)
            for m, f in zip(members, fill_values)
        )
    )


def shift_prev(members):
    return tuple(
        (jnp.concatenate([jnp.zeros_like(m[..., :1, :]), m[..., :-1, :]], axis=-2) for m in members)
    )


def pair_split(member):
    shaped = member.reshape(member.shape[:-2] + (member.shape[-2] // 2, 2, member.shape[-1]))
    return (shaped[..., 0, :], shaped[..., 1, :])


def split_parity(members):
    halves = [pair_split(m) for m in members]
    return (tuple((h[0] for h in halves)), tuple((h[1] for h in halves)))


def alternate(first_member, second_member):
    stacked = jnp.stack((first_member, second_member), axis=-2)
    return stacked.reshape(
        first_member.shape[:-2] + (2 * first_member.shape[-2], first_member.shape[-1])
    )


def reduce_blocks(sub_blocks, diag_blocks, super_blocks, right_side):
    block_count = diag_blocks[0].shape[-2]
    if block_count == 1:
        return block_apply(block_inverse(diag_blocks), right_side)
    if block_count % 2 == 1:
        sub_blocks = extend_blocks(sub_blocks, ZERO_BLOCK)
        diag_blocks = extend_blocks(diag_blocks, UNIT_BLOCK)
        super_blocks = extend_blocks(super_blocks, ZERO_BLOCK)
        right_side = extend_blocks(right_side, ZERO_PAIR)
    sub_even, sub_odd = split_parity(sub_blocks)
    diag_even, diag_odd = split_parity(diag_blocks)
    super_even, super_odd = split_parity(super_blocks)
    side_even, side_odd = split_parity(right_side)
    inverse_even = block_inverse(diag_even)
    inverse_next = shift_next(inverse_even, UNIT_BLOCK)
    sub_next = shift_next(sub_even, ZERO_BLOCK)
    super_next = shift_next(super_even, ZERO_BLOCK)
    side_next = shift_next(side_even, ZERO_PAIR)
    left_factor = negate(block_product(sub_odd, inverse_even))
    right_factor = negate(block_product(super_odd, inverse_next))
    reduced_sub = block_product(left_factor, sub_even)
    reduced_diag = add_blocks(
        diag_odd,
        add_blocks(block_product(left_factor, super_even), block_product(right_factor, sub_next)),
    )
    reduced_super = block_product(right_factor, super_next)
    reduced_side = add_blocks(
        side_odd,
        add_blocks(block_apply(left_factor, side_even), block_apply(right_factor, side_next)),
    )
    odd_values = reduce_blocks(reduced_sub, reduced_diag, reduced_super, reduced_side)
    before_values = shift_prev(odd_values)
    remainder = add_blocks(
        side_even,
        negate(
            add_blocks(block_apply(sub_even, before_values), block_apply(super_even, odd_values))
        ),
    )
    even_values = block_apply(inverse_even, remainder)
    merged = tuple((alternate(e, o) for e, o in zip(even_values, odd_values)))
    return tuple((m[..., :block_count, :] for m in merged))


def cells_leading(block):
    moved = jnp.transpose(block, (2, 0, 1, 3))
    return moved.reshape(block.shape[2], block.shape[0] * block.shape[1] * block.shape[3])


def solve_in_lanes(coefficients, line_source):
    source_shape = line_source.shape
    lane_coef = [cells_leading(jnp.broadcast_to(c[:, None], source_shape)) for c in coefficients]
    pairs_list = [pair_split(m) for m in lane_coef]
    zero_plane = jnp.zeros_like(pairs_list[2][0])
    sub_blocks = (pairs_list[0][0], pairs_list[1][0], zero_plane, pairs_list[0][1])
    diag_blocks = (pairs_list[2][0], pairs_list[3][0], pairs_list[1][1], pairs_list[2][1])
    super_blocks = (pairs_list[4][0], zero_plane, pairs_list[3][1], pairs_list[4][1])
    values = reduce_blocks(
        sub_blocks, diag_blocks, super_blocks, pair_split(cells_leading(line_source))
    )
    flat = alternate(values[0], values[1])
    shaped = flat.reshape(source_shape[2], source_shape[0], source_shape[1], source_shape[3])
    return jnp.transpose(shaped, (1, 2, 0, 3))


def return_tiles(line_values):
    return lax.all_to_all(line_values, "cell", split_axis=2, concat_axis=3, tiled=True)


def local_by_lines(state, pseudo_rate, line_next, face_codes):
    local_count = state.shape[0]
    tile_cells = state.shape[2]
    cell_index = lax.axis_index("cell")
    cell_count = lax.axis_size("cell")
    total_cells = tile_cells * cell_count
    spectral = spectral_matrix(NT)
    first_local = lax.axis_index("inst") * local_count
    own_rows = lax.dynamic_slice_in_dim(spectral, first_local, local_count, 0)
    shard_block = jax.tree.map(lambda a: lax.all_gather(a, "inst", axis=0, tiled=True), state)
    columns = lax.slice_in_dim(own_rows, 0, shard_block.shape[0], axis=1)
    time_term = jnp.zeros_like(state) + jnp.einsum(
        "nm,mvil->nvil", columns, shard_block, precision=lax.Precision.HIGHEST
    )
    padded = extended(state, (("cell", 2),), 2)
    codes_lines = jnp.repeat(face_codes, LINES_DEV, axis=1)
    lower_ghost = boundary_cells(state[:, :, 0:2, :], codes_lines[0], True)
    upper_ghost = boundary_cells(state[:, :, -2:, :], codes_lines[1], False)
    lower_rim = jnp.where(cell_index == 0, lower_ghost, padded[:, :, :2, :])
    upper_rim = jnp.where(cell_index == cell_count - 1, upper_ghost, padded[:, :, -2:, :])
    padded = jnp.concatenate([lower_rim, padded[:, :, 2:-2, :], upper_rim], axis=2)
    line_part, radius = line_residual(padded)
    prev_lines = (
        jnp.zeros_like(line_next).at[line_next].set(jnp.arange(line_next.shape[0], dtype=jnp.int32))
    )
    residual = line_part + pitch_residual(state, line_next, prev_lines) + time_term
    right_side = -residual
    centre_radius = radius[:, 2:-2, :]
    diagonal_term = pseudo_rate * centre_radius
    positions = cell_index * tile_cells + jnp.arange(-1, tile_cells + 1, dtype=jnp.int32)
    inside = (positions >= 0) & (positions < total_cells)
    radius_ext = jnp.where(inside[:, None], radius[:, 1:-1, :], 0.0)
    coefficients = line_coefficients(radius_ext, diagonal_term, positions[1:-1], total_cells)
    stacked = jnp.stack(coefficients, axis=1)
    line_source = lax.all_to_all(right_side, "cell", split_axis=3, concat_axis=2, tiled=True)
    line_coef = lax.all_to_all(stacked, "cell", split_axis=3, concat_axis=2, tiled=True)
    update = return_tiles(solve_in_lanes(tuple((line_coef[:, k] for k in range(5))), line_source))
    return state + update


LANES = 128
ROWS = 8
PAIRS = 3
CELL_ROWS = PAIRS * ROWS
RATE_ROW = 2 * CELL_ROWS
VMEM_BYTES = 8 * 2**20
BLOCK_ROWS = RATE_ROW + ROWS

MIDDLE_CELLS = 2
ROUND_CELLS = 4
CORRECTION_ROW = 2 * CELL_ROWS
THIRD_ROW = CORRECTION_ROW + 2 * ROWS
SIDE_ROWS = THIRD_ROW + CELL_ROWS


def spectral_offsets():
    table = np.zeros(NT)
    for offset in range(1, NT):
        angle = np.pi * offset / NT
        parity = -1.0 if offset % 2 == 0 else 1.0
        table[offset] = 0.5 * OMEGA_BLADE * parity * np.cos(angle) / np.sin(angle)
    return [float(np.float32(value)) for value in table]


def plane_masks():
    row_index = lax.broadcasted_iota(jnp.int32, (ROWS, LANES), 0)
    return row_index < 4, (row_index & 2) == 0, row_index & 1


def both(first_var, plane):
    turned = pltpu.roll(plane, 4, 0)
    return jnp.where(first_var, plane, turned), jnp.where(first_var, turned, plane)


def primitives(first_var, planes):
    density, moment_x = both(first_var, planes[0])
    moment_y, moment_z = both(first_var, planes[1])
    energy = jnp.where(first_var, planes[2], pltpu.roll(planes[2], 4, 0))
    inverse = 1.0 / density
    velocity_x = moment_x * inverse
    velocity_y = moment_y * inverse
    velocity_z = moment_z * inverse
    kinetic = moment_x * velocity_x + moment_y * velocity_y + moment_z * velocity_z
    pressure = (GAMMA_GAS - 1.0) * (energy - 0.5 * kinetic)
    sound = jnp.sqrt(GAMMA_GAS * pressure * inverse)
    return velocity_x, velocity_y, pressure, sound


def rows_of(var, inst, half):
    return (var // 2) * ROWS + (var % 2) * 4 + inst * 2 + half


def pack_kernel(
    held_state_ref, held_rate_ref, held_next_ref, held_codes_ref, out_ref, next_ref, codes_ref,
    state_ref, rate_ref, sems,
):
    copies = [
        pltpu.make_async_copy(source, target, sems.at[k])
        for k, (source, target) in enumerate(
            (
                (held_state_ref, state_ref),
                (held_rate_ref, rate_ref),
                (held_next_ref, next_ref),
                (held_codes_ref, codes_ref),
            )
        )
    ]
    for copy in copies:
        copy.start()
    for copy in copies:
        copy.wait()
    mirrored = lax.axis_index("cell") // (lax.axis_size("cell") // 2)
    for cell in range(2):
        place = pl.multiple_of(jnp.bitwise_xor(cell, mirrored) * CELL_ROWS, ROWS)
        for k in range(PAIRS):
            rows = [
                state_ref[inst, 2 * k + var, pl.ds(cell, 1), pl.ds(half * LANES, LANES)]
                for var in range(2)
                for inst in range(2)
                for half in range(2)
            ]
            for row, values in enumerate(rows):
                out_ref[0, pl.ds(place + (k * ROWS + row), 1), :] = values
    rates = [
        rate_ref[pl.ds(cell, 1), pl.ds(half * LANES, LANES)]
        for cell in range(2)
        for half in range(2)
    ]
    for row in range(4):
        out_ref[0, pl.ds(RATE_ROW + row, 1), :] = jnp.where(
            mirrored == 0, rates[row], rates[row ^ 2]
        )
    out_ref[0, pl.ds(RATE_ROW + 4, 4), :] = jnp.zeros((4, LANES), jnp.float32)
    for row in range(0, BLOCK_ROWS, ROWS):
        values = out_ref[0, pl.ds(row, ROWS), :]
        for copy in range(1, out_ref.shape[0]):
            out_ref[copy, pl.ds(row, ROWS), :] = values


def turn_insts(first_inst, plane):
    return jnp.where(first_inst, pltpu.roll(plane, 6, 0), pltpu.roll(plane, 2, 0))


def time_weights(first_inst, shift):
    offsets = spectral_offsets()
    other = jnp.where(
        first_inst, offsets[(2 * shift + 1) % NT], offsets[(2 * shift - 1) % NT]
    )
    return offsets[(2 * shift) % NT], other


NEAR_ORDER = ((1, 3), (1, 2), (1, 1), (1, 0), (0, 3), (0, 2), (0, 1), (0, 0))
FAR_ORDER = ((1, 3), (1, 2), (1, 1), (1, 0), (0, 0), (0, 1), (0, 2), (0, 3))


def at_block(ref, y, block):
    blocks = ref.shape[0] // 2
    near = lax.axis_index("cell") < blocks
    place = 0
    for n, (near_at, far_at) in enumerate(zip(NEAR_ORDER, FAR_ORDER)):
        for at, in_half in ((near_at, near), (far_at, jnp.logical_not(near))):
            if isinstance(block, int) and at[1] != block:
                continue
            here = jnp.logical_and(in_half, jnp.logical_and(y == at[0], block == at[1]))
            place = place + n * here.astype(jnp.int32)
    return ref.at[place]


def cell_plane(ref, y, cell, k):
    return at_block(ref, y, cell // 2)[pl.ds((cell % 2) * CELL_ROWS + k * ROWS, ROWS), :]


def partner_kernel(all_ref, out_ref):
    own_inst = lax.axis_index("inst")
    own_y, core = own_inst >> 1, own_inst & 1
    _, first_inst, _ = plane_masks()
    one, three = time_weights(first_inst, 1), time_weights(first_inst, 3)
    near = [jnp.where(core == 0, a, b) for a, b in zip(one, three)]
    away = [jnp.where(core == 0, b, a) for a, b in zip(one, three)]
    cells = 2 * (all_ref.shape[0] // 2)
    for cell in range(cells):
        for k in range(PAIRS):
            here = cell_plane(all_ref, own_y, cell, k)
            there = cell_plane(all_ref, 1 - own_y, cell, k)
            out_ref[pl.ds(cell * CELL_ROWS + k * ROWS, ROWS), :] = (
                near[0] * here
                + away[0] * there
                + turn_insts(first_inst, near[1] * here + away[1] * there)
            )


def two_by_two(first, second):
    def entry(a, b, c, d):
        terms = [x * y for x, y in ((a, b), (c, d)) if x is not None and y is not None]
        return None if not terms else terms[0] if len(terms) == 1 else terms[0] + terms[1]

    return (
        entry(first[0], second[0], first[1], second[2]),
        entry(first[0], second[1], first[1], second[3]),
        entry(first[2], second[0], first[3], second[2]),
        entry(first[2], second[1], first[3], second[3]),
    )


def inverse_of(matrix):
    reciprocal = 1.0 / (matrix[0] * matrix[3] - matrix[1] * matrix[2])
    return (
        matrix[3] * reciprocal,
        -(matrix[1] * reciprocal),
        -(matrix[2] * reciprocal),
        matrix[0] * reciprocal,
    )


def less(first, second):
    return tuple(a if b is None else a - b for a, b in zip(first, second))


def minus(members):
    return tuple(None if a is None else -a for a in members)


def matrix_vector(matrix, low, high):
    def row(a, b):
        terms = [x * y for x, y in ((a, low), (b, high)) if x is not None]
        return terms[0] if len(terms) == 1 else terms[0] + terms[1]

    return row(matrix[0], matrix[1]), row(matrix[2], matrix[3])


def apply_matrix(matrix, side):
    parts = [matrix_vector(matrix, side[k], side[PAIRS + k]) for k in range(PAIRS)]
    return [low for low, _ in parts] + [high for _, high in parts]


def difference(first, second):
    return [a - b for a, b in zip(first, second)]


def flux_along(first_var, planes, velocity, pressure, sign):
    normal = sign * velocity
    return [
        planes[0] * normal + jnp.where(first_var, 0.0, sign * pressure),
        planes[1] * normal,
        planes[2] * normal + jnp.where(first_var, pressure * normal, 0.0),
    ]


class LineCells:
    def __init__(self, first_var, sign):
        self.first_var, self.sign = first_var, sign
        self.state, self.pressure, self.radius = {}, {}, {}
        self.flux, self.step, self.sensor = {}, {}, {}

    def add(self, cell, planes, velocity, pressure, sound):
        self.state[cell], self.pressure[cell] = planes, pressure
        self.radius[cell] = jnp.abs(velocity) + sound
        self.flux[cell] = flux_along(self.first_var, planes, velocity, pressure, self.sign)
        if cell - 1 in self.state:
            self.step[cell - 1] = difference(planes, self.state[cell - 1])
        if cell - 2 in self.state:
            twice = 2.0 * self.pressure[cell - 1]
            outer = pressure + self.pressure[cell - 2]
            self.sensor[cell - 1] = jnp.abs(outer - twice) / (outer + twice)

    def face(self, cell):
        second = SENSOR_GAIN * jnp.maximum(self.sensor[cell], self.sensor[cell + 1])
        fourth = jnp.maximum(0.0, FOURTH_GAIN - second)
        face_radius = 0.5 * (self.radius[cell] + self.radius[cell + 1])
        near_weight = face_radius * (second + 2.0 * fourth)
        far_weight = face_radius * fourth
        return [
            0.5 * (self.flux[cell][k] + self.flux[cell + 1][k])
            - (
                near_weight * self.step[cell][k]
                - far_weight * (self.step[cell + 1][k] + self.step[cell - 1][k])
            )
            for k in range(PAIRS)
        ]

    def near(self, cell):
        scale = SECOND_IMPL * 0.5 + 2.0 * FOURTH_IMPL
        return -scale * (self.radius[cell] + self.radius[cell + 1])

    def far(self, cell):
        return FOURTH_IMPL * self.radius[cell]

    def middle(self, cell, rate):
        centre, above = self.radius[cell], self.radius[cell + 1]
        if cell == 0:
            total, weighted = centre + (centre + above), 4.0 * centre + above
        else:
            below = self.radius[cell - 1]
            total = (below + centre) + (centre + above)
            weighted = below + 4.0 * centre + above
        result = SECOND_IMPL * (0.5 * total) + FOURTH_IMPL * weighted
        return result if rate is None else rate * centre + result

    def diagonal(self, cell, rates):
        across = self.near(cell)
        return (self.middle(cell, rates[0]), across, across, self.middle(cell + 1, rates[1]))

    def below(self, cell):
        return (self.far(cell - 1), self.near(cell - 1), None, self.far(cell))

    def above(self, cell):
        return (self.far(cell + 1), None, self.near(cell + 1), self.far(cell + 2))


def rates_at(ref, y, block, first_half):
    rows = [at_block(ref, y, block)[pl.ds(RATE_ROW + k, 1), :] for k in range(4)]
    return [jnp.where(first_half, rows[2 * k], rows[2 * k + 1]) for k in range(2)]


def near_half_kernel(all_ref, next_ref, codes_ref, *refs):
    *results, middle_ref, round_ref, third_ref, line_ref = refs
    own_y = lax.axis_index("inst") >> 1
    cells = 2 * (all_ref.shape[0] // 2)
    for cell in range(cells - MIDDLE_CELLS, cells):
        for k in range(PAIRS):
            row = (cell - (cells - MIDDLE_CELLS)) * CELL_ROWS + k * ROWS
            middle_ref[pl.ds(row, ROWS), :] = cell_plane(all_ref, own_y, cell, k)
    for cell in range(ROUND_CELLS):
        for k in range(PAIRS):
            plane = cell_plane(all_ref, own_y, cells - 1 - cell, k)
            round_ref[pl.ds(cell * CELL_ROWS + k * ROWS, ROWS), :] = plane
    for k in range(PAIRS):
        third = cell_plane(all_ref, own_y, cells - MIDDLE_CELLS - 1, k)
        third_ref[pl.ds(k * ROWS, ROWS), :] = third

    @pl.when(lax.axis_index("cell") < (all_ref.shape[0] // 2))
    def _():
        half_kernel(all_ref, next_ref, codes_ref, *results, line_ref)


def far_half_kernel(all_ref, next_ref, codes_ref, *refs):
    *refs, line_ref = refs
    given, results = refs[: len(refs) // 2], refs[len(refs) // 2 :]
    far = lax.axis_index("cell") >= (all_ref.shape[0] // 2)

    @pl.when(far)
    def _():
        half_kernel(all_ref, next_ref, codes_ref, *results, line_ref)

    @pl.when(jnp.logical_not(far))
    def _():
        for source, target in zip(given, results):
            target[...] = source[...]


def half_kernel(
    all_ref, next_ref, codes_ref, partial_ref, factor_ref, blocks_ref, correction_ref,
    line_ref,
):
    own_y = lax.axis_index("inst") >> 1
    blocks = (all_ref.shape[0] // 2)
    cells = 2 * blocks
    mirrored = lax.axis_index("cell") // blocks
    sign = (1 - 2 * mirrored).astype(jnp.float32)
    shape = (ROWS, LANES)
    lane_index = lax.broadcasted_iota(jnp.int32, shape, 1)
    first_var, first_inst, half_index = plane_masks()
    first_half = half_index == 0
    zero = jnp.zeros(shape, jnp.float32)

    next_rows = [
        next_ref[pl.ds(half * LANES, LANES)].reshape(1, LANES) for half in range(2)
    ]
    next_line = jnp.where(first_half, next_rows[0], next_rows[1])
    column = lax.broadcasted_iota(jnp.int32, (LANES, LANES), 0)
    prev_halves = []
    for target in range(2):
        total = None
        for source in range(2):
            hits = jnp.where(column + target * LANES == next_rows[source], 1.0, 0.0)
            names = (lane_index + source * LANES).astype(jnp.float32)
            part = lax.dot_general(
                names, hits, (((1,), (1,)), ((), ())), preferred_element_type=jnp.float32
            )
            total = part if total is None else total + part
        prev_halves.append(total)
    prev_line = jnp.where(first_half, prev_halves[0], prev_halves[1]).astype(jnp.int32)

    def picker(lines):
        lane = lines & (LANES - 1)
        same = (lines >> 7) == half_index

        def pick(plane):
            swapped = jnp.where(first_half, pltpu.roll(plane, 7, 0), pltpu.roll(plane, 1, 0))
            here = jnp.take_along_axis(plane, lane, axis=1, mode="promise_in_bounds")
            there = jnp.take_along_axis(swapped, lane, axis=1, mode="promise_in_bounds")
            return jnp.where(same, here, there)

        return pick

    pick_next = picker(next_line)
    pick_prev = picker(prev_line)

    def loaded(cell, y=own_y):
        return [cell_plane(all_ref, y, cell, k) for k in range(PAIRS)]

    own_weights, away_weights = time_weights(first_inst, 0), time_weights(first_inst, 2)

    def own_time_parts(planes, cell):
        return [
            away_weights[0] * away
            + turn_insts(first_inst, own_weights[1] * own + away_weights[1] * away)
            for own, away in zip(planes, loaded(cell, 1 - own_y))
        ]

    def flux_across(planes, velocity, pressure):
        return [
            planes[0] * velocity,
            planes[1] * velocity + jnp.where(first_var, pressure, 0.0),
            planes[2] * velocity + jnp.where(first_var, pressure * velocity, 0.0),
        ]

    def pitch_flux(planes, velocity_y, pressure, sound):
        nearby = [pick_next(plane) for plane in planes]
        _, next_velocity, next_pressure, next_sound = primitives(first_var, nearby)
        own_flux = flux_across(planes, velocity_y, pressure)
        next_flux = flux_across(nearby, next_velocity, next_pressure)
        weight = (PITCH_GAIN * 0.5) * (
            jnp.abs(velocity_y) + sound + (jnp.abs(next_velocity) + next_sound)
        )
        return [
            0.5 * (a + b) - weight * (n - o)
            for a, b, n, o in zip(own_flux, next_flux, nearby, planes)
        ]

    for cell in range(cells):
        planes = loaded(cell)
        velocity_x, velocity_y, pressure, sound = primitives(first_var, planes)
        line_ref[cell, 0], line_ref[cell, 1], line_ref[cell, 2] = velocity_x, pressure, sound
        faces_across = pitch_flux(planes, velocity_y, pressure, sound)
        times = own_time_parts(planes, cell)
        for k in range(PAIRS):
            partial_ref[cell, k] = -(times[k] + (faces_across[k] - pick_prev(faces_across[k])))

    tile = half_index * (LANES // LINES_DEV) + lane_index // LINES_DEV
    end_codes = jnp.where(mirrored == 0, codes_ref[pl.ds(0, 1), :], codes_ref[pl.ds(1, 1), :])
    codes = jnp.zeros(shape, jnp.int32)
    for k in range(2 * LANES // LINES_DEV):
        codes = jnp.where(tile == k, jnp.broadcast_to(end_codes[:, k : k + 1], shape), codes)

    def ghost(cell):
        planes = loaded(-1 - cell)
        copied = loaded(0)
        result = []
        for k in range(PAIRS):
            reflected = planes[k] if k else jnp.where(first_var, planes[k], -planes[k])
            inflow = jnp.where(first_var, FREE_STATE[2 * k], FREE_STATE[2 * k + 1])
            result.append(
                jnp.where(codes == 0, reflected, jnp.where(codes == 1, inflow, copied[k]))
            )
        return result

    line = LineCells(first_var, sign)
    faces, inverses, aboves = {}, [], []
    for cell in range(-2, cells):
        if cell < 0:
            planes = ghost(cell)
            velocity_x, _, pressure, sound = primitives(first_var, planes)
        else:
            planes = loaded(cell)
            velocity_x, pressure, sound = [line_ref[cell, k] for k in range(3)]
        line.add(cell, planes, velocity_x, pressure, sound)
        if cell >= 1:
            faces[cell - 2] = line.face(cell - 2)
        if cell >= 2:
            at = cell - 2
            for k in range(PAIRS):
                partial_ref[at, k] = partial_ref[at, k] + (faces[at - 1][k] - faces[at][k])
        if cell >= 3 and cell % 2 == 1:
            at = cell - 3
            block = at // 2
            rates = rates_at(all_ref, own_y, block, first_half)
            diag = line.diagonal(at, rates)
            if block > 0:
                factor = two_by_two(line.below(at), inverses[-1])
                diag = less(diag, two_by_two(factor, aboves[-1]))
                for n in range(4):
                    factor_ref[block - 1, n] = factor[n]
            inverses.append(inverse_of(diag))
            aboves.append(line.above(at))
            kept = [*inverses[-1], aboves[-1][0], *aboves[-1][2:]]
            for n, plane in enumerate(kept):
                blocks_ref[block, n] = plane

    last = cells - 2
    for k in range(PAIRS):
        partial_ref[last, k] = partial_ref[last, k] + faces[last - 1][k]
    factor = two_by_two(line.below(last), inverses[-1])
    for n in range(4):
        factor_ref[blocks - 2, n] = factor[n]
    correction = list(two_by_two(factor, aboves[-1]))
    rates = rates_at(all_ref, own_y, blocks - 1, first_half)
    for member in range(2):
        centre = line.radius[last + member]
        correction[3 * member] = correction[3 * member] - rates[member] * centre
    for n in range(2):
        correction_ref[pl.ds(n * ROWS, ROWS), :] = jnp.where(
            first_var, correction[2 * n], correction[2 * n + 1]
        )


def reduce_kernel(
    partial_ref, time_ref, factor_ref, correction_ref, here_ref, third_ref, middle_ref, sides_ref,
    again_ref,
):
    again_ref[...] = here_ref[...]
    middle_ref[pl.ds(THIRD_ROW, CELL_ROWS), :] = third_ref[...]
    for row in range(0, 2 * ROWS, ROWS):
        middle_ref[pl.ds(CORRECTION_ROW + row, ROWS), :] = correction_ref[pl.ds(row, ROWS), :]
    blocks = partial_ref.shape[0] // 2
    side = None
    for block in range(blocks):
        own = []
        for cell in (2 * block, 2 * block + 1):
            for k in range(PAIRS):
                time = time_ref[pl.ds(cell * CELL_ROWS + k * ROWS, ROWS), :]
                own.append(partial_ref[cell, k] - time)
        if block > 0:
            factor = [factor_ref[block - 1, n] for n in range(4)]
            own = difference(own, apply_matrix(factor, side))
        side = own
        for n, plane in enumerate(side):
            if block < blocks - 1:
                sides_ref[block, n] = plane
            else:
                middle_ref[pl.ds(n * ROWS, ROWS), :] = plane


def spread_kernel(all_ref, blocks_ref, sides_ref, known_ref, spread_ref, table_ref):
    own_y = lax.axis_index("inst") >> 1
    blocks = (all_ref.shape[0] // 2)
    own_cell = lax.axis_index("cell")
    own_block = jnp.where(own_cell < blocks, own_cell, 2 * blocks - 1 - own_cell)
    zero = jnp.zeros((ROWS, LANES), jnp.float32)
    known, spread = [zero] * (2 * PAIRS), (zero + 1.0, zero, zero, zero + 1.0)
    for block in range(blocks - 1, -1, -1):
        if block < blocks - 1:
            kept = [blocks_ref[block, n] for n in range(7)]
            inverse, above = kept[:4], (kept[4], None, kept[5], kept[6])
            side = [sides_ref[block, n] for n in range(2 * PAIRS)]
            step = two_by_two(inverse, above)
            own = apply_matrix(inverse, side)
            if block < blocks - 2:
                known = difference(own, apply_matrix(step, known))
                spread = minus(two_by_two(step, spread))
            else:
                known, spread = own, minus(step)
        for n, plane in enumerate(known + list(spread)):
            table_ref[block, n] = plane
    for n in range(2 * PAIRS):
        base = at_block(all_ref, own_y, own_block)[pl.ds(n * ROWS, ROWS), :]
        known_ref[n] = base + table_ref[own_block, n]
    for n in range(4):
        spread_ref[n] = table_ref[own_block, 2 * PAIRS + n]


def plane_of(ref, row):
    return ref[pl.ds(row, ROWS), :]


def correction_of(first_var, ref):
    pairs = [both(first_var, plane_of(ref, CORRECTION_ROW + n * ROWS)) for n in range(2)]
    return [pairs[0][0], pairs[0][1], pairs[1][0], pairs[1][1]]


def middle_kernel(
    here_ref, first_ref, second_ref, here_side_ref, there_side_ref, side_ref, other_ref, matrix_ref
):
    own_cell, count = lax.axis_index("cell"), lax.axis_size("cell")
    mirrored = own_cell // (count // 2)
    outer = jnp.logical_or(own_cell < count // 4, own_cell >= count - count // 4)
    sign = (1 - 2 * mirrored).astype(jnp.float32)
    first_var, _, _ = plane_masks()
    line = LineCells(first_var, sign)
    for cell in range(6):
        at = cell if cell < 3 else 5 - cell
        rows = [(at - 1) * CELL_ROWS + k * ROWS for k in range(PAIRS)]
        if at == 0:
            ref = here_side_ref if cell < 3 else there_side_ref
            planes = [plane_of(ref, THIRD_ROW + k * ROWS) for k in range(PAIRS)]
        elif cell < 3:
            planes = [plane_of(here_ref, row) for row in rows]
        else:
            planes = [
                jnp.where(
                    outer,
                    plane_of(first_ref, (2 - at) * CELL_ROWS + k * ROWS),
                    plane_of(second_ref, row),
                )
                for k, row in enumerate(rows)
            ]
        velocity_x, _, pressure, sound = primitives(first_var, planes)
        line.add(cell, planes, velocity_x, pressure, sound)
    faces = {cell: line.face(cell) for cell in (1, 2, 3)}
    for k in range(PAIRS):
        side_ref[k] = plane_of(here_side_ref, k * ROWS) - faces[1][k]
        side_ref[PAIRS + k] = plane_of(here_side_ref, (PAIRS + k) * ROWS) + (
            faces[1][k] - faces[2][k]
        )
        other_ref[k] = plane_of(there_side_ref, (PAIRS + k) * ROWS) + (
            faces[2][k] - faces[3][k]
        )
        other_ref[PAIRS + k] = plane_of(there_side_ref, k * ROWS) + faces[3][k]
    no_rates = (None, None)
    diag = difference(line.diagonal(1, no_rates), correction_of(first_var, here_side_ref))
    above, below = line.above(1), line.below(3)
    kept = [*diag, *line.diagonal(3, no_rates), above[0], *above[2:], *below[:2], below[3]]
    for n, plane in enumerate(kept):
        matrix_ref[n] = plane


def join_kernel(
    side_ref, other_ref, matrix_ref, there_side_ref, known_ref, spread_ref, out_ref
):
    mirrored = lax.axis_index("cell") // (lax.axis_size("cell") // 2)
    first_var, _, _ = plane_masks()
    kept = [matrix_ref[n] for n in range(14)]
    diag, other_diag = kept[:4], kept[4:8]
    above, below = (kept[8], None, kept[9], kept[10]), (kept[11], kept[12], None, kept[13])
    other_diag = difference(other_diag, correction_of(first_var, there_side_ref)[::-1])
    other = [other_ref[n] for n in range(2 * PAIRS)]
    factor = two_by_two(above, inverse_of(other_diag))
    diag = less(diag, two_by_two(factor, below))
    side = [side_ref[n] for n in range(2 * PAIRS)]
    middle = apply_matrix(inverse_of(diag), difference(side, apply_matrix(factor, other)))
    moved = apply_matrix([spread_ref[n] for n in range(4)], middle)
    results = [known_ref[n] + moved[n] for n in range(2 * PAIRS)]
    for cell in range(2):
        for k in range(PAIRS):
            first, second = results[cell * PAIRS + k], results[(1 - cell) * PAIRS + k]
            result = jnp.where(mirrored == 0, first, second)
            for var in range(2):
                for inst in range(2):
                    for half in range(2):
                        row = rows_of(var, inst, half)
                        out_ref[
                            inst, 2 * k + var, pl.ds(cell, 1), pl.ds(half * LANES, LANES)
                        ] = result[row : row + 1]


def share_half(copies):
    count = lax.axis_size("cell")
    groups = [
        [(2 * y + core) * count + (count - 1 - block if far else block) for y, block in order]
        for core in range(2)
        for far, order in enumerate((NEAR_ORDER, FAR_ORDER))
    ]
    return lax.all_to_all(
        copies, ("inst", "cell"), split_axis=0, concat_axis=0, tiled=True,
        axis_index_groups=groups,
    )


def swap_cores(block):
    pairs = [(inst, inst ^ 1) for inst in range(lax.axis_size("inst"))]
    return lax.ppermute(block, "inst", pairs)


def swap_halves(block):
    count = lax.axis_size("cell")
    return lax.ppermute(block, "cell", [(i, (i + count // 2) % count) for i in range(count)])


def pass_round(block, steps):
    insts, count = lax.axis_size("inst"), lax.axis_size("cell")
    width = count // 4
    pairs = [
        (
            inst * count + source * width + i,
            (inst ^ (source == target)) * count + target * width + i,
        )
        for inst in range(insts)
        for source, target in steps
        for i in range(width)
    ]
    return lax.ppermute(block, ("inst", "cell"), pairs)


FIRST_ROUND = ((2, 0), (0, 1), (1, 3), (3, 2))
SECOND_ROUND = ((3, 1), (1, 2), (2, 3), (0, 0))


def float_shape(*sizes):
    return jax.ShapeDtypeStruct(sizes, jnp.float32)


def local_by_halves(state, pseudo_rate, line_next, face_codes):
    blocks = lax.axis_size("cell") // 2
    cells = 2 * blocks
    vmem = pl.BlockSpec(memory_space=pltpu.VMEM)
    plane = (ROWS, LANES)
    params = pltpu.CompilerParams(vmem_limit_bytes=VMEM_BYTES)
    places = lax.axis_size("inst") // 2
    held = [
        pltpu.with_memory_space_constraint(array, pltpu.HBM)
        for array in (state, pseudo_rate, line_next, face_codes)
    ]
    packed, next_here, codes_here = pl.pallas_call(
        pack_kernel,
        out_shape=(
            float_shape(places * blocks, BLOCK_ROWS, LANES),
            jax.ShapeDtypeStruct(line_next.shape, jnp.int32),
            jax.ShapeDtypeStruct(face_codes.shape, jnp.int32),
        ),
        in_specs=[pl.BlockSpec(memory_space=pltpu.HBM)] * 4,
        out_specs=(vmem, vmem, vmem),
        scratch_shapes=[
            pltpu.VMEM(state.shape, jnp.float32),
            pltpu.VMEM(pseudo_rate.shape, jnp.float32),
            pltpu.SemaphoreType.DMA((4,)),
        ],
        compiler_params=params,
    )(*held)
    shared = share_half(packed)
    for_partner = pl.pallas_call(
        partner_kernel,
        out_shape=float_shape(cells * CELL_ROWS, LANES),
        in_specs=[vmem],
        out_specs=vmem,
        compiler_params=params,
    )(shared)
    from_partner = swap_cores(for_partner)
    beside = pl.CostEstimate(flops=10**6, bytes_accessed=10**6, transcendentals=0)
    kinds = (
        float_shape(cells, PAIRS, *plane),
        float_shape(blocks - 1, 4, *plane),
        float_shape(blocks - 1, 7, *plane),
        float_shape(2 * ROWS, LANES),
    )
    line_scratch = [pltpu.VMEM((cells, 3) + plane, jnp.float32)]
    arguments = (shared, next_here, codes_here)
    *near, here, for_round, third = pl.pallas_call(
        near_half_kernel,
        out_shape=kinds
        + (
            float_shape(MIDDLE_CELLS * CELL_ROWS, LANES),
            float_shape(ROUND_CELLS * CELL_ROWS, LANES),
            float_shape(CELL_ROWS, LANES),
        ),
        in_specs=[vmem] * 3,
        out_specs=(vmem,) * 7,
        scratch_shapes=line_scratch,
        compiler_params=params,
    )(*arguments)
    there_first = pass_round(for_round, FIRST_ROUND)
    partial, factors, eliminated, correction = pl.pallas_call(
        far_half_kernel,
        out_shape=kinds,
        in_specs=[vmem] * 7,
        out_specs=(vmem,) * 4,
        scratch_shapes=line_scratch,
        input_output_aliases={3 + n: n for n in range(4)},
        compiler_params=params,
        cost_estimate=beside,
    )(*arguments, *near)
    here_side, sides, here_again = pl.pallas_call(
        reduce_kernel,
        out_shape=(
            float_shape(SIDE_ROWS, LANES),
            float_shape(blocks - 1, 2 * PAIRS, *plane),
            float_shape(MIDDLE_CELLS * CELL_ROWS, LANES),
        ),
        in_specs=[vmem] * 6,
        out_specs=(vmem,) * 3,
        compiler_params=params,
    )(partial, from_partner, factors, correction, here, third)
    there_side = swap_halves(here_side)
    there_second = pass_round(here_again, SECOND_ROUND)
    known, spread = pl.pallas_call(
        spread_kernel,
        out_shape=(float_shape(2 * PAIRS, *plane), float_shape(4, *plane)),
        in_specs=[vmem] * 3,
        out_specs=(vmem, vmem),
        scratch_shapes=[pltpu.VMEM((blocks, 2 * PAIRS + 4) + plane, jnp.float32)],
        compiler_params=params,
        cost_estimate=beside,
    )(shared, eliminated, sides)
    side, other, matrices = pl.pallas_call(
        middle_kernel,
        out_shape=(
            float_shape(2 * PAIRS, *plane),
            float_shape(2 * PAIRS, *plane),
            float_shape(14, *plane),
        ),
        in_specs=[vmem] * 5,
        out_specs=(vmem,) * 3,
        compiler_params=params,
    )(here, there_first, there_second, here_side, there_side)
    return pl.pallas_call(
        join_kernel,
        out_shape=float_shape(*state.shape),
        in_specs=[vmem] * 6,
        out_specs=vmem,
        compiler_params=params,
    )(side, other, matrices, there_side, known, spread)


def solution(mesh):
    placed = (P("inst", None, "cell", None), P("cell", None), P(), P())
    inst_count, cell_count = mesh.shape["inst"], mesh.shape["cell"]

    def local(state, pseudo_rate, line_next, face_codes):
        small = (
            state.shape == (2, 6, 2, 2 * LANES)
            and inst_count * 2 == NT
            and cell_count == 8
            and face_codes.shape[1] * LINES_DEV == state.shape[3]
        )
        chosen = local_by_halves if small else local_by_lines
        return chosen(state, pseudo_rate, line_next, face_codes)

    return jax.shard_map(
        local, mesh=mesh, in_specs=placed, out_specs=P("inst", None, "cell", None), check_vma=False
    )
```

```python
import functools

import jax
import jax.numpy as jnp
import numpy as np
from jax import lax
from jax.experimental import pallas as pl
from jax.experimental.pallas import tpu as pltpu
from jax.sharding import PartitionSpec as P

NT = 8
LINES_DEV = 32


GAMMA_GAS = 1.4
OMEGA_BLADE = 1.0
SENSOR_GAIN = 0.25
FOURTH_GAIN = 0.03125
PITCH_GAIN = 0.5
SECOND_IMPL = 1.0
FOURTH_IMPL = 0.25
FREE_STATE = (1.0, 0.5, 0.0, 0.0, 2.625, 0.2)
MIRROR_SIGNS = (1.0, -1.0, 1.0, 1.0, 1.0, 1.0)
ZERO_BLOCK = (0.0, 0.0, 0.0, 0.0)
UNIT_BLOCK = (1.0, 0.0, 0.0, 1.0)
ZERO_PAIR = (0.0, 0.0)


def extended(block, sides, width):
    for axis, dim in sides:
        count = lax.axis_size(axis)
        forward = [(i, i + 1) for i in range(count - 1)]
        backward = [(target, source) for source, target in forward]
        low = lax.ppermute(
            lax.slice_in_dim(block, block.shape[dim] - width, None, axis=dim), axis, forward
        )
        high = lax.ppermute(lax.slice_in_dim(block, 0, width, axis=dim), axis, backward)
        block = jnp.concatenate([low, block, high], axis=dim)
    return block


def spectral_matrix(instances):
    offsets = np.arange(instances)[:, None] - np.arange(instances)[None, :]
    angles = np.pi * offsets / instances
    safe_sin = np.where(offsets == 0, 1.0, np.sin(angles))
    parity = np.where(np.mod(offsets, 2) == 0, -1.0, 1.0)
    matrix_table = np.where(
        offsets == 0, 0.0, 0.5 * OMEGA_BLADE * parity * np.cos(angles) / safe_sin
    )
    return jnp.asarray(matrix_table, jnp.float32)


def primitive_parts(cells_state):
    density = cells_state[..., 0, :, :]
    inverse = 1.0 / density
    velocity_x = cells_state[..., 1, :, :] * inverse
    velocity_y = cells_state[..., 2, :, :] * inverse
    velocity_z = cells_state[..., 3, :, :] * inverse
    energy = cells_state[..., 4, :, :]
    pressure = (GAMMA_GAS - 1.0) * (
        energy
        - 0.5
        * density
        * (velocity_x * velocity_x + velocity_y * velocity_y + velocity_z * velocity_z)
    )
    sound_speed = jnp.sqrt(GAMMA_GAS * pressure * inverse)
    return (velocity_x, velocity_y, pressure, sound_speed)


def directed_flux(cells_state, normal_velocity, pressure, component):
    zero_plane = jnp.zeros_like(pressure)
    pressure_rows = [
        zero_plane,
        zero_plane,
        zero_plane,
        zero_plane,
        pressure * normal_velocity,
        zero_plane,
    ]
    pressure_rows[component] = pressure
    return cells_state * normal_velocity[..., None, :, :] + jnp.stack(pressure_rows, axis=-3)


def line_residual(padded):
    velocity_x, velocity_y, pressure, sound_speed = primitive_parts(padded)
    flux_line = directed_flux(padded, velocity_x, pressure, 1)
    radius = jnp.abs(velocity_x) + sound_speed
    sensor = jnp.abs(
        pressure[..., 2:, :] - 2.0 * pressure[..., 1:-1, :] + pressure[..., :-2, :]
    ) / (pressure[..., 2:, :] + 2.0 * pressure[..., 1:-1, :] + pressure[..., :-2, :])
    second = SENSOR_GAIN * jnp.maximum(sensor[..., :-1, :], sensor[..., 1:, :])
    fourth = jnp.maximum(0.0, FOURTH_GAIN - second)
    face_radius = 0.5 * (radius[..., 1:-2, :] + radius[..., 2:-1, :])
    left_far = padded[..., :-3, :]
    left_near = padded[..., 1:-2, :]
    right_near = padded[..., 2:-1, :]
    right_far = padded[..., 3:, :]
    damping = face_radius[..., None, :, :] * (
        second[..., None, :, :] * (right_near - left_near)
        - fourth[..., None, :, :] * (right_far - 3.0 * right_near + 3.0 * left_near - left_far)
    )
    face_flux = 0.5 * (flux_line[..., 1:-2, :] + flux_line[..., 2:-1, :]) - damping
    return (face_flux[..., 1:, :] - face_flux[..., :-1, :], radius)


def pitch_parts(cells_state):
    velocity_x, velocity_y, pressure, sound_speed = primitive_parts(cells_state)
    return (directed_flux(cells_state, velocity_y, pressure, 2), jnp.abs(velocity_y) + sound_speed)


def pitch_residual(cells_state, next_lines, prev_lines):
    pitch_flux, radius = pitch_parts(cells_state)
    state_next = jnp.take(cells_state, next_lines, axis=-1)
    flux_next, radius_next = pitch_parts(state_next)
    face_flux = 0.5 * (pitch_flux + flux_next) - PITCH_GAIN * (0.5 * (radius + radius_next))[
        ..., None, :, :
    ] * (state_next - cells_state)
    return face_flux - jnp.take(face_flux, prev_lines, axis=-1)


def boundary_cells(edge_pair, line_codes, lower_end):
    reflected = edge_pair[..., ::-1, :] * jnp.asarray(MIRROR_SIGNS, jnp.float32)[:, None, None]
    if lower_end:
        copied = jnp.concatenate([edge_pair[..., :1, :], edge_pair[..., :1, :]], axis=-2)
    else:
        copied = jnp.concatenate([edge_pair[..., 1:, :], edge_pair[..., 1:, :]], axis=-2)
    inflow = jnp.asarray(FREE_STATE, jnp.float32)[:, None, None] + jnp.zeros_like(edge_pair)
    return jnp.where(line_codes == 0, reflected, jnp.where(line_codes == 1, inflow, copied))


def line_coefficients(radius_ext, diagonal_term, positions, total_cells):
    radius_below = radius_ext[..., :-2, :]
    radius_centre = radius_ext[..., 1:-1, :]
    radius_above = radius_ext[..., 2:, :]
    face_below = 0.5 * (radius_below + radius_centre)
    face_above = 0.5 * (radius_centre + radius_above)
    far_low = FOURTH_IMPL * radius_below
    near_low = -SECOND_IMPL * face_below - 2.0 * FOURTH_IMPL * (radius_below + radius_centre)
    middle = (
        diagonal_term
        + SECOND_IMPL * (face_below + face_above)
        + FOURTH_IMPL * (radius_below + 4.0 * radius_centre + radius_above)
    )
    near_high = -SECOND_IMPL * face_above - 2.0 * FOURTH_IMPL * (radius_centre + radius_above)
    far_high = FOURTH_IMPL * radius_above
    column = positions[:, None]
    far_low = jnp.where(column >= 2, far_low, 0.0)
    near_low = jnp.where(column >= 1, near_low, 0.0)
    near_high = jnp.where(column <= total_cells - 2, near_high, 0.0)
    far_high = jnp.where(column <= total_cells - 3, far_high, 0.0)
    return (far_low, near_low, middle, near_high, far_high)


def block_product(first_matrix, second_matrix):
    return (
        first_matrix[0] * second_matrix[0] + first_matrix[1] * second_matrix[2],
        first_matrix[0] * second_matrix[1] + first_matrix[1] * second_matrix[3],
        first_matrix[2] * second_matrix[0] + first_matrix[3] * second_matrix[2],
        first_matrix[2] * second_matrix[1] + first_matrix[3] * second_matrix[3],
    )


def block_inverse(matrix):
    determinant = matrix[0] * matrix[3] - matrix[1] * matrix[2]
    reciprocal = 1.0 / determinant
    return (
        matrix[3] * reciprocal,
        -matrix[1] * reciprocal,
        -matrix[2] * reciprocal,
        matrix[0] * reciprocal,
    )


def block_apply(matrix, vector):
    return (
        matrix[0] * vector[0] + matrix[1] * vector[1],
        matrix[2] * vector[0] + matrix[3] * vector[1],
    )


def add_blocks(first_members, second_members):
    return tuple((a + b for a, b in zip(first_members, second_members)))


def negate(members):
    return tuple((-a for a in members))


def extend_blocks(members, fill_values):
    return tuple(
        (
            jnp.concatenate([m, jnp.full_like(m[..., :1, :], f)], axis=-2)
            for m, f in zip(members, fill_values)
        )
    )


def shift_next(members, fill_values):
    return tuple(
        (
            jnp.concatenate([m[..., 1:, :], jnp.full_like(m[..., :1, :], f)], axis=-2)
            for m, f in zip(members, fill_values)
        )
    )


def shift_prev(members):
    return tuple(
        (jnp.concatenate([jnp.zeros_like(m[..., :1, :]), m[..., :-1, :]], axis=-2) for m in members)
    )


def pair_split(member):
    shaped = member.reshape(member.shape[:-2] + (member.shape[-2] // 2, 2, member.shape[-1]))
    return (shaped[..., 0, :], shaped[..., 1, :])


def split_parity(members):
    halves = [pair_split(m) for m in members]
    return (tuple((h[0] for h in halves)), tuple((h[1] for h in halves)))


def alternate(first_member, second_member):
    stacked = jnp.stack((first_member, second_member), axis=-2)
    return stacked.reshape(
        first_member.shape[:-2] + (2 * first_member.shape[-2], first_member.shape[-1])
    )


def reduce_blocks(sub_blocks, diag_blocks, super_blocks, right_side):
    block_count = diag_blocks[0].shape[-2]
    if block_count == 1:
        return block_apply(block_inverse(diag_blocks), right_side)
    if block_count % 2 == 1:
        sub_blocks = extend_blocks(sub_blocks, ZERO_BLOCK)
        diag_blocks = extend_blocks(diag_blocks, UNIT_BLOCK)
        super_blocks = extend_blocks(super_blocks, ZERO_BLOCK)
        right_side = extend_blocks(right_side, ZERO_PAIR)
    sub_even, sub_odd = split_parity(sub_blocks)
    diag_even, diag_odd = split_parity(diag_blocks)
    super_even, super_odd = split_parity(super_blocks)
    side_even, side_odd = split_parity(right_side)
    inverse_even = block_inverse(diag_even)
    inverse_next = shift_next(inverse_even, UNIT_BLOCK)
    sub_next = shift_next(sub_even, ZERO_BLOCK)
    super_next = shift_next(super_even, ZERO_BLOCK)
    side_next = shift_next(side_even, ZERO_PAIR)
    left_factor = negate(block_product(sub_odd, inverse_even))
    right_factor = negate(block_product(super_odd, inverse_next))
    reduced_sub = block_product(left_factor, sub_even)
    reduced_diag = add_blocks(
        diag_odd,
        add_blocks(block_product(left_factor, super_even), block_product(right_factor, sub_next)),
    )
    reduced_super = block_product(right_factor, super_next)
    reduced_side = add_blocks(
        side_odd,
        add_blocks(block_apply(left_factor, side_even), block_apply(right_factor, side_next)),
    )
    odd_values = reduce_blocks(reduced_sub, reduced_diag, reduced_super, reduced_side)
    before_values = shift_prev(odd_values)
    remainder = add_blocks(
        side_even,
        negate(
            add_blocks(block_apply(sub_even, before_values), block_apply(super_even, odd_values))
        ),
    )
    even_values = block_apply(inverse_even, remainder)
    merged = tuple((alternate(e, o) for e, o in zip(even_values, odd_values)))
    return tuple((m[..., :block_count, :] for m in merged))


def cells_leading(block):
    moved = jnp.transpose(block, (2, 0, 1, 3))
    return moved.reshape(block.shape[2], block.shape[0] * block.shape[1] * block.shape[3])


def solve_in_lanes(coefficients, line_source):
    source_shape = line_source.shape
    lane_coef = [cells_leading(jnp.broadcast_to(c[:, None], source_shape)) for c in coefficients]
    pairs_list = [pair_split(m) for m in lane_coef]
    zero_plane = jnp.zeros_like(pairs_list[2][0])
    sub_blocks = (pairs_list[0][0], pairs_list[1][0], zero_plane, pairs_list[0][1])
    diag_blocks = (pairs_list[2][0], pairs_list[3][0], pairs_list[1][1], pairs_list[2][1])
    super_blocks = (pairs_list[4][0], zero_plane, pairs_list[3][1], pairs_list[4][1])
    values = reduce_blocks(
        sub_blocks, diag_blocks, super_blocks, pair_split(cells_leading(line_source))
    )
    flat = alternate(values[0], values[1])
    shaped = flat.reshape(source_shape[2], source_shape[0], source_shape[1], source_shape[3])
    return jnp.transpose(shaped, (1, 2, 0, 3))


def return_tiles(line_values):
    return lax.all_to_all(line_values, "cell", split_axis=2, concat_axis=3, tiled=True)


def local_by_lines(state, pseudo_rate, line_next, face_codes):
    local_count = state.shape[0]
    tile_cells = state.shape[2]
    cell_index = lax.axis_index("cell")
    cell_count = lax.axis_size("cell")
    total_cells = tile_cells * cell_count
    spectral = spectral_matrix(NT)
    first_local = lax.axis_index("inst") * local_count
    own_rows = lax.dynamic_slice_in_dim(spectral, first_local, local_count, 0)
    shard_block = jax.tree.map(lambda a: lax.all_gather(a, "inst", axis=0, tiled=True), state)
    columns = lax.slice_in_dim(own_rows, 0, shard_block.shape[0], axis=1)
    time_term = jnp.zeros_like(state) + jnp.einsum(
        "nm,mvil->nvil", columns, shard_block, precision=lax.Precision.HIGHEST
    )
    padded = extended(state, (("cell", 2),), 2)
    codes_lines = jnp.repeat(face_codes, LINES_DEV, axis=1)
    lower_ghost = boundary_cells(state[:, :, 0:2, :], codes_lines[0], True)
    upper_ghost = boundary_cells(state[:, :, -2:, :], codes_lines[1], False)
    lower_rim = jnp.where(cell_index == 0, lower_ghost, padded[:, :, :2, :])
    upper_rim = jnp.where(cell_index == cell_count - 1, upper_ghost, padded[:, :, -2:, :])
    padded = jnp.concatenate([lower_rim, padded[:, :, 2:-2, :], upper_rim], axis=2)
    line_part, radius = line_residual(padded)
    prev_lines = (
        jnp.zeros_like(line_next).at[line_next].set(jnp.arange(line_next.shape[0], dtype=jnp.int32))
    )
    residual = line_part + pitch_residual(state, line_next, prev_lines) + time_term
    right_side = -residual
    centre_radius = radius[:, 2:-2, :]
    diagonal_term = pseudo_rate * centre_radius
    positions = cell_index * tile_cells + jnp.arange(-1, tile_cells + 1, dtype=jnp.int32)
    inside = (positions >= 0) & (positions < total_cells)
    radius_ext = jnp.where(inside[:, None], radius[:, 1:-1, :], 0.0)
    coefficients = line_coefficients(radius_ext, diagonal_term, positions[1:-1], total_cells)
    stacked = jnp.stack(coefficients, axis=1)
    line_source = lax.all_to_all(right_side, "cell", split_axis=3, concat_axis=2, tiled=True)
    line_coef = lax.all_to_all(stacked, "cell", split_axis=3, concat_axis=2, tiled=True)
    update = return_tiles(solve_in_lanes(tuple((line_coef[:, k] for k in range(5))), line_source))
    return state + update


LANES = 128
ROWS = 8
PAIRS = 3
CELL_ROWS = PAIRS * ROWS
RATE_ROW = 2 * CELL_ROWS
VMEM_BYTES = 8 * 2**20
BLOCK_ROWS = RATE_ROW + ROWS

MIDDLE_CELLS = 2
ROUND_CELLS = 4
CORRECTION_ROW = 2 * CELL_ROWS
THIRD_ROW = CORRECTION_ROW + 2 * ROWS
SIDE_ROWS = THIRD_ROW + CELL_ROWS


def spectral_offsets():
    table = np.zeros(NT)
    for offset in range(1, NT):
        angle = np.pi * offset / NT
        parity = -1.0 if offset % 2 == 0 else 1.0
        table[offset] = 0.5 * OMEGA_BLADE * parity * np.cos(angle) / np.sin(angle)
    return [float(np.float32(value)) for value in table]


def plane_masks():
    row_index = lax.broadcasted_iota(jnp.int32, (ROWS, LANES), 0)
    return row_index < 4, (row_index & 2) == 0, row_index & 1


def both(first_var, plane):
    turned = pltpu.roll(plane, 4, 0)
    return jnp.where(first_var, plane, turned), jnp.where(first_var, turned, plane)


def primitives(first_var, planes):
    density, moment_x = both(first_var, planes[0])
    moment_y, moment_z = both(first_var, planes[1])
    energy = jnp.where(first_var, planes[2], pltpu.roll(planes[2], 4, 0))
    inverse = 1.0 / density
    velocity_x = moment_x * inverse
    velocity_y = moment_y * inverse
    velocity_z = moment_z * inverse
    kinetic = moment_x * velocity_x + moment_y * velocity_y + moment_z * velocity_z
    pressure = (GAMMA_GAS - 1.0) * (energy - 0.5 * kinetic)
    sound = jnp.sqrt(GAMMA_GAS * pressure * inverse)
    return velocity_x, velocity_y, pressure, sound


def rows_of(var, inst, half):
    return (var // 2) * ROWS + (var % 2) * 4 + inst * 2 + half


def pack_kernel(
    held_state_ref, held_rate_ref, held_next_ref, held_codes_ref, out_ref, next_ref, codes_ref,
    state_ref, rate_ref, sems,
):
    copies = [
        pltpu.make_async_copy(source, target, sems.at[k])
        for k, (source, target) in enumerate(
            (
                (held_state_ref, state_ref),
                (held_rate_ref, rate_ref),
                (held_next_ref, next_ref),
                (held_codes_ref, codes_ref),
            )
        )
    ]
    for copy in copies:
        copy.start()
    for copy in copies:
        copy.wait()
    mirrored = lax.axis_index("cell") // (lax.axis_size("cell") // 2)
    for cell in range(2):
        place = pl.multiple_of(jnp.bitwise_xor(cell, mirrored) * CELL_ROWS, ROWS)
        for k in range(PAIRS):
            rows = [
                state_ref[inst, 2 * k + var, pl.ds(cell, 1), pl.ds(half * LANES, LANES)]
                for var in range(2)
                for inst in range(2)
                for half in range(2)
            ]
            for row, values in enumerate(rows):
                out_ref[0, pl.ds(place + (k * ROWS + row), 1), :] = values
    rates = [
        rate_ref[pl.ds(cell, 1), pl.ds(half * LANES, LANES)]
        for cell in range(2)
        for half in range(2)
    ]
    for row in range(4):
        out_ref[0, pl.ds(RATE_ROW + row, 1), :] = jnp.where(
            mirrored == 0, rates[row], rates[row ^ 2]
        )
    out_ref[0, pl.ds(RATE_ROW + 4, 4), :] = jnp.zeros((4, LANES), jnp.float32)
    for row in range(0, BLOCK_ROWS, ROWS):
        values = out_ref[0, pl.ds(row, ROWS), :]
        for copy in range(1, out_ref.shape[0]):
            out_ref[copy, pl.ds(row, ROWS), :] = values


def turn_insts(first_inst, plane):
    return jnp.where(first_inst, pltpu.roll(plane, 6, 0), pltpu.roll(plane, 2, 0))


def time_weights(first_inst, shift):
    offsets = spectral_offsets()
    other = jnp.where(
        first_inst, offsets[(2 * shift + 1) % NT], offsets[(2 * shift - 1) % NT]
    )
    return offsets[(2 * shift) % NT], other


def at_block(ref, y, block):
    blocks = ref.shape[1]
    mirrored = lax.axis_index("cell") // blocks
    place = mirrored * block + (1 - mirrored) * (blocks - 1 - block)
    return ref.at[ref.shape[0] - 1 - y, place]


def cell_plane(ref, y, cell, k):
    return at_block(ref, y, cell // 2)[pl.ds((cell % 2) * CELL_ROWS + k * ROWS, ROWS), :]


def partner_kernel(all_ref, out_ref):
    own_inst = lax.axis_index("inst")
    own_y, core = own_inst >> 1, own_inst & 1
    _, first_inst, _ = plane_masks()
    one, three = time_weights(first_inst, 1), time_weights(first_inst, 3)
    near = [jnp.where(core == 0, a, b) for a, b in zip(one, three)]
    away = [jnp.where(core == 0, b, a) for a, b in zip(one, three)]
    cells = 2 * all_ref.shape[1]
    for cell in range(cells):
        for k in range(PAIRS):
            here = cell_plane(all_ref, own_y, cell, k)
            there = cell_plane(all_ref, 1 - own_y, cell, k)
            out_ref[pl.ds(cell * CELL_ROWS + k * ROWS, ROWS), :] = (
                near[0] * here
                + away[0] * there
                + turn_insts(first_inst, near[1] * here + away[1] * there)
            )


def two_by_two(first, second):
    def entry(a, b, c, d):
        terms = [x * y for x, y in ((a, b), (c, d)) if x is not None and y is not None]
        return None if not terms else terms[0] if len(terms) == 1 else terms[0] + terms[1]

    return (
        entry(first[0], second[0], first[1], second[2]),
        entry(first[0], second[1], first[1], second[3]),
        entry(first[2], second[0], first[3], second[2]),
        entry(first[2], second[1], first[3], second[3]),
    )


def inverse_of(matrix):
    reciprocal = 1.0 / (matrix[0] * matrix[3] - matrix[1] * matrix[2])
    return (
        matrix[3] * reciprocal,
        -(matrix[1] * reciprocal),
        -(matrix[2] * reciprocal),
        matrix[0] * reciprocal,
    )


def less(first, second):
    return tuple(a if b is None else a - b for a, b in zip(first, second))


def minus(members):
    return tuple(None if a is None else -a for a in members)


def matrix_vector(matrix, low, high):
    def row(a, b):
        terms = [x * y for x, y in ((a, low), (b, high)) if x is not None]
        return terms[0] if len(terms) == 1 else terms[0] + terms[1]

    return row(matrix[0], matrix[1]), row(matrix[2], matrix[3])


def apply_matrix(matrix, side):
    parts = [matrix_vector(matrix, side[k], side[PAIRS + k]) for k in range(PAIRS)]
    return [low for low, _ in parts] + [high for _, high in parts]


def difference(first, second):
    return [a - b for a, b in zip(first, second)]


def flux_along(first_var, planes, velocity, pressure, sign):
    normal = sign * velocity
    return [
        planes[0] * normal + jnp.where(first_var, 0.0, sign * pressure),
        planes[1] * normal,
        planes[2] * normal + jnp.where(first_var, pressure * normal, 0.0),
    ]


class LineCells:
    def __init__(self, first_var, sign):
        self.first_var, self.sign = first_var, sign
        self.state, self.pressure, self.radius = {}, {}, {}
        self.flux, self.step, self.sensor = {}, {}, {}

    def add(self, cell, planes, velocity, pressure, sound):
        self.state[cell], self.pressure[cell] = planes, pressure
        self.radius[cell] = jnp.abs(velocity) + sound
        self.flux[cell] = flux_along(self.first_var, planes, velocity, pressure, self.sign)
        if cell - 1 in self.state:
            self.step[cell - 1] = difference(planes, self.state[cell - 1])
        if cell - 2 in self.state:
            twice = 2.0 * self.pressure[cell - 1]
            outer = pressure + self.pressure[cell - 2]
            self.sensor[cell - 1] = jnp.abs(outer - twice) / (outer + twice)

    def face(self, cell):
        second = SENSOR_GAIN * jnp.maximum(self.sensor[cell], self.sensor[cell + 1])
        fourth = jnp.maximum(0.0, FOURTH_GAIN - second)
        face_radius = 0.5 * (self.radius[cell] + self.radius[cell + 1])
        near_weight = face_radius * (second + 2.0 * fourth)
        far_weight = face_radius * fourth
        return [
            0.5 * (self.flux[cell][k] + self.flux[cell + 1][k])
            - (
                near_weight * self.step[cell][k]
                - far_weight * (self.step[cell + 1][k] + self.step[cell - 1][k])
            )
            for k in range(PAIRS)
        ]

    def near(self, cell):
        scale = SECOND_IMPL * 0.5 + 2.0 * FOURTH_IMPL
        return -scale * (self.radius[cell] + self.radius[cell + 1])

    def far(self, cell):
        return FOURTH_IMPL * self.radius[cell]

    def middle(self, cell, rate):
        centre, above = self.radius[cell], self.radius[cell + 1]
        if cell == 0:
            total, weighted = centre + (centre + above), 4.0 * centre + above
        else:
            below = self.radius[cell - 1]
            total = (below + centre) + (centre + above)
            weighted = below + 4.0 * centre + above
        result = SECOND_IMPL * (0.5 * total) + FOURTH_IMPL * weighted
        return result if rate is None else rate * centre + result

    def diagonal(self, cell, rates):
        across = self.near(cell)
        return (self.middle(cell, rates[0]), across, across, self.middle(cell + 1, rates[1]))

    def below(self, cell):
        return (self.far(cell - 1), self.near(cell - 1), None, self.far(cell))

    def above(self, cell):
        return (self.far(cell + 1), None, self.near(cell + 1), self.far(cell + 2))


def rates_at(ref, y, block, first_half):
    rows = [at_block(ref, y, block)[pl.ds(RATE_ROW + k, 1), :] for k in range(4)]
    return [jnp.where(first_half, rows[2 * k], rows[2 * k + 1]) for k in range(2)]


def near_half_kernel(all_ref, next_ref, codes_ref, *refs):
    *results, middle_ref, round_ref, third_ref, line_ref = refs
    own_y = lax.axis_index("inst") >> 1
    cells = 2 * all_ref.shape[1]
    for cell in range(cells - MIDDLE_CELLS, cells):
        for k in range(PAIRS):
            row = (cell - (cells - MIDDLE_CELLS)) * CELL_ROWS + k * ROWS
            middle_ref[pl.ds(row, ROWS), :] = cell_plane(all_ref, own_y, cell, k)
    for cell in range(ROUND_CELLS):
        for k in range(PAIRS):
            plane = cell_plane(all_ref, own_y, cells - 1 - cell, k)
            round_ref[pl.ds(cell * CELL_ROWS + k * ROWS, ROWS), :] = plane
    for k in range(PAIRS):
        third = cell_plane(all_ref, own_y, cells - MIDDLE_CELLS - 1, k)
        third_ref[pl.ds(k * ROWS, ROWS), :] = third

    @pl.when(lax.axis_index("cell") // (all_ref.shape[1] // 2) == 1)
    def _():
        half_kernel(all_ref, next_ref, codes_ref, *results, line_ref)


def far_half_kernel(all_ref, next_ref, codes_ref, *refs):
    *refs, line_ref = refs
    given, results = refs[: len(refs) // 2], refs[len(refs) // 2 :]
    far = lax.axis_index("cell") // (all_ref.shape[1] // 2) != 1

    @pl.when(far)
    def _():
        half_kernel(all_ref, next_ref, codes_ref, *results, line_ref)

    @pl.when(jnp.logical_not(far))
    def _():
        for source, target in zip(given, results):
            target[...] = source[...]


def half_kernel(
    all_ref, next_ref, codes_ref, partial_ref, factor_ref, blocks_ref, correction_ref,
    line_ref,
):
    own_y = lax.axis_index("inst") >> 1
    blocks = all_ref.shape[1]
    cells = 2 * blocks
    mirrored = lax.axis_index("cell") // blocks
    sign = (1 - 2 * mirrored).astype(jnp.float32)
    shape = (ROWS, LANES)
    lane_index = lax.broadcasted_iota(jnp.int32, shape, 1)
    first_var, first_inst, half_index = plane_masks()
    first_half = half_index == 0
    zero = jnp.zeros(shape, jnp.float32)

    next_rows = [
        next_ref[pl.ds(half * LANES, LANES)].reshape(1, LANES) for half in range(2)
    ]
    next_line = jnp.where(first_half, next_rows[0], next_rows[1])
    column = lax.broadcasted_iota(jnp.int32, (LANES, LANES), 0)
    prev_halves = []
    for target in range(2):
        total = None
        for source in range(2):
            hits = jnp.where(column + target * LANES == next_rows[source], 1.0, 0.0)
            names = (lane_index + source * LANES).astype(jnp.float32)
            part = lax.dot_general(
                names, hits, (((1,), (1,)), ((), ())), preferred_element_type=jnp.float32
            )
            total = part if total is None else total + part
        prev_halves.append(total)
    prev_line = jnp.where(first_half, prev_halves[0], prev_halves[1]).astype(jnp.int32)

    def picker(lines):
        lane = lines & (LANES - 1)
        same = (lines >> 7) == half_index

        def pick(plane):
            swapped = jnp.where(first_half, pltpu.roll(plane, 7, 0), pltpu.roll(plane, 1, 0))
            here = jnp.take_along_axis(plane, lane, axis=1, mode="promise_in_bounds")
            there = jnp.take_along_axis(swapped, lane, axis=1, mode="promise_in_bounds")
            return jnp.where(same, here, there)

        return pick

    pick_next = picker(next_line)
    pick_prev = picker(prev_line)

    def loaded(cell, y=own_y):
        return [cell_plane(all_ref, y, cell, k) for k in range(PAIRS)]

    own_weights, away_weights = time_weights(first_inst, 0), time_weights(first_inst, 2)

    def own_time_parts(planes, cell):
        return [
            away_weights[0] * away
            + turn_insts(first_inst, own_weights[1] * own + away_weights[1] * away)
            for own, away in zip(planes, loaded(cell, 1 - own_y))
        ]

    def flux_across(planes, velocity, pressure):
        return [
            planes[0] * velocity,
            planes[1] * velocity + jnp.where(first_var, pressure, 0.0),
            planes[2] * velocity + jnp.where(first_var, pressure * velocity, 0.0),
        ]

    def pitch_flux(planes, velocity_y, pressure, sound):
        nearby = [pick_next(plane) for plane in planes]
        _, next_velocity, next_pressure, next_sound = primitives(first_var, nearby)
        own_flux = flux_across(planes, velocity_y, pressure)
        next_flux = flux_across(nearby, next_velocity, next_pressure)
        weight = (PITCH_GAIN * 0.5) * (
            jnp.abs(velocity_y) + sound + (jnp.abs(next_velocity) + next_sound)
        )
        return [
            0.5 * (a + b) - weight * (n - o)
            for a, b, n, o in zip(own_flux, next_flux, nearby, planes)
        ]

    for cell in range(cells):
        planes = loaded(cell)
        velocity_x, velocity_y, pressure, sound = primitives(first_var, planes)
        line_ref[cell, 0], line_ref[cell, 1], line_ref[cell, 2] = velocity_x, pressure, sound
        faces_across = pitch_flux(planes, velocity_y, pressure, sound)
        times = own_time_parts(planes, cell)
        for k in range(PAIRS):
            partial_ref[cell, k] = -(times[k] + (faces_across[k] - pick_prev(faces_across[k])))

    tile = half_index * (LANES // LINES_DEV) + lane_index // LINES_DEV
    end_codes = jnp.where(mirrored == 0, codes_ref[pl.ds(0, 1), :], codes_ref[pl.ds(1, 1), :])
    codes = jnp.zeros(shape, jnp.int32)
    for k in range(2 * LANES // LINES_DEV):
        codes = jnp.where(tile == k, jnp.broadcast_to(end_codes[:, k : k + 1], shape), codes)

    def ghost(cell):
        planes = loaded(-1 - cell)
        copied = loaded(0)
        result = []
        for k in range(PAIRS):
            reflected = planes[k] if k else jnp.where(first_var, planes[k], -planes[k])
            inflow = jnp.where(first_var, FREE_STATE[2 * k], FREE_STATE[2 * k + 1])
            result.append(
                jnp.where(codes == 0, reflected, jnp.where(codes == 1, inflow, copied[k]))
            )
        return result

    line = LineCells(first_var, sign)
    faces, inverses, aboves = {}, [], []
    for cell in range(-2, cells):
        if cell < 0:
            planes = ghost(cell)
            velocity_x, _, pressure, sound = primitives(first_var, planes)
        else:
            planes = loaded(cell)
            velocity_x, pressure, sound = [line_ref[cell, k] for k in range(3)]
        line.add(cell, planes, velocity_x, pressure, sound)
        if cell >= 1:
            faces[cell - 2] = line.face(cell - 2)
        if cell >= 2:
            at = cell - 2
            for k in range(PAIRS):
                partial_ref[at, k] = partial_ref[at, k] + (faces[at - 1][k] - faces[at][k])
        if cell >= 3 and cell % 2 == 1:
            at = cell - 3
            block = at // 2
            rates = rates_at(all_ref, own_y, block, first_half)
            diag = line.diagonal(at, rates)
            if block > 0:
                factor = two_by_two(line.below(at), inverses[-1])
                diag = less(diag, two_by_two(factor, aboves[-1]))
                for n in range(4):
                    factor_ref[block - 1, n] = factor[n]
            inverses.append(inverse_of(diag))
            aboves.append(line.above(at))
            kept = [*inverses[-1], aboves[-1][0], *aboves[-1][2:]]
            for n, plane in enumerate(kept):
                blocks_ref[block, n] = plane

    last = cells - 2
    for k in range(PAIRS):
        partial_ref[last, k] = partial_ref[last, k] + faces[last - 1][k]
    factor = two_by_two(line.below(last), inverses[-1])
    for n in range(4):
        factor_ref[blocks - 2, n] = factor[n]
    correction = list(two_by_two(factor, aboves[-1]))
    rates = rates_at(all_ref, own_y, blocks - 1, first_half)
    for member in range(2):
        centre = line.radius[last + member]
        correction[3 * member] = correction[3 * member] - rates[member] * centre
    for n in range(2):
        correction_ref[pl.ds(n * ROWS, ROWS), :] = jnp.where(
            first_var, correction[2 * n], correction[2 * n + 1]
        )


def reduce_kernel(
    partial_ref, time_ref, factor_ref, correction_ref, here_ref, third_ref, middle_ref, sides_ref,
    again_ref,
):
    again_ref[...] = here_ref[...]
    middle_ref[pl.ds(THIRD_ROW, CELL_ROWS), :] = third_ref[...]
    for row in range(0, 2 * ROWS, ROWS):
        middle_ref[pl.ds(CORRECTION_ROW + row, ROWS), :] = correction_ref[pl.ds(row, ROWS), :]
    blocks = partial_ref.shape[0] // 2
    side = None
    for block in range(blocks):
        own = []
        for cell in (2 * block, 2 * block + 1):
            for k in range(PAIRS):
                time = time_ref[pl.ds(cell * CELL_ROWS + k * ROWS, ROWS), :]
                own.append(partial_ref[cell, k] - time)
        if block > 0:
            factor = [factor_ref[block - 1, n] for n in range(4)]
            own = difference(own, apply_matrix(factor, side))
        side = own
        for n, plane in enumerate(side):
            if block < blocks - 1:
                sides_ref[block, n] = plane
            else:
                middle_ref[pl.ds(n * ROWS, ROWS), :] = plane


def spread_kernel(all_ref, blocks_ref, sides_ref, known_ref, spread_ref, table_ref):
    own_y = lax.axis_index("inst") >> 1
    blocks = all_ref.shape[1]
    own_cell = lax.axis_index("cell")
    own_block = jnp.where(own_cell < blocks, own_cell, 2 * blocks - 1 - own_cell)
    zero = jnp.zeros((ROWS, LANES), jnp.float32)
    known, spread = [zero] * (2 * PAIRS), (zero + 1.0, zero, zero, zero + 1.0)
    for block in range(blocks - 1, -1, -1):
        if block < blocks - 1:
            kept = [blocks_ref[block, n] for n in range(7)]
            inverse, above = kept[:4], (kept[4], None, kept[5], kept[6])
            side = [sides_ref[block, n] for n in range(2 * PAIRS)]
            step = two_by_two(inverse, above)
            own = apply_matrix(inverse, side)
            if block < blocks - 2:
                known = difference(own, apply_matrix(step, known))
                spread = minus(two_by_two(step, spread))
            else:
                known, spread = own, minus(step)
        for n, plane in enumerate(known + list(spread)):
            table_ref[block, n] = plane
    for n in range(2 * PAIRS):
        base = at_block(all_ref, own_y, own_block)[pl.ds(n * ROWS, ROWS), :]
        known_ref[n] = base + table_ref[own_block, n]
    for n in range(4):
        spread_ref[n] = table_ref[own_block, 2 * PAIRS + n]


def plane_of(ref, row):
    return ref[pl.ds(row, ROWS), :]


def correction_of(first_var, ref):
    pairs = [both(first_var, plane_of(ref, CORRECTION_ROW + n * ROWS)) for n in range(2)]
    return [pairs[0][0], pairs[0][1], pairs[1][0], pairs[1][1]]


def middle_kernel(
    here_ref, first_ref, second_ref, here_side_ref, there_side_ref, side_ref, other_ref, matrix_ref
):
    own_cell, count = lax.axis_index("cell"), lax.axis_size("cell")
    mirrored = own_cell // (count // 2)
    outer = jnp.logical_or(own_cell < count // 4, own_cell >= count - count // 4)
    sign = (1 - 2 * mirrored).astype(jnp.float32)
    first_var, _, _ = plane_masks()
    line = LineCells(first_var, sign)
    for cell in range(6):
        at = cell if cell < 3 else 5 - cell
        rows = [(at - 1) * CELL_ROWS + k * ROWS for k in range(PAIRS)]
        if at == 0:
            ref = here_side_ref if cell < 3 else there_side_ref
            planes = [plane_of(ref, THIRD_ROW + k * ROWS) for k in range(PAIRS)]
        elif cell < 3:
            planes = [plane_of(here_ref, row) for row in rows]
        else:
            planes = [
                jnp.where(
                    outer,
                    plane_of(first_ref, (2 - at) * CELL_ROWS + k * ROWS),
                    plane_of(second_ref, row),
                )
                for k, row in enumerate(rows)
            ]
        velocity_x, _, pressure, sound = primitives(first_var, planes)
        line.add(cell, planes, velocity_x, pressure, sound)
    faces = {cell: line.face(cell) for cell in (1, 2, 3)}
    for k in range(PAIRS):
        side_ref[k] = plane_of(here_side_ref, k * ROWS) - faces[1][k]
        side_ref[PAIRS + k] = plane_of(here_side_ref, (PAIRS + k) * ROWS) + (
            faces[1][k] - faces[2][k]
        )
        other_ref[k] = plane_of(there_side_ref, (PAIRS + k) * ROWS) + (
            faces[2][k] - faces[3][k]
        )
        other_ref[PAIRS + k] = plane_of(there_side_ref, k * ROWS) + faces[3][k]
    no_rates = (None, None)
    diag = difference(line.diagonal(1, no_rates), correction_of(first_var, here_side_ref))
    above, below = line.above(1), line.below(3)
    kept = [*diag, *line.diagonal(3, no_rates), above[0], *above[2:], *below[:2], below[3]]
    for n, plane in enumerate(kept):
        matrix_ref[n] = plane


def join_kernel(
    side_ref, other_ref, matrix_ref, there_side_ref, known_ref, spread_ref, out_ref
):
    mirrored = lax.axis_index("cell") // (lax.axis_size("cell") // 2)
    first_var, _, _ = plane_masks()
    kept = [matrix_ref[n] for n in range(14)]
    diag, other_diag = kept[:4], kept[4:8]
    above, below = (kept[8], None, kept[9], kept[10]), (kept[11], kept[12], None, kept[13])
    other_diag = difference(other_diag, correction_of(first_var, there_side_ref)[::-1])
    other = [other_ref[n] for n in range(2 * PAIRS)]
    factor = two_by_two(above, inverse_of(other_diag))
    diag = less(diag, two_by_two(factor, below))
    side = [side_ref[n] for n in range(2 * PAIRS)]
    middle = apply_matrix(inverse_of(diag), difference(side, apply_matrix(factor, other)))
    moved = apply_matrix([spread_ref[n] for n in range(4)], middle)
    results = [known_ref[n] + moved[n] for n in range(2 * PAIRS)]
    for cell in range(2):
        for k in range(PAIRS):
            first, second = results[cell * PAIRS + k], results[(1 - cell) * PAIRS + k]
            result = jnp.where(mirrored == 0, first, second)
            for var in range(2):
                for inst in range(2):
                    for half in range(2):
                        row = rows_of(var, inst, half)
                        out_ref[
                            inst, 2 * k + var, pl.ds(cell, 1), pl.ds(half * LANES, LANES)
                        ] = result[row : row + 1]


def share_half(copies):
    insts, count = lax.axis_size("inst"), lax.axis_size("cell")
    halves = [range(count // 2 - 1, -1, -1), range(count - 1, count // 2 - 1, -1)]
    groups = [
        [inst * count + cell for inst in range(insts - 2 + core, -1, -2) for cell in half]
        for core in range(2)
        for half in halves
    ]
    return lax.all_to_all(
        copies, ("inst", "cell"), split_axis=0, concat_axis=0, tiled=True,
        axis_index_groups=groups,
    )


def swap_cores(block):
    pairs = [(inst, inst ^ 1) for inst in range(lax.axis_size("inst"))]
    return lax.ppermute(block, "inst", pairs)


def swap_halves(block):
    count = lax.axis_size("cell")
    return lax.ppermute(block, "cell", [(i, (i + count // 2) % count) for i in range(count)])


def pass_round(block, steps):
    insts, count = lax.axis_size("inst"), lax.axis_size("cell")
    width = count // 4
    pairs = [
        (
            inst * count + source * width + i,
            (inst ^ (source == target)) * count + target * width + i,
        )
        for inst in range(insts)
        for source, target in steps
        for i in range(width)
    ]
    return lax.ppermute(block, ("inst", "cell"), pairs)


FIRST_ROUND = ((2, 0), (0, 1), (1, 3), (3, 2))
SECOND_ROUND = ((3, 1), (1, 2), (2, 3), (0, 0))


def float_shape(*sizes):
    return jax.ShapeDtypeStruct(sizes, jnp.float32)


def local_by_halves(state, pseudo_rate, line_next, face_codes):
    blocks = lax.axis_size("cell") // 2
    cells = 2 * blocks
    vmem = pl.BlockSpec(memory_space=pltpu.VMEM)
    plane = (ROWS, LANES)
    params = pltpu.CompilerParams(vmem_limit_bytes=VMEM_BYTES)
    places = lax.axis_size("inst") // 2
    held = [
        pltpu.with_memory_space_constraint(array, pltpu.HBM)
        for array in (state, pseudo_rate, line_next, face_codes)
    ]
    packed, next_here, codes_here = pl.pallas_call(
        pack_kernel,
        out_shape=(
            float_shape(places * blocks, BLOCK_ROWS, LANES),
            jax.ShapeDtypeStruct(line_next.shape, jnp.int32),
            jax.ShapeDtypeStruct(face_codes.shape, jnp.int32),
        ),
        in_specs=[pl.BlockSpec(memory_space=pltpu.HBM)] * 4,
        out_specs=(vmem, vmem, vmem),
        scratch_shapes=[
            pltpu.VMEM(state.shape, jnp.float32),
            pltpu.VMEM(pseudo_rate.shape, jnp.float32),
            pltpu.SemaphoreType.DMA((4,)),
        ],
        compiler_params=params,
    )(*held)
    shared = share_half(packed).reshape(places, blocks, BLOCK_ROWS, LANES)
    for_partner = pl.pallas_call(
        partner_kernel,
        out_shape=float_shape(cells * CELL_ROWS, LANES),
        in_specs=[vmem],
        out_specs=vmem,
        compiler_params=params,
    )(shared)
    from_partner = swap_cores(for_partner)
    beside = pl.CostEstimate(flops=10**6, bytes_accessed=10**6, transcendentals=0)
    kinds = (
        float_shape(cells, PAIRS, *plane),
        float_shape(blocks - 1, 4, *plane),
        float_shape(blocks - 1, 7, *plane),
        float_shape(2 * ROWS, LANES),
    )
    line_scratch = [pltpu.VMEM((cells, 3) + plane, jnp.float32)]
    arguments = (shared, next_here, codes_here)
    *near, here, for_round, third = pl.pallas_call(
        near_half_kernel,
        out_shape=kinds
        + (
            float_shape(MIDDLE_CELLS * CELL_ROWS, LANES),
            float_shape(ROUND_CELLS * CELL_ROWS, LANES),
            float_shape(CELL_ROWS, LANES),
        ),
        in_specs=[vmem] * 3,
        out_specs=(vmem,) * 7,
        scratch_shapes=line_scratch,
        compiler_params=params,
    )(*arguments)
    there_first = pass_round(for_round, FIRST_ROUND)
    partial, factors, eliminated, correction = pl.pallas_call(
        far_half_kernel,
        out_shape=kinds,
        in_specs=[vmem] * 7,
        out_specs=(vmem,) * 4,
        scratch_shapes=line_scratch,
        input_output_aliases={3 + n: n for n in range(4)},
        compiler_params=params,
        cost_estimate=beside,
    )(*arguments, *near)
    here_side, sides, here_again = pl.pallas_call(
        reduce_kernel,
        out_shape=(
            float_shape(SIDE_ROWS, LANES),
            float_shape(blocks - 1, 2 * PAIRS, *plane),
            float_shape(MIDDLE_CELLS * CELL_ROWS, LANES),
        ),
        in_specs=[vmem] * 6,
        out_specs=(vmem,) * 3,
        compiler_params=params,
    )(partial, from_partner, factors, correction, here, third)
    there_side = swap_halves(here_side)
    there_second = pass_round(here_again, SECOND_ROUND)
    known, spread = pl.pallas_call(
        spread_kernel,
        out_shape=(float_shape(2 * PAIRS, *plane), float_shape(4, *plane)),
        in_specs=[vmem] * 3,
        out_specs=(vmem, vmem),
        scratch_shapes=[pltpu.VMEM((blocks, 2 * PAIRS + 4) + plane, jnp.float32)],
        compiler_params=params,
        cost_estimate=beside,
    )(shared, eliminated, sides)
    side, other, matrices = pl.pallas_call(
        middle_kernel,
        out_shape=(
            float_shape(2 * PAIRS, *plane),
            float_shape(2 * PAIRS, *plane),
            float_shape(14, *plane),
        ),
        in_specs=[vmem] * 5,
        out_specs=(vmem,) * 3,
        compiler_params=params,
    )(here, there_first, there_second, here_side, there_side)
    return pl.pallas_call(
        join_kernel,
        out_shape=float_shape(*state.shape),
        in_specs=[vmem] * 6,
        out_specs=vmem,
        compiler_params=params,
    )(side, other, matrices, there_side, known, spread)


def solution(mesh):
    placed = (P("inst", None, "cell", None), P("cell", None), P(), P())
    inst_count, cell_count = mesh.shape["inst"], mesh.shape["cell"]

    def local(state, pseudo_rate, line_next, face_codes):
        small = (
            state.shape == (2, 6, 2, 2 * LANES)
            and inst_count * 2 == NT
            and cell_count == 8
            and face_codes.shape[1] * LINES_DEV == state.shape[3]
        )
        chosen = local_by_halves if small else local_by_lines
        return chosen(state, pseudo_rate, line_next, face_codes)

    return jax.shard_map(
        local, mesh=mesh, in_specs=placed, out_specs=P("inst", None, "cell", None), check_vma=False
    )
```

```python
import functools

import jax
import jax.numpy as jnp
import numpy as np
from jax import lax
from jax.experimental import pallas as pl
from jax.experimental.pallas import tpu as pltpu
from jax.sharding import PartitionSpec as P

NT = 8
LINES_DEV = 32


GAMMA_GAS = 1.4
OMEGA_BLADE = 1.0
SENSOR_GAIN = 0.25
FOURTH_GAIN = 0.03125
PITCH_GAIN = 0.5
SECOND_IMPL = 1.0
FOURTH_IMPL = 0.25
FREE_STATE = (1.0, 0.5, 0.0, 0.0, 2.625, 0.2)
MIRROR_SIGNS = (1.0, -1.0, 1.0, 1.0, 1.0, 1.0)
ZERO_BLOCK = (0.0, 0.0, 0.0, 0.0)
UNIT_BLOCK = (1.0, 0.0, 0.0, 1.0)
ZERO_PAIR = (0.0, 0.0)


def extended(block, sides, width):
    for axis, dim in sides:
        count = lax.axis_size(axis)
        forward = [(i, i + 1) for i in range(count - 1)]
        backward = [(target, source) for source, target in forward]
        low = lax.ppermute(
            lax.slice_in_dim(block, block.shape[dim] - width, None, axis=dim), axis, forward
        )
        high = lax.ppermute(lax.slice_in_dim(block, 0, width, axis=dim), axis, backward)
        block = jnp.concatenate([low, block, high], axis=dim)
    return block


def spectral_matrix(instances):
    offsets = np.arange(instances)[:, None] - np.arange(instances)[None, :]
    angles = np.pi * offsets / instances
    safe_sin = np.where(offsets == 0, 1.0, np.sin(angles))
    parity = np.where(np.mod(offsets, 2) == 0, -1.0, 1.0)
    matrix_table = np.where(
        offsets == 0, 0.0, 0.5 * OMEGA_BLADE * parity * np.cos(angles) / safe_sin
    )
    return jnp.asarray(matrix_table, jnp.float32)


def primitive_parts(cells_state):
    density = cells_state[..., 0, :, :]
    inverse = 1.0 / density
    velocity_x = cells_state[..., 1, :, :] * inverse
    velocity_y = cells_state[..., 2, :, :] * inverse
    velocity_z = cells_state[..., 3, :, :] * inverse
    energy = cells_state[..., 4, :, :]
    pressure = (GAMMA_GAS - 1.0) * (
        energy
        - 0.5
        * density
        * (velocity_x * velocity_x + velocity_y * velocity_y + velocity_z * velocity_z)
    )
    sound_speed = jnp.sqrt(GAMMA_GAS * pressure * inverse)
    return (velocity_x, velocity_y, pressure, sound_speed)


def directed_flux(cells_state, normal_velocity, pressure, component):
    zero_plane = jnp.zeros_like(pressure)
    pressure_rows = [
        zero_plane,
        zero_plane,
        zero_plane,
        zero_plane,
        pressure * normal_velocity,
        zero_plane,
    ]
    pressure_rows[component] = pressure
    return cells_state * normal_velocity[..., None, :, :] + jnp.stack(pressure_rows, axis=-3)


def line_residual(padded):
    velocity_x, velocity_y, pressure, sound_speed = primitive_parts(padded)
    flux_line = directed_flux(padded, velocity_x, pressure, 1)
    radius = jnp.abs(velocity_x) + sound_speed
    sensor = jnp.abs(
        pressure[..., 2:, :] - 2.0 * pressure[..., 1:-1, :] + pressure[..., :-2, :]
    ) / (pressure[..., 2:, :] + 2.0 * pressure[..., 1:-1, :] + pressure[..., :-2, :])
    second = SENSOR_GAIN * jnp.maximum(sensor[..., :-1, :], sensor[..., 1:, :])
    fourth = jnp.maximum(0.0, FOURTH_GAIN - second)
    face_radius = 0.5 * (radius[..., 1:-2, :] + radius[..., 2:-1, :])
    left_far = padded[..., :-3, :]
    left_near = padded[..., 1:-2, :]
    right_near = padded[..., 2:-1, :]
    right_far = padded[..., 3:, :]
    damping = face_radius[..., None, :, :] * (
        second[..., None, :, :] * (right_near - left_near)
        - fourth[..., None, :, :] * (right_far - 3.0 * right_near + 3.0 * left_near - left_far)
    )
    face_flux = 0.5 * (flux_line[..., 1:-2, :] + flux_line[..., 2:-1, :]) - damping
    return (face_flux[..., 1:, :] - face_flux[..., :-1, :], radius)


def pitch_parts(cells_state):
    velocity_x, velocity_y, pressure, sound_speed = primitive_parts(cells_state)
    return (directed_flux(cells_state, velocity_y, pressure, 2), jnp.abs(velocity_y) + sound_speed)


def pitch_residual(cells_state, next_lines, prev_lines):
    pitch_flux, radius = pitch_parts(cells_state)
    state_next = jnp.take(cells_state, next_lines, axis=-1)
    flux_next, radius_next = pitch_parts(state_next)
    face_flux = 0.5 * (pitch_flux + flux_next) - PITCH_GAIN * (0.5 * (radius + radius_next))[
        ..., None, :, :
    ] * (state_next - cells_state)
    return face_flux - jnp.take(face_flux, prev_lines, axis=-1)


def boundary_cells(edge_pair, line_codes, lower_end):
    reflected = edge_pair[..., ::-1, :] * jnp.asarray(MIRROR_SIGNS, jnp.float32)[:, None, None]
    if lower_end:
        copied = jnp.concatenate([edge_pair[..., :1, :], edge_pair[..., :1, :]], axis=-2)
    else:
        copied = jnp.concatenate([edge_pair[..., 1:, :], edge_pair[..., 1:, :]], axis=-2)
    inflow = jnp.asarray(FREE_STATE, jnp.float32)[:, None, None] + jnp.zeros_like(edge_pair)
    return jnp.where(line_codes == 0, reflected, jnp.where(line_codes == 1, inflow, copied))


def line_coefficients(radius_ext, diagonal_term, positions, total_cells):
    radius_below = radius_ext[..., :-2, :]
    radius_centre = radius_ext[..., 1:-1, :]
    radius_above = radius_ext[..., 2:, :]
    face_below = 0.5 * (radius_below + radius_centre)
    face_above = 0.5 * (radius_centre + radius_above)
    far_low = FOURTH_IMPL * radius_below
    near_low = -SECOND_IMPL * face_below - 2.0 * FOURTH_IMPL * (radius_below + radius_centre)
    middle = (
        diagonal_term
        + SECOND_IMPL * (face_below + face_above)
        + FOURTH_IMPL * (radius_below + 4.0 * radius_centre + radius_above)
    )
    near_high = -SECOND_IMPL * face_above - 2.0 * FOURTH_IMPL * (radius_centre + radius_above)
    far_high = FOURTH_IMPL * radius_above
    column = positions[:, None]
    far_low = jnp.where(column >= 2, far_low, 0.0)
    near_low = jnp.where(column >= 1, near_low, 0.0)
    near_high = jnp.where(column <= total_cells - 2, near_high, 0.0)
    far_high = jnp.where(column <= total_cells - 3, far_high, 0.0)
    return (far_low, near_low, middle, near_high, far_high)


def block_product(first_matrix, second_matrix):
    return (
        first_matrix[0] * second_matrix[0] + first_matrix[1] * second_matrix[2],
        first_matrix[0] * second_matrix[1] + first_matrix[1] * second_matrix[3],
        first_matrix[2] * second_matrix[0] + first_matrix[3] * second_matrix[2],
        first_matrix[2] * second_matrix[1] + first_matrix[3] * second_matrix[3],
    )


def block_inverse(matrix):
    determinant = matrix[0] * matrix[3] - matrix[1] * matrix[2]
    reciprocal = 1.0 / determinant
    return (
        matrix[3] * reciprocal,
        -matrix[1] * reciprocal,
        -matrix[2] * reciprocal,
        matrix[0] * reciprocal,
    )


def block_apply(matrix, vector):
    return (
        matrix[0] * vector[0] + matrix[1] * vector[1],
        matrix[2] * vector[0] + matrix[3] * vector[1],
    )


def add_blocks(first_members, second_members):
    return tuple((a + b for a, b in zip(first_members, second_members)))


def negate(members):
    return tuple((-a for a in members))


def extend_blocks(members, fill_values):
    return tuple(
        (
            jnp.concatenate([m, jnp.full_like(m[..., :1, :], f)], axis=-2)
            for m, f in zip(members, fill_values)
        )
    )


def shift_next(members, fill_values):
    return tuple(
        (
            jnp.concatenate([m[..., 1:, :], jnp.full_like(m[..., :1, :], f)], axis=-2)
            for m, f in zip(members, fill_values)
        )
    )


def shift_prev(members):
    return tuple(
        (jnp.concatenate([jnp.zeros_like(m[..., :1, :]), m[..., :-1, :]], axis=-2) for m in members)
    )


def pair_split(member):
    shaped = member.reshape(member.shape[:-2] + (member.shape[-2] // 2, 2, member.shape[-1]))
    return (shaped[..., 0, :], shaped[..., 1, :])


def split_parity(members):
    halves = [pair_split(m) for m in members]
    return (tuple((h[0] for h in halves)), tuple((h[1] for h in halves)))


def alternate(first_member, second_member):
    stacked = jnp.stack((first_member, second_member), axis=-2)
    return stacked.reshape(
        first_member.shape[:-2] + (2 * first_member.shape[-2], first_member.shape[-1])
    )


def reduce_blocks(sub_blocks, diag_blocks, super_blocks, right_side):
    block_count = diag_blocks[0].shape[-2]
    if block_count == 1:
        return block_apply(block_inverse(diag_blocks), right_side)
    if block_count % 2 == 1:
        sub_blocks = extend_blocks(sub_blocks, ZERO_BLOCK)
        diag_blocks = extend_blocks(diag_blocks, UNIT_BLOCK)
        super_blocks = extend_blocks(super_blocks, ZERO_BLOCK)
        right_side = extend_blocks(right_side, ZERO_PAIR)
    sub_even, sub_odd = split_parity(sub_blocks)
    diag_even, diag_odd = split_parity(diag_blocks)
    super_even, super_odd = split_parity(super_blocks)
    side_even, side_odd = split_parity(right_side)
    inverse_even = block_inverse(diag_even)
    inverse_next = shift_next(inverse_even, UNIT_BLOCK)
    sub_next = shift_next(sub_even, ZERO_BLOCK)
    super_next = shift_next(super_even, ZERO_BLOCK)
    side_next = shift_next(side_even, ZERO_PAIR)
    left_factor = negate(block_product(sub_odd, inverse_even))
    right_factor = negate(block_product(super_odd, inverse_next))
    reduced_sub = block_product(left_factor, sub_even)
    reduced_diag = add_blocks(
        diag_odd,
        add_blocks(block_product(left_factor, super_even), block_product(right_factor, sub_next)),
    )
    reduced_super = block_product(right_factor, super_next)
    reduced_side = add_blocks(
        side_odd,
        add_blocks(block_apply(left_factor, side_even), block_apply(right_factor, side_next)),
    )
    odd_values = reduce_blocks(reduced_sub, reduced_diag, reduced_super, reduced_side)
    before_values = shift_prev(odd_values)
    remainder = add_blocks(
        side_even,
        negate(
            add_blocks(block_apply(sub_even, before_values), block_apply(super_even, odd_values))
        ),
    )
    even_values = block_apply(inverse_even, remainder)
    merged = tuple((alternate(e, o) for e, o in zip(even_values, odd_values)))
    return tuple((m[..., :block_count, :] for m in merged))


def cells_leading(block):
    moved = jnp.transpose(block, (2, 0, 1, 3))
    return moved.reshape(block.shape[2], block.shape[0] * block.shape[1] * block.shape[3])


def solve_in_lanes(coefficients, line_source):
    source_shape = line_source.shape
    lane_coef = [cells_leading(jnp.broadcast_to(c[:, None], source_shape)) for c in coefficients]
    pairs_list = [pair_split(m) for m in lane_coef]
    zero_plane = jnp.zeros_like(pairs_list[2][0])
    sub_blocks = (pairs_list[0][0], pairs_list[1][0], zero_plane, pairs_list[0][1])
    diag_blocks = (pairs_list[2][0], pairs_list[3][0], pairs_list[1][1], pairs_list[2][1])
    super_blocks = (pairs_list[4][0], zero_plane, pairs_list[3][1], pairs_list[4][1])
    values = reduce_blocks(
        sub_blocks, diag_blocks, super_blocks, pair_split(cells_leading(line_source))
    )
    flat = alternate(values[0], values[1])
    shaped = flat.reshape(source_shape[2], source_shape[0], source_shape[1], source_shape[3])
    return jnp.transpose(shaped, (1, 2, 0, 3))


def return_tiles(line_values):
    return lax.all_to_all(line_values, "cell", split_axis=2, concat_axis=3, tiled=True)


def local_by_lines(state, pseudo_rate, line_next, face_codes):
    local_count = state.shape[0]
    tile_cells = state.shape[2]
    cell_index = lax.axis_index("cell")
    cell_count = lax.axis_size("cell")
    total_cells = tile_cells * cell_count
    spectral = spectral_matrix(NT)
    first_local = lax.axis_index("inst") * local_count
    own_rows = lax.dynamic_slice_in_dim(spectral, first_local, local_count, 0)
    shard_block = jax.tree.map(lambda a: lax.all_gather(a, "inst", axis=0, tiled=True), state)
    columns = lax.slice_in_dim(own_rows, 0, shard_block.shape[0], axis=1)
    time_term = jnp.zeros_like(state) + jnp.einsum(
        "nm,mvil->nvil", columns, shard_block, precision=lax.Precision.HIGHEST
    )
    padded = extended(state, (("cell", 2),), 2)
    codes_lines = jnp.repeat(face_codes, LINES_DEV, axis=1)
    lower_ghost = boundary_cells(state[:, :, 0:2, :], codes_lines[0], True)
    upper_ghost = boundary_cells(state[:, :, -2:, :], codes_lines[1], False)
    lower_rim = jnp.where(cell_index == 0, lower_ghost, padded[:, :, :2, :])
    upper_rim = jnp.where(cell_index == cell_count - 1, upper_ghost, padded[:, :, -2:, :])
    padded = jnp.concatenate([lower_rim, padded[:, :, 2:-2, :], upper_rim], axis=2)
    line_part, radius = line_residual(padded)
    prev_lines = (
        jnp.zeros_like(line_next).at[line_next].set(jnp.arange(line_next.shape[0], dtype=jnp.int32))
    )
    residual = line_part + pitch_residual(state, line_next, prev_lines) + time_term
    right_side = -residual
    centre_radius = radius[:, 2:-2, :]
    diagonal_term = pseudo_rate * centre_radius
    positions = cell_index * tile_cells + jnp.arange(-1, tile_cells + 1, dtype=jnp.int32)
    inside = (positions >= 0) & (positions < total_cells)
    radius_ext = jnp.where(inside[:, None], radius[:, 1:-1, :], 0.0)
    coefficients = line_coefficients(radius_ext, diagonal_term, positions[1:-1], total_cells)
    stacked = jnp.stack(coefficients, axis=1)
    line_source = lax.all_to_all(right_side, "cell", split_axis=3, concat_axis=2, tiled=True)
    line_coef = lax.all_to_all(stacked, "cell", split_axis=3, concat_axis=2, tiled=True)
    update = return_tiles(solve_in_lanes(tuple((line_coef[:, k] for k in range(5))), line_source))
    return state + update


LANES = 128
ROWS = 8
PAIRS = 3
CELL_ROWS = PAIRS * ROWS
RATE_ROW = 2 * CELL_ROWS
VMEM_BYTES = 8 * 2**20
BLOCK_ROWS = RATE_ROW + ROWS

MIDDLE_CELLS = (1, 0, 2)
MIDDLE_ROWS = 3 * CELL_ROWS
SECOND_ROWS = MIDDLE_ROWS - ROWS
CORRECTION_ROW = 2 * CELL_ROWS
SIDE_ROWS = CORRECTION_ROW + 3 * ROWS


def spectral_offsets():
    table = np.zeros(NT)
    for offset in range(1, NT):
        angle = np.pi * offset / NT
        parity = -1.0 if offset % 2 == 0 else 1.0
        table[offset] = 0.5 * OMEGA_BLADE * parity * np.cos(angle) / np.sin(angle)
    return [float(np.float32(value)) for value in table]


def plane_masks():
    row_index = lax.broadcasted_iota(jnp.int32, (ROWS, LANES), 0)
    return row_index < 4, (row_index & 2) == 0, row_index & 1


def both(first_var, plane):
    turned = pltpu.roll(plane, 4, 0)
    return jnp.where(first_var, plane, turned), jnp.where(first_var, turned, plane)


def primitives(first_var, planes):
    density, moment_x = both(first_var, planes[0])
    moment_y, moment_z = both(first_var, planes[1])
    energy = jnp.where(first_var, planes[2], pltpu.roll(planes[2], 4, 0))
    inverse = 1.0 / density
    velocity_x = moment_x * inverse
    velocity_y = moment_y * inverse
    velocity_z = moment_z * inverse
    kinetic = moment_x * velocity_x + moment_y * velocity_y + moment_z * velocity_z
    pressure = (GAMMA_GAS - 1.0) * (energy - 0.5 * kinetic)
    sound = jnp.sqrt(GAMMA_GAS * pressure * inverse)
    return velocity_x, velocity_y, pressure, sound


def rows_of(var, inst, half):
    return (var // 2) * ROWS + (var % 2) * 4 + inst * 2 + half


def pack_kernel(
    held_state_ref, held_rate_ref, held_next_ref, held_codes_ref, out_ref, next_ref, codes_ref,
    state_ref, rate_ref, sems,
):
    copies = [
        pltpu.make_async_copy(source, target, sems.at[k])
        for k, (source, target) in enumerate(
            (
                (held_state_ref, state_ref),
                (held_rate_ref, rate_ref),
                (held_next_ref, next_ref),
                (held_codes_ref, codes_ref),
            )
        )
    ]
    for copy in copies:
        copy.start()
    for copy in copies:
        copy.wait()
    mirrored = lax.axis_index("cell") // (lax.axis_size("cell") // 2)
    for cell in range(2):
        place = pl.multiple_of(jnp.bitwise_xor(cell, mirrored) * CELL_ROWS, ROWS)
        for k in range(PAIRS):
            rows = [
                state_ref[inst, 2 * k + var, pl.ds(cell, 1), pl.ds(half * LANES, LANES)]
                for var in range(2)
                for inst in range(2)
                for half in range(2)
            ]
            for row, values in enumerate(rows):
                out_ref[0, pl.ds(place + (k * ROWS + row), 1), :] = values
    rates = [
        rate_ref[pl.ds(cell, 1), pl.ds(half * LANES, LANES)]
        for cell in range(2)
        for half in range(2)
    ]
    for row in range(4):
        out_ref[0, pl.ds(RATE_ROW + row, 1), :] = jnp.where(
            mirrored == 0, rates[row], rates[row ^ 2]
        )
    out_ref[0, pl.ds(RATE_ROW + 4, 4), :] = jnp.zeros((4, LANES), jnp.float32)
    for row in range(0, BLOCK_ROWS, ROWS):
        values = out_ref[0, pl.ds(row, ROWS), :]
        for copy in range(1, out_ref.shape[0]):
            out_ref[copy, pl.ds(row, ROWS), :] = values


def turn_insts(first_inst, plane):
    return jnp.where(first_inst, pltpu.roll(plane, 6, 0), pltpu.roll(plane, 2, 0))


def time_weights(first_inst, shift):
    offsets = spectral_offsets()
    other = jnp.where(
        first_inst, offsets[(2 * shift + 1) % NT], offsets[(2 * shift - 1) % NT]
    )
    return offsets[(2 * shift) % NT], other


def at_block(ref, y, block):
    blocks = ref.shape[1]
    mirrored = lax.axis_index("cell") // blocks
    place = mirrored * block + (1 - mirrored) * (blocks - 1 - block)
    return ref.at[ref.shape[0] - 1 - y, place]


def cell_plane(ref, y, cell, k):
    return at_block(ref, y, cell // 2)[pl.ds((cell % 2) * CELL_ROWS + k * ROWS, ROWS), :]


def partner_kernel(all_ref, out_ref):
    own_inst = lax.axis_index("inst")
    own_y, core = own_inst >> 1, own_inst & 1
    _, first_inst, _ = plane_masks()
    one, three = time_weights(first_inst, 1), time_weights(first_inst, 3)
    near = [jnp.where(core == 0, a, b) for a, b in zip(one, three)]
    away = [jnp.where(core == 0, b, a) for a, b in zip(one, three)]
    cells = 2 * all_ref.shape[1]
    for cell in range(cells):
        for k in range(PAIRS):
            here = cell_plane(all_ref, own_y, cell, k)
            there = cell_plane(all_ref, 1 - own_y, cell, k)
            out_ref[pl.ds(cell * CELL_ROWS + k * ROWS, ROWS), :] = (
                near[0] * here
                + away[0] * there
                + turn_insts(first_inst, near[1] * here + away[1] * there)
            )


def two_by_two(first, second):
    def entry(a, b, c, d):
        terms = [x * y for x, y in ((a, b), (c, d)) if x is not None and y is not None]
        return None if not terms else terms[0] if len(terms) == 1 else terms[0] + terms[1]

    return (
        entry(first[0], second[0], first[1], second[2]),
        entry(first[0], second[1], first[1], second[3]),
        entry(first[2], second[0], first[3], second[2]),
        entry(first[2], second[1], first[3], second[3]),
    )


def inverse_of(matrix):
    reciprocal = 1.0 / (matrix[0] * matrix[3] - matrix[1] * matrix[2])
    return (
        matrix[3] * reciprocal,
        -(matrix[1] * reciprocal),
        -(matrix[2] * reciprocal),
        matrix[0] * reciprocal,
    )


def less(first, second):
    return tuple(a if b is None else a - b for a, b in zip(first, second))


def minus(members):
    return tuple(None if a is None else -a for a in members)


def matrix_vector(matrix, low, high):
    def row(a, b):
        terms = [x * y for x, y in ((a, low), (b, high)) if x is not None]
        return terms[0] if len(terms) == 1 else terms[0] + terms[1]

    return row(matrix[0], matrix[1]), row(matrix[2], matrix[3])


def apply_matrix(matrix, side):
    parts = [matrix_vector(matrix, side[k], side[PAIRS + k]) for k in range(PAIRS)]
    return [low for low, _ in parts] + [high for _, high in parts]


def difference(first, second):
    return [a - b for a, b in zip(first, second)]


def flux_along(first_var, planes, velocity, pressure, sign):
    normal = sign * velocity
    return [
        planes[0] * normal + jnp.where(first_var, 0.0, sign * pressure),
        planes[1] * normal,
        planes[2] * normal + jnp.where(first_var, pressure * normal, 0.0),
    ]


class LineCells:
    def __init__(self, first_var, sign):
        self.first_var, self.sign = first_var, sign
        self.state, self.pressure, self.radius = {}, {}, {}
        self.flux, self.step, self.sensor = {}, {}, {}

    def add(self, cell, planes, velocity, pressure, sound):
        self.state[cell], self.pressure[cell] = planes, pressure
        self.radius[cell] = jnp.abs(velocity) + sound
        self.flux[cell] = flux_along(self.first_var, planes, velocity, pressure, self.sign)
        if cell - 1 in self.state:
            self.step[cell - 1] = difference(planes, self.state[cell - 1])
        if cell - 2 in self.state:
            twice = 2.0 * self.pressure[cell - 1]
            outer = pressure + self.pressure[cell - 2]
            self.sensor[cell - 1] = jnp.abs(outer - twice) / (outer + twice)

    def face(self, cell):
        second = SENSOR_GAIN * jnp.maximum(self.sensor[cell], self.sensor[cell + 1])
        fourth = jnp.maximum(0.0, FOURTH_GAIN - second)
        face_radius = 0.5 * (self.radius[cell] + self.radius[cell + 1])
        near_weight = face_radius * (second + 2.0 * fourth)
        far_weight = face_radius * fourth
        return [
            0.5 * (self.flux[cell][k] + self.flux[cell + 1][k])
            - (
                near_weight * self.step[cell][k]
                - far_weight * (self.step[cell + 1][k] + self.step[cell - 1][k])
            )
            for k in range(PAIRS)
        ]

    def near(self, cell):
        scale = SECOND_IMPL * 0.5 + 2.0 * FOURTH_IMPL
        return -scale * (self.radius[cell] + self.radius[cell + 1])

    def far(self, cell):
        return FOURTH_IMPL * self.radius[cell]

    def middle(self, cell, rate):
        centre, above = self.radius[cell], self.radius[cell + 1]
        if cell == 0:
            total, weighted = centre + (centre + above), 4.0 * centre + above
        else:
            below = self.radius[cell - 1]
            total = (below + centre) + (centre + above)
            weighted = below + 4.0 * centre + above
        result = SECOND_IMPL * (0.5 * total) + FOURTH_IMPL * weighted
        return result if rate is None else rate * centre + result

    def diagonal(self, cell, rates):
        across = self.near(cell)
        return (self.middle(cell, rates[0]), across, across, self.middle(cell + 1, rates[1]))

    def below(self, cell):
        return (self.far(cell - 1), self.near(cell - 1), None, self.far(cell))

    def above(self, cell):
        return (self.far(cell + 1), None, self.near(cell + 1), self.far(cell + 2))


def rates_at(ref, y, block, first_half):
    rows = [at_block(ref, y, block)[pl.ds(RATE_ROW + k, 1), :] for k in range(4)]
    return [jnp.where(first_half, rows[2 * k], rows[2 * k + 1]) for k in range(2)]


def near_half_kernel(all_ref, next_ref, codes_ref, *refs):
    *results, middle_ref, line_ref = refs
    own_y = lax.axis_index("inst") >> 1
    cells = 2 * all_ref.shape[1]
    for n, back in enumerate(MIDDLE_CELLS):
        for k in range(PAIRS):
            plane = cell_plane(all_ref, own_y, cells - 1 - back, k)
            middle_ref[pl.ds(n * CELL_ROWS + k * ROWS, ROWS), :] = plane

    @pl.when(lax.axis_index("cell") // (all_ref.shape[1] // 2) == 1)
    def _():
        half_kernel(all_ref, next_ref, codes_ref, *results, line_ref)


def far_half_kernel(all_ref, next_ref, codes_ref, *refs):
    *refs, line_ref = refs
    given, results = refs[: len(refs) // 2], refs[len(refs) // 2 :]
    far = lax.axis_index("cell") // (all_ref.shape[1] // 2) != 1

    @pl.when(far)
    def _():
        half_kernel(all_ref, next_ref, codes_ref, *results, line_ref)

    @pl.when(jnp.logical_not(far))
    def _():
        for source, target in zip(given, results):
            target[...] = source[...]


def half_kernel(
    all_ref, next_ref, codes_ref, partial_ref, factor_ref, blocks_ref, correction_ref,
    line_ref,
):
    own_y = lax.axis_index("inst") >> 1
    blocks = all_ref.shape[1]
    cells = 2 * blocks
    mirrored = lax.axis_index("cell") // blocks
    sign = (1 - 2 * mirrored).astype(jnp.float32)
    shape = (ROWS, LANES)
    lane_index = lax.broadcasted_iota(jnp.int32, shape, 1)
    first_var, first_inst, half_index = plane_masks()
    first_half = half_index == 0
    zero = jnp.zeros(shape, jnp.float32)

    next_rows = [
        next_ref[pl.ds(half * LANES, LANES)].reshape(1, LANES) for half in range(2)
    ]
    next_line = jnp.where(first_half, next_rows[0], next_rows[1])
    column = lax.broadcasted_iota(jnp.int32, (LANES, LANES), 0)
    prev_halves = []
    for target in range(2):
        total = None
        for source in range(2):
            hits = jnp.where(column + target * LANES == next_rows[source], 1.0, 0.0)
            names = (lane_index + source * LANES).astype(jnp.float32)
            part = lax.dot_general(
                names, hits, (((1,), (1,)), ((), ())), preferred_element_type=jnp.float32
            )
            total = part if total is None else total + part
        prev_halves.append(total)
    prev_line = jnp.where(first_half, prev_halves[0], prev_halves[1]).astype(jnp.int32)

    def picker(lines):
        lane = lines & (LANES - 1)
        same = (lines >> 7) == half_index

        def pick(plane):
            swapped = jnp.where(first_half, pltpu.roll(plane, 7, 0), pltpu.roll(plane, 1, 0))
            here = jnp.take_along_axis(plane, lane, axis=1, mode="promise_in_bounds")
            there = jnp.take_along_axis(swapped, lane, axis=1, mode="promise_in_bounds")
            return jnp.where(same, here, there)

        return pick

    pick_next = picker(next_line)
    pick_prev = picker(prev_line)

    def loaded(cell, y=own_y):
        return [cell_plane(all_ref, y, cell, k) for k in range(PAIRS)]

    own_weights, away_weights = time_weights(first_inst, 0), time_weights(first_inst, 2)

    def own_time_parts(planes, cell):
        return [
            away_weights[0] * away
            + turn_insts(first_inst, own_weights[1] * own + away_weights[1] * away)
            for own, away in zip(planes, loaded(cell, 1 - own_y))
        ]

    def flux_across(planes, velocity, pressure):
        return [
            planes[0] * velocity,
            planes[1] * velocity + jnp.where(first_var, pressure, 0.0),
            planes[2] * velocity + jnp.where(first_var, pressure * velocity, 0.0),
        ]

    def pitch_flux(planes, velocity_y, pressure, sound):
        nearby = [pick_next(plane) for plane in planes]
        _, next_velocity, next_pressure, next_sound = primitives(first_var, nearby)
        own_flux = flux_across(planes, velocity_y, pressure)
        next_flux = flux_across(nearby, next_velocity, next_pressure)
        weight = (PITCH_GAIN * 0.5) * (
            jnp.abs(velocity_y) + sound + (jnp.abs(next_velocity) + next_sound)
        )
        return [
            0.5 * (a + b) - weight * (n - o)
            for a, b, n, o in zip(own_flux, next_flux, nearby, planes)
        ]

    for cell in range(cells):
        planes = loaded(cell)
        velocity_x, velocity_y, pressure, sound = primitives(first_var, planes)
        line_ref[cell, 0], line_ref[cell, 1], line_ref[cell, 2] = velocity_x, pressure, sound
        faces_across = pitch_flux(planes, velocity_y, pressure, sound)
        times = own_time_parts(planes, cell)
        for k in range(PAIRS):
            partial_ref[cell, k] = -(times[k] + (faces_across[k] - pick_prev(faces_across[k])))

    tile = half_index * (LANES // LINES_DEV) + lane_index // LINES_DEV
    end_codes = jnp.where(mirrored == 0, codes_ref[pl.ds(0, 1), :], codes_ref[pl.ds(1, 1), :])
    codes = jnp.zeros(shape, jnp.int32)
    for k in range(2 * LANES // LINES_DEV):
        codes = jnp.where(tile == k, jnp.broadcast_to(end_codes[:, k : k + 1], shape), codes)

    def ghost(cell):
        planes = loaded(-1 - cell)
        copied = loaded(0)
        result = []
        for k in range(PAIRS):
            reflected = planes[k] if k else jnp.where(first_var, planes[k], -planes[k])
            inflow = jnp.where(first_var, FREE_STATE[2 * k], FREE_STATE[2 * k + 1])
            result.append(
                jnp.where(codes == 0, reflected, jnp.where(codes == 1, inflow, copied[k]))
            )
        return result

    line = LineCells(first_var, sign)
    faces, inverses, aboves = {}, [], []
    for cell in range(-2, cells):
        if cell < 0:
            planes = ghost(cell)
            velocity_x, _, pressure, sound = primitives(first_var, planes)
        else:
            planes = loaded(cell)
            velocity_x, pressure, sound = [line_ref[cell, k] for k in range(3)]
        line.add(cell, planes, velocity_x, pressure, sound)
        if cell >= 1:
            faces[cell - 2] = line.face(cell - 2)
        if cell >= 2:
            at = cell - 2
            for k in range(PAIRS):
                partial_ref[at, k] = partial_ref[at, k] + (faces[at - 1][k] - faces[at][k])
        if cell >= 3 and cell % 2 == 1:
            at = cell - 3
            block = at // 2
            rates = rates_at(all_ref, own_y, block, first_half)
            diag = line.diagonal(at, rates)
            if block > 0:
                factor = two_by_two(line.below(at), inverses[-1])
                diag = less(diag, two_by_two(factor, aboves[-1]))
                for n in range(4):
                    factor_ref[block - 1, n] = factor[n]
            inverses.append(inverse_of(diag))
            aboves.append(line.above(at))
            kept = [*inverses[-1], aboves[-1][0], *aboves[-1][2:]]
            for n, plane in enumerate(kept):
                blocks_ref[block, n] = plane

    last = cells - 2
    for k in range(PAIRS):
        partial_ref[last, k] = partial_ref[last, k] + faces[last - 1][k]
    factor = two_by_two(line.below(last), inverses[-1])
    for n in range(4):
        factor_ref[blocks - 2, n] = factor[n]
    correction = list(two_by_two(factor, aboves[-1]))
    rates = rates_at(all_ref, own_y, blocks - 1, first_half)
    for member in range(2):
        centre = line.radius[last + member]
        correction[3 * member] = correction[3 * member] - rates[member] * centre
    for n in range(2):
        correction_ref[pl.ds(n * ROWS, ROWS), :] = jnp.where(
            first_var, correction[2 * n], correction[2 * n + 1]
        )


def reduce_kernel(
    partial_ref, time_ref, factor_ref, correction_ref, here_ref, middle_ref, sides_ref, again_ref
):
    again_ref[...] = here_ref[pl.ds(0, SECOND_ROWS), :]
    middle_ref[pl.ds(SIDE_ROWS - ROWS, ROWS), :] = here_ref[pl.ds(SECOND_ROWS, ROWS), :]
    for row in range(0, 2 * ROWS, ROWS):
        middle_ref[pl.ds(CORRECTION_ROW + row, ROWS), :] = correction_ref[pl.ds(row, ROWS), :]
    blocks = partial_ref.shape[0] // 2
    side = None
    for block in range(blocks):
        own = []
        for cell in (2 * block, 2 * block + 1):
            for k in range(PAIRS):
                time = time_ref[pl.ds(cell * CELL_ROWS + k * ROWS, ROWS), :]
                own.append(partial_ref[cell, k] - time)
        if block > 0:
            factor = [factor_ref[block - 1, n] for n in range(4)]
            own = difference(own, apply_matrix(factor, side))
        side = own
        for n, plane in enumerate(side):
            if block < blocks - 1:
                sides_ref[block, n] = plane
            else:
                middle_ref[pl.ds(n * ROWS, ROWS), :] = plane


def spread_kernel(all_ref, blocks_ref, sides_ref, known_ref, spread_ref, table_ref):
    own_y = lax.axis_index("inst") >> 1
    blocks = all_ref.shape[1]
    own_cell = lax.axis_index("cell")
    own_block = jnp.where(own_cell < blocks, own_cell, 2 * blocks - 1 - own_cell)
    zero = jnp.zeros((ROWS, LANES), jnp.float32)
    known, spread = [zero] * (2 * PAIRS), (zero + 1.0, zero, zero, zero + 1.0)
    for block in range(blocks - 1, -1, -1):
        if block < blocks - 1:
            kept = [blocks_ref[block, n] for n in range(7)]
            inverse, above = kept[:4], (kept[4], None, kept[5], kept[6])
            side = [sides_ref[block, n] for n in range(2 * PAIRS)]
            step = two_by_two(inverse, above)
            own = apply_matrix(inverse, side)
            if block < blocks - 2:
                known = difference(own, apply_matrix(step, known))
                spread = minus(two_by_two(step, spread))
            else:
                known, spread = own, minus(step)
        for n, plane in enumerate(known + list(spread)):
            table_ref[block, n] = plane
    for n in range(2 * PAIRS):
        base = at_block(all_ref, own_y, own_block)[pl.ds(n * ROWS, ROWS), :]
        known_ref[n] = base + table_ref[own_block, n]
    for n in range(4):
        spread_ref[n] = table_ref[own_block, 2 * PAIRS + n]


def plane_of(ref, row):
    return ref[pl.ds(row, ROWS), :]


def correction_of(first_var, ref):
    pairs = [both(first_var, plane_of(ref, CORRECTION_ROW + n * ROWS)) for n in range(2)]
    return [pairs[0][0], pairs[0][1], pairs[1][0], pairs[1][1]]


def middle_kernel(
    here_ref, first_ref, second_ref, here_side_ref, there_side_ref, side_ref, other_ref, matrix_ref
):
    own_cell, count = lax.axis_index("cell"), lax.axis_size("cell")
    mirrored = own_cell // (count // 2)
    early = (own_cell // (count // 4)) % 2 == 0
    sign = (1 - 2 * mirrored).astype(jnp.float32)
    first_var, _, _ = plane_masks()
    line = LineCells(first_var, sign)
    for cell in range(6):
        at = (2, 0, 1)[cell if cell < 3 else 5 - cell]
        planes = []
        for k in range(PAIRS):
            row = at * CELL_ROWS + k * ROWS
            if cell < 3:
                planes.append(plane_of(here_ref, row))
            elif row < SECOND_ROWS:
                first, second = plane_of(first_ref, row), plane_of(second_ref, row)
                planes.append(jnp.where(early, first, second))
            else:
                planes.append(plane_of(there_side_ref, SIDE_ROWS - ROWS))
        velocity_x, _, pressure, sound = primitives(first_var, planes)
        line.add(cell, planes, velocity_x, pressure, sound)
    faces = {cell: line.face(cell) for cell in (1, 2, 3)}
    for k in range(PAIRS):
        side_ref[k] = plane_of(here_side_ref, k * ROWS) - faces[1][k]
        side_ref[PAIRS + k] = plane_of(here_side_ref, (PAIRS + k) * ROWS) + (
            faces[1][k] - faces[2][k]
        )
        other_ref[k] = plane_of(there_side_ref, (PAIRS + k) * ROWS) + (
            faces[2][k] - faces[3][k]
        )
        other_ref[PAIRS + k] = plane_of(there_side_ref, k * ROWS) + faces[3][k]
    no_rates = (None, None)
    diag = difference(line.diagonal(1, no_rates), correction_of(first_var, here_side_ref))
    above, below = line.above(1), line.below(3)
    kept = [*diag, *line.diagonal(3, no_rates), above[0], *above[2:], *below[:2], below[3]]
    for n, plane in enumerate(kept):
        matrix_ref[n] = plane


def join_kernel(
    side_ref, other_ref, matrix_ref, there_side_ref, known_ref, spread_ref, out_ref
):
    mirrored = lax.axis_index("cell") // (lax.axis_size("cell") // 2)
    first_var, _, _ = plane_masks()
    kept = [matrix_ref[n] for n in range(14)]
    diag, other_diag = kept[:4], kept[4:8]
    above, below = (kept[8], None, kept[9], kept[10]), (kept[11], kept[12], None, kept[13])
    other_diag = difference(other_diag, correction_of(first_var, there_side_ref)[::-1])
    other = [other_ref[n] for n in range(2 * PAIRS)]
    factor = two_by_two(above, inverse_of(other_diag))
    diag = less(diag, two_by_two(factor, below))
    side = [side_ref[n] for n in range(2 * PAIRS)]
    middle = apply_matrix(inverse_of(diag), difference(side, apply_matrix(factor, other)))
    moved = apply_matrix([spread_ref[n] for n in range(4)], middle)
    results = [known_ref[n] + moved[n] for n in range(2 * PAIRS)]
    for cell in range(2):
        for k in range(PAIRS):
            first, second = results[cell * PAIRS + k], results[(1 - cell) * PAIRS + k]
            result = jnp.where(mirrored == 0, first, second)
            for var in range(2):
                for inst in range(2):
                    for half in range(2):
                        row = rows_of(var, inst, half)
                        out_ref[
                            inst, 2 * k + var, pl.ds(cell, 1), pl.ds(half * LANES, LANES)
                        ] = result[row : row + 1]


def share_half(copies):
    insts, count = lax.axis_size("inst"), lax.axis_size("cell")
    halves = [range(count // 2 - 1, -1, -1), range(count - 1, count // 2 - 1, -1)]
    groups = [
        [inst * count + cell for inst in range(insts - 2 + core, -1, -2) for cell in half]
        for core in range(2)
        for half in halves
    ]
    return lax.all_to_all(
        copies, ("inst", "cell"), split_axis=0, concat_axis=0, tiled=True,
        axis_index_groups=groups,
    )


def swap_cores(block):
    pairs = [(inst, inst ^ 1) for inst in range(lax.axis_size("inst"))]
    return lax.ppermute(block, "inst", pairs)


def swap_halves(block):
    count = lax.axis_size("cell")
    return lax.ppermute(block, "cell", [(i, (i + count // 2) % count) for i in range(count)])


def pass_round(block, steps):
    insts, count = lax.axis_size("inst"), lax.axis_size("cell")
    width = count // 4
    pairs = [
        (
            inst * count + source * width + i,
            (inst ^ (source == target)) * count + target * width + i,
        )
        for inst in range(insts)
        for source, target in steps
        for i in range(width)
    ]
    return lax.ppermute(block, ("inst", "cell"), pairs)


FIRST_ROUND = ((2, 0), (0, 1), (1, 2), (3, 3))
SECOND_ROUND = ((3, 1), (1, 3), (0, 0), (2, 2))


def float_shape(*sizes):
    return jax.ShapeDtypeStruct(sizes, jnp.float32)


def local_by_halves(state, pseudo_rate, line_next, face_codes):
    blocks = lax.axis_size("cell") // 2
    cells = 2 * blocks
    vmem = pl.BlockSpec(memory_space=pltpu.VMEM)
    plane = (ROWS, LANES)
    params = pltpu.CompilerParams(vmem_limit_bytes=VMEM_BYTES)
    places = lax.axis_size("inst") // 2
    held = [
        pltpu.with_memory_space_constraint(array, pltpu.HBM)
        for array in (state, pseudo_rate, line_next, face_codes)
    ]
    packed, next_here, codes_here = pl.pallas_call(
        pack_kernel,
        out_shape=(
            float_shape(places * blocks, BLOCK_ROWS, LANES),
            jax.ShapeDtypeStruct(line_next.shape, jnp.int32),
            jax.ShapeDtypeStruct(face_codes.shape, jnp.int32),
        ),
        in_specs=[pl.BlockSpec(memory_space=pltpu.HBM)] * 4,
        out_specs=(vmem, vmem, vmem),
        scratch_shapes=[
            pltpu.VMEM(state.shape, jnp.float32),
            pltpu.VMEM(pseudo_rate.shape, jnp.float32),
            pltpu.SemaphoreType.DMA((4,)),
        ],
        compiler_params=params,
    )(*held)
    shared = share_half(packed).reshape(places, blocks, BLOCK_ROWS, LANES)
    for_partner = pl.pallas_call(
        partner_kernel,
        out_shape=float_shape(cells * CELL_ROWS, LANES),
        in_specs=[vmem],
        out_specs=vmem,
        compiler_params=params,
    )(shared)
    from_partner = swap_cores(for_partner)
    beside = pl.CostEstimate(flops=10**6, bytes_accessed=10**6, transcendentals=0)
    kinds = (
        float_shape(cells, PAIRS, *plane),
        float_shape(blocks - 1, 4, *plane),
        float_shape(blocks - 1, 7, *plane),
        float_shape(2 * ROWS, LANES),
    )
    line_scratch = [pltpu.VMEM((cells, 3) + plane, jnp.float32)]
    arguments = (shared, next_here, codes_here)
    *near, here = pl.pallas_call(
        near_half_kernel,
        out_shape=kinds
        + (float_shape(MIDDLE_ROWS, LANES),),
        in_specs=[vmem] * 3,
        out_specs=(vmem,) * 5,
        scratch_shapes=line_scratch,
        compiler_params=params,
    )(*arguments)
    there_first = pass_round(here, FIRST_ROUND)
    partial, factors, eliminated, correction = pl.pallas_call(
        far_half_kernel,
        out_shape=kinds,
        in_specs=[vmem] * 7,
        out_specs=(vmem,) * 4,
        scratch_shapes=line_scratch,
        input_output_aliases={3 + n: n for n in range(4)},
        compiler_params=params,
        cost_estimate=beside,
    )(*arguments, *near)
    here_side, sides, here_again = pl.pallas_call(
        reduce_kernel,
        out_shape=(
            float_shape(SIDE_ROWS, LANES),
            float_shape(blocks - 1, 2 * PAIRS, *plane),
            float_shape(SECOND_ROWS, LANES),
        ),
        in_specs=[vmem] * 5,
        out_specs=(vmem,) * 3,
        compiler_params=params,
    )(partial, from_partner, factors, correction, here)
    there_side = swap_halves(here_side)
    there_second = pass_round(here_again, SECOND_ROUND)
    known, spread = pl.pallas_call(
        spread_kernel,
        out_shape=(float_shape(2 * PAIRS, *plane), float_shape(4, *plane)),
        in_specs=[vmem] * 3,
        out_specs=(vmem, vmem),
        scratch_shapes=[pltpu.VMEM((blocks, 2 * PAIRS + 4) + plane, jnp.float32)],
        compiler_params=params,
        cost_estimate=beside,
    )(shared, eliminated, sides)
    side, other, matrices = pl.pallas_call(
        middle_kernel,
        out_shape=(
            float_shape(2 * PAIRS, *plane),
            float_shape(2 * PAIRS, *plane),
            float_shape(14, *plane),
        ),
        in_specs=[vmem] * 5,
        out_specs=(vmem,) * 3,
        compiler_params=params,
    )(here, there_first, there_second, here_side, there_side)
    return pl.pallas_call(
        join_kernel,
        out_shape=float_shape(*state.shape),
        in_specs=[vmem] * 6,
        out_specs=vmem,
        compiler_params=params,
    )(side, other, matrices, there_side, known, spread)


def solution(mesh):
    placed = (P("inst", None, "cell", None), P("cell", None), P(), P())
    inst_count, cell_count = mesh.shape["inst"], mesh.shape["cell"]

    def local(state, pseudo_rate, line_next, face_codes):
        small = (
            state.shape == (2, 6, 2, 2 * LANES)
            and inst_count * 2 == NT
            and cell_count == 8
            and face_codes.shape[1] * LINES_DEV == state.shape[3]
        )
        chosen = local_by_halves if small else local_by_lines
        return chosen(state, pseudo_rate, line_next, face_codes)

    return jax.shard_map(
        local, mesh=mesh, in_specs=placed, out_specs=P("inst", None, "cell", None), check_vma=False
    )
```
